32 devices in a mesh: dp: 8 (over z, x), mp: 4 (over y, core).
Axes of the slice: x: 2, y: 2, z: 4, core: 2. Of those that a mesh axis runs over, the one named last changes fastest.
Arguments:
- patches: bfloat16 [128, 196, 384], P(('dp', 'mp')), may hold values from -6 to 6
- qkv_weight: bfloat16 [2, 384, 1152], P(None, None, 'mp'), may hold values from -0.3125 to 0.3125
- proj_weight: bfloat16 [2, 384, 384], P(None, None, 'mp'), may hold values from -0.875 to 0.875
- core_up: bfloat16 [2, 384, 1536], P(None, None, 'mp'), may hold values from -0.3125 to 0.3125
- core_down: bfloat16 [2, 1536, 384], P(None, None, 'mp'), may hold values from -1.25 to 1.25
- residual_up: bfloat16 [2, 8, 384, 1536], P(None, 'dp'), may hold values from -0.15625 to 0.15625
- residual_down: bfloat16 [2, 8, 1536, 384], P(None, 'dp'), may hold values from -0.625 to 0.625
- position_bias: float32 [2, 169, 12], replicated, may hold values from -6 to 6
- router_weight: bfloat16 [2, 384, 8], replicated, may hold values from -0.21875 to 0.21875
- norm_gain: float32 [2, 2, 384], replicated, may hold values from 0.5 to 1.5
- norm_bias: float32 [2, 2, 384], replicated, may hold values from -1.25 to 1.25
- cotangent: bfloat16 [128, 196, 384], P(('dp', 'mp')), may hold values from -6 to 6
- image_valid: int32 [128], P(('dp', 'mp')), may hold values from 0 to 1, as said below
- expert_index: int32 [128, 196], P(('dp', 'mp')), may hold values from 0 to 7
- slot_index: int32 [128, 196], P(('dp', 'mp')), may hold values from -1 to 121, as said below
- region_id: int32 [128, 14, 14], P(('dp', 'mp')), may hold values from 0 to 3
Outputs:
- block_output: bfloat16 [128, 196, 384], P(('dp', 'mp'))
- input_grad: float32 [128, 196, 384], P(('dp', 'mp'))
- qkv_grad: float32 [2, 384, 1152], P(None, None, 'mp')
- proj_grad: float32 [2, 384, 384], P(None, None, 'mp')
- core_up_grad: float32 [2, 384, 1536], P(None, None, 'mp')
- core_down_grad: float32 [2, 1536, 384], P(None, None, 'mp')
- residual_up_grad: float32 [2, 8, 384, 1536], P(None, 'dp')
- residual_down_grad: float32 [2, 8, 1536, 384], P(None, 'dp')
- position_grad: float32 [2, 169, 12], replicated
- router_grad: float32 [2, 384, 8], replicated
- gain_grad: float32 [2, 2, 384], replicated
- bias_grad: float32 [2, 2, 384], replicated
The draws below stay inside these ranges and needn't reach their ends.
Inputs may be any that keep to these rules, and one draw needn't show every extreme that they name: `image_valid`: on each device (the 4 image slots of one index of dp+mp) the real images come first, and there are 4 or 2 of them. `slot_index`: among the tokens of one device, each pair of expert and slot belongs to at most one token; tokens of padding slots have -1.
All inputs are finite; a program needn't handle non-finite values.
Results may differ from the reference program's by a relative error of at most 0.024.
Values may be sent and summed in bfloat16 or wider, within the bound.
A program may use at most 192 MiB of HBM per device.

```python
import jax
import jax.numpy as jnp
from jax import lax

D = 384
HEADS = 12
HEAD_DIM = 32
FF = 1536
EXPERTS = 8
WINDOW = 7
GRID = 14
SHIFT = 3
LAYERS = 2
IMG_DEV = 4
PATCHES = 196
WINPOS = 49
OFFSETS = 169
TOK_DEV = 784
IMAGES = 128
CAP = 122
SPLIT = 1
HSL = 1536
N_DP = 8
N_MP = 4
DEVICES = 32


def routing_draw(key):
    device_count = IMAGES // IMG_DEV
    halved_key, favored_key, picked_key, anyone_key = jax.random.split(key, 4)
    halved = jax.random.randint(halved_key, (device_count,), 0, 4) == 0
    live_images = jnp.where(halved, IMG_DEV // 2, IMG_DEV)
    valid_flags = (jnp.arange(IMG_DEV)[None, :] < live_images[:, None]).astype(jnp.int32).reshape(IMAGES)
    favored = jax.random.randint(favored_key, (), 0, EXPERTS)
    picked = jax.random.randint(picked_key, (IMAGES, PATCHES), 0, 4) == 0
    anyone = jax.random.randint(anyone_key, (IMAGES, PATCHES), 0, EXPERTS)
    expert = jnp.where(picked, favored, anyone).astype(jnp.int32)
    per_device = expert.reshape(device_count, TOK_DEV)
    live_tokens = jnp.repeat(valid_flags, PATCHES).reshape(device_count, TOK_DEV)
    onehot = (per_device[..., None] == jnp.arange(EXPERTS)[None, None, :]).astype(jnp.int32) * live_tokens[..., None]
    before = jnp.cumsum(onehot, axis=1) - onehot
    ordinal = jnp.sum(before * onehot, -1)
    slot_numbers = jnp.where((live_tokens == 1) & (ordinal < CAP), ordinal, -1).astype(jnp.int32)
    return (valid_flags, expert, slot_numbers.reshape(IMAGES, PATCHES))


def draw_image_valid(key, part):
    return routing_draw(key)[0]


def draw_expert_index(key, part):
    return routing_draw(key)[1]


def draw_slot_index(key, part):
    return routing_draw(key)[2]


def draw_region_id(key, part):
    key = jax.random.fold_in(key, 7)
    rows_key, cols_key = jax.random.split(key, 2)
    rows_cut = jax.random.randint(rows_key, (IMAGES, 1, 1), 1, GRID)
    cols_cut = jax.random.randint(cols_key, (IMAGES, 1, 1), 1, GRID)
    rowpos = jnp.arange(GRID)[None, :, None]
    colpos = jnp.arange(GRID)[None, None, :]
    return (2 * (rowpos >= rows_cut) + (colpos >= cols_cut)).astype(jnp.int32)


def levels(stream_key, dims, cuts, least, largest):
    def one(dim, parts):
        draws = jax.random.uniform(jax.random.fold_in(jax.random.fold_in(stream_key, 6), dim), (parts,), jnp.float32, least / len(cuts), largest / len(cuts))
        return jnp.repeat(jnp.exp(draws), dims[dim] // parts).reshape((-1,) + (1,) * (len(dims) - dim - 1))

    loudness = one(*cuts[0])
    for cut in cuts[1:]:
        loudness = loudness * one(*cut)
    return loudness


def centred(rng, dims, scale, reach, pieces=(), kind=jnp.bfloat16):
    level = levels(rng, dims, pieces, -0.22, 0.18) if pieces else 1.0
    values = jax.random.normal(rng, dims, jnp.float32) * scale * level
    return jnp.minimum(jnp.maximum(values, -reach), reach).astype(kind)


def setup_inputs(seed: int = 0) -> dict:
    keys = jax.random.split(jax.random.key(seed), 17)
    return {
        "patches": centred(keys[0], (IMAGES, PATCHES, D), 1.0, 6.0, ((0, 32),)),
        "qkv_weight": centred(keys[1], (LAYERS, D, 3 * D), D ** -0.5, 0.3125, ((2, 4),)),
        "proj_weight": centred(keys[2], (LAYERS, D, D), (D // 8) ** -0.5, 0.875, ((2, 4),)),
        "core_up": centred(keys[3], (LAYERS, D, FF), D ** -0.5, 0.3125, ((2, 4),)),
        "core_down": centred(keys[4], (LAYERS, FF, D), (FF // 64) ** -0.5, 1.25, ((2, 4),)),
        "residual_up": centred(keys[5], (LAYERS, EXPERTS * SPLIT, D, HSL), (4 * D) ** -0.5, 0.15625, ((1, 8),)),
        "residual_down": centred(keys[6], (LAYERS, EXPERTS * SPLIT, HSL, D), (FF // 16) ** -0.5, 0.625, ((1, 8),)),
        "position_bias": centred(keys[7], (LAYERS, OFFSETS, HEADS), 1.0, 6.0, (), jnp.float32),
        "router_weight": centred(keys[8], (LAYERS, D, EXPERTS), (2 * D) ** -0.5, 0.21875),
        "norm_gain": jnp.clip(1.0 + 0.1 * jax.random.normal(keys[9], (LAYERS, 2, D), jnp.float32), 0.5, 1.5),
        "norm_bias": centred(keys[10], (LAYERS, 2, D), 0.2, 1.25, (), jnp.float32),
        "cotangent": centred(keys[11], (IMAGES, PATCHES, D), 1.0, 6.0, ((0, 32),)),
        "image_valid": draw_image_valid(jax.random.fold_in(keys[16], 71), 0),
        "expert_index": draw_expert_index(jax.random.fold_in(keys[16], 71), 0),
        "slot_index": draw_slot_index(jax.random.fold_in(keys[16], 71), 0),
        "region_id": draw_region_id(jax.random.fold_in(keys[16], 71), 0),
    }


highest = lax.Precision.HIGHEST
norm_epsilon = 1e-05
mask_fill = -100.0

@jax.custom_vjp
def low(v):
    return lax.optimization_barrier(v.astype(jnp.bfloat16)).astype(jnp.float32)

@jax.custom_vjp
def low_back(v):
    return v

def low_keep(v):
    return (low(v), None)

def low_pass(kept, grad):
    return (grad,)

def back_keep(v):
    return (v, None)

def back_low(kept, grad):
    return (low(grad),)
low.defvjp(low_keep, low_pass)
low_back.defvjp(back_keep, back_low)

def normalize(values, gain, bias):
    center = values - lax.optimization_barrier(jnp.mean(values, -1, keepdims=True))
    spread = lax.optimization_barrier(jnp.mean(center * center, -1, keepdims=True))
    return center * lax.rsqrt(spread + norm_epsilon) * gain + bias

def to_windows(layout, shifted):
    if shifted:
        layout = jnp.roll(layout, (-SHIFT, -SHIFT), (1, 2))
    image_count = layout.shape[0]
    channels = layout.shape[-1]
    blocks = GRID // WINDOW
    layout = layout.reshape(image_count, blocks, WINDOW, blocks, WINDOW, channels).transpose(0, 1, 3, 2, 4, 5)
    return layout.reshape(image_count * blocks * blocks, WINDOW * WINDOW, channels)

def from_windows(windows, shifted):
    channels = windows.shape[-1]
    blocks = GRID // WINDOW
    image_count = windows.shape[0] // (blocks * blocks)
    layout = windows.reshape(image_count, blocks, blocks, WINDOW, WINDOW, channels).transpose(0, 1, 3, 2, 4, 5)
    layout = layout.reshape(image_count, GRID, GRID, channels)
    if shifted:
        layout = jnp.roll(layout, (SHIFT, SHIFT), (1, 2))
    return layout

def offset_onehot():
    cell_ids = jnp.arange(WINPOS)
    rowpos = cell_ids // WINDOW
    colpos = cell_ids % WINDOW
    offset = (rowpos[:, None] - rowpos[None, :] + WINDOW - 1) * (2 * WINDOW - 1) + colpos[:, None] - colpos[None, :] + WINDOW - 1
    return (offset.reshape(-1)[:, None] == jnp.arange(OFFSETS)[None, :]).astype(jnp.float32)

def relative_bias(table):
    return jnp.dot(offset_onehot(), table, precision=highest).reshape(WINPOS, WINPOS, HEADS).transpose(2, 0, 1)

def region_mask(region):
    labels = to_windows(region[..., None], True)[..., 0]
    return jnp.where(labels[:, :, None] == labels[:, None, :], 0.0, mask_fill).astype(jnp.float32)

def attend_group(normed, region, qkv_full, proj_full, table, shifted):
    inputs_low = low(to_windows(normed, shifted))
    window_count = inputs_low.shape[0]
    mixed = low_back(low(jnp.dot(inputs_low.reshape(-1, D), qkv_full, precision=highest)))
    mixed = mixed.reshape(window_count, WINPOS, 3, HEADS, HEAD_DIM)
    query_rows = mixed[:, :, 0]
    key_rows = mixed[:, :, 1]
    value_rows = mixed[:, :, 2]
    raw = low_back(jnp.einsum('wihd,wjhd->whij', query_rows, key_rows, precision=highest) * HEAD_DIM ** (-0.5))
    scores = raw + relative_bias(table)[None]
    if shifted:
        scores = scores + region_mask(region)[:, None]
    probs = jax.nn.softmax(scores, axis=-1)
    attended = low_back(low(jnp.einsum('whij,wjhd->wihd', low(probs), value_rows, precision=highest)))
    branch = low_back(jnp.dot(attended.reshape(-1, D), proj_full, precision=highest))
    return from_windows(branch.reshape(window_count, WINPOS, D), shifted)

def expert_rows(inputs):
    rows, up_eff, down_eff = inputs
    split = N_DP // EXPERTS
    hidden_slice = FF // split
    total = jnp.zeros(rows.shape, jnp.float32)
    for piece_number in range(split):
        start = piece_number * hidden_slice
        rows_piece = low_back(rows)
        hidden_pre = low_back(jnp.dot(rows_piece, up_eff[:, start:start + hidden_slice], precision=highest))
        hidden_low = low(jax.nn.gelu(hidden_pre))
        total = total + low_back(low(jnp.dot(hidden_low, down_eff[start:start + hidden_slice, :], precision=highest)))
    return total

def forward(patches, qkv_weight, proj_weight, core_up, core_down, residual_up, residual_down, position_bias, router_weight, norm_gain, norm_bias, image_valid, expert_index, slot_index, region_id):
    image_count = patches.shape[0]
    split = N_DP // EXPERTS
    hidden_slice = FF // split
    carried = patches.reshape(image_count, GRID, GRID, D)
    valid_rows = image_valid.astype(jnp.float32)[:, None, None, None]
    expert_flat = expert_index.reshape(-1)
    slot_flat = slot_index.reshape(-1)
    kept = (slot_flat >= 0).astype(jnp.float32)
    device_of = jnp.arange(IMAGES * PATCHES).astype(jnp.int32) // TOK_DEV
    buffer_rows = EXPERTS * DEVICES * CAP
    position = jnp.where(slot_flat >= 0, expert_flat * (DEVICES * CAP) + device_of * CAP + slot_flat, buffer_rows).astype(jnp.int32)
    chosen = jax.nn.one_hot(expert_flat, EXPERTS, dtype=jnp.float32)
    group_images = IMG_DEV * N_MP
    for layer_number in range(LAYERS):
        shifted = layer_number % 2 == 1
        qkv_full = qkv_weight[layer_number]
        proj_full = proj_weight[layer_number]
        table = position_bias[layer_number]
        first_norm = normalize(carried, norm_gain[layer_number, 0], norm_bias[layer_number, 0])

        def one_group(inputs):
            return attend_group(inputs[0], inputs[1], qkv_full, proj_full, table, shifted)
        branch = lax.map(jax.checkpoint(one_group), (first_norm.reshape(-1, group_images, GRID, GRID, D), region_id.reshape(-1, group_images, GRID, GRID)))
        middle = carried + valid_rows * branch.reshape(carried.shape)
        second_low = low(normalize(middle, norm_gain[layer_number, 1], norm_bias[layer_number, 1]).reshape(-1, D))
        router_probs = jax.nn.softmax(jnp.dot(second_low, router_weight[layer_number], precision=highest), axis=-1)
        gate = lax.optimization_barrier(jnp.sum(router_probs * chosen, -1))
        buffers = jnp.zeros((buffer_rows, D), jnp.float32).at[position].set(second_low, mode='drop')
        buffers = buffers.reshape(EXPERTS, DEVICES * CAP, D)
        up_whole = residual_up[layer_number].reshape(EXPERTS, split, D, hidden_slice).transpose(0, 2, 1, 3).reshape(EXPERTS, D, FF)
        down_whole = residual_down[layer_number].reshape(EXPERTS, FF, D)
        up_eff = low(core_up[layer_number][None] + up_whole)
        down_eff = low(core_down[layer_number][None] + down_whole)
        outputs = lax.map(jax.checkpoint(expert_rows), (buffers, up_eff, down_eff))
        expert_out = jnp.take(outputs.reshape(-1, D), jnp.minimum(position, buffer_rows - 1), axis=0) * kept[:, None]
        carried = middle + ((gate * kept)[:, None] * expert_out).reshape(middle.shape)
    return carried.reshape(patches.shape)

def reference(patches, qkv_weight, proj_weight, core_up, core_down, residual_up, residual_down, position_bias, router_weight, norm_gain, norm_bias, cotangent, image_valid, expert_index, slot_index, region_id):
    floats = tuple((array.astype(jnp.float32) for array in (patches, qkv_weight, proj_weight, core_up, core_down, residual_up, residual_down, position_bias, router_weight, norm_gain, norm_bias)))

    def wrapped(*weights):
        return forward(*weights, image_valid, expert_index, slot_index, region_id)
    result, pullback = jax.vjp(wrapped, *floats)
    grads = pullback(cotangent.astype(jnp.float32))
    return (result.astype(jnp.bfloat16), grads[0], grads[1], grads[2], grads[3], grads[4], grads[5], grads[6], grads[7], grads[8], grads[9], grads[10])
```

```python
import functools

import jax
import jax.numpy as jnp
import numpy as np
from jax import lax
from jax.experimental import pallas as pl
from jax.experimental.pallas import tpu as pltpu
from jax.sharding import PartitionSpec as P

HEADS = 12
HEAD_DIM = 32
EXPERTS = 8
WINDOW = 7
GRID = 14
SHIFT = 3
LAYERS = 2
WINPOS = 49
OFFSETS = 169
CAP = 122

WPAD = 64
IMGROWS = 256
PATCHES = 196
SLOTS = 128
ROWS = EXPERTS * SLOTS
LANES = 128
GROUP = 4
PAIRS = 2

bf16 = jnp.bfloat16
f32 = jnp.float32
highest = lax.Precision.HIGHEST
norm_epsilon = 1e-05
mask_fill = -100.0
head_scale = HEAD_DIM ** (-0.5)
MESH = pl.DeviceIdType.MESH
MIB = 1024 * 1024


def nn(a, b):
    return lax.dot_general(a, b, (((1,), (0,)), ((), ())), preferred_element_type=f32)


def nt(a, b):
    return lax.dot_general(a, b, (((1,), (1,)), ((), ())), preferred_element_type=f32)


def tn(a, b):
    return lax.dot_general(a, b, (((0,), (0,)), ((), ())), preferred_element_type=f32)


def iota(shape, dim):
    return lax.broadcasted_iota(jnp.int32, shape, dim)


def onehot(flags):
    return jnp.where(flags, 1.0, 0.0).astype(bf16)


def natural_of_row(shifted):
    moved = SHIFT if shifted else 0
    blocks = GRID // WINDOW
    out = -np.ones(IMGROWS, np.int32)
    for window in range(blocks * blocks):
        for cell in range(WINPOS):
            row = (window // blocks * WINDOW + cell // WINDOW + moved) % GRID
            col = (window % blocks * WINDOW + cell % WINDOW + moved) % GRID
            out[window * WPAD + cell] = row * GRID + col
    return out


def enter_table():
    held = natural_of_row(False)
    return (held[:, None] == np.arange(PATCHES)[None, :]).astype(np.float32)


def move_table(shifted):
    first, second = natural_of_row(False), natural_of_row(shifted)
    same = (second[:, None] == first[None, :]) & (second[:, None] >= 0)
    return same.astype(np.float32)


def offset_index():
    key = np.arange(WPAD)[:, None]
    query = np.arange(LANES)[None, :] % WPAD
    entry = (
        (query // WINDOW - key // WINDOW + WINDOW - 1) * (2 * WINDOW - 1)
        + query % WINDOW
        - key % WINDOW
        + WINDOW
        - 1
    )
    real = (key < WINPOS) & (query < WINPOS)
    return np.where(real, entry, np.where(key < WINPOS, -1, OFFSETS)).astype(np.int32)


def norm_parts(x):
    width = x.shape[-1]
    center = x - jnp.sum(x, -1, keepdims=True) * (1.0 / width)
    spread = jnp.sum(center * center, -1, keepdims=True) * (1.0 / width)
    rstd = lax.rsqrt(spread + norm_epsilon)
    return center * rstd, rstd


def norm_back(grad, gain, xhat, rstd):
    width = xhat.shape[-1]
    dxhat = grad * gain
    mean_one = jnp.sum(dxhat, -1, keepdims=True) * (1.0 / width)
    mean_two = jnp.sum(dxhat * xhat, -1, keepdims=True) * (1.0 / width)
    return rstd * (dxhat - mean_one - xhat * mean_two)


def split_two(x):
    high = x.astype(bf16)
    return high, (x - high.astype(f32)).astype(bf16)


def collect(pos_col, returned_ref):
    pick = onehot(pos_col == iota((IMGROWS, ROWS), 1))
    out = nn(pick, returned_ref[0])
    for piece in range(1, returned_ref.shape[0]):
        out = out + nn(pick, returned_ref[piece])
    return out


def spread_rows(pos_row, rows_low):
    return nn(onehot(iota((ROWS, IMGROWS), 0) == pos_row), rows_low)


def route(second_low, router, pos_col):
    logits = nn(second_low, router)
    lane = iota(logits.shape, 1)
    logits = jnp.where(lane < EXPERTS, logits, -1e30)
    expo = jnp.exp(logits - jnp.max(logits, -1, keepdims=True))
    probs = expo / jnp.sum(expo, -1, keepdims=True)
    expert = jnp.where(pos_col >= 0, pos_col // SLOTS, -1)
    chosen = jnp.where(lane == expert, 1.0, 0.0)
    return probs, chosen, jnp.sum(probs * chosen, -1, keepdims=True)


def head_masks():
    rows = iota((LANES, LANES), 0) // HEAD_DIM
    return [onehot(rows == h) for h in range(GROUP)]


def lane_masks():
    lane = iota((WPAD, LANES), 1)
    return [onehot(lane < WPAD), onehot(lane >= WPAD)]


def place_columns(target, shards_ref, count, transposed):
    size = shards_ref.shape[-1]
    target[...] = jnp.zeros(target.shape, target.dtype)
    for m in range(count):
        start = m * size // LANES * LANES
        stop = -(-(m + 1) * size // LANES) * LANES
        span = stop - start
        if transposed:
            put = onehot(iota((span, size), 0) + start == iota((span, size), 1) + m * size)
            target[start:stop, :] += nt(put, shards_ref[m]).astype(bf16)
        else:
            put = onehot(iota((size, span), 0) + m * size == iota((size, span), 1) + start)
            target[:, start:stop] += nn(shards_ref[m], put).astype(bf16)


def attention_forward_kernel(first, shifted, mp, *refs):
    refs = list(refs)
    if first:
        patches_ref, enter_ref = refs[:2]
        refs = refs[2:]
    else:
        prev_ref, prev_gate_ref, returned_ref = refs[:3]
        refs = refs[3:]
    (
        valid_ref, col_ref, row_ref, qkv_ref, proj_ref, bias_ref, move_ref, back_ref, gain_ref, nbias_ref, router_ref,
    ) = refs[:11]
    refs = refs[11:]
    carried_ref = refs.pop(0)
    expert_out_ref = None if first else refs.pop(0)
    (
        middle_ref, second_ref, gate_ref, buffer_ref, window_ref, qk_ref, v_ref, probs_ref, att_ref, qkv_full, proj_full,
        qkv_turned, total_ref,
    ) = refs
    image = pl.program_id(0)
    width = carried_ref.shape[-1]

    @pl.when(image == 0)
    def _():
        place_columns(qkv_full, qkv_ref, mp, False)
        place_columns(qkv_turned, qkv_ref, mp, True)
        place_columns(proj_full, proj_ref, mp, False)
        total_ref[...] = jnp.zeros(total_ref.shape, f32)

    pos_col = col_ref[0, :, 0:1]
    pos_row = row_ref[0, 0:1, :]
    if first:
        x = nn(enter_ref[...], patches_ref[0])
    else:
        expert_out = collect(pos_col, returned_ref)
        expert_out_ref[0] = expert_out
        x = prev_ref[0] + prev_gate_ref[0] * expert_out
    carried_ref[0] = x
    xhat, _ = norm_parts(x)
    normed = (xhat * gain_ref[0:1, :] + nbias_ref[0:1, :]).astype(bf16)
    window_in = nn(move_ref[...], normed).astype(bf16)
    window_ref[0] = window_in
    turned = nt(qkv_turned[...], window_in).astype(bf16)
    straight = nn(window_in, qkv_full[:, width:]).astype(bf16)
    qk_ref[0] = turned[: 2 * width]
    v_ref[0] = straight[:, width:]
    heads_rows = head_masks()
    halves = lane_masks()
    low_lane = iota((WPAD, LANES), 1) < WPAD
    for pair in range(PAIRS):
        across = slice(pair * LANES, (pair + 1) * LANES)
        if shifted:
            ahead = col_ref[0, pair * LANES : pair * LANES + WPAD, 1:2]
            behind = col_ref[0, pair * LANES + WPAD : (pair + 1) * LANES, 1:2]
            key_label = jnp.where(low_lane, ahead, behind)
            mask = jnp.where(key_label == row_ref[0, 1:2, across], 0.0, mask_fill)
        for group in range(HEADS // GROUP):
            features = slice(group * LANES, (group + 1) * LANES)
            queries = turned[features, across]
            spread = jnp.concatenate([queries * heads_rows[h] for h in range(GROUP)], 1)
            raw = nn(straight[across, features], spread)
            for h in range(GROUP):
                head = group * GROUP + h
                part = raw[:, h * LANES : (h + 1) * LANES]
                scores = jnp.where(low_lane, part[:WPAD], part[WPAD:]) * head_scale + bias_ref[head]
                if shifted:
                    scores = scores + mask
                expo = jnp.exp(scores - jnp.max(scores, 0, keepdims=True))
                probs = (expo * (1.0 / jnp.sum(expo, 0, keepdims=True))).astype(bf16)
                probs_ref[0, pair * HEADS + head] = probs
                both = jnp.concatenate([probs * halves[0], probs * halves[1]], 0)
                at = slice(head * HEAD_DIM, (head + 1) * HEAD_DIM)
                values = turned[2 * width + head * HEAD_DIM : 2 * width + (head + 1) * HEAD_DIM, across]
                att_ref[0, at, across] = nn(values, both).astype(bf16)
    attended = nt(back_ref[...], att_ref[0]).astype(bf16)
    middle = x + valid_ref[image].astype(f32) * nn(attended, proj_full[...])
    middle_ref[0] = middle
    xhat, _ = norm_parts(middle)
    second_low = (xhat * gain_ref[1:2, :] + nbias_ref[1:2, :]).astype(bf16)
    second_ref[0] = second_low
    _, _, gate = route(second_low, router_ref[...], pos_col)
    gate_ref[0] = gate
    total_ref[...] += spread_rows(pos_row, second_low)

    @pl.when(image == pl.num_programs(0) - 1)
    def _():
        buffer_ref[...] = total_ref[...].astype(bf16)


def image_spec(array_shape):
    rest = tuple(array_shape[1:])
    zeros = (0,) * len(rest)
    return pl.BlockSpec((1,) + rest, lambda i: (i,) + zeros)


def whole_spec(array_shape):
    zeros = (0,) * len(array_shape)
    return pl.BlockSpec(tuple(array_shape), lambda i: zeros)


def image_call(kernel, images, arrays, outs, scratch, name):
    def spec(kind, shape):
        if kind == "smem":
            return pl.BlockSpec(memory_space=pltpu.SMEM)
        return image_spec(shape) if kind == "image" else whole_spec(shape)

    return pl.pallas_call(
        kernel,
        grid=(images,),
        out_shape=[jax.ShapeDtypeStruct(shape, dtype) for _, shape, dtype in outs],
        in_specs=[spec(kind, array.shape) for kind, array in arrays],
        out_specs=[spec(kind, shape) for kind, shape, _ in outs],
        scratch_shapes=scratch,
        compiler_params=pltpu.CompilerParams(
            vmem_limit_bytes=56 * MIB, dimension_semantics=("arbitrary",)
        ),
        name=name,
    )(*[array for _, array in arrays])


def send_part(g, expert_out, second_low, router, pos_col, pos_row, logit_ref, router_grad_ref, total_ref):
    probs, chosen, gate = route(second_low, router, pos_col)
    gate_grad = jnp.where(pos_col >= 0, jnp.sum(g * expert_out, -1, keepdims=True), 0.0)
    sent = (gate * g).astype(bf16)
    logit_grad = gate_grad * gate * (chosen - probs)
    logit_ref[0] = logit_grad
    high, low = split_two(logit_grad)
    router_grad_ref[...] += tn(high, second_low) + tn(low, second_low)
    total_ref[...] += spread_rows(pos_row, sent)


def turn_kernel(
    prev_ref, gate_ref, returned_ref, cotangent_ref, enter_ref, leave_ref, col_ref, row_ref, second_ref, router_ref,
    block_ref, grad_ref, logit_ref, router_grad_ref, buffer_ref, total_ref,
):
    image = pl.program_id(0)

    @pl.when(image == 0)
    def _():
        total_ref[...] = jnp.zeros(total_ref.shape, f32)
        router_grad_ref[...] = jnp.zeros(router_grad_ref.shape, f32)

    pos_col = col_ref[0, :, 0:1]
    expert_out = collect(pos_col, returned_ref)
    x = prev_ref[0] + gate_ref[0] * expert_out
    block_ref[0] = nn(leave_ref[...], x.astype(bf16)).astype(bf16)
    g = nn(enter_ref[...], cotangent_ref[0])
    grad_ref[0] = g
    send_part(
        g, expert_out, second_ref[0], router_ref[...], pos_col, row_ref[0, 0:1, :], logit_ref, router_grad_ref, total_ref
    )

    @pl.when(image == pl.num_programs(0) - 1)
    def _():
        buffer_ref[...] = total_ref[...].astype(bf16)


def attention_backward_kernel(last, *refs):
    (
        valid_ref, grad_ref, returned_ref, logit_ref, middle_ref, carried_ref, router_ref, col_ref, move_ref, back_ref,
        gain_ref, proj_ref, qkv_ref, window_ref, qk_ref, v_ref, probs_ref, att_ref,
    ) = refs[:18]
    refs = refs[18:]
    if last:
        (leave_ref, out_ref, qkv_grad_ref, proj_grad_ref, table_ref, small_ref, turned) = refs
    else:
        (
            row_ref, expert_out_ref, second_ref, router_next_ref, out_ref, qkv_grad_ref, proj_grad_ref, table_ref,
            small_ref, logit_out_ref, router_grad_ref, buffer_ref, turned, total_ref,
        ) = refs
    image = pl.program_id(0)
    width = carried_ref.shape[-1]

    @pl.when(image == 0)
    def _():
        qkv_grad_ref[...] = jnp.zeros(qkv_grad_ref.shape, f32)
        proj_grad_ref[...] = jnp.zeros(proj_grad_ref.shape, f32)
        table_ref[...] = jnp.zeros(table_ref.shape, f32)
        small_ref[...] = jnp.zeros(small_ref.shape, f32)
        if not last:
            total_ref[...] = jnp.zeros(total_ref.shape, f32)
            router_grad_ref[...] = jnp.zeros(router_grad_ref.shape, f32)

    pos_col = col_ref[0, :, 0:1]
    g = grad_ref[0]
    high, low = split_two(logit_ref[0])
    router = router_ref[...]
    normed_grad = collect(pos_col, returned_ref) + nt(high, router) + nt(low, router)
    xhat, rstd = norm_parts(middle_ref[0])
    small_ref[1:2, :] += jnp.sum(normed_grad * xhat, 0, keepdims=True)
    small_ref[3:4, :] += jnp.sum(normed_grad, 0, keepdims=True)
    middle_grad = g + norm_back(normed_grad, gain_ref[1:2, :], xhat, rstd)
    branch_grad = (valid_ref[image].astype(f32) * middle_grad).astype(bf16)
    branch_grad = nn(move_ref[...], branch_grad).astype(bf16)
    proj_grad_ref[...] += nn(att_ref[0], branch_grad)
    att_grad = nt(proj_ref[...], branch_grad).astype(bf16)
    heads_rows = head_masks()
    halves = lane_masks()
    low_lane = iota((WPAD, LANES), 1) < WPAD
    for pair in range(PAIRS):
        across = slice(pair * LANES, (pair + 1) * LANES)
        for group in range(HEADS // GROUP):
            features = slice(group * LANES, (group + 1) * LANES)
            grads = att_grad[features, across]
            spread = jnp.concatenate([grads * heads_rows[h] for h in range(GROUP)], 1)
            raw = nn(v_ref[0, across, features], spread)
            for h in range(GROUP):
                head = group * GROUP + h
                at = slice(head * HEAD_DIM, (head + 1) * HEAD_DIM)
                below = slice(width + head * HEAD_DIM, width + (head + 1) * HEAD_DIM)
                lowest = slice(2 * width + head * HEAD_DIM, 2 * width + (head + 1) * HEAD_DIM)
                part = raw[:, h * LANES : (h + 1) * LANES]
                probs_grad = jnp.where(low_lane, part[:WPAD], part[WPAD:])
                probs_low = probs_ref[0, pair * HEADS + head]
                probs = probs_low.astype(f32)
                weighted = probs * probs_grad
                scores_grad = weighted - probs * jnp.sum(weighted, 0, keepdims=True)
                table_ref[head] += scores_grad
                scores_low = scores_grad.astype(bf16)
                both = jnp.concatenate([scores_low * halves[0], scores_low * halves[1]], 0)
                probs_both = jnp.concatenate([probs_low * halves[0], probs_low * halves[1]], 0)
                turned[at, across] = (nn(qk_ref[0, below, across], both) * head_scale).astype(bf16)
                turned[below, across] = (nt(qk_ref[0, at, across], both) * head_scale).astype(bf16)
                turned[lowest, across] = nt(att_grad[at, across], probs_both).astype(bf16)
    qkv_grad_ref[...] += nn(turned[...], window_ref[0])
    mixed_grad = nt(back_ref[...], turned[...]).astype(bf16)
    first_grad = nt(mixed_grad, qkv_ref[...])
    xhat, rstd = norm_parts(carried_ref[0])
    small_ref[0:1, :] += jnp.sum(first_grad * xhat, 0, keepdims=True)
    small_ref[2:3, :] += jnp.sum(first_grad, 0, keepdims=True)
    out = middle_grad + norm_back(first_grad, gain_ref[0:1, :], xhat, rstd)
    if last:
        top = out.astype(bf16)
        rest = out - top.astype(f32)
        mid, low = split_two(rest)
        leave = leave_ref[...]
        out_ref[0] = nn(leave, top) + nn(leave, mid) + nn(leave, low)
        return
    out_ref[0] = out
    send_part(
        out, expert_out_ref[0], second_ref[0], router_next_ref[...], pos_col, row_ref[0, 0:1, :], logit_out_ref,
        router_grad_ref, total_ref,
    )

    @pl.when(image == pl.num_programs(0) - 1)
    def _():
        buffer_ref[...] = total_ref[...].astype(bf16)


def greet(dp, me):
    barrier = pltpu.get_barrier_semaphore()

    def signal(off, carry):
        pl.semaphore_signal(barrier, inc=1, device_id={"dp": lax.rem(me + off, dp)}, device_id_type=MESH)
        return carry

    lax.fori_loop(1, dp, signal, 0)
    pl.semaphore_wait(barrier, dp - 1)


def to_peer(source, target, send_sem, recv_sem, peer):
    return pltpu.make_async_remote_copy(
        src_ref=source,
        dst_ref=target,
        send_sem=send_sem,
        recv_sem=recv_sem,
        device_id={"dp": peer},
        device_id_type=MESH,
    )


def gelu_parts(h):
    root = np.float32(np.sqrt(2.0 / np.pi))
    square = h * h
    t = jnp.tanh(root * h * (1.0 + 0.044715 * square))
    half = 0.5 * (1.0 + t)
    slope = half + 0.5 * h * (1.0 - t * t) * root * (1.0 + 3 * 0.044715 * square)
    return h * half, slope


def expert_forward_kernel(
    dp, mp, buffer_ref, up_ref, down_ref, rup_ref, rdown_ref, recv_ref, returned_ref, up_eff, down_eff, part, core,
    send_one, recv_one, send_two, recv_two,
):
    split = dp // EXPERTS
    me = lax.axis_index("dp")
    greet(dp, me)

    def first(off):
        peer = lax.rem(me + off, dp)
        return to_peer(
            buffer_ref.at[lax.div(peer, split)], recv_ref.at[me], send_one.at[off], recv_one.at[off], peer
        )

    def second(off):
        source = lax.rem(me + dp - off, dp)
        return to_peer(part.at[source], returned_ref.at[me], send_two.at[off], recv_two.at[off], source)

    def start_first(off, carry):
        first(off).start()
        return carry

    lax.fori_loop(1, dp, start_first, 0)
    recv_ref[me] = buffer_ref[lax.div(me, split)]
    hidden = up_eff.shape[1]
    columns = up_ref.shape[-1]
    if split == 1 and columns % LANES == 0:
        for m in range(mp):
            at = slice(m * columns, (m + 1) * columns)
            up_eff[:, at] = (up_ref[m].astype(f32) + rup_ref[:, at].astype(f32)).astype(bf16)
    else:
        core[...] = rup_ref[...].astype(f32)
        begin = lax.rem(me, split) * hidden
        for m in range(mp):
            put = onehot(iota((columns, hidden), 0) + m * columns == iota((columns, hidden), 1) + begin)
            core[...] += nn(up_ref[m], put)
        up_eff[...] = core[...].astype(bf16)
    columns = down_ref.shape[-1]
    width = down_eff.shape[1]
    rows = pl.ds(pl.multiple_of(lax.rem(me, split) * hidden, LANES), hidden)
    total = rdown_ref[...].astype(f32)
    for m in range(mp):
        put = onehot(iota((columns, width), 0) + m * columns == iota((columns, width), 1))
        total = total + nn(down_ref[m, rows, :], put)
    down_eff[...] = total.astype(bf16)

    def work(source):
        hidden_pre = nn(recv_ref[source], up_eff[...])
        hidden_low = gelu_parts(hidden_pre)[0].astype(bf16)
        return nn(hidden_low, down_eff[...]).astype(bf16)

    returned_ref[me] = work(me)

    def step(off, carry):
        source = lax.rem(me + dp - off, dp)
        first(off).wait_recv()
        part[source] = work(source)
        second(off).start()
        return carry

    lax.fori_loop(1, dp, step, 0)

    def finish(off, carry):
        first(off).wait_send()
        second(off).wait()
        return carry

    lax.fori_loop(1, dp, finish, 0)


def expert_backward_kernel(
    dp, buffer_ref, recv_ref, up_ref, down_ref, returned_ref, up_term_ref, down_term_ref, grads, hidden_low, slope, pre,
    part, send_one, recv_one, send_two, recv_two,
):
    split = dp // EXPERTS
    me = lax.axis_index("dp")
    greet(dp, me)

    def first(off):
        peer = lax.rem(me + off, dp)
        return to_peer(buffer_ref.at[lax.div(peer, split)], grads.at[me], send_one.at[off], recv_one.at[off], peer)

    def second(off):
        source = lax.rem(me + dp - off, dp)
        return to_peer(part.at[source], returned_ref.at[me], send_two.at[off], recv_two.at[off], source)

    def start_first(off, carry):
        first(off).start()
        return carry

    lax.fori_loop(1, dp, start_first, 0)
    grads[me] = buffer_ref[lax.div(me, split)]

    def again(source, carry):
        value, rate = gelu_parts(nn(recv_ref[source], up_ref[...]))
        hidden_low[source] = value.astype(bf16)
        slope[source] = rate
        return carry

    lax.fori_loop(0, dp, again, 0)

    def work(source):
        hidden_grad = nt(grads[source], down_ref[...])
        pre_grad = (slope[source] * hidden_grad).astype(bf16)
        pre[source] = pre_grad
        return nt(pre_grad, up_ref[...]).astype(bf16)

    returned_ref[me] = work(me)

    def step(off, carry):
        source = lax.rem(me + dp - off, dp)
        first(off).wait_recv()
        part[source] = work(source)
        second(off).start()
        return carry

    lax.fori_loop(1, dp, step, 0)
    up_term_ref[...] = jnp.zeros(up_term_ref.shape, f32)
    down_term_ref[...] = jnp.zeros(down_term_ref.shape, f32)

    def terms(block, carry):
        up_term_ref[...] += tn(recv_ref[block], pre[block])
        down_term_ref[...] += tn(grads[block], hidden_low[block])
        return carry

    lax.fori_loop(0, dp, terms, 0)

    def finish(off, carry):
        first(off).wait_send()
        second(off).wait()
        return carry

    lax.fori_loop(1, dp, finish, 0)


def expert_call(kernel, arrays, outs, scratch, dp, collective_id, name, flops):
    sems = [pltpu.SemaphoreType.DMA((dp,))] * 4
    return pl.pallas_call(
        kernel,
        out_shape=[jax.ShapeDtypeStruct(shape, dtype) for shape, dtype in outs],
        in_specs=[pl.BlockSpec(memory_space=pltpu.VMEM)] * len(arrays),
        out_specs=[pl.BlockSpec(memory_space=pltpu.VMEM)] * len(outs),
        scratch_shapes=scratch + sems,
        compiler_params=pltpu.CompilerParams(
            vmem_limit_bytes=56 * MIB, collective_id=collective_id, has_side_effects=True
        ),
        cost_estimate=pl.CostEstimate(flops=flops, bytes_accessed=20 * MIB, transcendentals=0),
        name=name,
    )(*arrays)


def by_windows(grid):
    images, kinds = grid.shape[:2]
    blocks = GRID // WINDOW
    grid = grid.reshape(images, kinds, blocks, WINDOW, blocks, WINDOW).transpose(0, 1, 2, 4, 3, 5)
    grid = grid.reshape(images, kinds, blocks * blocks, WINPOS)
    grid = jnp.pad(grid, ((0, 0), (0, 0), (0, 0), (0, WPAD - WINPOS)), constant_values=-1)
    return grid.reshape(images, kinds, IMGROWS)


def per_device(
    patches,
    qkv_weight,
    proj_weight,
    core_up,
    core_down,
    residual_up,
    residual_down,
    position_bias,
    router_weight,
    norm_gain,
    norm_bias,
    cotangent,
    image_valid,
    expert_index,
    slot_index,
    region_id,
):
    dp, mp = lax.axis_size("dp"), lax.axis_size("mp")
    images, _, width = patches.shape
    split = dp // EXPERTS
    hidden = residual_up.shape[-1]
    hidden_full = core_up.shape[-1] * mp
    row_index = lax.axis_index("mp")

    gathered = []
    for l in range(LAYERS):
        gathered.append(
            tuple(
                lax.all_gather(a[l], "mp", axis=0, tiled=False)
                for a in (qkv_weight, proj_weight, core_up, core_down)
            )
        )

    position = jnp.where(slot_index >= 0, expert_index * SLOTS + slot_index, -1)
    labels = jnp.roll(region_id, (-SHIFT, -SHIFT), (1, 2))
    row_form = by_windows(jnp.stack([position.reshape(images, GRID, GRID), labels], 1))
    col_form = row_form.transpose(0, 2, 1)
    enter = jnp.asarray(enter_table(), bf16)
    leave = jnp.asarray(enter_table().T, bf16)
    moves = [jnp.asarray(move_table(l % 2 == 1), bf16) for l in range(LAYERS)]
    backs = [jnp.asarray(move_table(l % 2 == 1).T, bf16) for l in range(LAYERS)]
    entries = jnp.asarray(offset_index().reshape(-1))
    entry_hot = (jnp.arange(OFFSETS + 1)[:, None] == entries[None, :]).astype(f32)
    table_rows = position_bias.transpose(0, 2, 1).reshape(LAYERS * HEADS, OFFSETS)
    padded_rows = jnp.pad(table_rows, ((0, 0), (0, 1)), constant_values=-1e30)
    biases = jnp.dot(padded_rows, entry_hot, precision=highest).reshape(LAYERS, HEADS, WPAD, LANES)
    routers = jnp.pad(router_weight, ((0, 0), (0, 0), (0, LANES - EXPERTS)))

    token = (images, IMGROWS, width)
    buffer_shape = (ROWS, width)
    block_rows = (dp, SLOTS, width)
    pieces = (split, ROWS, width)

    def by_piece(returned):
        return returned.reshape(EXPERTS, split, SLOTS, width).transpose(1, 0, 2, 3).reshape(pieces)

    records = []
    before = None
    for l in range(LAYERS):
        first = l == 0
        if first:
            arrays = [("image", patches), ("whole", enter)]
        else:
            arrays = [("image", before[0]), ("image", before[1]), ("whole", before[2])]
        arrays += [
            ("smem", image_valid),
            ("image", col_form),
            ("image", row_form),
            ("whole", gathered[l][0]),
            ("whole", gathered[l][1]),
            ("whole", biases[l]),
            ("whole", moves[l]),
            ("whole", backs[l]),
            ("whole", norm_gain[l]),
            ("whole", norm_bias[l]),
            ("whole", routers[l]),
        ]
        outs = [("image", token, f32)]
        if not first:
            outs.append(("image", token, f32))
        outs += [
            ("image", token, f32),
            ("image", token, bf16),
            ("image", (images, IMGROWS, 1), f32),
            ("whole", buffer_shape, bf16),
            ("image", token, bf16),
            ("image", (images, 2 * width, IMGROWS), bf16),
            ("image", token, bf16),
            ("image", (images, PAIRS * HEADS, WPAD, LANES), bf16),
            ("image", (images, width, IMGROWS), bf16),
            ("whole", (width, 3 * width), bf16),
            ("whole", (width, width), bf16),
        ]
        scratch = [pltpu.VMEM((3 * width, width), bf16), pltpu.VMEM(buffer_shape, f32)]
        results = list(
            image_call(
                functools.partial(attention_forward_kernel, first, l % 2 == 1, mp),
                images, arrays, outs, scratch, f"attend_{l}",
            )
        )
        carried = results.pop(0)
        if not first:
            records[-1]["expert_out"] = results.pop(0)
        middle, second_low, gate, buffer = results[:4]
        received, returned, up_eff, down_eff = expert_call(
            functools.partial(expert_forward_kernel, dp, mp),
            [
                buffer.reshape(EXPERTS, SLOTS, width),
                gathered[l][2],
                gathered[l][3],
                residual_up[l, 0],
                residual_down[l, 0],
            ],
            [
                (block_rows, bf16),
                (block_rows, bf16),
                ((width, hidden), bf16),
                ((hidden, width), bf16),
            ],
            [pltpu.VMEM(block_rows, bf16), pltpu.VMEM((width, hidden), f32)],
            dp, l, f"experts_{l}", 4 * dp * SLOTS * width * hidden,
        )
        returned = by_piece(returned)
        before = (middle, gate, returned)
        records.append(
            dict(
                carried=carried, middle=middle, second_low=second_low, gate=gate, saved=results[4:], received=received,
                up_eff=up_eff, down_eff=down_eff,
            )
        )

    top = records[-1]
    block_output, grad, logit_grad, router_part, buffer = image_call(
        turn_kernel,
        images,
        [
            ("image", before[0]),
            ("image", before[1]),
            ("whole", before[2]),
            ("image", cotangent),
            ("whole", enter),
            ("whole", leave),
            ("image", col_form),
            ("image", row_form),
            ("image", top["second_low"]),
            ("whole", routers[LAYERS - 1]),
        ],
        [
            ("image", patches.shape, bf16),
            ("image", token, f32),
            ("image", (images, IMGROWS, LANES), f32),
            ("whole", (LANES, width), f32),
            ("whole", buffer_shape, bf16),
        ],
        [pltpu.VMEM(buffer_shape, f32)],
        "turn",
    )
    router_parts, tables, smalls = [None] * LAYERS, [None] * LAYERS, [None] * LAYERS
    residual_sums, shard_sums = [None] * LAYERS, [None] * LAYERS
    router_parts[LAYERS - 1] = router_part
    for l in reversed(range(LAYERS)):
        rec = records[l]
        last = l == 0
        returned_grad, up_term, down_term = expert_call(
            functools.partial(expert_backward_kernel, dp),
            [buffer.reshape(EXPERTS, SLOTS, width), rec["received"], rec["up_eff"], rec["down_eff"]],
            [(block_rows, bf16), ((width, hidden), f32), ((width, hidden), f32)],
            [
                pltpu.VMEM(block_rows, bf16),
                pltpu.VMEM((dp, SLOTS, hidden), bf16),
                pltpu.VMEM((dp, SLOTS, hidden), f32),
                pltpu.VMEM((dp, SLOTS, hidden), bf16),
                pltpu.VMEM(block_rows, bf16),
            ],
            dp, LAYERS + l, f"experts_back_{l}", 10 * dp * SLOTS * width * hidden,
        )
        residual_sums[l] = lax.psum((up_term.astype(bf16), down_term.astype(bf16)), "mp")
        window_in, qk, v, probs, att, qkv_full, proj_full = rec["saved"]
        arrays = [
            ("smem", image_valid),
            ("image", grad),
            ("whole", by_piece(returned_grad)),
            ("image", logit_grad),
            ("image", rec["middle"]),
            ("image", rec["carried"]),
            ("whole", routers[l]),
            ("image", col_form),
            ("whole", moves[l]),
            ("whole", backs[l]),
            ("whole", norm_gain[l]),
            ("whole", proj_full),
            ("whole", qkv_full),
            ("image", window_in),
            ("image", qk),
            ("image", v),
            ("image", probs),
            ("image", att),
        ]
        outs = [
            ("image", patches.shape if last else token, f32),
            ("whole", (3 * width, width), f32),
            ("whole", (width, width), f32),
            ("whole", (HEADS, WPAD, LANES), f32),
            ("whole", (8, width), f32),
        ]
        scratch = [pltpu.VMEM((3 * width, IMGROWS), bf16)]
        if last:
            arrays.append(("whole", leave))
        else:
            below = records[l - 1]
            arrays += [
                ("image", row_form),
                ("image", below["expert_out"]),
                ("image", below["second_low"]),
                ("whole", routers[l - 1]),
            ]
            outs += [
                ("image", (images, IMGROWS, LANES), f32),
                ("whole", (LANES, width), f32),
                ("whole", buffer_shape, bf16),
            ]
            scratch.append(pltpu.VMEM(buffer_shape, f32))
        results = image_call(
            functools.partial(attention_backward_kernel, last), images, arrays, outs, scratch, f"attend_back_{l}"
        )
        grad, qkv_part, proj_part, tables[l], smalls[l] = results[:5]
        if not last:
            logit_grad, router_parts[l - 1], buffer = results[5:]
        attn = (
            lax.psum_scatter(qkv_part.astype(bf16), "mp", scatter_dimension=0, tiled=True),
            lax.psum_scatter(proj_part.T.astype(bf16), "mp", scatter_dimension=0, tiled=True),
        )
        up_sum, down_sum = residual_sums[l]
        if split > 1:
            begin = lax.axis_index("dp") % split * hidden
            empty = jnp.zeros((width, hidden_full), bf16)
            up_sum = lax.dynamic_update_slice_in_dim(empty, up_sum, begin, 1)
            down_sum = lax.dynamic_update_slice_in_dim(empty, down_sum, begin, 1)
        up_columns, down_columns = core_up.shape[-1], core_down.shape[-1]
        up_shard = lax.dynamic_slice_in_dim(up_sum, row_index * up_columns, up_columns, 1)
        down_shard = lax.dynamic_slice_in_dim(down_sum, row_index * down_columns, down_columns, 0)
        shard_sums[l] = lax.psum((attn[0], attn[1], up_shard, down_shard), "dp")

    entry_turned = (entries[:, None] == jnp.arange(OFFSETS)[None, :]).astype(f32)
    table_part = jnp.dot(
        jnp.stack(tables, 0).reshape(LAYERS * HEADS, WPAD * LANES), entry_turned, precision=highest
    )
    small_part = jnp.stack(smalls, 0)[:, :4]
    router_part = jnp.stack(router_parts, 0)[:, :EXPERTS]
    table_sum, small_sum, router_sum = lax.psum((table_part, small_part, router_part), ("dp", "mp"))

    def shard(k):
        return jnp.stack([shard_sums[l][k] for l in range(LAYERS)], 0).astype(f32)

    return (
        block_output,
        grad,
        shard(0).transpose(0, 2, 1),
        shard(1).transpose(0, 2, 1),
        shard(2),
        shard(3).transpose(0, 2, 1),
        jnp.stack([residual_sums[l][0] for l in range(LAYERS)], 0).astype(f32)[:, None],
        jnp.stack([residual_sums[l][1] for l in range(LAYERS)], 0).astype(f32).transpose(0, 2, 1)[:, None],
        table_sum.reshape(LAYERS, HEADS, OFFSETS).transpose(0, 2, 1),
        router_sum.transpose(0, 2, 1),
        small_sum[:, 0:2],
        small_sum[:, 2:4],
    )


def solution(mesh):
    placed = (
        P(("dp", "mp"), None, None),
        P(None, None, "mp"),
        P(None, None, "mp"),
        P(None, None, "mp"),
        P(None, None, "mp"),
        P(None, "dp", None, None),
        P(None, "dp", None, None),
        P(),
        P(),
        P(),
        P(),
        P(("dp", "mp"), None, None),
        P(("dp", "mp")),
        P(("dp", "mp"), None),
        P(("dp", "mp"), None),
        P(("dp", "mp"), None, None),
    )
    return jax.shard_map(
        per_device,
        mesh=mesh,
        in_specs=placed,
        out_specs=(
            P(("dp", "mp"), None, None),
            P(("dp", "mp"), None, None),
            P(None, None, "mp"),
            P(None, None, "mp"),
            P(None, None, "mp"),
            P(None, None, "mp"),
            P(None, "dp", None, None),
            P(None, "dp", None, None),
            P(),
            P(),
            P(),
            P(),
        ),
        check_vma=False,
    )
```

```python
import functools

import jax
import jax.numpy as jnp
import numpy as np
from jax import lax
from jax.experimental import pallas as pl
from jax.experimental.pallas import tpu as pltpu
from jax.sharding import PartitionSpec as P

HEADS = 12
HEAD_DIM = 32
EXPERTS = 8
WINDOW = 7
GRID = 14
SHIFT = 3
LAYERS = 2
WINPOS = 49
OFFSETS = 169
CAP = 122

WPAD = 64
IMGROWS = 256
PATCHES = 196
SLOTS = 128
ROWS = EXPERTS * SLOTS
LANES = 128
GROUP = 4
PAIRS = 2

bf16 = jnp.bfloat16
f32 = jnp.float32
highest = lax.Precision.HIGHEST
norm_epsilon = 1e-05
mask_fill = -100.0
head_scale = HEAD_DIM ** (-0.5)
MESH = pl.DeviceIdType.MESH
MIB = 1024 * 1024


def nn(a, b):
    return lax.dot_general(a, b, (((1,), (0,)), ((), ())), preferred_element_type=f32)


def nt(a, b):
    return lax.dot_general(a, b, (((1,), (1,)), ((), ())), preferred_element_type=f32)


def tn(a, b):
    return lax.dot_general(a, b, (((0,), (0,)), ((), ())), preferred_element_type=f32)


def iota(shape, dim):
    return lax.broadcasted_iota(jnp.int32, shape, dim)


def onehot(flags):
    return jnp.where(flags, 1.0, 0.0).astype(bf16)


def natural_of_row(shifted):
    moved = SHIFT if shifted else 0
    blocks = GRID // WINDOW
    out = -np.ones(IMGROWS, np.int32)
    for window in range(blocks * blocks):
        for cell in range(WINPOS):
            row = (window // blocks * WINDOW + cell // WINDOW + moved) % GRID
            col = (window % blocks * WINDOW + cell % WINDOW + moved) % GRID
            out[window * WPAD + cell] = row * GRID + col
    return out


def enter_table():
    held = natural_of_row(False)
    return (held[:, None] == np.arange(PATCHES)[None, :]).astype(np.float32)


def move_table(shifted):
    first, second = natural_of_row(False), natural_of_row(shifted)
    same = (second[:, None] == first[None, :]) & (second[:, None] >= 0)
    return same.astype(np.float32)


def offset_index():
    key = np.arange(WPAD)[:, None]
    query = np.arange(LANES)[None, :] % WPAD
    entry = (
        (query // WINDOW - key // WINDOW + WINDOW - 1) * (2 * WINDOW - 1)
        + query % WINDOW
        - key % WINDOW
        + WINDOW
        - 1
    )
    real = (key < WINPOS) & (query < WINPOS)
    return np.where(real, entry, np.where(key < WINPOS, -1, OFFSETS)).astype(np.int32)


def norm_parts(x):
    width = x.shape[-1]
    center = x - jnp.sum(x, -1, keepdims=True) * (1.0 / width)
    spread = jnp.sum(center * center, -1, keepdims=True) * (1.0 / width)
    rstd = lax.rsqrt(spread + norm_epsilon)
    return center * rstd, rstd


def norm_back(grad, gain, xhat, rstd):
    width = xhat.shape[-1]
    dxhat = grad * gain
    mean_one = jnp.sum(dxhat, -1, keepdims=True) * (1.0 / width)
    mean_two = jnp.sum(dxhat * xhat, -1, keepdims=True) * (1.0 / width)
    return rstd * (dxhat - mean_one - xhat * mean_two)


def split_two(x):
    high = x.astype(bf16)
    return high, (x - high.astype(f32)).astype(bf16)


def collect(pos_col, returned_ref):
    pick = onehot(pos_col == iota((IMGROWS, ROWS), 1))
    out = nn(pick, returned_ref[0])
    for piece in range(1, returned_ref.shape[0]):
        out = out + nn(pick, returned_ref[piece])
    return out


def spread_rows(pos_row, rows_low):
    return nn(onehot(iota((ROWS, IMGROWS), 0) == pos_row), rows_low)


def route(second_low, router, pos_col):
    logits = nn(second_low, router)
    lane = iota(logits.shape, 1)
    logits = jnp.where(lane < EXPERTS, logits, -1e30)
    expo = jnp.exp(logits - jnp.max(logits, -1, keepdims=True))
    probs = expo / jnp.sum(expo, -1, keepdims=True)
    expert = jnp.where(pos_col >= 0, pos_col // SLOTS, -1)
    chosen = jnp.where(lane == expert, 1.0, 0.0)
    return probs, chosen, jnp.sum(probs * chosen, -1, keepdims=True)


def head_masks():
    rows = iota((LANES, LANES), 0) // HEAD_DIM
    return [onehot(rows == h) for h in range(GROUP)]


def lane_masks():
    lane = iota((WPAD, LANES), 1)
    return [onehot(lane < WPAD), onehot(lane >= WPAD)]


def place_columns(target, shards_ref, count, transposed):
    size = shards_ref.shape[-1]
    target[...] = jnp.zeros(target.shape, target.dtype)
    for m in range(count):
        start = m * size // LANES * LANES
        stop = -(-(m + 1) * size // LANES) * LANES
        span = stop - start
        if transposed:
            put = onehot(iota((span, size), 0) + start == iota((span, size), 1) + m * size)
            target[start:stop, :] += nt(put, shards_ref[m]).astype(bf16)
        else:
            put = onehot(iota((size, span), 0) + m * size == iota((size, span), 1) + start)
            target[:, start:stop] += nn(shards_ref[m], put).astype(bf16)


def attention_forward_kernel(first, shifted, mp, *refs):
    refs = list(refs)
    if first:
        patches_ref, enter_ref = refs[:2]
        refs = refs[2:]
    else:
        prev_ref, prev_gate_ref, returned_ref = refs[:3]
        refs = refs[3:]
    (
        valid_ref, col_ref, row_ref, qkv_ref, proj_ref, bias_ref, move_ref, back_ref, gain_ref, nbias_ref, router_ref,
    ) = refs[:11]
    refs = refs[11:]
    carried_ref = refs.pop(0)
    expert_out_ref = None if first else refs.pop(0)
    (
        middle_ref, second_ref, gate_ref, buffer_ref, window_ref, qk_ref, v_ref, probs_ref, att_ref, qkv_full, proj_full,
        qkv_turned, total_ref,
    ) = refs
    image = pl.program_id(0)
    width = carried_ref.shape[-1]

    @pl.when(image == 0)
    def _():
        place_columns(qkv_full, qkv_ref, mp, False)
        place_columns(qkv_turned, qkv_ref, mp, True)
        place_columns(proj_full, proj_ref, mp, False)
        total_ref[...] = jnp.zeros(total_ref.shape, f32)

    pos_col = col_ref[0, :, 0:1]
    pos_row = row_ref[0, 0:1, :]
    if first:
        x = nn(enter_ref[...], patches_ref[0])
    else:
        expert_out = collect(pos_col, returned_ref)
        expert_out_ref[0] = expert_out
        x = prev_ref[0] + prev_gate_ref[0] * expert_out
    carried_ref[0] = x
    xhat, _ = norm_parts(x)
    normed = (xhat * gain_ref[0:1, :] + nbias_ref[0:1, :]).astype(bf16)
    window_in = nn(move_ref[...], normed).astype(bf16)
    window_ref[0] = window_in
    turned = nt(qkv_turned[...], window_in).astype(bf16)
    straight = nn(window_in, qkv_full[:, width:]).astype(bf16)
    qk_ref[0] = turned[: 2 * width]
    v_ref[0] = straight[:, width:]
    heads_rows = head_masks()
    halves = lane_masks()
    low_lane = iota((WPAD, LANES), 1) < WPAD
    for pair in range(PAIRS):
        across = slice(pair * LANES, (pair + 1) * LANES)
        if shifted:
            ahead = col_ref[0, pair * LANES : pair * LANES + WPAD, 1:2]
            behind = col_ref[0, pair * LANES + WPAD : (pair + 1) * LANES, 1:2]
            key_label = jnp.where(low_lane, ahead, behind)
            mask = jnp.where(key_label == row_ref[0, 1:2, across], 0.0, mask_fill)
        for group in range(HEADS // GROUP):
            features = slice(group * LANES, (group + 1) * LANES)
            queries = turned[features, across]
            spread = jnp.concatenate([queries * heads_rows[h] for h in range(GROUP)], 1)
            raw = nn(straight[across, features], spread)
            for h in range(GROUP):
                head = group * GROUP + h
                part = raw[:, h * LANES : (h + 1) * LANES]
                scores = jnp.where(low_lane, part[:WPAD], part[WPAD:]) * head_scale + bias_ref[head]
                if shifted:
                    scores = scores + mask
                expo = jnp.exp(scores - jnp.max(scores, 0, keepdims=True))
                probs = (expo * (1.0 / jnp.sum(expo, 0, keepdims=True))).astype(bf16)
                probs_ref[0, pair * HEADS + head] = probs
                both = jnp.concatenate([probs * halves[0], probs * halves[1]], 0)
                at = slice(head * HEAD_DIM, (head + 1) * HEAD_DIM)
                values = turned[2 * width + head * HEAD_DIM : 2 * width + (head + 1) * HEAD_DIM, across]
                att_ref[0, at, across] = nn(values, both).astype(bf16)
    attended = nt(back_ref[...], att_ref[0]).astype(bf16)
    middle = x + valid_ref[image].astype(f32) * nn(attended, proj_full[...])
    middle_ref[0] = middle
    xhat, _ = norm_parts(middle)
    second_low = (xhat * gain_ref[1:2, :] + nbias_ref[1:2, :]).astype(bf16)
    second_ref[0] = second_low
    _, _, gate = route(second_low, router_ref[...], pos_col)
    gate_ref[0] = gate
    total_ref[...] += spread_rows(pos_row, second_low)

    @pl.when(image == pl.num_programs(0) - 1)
    def _():
        buffer_ref[...] = total_ref[...].astype(bf16)


def image_spec(array_shape):
    rest = tuple(array_shape[1:])
    zeros = (0,) * len(rest)
    return pl.BlockSpec((1,) + rest, lambda i: (i,) + zeros)


def whole_spec(array_shape):
    zeros = (0,) * len(array_shape)
    return pl.BlockSpec(tuple(array_shape), lambda i: zeros)


def image_call(kernel, images, arrays, outs, scratch, name):
    def spec(kind, shape):
        if kind == "smem":
            return pl.BlockSpec(memory_space=pltpu.SMEM)
        return image_spec(shape) if kind == "image" else whole_spec(shape)

    return pl.pallas_call(
        kernel,
        grid=(images,),
        out_shape=[jax.ShapeDtypeStruct(shape, dtype) for _, shape, dtype in outs],
        in_specs=[spec(kind, array.shape) for kind, array in arrays],
        out_specs=[spec(kind, shape) for kind, shape, _ in outs],
        scratch_shapes=scratch,
        compiler_params=pltpu.CompilerParams(
            vmem_limit_bytes=56 * MIB, dimension_semantics=("arbitrary",)
        ),
        name=name,
    )(*[array for _, array in arrays])


def send_part(g, expert_out, second_low, router, pos_col, pos_row, logit_ref, router_grad_ref, total_ref):
    probs, chosen, gate = route(second_low, router, pos_col)
    gate_grad = jnp.where(pos_col >= 0, jnp.sum(g * expert_out, -1, keepdims=True), 0.0)
    sent = (gate * g).astype(bf16)
    logit_grad = gate_grad * gate * (chosen - probs)
    logit_ref[0] = logit_grad
    high, low = split_two(logit_grad)
    router_grad_ref[...] += tn(high, second_low) + tn(low, second_low)
    total_ref[...] += spread_rows(pos_row, sent)


def turn_kernel(
    prev_ref, gate_ref, returned_ref, cotangent_ref, enter_ref, leave_ref, col_ref, row_ref, second_ref, router_ref,
    block_ref, grad_ref, logit_ref, router_grad_ref, buffer_ref, total_ref,
):
    image = pl.program_id(0)

    @pl.when(image == 0)
    def _():
        total_ref[...] = jnp.zeros(total_ref.shape, f32)
        router_grad_ref[...] = jnp.zeros(router_grad_ref.shape, f32)

    pos_col = col_ref[0, :, 0:1]
    expert_out = collect(pos_col, returned_ref)
    x = prev_ref[0] + gate_ref[0] * expert_out
    block_ref[0] = nn(leave_ref[...], x.astype(bf16)).astype(bf16)
    g = nn(enter_ref[...], cotangent_ref[0])
    grad_ref[0] = g
    send_part(
        g, expert_out, second_ref[0], router_ref[...], pos_col, row_ref[0, 0:1, :], logit_ref, router_grad_ref, total_ref
    )

    @pl.when(image == pl.num_programs(0) - 1)
    def _():
        buffer_ref[...] = total_ref[...].astype(bf16)


def attention_backward_kernel(last, mp, fast, *refs):
    (
        valid_ref, grad_ref, returned_ref, logit_ref, middle_ref, carried_ref, router_ref, col_ref, move_ref, back_ref,
        gain_ref, proj_ref, qkv_ref, window_ref, qk_ref, v_ref, probs_ref, att_ref,
    ) = refs[:18]
    refs = refs[18:]
    refs = list(refs)
    if last:
        leave_ref = refs.pop(0)
    else:
        row_ref, expert_out_ref, second_ref, router_next_ref = refs[:4]
        refs = refs[4:]
    out_ref = refs.pop(0)
    if fast:
        unit_ref = refs.pop(0)
    else:
        qkv_grad_ref, proj_grad_ref = refs[:2]
        refs = refs[2:]
    table_ref, small_ref = refs[:2]
    refs = refs[2:]
    if not last:
        logit_out_ref, router_grad_ref, buffer_ref = refs[:3]
        refs = refs[3:]
    turned = refs.pop(0)
    if fast:
        qkv_grad_ref, proj_grad_ref = refs[:2]
        refs = refs[2:]
    if not last:
        total_ref = refs.pop(0)
    image = pl.program_id(0)
    width = carried_ref.shape[-1]

    @pl.when(image == 0)
    def _():
        qkv_grad_ref[...] = jnp.zeros(qkv_grad_ref.shape, f32)
        proj_grad_ref[...] = jnp.zeros(proj_grad_ref.shape, f32)
        table_ref[...] = jnp.zeros(table_ref.shape, f32)
        small_ref[...] = jnp.zeros(small_ref.shape, f32)
        if not last:
            total_ref[...] = jnp.zeros(total_ref.shape, f32)
            router_grad_ref[...] = jnp.zeros(router_grad_ref.shape, f32)

    pos_col = col_ref[0, :, 0:1]
    g = grad_ref[0]
    high, low = split_two(logit_ref[0])
    router = router_ref[...]
    normed_grad = collect(pos_col, returned_ref) + nt(high, router) + nt(low, router)
    xhat, rstd = norm_parts(middle_ref[0])
    small_ref[1:2, :] += jnp.sum(normed_grad * xhat, 0, keepdims=True)
    small_ref[3:4, :] += jnp.sum(normed_grad, 0, keepdims=True)
    middle_grad = g + norm_back(normed_grad, gain_ref[1:2, :], xhat, rstd)
    branch_grad = (valid_ref[image].astype(f32) * middle_grad).astype(bf16)
    branch_grad = nn(move_ref[...], branch_grad).astype(bf16)
    proj_grad_ref[...] += nn(att_ref[0], branch_grad)
    att_grad = nt(proj_ref[...], branch_grad).astype(bf16)
    heads_rows = head_masks()
    halves = lane_masks()
    low_lane = iota((WPAD, LANES), 1) < WPAD
    for pair in range(PAIRS):
        across = slice(pair * LANES, (pair + 1) * LANES)
        for group in range(HEADS // GROUP):
            features = slice(group * LANES, (group + 1) * LANES)
            grads = att_grad[features, across]
            spread = jnp.concatenate([grads * heads_rows[h] for h in range(GROUP)], 1)
            raw = nn(v_ref[0, across, features], spread)
            for h in range(GROUP):
                head = group * GROUP + h
                at = slice(head * HEAD_DIM, (head + 1) * HEAD_DIM)
                below = slice(width + head * HEAD_DIM, width + (head + 1) * HEAD_DIM)
                lowest = slice(2 * width + head * HEAD_DIM, 2 * width + (head + 1) * HEAD_DIM)
                part = raw[:, h * LANES : (h + 1) * LANES]
                probs_grad = jnp.where(low_lane, part[:WPAD], part[WPAD:])
                probs_low = probs_ref[0, pair * HEADS + head]
                probs = probs_low.astype(f32)
                weighted = probs * probs_grad
                scores_grad = weighted - probs * jnp.sum(weighted, 0, keepdims=True)
                table_ref[head] += scores_grad
                scores_low = scores_grad.astype(bf16)
                both = jnp.concatenate([scores_low * halves[0], scores_low * halves[1]], 0)
                probs_both = jnp.concatenate([probs_low * halves[0], probs_low * halves[1]], 0)
                turned[at, across] = (nn(qk_ref[0, below, across], both) * head_scale).astype(bf16)
                turned[below, across] = (nt(qk_ref[0, at, across], both) * head_scale).astype(bf16)
                turned[lowest, across] = nt(att_grad[at, across], probs_both).astype(bf16)
    qkv_grad_ref[...] += nn(turned[...], window_ref[0])
    mixed_grad = nt(back_ref[...], turned[...]).astype(bf16)
    first_grad = nt(mixed_grad, qkv_ref[...])
    xhat, rstd = norm_parts(carried_ref[0])
    small_ref[0:1, :] += jnp.sum(first_grad * xhat, 0, keepdims=True)
    small_ref[2:3, :] += jnp.sum(first_grad, 0, keepdims=True)
    out = middle_grad + norm_back(first_grad, gain_ref[0:1, :], xhat, rstd)
    if fast:

        @pl.when(image == pl.num_programs(0) - 1)
        def _():
            columns, rows = 3 * width // mp, width // mp
            proj_turned = proj_grad_ref[...].T
            for place in range(mp):
                q = quarter_at(place, mp)
                unit_ref[place, :columns] = qkv_grad_ref[q * columns : (q + 1) * columns].astype(bf16)
                unit_ref[place, columns:] = proj_turned[q * rows : (q + 1) * rows].astype(bf16)

    if last:
        top = out.astype(bf16)
        rest = out - top.astype(f32)
        mid, low = split_two(rest)
        leave = leave_ref[...]
        out_ref[0] = nn(leave, top) + nn(leave, mid) + nn(leave, low)
        return
    out_ref[0] = out
    send_part(
        out, expert_out_ref[0], second_ref[0], router_next_ref[...], pos_col, row_ref[0, 0:1, :], logit_out_ref,
        router_grad_ref, total_ref,
    )

    @pl.when(image == pl.num_programs(0) - 1)
    def _():
        buffer_ref[...] = total_ref[...].astype(bf16)


def quarter_at(place, mp):
    return place % (mp // 2) * 2 + place // (mp // 2)


def add_up(*parts):
    total = parts[0].astype(f32)
    for part in parts[1:]:
        total = total + part.astype(f32)
    return total


def to_row(source, target, sems, k, row):
    return pltpu.make_async_remote_copy(
        src_ref=source,
        dst_ref=target,
        send_sem=sems[0].at[k],
        recv_sem=sems[1].at[k],
        device_id={"mp": row},
        device_id_type=MESH,
    )


class RowSum:
    def __init__(self, units, core_in, y_out, y_in, mine, full, sems):
        self.units, self.core_in, self.y_out, self.y_in = units, core_in, y_out, y_in
        self.mine, self.full, self.sems = mine, full, sems
        row = lax.axis_index("mp")
        self.core, self.y = lax.rem(row, 2), lax.div(row, 2)
        self.sibling, self.across = row + 1 - 2 * self.core, row + 2 - 4 * self.y
        self.place = self.core * 2 + self.y
        self.place_across = self.core * 2 + 1 - self.y

    def pair(self, k):
        return to_row(
            self.units[k].at[pl.ds(2 * (1 - self.core), 2)], self.core_in.at[k], self.sems[0], k, self.sibling
        )

    def cross(self, k):
        return to_row(self.y_out.at[k], self.y_in.at[k], self.sems[1], k, self.across)

    def back(self, k):
        return to_row(self.mine.at[k], self.full.at[k, self.place], self.sems[2], k, self.across)

    def near(self, k):
        return to_row(self.mine.at[k], self.full.at[k, self.place], self.sems[3], k, self.sibling)

    def pass_on(self, k):
        block = self.full.at[k, self.place_across]
        return to_row(block, block, self.sems[4], k, self.sibling)

    def start(self, k):
        self.pair(k).start()

    def middle(self, k):
        self.pair(k).wait_recv()
        other = 1 - self.y
        mixed = add_up(self.units[k][self.core * 2 + other], self.core_in[k, other])
        self.y_out[k] = mixed.astype(bf16)
        self.cross(k).start()

    def end(self, k, gather):
        self.cross(k).wait_recv()
        self.mine[k] = add_up(
            self.units[k][self.place], self.core_in[k, self.y], self.y_in[k]
        ).astype(bf16)
        if gather:
            self.back(k).start()
            self.near(k).start()
            self.full[k, self.place] = self.mine[k]

    def forward(self, k):
        self.back(k).wait_recv()
        self.pass_on(k).start()

    def finish(self, k, gather):
        self.pair(k).wait_send()
        self.cross(k).wait_send()
        if gather:
            self.back(k).wait_send()
            self.near(k).wait()
            self.pass_on(k).wait()

    @staticmethod
    def scratch(count, width):
        return [
            pltpu.VMEM((count, 2, width, width), bf16),
            pltpu.VMEM((count, width, width), bf16),
            pltpu.VMEM((count, width, width), bf16),
        ] + [pltpu.SemaphoreType.DMA((count,))] * 10


def closing_kernel(
    dp, mp, units_ref, attn_ref, small_ref, full_ref, shard_ref, small_out, core_in, y_out, y_in, a0, a1, b0, b1, c0, c1, d0,
    d1, e0, e1, mine, x_in, half, z_in, s_core, s_one, s_y, s_mine, s_x, s_half, s_z, s0, s1, s2, s3, x0, x1, z0, z1, w0, w1,
    v0, v1,
):
    me = lax.axis_index("dp")
    x, z = lax.rem(me, 2), lax.div(me, 2)
    deep = dp // 2
    partner = me + 1 - 2 * x
    rows = RowSum(
        [units_ref.at[0], units_ref.at[1], attn_ref], core_in, y_out, y_in, mine, full_ref,
        [(a0, a1), (b0, b1), (c0, c1), (d0, d1), (e0, e1)],
    )
    barrier = pltpu.get_barrier_semaphore()
    for row in (rows.sibling, rows.across):
        pl.semaphore_signal(barrier, inc=1, device_id={"mp": row}, device_id_type=MESH)
    pl.semaphore_signal(barrier, inc=1, device_id={"dp": partner}, device_id_type=MESH)
    for off in range(1, deep):
        peer = lax.rem(z + off, deep) * 2 + x
        pl.semaphore_signal(barrier, inc=1, device_id={"dp": peer}, device_id_type=MESH)
    pl.semaphore_wait(barrier, 3 + deep - 1)

    small = 3
    s_pair = to_row(small_ref, s_core, (s0, s1), 0, rows.sibling)
    s_cross = to_row(s_one, s_y, (s2, s3), 0, rows.across)
    order = range(4)
    total = [mine.at[k] for k in range(3)] + [s_mine]
    arrived = [x_in.at[k] for k in range(3)] + [s_x]
    halves = [half.at[k] for k in range(3)] + [s_half]
    slots = [z_in.at[k] for k in range(3)] + [s_z]
    result = [shard_ref.at[k] for k in range(3)] + [small_out]

    def cut(k):
        height = total[k].shape[0] // 2
        return height, height // deep

    def over_x(k):
        height, _ = cut(k)
        away = total[k].at[pl.ds(pl.multiple_of((1 - x) * height, height), height)]
        return to_peer(away, arrived[k], x0.at[k], x1.at[k], partner)

    def over_z(k, off):
        _, piece = cut(k)
        to = lax.rem(z + off, deep)
        part = halves[k].at[pl.ds(pl.multiple_of(to * piece, piece), piece)]
        return to_peer(part, slots[k].at[off], z0.at[k, off], z1.at[k, off], to * 2 + x)

    def own_piece(k):
        height, piece = cut(k)
        return result[k].at[pl.ds(pl.multiple_of(x * height + z * piece, piece), piece)]

    def own_half(k):
        height, _ = cut(k)
        return result[k].at[pl.ds(pl.multiple_of(x * height, height), height)]

    def back_z(k, off):
        to = lax.rem(z + off, deep)
        return to_peer(own_piece(k), own_piece(k), w0.at[k, off], w1.at[k, off], to * 2 + x)

    def back_x(k):
        return to_peer(own_half(k), own_half(k), v0.at[k], v1.at[k], partner)

    s_pair.start()
    for k in range(3):
        rows.start(k)
    for k in range(3):
        rows.middle(k)
    s_pair.wait_recv()
    s_one[...] = small_ref[...] + s_core[...]
    s_cross.start()
    for k in range(3):
        rows.end(k, k < 2)
        over_x(k).start()
    s_cross.wait_recv()
    s_mine[...] = s_one[...] + s_y[...]
    over_x(small).start()
    for k in order:
        over_x(k).wait_recv()
        height, _ = cut(k)
        keep = total[k][pl.ds(pl.multiple_of(x * height, height), height)]
        halves[k][...] = add_up(keep, arrived[k][...]).astype(halves[k].dtype)
        for off in range(1, deep):
            over_z(k, off).start()
    for k in order:
        for off in range(1, deep):
            over_z(k, off).wait_recv()
        _, piece = cut(k)
        keep = halves[k][pl.ds(pl.multiple_of(z * piece, piece), piece)]
        own_piece(k)[...] = add_up(keep, *[slots[k][off] for off in range(1, deep)]).astype(result[k].dtype)
        for off in range(1, deep):
            back_z(k, off).start()
    for k in range(2):
        rows.forward(k)
    for k in order:
        for off in range(1, deep):
            back_z(k, off).wait_recv()
        back_x(k).start()
    s_pair.wait_send()
    s_cross.wait_send()
    for k in range(3):
        rows.finish(k, k < 2)
    for k in order:
        over_x(k).wait_send()
        for off in range(1, deep):
            over_z(k, off).wait_send()
            back_z(k, off).wait_send()
        back_x(k).wait()


def closing_call(dp, mp, units, attn, small, collective_id):
    width = attn.shape[-1]
    deep = dp // 2
    lines = small.shape[0]
    dma = pltpu.SemaphoreType.DMA
    shape = jax.ShapeDtypeStruct
    scratch = RowSum.scratch(3, width) + [
        pltpu.VMEM((3, width, width), bf16),
        pltpu.VMEM((3, width // 2, width), bf16),
        pltpu.VMEM((3, width // 2, width), bf16),
        pltpu.VMEM((3, deep, width // dp, width), bf16),
        pltpu.VMEM((lines, width), f32),
        pltpu.VMEM((lines, width), f32),
        pltpu.VMEM((lines, width), f32),
        pltpu.VMEM((lines, width), f32),
        pltpu.VMEM((lines // 2, width), f32),
        pltpu.VMEM((lines // 2, width), f32),
        pltpu.VMEM((deep, lines // dp, width), f32),
        dma((1,)), dma((1,)), dma((1,)), dma((1,)),
        dma((4,)), dma((4,)), dma((4, deep)), dma((4, deep)), dma((4, deep)), dma((4, deep)), dma((4,)), dma((4,)),
    ]
    vmem = pl.BlockSpec(memory_space=pltpu.VMEM)
    return pl.pallas_call(
        functools.partial(closing_kernel, dp, mp),
        out_shape=[shape((2, mp, width, width), bf16), shape((3, width, width), bf16), shape(small.shape, f32)],
        in_specs=[vmem] * 3,
        out_specs=[vmem] * 3,
        scratch_shapes=scratch,
        compiler_params=pltpu.CompilerParams(
            vmem_limit_bytes=56 * MIB, collective_id=collective_id, has_side_effects=True
        ),
        name="closing",
    )(units, attn, small)


def residual_kernel(full_ref, up_ref, down_ref):
    mp, width = full_ref.shape[2], full_ref.shape[3]
    rows = width // mp
    for place in range(mp):
        q = quarter_at(place, mp)
        up_ref[0, 0, :, q * width : (q + 1) * width] = full_ref[0, 0, place].astype(f32)
    for chunk in range(up_ref.shape[-1] // width):
        block = [None] * mp
        for place in range(mp):
            block[quarter_at(place, mp)] = full_ref[0, 1, place, chunk * rows : (chunk + 1) * rows].astype(f32)
        down_ref[0, 0, chunk * width : (chunk + 1) * width, :] = jnp.concatenate(block, 0).T


def residual_call(fulls, hidden):
    layers, _, mp, width, _ = fulls.shape
    return pl.pallas_call(
        residual_kernel,
        grid=(layers,),
        out_shape=[
            jax.ShapeDtypeStruct((layers, 1, width, hidden), f32),
            jax.ShapeDtypeStruct((layers, 1, hidden, width), f32),
        ],
        in_specs=[pl.BlockSpec((1, 2, mp, width, width), lambda i: (i, 0, 0, 0, 0))],
        out_specs=[
            pl.BlockSpec((1, 1, width, hidden), lambda i: (i, 0, 0, 0)),
            pl.BlockSpec((1, 1, hidden, width), lambda i: (i, 0, 0, 0)),
        ],
        compiler_params=pltpu.CompilerParams(vmem_limit_bytes=40 * MIB),
        name="residuals",
    )(fulls)


def greet(dp, me, rows=()):
    barrier = pltpu.get_barrier_semaphore()
    for row in rows:
        pl.semaphore_signal(barrier, inc=1, device_id={"mp": row}, device_id_type=MESH)

    def signal(off, carry):
        pl.semaphore_signal(barrier, inc=1, device_id={"dp": lax.rem(me + off, dp)}, device_id_type=MESH)
        return carry

    lax.fori_loop(1, dp, signal, 0)
    pl.semaphore_wait(barrier, dp - 1 + len(rows))


def to_peer(source, target, send_sem, recv_sem, peer):
    return pltpu.make_async_remote_copy(
        src_ref=source,
        dst_ref=target,
        send_sem=send_sem,
        recv_sem=recv_sem,
        device_id={"dp": peer},
        device_id_type=MESH,
    )


def gelu_parts(h):
    root = np.float32(np.sqrt(2.0 / np.pi))
    square = h * h
    t = jnp.tanh(root * h * (1.0 + 0.044715 * square))
    half = 0.5 * (1.0 + t)
    slope = half + 0.5 * h * (1.0 - t * t) * root * (1.0 + 3 * 0.044715 * square)
    return h * half, slope


def expert_forward_kernel(
    dp, mp, buffer_ref, up_ref, down_ref, rup_ref, rdown_ref, recv_ref, returned_ref, up_eff, down_eff, part, core,
    send_one, recv_one, send_two, recv_two,
):
    split = dp // EXPERTS
    me = lax.axis_index("dp")
    greet(dp, me)

    def first(off):
        peer = lax.rem(me + off, dp)
        return to_peer(
            buffer_ref.at[lax.div(peer, split)], recv_ref.at[me], send_one.at[off], recv_one.at[off], peer
        )

    def second(off):
        source = lax.rem(me + dp - off, dp)
        return to_peer(part.at[source], returned_ref.at[me], send_two.at[off], recv_two.at[off], source)

    def start_first(off, carry):
        first(off).start()
        return carry

    lax.fori_loop(1, dp, start_first, 0)
    recv_ref[me] = buffer_ref[lax.div(me, split)]
    hidden = up_eff.shape[1]
    columns = up_ref.shape[-1]
    if split == 1 and columns % LANES == 0:
        for m in range(mp):
            at = slice(m * columns, (m + 1) * columns)
            up_eff[:, at] = (up_ref[m].astype(f32) + rup_ref[:, at].astype(f32)).astype(bf16)
    else:
        core[...] = rup_ref[...].astype(f32)
        begin = lax.rem(me, split) * hidden
        for m in range(mp):
            put = onehot(iota((columns, hidden), 0) + m * columns == iota((columns, hidden), 1) + begin)
            core[...] += nn(up_ref[m], put)
        up_eff[...] = core[...].astype(bf16)
    columns = down_ref.shape[-1]
    width = down_eff.shape[1]
    rows = pl.ds(pl.multiple_of(lax.rem(me, split) * hidden, LANES), hidden)
    total = rdown_ref[...].astype(f32)
    for m in range(mp):
        put = onehot(iota((columns, width), 0) + m * columns == iota((columns, width), 1))
        total = total + nn(down_ref[m, rows, :], put)
    down_eff[...] = total.astype(bf16)

    def work(source):
        hidden_pre = nn(recv_ref[source], up_eff[...])
        hidden_low = gelu_parts(hidden_pre)[0].astype(bf16)
        return nn(hidden_low, down_eff[...]).astype(bf16)

    returned_ref[me] = work(me)

    def step(off, carry):
        source = lax.rem(me + dp - off, dp)
        first(off).wait_recv()
        part[source] = work(source)
        second(off).start()
        return carry

    lax.fori_loop(1, dp, step, 0)

    def finish(off, carry):
        first(off).wait_send()
        second(off).wait()
        return carry

    lax.fori_loop(1, dp, finish, 0)


def expert_backward_kernel(dp, mp, fast, reduce, *refs):
    refs = list(refs)
    buffer_ref, recv_ref, up_ref, down_ref = refs[:4]
    refs = refs[4:]
    if reduce:
        above_ref, attn_ref = refs[:2]
        refs = refs[2:]
    returned_ref = refs.pop(0)
    if fast:
        units_ref = refs.pop(0)
    else:
        up_term, down_term = refs[:2]
        refs = refs[2:]
    if reduce:
        full_ref, mine_ref = refs[:2]
        refs = refs[2:]
    grads, hidden_low, slope, pre, part = refs[:5]
    refs = refs[5:]
    if fast:
        up_term, down_term = refs[:2]
        refs = refs[2:]
    rows = None
    if reduce:
        core_in, y_out, y_in = refs[:3]
        pairs = [(refs[3 + 2 * k], refs[4 + 2 * k]) for k in range(5)]
        refs = refs[13:]
        rows = RowSum([above_ref.at[0], above_ref.at[1], attn_ref], core_in, y_out, y_in, mine_ref, full_ref, pairs)
    send_one, recv_one, send_two, recv_two = refs
    split = dp // EXPERTS
    me = lax.axis_index("dp")
    greet(dp, me, (rows.sibling, rows.across) if reduce else ())

    def first(off):
        peer = lax.rem(me + off, dp)
        return to_peer(buffer_ref.at[lax.div(peer, split)], grads.at[me], send_one.at[off], recv_one.at[off], peer)

    def second(off):
        source = lax.rem(me + dp - off, dp)
        return to_peer(part.at[source], returned_ref.at[me], send_two.at[off], recv_two.at[off], source)

    def start_first(off, carry):
        first(off).start()
        return carry

    lax.fori_loop(1, dp, start_first, 0)
    if reduce:
        for k in range(3):
            rows.start(k)
    grads[me] = buffer_ref[lax.div(me, split)]

    def again(source, carry):
        value, rate = gelu_parts(nn(recv_ref[source], up_ref[...]))
        hidden_low[source] = value.astype(bf16)
        slope[source] = rate
        return carry

    if reduce:
        lax.fori_loop(0, dp // 2, again, 0)
        for k in range(3):
            rows.middle(k)
        lax.fori_loop(dp // 2, dp, again, 0)
    else:
        lax.fori_loop(0, dp, again, 0)

    def work(source):
        hidden_grad = nt(grads[source], down_ref[...])
        pre_grad = (slope[source] * hidden_grad).astype(bf16)
        pre[source] = pre_grad
        return nt(pre_grad, up_ref[...]).astype(bf16)

    returned_ref[me] = work(me)

    def step(off, carry):
        source = lax.rem(me + dp - off, dp)
        first(off).wait_recv()
        part[source] = work(source)
        second(off).start()
        return carry

    if reduce:
        lax.fori_loop(1, dp // 2, step, 0)
        for k in range(2):
            rows.end(k, True)
        lax.fori_loop(dp // 2, dp, step, 0)
        rows.end(2, False)
        for k in range(2):
            rows.forward(k)
    else:
        lax.fori_loop(1, dp, step, 0)
    up_term[...] = jnp.zeros(up_term.shape, f32)
    down_term[...] = jnp.zeros(down_term.shape, f32)

    def terms(block, carry):
        up_term[...] += tn(recv_ref[block], pre[block])
        down_term[...] += tn(grads[block], hidden_low[block])
        return carry

    lax.fori_loop(0, dp, terms, 0)
    if fast:
        width = up_term.shape[0]
        height = width // mp
        for place in range(mp):
            q = quarter_at(place, mp)
            units_ref[0, place] = up_term[:, q * width : (q + 1) * width].astype(bf16)
            for chunk in range(mp):
                block = down_term[q * height : (q + 1) * height, chunk * width : (chunk + 1) * width]
                units_ref[1, place, chunk * height : (chunk + 1) * height] = block.astype(bf16)

    def finish(off, carry):
        first(off).wait_send()
        second(off).wait()
        return carry

    lax.fori_loop(1, dp, finish, 0)
    if reduce:
        for k in range(3):
            rows.finish(k, k < 2)


def expert_call(kernel, arrays, outs, scratch, dp, collective_id, name, flops):
    sems = [pltpu.SemaphoreType.DMA((dp,))] * 4
    return pl.pallas_call(
        kernel,
        out_shape=[jax.ShapeDtypeStruct(shape, dtype) for shape, dtype in outs],
        in_specs=[pl.BlockSpec(memory_space=pltpu.VMEM)] * len(arrays),
        out_specs=[pl.BlockSpec(memory_space=pltpu.VMEM)] * len(outs),
        scratch_shapes=scratch + sems,
        compiler_params=pltpu.CompilerParams(
            vmem_limit_bytes=56 * MIB, collective_id=collective_id, has_side_effects=True
        ),
        cost_estimate=pl.CostEstimate(flops=flops, bytes_accessed=20 * MIB, transcendentals=0),
        name=name,
    )(*arrays)


def by_windows(grid):
    images, kinds = grid.shape[:2]
    blocks = GRID // WINDOW
    grid = grid.reshape(images, kinds, blocks, WINDOW, blocks, WINDOW).transpose(0, 1, 2, 4, 3, 5)
    grid = grid.reshape(images, kinds, blocks * blocks, WINPOS)
    grid = jnp.pad(grid, ((0, 0), (0, 0), (0, 0), (0, WPAD - WINPOS)), constant_values=-1)
    return grid.reshape(images, kinds, IMGROWS)


def per_device(
    patches,
    qkv_weight,
    proj_weight,
    core_up,
    core_down,
    residual_up,
    residual_down,
    position_bias,
    router_weight,
    norm_gain,
    norm_bias,
    cotangent,
    image_valid,
    expert_index,
    slot_index,
    region_id,
):
    dp, mp = lax.axis_size("dp"), lax.axis_size("mp")
    images, _, width = patches.shape
    split = dp // EXPERTS
    hidden = residual_up.shape[-1]
    hidden_full = core_up.shape[-1] * mp
    row_index = lax.axis_index("mp")

    gathered = []
    for l in range(LAYERS):
        gathered.append(
            tuple(
                lax.all_gather(a[l], "mp", axis=0, tiled=False)
                for a in (qkv_weight, proj_weight, core_up, core_down)
            )
        )

    position = jnp.where(slot_index >= 0, expert_index * SLOTS + slot_index, -1)
    labels = jnp.roll(region_id, (-SHIFT, -SHIFT), (1, 2))
    row_form = by_windows(jnp.stack([position.reshape(images, GRID, GRID), labels], 1))
    col_form = row_form.transpose(0, 2, 1)
    enter = jnp.asarray(enter_table(), bf16)
    leave = jnp.asarray(enter_table().T, bf16)
    moves = [jnp.asarray(move_table(l % 2 == 1), bf16) for l in range(LAYERS)]
    backs = [jnp.asarray(move_table(l % 2 == 1).T, bf16) for l in range(LAYERS)]
    entries = jnp.asarray(offset_index().reshape(-1))
    entry_hot = (jnp.arange(OFFSETS + 1)[:, None] == entries[None, :]).astype(f32)
    table_rows = position_bias.transpose(0, 2, 1).reshape(LAYERS * HEADS, OFFSETS)
    padded_rows = jnp.pad(table_rows, ((0, 0), (0, 1)), constant_values=-1e30)
    biases = jnp.dot(padded_rows, entry_hot, precision=highest).reshape(LAYERS, HEADS, WPAD, LANES)
    routers = jnp.pad(router_weight, ((0, 0), (0, 0), (0, LANES - EXPERTS)))

    token = (images, IMGROWS, width)
    buffer_shape = (ROWS, width)
    block_rows = (dp, SLOTS, width)
    pieces = (split, ROWS, width)

    def by_piece(returned):
        return returned.reshape(EXPERTS, split, SLOTS, width).transpose(1, 0, 2, 3).reshape(pieces)

    records = []
    before = None
    for l in range(LAYERS):
        first = l == 0
        if first:
            arrays = [("image", patches), ("whole", enter)]
        else:
            arrays = [("image", before[0]), ("image", before[1]), ("whole", before[2])]
        arrays += [
            ("smem", image_valid),
            ("image", col_form),
            ("image", row_form),
            ("whole", gathered[l][0]),
            ("whole", gathered[l][1]),
            ("whole", biases[l]),
            ("whole", moves[l]),
            ("whole", backs[l]),
            ("whole", norm_gain[l]),
            ("whole", norm_bias[l]),
            ("whole", routers[l]),
        ]
        outs = [("image", token, f32)]
        if not first:
            outs.append(("image", token, f32))
        outs += [
            ("image", token, f32),
            ("image", token, bf16),
            ("image", (images, IMGROWS, 1), f32),
            ("whole", buffer_shape, bf16),
            ("image", token, bf16),
            ("image", (images, 2 * width, IMGROWS), bf16),
            ("image", token, bf16),
            ("image", (images, PAIRS * HEADS, WPAD, LANES), bf16),
            ("image", (images, width, IMGROWS), bf16),
            ("whole", (width, 3 * width), bf16),
            ("whole", (width, width), bf16),
        ]
        scratch = [pltpu.VMEM((3 * width, width), bf16), pltpu.VMEM(buffer_shape, f32)]
        results = list(
            image_call(
                functools.partial(attention_forward_kernel, first, l % 2 == 1, mp),
                images, arrays, outs, scratch, f"attend_{l}",
            )
        )
        carried = results.pop(0)
        if not first:
            records[-1]["expert_out"] = results.pop(0)
        middle, second_low, gate, buffer = results[:4]
        received, returned, up_eff, down_eff = expert_call(
            functools.partial(expert_forward_kernel, dp, mp),
            [
                buffer.reshape(EXPERTS, SLOTS, width),
                gathered[l][2],
                gathered[l][3],
                residual_up[l, 0],
                residual_down[l, 0],
            ],
            [
                (block_rows, bf16),
                (block_rows, bf16),
                ((width, hidden), bf16),
                ((hidden, width), bf16),
            ],
            [pltpu.VMEM(block_rows, bf16), pltpu.VMEM((width, hidden), f32)],
            dp, l, f"experts_{l}", 4 * dp * SLOTS * width * hidden,
        )
        returned = by_piece(returned)
        before = (middle, gate, returned)
        records.append(
            dict(
                carried=carried, middle=middle, second_low=second_low, gate=gate, saved=results[4:], received=received,
                up_eff=up_eff, down_eff=down_eff,
            )
        )

    top = records[-1]
    block_output, grad, logit_grad, router_part, buffer = image_call(
        turn_kernel,
        images,
        [
            ("image", before[0]),
            ("image", before[1]),
            ("whole", before[2]),
            ("image", cotangent),
            ("whole", enter),
            ("whole", leave),
            ("image", col_form),
            ("image", row_form),
            ("image", top["second_low"]),
            ("whole", routers[LAYERS - 1]),
        ],
        [
            ("image", patches.shape, bf16),
            ("image", token, f32),
            ("image", (images, IMGROWS, LANES), f32),
            ("whole", (LANES, width), f32),
            ("whole", buffer_shape, bf16),
        ],
        [pltpu.VMEM(buffer_shape, f32)],
        "turn",
    )
    router_parts, tables, smalls = [None] * LAYERS, [None] * LAYERS, [None] * LAYERS
    residual_sums, shard_sums = [None] * LAYERS, [None] * LAYERS
    router_parts[LAYERS - 1] = router_part
    fast = split == 1 and dp == 8 and mp == 4 and hidden == mp * width
    units, attn_units = [None] * LAYERS, [None] * LAYERS
    for l in reversed(range(LAYERS)):
        rec = records[l]
        last = l == 0
        reduce = fast and l < LAYERS - 1
        arrays = [buffer.reshape(EXPERTS, SLOTS, width), rec["received"], rec["up_eff"], rec["down_eff"]]
        outs = [(block_rows, bf16)]
        scratch = [
            pltpu.VMEM(block_rows, bf16),
            pltpu.VMEM((dp, SLOTS, hidden), bf16),
            pltpu.VMEM((dp, SLOTS, hidden), f32),
            pltpu.VMEM((dp, SLOTS, hidden), bf16),
            pltpu.VMEM(block_rows, bf16),
        ]
        if fast:
            outs.append(((2, mp, width, width), bf16))
            scratch += [pltpu.VMEM((width, hidden), f32)] * 2
        else:
            outs += [((width, hidden), f32)] * 2
        if reduce:
            arrays += [units[l + 1], attn_units[l + 1]]
            outs += [((2, mp, width, width), bf16), ((3, width, width), bf16)]
            scratch += RowSum.scratch(3, width)
        results = list(
            expert_call(
                functools.partial(expert_backward_kernel, dp, mp, fast, reduce), arrays, outs, scratch, dp, LAYERS + l,
                f"experts_back_{l}", 10 * dp * SLOTS * width * hidden,
            )
        )
        returned_grad = results.pop(0)
        if fast:
            units[l] = results.pop(0)
        else:
            residual_sums[l] = lax.psum(tuple(t.astype(bf16) for t in results[:2]), "mp")
        if reduce:
            full_above, mine_above = results
            shard_above = lax.psum(mine_above, "dp")
        window_in, qk, v, probs, att, qkv_full, proj_full = rec["saved"]
        arrays = [
            ("smem", image_valid),
            ("image", grad),
            ("whole", by_piece(returned_grad)),
            ("image", logit_grad),
            ("image", rec["middle"]),
            ("image", rec["carried"]),
            ("whole", routers[l]),
            ("image", col_form),
            ("whole", moves[l]),
            ("whole", backs[l]),
            ("whole", norm_gain[l]),
            ("whole", proj_full),
            ("whole", qkv_full),
            ("image", window_in),
            ("image", qk),
            ("image", v),
            ("image", probs),
            ("image", att),
        ]
        outs = [("image", patches.shape if last else token, f32)]
        scratch = [pltpu.VMEM((3 * width, IMGROWS), bf16)]
        if fast:
            outs.append(("whole", (mp, width, width), bf16))
            scratch += [pltpu.VMEM((3 * width, width), f32), pltpu.VMEM((width, width), f32)]
        else:
            outs += [("whole", (3 * width, width), f32), ("whole", (width, width), f32)]
        outs += [("whole", (HEADS, WPAD, LANES), f32), ("whole", (8, width), f32)]
        if last:
            arrays.append(("whole", leave))
        else:
            below = records[l - 1]
            arrays += [
                ("image", row_form),
                ("image", below["expert_out"]),
                ("image", below["second_low"]),
                ("whole", routers[l - 1]),
            ]
            outs += [
                ("image", (images, IMGROWS, LANES), f32),
                ("whole", (LANES, width), f32),
                ("whole", buffer_shape, bf16),
            ]
            scratch.append(pltpu.VMEM(buffer_shape, f32))
        results = list(
            image_call(
                functools.partial(attention_backward_kernel, last, mp, fast),
                images, arrays, outs, scratch, f"attend_back_{l}",
            )
        )
        grad = results.pop(0)
        if fast:
            attn_units[l] = results.pop(0)
        else:
            qkv_part, proj_part = results[:2]
            results = results[2:]
        tables[l], smalls[l] = results[:2]
        if not last:
            logit_grad, router_parts[l - 1], buffer = results[2:]
        if fast:
            continue
        attn = (
            lax.psum_scatter(qkv_part.astype(bf16), "mp", scatter_dimension=0, tiled=True),
            lax.psum_scatter(proj_part.T.astype(bf16), "mp", scatter_dimension=0, tiled=True),
        )
        up_sum, down_sum = residual_sums[l]
        if split > 1:
            begin = lax.axis_index("dp") % split * hidden
            empty = jnp.zeros((width, hidden_full), bf16)
            up_sum = lax.dynamic_update_slice_in_dim(empty, up_sum, begin, 1)
            down_sum = lax.dynamic_update_slice_in_dim(empty, down_sum, begin, 1)
        up_columns, down_columns = core_up.shape[-1], core_down.shape[-1]
        up_shard = lax.dynamic_slice_in_dim(up_sum, row_index * up_columns, up_columns, 1)
        down_shard = lax.dynamic_slice_in_dim(down_sum, row_index * down_columns, down_columns, 0)
        shard_sums[l] = lax.psum((attn[0], attn[1], up_shard, down_shard), "dp")

    entry_turned = (entries[:, None] == jnp.arange(OFFSETS)[None, :]).astype(f32)
    table_part = jnp.dot(
        jnp.stack(tables, 0).reshape(LAYERS * HEADS, WPAD * LANES), entry_turned, precision=highest
    )
    small_part = jnp.stack(smalls, 0)[:, :4]
    router_part = jnp.stack(router_parts, 0)[:, :EXPERTS]
    if fast:
        lines = jnp.concatenate(
            [
                jnp.pad(table_part, ((0, 0), (0, width - OFFSETS))),
                router_part.reshape(-1, width),
                small_part.reshape(-1, width),
            ],
            0,
        )
        count = -(-lines.shape[0] // 64) * 64
        full, shards, lines = closing_call(
            dp, mp, units[0], attn_units[0], jnp.pad(lines, ((0, count - lines.shape[0]), (0, 0))), 2 * LAYERS
        )
        shards = jnp.stack([shards, shard_above], 0)
        residual_up_grad, residual_down_grad = residual_call(jnp.stack([full, full_above], 0), hidden)
        columns = qkv_weight.shape[-1]
        attn = shards[:, 2].astype(f32)
        at = LAYERS * HEADS
        table_sum = lines[:at, :OFFSETS]
        router_sum = lines[at : at + LAYERS * EXPERTS].reshape(LAYERS, EXPERTS, width)
        at += LAYERS * EXPERTS
        small_sum = lines[at : at + LAYERS * 4].reshape(LAYERS, 4, width)
        down = shards[:, 1].astype(f32).reshape(LAYERS, mp, width // mp, width).transpose(0, 1, 3, 2)
        attn_grads = (attn[:, :columns].transpose(0, 2, 1), attn[:, columns:].transpose(0, 2, 1))
        core_grads = (shards[:, 0].astype(f32), down.reshape(LAYERS, mp * width, width // mp))
    else:
        table_sum, small_sum, router_sum = lax.psum((table_part, small_part, router_part), ("dp", "mp"))

        def shard(k):
            return jnp.stack([shard_sums[l][k] for l in range(LAYERS)], 0).astype(f32)

        attn_grads = (shard(0).transpose(0, 2, 1), shard(1).transpose(0, 2, 1))
        core_grads = (shard(2), shard(3).transpose(0, 2, 1))
        residual_up_grad, residual_down_grad = (
            jnp.stack([residual_sums[l][k] for l in range(LAYERS)], 0).astype(f32) for k in range(2)
        )
        residual_up_grad = residual_up_grad[:, None]
        residual_down_grad = residual_down_grad.transpose(0, 2, 1)[:, None]

    return (
        block_output,
        grad,
        attn_grads[0],
        attn_grads[1],
        core_grads[0],
        core_grads[1],
        residual_up_grad,
        residual_down_grad,
        table_sum.reshape(LAYERS, HEADS, OFFSETS).transpose(0, 2, 1),
        router_sum.transpose(0, 2, 1),
        small_sum[:, 0:2],
        small_sum[:, 2:4],
    )


def solution(mesh):
    placed = (
        P(("dp", "mp"), None, None),
        P(None, None, "mp"),
        P(None, None, "mp"),
        P(None, None, "mp"),
        P(None, None, "mp"),
        P(None, "dp", None, None),
        P(None, "dp", None, None),
        P(),
        P(),
        P(),
        P(),
        P(("dp", "mp"), None, None),
        P(("dp", "mp")),
        P(("dp", "mp"), None),
        P(("dp", "mp"), None),
        P(("dp", "mp"), None, None),
    )
    return jax.shard_map(
        per_device,
        mesh=mesh,
        in_specs=placed,
        out_specs=(
            P(("dp", "mp"), None, None),
            P(("dp", "mp"), None, None),
            P(None, None, "mp"),
            P(None, None, "mp"),
            P(None, None, "mp"),
            P(None, None, "mp"),
            P(None, "dp", None, None),
            P(None, "dp", None, None),
            P(),
            P(),
            P(),
            P(),
        ),
        check_vma=False,
    )
```

```python
import functools

import jax
import jax.numpy as jnp
import numpy as np
from jax import lax
from jax.experimental import pallas as pl
from jax.experimental.pallas import tpu as pltpu
from jax.sharding import PartitionSpec as P

HEADS = 12
HEAD_DIM = 32
EXPERTS = 8
WINDOW = 7
GRID = 14
SHIFT = 3
LAYERS = 2
WINPOS = 49
OFFSETS = 169
CAP = 122

WPAD = 64
IMGROWS = 256
PATCHES = 196
SLOTS = 128
ROWS = EXPERTS * SLOTS
LANES = 128
GROUP = 4
PAIRS = 2

bf16 = jnp.bfloat16
f32 = jnp.float32
highest = lax.Precision.HIGHEST
norm_epsilon = 1e-05
mask_fill = -100.0
head_scale = HEAD_DIM ** (-0.5)
MESH = pl.DeviceIdType.MESH
MIB = 1024 * 1024


def nn(a, b):
    return lax.dot_general(a, b, (((1,), (0,)), ((), ())), preferred_element_type=f32)


def nt(a, b):
    return lax.dot_general(a, b, (((1,), (1,)), ((), ())), preferred_element_type=f32)


def tn(a, b):
    return lax.dot_general(a, b, (((0,), (0,)), ((), ())), preferred_element_type=f32)


def iota(shape, dim):
    return lax.broadcasted_iota(jnp.int32, shape, dim)


def onehot(flags):
    return jnp.where(flags, 1.0, 0.0).astype(bf16)


def natural_of_row(shifted):
    moved = SHIFT if shifted else 0
    blocks = GRID // WINDOW
    out = -np.ones(IMGROWS, np.int32)
    for window in range(blocks * blocks):
        for cell in range(WINPOS):
            row = (window // blocks * WINDOW + cell // WINDOW + moved) % GRID
            col = (window % blocks * WINDOW + cell % WINDOW + moved) % GRID
            out[window * WPAD + cell] = row * GRID + col
    return out


def enter_table():
    held = natural_of_row(False)
    return (held[:, None] == np.arange(PATCHES)[None, :]).astype(np.float32)


def move_table(shifted):
    first, second = natural_of_row(False), natural_of_row(shifted)
    same = (second[:, None] == first[None, :]) & (second[:, None] >= 0)
    return same.astype(np.float32)


def offset_index():
    key = np.arange(WPAD)[:, None]
    query = np.arange(LANES)[None, :] % WPAD
    entry = (
        (query // WINDOW - key // WINDOW + WINDOW - 1) * (2 * WINDOW - 1)
        + query % WINDOW
        - key % WINDOW
        + WINDOW
        - 1
    )
    real = (key < WINPOS) & (query < WINPOS)
    return np.where(real, entry, np.where(key < WINPOS, -1, OFFSETS)).astype(np.int32)


def norm_parts(x):
    width = x.shape[-1]
    center = x - jnp.sum(x, -1, keepdims=True) * (1.0 / width)
    spread = jnp.sum(center * center, -1, keepdims=True) * (1.0 / width)
    rstd = lax.rsqrt(spread + norm_epsilon)
    return center * rstd, rstd


def norm_back(grad, gain, xhat, rstd):
    width = xhat.shape[-1]
    dxhat = grad * gain
    mean_one = jnp.sum(dxhat, -1, keepdims=True) * (1.0 / width)
    mean_two = jnp.sum(dxhat * xhat, -1, keepdims=True) * (1.0 / width)
    return rstd * (dxhat - mean_one - xhat * mean_two)


def split_two(x):
    high = x.astype(bf16)
    return high, (x - high.astype(f32)).astype(bf16)


def collect(pos_col, returned_ref):
    pick = onehot(pos_col == iota((IMGROWS, ROWS), 1))
    out = nn(pick, returned_ref[0])
    for piece in range(1, returned_ref.shape[0]):
        out = out + nn(pick, returned_ref[piece])
    return out


def spread_rows(pos_row, rows_low):
    return nn(onehot(iota((ROWS, IMGROWS), 0) == pos_row), rows_low)


def route(second_low, router, pos_col):
    logits = nn(second_low, router)
    lane = iota(logits.shape, 1)
    logits = jnp.where(lane < EXPERTS, logits, -1e30)
    expo = jnp.exp(logits - jnp.max(logits, -1, keepdims=True))
    probs = expo / jnp.sum(expo, -1, keepdims=True)
    expert = jnp.where(pos_col >= 0, pos_col // SLOTS, -1)
    chosen = jnp.where(lane == expert, 1.0, 0.0)
    return probs, chosen, jnp.sum(probs * chosen, -1, keepdims=True)


def head_masks():
    rows = iota((LANES, LANES), 0) // HEAD_DIM
    return [onehot(rows == h) for h in range(GROUP)]


def lane_masks():
    lane = iota((WPAD, LANES), 1)
    return [onehot(lane < WPAD), onehot(lane >= WPAD)]


def place_columns(target, shards_ref, count, transposed):
    size = shards_ref.shape[-1]
    target[...] = jnp.zeros(target.shape, target.dtype)
    for m in range(count):
        start = m * size // LANES * LANES
        stop = -(-(m + 1) * size // LANES) * LANES
        span = stop - start
        if transposed:
            put = onehot(iota((span, size), 0) + start == iota((span, size), 1) + m * size)
            target[start:stop, :] += nt(put, shards_ref[m]).astype(bf16)
        else:
            put = onehot(iota((size, span), 0) + m * size == iota((size, span), 1) + start)
            target[:, start:stop] += nn(shards_ref[m], put).astype(bf16)


def attention_forward_kernel(first, shifted, mp, *refs):
    refs = list(refs)
    if first:
        patches_ref, enter_ref = refs[:2]
        refs = refs[2:]
    else:
        prev_ref, prev_gate_ref, returned_ref = refs[:3]
        refs = refs[3:]
    (
        valid_ref, col_ref, row_ref, qkv_ref, proj_ref, bias_ref, move_ref, back_ref, gain_ref, nbias_ref, router_ref,
    ) = refs[:11]
    refs = refs[11:]
    carried_ref = refs.pop(0)
    expert_out_ref = None if first else refs.pop(0)
    (
        middle_ref, second_ref, gate_ref, buffer_ref, window_ref, qk_ref, v_ref, probs_ref, att_ref, qkv_full, proj_full,
        qkv_turned, total_ref,
    ) = refs
    image = pl.program_id(0)
    width = carried_ref.shape[-1]

    @pl.when(image == 0)
    def _():
        place_columns(qkv_full, qkv_ref, mp, False)
        place_columns(qkv_turned, qkv_ref, mp, True)
        place_columns(proj_full, proj_ref, mp, False)
        total_ref[...] = jnp.zeros(total_ref.shape, f32)

    pos_col = col_ref[0, :, 0:1]
    pos_row = row_ref[0, 0:1, :]
    if first:
        x = nn(enter_ref[...], patches_ref[0])
    else:
        expert_out = collect(pos_col, returned_ref)
        expert_out_ref[0] = expert_out
        x = prev_ref[0] + prev_gate_ref[0] * expert_out
    carried_ref[0] = x
    xhat, _ = norm_parts(x)
    normed = (xhat * gain_ref[0:1, :] + nbias_ref[0:1, :]).astype(bf16)
    window_in = nn(move_ref[...], normed).astype(bf16)
    window_ref[0] = window_in
    turned = nt(qkv_turned[...], window_in).astype(bf16)
    straight = nn(window_in, qkv_full[:, width:]).astype(bf16)
    qk_ref[0] = turned[: 2 * width]
    v_ref[0] = straight[:, width:]
    heads_rows = head_masks()
    halves = lane_masks()
    low_lane = iota((WPAD, LANES), 1) < WPAD
    for pair in range(PAIRS):
        across = slice(pair * LANES, (pair + 1) * LANES)
        if shifted:
            ahead = col_ref[0, pair * LANES : pair * LANES + WPAD, 1:2]
            behind = col_ref[0, pair * LANES + WPAD : (pair + 1) * LANES, 1:2]
            key_label = jnp.where(low_lane, ahead, behind)
            mask = jnp.where(key_label == row_ref[0, 1:2, across], 0.0, mask_fill)
        for group in range(HEADS // GROUP):
            features = slice(group * LANES, (group + 1) * LANES)
            queries = turned[features, across]
            spread = jnp.concatenate([queries * heads_rows[h] for h in range(GROUP)], 1)
            raw = nn(straight[across, features], spread)
            for h in range(GROUP):
                head = group * GROUP + h
                part = raw[:, h * LANES : (h + 1) * LANES]
                scores = jnp.where(low_lane, part[:WPAD], part[WPAD:]) * head_scale + bias_ref[head]
                if shifted:
                    scores = scores + mask
                expo = jnp.exp(scores - jnp.max(scores, 0, keepdims=True))
                probs = (expo * (1.0 / jnp.sum(expo, 0, keepdims=True))).astype(bf16)
                probs_ref[0, pair * HEADS + head] = probs
                both = jnp.concatenate([probs * halves[0], probs * halves[1]], 0)
                at = slice(head * HEAD_DIM, (head + 1) * HEAD_DIM)
                values = turned[2 * width + head * HEAD_DIM : 2 * width + (head + 1) * HEAD_DIM, across]
                att_ref[0, at, across] = nn(values, both).astype(bf16)
    attended = nt(back_ref[...], att_ref[0]).astype(bf16)
    middle = x + valid_ref[image].astype(f32) * nn(attended, proj_full[...])
    middle_ref[0] = middle
    xhat, _ = norm_parts(middle)
    second_low = (xhat * gain_ref[1:2, :] + nbias_ref[1:2, :]).astype(bf16)
    second_ref[0] = second_low
    _, _, gate = route(second_low, router_ref[...], pos_col)
    gate_ref[0] = gate
    total_ref[...] += spread_rows(pos_row, second_low)

    @pl.when(image == pl.num_programs(0) - 1)
    def _():
        buffer_ref[...] = total_ref[...].astype(bf16)


def image_spec(array_shape):
    rest = tuple(array_shape[1:])
    zeros = (0,) * len(rest)
    return pl.BlockSpec((1,) + rest, lambda i: (i,) + zeros)


def whole_spec(array_shape):
    zeros = (0,) * len(array_shape)
    return pl.BlockSpec(tuple(array_shape), lambda i: zeros)


def image_call(kernel, images, arrays, outs, scratch, name, collective_id=None):
    def spec(kind, shape):
        if kind in ("smem", "any"):
            return pl.BlockSpec(memory_space=pltpu.SMEM if kind == "smem" else pl.ANY)
        return image_spec(shape) if kind == "image" else whole_spec(shape)

    return pl.pallas_call(
        kernel,
        grid=(images,),
        out_shape=[jax.ShapeDtypeStruct(shape, dtype) for _, shape, dtype in outs],
        in_specs=[spec(kind, array.shape) for kind, array in arrays],
        out_specs=[spec(kind, shape) for kind, shape, _ in outs],
        scratch_shapes=scratch,
        compiler_params=pltpu.CompilerParams(
            vmem_limit_bytes=56 * MIB,
            dimension_semantics=("arbitrary",),
            collective_id=collective_id,
            has_side_effects=collective_id is not None,
        ),
        name=name,
    )(*[array for _, array in arrays])


def send_part(g, expert_out, second_low, router, pos_col, pos_row, logit_ref, router_grad_ref, total_ref):
    probs, chosen, gate = route(second_low, router, pos_col)
    gate_grad = jnp.where(pos_col >= 0, jnp.sum(g * expert_out, -1, keepdims=True), 0.0)
    sent = (gate * g).astype(bf16)
    logit_grad = gate_grad * gate * (chosen - probs)
    logit_ref[0] = logit_grad
    high, low = split_two(logit_grad)
    router_grad_ref[...] += tn(high, second_low) + tn(low, second_low)
    total_ref[...] += spread_rows(pos_row, sent)


def turn_kernel(
    prev_ref, gate_ref, returned_ref, cotangent_ref, enter_ref, leave_ref, col_ref, row_ref, second_ref, router_ref,
    block_ref, grad_ref, logit_ref, router_grad_ref, buffer_ref, total_ref,
):
    image = pl.program_id(0)

    @pl.when(image == 0)
    def _():
        total_ref[...] = jnp.zeros(total_ref.shape, f32)
        router_grad_ref[...] = jnp.zeros(router_grad_ref.shape, f32)

    pos_col = col_ref[0, :, 0:1]
    expert_out = collect(pos_col, returned_ref)
    x = prev_ref[0] + gate_ref[0] * expert_out
    block_ref[0] = nn(leave_ref[...], x.astype(bf16)).astype(bf16)
    g = nn(enter_ref[...], cotangent_ref[0])
    grad_ref[0] = g
    send_part(
        g, expert_out, second_ref[0], router_ref[...], pos_col, row_ref[0, 0:1, :], logit_ref, router_grad_ref, total_ref
    )

    @pl.when(image == pl.num_programs(0) - 1)
    def _():
        buffer_ref[...] = total_ref[...].astype(bf16)


def attention_backward_kernel(last, mp, fast, *refs):
    (
        valid_ref, grad_ref, returned_ref, logit_ref, middle_ref, carried_ref, router_ref, col_ref, move_ref, back_ref,
        gain_ref, proj_ref, qkv_ref, window_ref, qk_ref, v_ref, probs_ref, att_ref,
    ) = refs[:18]
    refs = refs[18:]
    refs = list(refs)
    if fast:
        units_ref = refs.pop(0)
    if last:
        leave_ref = refs.pop(0)
    else:
        row_ref, expert_out_ref, second_ref, router_next_ref = refs[:4]
        refs = refs[4:]
    out_ref = refs.pop(0)
    if fast:
        unit_ref, mine_ref = refs[:2]
        refs = refs[2:]
    else:
        qkv_grad_ref, proj_grad_ref = refs[:2]
        refs = refs[2:]
    table_ref, small_ref = refs[:2]
    refs = refs[2:]
    if not last:
        logit_out_ref, router_grad_ref, buffer_ref = refs[:3]
        refs = refs[3:]
    turned = refs.pop(0)
    if fast:
        qkv_grad_ref, proj_grad_ref = refs[:2]
        refs = refs[2:]
    if not last:
        total_ref = refs.pop(0)
    image = pl.program_id(0)
    if fast:
        row = Row()
        sums = RowSum(
            row, [units_ref.at[k] for k in range(2)], refs[0], refs[1], refs[2], [mine_ref.at[k] for k in range(2)],
            refs[3:7],
        )

        @pl.when(image == 0)
        def _():
            pl.semaphore_wait(row.greet(), 2)
            for k in range(2):
                sums.start(k)

        @pl.when(image == 1)
        def _():
            for k in range(2):
                sums.middle(k)

    width = carried_ref.shape[-1]

    @pl.when(image == 0)
    def _():
        qkv_grad_ref[...] = jnp.zeros(qkv_grad_ref.shape, f32)
        proj_grad_ref[...] = jnp.zeros(proj_grad_ref.shape, f32)
        table_ref[...] = jnp.zeros(table_ref.shape, f32)
        small_ref[...] = jnp.zeros(small_ref.shape, f32)
        if not last:
            total_ref[...] = jnp.zeros(total_ref.shape, f32)
            router_grad_ref[...] = jnp.zeros(router_grad_ref.shape, f32)

    pos_col = col_ref[0, :, 0:1]
    g = grad_ref[0]
    high, low = split_two(logit_ref[0])
    router = router_ref[...]
    normed_grad = collect(pos_col, returned_ref) + nt(high, router) + nt(low, router)
    xhat, rstd = norm_parts(middle_ref[0])
    small_ref[1:2, :] += jnp.sum(normed_grad * xhat, 0, keepdims=True)
    small_ref[3:4, :] += jnp.sum(normed_grad, 0, keepdims=True)
    middle_grad = g + norm_back(normed_grad, gain_ref[1:2, :], xhat, rstd)
    branch_grad = (valid_ref[image].astype(f32) * middle_grad).astype(bf16)
    branch_grad = nn(move_ref[...], branch_grad).astype(bf16)
    proj_grad_ref[...] += nn(att_ref[0], branch_grad)
    att_grad = nt(proj_ref[...], branch_grad).astype(bf16)
    heads_rows = head_masks()
    halves = lane_masks()
    low_lane = iota((WPAD, LANES), 1) < WPAD
    for pair in range(PAIRS):
        across = slice(pair * LANES, (pair + 1) * LANES)
        for group in range(HEADS // GROUP):
            features = slice(group * LANES, (group + 1) * LANES)
            grads = att_grad[features, across]
            spread = jnp.concatenate([grads * heads_rows[h] for h in range(GROUP)], 1)
            raw = nn(v_ref[0, across, features], spread)
            for h in range(GROUP):
                head = group * GROUP + h
                at = slice(head * HEAD_DIM, (head + 1) * HEAD_DIM)
                below = slice(width + head * HEAD_DIM, width + (head + 1) * HEAD_DIM)
                lowest = slice(2 * width + head * HEAD_DIM, 2 * width + (head + 1) * HEAD_DIM)
                part = raw[:, h * LANES : (h + 1) * LANES]
                probs_grad = jnp.where(low_lane, part[:WPAD], part[WPAD:])
                probs_low = probs_ref[0, pair * HEADS + head]
                probs = probs_low.astype(f32)
                weighted = probs * probs_grad
                scores_grad = weighted - probs * jnp.sum(weighted, 0, keepdims=True)
                table_ref[head] += scores_grad
                scores_low = scores_grad.astype(bf16)
                both = jnp.concatenate([scores_low * halves[0], scores_low * halves[1]], 0)
                probs_both = jnp.concatenate([probs_low * halves[0], probs_low * halves[1]], 0)
                turned[at, across] = (nn(qk_ref[0, below, across], both) * head_scale).astype(bf16)
                turned[below, across] = (nt(qk_ref[0, at, across], both) * head_scale).astype(bf16)
                turned[lowest, across] = nt(att_grad[at, across], probs_both).astype(bf16)
    qkv_grad_ref[...] += nn(turned[...], window_ref[0])
    mixed_grad = nt(back_ref[...], turned[...]).astype(bf16)
    first_grad = nt(mixed_grad, qkv_ref[...])
    xhat, rstd = norm_parts(carried_ref[0])
    small_ref[0:1, :] += jnp.sum(first_grad * xhat, 0, keepdims=True)
    small_ref[2:3, :] += jnp.sum(first_grad, 0, keepdims=True)
    out = middle_grad + norm_back(first_grad, gain_ref[0:1, :], xhat, rstd)
    if fast:

        @pl.when(image == pl.num_programs(0) - 1)
        def _():
            columns, rows = 3 * width // mp, width // mp
            proj_turned = proj_grad_ref[...].T
            for place in range(mp):
                q = quarter_at(place, mp)
                unit_ref[place, :columns] = qkv_grad_ref[q * columns : (q + 1) * columns].astype(bf16)
                unit_ref[place, columns:] = proj_turned[q * rows : (q + 1) * rows].astype(bf16)
            for k in range(2):
                sums.end(k)
                sums.finish(k)

    if last:
        top = out.astype(bf16)
        rest = out - top.astype(f32)
        mid, low = split_two(rest)
        leave = leave_ref[...]
        out_ref[0] = nn(leave, top) + nn(leave, mid) + nn(leave, low)
        return
    out_ref[0] = out
    send_part(
        out, expert_out_ref[0], second_ref[0], router_next_ref[...], pos_col, row_ref[0, 0:1, :], logit_out_ref,
        router_grad_ref, total_ref,
    )

    @pl.when(image == pl.num_programs(0) - 1)
    def _():
        buffer_ref[...] = total_ref[...].astype(bf16)


def quarter_at(place, mp):
    return place % (mp // 2) * 2 + place // (mp // 2)


def add_up(*parts):
    total = parts[0].astype(f32)
    for part in parts[1:]:
        total = total + part.astype(f32)
    return total


def to_row(source, target, sems, k, row):
    return pltpu.make_async_remote_copy(
        src_ref=source,
        dst_ref=target,
        send_sem=sems[0].at[k],
        recv_sem=sems[1].at[k],
        device_id={"mp": row},
        device_id_type=MESH,
    )


class Row:
    def __init__(self):
        row = lax.axis_index("mp")
        self.row, self.core, self.y = row, lax.rem(row, 2), lax.div(row, 2)
        self.sibling, self.across = row + 1 - 2 * self.core, row + 2 - 4 * self.y
        self.place = self.core * 2 + self.y
        self.place_across = self.core * 2 + 1 - self.y

    def greet(self):
        barrier = pltpu.get_barrier_semaphore()
        for row in (self.sibling, self.across):
            pl.semaphore_signal(barrier, inc=1, device_id={"mp": row}, device_id_type=MESH)
        return barrier


class RowSum:
    semaphores = 4

    def __init__(self, row, units, core_in, y_out, y_in, mine, sems):
        self.row, self.units, self.mine = row, units, mine
        self.core_in, self.y_out, self.y_in = core_in, y_out, y_in
        self.sems = (sems[:2], sems[2:])

    def pair(self, k):
        theirs = self.units[k].at[pl.ds(2 * (1 - self.row.core), 2)]
        return to_row(theirs, self.core_in.at[k], self.sems[0], k, self.row.sibling)

    def cross(self, k):
        return to_row(self.y_out.at[k], self.y_in.at[k], self.sems[1], k, self.row.across)

    def start(self, k):
        self.pair(k).start()

    def middle(self, k):
        self.pair(k).wait_recv()
        other = 1 - self.row.y
        mixed = add_up(self.units[k][self.row.core * 2 + other], self.core_in[k, other])
        self.y_out[k] = mixed.astype(bf16)
        self.cross(k).start()

    def end(self, k):
        self.cross(k).wait_recv()
        self.mine[k][...] = add_up(
            self.units[k][self.row.place], self.core_in[k, self.row.y], self.y_in[k]
        ).astype(bf16)

    def finish(self, k):
        self.pair(k).wait_send()
        self.cross(k).wait_send()

    @classmethod
    def scratch(cls, count, width):
        return [
            pltpu.VMEM((count, 2, width, width), bf16),
            pltpu.VMEM((count, width, width), bf16),
            pltpu.VMEM((count, width, width), bf16),
        ] + [pltpu.SemaphoreType.DMA((count,))] * cls.semaphores


class RowGather:
    semaphores = 6

    def __init__(self, row, sources, fulls, slot, slot_across, sems):
        self.row, self.sources, self.fulls = row, sources, fulls
        self.slot, self.slot_across = slot, slot_across
        self.sems = (sems[:2], sems[2:4], sems[4:])

    def over(self, k):
        return to_row(self.sources[k], self.fulls[k].at[self.slot], self.sems[0], k, self.row.across)

    def near(self, k):
        return to_row(self.sources[k], self.fulls[k].at[self.slot], self.sems[1], k, self.row.sibling)

    def onward(self, k):
        block = self.fulls[k].at[self.slot_across]
        return to_row(block, block, self.sems[2], k, self.row.sibling)

    def start(self, k):
        self.over(k).start()
        self.near(k).start()

    def forward(self, k):
        self.over(k).wait_recv()
        self.onward(k).start()

    def arrive(self, k):
        self.near(k).wait_recv()
        self.onward(k).wait_recv()

    def sent(self, k):
        self.over(k).wait_send()
        self.near(k).wait_send()
        self.onward(k).wait_send()

    @classmethod
    def scratch(cls, count):
        return [pltpu.SemaphoreType.DMA((count,))] * cls.semaphores


def closing_kernel(
    dp, mp, given_ref, attn_ref, small_ref, full_ref, shard_ref, small_out, core_in, y_out, y_in, a0, a1, b0, b1, g0, g1, g2,
    g3, g4, g5, mine, x_in, half, z_in, s_core, s_one, s_y, s_mine, s_x, s_half, s_z, s0, s1, s2, s3, x0, x1, z0, z1, w0, w1,
    v0, v1,
):
    me = lax.axis_index("dp")
    x, z = lax.rem(me, 2), lax.div(me, 2)
    deep = dp // 2
    partner = me + 1 - 2 * x
    row = Row()
    sums = RowSum(row, [attn_ref], core_in, y_out, y_in, [mine], (a0, a1, b0, b1))
    gather = RowGather(
        row, [given_ref.at[0], given_ref.at[1]], [full_ref.at[0], full_ref.at[1]], row.place, row.place_across,
        (g0, g1, g2, g3, g4, g5),
    )
    barrier = row.greet()
    pl.semaphore_signal(barrier, inc=1, device_id={"dp": partner}, device_id_type=MESH)
    for off in range(1, deep):
        peer = lax.rem(z + off, deep) * 2 + x
        pl.semaphore_signal(barrier, inc=1, device_id={"dp": peer}, device_id_type=MESH)
    pl.semaphore_wait(barrier, 3 + deep - 1)

    s_pair = to_row(small_ref, s_core, (s0, s1), 0, row.sibling)
    s_cross = to_row(s_one, s_y, (s2, s3), 0, row.across)
    early, late, every = (0, 1), (2, 3), (0, 1, 2, 3)
    total = [given_ref.at[0], given_ref.at[1], mine, s_mine]
    arrived = [x_in.at[k] for k in range(3)] + [s_x]
    halves = [half.at[k] for k in range(3)] + [s_half]
    slots = [z_in.at[k] for k in range(3)] + [s_z]
    result = [shard_ref.at[k] for k in range(3)] + [small_out]

    def cut(k):
        height = total[k].shape[0] // 2
        return height, height // deep

    def over_x(k):
        height, _ = cut(k)
        away = total[k].at[pl.ds(pl.multiple_of((1 - x) * height, height), height)]
        return to_peer(away, arrived[k], x0.at[k], x1.at[k], partner)

    def over_z(k, off):
        _, piece = cut(k)
        to = lax.rem(z + off, deep)
        part = halves[k].at[pl.ds(pl.multiple_of(to * piece, piece), piece)]
        return to_peer(part, slots[k].at[off], z0.at[k, off], z1.at[k, off], to * 2 + x)

    def own_piece(k):
        height, piece = cut(k)
        return result[k].at[pl.ds(pl.multiple_of(x * height + z * piece, piece), piece)]

    def own_half(k):
        height, _ = cut(k)
        return result[k].at[pl.ds(pl.multiple_of(x * height, height), height)]

    def back_z(k, off):
        to = lax.rem(z + off, deep)
        return to_peer(own_piece(k), own_piece(k), w0.at[k, off], w1.at[k, off], to * 2 + x)

    def back_x(k):
        return to_peer(own_half(k), own_half(k), v0.at[k], v1.at[k], partner)

    def halve(k):
        over_x(k).wait_recv()
        height, _ = cut(k)
        keep = total[k][pl.ds(pl.multiple_of(x * height, height), height)]
        halves[k][...] = add_up(keep, arrived[k][...]).astype(halves[k].dtype)
        for off in range(1, deep):
            over_z(k, off).start()

    def quarter(k):
        for off in range(1, deep):
            over_z(k, off).wait_recv()
        _, piece = cut(k)
        keep = halves[k][pl.ds(pl.multiple_of(z * piece, piece), piece)]
        own_piece(k)[...] = add_up(keep, *[slots[k][off] for off in range(1, deep)]).astype(result[k].dtype)
        for off in range(1, deep):
            back_z(k, off).start()

    def widen(k):
        for off in range(1, deep):
            back_z(k, off).wait_recv()
        back_x(k).start()

    sums.start(0)
    s_pair.start()
    for k in early:
        over_x(k).start()
    sums.middle(0)
    s_pair.wait_recv()
    s_one[...] = small_ref[...] + s_core[...]
    s_cross.start()
    for k in early:
        gather.start(k)
        full_ref[k, row.place] = given_ref[k]
    for k in early:
        halve(k)
    sums.end(0)
    over_x(2).start()
    s_cross.wait_recv()
    s_mine[...] = s_one[...] + s_y[...]
    over_x(3).start()
    for k in early:
        quarter(k)
    for k in late:
        halve(k)
    for k in early:
        widen(k)
    for k in late:
        quarter(k)
    gather.forward(0)
    for k in late:
        widen(k)
    gather.forward(1)
    s_pair.wait_send()
    s_cross.wait_send()
    sums.finish(0)
    for k in early:
        gather.arrive(k)
        gather.sent(k)
    for k in every:
        over_x(k).wait_send()
        for off in range(1, deep):
            over_z(k, off).wait_send()
            back_z(k, off).wait_send()
        back_x(k).wait()


def closing_call(dp, mp, given, attn, small, collective_id):
    width = attn.shape[-1]
    deep = dp // 2
    lines = small.shape[0]
    dma = pltpu.SemaphoreType.DMA
    shape = jax.ShapeDtypeStruct
    scratch = RowSum.scratch(1, width) + RowGather.scratch(2) + [
        pltpu.VMEM((width, width), bf16),
        pltpu.VMEM((3, width // 2, width), bf16),
        pltpu.VMEM((3, width // 2, width), bf16),
        pltpu.VMEM((3, deep, width // dp, width), bf16),
        pltpu.VMEM((lines, width), f32),
        pltpu.VMEM((lines, width), f32),
        pltpu.VMEM((lines, width), f32),
        pltpu.VMEM((lines, width), f32),
        pltpu.VMEM((lines // 2, width), f32),
        pltpu.VMEM((lines // 2, width), f32),
        pltpu.VMEM((deep, lines // dp, width), f32),
        dma((1,)), dma((1,)), dma((1,)), dma((1,)),
        dma((4,)), dma((4,)), dma((4, deep)), dma((4, deep)), dma((4, deep)), dma((4, deep)), dma((4,)), dma((4,)),
    ]
    vmem = pl.BlockSpec(memory_space=pltpu.VMEM)
    return pl.pallas_call(
        functools.partial(closing_kernel, dp, mp),
        out_shape=[shape((2, mp, width, width), bf16), shape((3, width, width), bf16), shape(small.shape, f32)],
        in_specs=[vmem] * 3,
        out_specs=[vmem] * 3,
        scratch_shapes=scratch,
        compiler_params=pltpu.CompilerParams(
            vmem_limit_bytes=56 * MIB, collective_id=collective_id, has_side_effects=True
        ),
        name="closing",
    )(given, attn, small)


def residual_kernel(full_ref, up_ref, down_ref):
    mp, width = full_ref.shape[2], full_ref.shape[3]
    rows = width // mp
    for place in range(mp):
        q = quarter_at(place, mp)
        up_ref[0, 0, :, q * width : (q + 1) * width] = full_ref[0, 0, place].astype(f32)
    for chunk in range(up_ref.shape[-1] // width):
        block = [None] * mp
        for place in range(mp):
            block[quarter_at(place, mp)] = full_ref[0, 1, place, chunk * rows : (chunk + 1) * rows].astype(f32)
        down_ref[0, 0, chunk * width : (chunk + 1) * width, :] = jnp.concatenate(block, 0).T


def residual_call(fulls, hidden):
    layers, _, mp, width, _ = fulls.shape
    return pl.pallas_call(
        residual_kernel,
        grid=(layers,),
        out_shape=[
            jax.ShapeDtypeStruct((layers, 1, width, hidden), f32),
            jax.ShapeDtypeStruct((layers, 1, hidden, width), f32),
        ],
        in_specs=[pl.BlockSpec((1, 2, mp, width, width), lambda i: (i, 0, 0, 0, 0))],
        out_specs=[
            pl.BlockSpec((1, 1, width, hidden), lambda i: (i, 0, 0, 0)),
            pl.BlockSpec((1, 1, hidden, width), lambda i: (i, 0, 0, 0)),
        ],
        compiler_params=pltpu.CompilerParams(vmem_limit_bytes=40 * MIB),
        name="residuals",
    )(fulls)


def greet(dp, me, rows=()):
    barrier = pltpu.get_barrier_semaphore()
    for row in rows:
        pl.semaphore_signal(barrier, inc=1, device_id={"mp": row}, device_id_type=MESH)

    def signal(off, carry):
        pl.semaphore_signal(barrier, inc=1, device_id={"dp": lax.rem(me + off, dp)}, device_id_type=MESH)
        return carry

    lax.fori_loop(1, dp, signal, 0)
    pl.semaphore_wait(barrier, dp - 1 + len(rows))


def to_peer(source, target, send_sem, recv_sem, peer):
    return pltpu.make_async_remote_copy(
        src_ref=source,
        dst_ref=target,
        send_sem=send_sem,
        recv_sem=recv_sem,
        device_id={"dp": peer},
        device_id_type=MESH,
    )


def gelu_parts(h):
    root = np.float32(np.sqrt(2.0 / np.pi))
    square = h * h
    t = jnp.tanh(root * h * (1.0 + 0.044715 * square))
    half = 0.5 * (1.0 + t)
    slope = half + 0.5 * h * (1.0 - t * t) * root * (1.0 + 3 * 0.044715 * square)
    return h * half, slope


def expert_forward_kernel(
    dp, mp, buffer_ref, up_ref, down_ref, rup_ref, rdown_ref, recv_ref, returned_ref, up_eff, down_eff, part, core,
    send_one, recv_one, send_two, recv_two,
):
    split = dp // EXPERTS
    me = lax.axis_index("dp")
    greet(dp, me)

    def first(off):
        peer = lax.rem(me + off, dp)
        return to_peer(
            buffer_ref.at[lax.div(peer, split)], recv_ref.at[me], send_one.at[off], recv_one.at[off], peer
        )

    def second(off):
        source = lax.rem(me + dp - off, dp)
        return to_peer(part.at[source], returned_ref.at[me], send_two.at[off], recv_two.at[off], source)

    def start_first(off, carry):
        first(off).start()
        return carry

    lax.fori_loop(1, dp, start_first, 0)
    recv_ref[me] = buffer_ref[lax.div(me, split)]
    hidden = up_eff.shape[1]
    columns = up_ref.shape[-1]
    if split == 1 and columns % LANES == 0:
        for m in range(mp):
            at = slice(m * columns, (m + 1) * columns)
            up_eff[:, at] = (up_ref[m].astype(f32) + rup_ref[:, at].astype(f32)).astype(bf16)
    else:
        core[...] = rup_ref[...].astype(f32)
        begin = lax.rem(me, split) * hidden
        for m in range(mp):
            put = onehot(iota((columns, hidden), 0) + m * columns == iota((columns, hidden), 1) + begin)
            core[...] += nn(up_ref[m], put)
        up_eff[...] = core[...].astype(bf16)
    columns = down_ref.shape[-1]
    width = down_eff.shape[1]
    rows = pl.ds(pl.multiple_of(lax.rem(me, split) * hidden, LANES), hidden)
    total = rdown_ref[...].astype(f32)
    for m in range(mp):
        put = onehot(iota((columns, width), 0) + m * columns == iota((columns, width), 1))
        total = total + nn(down_ref[m, rows, :], put)
    down_eff[...] = total.astype(bf16)

    def work(source):
        hidden_pre = nn(recv_ref[source], up_eff[...])
        hidden_low = gelu_parts(hidden_pre)[0].astype(bf16)
        return nn(hidden_low, down_eff[...]).astype(bf16)

    returned_ref[me] = work(me)

    def step(off, carry):
        source = lax.rem(me + dp - off, dp)
        first(off).wait_recv()
        part[source] = work(source)
        second(off).start()
        return carry

    lax.fori_loop(1, dp, step, 0)

    def finish(off, carry):
        first(off).wait_send()
        second(off).wait()
        return carry

    lax.fori_loop(1, dp, finish, 0)


def expert_backward_kernel(dp, mp, fast, reduce, *refs):
    refs = list(refs)
    buffer_ref, recv_ref, up_ref, down_ref = refs[:4]
    refs = refs[4:]
    if reduce:
        given_ref, attn_ref = refs[:2]
        refs = refs[2:]
    returned_ref = refs.pop(0)
    if fast:
        units_ref = refs.pop(0)
    else:
        up_term, down_term = refs[:2]
        refs = refs[2:]
    if reduce:
        full_ref, mine_ref = refs[:2]
        refs = refs[2:]
    grads, hidden_low, slope, pre, part = refs[:5]
    refs = refs[5:]
    if fast:
        up_term, down_term = refs[:2]
        refs = refs[2:]
    row = Row() if reduce else None
    if reduce:
        core_in, y_out, y_in = refs[:3]
        sums = RowSum(row, [attn_ref], core_in, y_out, y_in, [mine_ref], refs[3:7])
        gather = RowGather(
            row, [given_ref.at[k] for k in range(2)], [full_ref.at[k] for k in range(2)], row.place, row.place_across,
            refs[7:13],
        )
        refs = refs[13:]
    send_one, recv_one, send_two, recv_two = refs
    split = dp // EXPERTS
    me = lax.axis_index("dp")
    greet(dp, me, (row.sibling, row.across) if reduce else ())

    def first(off):
        peer = lax.rem(me + off, dp)
        return to_peer(buffer_ref.at[lax.div(peer, split)], grads.at[me], send_one.at[off], recv_one.at[off], peer)

    def second(off):
        source = lax.rem(me + dp - off, dp)
        return to_peer(part.at[source], returned_ref.at[me], send_two.at[off], recv_two.at[off], source)

    def start_first(off, carry):
        first(off).start()
        return carry

    lax.fori_loop(1, dp, start_first, 0)
    if reduce:
        sums.start(0)
        for k in range(2):
            gather.start(k)
    grads[me] = buffer_ref[lax.div(me, split)]

    def again(source, carry):
        value, rate = gelu_parts(nn(recv_ref[source], up_ref[...]))
        hidden_low[source] = value.astype(bf16)
        slope[source] = rate
        return carry

    lax.fori_loop(0, dp, again, 0)
    if reduce:
        sums.middle(0)
        for k in range(2):
            full_ref[k, row.place] = given_ref[k]

    def work(source):
        hidden_grad = nt(grads[source], down_ref[...])
        pre_grad = (slope[source] * hidden_grad).astype(bf16)
        pre[source] = pre_grad
        return nt(pre_grad, up_ref[...]).astype(bf16)

    returned_ref[me] = work(me)

    def step(off, carry):
        source = lax.rem(me + dp - off, dp)
        first(off).wait_recv()
        part[source] = work(source)
        second(off).start()
        return carry

    lax.fori_loop(1, dp, step, 0)
    if reduce:
        for k in range(2):
            gather.forward(k)
        sums.end(0)
    up_term[...] = jnp.zeros(up_term.shape, f32)
    down_term[...] = jnp.zeros(down_term.shape, f32)

    def terms(block, carry):
        up_term[...] += tn(recv_ref[block], pre[block])
        down_term[...] += tn(grads[block], hidden_low[block])
        return carry

    lax.fori_loop(0, dp, terms, 0)
    if fast:
        width = up_term.shape[0]
        height = width // mp
        for place in range(mp):
            q = quarter_at(place, mp)
            units_ref[0, place] = up_term[:, q * width : (q + 1) * width].astype(bf16)
            for chunk in range(mp):
                block = down_term[q * height : (q + 1) * height, chunk * width : (chunk + 1) * width]
                units_ref[1, place, chunk * height : (chunk + 1) * height] = block.astype(bf16)

    def finish(off, carry):
        first(off).wait_send()
        second(off).wait()
        return carry

    lax.fori_loop(1, dp, finish, 0)
    if reduce:
        sums.finish(0)
        for k in range(2):
            gather.arrive(k)
            gather.sent(k)


def expert_call(kernel, arrays, outs, scratch, dp, collective_id, name, flops):
    sems = [pltpu.SemaphoreType.DMA((dp,))] * 4
    return pl.pallas_call(
        kernel,
        out_shape=[jax.ShapeDtypeStruct(shape, dtype) for shape, dtype in outs],
        in_specs=[pl.BlockSpec(memory_space=pltpu.VMEM)] * len(arrays),
        out_specs=[pl.BlockSpec(memory_space=pltpu.VMEM)] * len(outs),
        scratch_shapes=scratch + sems,
        compiler_params=pltpu.CompilerParams(
            vmem_limit_bytes=56 * MIB, collective_id=collective_id, has_side_effects=True
        ),
        cost_estimate=pl.CostEstimate(flops=flops, bytes_accessed=20 * MIB, transcendentals=0),
        name=name,
    )(*arrays)


def by_windows(grid):
    images, kinds = grid.shape[:2]
    blocks = GRID // WINDOW
    grid = grid.reshape(images, kinds, blocks, WINDOW, blocks, WINDOW).transpose(0, 1, 2, 4, 3, 5)
    grid = grid.reshape(images, kinds, blocks * blocks, WINPOS)
    grid = jnp.pad(grid, ((0, 0), (0, 0), (0, 0), (0, WPAD - WINPOS)), constant_values=-1)
    return grid.reshape(images, kinds, IMGROWS)


def per_device(
    patches,
    qkv_weight,
    proj_weight,
    core_up,
    core_down,
    residual_up,
    residual_down,
    position_bias,
    router_weight,
    norm_gain,
    norm_bias,
    cotangent,
    image_valid,
    expert_index,
    slot_index,
    region_id,
):
    dp, mp = lax.axis_size("dp"), lax.axis_size("mp")
    images, _, width = patches.shape
    split = dp // EXPERTS
    hidden = residual_up.shape[-1]
    hidden_full = core_up.shape[-1] * mp
    row_index = lax.axis_index("mp")

    gathered = []
    for l in range(LAYERS):
        gathered.append(
            tuple(
                lax.all_gather(a[l], "mp", axis=0, tiled=False)
                for a in (qkv_weight, proj_weight, core_up, core_down)
            )
        )

    position = jnp.where(slot_index >= 0, expert_index * SLOTS + slot_index, -1)
    labels = jnp.roll(region_id, (-SHIFT, -SHIFT), (1, 2))
    row_form = by_windows(jnp.stack([position.reshape(images, GRID, GRID), labels], 1))
    col_form = row_form.transpose(0, 2, 1)
    enter = jnp.asarray(enter_table(), bf16)
    leave = jnp.asarray(enter_table().T, bf16)
    moves = [jnp.asarray(move_table(l % 2 == 1), bf16) for l in range(LAYERS)]
    backs = [jnp.asarray(move_table(l % 2 == 1).T, bf16) for l in range(LAYERS)]
    entries = jnp.asarray(offset_index().reshape(-1))
    entry_hot = (jnp.arange(OFFSETS + 1)[:, None] == entries[None, :]).astype(f32)
    table_rows = position_bias.transpose(0, 2, 1).reshape(LAYERS * HEADS, OFFSETS)
    padded_rows = jnp.pad(table_rows, ((0, 0), (0, 1)), constant_values=-1e30)
    biases = jnp.dot(padded_rows, entry_hot, precision=highest).reshape(LAYERS, HEADS, WPAD, LANES)
    routers = jnp.pad(router_weight, ((0, 0), (0, 0), (0, LANES - EXPERTS)))

    token = (images, IMGROWS, width)
    buffer_shape = (ROWS, width)
    block_rows = (dp, SLOTS, width)
    pieces = (split, ROWS, width)

    def by_piece(returned):
        return returned.reshape(EXPERTS, split, SLOTS, width).transpose(1, 0, 2, 3).reshape(pieces)

    records = []
    before = None
    for l in range(LAYERS):
        first = l == 0
        if first:
            arrays = [("image", patches), ("whole", enter)]
        else:
            arrays = [("image", before[0]), ("image", before[1]), ("whole", before[2])]
        arrays += [
            ("smem", image_valid),
            ("image", col_form),
            ("image", row_form),
            ("whole", gathered[l][0]),
            ("whole", gathered[l][1]),
            ("whole", biases[l]),
            ("whole", moves[l]),
            ("whole", backs[l]),
            ("whole", norm_gain[l]),
            ("whole", norm_bias[l]),
            ("whole", routers[l]),
        ]
        outs = [("image", token, f32)]
        if not first:
            outs.append(("image", token, f32))
        outs += [
            ("image", token, f32),
            ("image", token, bf16),
            ("image", (images, IMGROWS, 1), f32),
            ("whole", buffer_shape, bf16),
            ("image", token, bf16),
            ("image", (images, 2 * width, IMGROWS), bf16),
            ("image", token, bf16),
            ("image", (images, PAIRS * HEADS, WPAD, LANES), bf16),
            ("image", (images, width, IMGROWS), bf16),
            ("whole", (width, 3 * width), bf16),
            ("whole", (width, width), bf16),
        ]
        scratch = [pltpu.VMEM((3 * width, width), bf16), pltpu.VMEM(buffer_shape, f32)]
        results = list(
            image_call(
                functools.partial(attention_forward_kernel, first, l % 2 == 1, mp),
                images, arrays, outs, scratch, f"attend_{l}",
            )
        )
        carried = results.pop(0)
        if not first:
            records[-1]["expert_out"] = results.pop(0)
        middle, second_low, gate, buffer = results[:4]
        received, returned, up_eff, down_eff = expert_call(
            functools.partial(expert_forward_kernel, dp, mp),
            [
                buffer.reshape(EXPERTS, SLOTS, width),
                gathered[l][2],
                gathered[l][3],
                residual_up[l, 0],
                residual_down[l, 0],
            ],
            [
                (block_rows, bf16),
                (block_rows, bf16),
                ((width, hidden), bf16),
                ((hidden, width), bf16),
            ],
            [pltpu.VMEM(block_rows, bf16), pltpu.VMEM((width, hidden), f32)],
            dp, l, f"experts_{l}", 4 * dp * SLOTS * width * hidden,
        )
        returned = by_piece(returned)
        before = (middle, gate, returned)
        records.append(
            dict(
                carried=carried, middle=middle, second_low=second_low, gate=gate, saved=results[4:], received=received,
                up_eff=up_eff, down_eff=down_eff,
            )
        )

    top = records[-1]
    block_output, grad, logit_grad, router_part, buffer = image_call(
        turn_kernel,
        images,
        [
            ("image", before[0]),
            ("image", before[1]),
            ("whole", before[2]),
            ("image", cotangent),
            ("whole", enter),
            ("whole", leave),
            ("image", col_form),
            ("image", row_form),
            ("image", top["second_low"]),
            ("whole", routers[LAYERS - 1]),
        ],
        [
            ("image", patches.shape, bf16),
            ("image", token, f32),
            ("image", (images, IMGROWS, LANES), f32),
            ("whole", (LANES, width), f32),
            ("whole", buffer_shape, bf16),
        ],
        [pltpu.VMEM(buffer_shape, f32)],
        "turn",
    )
    router_parts, tables, smalls = [None] * LAYERS, [None] * LAYERS, [None] * LAYERS
    residual_sums, shard_sums = [None] * LAYERS, [None] * LAYERS
    router_parts[LAYERS - 1] = router_part
    fast = split == 1 and dp == 8 and mp == 4 and hidden == mp * width
    units, attn_units, mines = [None] * LAYERS, [None] * LAYERS, [None] * LAYERS
    for l in reversed(range(LAYERS)):
        rec = records[l]
        last = l == 0
        reduce = fast and l < LAYERS - 1
        arrays = [buffer.reshape(EXPERTS, SLOTS, width), rec["received"], rec["up_eff"], rec["down_eff"]]
        outs = [(block_rows, bf16)]
        scratch = [
            pltpu.VMEM(block_rows, bf16),
            pltpu.VMEM((dp, SLOTS, hidden), bf16),
            pltpu.VMEM((dp, SLOTS, hidden), f32),
            pltpu.VMEM((dp, SLOTS, hidden), bf16),
            pltpu.VMEM(block_rows, bf16),
        ]
        if fast:
            outs.append(((2, mp, width, width), bf16))
            scratch += [pltpu.VMEM((width, hidden), f32)] * 2
        else:
            outs += [((width, hidden), f32)] * 2
        if reduce:
            arrays += [mines[l + 1], attn_units[l + 1]]
            outs += [((2, mp, width, width), bf16), ((width, width), bf16)]
            scratch += RowSum.scratch(1, width) + RowGather.scratch(2)
        results = list(
            expert_call(
                functools.partial(expert_backward_kernel, dp, mp, fast, reduce), arrays, outs, scratch, dp, LAYERS + l,
                f"experts_back_{l}", 10 * dp * SLOTS * width * hidden,
            )
        )
        returned_grad = results.pop(0)
        if fast:
            units[l] = results.pop(0)
        else:
            residual_sums[l] = lax.psum(tuple(t.astype(bf16) for t in results[:2]), "mp")
        if reduce:
            full_above, mine_above = results
            shard_above = lax.psum(jnp.concatenate([mines[l + 1], mine_above[None]], 0), "dp")
        window_in, qk, v, probs, att, qkv_full, proj_full = rec["saved"]
        arrays = [
            ("smem", image_valid),
            ("image", grad),
            ("whole", by_piece(returned_grad)),
            ("image", logit_grad),
            ("image", rec["middle"]),
            ("image", rec["carried"]),
            ("whole", routers[l]),
            ("image", col_form),
            ("whole", moves[l]),
            ("whole", backs[l]),
            ("whole", norm_gain[l]),
            ("whole", proj_full),
            ("whole", qkv_full),
            ("image", window_in),
            ("image", qk),
            ("image", v),
            ("image", probs),
            ("image", att),
        ]
        outs = [("image", patches.shape if last else token, f32)]
        scratch = [pltpu.VMEM((3 * width, IMGROWS), bf16)]
        if fast:
            arrays.append(("whole", units[l]))
            outs += [("whole", (mp, width, width), bf16), ("whole", (2, width, width), bf16)]
            scratch += [pltpu.VMEM((3 * width, width), f32), pltpu.VMEM((width, width), f32)]
        else:
            outs += [("whole", (3 * width, width), f32), ("whole", (width, width), f32)]
        outs += [("whole", (HEADS, WPAD, LANES), f32), ("whole", (8, width), f32)]
        if last:
            arrays.append(("whole", leave))
        else:
            below = records[l - 1]
            arrays += [
                ("image", row_form),
                ("image", below["expert_out"]),
                ("image", below["second_low"]),
                ("whole", routers[l - 1]),
            ]
            outs += [
                ("image", (images, IMGROWS, LANES), f32),
                ("whole", (LANES, width), f32),
                ("whole", buffer_shape, bf16),
            ]
            scratch.append(pltpu.VMEM(buffer_shape, f32))
        if fast:
            scratch += RowSum.scratch(2, width)
        results = list(
            image_call(
                functools.partial(attention_backward_kernel, last, mp, fast),
                images, arrays, outs, scratch, f"attend_back_{l}", 2 * LAYERS + 1 + l if fast else None,
            )
        )
        grad = results.pop(0)
        if fast:
            attn_units[l], mines[l] = results[:2]
            results = results[2:]
        else:
            qkv_part, proj_part = results[:2]
            results = results[2:]
        tables[l], smalls[l] = results[:2]
        if not last:
            logit_grad, router_parts[l - 1], buffer = results[2:]
        if fast:
            continue
        attn = (
            lax.psum_scatter(qkv_part.astype(bf16), "mp", scatter_dimension=0, tiled=True),
            lax.psum_scatter(proj_part.T.astype(bf16), "mp", scatter_dimension=0, tiled=True),
        )
        up_sum, down_sum = residual_sums[l]
        if split > 1:
            begin = lax.axis_index("dp") % split * hidden
            empty = jnp.zeros((width, hidden_full), bf16)
            up_sum = lax.dynamic_update_slice_in_dim(empty, up_sum, begin, 1)
            down_sum = lax.dynamic_update_slice_in_dim(empty, down_sum, begin, 1)
        up_columns, down_columns = core_up.shape[-1], core_down.shape[-1]
        up_shard = lax.dynamic_slice_in_dim(up_sum, row_index * up_columns, up_columns, 1)
        down_shard = lax.dynamic_slice_in_dim(down_sum, row_index * down_columns, down_columns, 0)
        shard_sums[l] = lax.psum((attn[0], attn[1], up_shard, down_shard), "dp")

    entry_turned = (entries[:, None] == jnp.arange(OFFSETS)[None, :]).astype(f32)
    table_part = jnp.dot(
        jnp.stack(tables, 0).reshape(LAYERS * HEADS, WPAD * LANES), entry_turned, precision=highest
    )
    small_part = jnp.stack(smalls, 0)[:, :4]
    router_part = jnp.stack(router_parts, 0)[:, :EXPERTS]
    if fast:
        lines = jnp.concatenate(
            [
                jnp.pad(table_part, ((0, 0), (0, width - OFFSETS))),
                router_part.reshape(-1, width),
                small_part.reshape(-1, width),
            ],
            0,
        )
        count = -(-lines.shape[0] // 64) * 64
        full, shards, lines = closing_call(
            dp, mp, mines[0], attn_units[0], jnp.pad(lines, ((0, count - lines.shape[0]), (0, 0))), 2 * LAYERS
        )
        shards = jnp.stack([shards, shard_above], 0)
        residual_up_grad, residual_down_grad = residual_call(jnp.stack([full, full_above], 0), hidden)
        columns = qkv_weight.shape[-1]
        attn = shards[:, 2].astype(f32)
        at = LAYERS * HEADS
        table_sum = lines[:at, :OFFSETS]
        router_sum = lines[at : at + LAYERS * EXPERTS].reshape(LAYERS, EXPERTS, width)
        at += LAYERS * EXPERTS
        small_sum = lines[at : at + LAYERS * 4].reshape(LAYERS, 4, width)
        down = shards[:, 1].astype(f32).reshape(LAYERS, mp, width // mp, width).transpose(0, 1, 3, 2)
        attn_grads = (attn[:, :columns].transpose(0, 2, 1), attn[:, columns:].transpose(0, 2, 1))
        core_grads = (shards[:, 0].astype(f32), down.reshape(LAYERS, mp * width, width // mp))
    else:
        table_sum, small_sum, router_sum = lax.psum((table_part, small_part, router_part), ("dp", "mp"))

        def shard(k):
            return jnp.stack([shard_sums[l][k] for l in range(LAYERS)], 0).astype(f32)

        attn_grads = (shard(0).transpose(0, 2, 1), shard(1).transpose(0, 2, 1))
        core_grads = (shard(2), shard(3).transpose(0, 2, 1))
        residual_up_grad, residual_down_grad = (
            jnp.stack([residual_sums[l][k] for l in range(LAYERS)], 0).astype(f32) for k in range(2)
        )
        residual_up_grad = residual_up_grad[:, None]
        residual_down_grad = residual_down_grad.transpose(0, 2, 1)[:, None]

    return (
        block_output,
        grad,
        attn_grads[0],
        attn_grads[1],
        core_grads[0],
        core_grads[1],
        residual_up_grad,
        residual_down_grad,
        table_sum.reshape(LAYERS, HEADS, OFFSETS).transpose(0, 2, 1),
        router_sum.transpose(0, 2, 1),
        small_sum[:, 0:2],
        small_sum[:, 2:4],
    )


def solution(mesh):
    placed = (
        P(("dp", "mp"), None, None),
        P(None, None, "mp"),
        P(None, None, "mp"),
        P(None, None, "mp"),
        P(None, None, "mp"),
        P(None, "dp", None, None),
        P(None, "dp", None, None),
        P(),
        P(),
        P(),
        P(),
        P(("dp", "mp"), None, None),
        P(("dp", "mp")),
        P(("dp", "mp"), None),
        P(("dp", "mp"), None),
        P(("dp", "mp"), None, None),
    )
    return jax.shard_map(
        per_device,
        mesh=mesh,
        in_specs=placed,
        out_specs=(
            P(("dp", "mp"), None, None),
            P(("dp", "mp"), None, None),
            P(None, None, "mp"),
            P(None, None, "mp"),
            P(None, None, "mp"),
            P(None, None, "mp"),
            P(None, "dp", None, None),
            P(None, "dp", None, None),
            P(),
            P(),
            P(),
            P(),
        ),
        check_vma=False,
    )
```

```python
import functools

import jax
import jax.numpy as jnp
import numpy as np
from jax import lax
from jax.experimental import pallas as pl
from jax.experimental.pallas import tpu as pltpu
from jax.sharding import PartitionSpec as P

HEADS = 12
HEAD_DIM = 32
EXPERTS = 8
WINDOW = 7
GRID = 14
SHIFT = 3
LAYERS = 2
WINPOS = 49
OFFSETS = 169
CAP = 122

WPAD = 64
IMGROWS = 256
PATCHES = 196
SLOTS = 128
ROWS = EXPERTS * SLOTS
LANES = 128
GROUP = 4
PAIRS = 2

bf16 = jnp.bfloat16
f32 = jnp.float32
highest = lax.Precision.HIGHEST
norm_epsilon = 1e-05
mask_fill = -100.0
head_scale = HEAD_DIM ** (-0.5)
MESH = pl.DeviceIdType.MESH
MIB = 1024 * 1024


def nn(a, b):
    return lax.dot_general(a, b, (((1,), (0,)), ((), ())), preferred_element_type=f32)


def nt(a, b):
    return lax.dot_general(a, b, (((1,), (1,)), ((), ())), preferred_element_type=f32)


def tn(a, b):
    return lax.dot_general(a, b, (((0,), (0,)), ((), ())), preferred_element_type=f32)


def iota(shape, dim):
    return lax.broadcasted_iota(jnp.int32, shape, dim)


def onehot(flags):
    return jnp.where(flags, 1.0, 0.0).astype(bf16)


def natural_of_row(shifted):
    moved = SHIFT if shifted else 0
    blocks = GRID // WINDOW
    out = -np.ones(IMGROWS, np.int32)
    for window in range(blocks * blocks):
        for cell in range(WINPOS):
            row = (window // blocks * WINDOW + cell // WINDOW + moved) % GRID
            col = (window % blocks * WINDOW + cell % WINDOW + moved) % GRID
            out[window * WPAD + cell] = row * GRID + col
    return out


def enter_table():
    held = natural_of_row(False)
    return (held[:, None] == np.arange(PATCHES)[None, :]).astype(np.float32)


def move_table(shifted):
    first, second = natural_of_row(False), natural_of_row(shifted)
    same = (second[:, None] == first[None, :]) & (second[:, None] >= 0)
    return same.astype(np.float32)


def offset_index():
    key = np.arange(WPAD)[:, None]
    query = np.arange(LANES)[None, :] % WPAD
    entry = (
        (query // WINDOW - key // WINDOW + WINDOW - 1) * (2 * WINDOW - 1)
        + query % WINDOW
        - key % WINDOW
        + WINDOW
        - 1
    )
    real = (key < WINPOS) & (query < WINPOS)
    return np.where(real, entry, np.where(key < WINPOS, -1, OFFSETS)).astype(np.int32)


def norm_parts(x):
    width = x.shape[-1]
    center = x - jnp.sum(x, -1, keepdims=True) * (1.0 / width)
    spread = jnp.sum(center * center, -1, keepdims=True) * (1.0 / width)
    rstd = lax.rsqrt(spread + norm_epsilon)
    return center * rstd, rstd


def norm_back(grad, gain, xhat, rstd):
    width = xhat.shape[-1]
    dxhat = grad * gain
    mean_one = jnp.sum(dxhat, -1, keepdims=True) * (1.0 / width)
    mean_two = jnp.sum(dxhat * xhat, -1, keepdims=True) * (1.0 / width)
    return rstd * (dxhat - mean_one - xhat * mean_two)


def split_two(x):
    high = x.astype(bf16)
    return high, (x - high.astype(f32)).astype(bf16)


def collect(pos_col, returned_ref):
    pick = onehot(pos_col == iota((IMGROWS, ROWS), 1))
    out = nn(pick, returned_ref[0])
    for piece in range(1, returned_ref.shape[0]):
        out = out + nn(pick, returned_ref[piece])
    return out


def spread_rows(pos_row, rows_low):
    return nn(onehot(iota((ROWS, IMGROWS), 0) == pos_row), rows_low)


def route(second_low, router, pos_col):
    logits = nn(second_low, router)
    lane = iota(logits.shape, 1)
    logits = jnp.where(lane < EXPERTS, logits, -1e30)
    expo = jnp.exp(logits - jnp.max(logits, -1, keepdims=True))
    probs = expo / jnp.sum(expo, -1, keepdims=True)
    expert = jnp.where(pos_col >= 0, pos_col // SLOTS, -1)
    chosen = jnp.where(lane == expert, 1.0, 0.0)
    return probs, chosen, jnp.sum(probs * chosen, -1, keepdims=True)


def head_masks():
    rows = iota((LANES, LANES), 0) // HEAD_DIM
    return [onehot(rows == h) for h in range(GROUP)]


def lane_masks():
    lane = iota((WPAD, LANES), 1)
    return [onehot(lane < WPAD), onehot(lane >= WPAD)]


def place_columns(target, shards_ref, count, transposed):
    size = shards_ref.shape[-1]
    target[...] = jnp.zeros(target.shape, target.dtype)
    for m in range(count):
        start = m * size // LANES * LANES
        stop = -(-(m + 1) * size // LANES) * LANES
        span = stop - start
        if transposed:
            put = onehot(iota((span, size), 0) + start == iota((span, size), 1) + m * size)
            target[start:stop, :] += nt(put, shards_ref[m]).astype(bf16)
        else:
            put = onehot(iota((size, span), 0) + m * size == iota((size, span), 1) + start)
            target[:, start:stop] += nn(shards_ref[m], put).astype(bf16)


def attention_forward_kernel(first, shifted, mp, gather, *refs):
    refs = list(refs)
    if first:
        patches_ref, enter_ref = refs[:2]
        refs = refs[2:]
    else:
        prev_ref, prev_gate_ref, returned_ref = refs[:3]
        refs = refs[3:]
    (
        valid_ref, col_ref, row_ref, qkv_ref, proj_ref, bias_ref, move_ref, back_ref, gain_ref, nbias_ref, router_ref,
    ) = refs[:11]
    bias_ref, gain_ref, nbias_ref, router_ref = (ref.at[0] for ref in (bias_ref, gain_ref, nbias_ref, router_ref))
    refs = refs[11:]
    if gather:
        core_up_ref, core_down_ref = refs[:2]
        refs = refs[2:]
    carried_ref = refs.pop(0)
    expert_out_ref = None if first else refs.pop(0)
    (
        middle_ref, second_ref, gate_ref, buffer_ref, window_ref, qk_ref, v_ref, probs_ref, att_ref, qkv_full, proj_full,
    ) = refs[:11]
    refs = refs[11:]
    if gather:
        up_out, down_out = refs[:2]
        refs = refs[2:]
    qkv_turned, total_ref = refs[:2]
    image = pl.program_id(0)
    width = carried_ref.shape[-1]
    if gather:
        shards = [ref.at[0] for ref in (qkv_ref, proj_ref, core_up_ref, core_down_ref)]
        qkv_ref, proj_ref = refs[2:4]
        moving = WeightGather(shards, [qkv_ref, proj_ref, up_out, down_out], refs[4:])

        @pl.when(image == 0)
        def _():
            pl.semaphore_wait(moving.row.greet(), 2)
            for k in (0, 1):
                moving.start(k)
            for k in (0, 1):
                moving.forward(k)
            for k in (2, 3):
                moving.start(k)
            for k in (0, 1):
                moving.arrive(k)

        @pl.when(image == pl.num_programs(0) - 1)
        def _():
            for k in (2, 3):
                moving.forward(k)

    @pl.when(image == 0)
    def _():
        place_columns(qkv_full, qkv_ref, mp, False)
        place_columns(qkv_turned, qkv_ref, mp, True)
        place_columns(proj_full, proj_ref, mp, False)
        total_ref[...] = jnp.zeros(total_ref.shape, f32)

    pos_col = col_ref[0, :, 0:1]
    pos_row = row_ref[0, 0:1, :]
    if first:
        x = nn(enter_ref[...], patches_ref[0])
    else:
        expert_out = collect(pos_col, returned_ref)
        expert_out_ref[0] = expert_out
        x = prev_ref[0] + prev_gate_ref[0] * expert_out
    carried_ref[0] = x
    xhat, _ = norm_parts(x)
    normed = (xhat * gain_ref[0:1, :] + nbias_ref[0:1, :]).astype(bf16)
    window_in = nn(move_ref[...], normed).astype(bf16)
    window_ref[0] = window_in
    turned = nt(qkv_turned[...], window_in).astype(bf16)
    straight = nn(window_in, qkv_full[:, width:]).astype(bf16)
    qk_ref[0] = turned[: 2 * width]
    v_ref[0] = straight[:, width:]
    heads_rows = head_masks()
    halves = lane_masks()
    low_lane = iota((WPAD, LANES), 1) < WPAD
    for pair in range(PAIRS):
        across = slice(pair * LANES, (pair + 1) * LANES)
        if shifted:
            ahead = col_ref[0, pair * LANES : pair * LANES + WPAD, 1:2]
            behind = col_ref[0, pair * LANES + WPAD : (pair + 1) * LANES, 1:2]
            key_label = jnp.where(low_lane, ahead, behind)
            mask = jnp.where(key_label == row_ref[0, 1:2, across], 0.0, mask_fill)
        for group in range(HEADS // GROUP):
            features = slice(group * LANES, (group + 1) * LANES)
            queries = turned[features, across]
            spread = jnp.concatenate([queries * heads_rows[h] for h in range(GROUP)], 1)
            raw = nn(straight[across, features], spread)
            for h in range(GROUP):
                head = group * GROUP + h
                part = raw[:, h * LANES : (h + 1) * LANES]
                scores = jnp.where(low_lane, part[:WPAD], part[WPAD:]) * head_scale + bias_ref[head]
                if shifted:
                    scores = scores + mask
                expo = jnp.exp(scores - jnp.max(scores, 0, keepdims=True))
                probs = (expo * (1.0 / jnp.sum(expo, 0, keepdims=True))).astype(bf16)
                probs_ref[0, pair * HEADS + head] = probs
                both = jnp.concatenate([probs * halves[0], probs * halves[1]], 0)
                at = slice(head * HEAD_DIM, (head + 1) * HEAD_DIM)
                values = turned[2 * width + head * HEAD_DIM : 2 * width + (head + 1) * HEAD_DIM, across]
                att_ref[0, at, across] = nn(values, both).astype(bf16)
    attended = nt(back_ref[...], att_ref[0]).astype(bf16)
    middle = x + valid_ref[image].astype(f32) * nn(attended, proj_full[...])
    middle_ref[0] = middle
    xhat, _ = norm_parts(middle)
    second_low = (xhat * gain_ref[1:2, :] + nbias_ref[1:2, :]).astype(bf16)
    second_ref[0] = second_low
    _, _, gate = route(second_low, router_ref[...], pos_col)
    gate_ref[0] = gate
    total_ref[...] += spread_rows(pos_row, second_low)

    @pl.when(image == pl.num_programs(0) - 1)
    def _():
        buffer_ref[...] = total_ref[...].astype(bf16)
        if gather:
            for k in (2, 3):
                moving.arrive(k)
            for k in range(4):
                moving.sent(k)


def image_spec(array_shape):
    rest = tuple(array_shape[1:])
    zeros = (0,) * len(rest)
    return pl.BlockSpec((1,) + rest, lambda i: (i,) + zeros)


def whole_spec(array_shape):
    zeros = (0,) * len(array_shape)
    return pl.BlockSpec(tuple(array_shape), lambda i: zeros)


def image_call(kernel, images, arrays, outs, scratch, name, collective_id=None):
    def spec(kind, shape):
        if isinstance(kind, int):
            rest = tuple(shape[1:])
            return pl.BlockSpec((1,) + rest, lambda i: (kind,) + (0,) * len(rest))
        if kind in ("smem", "any"):
            return pl.BlockSpec(memory_space=pltpu.SMEM if kind == "smem" else pl.ANY)
        return image_spec(shape) if kind == "image" else whole_spec(shape)

    return pl.pallas_call(
        kernel,
        grid=(images,),
        out_shape=[jax.ShapeDtypeStruct(shape, dtype) for _, shape, dtype in outs],
        in_specs=[spec(kind, array.shape) for kind, array in arrays],
        out_specs=[spec(kind, shape) for kind, shape, _ in outs],
        scratch_shapes=scratch,
        compiler_params=pltpu.CompilerParams(
            vmem_limit_bytes=56 * MIB,
            dimension_semantics=("arbitrary",),
            collective_id=collective_id,
            has_side_effects=collective_id is not None,
        ),
        name=name,
    )(*[array for _, array in arrays])


def send_part(g, expert_out, second_low, router, pos_col, pos_row, logit_ref, router_grad_ref, total_ref):
    probs, chosen, gate = route(second_low, router, pos_col)
    gate_grad = jnp.where(pos_col >= 0, jnp.sum(g * expert_out, -1, keepdims=True), 0.0)
    sent = (gate * g).astype(bf16)
    logit_grad = gate_grad * gate * (chosen - probs)
    logit_ref[0] = logit_grad
    high, low = split_two(logit_grad)
    router_grad_ref[...] += tn(high, second_low) + tn(low, second_low)
    total_ref[...] += spread_rows(pos_row, sent)


def turn_kernel(
    prev_ref, gate_ref, returned_ref, cotangent_ref, enter_ref, leave_ref, col_ref, row_ref, second_ref, router_ref,
    block_ref, grad_ref, logit_ref, router_grad_ref, buffer_ref, total_ref,
):
    image = pl.program_id(0)

    @pl.when(image == 0)
    def _():
        total_ref[...] = jnp.zeros(total_ref.shape, f32)
        router_grad_ref[...] = jnp.zeros(router_grad_ref.shape, f32)

    pos_col = col_ref[0, :, 0:1]
    expert_out = collect(pos_col, returned_ref)
    x = prev_ref[0] + gate_ref[0] * expert_out
    block_ref[0] = nn(leave_ref[...], x.astype(bf16)).astype(bf16)
    g = nn(enter_ref[...], cotangent_ref[0])
    grad_ref[0] = g
    send_part(
        g, expert_out, second_ref[0], router_ref[0], pos_col, row_ref[0, 0:1, :], logit_ref, router_grad_ref, total_ref
    )

    @pl.when(image == pl.num_programs(0) - 1)
    def _():
        buffer_ref[...] = total_ref[...].astype(bf16)


def attention_backward_kernel(last, mp, fast, *refs):
    (
        valid_ref, grad_ref, returned_ref, logit_ref, middle_ref, carried_ref, router_ref, col_ref, move_ref, back_ref,
        gain_ref, proj_ref, qkv_ref, window_ref, qk_ref, v_ref, probs_ref, att_ref,
    ) = refs[:18]
    refs = refs[18:]
    refs = list(refs)
    if fast:
        units_ref = refs.pop(0)
    if last:
        leave_ref = refs.pop(0)
    else:
        row_ref, expert_out_ref, second_ref, router_next_ref = refs[:4]
        refs = refs[4:]
    out_ref = refs.pop(0)
    if fast:
        unit_ref, mine_ref = refs[:2]
        refs = refs[2:]
    else:
        qkv_grad_ref, proj_grad_ref = refs[:2]
        refs = refs[2:]
    table_ref, small_ref = refs[:2]
    refs = refs[2:]
    if not last:
        logit_out_ref, router_grad_ref, buffer_ref = refs[:3]
        refs = refs[3:]
    turned = refs.pop(0)
    if fast:
        qkv_grad_ref, proj_grad_ref = refs[:2]
        refs = refs[2:]
    if not last:
        total_ref = refs.pop(0)
    image = pl.program_id(0)
    if fast:
        row = Row()
        sums = RowSum(
            row, [units_ref.at[k] for k in range(2)], refs[0], refs[1], refs[2], [mine_ref.at[k] for k in range(2)],
            refs[3:7],
        )

        @pl.when(image == 0)
        def _():
            pl.semaphore_wait(row.greet(), 2)
            for k in range(2):
                sums.start(k)

        @pl.when(image == 1)
        def _():
            for k in range(2):
                sums.middle(k)

    width = carried_ref.shape[-1]

    @pl.when(image == 0)
    def _():
        qkv_grad_ref[...] = jnp.zeros(qkv_grad_ref.shape, f32)
        proj_grad_ref[...] = jnp.zeros(proj_grad_ref.shape, f32)
        table_ref[...] = jnp.zeros(table_ref.shape, f32)
        small_ref[...] = jnp.zeros(small_ref.shape, f32)
        if not last:
            total_ref[...] = jnp.zeros(total_ref.shape, f32)
            router_grad_ref[...] = jnp.zeros(router_grad_ref.shape, f32)

    pos_col = col_ref[0, :, 0:1]
    g = grad_ref[0]
    high, low = split_two(logit_ref[0])
    gain_ref, router = gain_ref.at[0], router_ref[0]
    normed_grad = collect(pos_col, returned_ref) + nt(high, router) + nt(low, router)
    xhat, rstd = norm_parts(middle_ref[0])
    small_ref[1:2, :] += jnp.sum(normed_grad * xhat, 0, keepdims=True)
    small_ref[3:4, :] += jnp.sum(normed_grad, 0, keepdims=True)
    middle_grad = g + norm_back(normed_grad, gain_ref[1:2, :], xhat, rstd)
    branch_grad = (valid_ref[image].astype(f32) * middle_grad).astype(bf16)
    branch_grad = nn(move_ref[...], branch_grad).astype(bf16)
    proj_grad_ref[...] += nn(att_ref[0], branch_grad)
    att_grad = nt(proj_ref[...], branch_grad).astype(bf16)
    heads_rows = head_masks()
    halves = lane_masks()
    low_lane = iota((WPAD, LANES), 1) < WPAD
    for pair in range(PAIRS):
        across = slice(pair * LANES, (pair + 1) * LANES)
        for group in range(HEADS // GROUP):
            features = slice(group * LANES, (group + 1) * LANES)
            grads = att_grad[features, across]
            spread = jnp.concatenate([grads * heads_rows[h] for h in range(GROUP)], 1)
            raw = nn(v_ref[0, across, features], spread)
            for h in range(GROUP):
                head = group * GROUP + h
                at = slice(head * HEAD_DIM, (head + 1) * HEAD_DIM)
                below = slice(width + head * HEAD_DIM, width + (head + 1) * HEAD_DIM)
                lowest = slice(2 * width + head * HEAD_DIM, 2 * width + (head + 1) * HEAD_DIM)
                part = raw[:, h * LANES : (h + 1) * LANES]
                probs_grad = jnp.where(low_lane, part[:WPAD], part[WPAD:])
                probs_low = probs_ref[0, pair * HEADS + head]
                probs = probs_low.astype(f32)
                weighted = probs * probs_grad
                scores_grad = weighted - probs * jnp.sum(weighted, 0, keepdims=True)
                table_ref[head] += scores_grad
                scores_low = scores_grad.astype(bf16)
                both = jnp.concatenate([scores_low * halves[0], scores_low * halves[1]], 0)
                probs_both = jnp.concatenate([probs_low * halves[0], probs_low * halves[1]], 0)
                turned[at, across] = (nn(qk_ref[0, below, across], both) * head_scale).astype(bf16)
                turned[below, across] = (nt(qk_ref[0, at, across], both) * head_scale).astype(bf16)
                turned[lowest, across] = nt(att_grad[at, across], probs_both).astype(bf16)
    qkv_grad_ref[...] += nn(turned[...], window_ref[0])
    mixed_grad = nt(back_ref[...], turned[...]).astype(bf16)
    first_grad = nt(mixed_grad, qkv_ref[...])
    xhat, rstd = norm_parts(carried_ref[0])
    small_ref[0:1, :] += jnp.sum(first_grad * xhat, 0, keepdims=True)
    small_ref[2:3, :] += jnp.sum(first_grad, 0, keepdims=True)
    out = middle_grad + norm_back(first_grad, gain_ref[0:1, :], xhat, rstd)
    if fast:

        @pl.when(image == pl.num_programs(0) - 1)
        def _():
            columns, rows = 3 * width // mp, width // mp
            proj_turned = proj_grad_ref[...].T
            for place in range(mp):
                q = quarter_at(place, mp)
                unit_ref[place, :columns] = qkv_grad_ref[q * columns : (q + 1) * columns].astype(bf16)
                unit_ref[place, columns:] = proj_turned[q * rows : (q + 1) * rows].astype(bf16)
            for k in range(2):
                sums.end(k)
                sums.finish(k)

    if last:
        top = out.astype(bf16)
        rest = out - top.astype(f32)
        mid, low = split_two(rest)
        leave = leave_ref[...]
        out_ref[0] = nn(leave, top) + nn(leave, mid) + nn(leave, low)
        return
    out_ref[0] = out
    send_part(
        out, expert_out_ref[0], second_ref[0], router_next_ref[0], pos_col, row_ref[0, 0:1, :], logit_out_ref,
        router_grad_ref, total_ref,
    )

    @pl.when(image == pl.num_programs(0) - 1)
    def _():
        buffer_ref[...] = total_ref[...].astype(bf16)


def quarter_at(place, mp):
    return place % (mp // 2) * 2 + place // (mp // 2)


def add_up(*parts):
    total = parts[0].astype(f32)
    for part in parts[1:]:
        total = total + part.astype(f32)
    return total


def to_row(source, target, sems, k, row):
    return pltpu.make_async_remote_copy(
        src_ref=source,
        dst_ref=target,
        send_sem=sems[0].at[k],
        recv_sem=sems[1].at[k],
        device_id={"mp": row},
        device_id_type=MESH,
    )


class Row:
    def __init__(self):
        row = lax.axis_index("mp")
        self.row, self.core, self.y = row, lax.rem(row, 2), lax.div(row, 2)
        self.sibling, self.across = row + 1 - 2 * self.core, row + 2 - 4 * self.y
        self.place = self.core * 2 + self.y
        self.place_across = self.core * 2 + 1 - self.y

    def greet(self):
        barrier = pltpu.get_barrier_semaphore()
        for row in (self.sibling, self.across):
            pl.semaphore_signal(barrier, inc=1, device_id={"mp": row}, device_id_type=MESH)
        return barrier


class RowSum:
    semaphores = 4

    def __init__(self, row, units, core_in, y_out, y_in, mine, sems):
        self.row, self.units, self.mine = row, units, mine
        self.core_in, self.y_out, self.y_in = core_in, y_out, y_in
        self.sems = (sems[:2], sems[2:])

    def pair(self, k):
        theirs = self.units[k].at[pl.ds(2 * (1 - self.row.core), 2)]
        return to_row(theirs, self.core_in.at[k], self.sems[0], k, self.row.sibling)

    def cross(self, k):
        return to_row(self.y_out.at[k], self.y_in.at[k], self.sems[1], k, self.row.across)

    def start(self, k):
        self.pair(k).start()

    def middle(self, k):
        self.pair(k).wait_recv()
        other = 1 - self.row.y
        mixed = add_up(self.units[k][self.row.core * 2 + other], self.core_in[k, other])
        self.y_out[k] = mixed.astype(bf16)
        self.cross(k).start()

    def end(self, k):
        self.cross(k).wait_recv()
        self.mine[k][...] = add_up(
            self.units[k][self.row.place], self.core_in[k, self.row.y], self.y_in[k]
        ).astype(bf16)

    def finish(self, k):
        self.pair(k).wait_send()
        self.cross(k).wait_send()

    @classmethod
    def scratch(cls, count, width):
        return [
            pltpu.VMEM((count, 2, width, width), bf16),
            pltpu.VMEM((count, width, width), bf16),
            pltpu.VMEM((count, width, width), bf16),
        ] + [pltpu.SemaphoreType.DMA((count,))] * cls.semaphores


class RowGather:
    semaphores = 6

    def __init__(self, row, sources, fulls, slot, slot_across, sems):
        self.row, self.sources, self.fulls = row, sources, fulls
        self.slot, self.slot_across = slot, slot_across
        self.sems = (sems[:2], sems[2:4], sems[4:])

    def over(self, k):
        return to_row(self.sources[k], self.fulls[k].at[self.slot], self.sems[0], k, self.row.across)

    def near(self, k):
        return to_row(self.sources[k], self.fulls[k].at[self.slot], self.sems[1], k, self.row.sibling)

    def onward(self, k):
        block = self.fulls[k].at[self.slot_across]
        return to_row(block, block, self.sems[2], k, self.row.sibling)

    def start(self, k):
        self.over(k).start()
        self.near(k).start()

    def forward(self, k):
        self.over(k).wait_recv()
        self.onward(k).start()

    def arrive(self, k):
        self.near(k).wait_recv()
        self.onward(k).wait_recv()

    def sent(self, k):
        self.over(k).wait_send()
        self.near(k).wait_send()
        self.onward(k).wait_send()

    @classmethod
    def scratch(cls, count):
        return [pltpu.SemaphoreType.DMA((count,))] * cls.semaphores


class WeightGather(RowGather):
    def __init__(self, shards, fulls, sems):
        row = Row()
        super().__init__(row, shards, fulls, row.row, row.across, sems[:6])
        self.own_sem = sems[6]

    def own(self, k):
        return pltpu.make_async_copy(self.sources[k], self.fulls[k].at[self.slot], self.own_sem.at[k])

    def start(self, k):
        super().start(k)
        self.own(k).start()

    def arrive(self, k):
        super().arrive(k)
        self.own(k).wait()

    @classmethod
    def scratch(cls, count):
        return super().scratch(count) + [pltpu.SemaphoreType.DMA((count,))]


def closing_kernel(
    dp, mp, given_ref, attn_ref, small_ref, full_ref, shard_ref, small_out, core_in, y_out, y_in, a0, a1, b0, b1, g0, g1, g2,
    g3, g4, g5, mine, x_in, half, z_in, s_core, s_one, s_y, s_mine, s_x, s_half, s_z, s0, s1, s2, s3, x0, x1, z0, z1, w0, w1,
    v0, v1,
):
    me = lax.axis_index("dp")
    x, z = lax.rem(me, 2), lax.div(me, 2)
    deep = dp // 2
    partner = me + 1 - 2 * x
    row = Row()
    sums = RowSum(row, [attn_ref], core_in, y_out, y_in, [mine], (a0, a1, b0, b1))
    gather = RowGather(
        row, [given_ref.at[0], given_ref.at[1]], [full_ref.at[0], full_ref.at[1]], row.place, row.place_across,
        (g0, g1, g2, g3, g4, g5),
    )
    barrier = row.greet()
    pl.semaphore_signal(barrier, inc=1, device_id={"dp": partner}, device_id_type=MESH)
    for off in range(1, deep):
        peer = lax.rem(z + off, deep) * 2 + x
        pl.semaphore_signal(barrier, inc=1, device_id={"dp": peer}, device_id_type=MESH)
    pl.semaphore_wait(barrier, 3 + deep - 1)

    s_pair = to_row(small_ref, s_core, (s0, s1), 0, row.sibling)
    s_cross = to_row(s_one, s_y, (s2, s3), 0, row.across)
    early, late, every = (0, 1), (2, 3), (0, 1, 2, 3)
    total = [given_ref.at[0], given_ref.at[1], mine, s_mine]
    arrived = [x_in.at[k] for k in range(3)] + [s_x]
    halves = [half.at[k] for k in range(3)] + [s_half]
    slots = [z_in.at[k] for k in range(3)] + [s_z]
    result = [shard_ref.at[k] for k in range(3)] + [small_out]

    def cut(k):
        height = total[k].shape[0] // 2
        return height, height // deep

    def over_x(k):
        height, _ = cut(k)
        away = total[k].at[pl.ds(pl.multiple_of((1 - x) * height, height), height)]
        return to_peer(away, arrived[k], x0.at[k], x1.at[k], partner)

    def over_z(k, off):
        _, piece = cut(k)
        to = lax.rem(z + off, deep)
        part = halves[k].at[pl.ds(pl.multiple_of(to * piece, piece), piece)]
        return to_peer(part, slots[k].at[off], z0.at[k, off], z1.at[k, off], to * 2 + x)

    def own_piece(k):
        height, piece = cut(k)
        return result[k].at[pl.ds(pl.multiple_of(x * height + z * piece, piece), piece)]

    def own_half(k):
        height, _ = cut(k)
        return result[k].at[pl.ds(pl.multiple_of(x * height, height), height)]

    def back_z(k, off):
        to = lax.rem(z + off, deep)
        return to_peer(own_piece(k), own_piece(k), w0.at[k, off], w1.at[k, off], to * 2 + x)

    def back_x(k):
        return to_peer(own_half(k), own_half(k), v0.at[k], v1.at[k], partner)

    def halve(k):
        over_x(k).wait_recv()
        height, _ = cut(k)
        keep = total[k][pl.ds(pl.multiple_of(x * height, height), height)]
        halves[k][...] = add_up(keep, arrived[k][...]).astype(halves[k].dtype)
        for off in range(1, deep):
            over_z(k, off).start()

    def quarter(k):
        for off in range(1, deep):
            over_z(k, off).wait_recv()
        _, piece = cut(k)
        keep = halves[k][pl.ds(pl.multiple_of(z * piece, piece), piece)]
        own_piece(k)[...] = add_up(keep, *[slots[k][off] for off in range(1, deep)]).astype(result[k].dtype)
        for off in range(1, deep):
            back_z(k, off).start()

    def widen(k):
        for off in range(1, deep):
            back_z(k, off).wait_recv()
        back_x(k).start()

    sums.start(0)
    s_pair.start()
    for k in early:
        over_x(k).start()
    sums.middle(0)
    s_pair.wait_recv()
    s_one[...] = small_ref[...] + s_core[...]
    s_cross.start()
    for k in early:
        gather.start(k)
        full_ref[k, row.place] = given_ref[k]
    for k in early:
        halve(k)
    sums.end(0)
    over_x(2).start()
    s_cross.wait_recv()
    s_mine[...] = s_one[...] + s_y[...]
    over_x(3).start()
    for k in early:
        quarter(k)
    for k in late:
        halve(k)
    for k in early:
        widen(k)
    for k in late:
        quarter(k)
    gather.forward(0)
    for k in late:
        widen(k)
    gather.forward(1)
    s_pair.wait_send()
    s_cross.wait_send()
    sums.finish(0)
    for k in early:
        gather.arrive(k)
        gather.sent(k)
    for k in every:
        over_x(k).wait_send()
        for off in range(1, deep):
            over_z(k, off).wait_send()
            back_z(k, off).wait_send()
        back_x(k).wait()


def closing_call(dp, mp, given, attn, small, collective_id):
    width = attn.shape[-1]
    deep = dp // 2
    lines = small.shape[0]
    dma = pltpu.SemaphoreType.DMA
    shape = jax.ShapeDtypeStruct
    scratch = RowSum.scratch(1, width) + RowGather.scratch(2) + [
        pltpu.VMEM((width, width), bf16),
        pltpu.VMEM((3, width // 2, width), bf16),
        pltpu.VMEM((3, width // 2, width), bf16),
        pltpu.VMEM((3, deep, width // dp, width), bf16),
        pltpu.VMEM((lines, width), f32),
        pltpu.VMEM((lines, width), f32),
        pltpu.VMEM((lines, width), f32),
        pltpu.VMEM((lines, width), f32),
        pltpu.VMEM((lines // 2, width), f32),
        pltpu.VMEM((lines // 2, width), f32),
        pltpu.VMEM((deep, lines // dp, width), f32),
        dma((1,)), dma((1,)), dma((1,)), dma((1,)),
        dma((4,)), dma((4,)), dma((4, deep)), dma((4, deep)), dma((4, deep)), dma((4, deep)), dma((4,)), dma((4,)),
    ]
    vmem = pl.BlockSpec(memory_space=pltpu.VMEM)
    return pl.pallas_call(
        functools.partial(closing_kernel, dp, mp),
        out_shape=[shape((2, mp, width, width), bf16), shape((3, width, width), bf16), shape(small.shape, f32)],
        in_specs=[vmem] * 3,
        out_specs=[vmem] * 3,
        scratch_shapes=scratch,
        compiler_params=pltpu.CompilerParams(
            vmem_limit_bytes=56 * MIB, collective_id=collective_id, has_side_effects=True
        ),
        name="closing",
    )(given, attn, small)


def format_kernel(columns, *refs):
    count = (len(refs) - 6) // 2
    fulls, shards = refs[:count], refs[count : 2 * count]
    qkv_out, proj_out, core_up_out, core_down_out, up_out, down_out = refs[2 * count :]
    for layer in range(count):
        full, shard = fulls[layer], shards[layer]
        mp, width = full.shape[1], full.shape[2]
        rows = width // mp
        attn = shard[2].astype(f32).T
        qkv_out[layer] = attn[:, :columns]
        proj_out[layer] = attn[:, columns:]
        core_up_out[layer] = shard[0].astype(f32)
        down = shard[1].astype(f32).T
        for place in range(mp):
            q = quarter_at(place, mp)
            up_out[layer, 0, :, q * width : (q + 1) * width] = full[0, place].astype(f32)
        for chunk in range(mp):
            at = slice(chunk * width, (chunk + 1) * width)
            core_down_out[layer, at, :] = down[:, chunk * rows : (chunk + 1) * rows]
            block = [None] * mp
            for place in range(mp):
                block[quarter_at(place, mp)] = full[1, place, chunk * rows : (chunk + 1) * rows].astype(f32)
            down_out[layer, 0, at, :] = jnp.concatenate(block, 0).T


def format_call(fulls, shards, columns):
    layers = len(fulls)
    _, mp, width, _ = fulls[0].shape
    hidden = mp * width
    shapes = [
        (layers, width, columns),
        (layers, width, width - columns),
        (layers, width, width),
        (layers, hidden, width // mp),
        (layers, 1, width, hidden),
        (layers, 1, hidden, width),
    ]
    return pl.pallas_call(
        functools.partial(format_kernel, columns),
        out_shape=[jax.ShapeDtypeStruct(shape, f32) for shape in shapes],
        in_specs=[pl.BlockSpec(memory_space=pltpu.VMEM)] * (2 * layers),
        out_specs=[pl.BlockSpec(memory_space=pltpu.VMEM)] * len(shapes),
        compiler_params=pltpu.CompilerParams(vmem_limit_bytes=56 * MIB),
        name="format",
    )(*fulls, *shards)


def greet(dp, me, rows=()):
    barrier = pltpu.get_barrier_semaphore()
    for row in rows:
        pl.semaphore_signal(barrier, inc=1, device_id={"mp": row}, device_id_type=MESH)

    def signal(off, carry):
        pl.semaphore_signal(barrier, inc=1, device_id={"dp": lax.rem(me + off, dp)}, device_id_type=MESH)
        return carry

    lax.fori_loop(1, dp, signal, 0)
    pl.semaphore_wait(barrier, dp - 1 + len(rows))


def to_peer(source, target, send_sem, recv_sem, peer):
    return pltpu.make_async_remote_copy(
        src_ref=source,
        dst_ref=target,
        send_sem=send_sem,
        recv_sem=recv_sem,
        device_id={"dp": peer},
        device_id_type=MESH,
    )


def gelu_parts(h):
    root = np.float32(np.sqrt(2.0 / np.pi))
    square = h * h
    t = jnp.tanh(root * h * (1.0 + 0.044715 * square))
    half = 0.5 * (1.0 + t)
    slope = half + 0.5 * h * (1.0 - t * t) * root * (1.0 + 3 * 0.044715 * square)
    return h * half, slope


def expert_forward_kernel(dp, mp, layer, gather, *refs):
    refs = list(refs)
    buffer_ref, up_any, down_any, rup_any, rdown_any = refs[:5]
    refs = refs[5:]
    if gather:
        shards = [ref.at[layer + 1] for ref in refs[:4]]
        refs = refs[4:]
    recv_ref, returned_ref, up_eff, down_eff = refs[:4]
    refs = refs[4:]
    if gather:
        fulls = refs[:4]
        refs = refs[4:]
    part, core, up_ref, down_ref, rup_ref, rdown_ref, local = refs[:7]
    refs = refs[7:]
    moving = WeightGather(shards, fulls, refs[:7]) if gather else None
    send_one, recv_one, send_two, recv_two = refs[-4:]
    split = dp // EXPERTS
    me = lax.axis_index("dp")
    loads = [
        pltpu.make_async_copy(source, target, local.at[k])
        for k, (source, target) in enumerate(
            [
                (up_any, up_ref),
                (rup_any.at[layer, 0], rup_ref),
                (down_any, down_ref),
                (rdown_any.at[layer, 0], rdown_ref),
            ]
        )
    ]
    for load in loads:
        load.start()
    greet(dp, me, (moving.row.sibling, moving.row.across) if gather else ())

    def first(off):
        peer = lax.rem(me + off, dp)
        return to_peer(
            buffer_ref.at[lax.div(peer, split)], recv_ref.at[me], send_one.at[off], recv_one.at[off], peer
        )

    def second(off):
        source = lax.rem(me + dp - off, dp)
        return to_peer(part.at[source], returned_ref.at[me], send_two.at[off], recv_two.at[off], source)

    def start_first(off, carry):
        first(off).start()
        return carry

    lax.fori_loop(1, dp, start_first, 0)
    if gather:
        for k in range(4):
            moving.start(k)
    recv_ref[me] = buffer_ref[lax.div(me, split)]
    hidden = up_eff.shape[1]
    columns = up_ref.shape[-1]
    loads[0].wait()
    loads[1].wait()
    if split == 1 and columns % LANES == 0:
        for m in range(mp):
            at = slice(m * columns, (m + 1) * columns)
            up_eff[:, at] = (up_ref[m].astype(f32) + rup_ref[:, at].astype(f32)).astype(bf16)
    else:
        core[...] = rup_ref[...].astype(f32)
        begin = lax.rem(me, split) * hidden
        for m in range(mp):
            put = onehot(iota((columns, hidden), 0) + m * columns == iota((columns, hidden), 1) + begin)
            core[...] += nn(up_ref[m], put)
        up_eff[...] = core[...].astype(bf16)
    columns = down_ref.shape[-1]
    width = down_eff.shape[1]
    rows = pl.ds(pl.multiple_of(lax.rem(me, split) * hidden, LANES), hidden)
    loads[2].wait()
    loads[3].wait()
    total = rdown_ref[...].astype(f32)
    for m in range(mp):
        put = onehot(iota((columns, width), 0) + m * columns == iota((columns, width), 1))
        total = total + nn(down_ref[m, rows, :], put)
    down_eff[...] = total.astype(bf16)

    def work(source):
        hidden_pre = nn(recv_ref[source], up_eff[...])
        hidden_low = gelu_parts(hidden_pre)[0].astype(bf16)
        return nn(hidden_low, down_eff[...]).astype(bf16)

    returned_ref[me] = work(me)

    def step(off, carry):
        source = lax.rem(me + dp - off, dp)
        first(off).wait_recv()
        part[source] = work(source)
        second(off).start()
        return carry

    lax.fori_loop(1, dp, step, 0)
    if gather:
        for k in range(4):
            moving.forward(k)

    def finish(off, carry):
        first(off).wait_send()
        second(off).wait()
        return carry

    lax.fori_loop(1, dp, finish, 0)
    if gather:
        for k in range(4):
            moving.arrive(k)
            moving.sent(k)


def expert_backward_kernel(dp, mp, fast, reduce, *refs):
    refs = list(refs)
    buffer_ref, recv_ref, up_ref, down_ref = refs[:4]
    refs = refs[4:]
    if reduce:
        given_ref, attn_ref = refs[:2]
        refs = refs[2:]
    returned_ref = refs.pop(0)
    if fast:
        units_ref = refs.pop(0)
    else:
        up_term, down_term = refs[:2]
        refs = refs[2:]
    if reduce:
        full_ref, mine_ref = refs[:2]
        refs = refs[2:]
    grads, hidden_low, slope, pre, part = refs[:5]
    refs = refs[5:]
    if fast:
        up_term, down_term = refs[:2]
        refs = refs[2:]
    row = Row() if reduce else None
    if reduce:
        core_in, y_out, y_in = refs[:3]
        sums = RowSum(row, [attn_ref], core_in, y_out, y_in, [mine_ref], refs[3:7])
        gather = RowGather(
            row, [given_ref.at[k] for k in range(2)], [full_ref.at[k] for k in range(2)], row.place, row.place_across,
            refs[7:13],
        )
        refs = refs[13:]
    send_one, recv_one, send_two, recv_two = refs
    split = dp // EXPERTS
    me = lax.axis_index("dp")
    greet(dp, me, (row.sibling, row.across) if reduce else ())

    def first(off):
        peer = lax.rem(me + off, dp)
        return to_peer(buffer_ref.at[lax.div(peer, split)], grads.at[me], send_one.at[off], recv_one.at[off], peer)

    def second(off):
        source = lax.rem(me + dp - off, dp)
        return to_peer(part.at[source], returned_ref.at[me], send_two.at[off], recv_two.at[off], source)

    def start_first(off, carry):
        first(off).start()
        return carry

    lax.fori_loop(1, dp, start_first, 0)
    if reduce:
        sums.start(0)
        for k in range(2):
            gather.start(k)
    grads[me] = buffer_ref[lax.div(me, split)]

    def again(source, carry):
        value, rate = gelu_parts(nn(recv_ref[source], up_ref[...]))
        hidden_low[source] = value.astype(bf16)
        slope[source] = rate
        return carry

    lax.fori_loop(0, dp, again, 0)
    if reduce:
        sums.middle(0)
        for k in range(2):
            full_ref[k, row.place] = given_ref[k]

    def work(source):
        hidden_grad = nt(grads[source], down_ref[...])
        pre_grad = (slope[source] * hidden_grad).astype(bf16)
        pre[source] = pre_grad
        return nt(pre_grad, up_ref[...]).astype(bf16)

    returned_ref[me] = work(me)

    def step(off, carry):
        source = lax.rem(me + dp - off, dp)
        first(off).wait_recv()
        part[source] = work(source)
        second(off).start()
        return carry

    lax.fori_loop(1, dp, step, 0)
    if reduce:
        for k in range(2):
            gather.forward(k)
        sums.end(0)
    up_term[...] = jnp.zeros(up_term.shape, f32)
    down_term[...] = jnp.zeros(down_term.shape, f32)

    def terms(block, carry):
        up_term[...] += tn(recv_ref[block], pre[block])
        down_term[...] += tn(grads[block], hidden_low[block])
        return carry

    lax.fori_loop(0, dp, terms, 0)
    if fast:
        width = up_term.shape[0]
        height = width // mp
        for place in range(mp):
            q = quarter_at(place, mp)
            units_ref[0, place] = up_term[:, q * width : (q + 1) * width].astype(bf16)
            for chunk in range(mp):
                block = down_term[q * height : (q + 1) * height, chunk * width : (chunk + 1) * width]
                units_ref[1, place, chunk * height : (chunk + 1) * height] = block.astype(bf16)

    def finish(off, carry):
        first(off).wait_send()
        second(off).wait()
        return carry

    lax.fori_loop(1, dp, finish, 0)
    if reduce:
        sums.finish(0)
        for k in range(2):
            gather.arrive(k)
            gather.sent(k)


def expert_call(kernel, arrays, outs, scratch, dp, collective_id, name, flops, anys=(), any_outs=()):
    sems = [pltpu.SemaphoreType.DMA((dp,))] * 4
    vmem, anywhere = pl.BlockSpec(memory_space=pltpu.VMEM), pl.BlockSpec(memory_space=pl.ANY)
    return pl.pallas_call(
        kernel,
        out_shape=[jax.ShapeDtypeStruct(shape, dtype) for shape, dtype in (*outs, *any_outs)],
        in_specs=[vmem] * len(arrays) + [anywhere] * len(anys),
        out_specs=[vmem] * len(outs) + [anywhere] * len(any_outs),
        scratch_shapes=scratch + sems,
        compiler_params=pltpu.CompilerParams(
            vmem_limit_bytes=56 * MIB, collective_id=collective_id, has_side_effects=True
        ),
        cost_estimate=pl.CostEstimate(flops=flops, bytes_accessed=20 * MIB, transcendentals=0),
        name=name,
    )(*arrays, *anys)


def by_windows(grid):
    images, kinds = grid.shape[:2]
    blocks = GRID // WINDOW
    grid = grid.reshape(images, kinds, blocks, WINDOW, blocks, WINDOW).transpose(0, 1, 2, 4, 3, 5)
    grid = grid.reshape(images, kinds, blocks * blocks, WINPOS)
    grid = jnp.pad(grid, ((0, 0), (0, 0), (0, 0), (0, WPAD - WINPOS)), constant_values=-1)
    return grid.reshape(images, kinds, IMGROWS)


def per_device(
    patches,
    qkv_weight,
    proj_weight,
    core_up,
    core_down,
    residual_up,
    residual_down,
    position_bias,
    router_weight,
    norm_gain,
    norm_bias,
    cotangent,
    image_valid,
    expert_index,
    slot_index,
    region_id,
):
    dp, mp = lax.axis_size("dp"), lax.axis_size("mp")
    images, _, width = patches.shape
    split = dp // EXPERTS
    hidden = residual_up.shape[-1]
    hidden_full = core_up.shape[-1] * mp
    row_index = lax.axis_index("mp")

    fast = split == 1 and dp == 8 and mp == 4 and hidden == mp * width
    shards = (qkv_weight, proj_weight, core_up, core_down)
    gathered = [[None] * len(shards)] * LAYERS
    if not fast:
        gathered = [[lax.all_gather(a[l], "mp", axis=0, tiled=False) for a in shards] for l in range(LAYERS)]

    position = jnp.where(slot_index >= 0, expert_index * SLOTS + slot_index, -1)
    labels = jnp.roll(region_id, (-SHIFT, -SHIFT), (1, 2))
    row_form = by_windows(jnp.stack([position.reshape(images, GRID, GRID), labels], 1))
    col_form = row_form.transpose(0, 2, 1)
    enter = jnp.asarray(enter_table(), bf16)
    leave = jnp.asarray(enter_table().T, bf16)
    moves = [jnp.asarray(move_table(l % 2 == 1), bf16) for l in range(LAYERS)]
    backs = [jnp.asarray(move_table(l % 2 == 1).T, bf16) for l in range(LAYERS)]
    entries = jnp.asarray(offset_index().reshape(-1))
    entry_hot = (jnp.arange(OFFSETS + 1)[:, None] == entries[None, :]).astype(f32)
    table_rows = position_bias.transpose(0, 2, 1).reshape(LAYERS * HEADS, OFFSETS)
    padded_rows = jnp.pad(table_rows, ((0, 0), (0, 1)), constant_values=-1e30)
    biases = jnp.dot(padded_rows, entry_hot, precision=highest).reshape(LAYERS, HEADS, WPAD, LANES)
    routers = jnp.pad(router_weight, ((0, 0), (0, 0), (0, LANES - EXPERTS)))

    token = (images, IMGROWS, width)
    buffer_shape = (ROWS, width)
    block_rows = (dp, SLOTS, width)
    pieces = (split, ROWS, width)

    def by_piece(returned):
        return returned.reshape(EXPERTS, split, SLOTS, width).transpose(1, 0, 2, 3).reshape(pieces)

    records = []
    before = None
    for l in range(LAYERS):
        first = l == 0
        gather = fast and first
        if first:
            arrays = [("image", patches), ("whole", enter)]
        else:
            arrays = [("image", before[0]), ("image", before[1]), ("whole", before[2])]
        arrays += [
            ("smem", image_valid),
            ("image", col_form),
            ("image", row_form),
            ("any", qkv_weight) if gather else ("whole", gathered[l][0]),
            ("any", proj_weight) if gather else ("whole", gathered[l][1]),
            (l, biases),
            ("whole", moves[l]),
            ("whole", backs[l]),
            (l, norm_gain),
            (l, norm_bias),
            (l, routers),
        ]
        if gather:
            arrays += [("any", core_up), ("any", core_down)]
        outs = [("image", token, f32)]
        if not first:
            outs.append(("image", token, f32))
        outs += [
            ("image", token, f32),
            ("image", token, bf16),
            ("image", (images, IMGROWS, 1), f32),
            ("whole", buffer_shape, bf16),
            ("image", token, bf16),
            ("image", (images, 2 * width, IMGROWS), bf16),
            ("image", token, bf16),
            ("image", (images, PAIRS * HEADS, WPAD, LANES), bf16),
            ("image", (images, width, IMGROWS), bf16),
            ("whole", (width, 3 * width), bf16),
            ("whole", (width, width), bf16),
        ]
        scratch = [pltpu.VMEM((3 * width, width), bf16), pltpu.VMEM(buffer_shape, f32)]
        gathered_shapes = [(mp, *a.shape[1:]) for a in shards]
        if gather:
            outs += [("any", shape, bf16) for shape in gathered_shapes[2:]]
            scratch += [pltpu.VMEM(shape, bf16) for shape in gathered_shapes[:2]] + WeightGather.scratch(4)
        results = list(
            image_call(
                functools.partial(attention_forward_kernel, first, l % 2 == 1, mp, gather),
                images, arrays, outs, scratch, f"attend_{l}", 3 * LAYERS + 1 if gather else None,
            )
        )
        if gather:
            gathered[l] = [None, None] + results[-2:]
            results = results[:-2]
        carried = results.pop(0)
        if not first:
            records[-1]["expert_out"] = results.pop(0)
        middle, second_low, gate, buffer = results[:4]
        gather = fast and l < LAYERS - 1
        received, returned, up_eff, down_eff, *more = expert_call(
            functools.partial(expert_forward_kernel, dp, mp, l, gather),
            [buffer.reshape(EXPERTS, SLOTS, width)],
            [
                (block_rows, bf16),
                (block_rows, bf16),
                ((width, hidden), bf16),
                ((hidden, width), bf16),
            ],
            [
                pltpu.VMEM(block_rows, bf16),
                pltpu.VMEM((8, LANES) if fast else (width, hidden), f32),
                pltpu.VMEM(gathered_shapes[2], bf16),
                pltpu.VMEM(gathered_shapes[3], bf16),
                pltpu.VMEM((width, hidden), bf16),
                pltpu.VMEM((hidden, width), bf16),
                pltpu.SemaphoreType.DMA((4,)),
            ]
            + (WeightGather.scratch(4) if gather else []),
            dp, l, f"experts_{l}", 4 * dp * SLOTS * width * hidden,
            [gathered[l][2], gathered[l][3], residual_up, residual_down, *(shards if gather else ())],
            [(shape, bf16) for shape in gathered_shapes] if gather else (),
        )
        if gather:
            gathered[l + 1] = more
        returned = by_piece(returned)
        before = (middle, gate, returned)
        records.append(
            dict(
                carried=carried, middle=middle, second_low=second_low, gate=gate, saved=results[4:], received=received,
                up_eff=up_eff, down_eff=down_eff,
            )
        )

    top = records[-1]
    block_output, grad, logit_grad, router_part, buffer = image_call(
        turn_kernel,
        images,
        [
            ("image", before[0]),
            ("image", before[1]),
            ("whole", before[2]),
            ("image", cotangent),
            ("whole", enter),
            ("whole", leave),
            ("image", col_form),
            ("image", row_form),
            ("image", top["second_low"]),
            (LAYERS - 1, routers),
        ],
        [
            ("image", patches.shape, bf16),
            ("image", token, f32),
            ("image", (images, IMGROWS, LANES), f32),
            ("whole", (LANES, width), f32),
            ("whole", buffer_shape, bf16),
        ],
        [pltpu.VMEM(buffer_shape, f32)],
        "turn",
    )
    router_parts, tables, smalls = [None] * LAYERS, [None] * LAYERS, [None] * LAYERS
    residual_sums, shard_sums = [None] * LAYERS, [None] * LAYERS
    router_parts[LAYERS - 1] = router_part
    units, attn_units, mines = [None] * LAYERS, [None] * LAYERS, [None] * LAYERS
    for l in reversed(range(LAYERS)):
        rec = records[l]
        last = l == 0
        reduce = fast and l < LAYERS - 1
        arrays = [buffer.reshape(EXPERTS, SLOTS, width), rec["received"], rec["up_eff"], rec["down_eff"]]
        outs = [(block_rows, bf16)]
        scratch = [
            pltpu.VMEM(block_rows, bf16),
            pltpu.VMEM((dp, SLOTS, hidden), bf16),
            pltpu.VMEM((dp, SLOTS, hidden), f32),
            pltpu.VMEM((dp, SLOTS, hidden), bf16),
            pltpu.VMEM(block_rows, bf16),
        ]
        if fast:
            outs.append(((2, mp, width, width), bf16))
            scratch += [pltpu.VMEM((width, hidden), f32)] * 2
        else:
            outs += [((width, hidden), f32)] * 2
        if reduce:
            arrays += [mines[l + 1], attn_units[l + 1]]
            outs += [((2, mp, width, width), bf16), ((width, width), bf16)]
            scratch += RowSum.scratch(1, width) + RowGather.scratch(2)
        results = list(
            expert_call(
                functools.partial(expert_backward_kernel, dp, mp, fast, reduce), arrays, outs, scratch, dp, LAYERS + l,
                f"experts_back_{l}", 10 * dp * SLOTS * width * hidden,
            )
        )
        returned_grad = results.pop(0)
        if fast:
            units[l] = results.pop(0)
        else:
            residual_sums[l] = lax.psum(tuple(t.astype(bf16) for t in results[:2]), "mp")
        if reduce:
            full_above, mine_above = results
            shard_above = lax.psum(jnp.concatenate([mines[l + 1], mine_above[None]], 0), "dp")
        window_in, qk, v, probs, att, qkv_full, proj_full = rec["saved"]
        arrays = [
            ("smem", image_valid),
            ("image", grad),
            ("whole", by_piece(returned_grad)),
            ("image", logit_grad),
            ("image", rec["middle"]),
            ("image", rec["carried"]),
            (l, routers),
            ("image", col_form),
            ("whole", moves[l]),
            ("whole", backs[l]),
            (l, norm_gain),
            ("whole", proj_full),
            ("whole", qkv_full),
            ("image", window_in),
            ("image", qk),
            ("image", v),
            ("image", probs),
            ("image", att),
        ]
        outs = [("image", patches.shape if last else token, f32)]
        scratch = [pltpu.VMEM((3 * width, IMGROWS), bf16)]
        if fast:
            arrays.append(("whole", units[l]))
            outs += [("whole", (mp, width, width), bf16), ("whole", (2, width, width), bf16)]
            scratch += [pltpu.VMEM((3 * width, width), f32), pltpu.VMEM((width, width), f32)]
        else:
            outs += [("whole", (3 * width, width), f32), ("whole", (width, width), f32)]
        outs += [("whole", (HEADS, WPAD, LANES), f32), ("whole", (8, width), f32)]
        if last:
            arrays.append(("whole", leave))
        else:
            below = records[l - 1]
            arrays += [
                ("image", row_form),
                ("image", below["expert_out"]),
                ("image", below["second_low"]),
                (l - 1, routers),
            ]
            outs += [
                ("image", (images, IMGROWS, LANES), f32),
                ("whole", (LANES, width), f32),
                ("whole", buffer_shape, bf16),
            ]
            scratch.append(pltpu.VMEM(buffer_shape, f32))
        if fast:
            scratch += RowSum.scratch(2, width)
        results = list(
            image_call(
                functools.partial(attention_backward_kernel, last, mp, fast),
                images, arrays, outs, scratch, f"attend_back_{l}", 2 * LAYERS + 1 + l if fast else None,
            )
        )
        grad = results.pop(0)
        if fast:
            attn_units[l], mines[l] = results[:2]
            results = results[2:]
        else:
            qkv_part, proj_part = results[:2]
            results = results[2:]
        tables[l], smalls[l] = results[:2]
        if not last:
            logit_grad, router_parts[l - 1], buffer = results[2:]
        if fast:
            continue
        attn = (
            lax.psum_scatter(qkv_part.astype(bf16), "mp", scatter_dimension=0, tiled=True),
            lax.psum_scatter(proj_part.T.astype(bf16), "mp", scatter_dimension=0, tiled=True),
        )
        up_sum, down_sum = residual_sums[l]
        if split > 1:
            begin = lax.axis_index("dp") % split * hidden
            empty = jnp.zeros((width, hidden_full), bf16)
            up_sum = lax.dynamic_update_slice_in_dim(empty, up_sum, begin, 1)
            down_sum = lax.dynamic_update_slice_in_dim(empty, down_sum, begin, 1)
        up_columns, down_columns = core_up.shape[-1], core_down.shape[-1]
        up_shard = lax.dynamic_slice_in_dim(up_sum, row_index * up_columns, up_columns, 1)
        down_shard = lax.dynamic_slice_in_dim(down_sum, row_index * down_columns, down_columns, 0)
        shard_sums[l] = lax.psum((attn[0], attn[1], up_shard, down_shard), "dp")

    entry_turned = (entries[:, None] == jnp.arange(OFFSETS)[None, :]).astype(f32)
    table_part = jnp.dot(
        jnp.stack(tables, 0).reshape(LAYERS * HEADS, WPAD * LANES), entry_turned, precision=highest
    )
    small_part = jnp.stack(smalls, 0)[:, :4]
    router_part = jnp.stack(router_parts, 0)[:, :EXPERTS]
    if fast:
        lines = jnp.concatenate(
            [
                jnp.pad(table_part, ((0, 0), (0, width - OFFSETS))),
                router_part.reshape(-1, width),
                small_part.reshape(-1, width),
            ],
            0,
        )
        count = -(-lines.shape[0] // 64) * 64
        full, closed, lines = closing_call(
            dp, mp, mines[0], attn_units[0], jnp.pad(lines, ((0, count - lines.shape[0]), (0, 0))), 2 * LAYERS
        )
        *attn_grads, core_up_grad, core_down_grad, residual_up_grad, residual_down_grad = format_call(
            [full, full_above], [closed, shard_above], qkv_weight.shape[-1]
        )
        core_grads = (core_up_grad, core_down_grad)
        at = LAYERS * HEADS
        table_sum = lines[:at, :OFFSETS]
        router_sum = lines[at : at + LAYERS * EXPERTS].reshape(LAYERS, EXPERTS, width)
        at += LAYERS * EXPERTS
        small_sum = lines[at : at + LAYERS * 4].reshape(LAYERS, 4, width)
    else:
        table_sum, small_sum, router_sum = lax.psum((table_part, small_part, router_part), ("dp", "mp"))

        def shard(k):
            return jnp.stack([shard_sums[l][k] for l in range(LAYERS)], 0).astype(f32)

        attn_grads = (shard(0).transpose(0, 2, 1), shard(1).transpose(0, 2, 1))
        core_grads = (shard(2), shard(3).transpose(0, 2, 1))
        residual_up_grad, residual_down_grad = (
            jnp.stack([residual_sums[l][k] for l in range(LAYERS)], 0).astype(f32) for k in range(2)
        )
        residual_up_grad = residual_up_grad[:, None]
        residual_down_grad = residual_down_grad.transpose(0, 2, 1)[:, None]

    return (
        block_output,
        grad,
        attn_grads[0],
        attn_grads[1],
        core_grads[0],
        core_grads[1],
        residual_up_grad,
        residual_down_grad,
        table_sum.reshape(LAYERS, HEADS, OFFSETS).transpose(0, 2, 1),
        router_sum.transpose(0, 2, 1),
        small_sum[:, 0:2],
        small_sum[:, 2:4],
    )


def solution(mesh):
    placed = (
        P(("dp", "mp"), None, None),
        P(None, None, "mp"),
        P(None, None, "mp"),
        P(None, None, "mp"),
        P(None, None, "mp"),
        P(None, "dp", None, None),
        P(None, "dp", None, None),
        P(),
        P(),
        P(),
        P(),
        P(("dp", "mp"), None, None),
        P(("dp", "mp")),
        P(("dp", "mp"), None),
        P(("dp", "mp"), None),
        P(("dp", "mp"), None, None),
    )
    return jax.shard_map(
        per_device,
        mesh=mesh,
        in_specs=placed,
        out_specs=(
            P(("dp", "mp"), None, None),
            P(("dp", "mp"), None, None),
            P(None, None, "mp"),
            P(None, None, "mp"),
            P(None, None, "mp"),
            P(None, None, "mp"),
            P(None, "dp", None, None),
            P(None, "dp", None, None),
            P(),
            P(),
            P(),
            P(),
        ),
        check_vma=False,
    )
```

```python
import functools

import jax
import jax.numpy as jnp
import numpy as np
from jax import lax
from jax.experimental import pallas as pl
from jax.experimental.pallas import tpu as pltpu
from jax.sharding import PartitionSpec as P

HEADS = 12
HEAD_DIM = 32
EXPERTS = 8
WINDOW = 7
GRID = 14
SHIFT = 3
LAYERS = 2
WINPOS = 49
OFFSETS = 169
CAP = 122

WPAD = 64
IMGROWS = 256
PATCHES = 196
SLOTS = 128
ROWS = EXPERTS * SLOTS
LANES = 128
GROUP = 4
PAIRS = 2

bf16 = jnp.bfloat16
f32 = jnp.float32
highest = lax.Precision.HIGHEST
norm_epsilon = 1e-05
mask_fill = -100.0
head_scale = HEAD_DIM ** (-0.5)
MESH = pl.DeviceIdType.MESH
MIB = 1024 * 1024


def nn(a, b):
    return lax.dot_general(a, b, (((1,), (0,)), ((), ())), preferred_element_type=f32)


def nt(a, b):
    return lax.dot_general(a, b, (((1,), (1,)), ((), ())), preferred_element_type=f32)


def tn(a, b):
    return lax.dot_general(a, b, (((0,), (0,)), ((), ())), preferred_element_type=f32)


def iota(shape, dim):
    return lax.broadcasted_iota(jnp.int32, shape, dim)


def onehot(flags):
    return jnp.where(flags, 1.0, 0.0).astype(bf16)


def natural_of_row(shifted):
    moved = SHIFT if shifted else 0
    blocks = GRID // WINDOW
    out = -np.ones(IMGROWS, np.int32)
    for window in range(blocks * blocks):
        for cell in range(WINPOS):
            row = (window // blocks * WINDOW + cell // WINDOW + moved) % GRID
            col = (window % blocks * WINDOW + cell % WINDOW + moved) % GRID
            out[window * WPAD + cell] = row * GRID + col
    return out


def enter_table():
    held = natural_of_row(False)
    return (held[:, None] == np.arange(PATCHES)[None, :]).astype(np.float32)


def move_table(shifted):
    first, second = natural_of_row(False), natural_of_row(shifted)
    same = (second[:, None] == first[None, :]) & (second[:, None] >= 0)
    return same.astype(np.float32)


def offset_index():
    key = np.arange(WPAD)[:, None]
    query = np.arange(LANES)[None, :] % WPAD
    entry = (
        (query // WINDOW - key // WINDOW + WINDOW - 1) * (2 * WINDOW - 1)
        + query % WINDOW
        - key % WINDOW
        + WINDOW
        - 1
    )
    real = (key < WINPOS) & (query < WINPOS)
    return np.where(real, entry, np.where(key < WINPOS, -1, OFFSETS)).astype(np.int32)


def norm_parts(x):
    width = x.shape[-1]
    center = x - jnp.sum(x, -1, keepdims=True) * (1.0 / width)
    spread = jnp.sum(center * center, -1, keepdims=True) * (1.0 / width)
    rstd = lax.rsqrt(spread + norm_epsilon)
    return center * rstd, rstd


def norm_back(grad, gain, xhat, rstd):
    width = xhat.shape[-1]
    dxhat = grad * gain
    mean_one = jnp.sum(dxhat, -1, keepdims=True) * (1.0 / width)
    mean_two = jnp.sum(dxhat * xhat, -1, keepdims=True) * (1.0 / width)
    return rstd * (dxhat - mean_one - xhat * mean_two)


def split_two(x):
    high = x.astype(bf16)
    return high, (x - high.astype(f32)).astype(bf16)


def collect(pos_col, returned_ref):
    pick = onehot(pos_col == iota((pos_col.shape[0], ROWS), 1))
    out = nn(pick, returned_ref[0])
    for piece in range(1, returned_ref.shape[0]):
        out = out + nn(pick, returned_ref[piece])
    return out


def join(ref):
    return ref[...].reshape(ref.shape[0] * ref.shape[1], *ref.shape[2:])


def store(ref, rows):
    ref[...] = rows.reshape(ref.shape).astype(ref.dtype)


def per_image(function, count):
    return jnp.concatenate([function(i) for i in range(count)], 0)


def image_rows(i):
    return slice(i * IMGROWS, (i + 1) * IMGROWS)


def lay_positions(row_ref):
    return jnp.concatenate([row_ref[i, 0:1, :] for i in range(row_ref.shape[0])], 1)


def spread_rows(pos_row, rows_low):
    return nn(onehot(iota((ROWS, pos_row.shape[1]), 0) == pos_row), rows_low)


def route(second_low, router, pos_col):
    logits = nn(second_low, router)
    lane = iota(logits.shape, 1)
    logits = jnp.where(lane < EXPERTS, logits, -1e30)
    expo = jnp.exp(logits - jnp.max(logits, -1, keepdims=True))
    probs = expo / jnp.sum(expo, -1, keepdims=True)
    expert = jnp.where(pos_col >= 0, pos_col // SLOTS, -1)
    chosen = jnp.where(lane == expert, 1.0, 0.0)
    return probs, chosen, jnp.sum(probs * chosen, -1, keepdims=True)


def head_masks():
    rows = iota((LANES, LANES), 0) // HEAD_DIM
    return [onehot(rows == h) for h in range(GROUP)]


def lane_masks():
    lane = iota((WPAD, LANES), 1)
    return [onehot(lane < WPAD), onehot(lane >= WPAD)]


def attention_forward_kernel(first, shifted, mp, gather, *refs):
    refs = list(refs)
    if first:
        patches_ref, enter_ref = refs[:2]
        refs = refs[2:]
    else:
        prev_ref, prev_gate_ref, returned_ref = refs[:3]
        refs = refs[3:]
    (
        valid_ref, col_ref, row_ref, qkv_ref, proj_ref, bias_ref, move_ref, back_ref, gain_ref, nbias_ref, router_ref,
    ) = refs[:11]
    bias_ref, gain_ref, nbias_ref, router_ref = (ref.at[0] for ref in (bias_ref, gain_ref, nbias_ref, router_ref))
    refs = refs[11:]
    if gather:
        core_up_ref, core_down_ref = refs[:2]
        refs = refs[2:]
    carried_ref = refs.pop(0)
    expert_out_ref = None if first else refs.pop(0)
    middle_ref, second_ref, gate_ref, buffer_ref, window_ref, qk_ref, v_ref, probs_ref, att_ref, proj_full = refs[:10]
    refs = refs[10:]
    if gather:
        qkv_full = refs.pop(0)
        up_out, down_out = refs[:2]
        refs = refs[2:]
    total_ref = refs.pop(0)
    step = pl.program_id(0)
    final = pl.num_programs(0) - 1
    count, _, width = carried_ref.shape
    if gather:
        shards = [ref.at[0] for ref in (qkv_ref, proj_ref, core_up_ref, core_down_ref)]
        qkv_ref, proj_ref = refs[:2]
        moving = WeightGather(shards, [qkv_ref, proj_ref, up_out, down_out], refs[2:])

        @pl.when(step == 0)
        def _():
            pl.semaphore_wait(moving.row.greet(), 2)
            for k in (0, 1):
                moving.start(k)
            for k in (0, 1):
                moving.forward(k)
            for k in (2, 3):
                moving.start(k)
            for k in (0, 1):
                moving.arrive(k)

        @pl.when(step == final)
        def _():
            for k in (2, 3):
                moving.forward(k)

    @pl.when(step == 0)
    def _():
        if gather:
            qkv_full[...] = join(qkv_ref)
        proj_full[...] = join(proj_ref).astype(f32).T.astype(bf16)
        total_ref[...] = jnp.zeros(total_ref.shape, f32)

    pos_col = join(col_ref)[:, 0:1]
    if first:
        x = per_image(lambda i: nn(enter_ref[...], patches_ref[i]), count)
    else:
        expert_out = collect(pos_col, returned_ref)
        store(expert_out_ref, expert_out)
        x = join(prev_ref) + join(prev_gate_ref) * expert_out
    store(carried_ref, x)
    xhat, _ = norm_parts(x)
    normed = (xhat * gain_ref[0:1, :] + nbias_ref[0:1, :]).astype(bf16)
    window_in = per_image(lambda i: nn(move_ref[...], normed[image_rows(i)]), count).astype(bf16)
    store(window_ref, window_in)
    qkv = join(qkv_ref)
    turned = nt(qkv, window_in).astype(bf16)
    straight = nt(window_in, qkv[width:]).astype(bf16)
    for i in range(count):
        qk_ref[i] = turned[: 2 * width, image_rows(i)]
    store(v_ref, straight[:, width:])
    heads_rows = head_masks()
    halves = lane_masks()
    low_lane = iota((WPAD, LANES), 1) < WPAD
    for pair in range(PAIRS * count):
        image, side = pair // PAIRS, pair % PAIRS
        across = slice(pair * LANES, (pair + 1) * LANES)
        within = slice(side * LANES, (side + 1) * LANES)
        if shifted:
            ahead = col_ref[image, side * LANES : side * LANES + WPAD, 1:2]
            behind = col_ref[image, side * LANES + WPAD : (side + 1) * LANES, 1:2]
            key_label = jnp.where(low_lane, ahead, behind)
            mask = jnp.where(key_label == row_ref[image, 1:2, within], 0.0, mask_fill)
        for group in range(HEADS // GROUP):
            features = slice(group * LANES, (group + 1) * LANES)
            queries = turned[features, across]
            spread = jnp.concatenate([queries * heads_rows[h] for h in range(GROUP)], 1)
            raw = nn(straight[across, features], spread)
            for h in range(GROUP):
                head = group * GROUP + h
                part = raw[:, h * LANES : (h + 1) * LANES]
                scores = jnp.where(low_lane, part[:WPAD], part[WPAD:]) * head_scale + bias_ref[head]
                if shifted:
                    scores = scores + mask
                expo = jnp.exp(scores - jnp.max(scores, 0, keepdims=True))
                probs = (expo * (1.0 / jnp.sum(expo, 0, keepdims=True))).astype(bf16)
                probs_ref[image, side * HEADS + head] = probs
                both = jnp.concatenate([probs * halves[0], probs * halves[1]], 0)
                at = slice(head * HEAD_DIM, (head + 1) * HEAD_DIM)
                values = turned[2 * width + head * HEAD_DIM : 2 * width + (head + 1) * HEAD_DIM, across]
                att_ref[image, at, within] = nn(values, both).astype(bf16)
    attended = per_image(lambda i: nt(back_ref[...], att_ref[i]), count).astype(bf16)
    branch = nt(attended, join(proj_ref))
    middle = x + per_image(lambda i: valid_ref[step * count + i].astype(f32) * branch[image_rows(i)], count)
    store(middle_ref, middle)
    xhat, _ = norm_parts(middle)
    second_low = (xhat * gain_ref[1:2, :] + nbias_ref[1:2, :]).astype(bf16)
    store(second_ref, second_low)
    _, _, gate = route(second_low, router_ref[...], pos_col)
    store(gate_ref, gate)
    total_ref[...] += spread_rows(lay_positions(row_ref), second_low)

    @pl.when(step == final)
    def _():
        buffer_ref[...] = total_ref[...].astype(bf16)
        if gather:
            for k in (2, 3):
                moving.arrive(k)
            for k in range(4):
                moving.sent(k)


def image_spec(array_shape, count):
    rest = tuple(array_shape[1:])
    zeros = (0,) * len(rest)
    return pl.BlockSpec((count,) + rest, lambda i: (i,) + zeros)


def whole_spec(array_shape):
    zeros = (0,) * len(array_shape)
    return pl.BlockSpec(tuple(array_shape), lambda i: zeros)


def image_call(kernel, images, arrays, outs, scratch, name, collective_id=None):
    count = 2 - images % 2

    def spec(kind, shape):
        if isinstance(kind, int):
            rest = tuple(shape[1:])
            return pl.BlockSpec((1,) + rest, lambda i: (kind,) + (0,) * len(rest))
        if kind in ("smem", "any"):
            return pl.BlockSpec(memory_space=pltpu.SMEM if kind == "smem" else pl.ANY)
        return image_spec(shape, count) if kind == "image" else whole_spec(shape)

    return pl.pallas_call(
        kernel,
        grid=(images // count,),
        out_shape=[jax.ShapeDtypeStruct(shape, dtype) for _, shape, dtype in outs],
        in_specs=[spec(kind, array.shape) for kind, array in arrays],
        out_specs=[spec(kind, shape) for kind, shape, _ in outs],
        scratch_shapes=scratch,
        compiler_params=pltpu.CompilerParams(
            vmem_limit_bytes=56 * MIB,
            dimension_semantics=("arbitrary",),
            collective_id=collective_id,
            has_side_effects=collective_id is not None,
        ),
        name=name,
    )(*[array for _, array in arrays])


def send_part(g, expert_out, second_low, router, pos_col, pos_row, logit_ref, router_grad_ref, total_ref):
    probs, chosen, gate = route(second_low, router, pos_col)
    gate_grad = jnp.where(pos_col >= 0, jnp.sum(g * expert_out, -1, keepdims=True), 0.0)
    sent = (gate * g).astype(bf16)
    logit_grad = gate_grad * gate * (chosen - probs)
    store(logit_ref, logit_grad)
    high, low = split_two(logit_grad)
    router_grad_ref[...] += tn(high, second_low) + tn(low, second_low)
    total_ref[...] += spread_rows(pos_row, sent)


def turn_kernel(
    prev_ref, gate_ref, returned_ref, cotangent_ref, enter_ref, leave_ref, col_ref, row_ref, second_ref, router_ref,
    block_ref, grad_ref, logit_ref, router_grad_ref, buffer_ref, total_ref,
):
    step = pl.program_id(0)
    count = cotangent_ref.shape[0]

    @pl.when(step == 0)
    def _():
        total_ref[...] = jnp.zeros(total_ref.shape, f32)
        router_grad_ref[...] = jnp.zeros(router_grad_ref.shape, f32)

    pos_col = join(col_ref)[:, 0:1]
    expert_out = collect(pos_col, returned_ref)
    x = (join(prev_ref) + join(gate_ref) * expert_out).astype(bf16)
    for i in range(count):
        block_ref[i] = nn(leave_ref[...], x[image_rows(i)]).astype(bf16)
    g = per_image(lambda i: nn(enter_ref[...], cotangent_ref[i]), count)
    store(grad_ref, g)
    send_part(
        g, expert_out, join(second_ref), router_ref[0], pos_col, lay_positions(row_ref), logit_ref, router_grad_ref, total_ref
    )

    @pl.when(step == pl.num_programs(0) - 1)
    def _():
        buffer_ref[...] = total_ref[...].astype(bf16)


def attention_backward_kernel(last, mp, fast, *refs):
    (
        valid_ref, grad_ref, returned_ref, logit_ref, middle_ref, carried_ref, router_ref, col_ref, move_ref, back_ref,
        gain_ref, proj_ref, qkv_ref, window_ref, qk_ref, v_ref, probs_ref, att_ref,
    ) = refs[:18]
    refs = refs[18:]
    refs = list(refs)
    if fast:
        units_ref = refs.pop(0)
    if last:
        leave_ref = refs.pop(0)
    else:
        row_ref, expert_out_ref, second_ref, router_next_ref = refs[:4]
        refs = refs[4:]
    out_ref = refs.pop(0)
    if fast:
        unit_ref, mine_ref = refs[:2]
        refs = refs[2:]
    else:
        qkv_grad_ref, proj_grad_ref = refs[:2]
        refs = refs[2:]
    table_ref, small_ref = refs[:2]
    refs = refs[2:]
    if not last:
        logit_out_ref, router_grad_ref, buffer_ref = refs[:3]
        refs = refs[3:]
    turned = refs.pop(0)
    if fast:
        qkv_grad_ref, proj_grad_ref = refs[:2]
        refs = refs[2:]
    if not last:
        total_ref = refs.pop(0)
    step = pl.program_id(0)
    final = pl.num_programs(0) - 1
    count, _, width = carried_ref.shape
    if fast:
        row = Row()
        sums = RowSum(
            row, [units_ref.at[k] for k in range(2)], refs[0], refs[1], refs[2], [mine_ref.at[k] for k in range(2)],
            refs[3:7],
        )

        @pl.when(step == 0)
        def _():
            pl.semaphore_wait(row.greet(), 2)
            for k in range(2):
                sums.start(k)

    @pl.when(step == 0)
    def _():
        qkv_grad_ref[...] = jnp.zeros(qkv_grad_ref.shape, f32)
        proj_grad_ref[...] = jnp.zeros(proj_grad_ref.shape, f32)
        table_ref[...] = jnp.zeros(table_ref.shape, f32)
        small_ref[...] = jnp.zeros(small_ref.shape, f32)
        if not last:
            total_ref[...] = jnp.zeros(total_ref.shape, f32)
            router_grad_ref[...] = jnp.zeros(router_grad_ref.shape, f32)

    pos_col = join(col_ref)[:, 0:1]
    g = join(grad_ref)
    high, low = split_two(join(logit_ref))
    gain_ref, router = gain_ref.at[0], router_ref[0]
    normed_grad = collect(pos_col, returned_ref) + nt(high, router) + nt(low, router)
    xhat, rstd = norm_parts(join(middle_ref))
    small_ref[1:2, :] += jnp.sum(normed_grad * xhat, 0, keepdims=True)
    small_ref[3:4, :] += jnp.sum(normed_grad, 0, keepdims=True)
    middle_grad = g + norm_back(normed_grad, gain_ref[1:2, :], xhat, rstd)

    def branch_part(i):
        low_part = (valid_ref[step * count + i].astype(f32) * middle_grad[image_rows(i)]).astype(bf16)
        return nn(move_ref[...], low_part)

    branch_grad = per_image(branch_part, count).astype(bf16)
    for i in range(count):
        proj_grad_ref[...] += nn(att_ref[i], branch_grad[image_rows(i)])
    att_grad = nt(proj_ref[...], branch_grad).astype(bf16)
    if fast:

        @pl.when(step == 0)
        def _():
            for k in range(2):
                sums.middle(k)

    heads_rows = head_masks()
    halves = lane_masks()
    low_lane = iota((WPAD, LANES), 1) < WPAD
    for pair in range(PAIRS * count):
        image, side = pair // PAIRS, pair % PAIRS
        across = slice(pair * LANES, (pair + 1) * LANES)
        within = slice(side * LANES, (side + 1) * LANES)
        for group in range(HEADS // GROUP):
            features = slice(group * LANES, (group + 1) * LANES)
            grads = att_grad[features, across]
            spread = jnp.concatenate([grads * heads_rows[h] for h in range(GROUP)], 1)
            raw = nn(v_ref[image, within, features], spread)
            for h in range(GROUP):
                head = group * GROUP + h
                at = slice(head * HEAD_DIM, (head + 1) * HEAD_DIM)
                below = slice(width + head * HEAD_DIM, width + (head + 1) * HEAD_DIM)
                lowest = slice(2 * width + head * HEAD_DIM, 2 * width + (head + 1) * HEAD_DIM)
                part = raw[:, h * LANES : (h + 1) * LANES]
                probs_grad = jnp.where(low_lane, part[:WPAD], part[WPAD:])
                probs_low = probs_ref[image, side * HEADS + head]
                probs = probs_low.astype(f32)
                weighted = probs * probs_grad
                scores_grad = weighted - probs * jnp.sum(weighted, 0, keepdims=True)
                table_ref[head] += scores_grad
                scores_low = scores_grad.astype(bf16)
                both = jnp.concatenate([scores_low * halves[0], scores_low * halves[1]], 0)
                probs_both = jnp.concatenate([probs_low * halves[0], probs_low * halves[1]], 0)
                turned[at, across] = (nn(qk_ref[image, below, within], both) * head_scale).astype(bf16)
                turned[below, across] = (nt(qk_ref[image, at, within], both) * head_scale).astype(bf16)
                turned[lowest, across] = nt(att_grad[at, across], probs_both).astype(bf16)
    qkv_grad_ref[...] += nn(turned[...], join(window_ref))
    mixed_grad = per_image(lambda i: nt(back_ref[...], turned[:, image_rows(i)]), count).astype(bf16)
    first_grad = nn(mixed_grad, qkv_ref[...])
    xhat, rstd = norm_parts(join(carried_ref))
    small_ref[0:1, :] += jnp.sum(first_grad * xhat, 0, keepdims=True)
    small_ref[2:3, :] += jnp.sum(first_grad, 0, keepdims=True)
    out = middle_grad + norm_back(first_grad, gain_ref[0:1, :], xhat, rstd)
    if last:
        top = out.astype(bf16)
        rest = out - top.astype(f32)
        mid, low = split_two(rest)
        leave = leave_ref[...]
        for i in range(count):
            at = image_rows(i)
            out_ref[i] = nn(leave, top[at]) + nn(leave, mid[at]) + nn(leave, low[at])
    else:
        store(out_ref, out)
        send_part(
            out, join(expert_out_ref), join(second_ref), router_next_ref[0], pos_col, lay_positions(row_ref), logit_out_ref,
            router_grad_ref, total_ref,
        )

    @pl.when(step == final)
    def _():
        if not last:
            buffer_ref[...] = total_ref[...].astype(bf16)
        if fast:
            columns, rows = 3 * width // mp, width // mp
            proj_turned = proj_grad_ref[...].T
            for place in range(mp):
                q = quarter_at(place, mp)
                unit_ref[place, :columns] = qkv_grad_ref[q * columns : (q + 1) * columns].astype(bf16)
                unit_ref[place, columns:] = proj_turned[q * rows : (q + 1) * rows].astype(bf16)
            for k in range(2):
                sums.end(k)
                sums.finish(k)


def quarter_at(place, mp):
    return place % (mp // 2) * 2 + place // (mp // 2)


def add_up(*parts):
    total = parts[0].astype(f32)
    for part in parts[1:]:
        total = total + part.astype(f32)
    return total


def to_row(source, target, sems, k, row):
    return pltpu.make_async_remote_copy(
        src_ref=source,
        dst_ref=target,
        send_sem=sems[0].at[k],
        recv_sem=sems[1].at[k],
        device_id={"mp": row},
        device_id_type=MESH,
    )


class Row:
    def __init__(self):
        row = lax.axis_index("mp")
        self.row, self.core, self.y = row, lax.rem(row, 2), lax.div(row, 2)
        self.sibling, self.across = row + 1 - 2 * self.core, row + 2 - 4 * self.y
        self.place = self.core * 2 + self.y
        self.place_across = self.core * 2 + 1 - self.y

    def greet(self):
        barrier = pltpu.get_barrier_semaphore()
        for row in (self.sibling, self.across):
            pl.semaphore_signal(barrier, inc=1, device_id={"mp": row}, device_id_type=MESH)
        return barrier


class RowSum:
    semaphores = 4

    def __init__(self, row, units, core_in, y_out, y_in, mine, sems):
        self.row, self.units, self.mine = row, units, mine
        self.core_in, self.y_out, self.y_in = core_in, y_out, y_in
        self.sems = (sems[:2], sems[2:])

    def pair(self, k):
        theirs = self.units[k].at[pl.ds(2 * (1 - self.row.core), 2)]
        return to_row(theirs, self.core_in.at[k], self.sems[0], k, self.row.sibling)

    def cross(self, k):
        return to_row(self.y_out.at[k], self.y_in.at[k], self.sems[1], k, self.row.across)

    def start(self, k):
        self.pair(k).start()

    def middle(self, k):
        self.pair(k).wait_recv()
        other = 1 - self.row.y
        mixed = add_up(self.units[k][self.row.core * 2 + other], self.core_in[k, other])
        self.y_out[k] = mixed.astype(bf16)
        self.cross(k).start()

    def end(self, k):
        self.cross(k).wait_recv()
        self.mine[k][...] = add_up(
            self.units[k][self.row.place], self.core_in[k, self.row.y], self.y_in[k]
        ).astype(bf16)

    def finish(self, k):
        self.pair(k).wait_send()
        self.cross(k).wait_send()

    @classmethod
    def scratch(cls, count, width):
        return [
            pltpu.VMEM((count, 2, width, width), bf16),
            pltpu.VMEM((count, width, width), bf16),
            pltpu.VMEM((count, width, width), bf16),
        ] + [pltpu.SemaphoreType.DMA((count,))] * cls.semaphores


class RowGather:
    semaphores = 6

    def __init__(self, row, sources, fulls, slot, slot_across, sems):
        self.row, self.sources, self.fulls = row, sources, fulls
        self.slot, self.slot_across = slot, slot_across
        self.sems = (sems[:2], sems[2:4], sems[4:])

    def over(self, k):
        return to_row(self.sources[k], self.fulls[k].at[self.slot], self.sems[0], k, self.row.across)

    def near(self, k):
        return to_row(self.sources[k], self.fulls[k].at[self.slot], self.sems[1], k, self.row.sibling)

    def onward(self, k):
        block = self.fulls[k].at[self.slot_across]
        return to_row(block, block, self.sems[2], k, self.row.sibling)

    def start(self, k):
        self.over(k).start()
        self.near(k).start()

    def forward(self, k):
        self.over(k).wait_recv()
        self.onward(k).start()

    def arrive(self, k):
        self.near(k).wait_recv()
        self.onward(k).wait_recv()

    def sent(self, k):
        self.over(k).wait_send()
        self.near(k).wait_send()
        self.onward(k).wait_send()

    @classmethod
    def scratch(cls, count):
        return [pltpu.SemaphoreType.DMA((count,))] * cls.semaphores


class WeightGather(RowGather):
    def __init__(self, shards, fulls, sems):
        row = Row()
        super().__init__(row, shards, fulls, row.row, row.across, sems[:6])
        self.own_sem = sems[6]

    def own(self, k):
        return pltpu.make_async_copy(self.sources[k], self.fulls[k].at[self.slot], self.own_sem.at[k])

    def start(self, k):
        super().start(k)
        self.own(k).start()

    def arrive(self, k):
        super().arrive(k)
        self.own(k).wait()

    @classmethod
    def scratch(cls, count):
        return super().scratch(count) + [pltpu.SemaphoreType.DMA((count,))]


def closing_kernel(
    dp, mp, given_ref, attn_ref, small_ref, full_ref, shard_ref, small_out, core_in, y_out, y_in, a0, a1, b0, b1, g0, g1, g2,
    g3, g4, g5, mine, x_in, half, z_in, s_core, s_one, s_y, s_mine, s_x, s_half, s_z, s0, s1, s2, s3, x0, x1, z0, z1, w0, w1,
    v0, v1,
):
    me = lax.axis_index("dp")
    x, z = lax.rem(me, 2), lax.div(me, 2)
    deep = dp // 2
    partner = me + 1 - 2 * x
    row = Row()
    sums = RowSum(row, [attn_ref], core_in, y_out, y_in, [mine], (a0, a1, b0, b1))
    gather = RowGather(
        row, [given_ref.at[0], given_ref.at[1]], [full_ref.at[0], full_ref.at[1]], row.place, row.place_across,
        (g0, g1, g2, g3, g4, g5),
    )
    barrier = row.greet()
    pl.semaphore_signal(barrier, inc=1, device_id={"dp": partner}, device_id_type=MESH)
    for off in range(1, deep):
        peer = lax.rem(z + off, deep) * 2 + x
        pl.semaphore_signal(barrier, inc=1, device_id={"dp": peer}, device_id_type=MESH)
    pl.semaphore_wait(barrier, 3 + deep - 1)

    s_pair = to_row(small_ref, s_core, (s0, s1), 0, row.sibling)
    s_cross = to_row(s_one, s_y, (s2, s3), 0, row.across)
    early, late, every = (0, 1), (2, 3), (0, 1, 2, 3)
    total = [given_ref.at[0], given_ref.at[1], mine, s_mine]
    arrived = [x_in.at[k] for k in range(3)] + [s_x]
    halves = [half.at[k] for k in range(3)] + [s_half]
    slots = [z_in.at[k] for k in range(3)] + [s_z]
    result = [shard_ref.at[k] for k in range(3)] + [small_out]

    def cut(k):
        height = total[k].shape[0] // 2
        return height, height // deep

    def over_x(k):
        height, _ = cut(k)
        away = total[k].at[pl.ds(pl.multiple_of((1 - x) * height, height), height)]
        return to_peer(away, arrived[k], x0.at[k], x1.at[k], partner)

    def over_z(k, off):
        _, piece = cut(k)
        to = lax.rem(z + off, deep)
        part = halves[k].at[pl.ds(pl.multiple_of(to * piece, piece), piece)]
        return to_peer(part, slots[k].at[off], z0.at[k, off], z1.at[k, off], to * 2 + x)

    def own_piece(k):
        height, piece = cut(k)
        return result[k].at[pl.ds(pl.multiple_of(x * height + z * piece, piece), piece)]

    def own_half(k):
        height, _ = cut(k)
        return result[k].at[pl.ds(pl.multiple_of(x * height, height), height)]

    def back_z(k, off):
        to = lax.rem(z + off, deep)
        return to_peer(own_piece(k), own_piece(k), w0.at[k, off], w1.at[k, off], to * 2 + x)

    def back_x(k):
        return to_peer(own_half(k), own_half(k), v0.at[k], v1.at[k], partner)

    def halve(k):
        over_x(k).wait_recv()
        height, _ = cut(k)
        keep = total[k][pl.ds(pl.multiple_of(x * height, height), height)]
        halves[k][...] = add_up(keep, arrived[k][...]).astype(halves[k].dtype)
        for off in range(1, deep):
            over_z(k, off).start()

    def quarter(k):
        for off in range(1, deep):
            over_z(k, off).wait_recv()
        _, piece = cut(k)
        keep = halves[k][pl.ds(pl.multiple_of(z * piece, piece), piece)]
        own_piece(k)[...] = add_up(keep, *[slots[k][off] for off in range(1, deep)]).astype(result[k].dtype)
        for off in range(1, deep):
            back_z(k, off).start()

    def widen(k):
        for off in range(1, deep):
            back_z(k, off).wait_recv()
        back_x(k).start()

    sums.start(0)
    s_pair.start()
    for k in early:
        over_x(k).start()
    sums.middle(0)
    s_pair.wait_recv()
    s_one[...] = small_ref[...] + s_core[...]
    s_cross.start()
    for k in early:
        gather.start(k)
        full_ref[k, row.place] = given_ref[k]
    for k in early:
        halve(k)
    sums.end(0)
    over_x(2).start()
    s_cross.wait_recv()
    s_mine[...] = s_one[...] + s_y[...]
    over_x(3).start()
    for k in early:
        quarter(k)
    for k in late:
        halve(k)
    for k in early:
        widen(k)
    for k in late:
        quarter(k)
    gather.forward(0)
    for k in late:
        widen(k)
    gather.forward(1)
    s_pair.wait_send()
    s_cross.wait_send()
    sums.finish(0)
    for k in early:
        gather.arrive(k)
        gather.sent(k)
    for k in every:
        over_x(k).wait_send()
        for off in range(1, deep):
            over_z(k, off).wait_send()
            back_z(k, off).wait_send()
        back_x(k).wait()


def closing_call(dp, mp, given, attn, small, collective_id):
    width = attn.shape[-1]
    deep = dp // 2
    lines = small.shape[0]
    dma = pltpu.SemaphoreType.DMA
    shape = jax.ShapeDtypeStruct
    scratch = RowSum.scratch(1, width) + RowGather.scratch(2) + [
        pltpu.VMEM((width, width), bf16),
        pltpu.VMEM((3, width // 2, width), bf16),
        pltpu.VMEM((3, width // 2, width), bf16),
        pltpu.VMEM((3, deep, width // dp, width), bf16),
        pltpu.VMEM((lines, width), f32),
        pltpu.VMEM((lines, width), f32),
        pltpu.VMEM((lines, width), f32),
        pltpu.VMEM((lines, width), f32),
        pltpu.VMEM((lines // 2, width), f32),
        pltpu.VMEM((lines // 2, width), f32),
        pltpu.VMEM((deep, lines // dp, width), f32),
        dma((1,)), dma((1,)), dma((1,)), dma((1,)),
        dma((4,)), dma((4,)), dma((4, deep)), dma((4, deep)), dma((4, deep)), dma((4, deep)), dma((4,)), dma((4,)),
    ]
    vmem = pl.BlockSpec(memory_space=pltpu.VMEM)
    return pl.pallas_call(
        functools.partial(closing_kernel, dp, mp),
        out_shape=[shape((2, mp, width, width), bf16), shape((3, width, width), bf16), shape(small.shape, f32)],
        in_specs=[vmem] * 3,
        out_specs=[vmem] * 3,
        scratch_shapes=scratch,
        compiler_params=pltpu.CompilerParams(
            vmem_limit_bytes=56 * MIB, collective_id=collective_id, has_side_effects=True
        ),
        name="closing",
    )(given, attn, small)


def format_kernel(columns, *refs):
    count = (len(refs) - 6) // 2
    qkv_out, proj_out, core_up_out, core_down_out, up_out, down_out = refs[2 * count :]

    def form(full, shard):
        mp, width = full.shape[1], full.shape[2]
        rows = width // mp
        qkv_out[0] = shard[2, :columns].astype(f32)
        proj_out[0] = shard[2, columns:].astype(f32)
        core_up_out[0] = shard[0].astype(f32)
        for place in range(mp):
            q = quarter_at(place, mp)
            up_out[0, 0, :, q * width : (q + 1) * width] = full[0, place].astype(f32)
        for chunk in range(mp):
            at = slice(chunk * width, (chunk + 1) * width)
            core_down_out[0, :, at] = shard[1, chunk * rows : (chunk + 1) * rows].astype(f32)
            block = [None] * mp
            for place in range(mp):
                block[quarter_at(place, mp)] = full[1, place, chunk * rows : (chunk + 1) * rows].astype(f32)
            down_out[0, 0, at, :] = jnp.concatenate(block, 0).T

    for layer in range(count):
        pl.when(pl.program_id(0) == layer)(functools.partial(form, refs[layer], refs[count + layer]))


def format_call(fulls, shards, columns):
    layers = len(fulls)
    _, mp, width, _ = fulls[0].shape
    hidden = mp * width
    shapes = [
        (layers, columns, width),
        (layers, width - columns, width),
        (layers, width, width),
        (layers, width // mp, hidden),
        (layers, 1, width, hidden),
        (layers, 1, hidden, width),
    ]
    return pl.pallas_call(
        functools.partial(format_kernel, columns),
        grid=(layers,),
        out_shape=[jax.ShapeDtypeStruct(shape, f32) for shape in shapes],
        in_specs=[whole_spec(a.shape) for a in (*fulls, *shards)],
        out_specs=[image_spec(shape, 1) for shape in shapes],
        compiler_params=pltpu.CompilerParams(vmem_limit_bytes=56 * MIB),
        name="format",
    )(*fulls, *shards)


def greet(dp, me, rows=()):
    barrier = pltpu.get_barrier_semaphore()
    for row in rows:
        pl.semaphore_signal(barrier, inc=1, device_id={"mp": row}, device_id_type=MESH)

    def signal(off, carry):
        pl.semaphore_signal(barrier, inc=1, device_id={"dp": lax.rem(me + off, dp)}, device_id_type=MESH)
        return carry

    lax.fori_loop(1, dp, signal, 0)
    pl.semaphore_wait(barrier, dp - 1 + len(rows))


def to_peer(source, target, send_sem, recv_sem, peer):
    return pltpu.make_async_remote_copy(
        src_ref=source,
        dst_ref=target,
        send_sem=send_sem,
        recv_sem=recv_sem,
        device_id={"dp": peer},
        device_id_type=MESH,
    )


def gelu_parts(h):
    root = np.float32(np.sqrt(2.0 / np.pi))
    square = h * h
    t = jnp.tanh(root * h * (1.0 + 0.044715 * square))
    half = 0.5 * (1.0 + t)
    slope = half + 0.5 * h * (1.0 - t * t) * root * (1.0 + 3 * 0.044715 * square)
    return h * half, slope


def expert_forward_kernel(dp, mp, layer, gather, *refs):
    refs = list(refs)
    buffer_ref, up_any, down_any, rup_any, rdown_any = refs[:5]
    refs = refs[5:]
    if gather:
        shards = [ref.at[layer + 1] for ref in refs[:4]]
        refs = refs[4:]
    recv_ref, returned_ref, up_eff, down_eff = refs[:4]
    refs = refs[4:]
    if gather:
        fulls = refs[:4]
        refs = refs[4:]
    part, core, up_ref, down_ref, rup_ref, rdown_ref, local = refs[:7]
    refs = refs[7:]
    moving = WeightGather(shards, fulls, refs[:7]) if gather else None
    send_one, recv_one, send_two, recv_two = refs[-4:]
    split = dp // EXPERTS
    me = lax.axis_index("dp")
    loads = [
        pltpu.make_async_copy(source, target, local.at[k])
        for k, (source, target) in enumerate(
            [
                (up_any, up_ref),
                (rup_any.at[layer, 0], rup_ref),
                (down_any, down_ref),
                (rdown_any.at[layer, 0], rdown_ref),
            ]
        )
    ]
    for load in loads:
        load.start()
    greet(dp, me, (moving.row.sibling, moving.row.across) if gather else ())

    def first(off):
        peer = lax.rem(me + off, dp)
        return to_peer(
            buffer_ref.at[lax.div(peer, split)], recv_ref.at[me], send_one.at[off], recv_one.at[off], peer
        )

    def second(off):
        source = lax.rem(me + dp - off, dp)
        return to_peer(part.at[source], returned_ref.at[me], send_two.at[off], recv_two.at[off], source)

    def start_first(off, carry):
        first(off).start()
        return carry

    lax.fori_loop(1, dp, start_first, 0)
    if gather:
        for k in range(4):
            moving.start(k)
    recv_ref[me] = buffer_ref[lax.div(me, split)]
    hidden = up_eff.shape[1]
    columns = up_ref.shape[-1]
    loads[0].wait()
    loads[1].wait()
    if split == 1 and columns % LANES == 0:
        for m in range(mp):
            at = slice(m * columns, (m + 1) * columns)
            up_eff[:, at] = (up_ref[m].astype(f32) + rup_ref[:, at].astype(f32)).astype(bf16)
    else:
        core[...] = rup_ref[...].astype(f32)
        begin = lax.rem(me, split) * hidden
        for m in range(mp):
            put = onehot(iota((columns, hidden), 0) + m * columns == iota((columns, hidden), 1) + begin)
            core[...] += nn(up_ref[m], put)
        up_eff[...] = core[...].astype(bf16)
    begin = pl.multiple_of(lax.rem(me, split) * hidden, LANES)
    loads[2].wait()
    loads[3].wait()
    core_part = down_ref[:, :, pl.ds(begin, hidden)].reshape(down_eff.shape[1], hidden)
    down_eff[...] = (core_part.astype(f32).T + rdown_ref[...].astype(f32)).astype(bf16)

    def work(source):
        hidden_pre = nn(recv_ref[source], up_eff[...])
        hidden_low = gelu_parts(hidden_pre)[0].astype(bf16)
        return nn(hidden_low, down_eff[...]).astype(bf16)

    returned_ref[me] = work(me)

    def step(off, carry):
        source = lax.rem(me + dp - off, dp)
        first(off).wait_recv()
        part[source] = work(source)
        second(off).start()
        return carry

    lax.fori_loop(1, dp, step, 0)
    if gather:
        for k in range(4):
            moving.forward(k)

    def finish(off, carry):
        first(off).wait_send()
        second(off).wait()
        return carry

    lax.fori_loop(1, dp, finish, 0)
    if gather:
        for k in range(4):
            moving.arrive(k)
            moving.sent(k)


def expert_backward_kernel(dp, mp, fast, reduce, *refs):
    refs = list(refs)
    buffer_ref, recv_ref, up_ref, down_ref = refs[:4]
    refs = refs[4:]
    if reduce:
        given_ref, attn_ref = refs[:2]
        refs = refs[2:]
    returned_ref = refs.pop(0)
    if fast:
        units_ref = refs.pop(0)
    else:
        up_term, down_term = refs[:2]
        refs = refs[2:]
    if reduce:
        full_ref, mine_ref = refs[:2]
        refs = refs[2:]
    grads, hidden_low, slope, pre, part = refs[:5]
    refs = refs[5:]
    if fast:
        up_term, down_term = refs[:2]
        refs = refs[2:]
    row = Row() if reduce else None
    if reduce:
        core_in, y_out, y_in = refs[:3]
        sums = RowSum(row, [attn_ref], core_in, y_out, y_in, [mine_ref], refs[3:7])
        gather = RowGather(
            row, [given_ref.at[k] for k in range(2)], [full_ref.at[k] for k in range(2)], row.place, row.place_across,
            refs[7:13],
        )
        refs = refs[13:]
    send_one, recv_one, send_two, recv_two = refs
    split = dp // EXPERTS
    me = lax.axis_index("dp")
    greet(dp, me, (row.sibling, row.across) if reduce else ())

    def first(off):
        peer = lax.rem(me + off, dp)
        return to_peer(buffer_ref.at[lax.div(peer, split)], grads.at[me], send_one.at[off], recv_one.at[off], peer)

    def second(off):
        source = lax.rem(me + dp - off, dp)
        return to_peer(part.at[source], returned_ref.at[me], send_two.at[off], recv_two.at[off], source)

    def start_first(off, carry):
        first(off).start()
        return carry

    lax.fori_loop(1, dp, start_first, 0)
    if reduce:
        sums.start(0)
        for k in range(2):
            gather.start(k)
    grads[me] = buffer_ref[lax.div(me, split)]

    def again(source, carry):
        value, rate = gelu_parts(nn(recv_ref[source], up_ref[...]))
        hidden_low[source] = value.astype(bf16)
        slope[source] = rate
        return carry

    lax.fori_loop(0, dp, again, 0)
    if reduce:
        sums.middle(0)
        for k in range(2):
            full_ref[k, row.place] = given_ref[k]

    def work(source):
        hidden_grad = nt(grads[source], down_ref[...])
        pre_grad = (slope[source] * hidden_grad).astype(bf16)
        pre[source] = pre_grad
        return nt(pre_grad, up_ref[...]).astype(bf16)

    returned_ref[me] = work(me)

    def step(off, carry):
        source = lax.rem(me + dp - off, dp)
        first(off).wait_recv()
        part[source] = work(source)
        second(off).start()
        return carry

    lax.fori_loop(1, dp, step, 0)
    if reduce:
        for k in range(2):
            gather.forward(k)
        sums.end(0)
    up_term[...] = jnp.zeros(up_term.shape, f32)
    down_term[...] = jnp.zeros(down_term.shape, f32)

    def terms(block, carry):
        up_term[...] += tn(recv_ref[block], pre[block])
        down_term[...] += tn(grads[block], hidden_low[block])
        return carry

    lax.fori_loop(0, dp, terms, 0)
    if fast:
        width = up_term.shape[0]
        height = width // mp
        for place in range(mp):
            q = quarter_at(place, mp)
            units_ref[0, place] = up_term[:, q * width : (q + 1) * width].astype(bf16)
            for chunk in range(mp):
                block = down_term[q * height : (q + 1) * height, chunk * width : (chunk + 1) * width]
                units_ref[1, place, chunk * height : (chunk + 1) * height] = block.astype(bf16)

    def finish(off, carry):
        first(off).wait_send()
        second(off).wait()
        return carry

    lax.fori_loop(1, dp, finish, 0)
    if reduce:
        sums.finish(0)
        for k in range(2):
            gather.arrive(k)
            gather.sent(k)


def expert_call(kernel, arrays, outs, scratch, dp, collective_id, name, flops, anys=(), any_outs=()):
    sems = [pltpu.SemaphoreType.DMA((dp,))] * 4
    vmem, anywhere = pl.BlockSpec(memory_space=pltpu.VMEM), pl.BlockSpec(memory_space=pl.ANY)
    return pl.pallas_call(
        kernel,
        out_shape=[jax.ShapeDtypeStruct(shape, dtype) for shape, dtype in (*outs, *any_outs)],
        in_specs=[vmem] * len(arrays) + [anywhere] * len(anys),
        out_specs=[vmem] * len(outs) + [anywhere] * len(any_outs),
        scratch_shapes=scratch + sems,
        compiler_params=pltpu.CompilerParams(
            vmem_limit_bytes=56 * MIB, collective_id=collective_id, has_side_effects=True
        ),
        cost_estimate=pl.CostEstimate(flops=flops, bytes_accessed=20 * MIB, transcendentals=0),
        name=name,
    )(*arrays, *anys)


def by_windows(grid):
    images, kinds = grid.shape[:2]
    blocks = GRID // WINDOW
    grid = grid.reshape(images, kinds, blocks, WINDOW, blocks, WINDOW).transpose(0, 1, 2, 4, 3, 5)
    grid = grid.reshape(images, kinds, blocks * blocks, WINPOS)
    grid = jnp.pad(grid, ((0, 0), (0, 0), (0, 0), (0, WPAD - WINPOS)), constant_values=-1)
    return grid.reshape(images, kinds, IMGROWS)


def per_device(
    patches,
    qkv_weight,
    proj_weight,
    core_up,
    core_down,
    residual_up,
    residual_down,
    position_bias,
    router_weight,
    norm_gain,
    norm_bias,
    cotangent,
    image_valid,
    expert_index,
    slot_index,
    region_id,
):
    dp, mp = lax.axis_size("dp"), lax.axis_size("mp")
    images, _, width = patches.shape
    split = dp // EXPERTS
    hidden = residual_up.shape[-1]
    hidden_full = core_up.shape[-1] * mp
    row_index = lax.axis_index("mp")

    fast = split == 1 and dp == 8 and mp == 4 and hidden == mp * width
    qkv_rows, proj_rows, down_rows = (a.transpose(0, 2, 1) for a in (qkv_weight, proj_weight, core_down))
    shards = (qkv_rows, proj_rows, core_up, down_rows)
    gathered = [[None] * len(shards)] * LAYERS
    if not fast:
        gathered = [[lax.all_gather(a[l], "mp", axis=0, tiled=False) for a in shards] for l in range(LAYERS)]

    position = jnp.where(slot_index >= 0, expert_index * SLOTS + slot_index, -1)
    labels = jnp.roll(region_id, (-SHIFT, -SHIFT), (1, 2))
    row_form = by_windows(jnp.stack([position.reshape(images, GRID, GRID), labels], 1))
    col_form = row_form.transpose(0, 2, 1)
    enter = jnp.asarray(enter_table(), bf16)
    leave = jnp.asarray(enter_table().T, bf16)
    moves = [jnp.asarray(move_table(l % 2 == 1), bf16) for l in range(LAYERS)]
    backs = [jnp.asarray(move_table(l % 2 == 1).T, bf16) for l in range(LAYERS)]
    entries = jnp.asarray(offset_index().reshape(-1))
    entry_hot = (jnp.arange(OFFSETS + 1)[:, None] == entries[None, :]).astype(f32)
    table_rows = position_bias.transpose(0, 2, 1).reshape(LAYERS * HEADS, OFFSETS)
    padded_rows = jnp.pad(table_rows, ((0, 0), (0, 1)), constant_values=-1e30)
    biases = jnp.dot(padded_rows, entry_hot, precision=highest).reshape(LAYERS, HEADS, WPAD, LANES)
    routers = jnp.pad(router_weight, ((0, 0), (0, 0), (0, LANES - EXPERTS)))

    token = (images, IMGROWS, width)
    buffer_shape = (ROWS, width)
    block_rows = (dp, SLOTS, width)
    pieces = (split, ROWS, width)

    def by_piece(returned):
        return returned.reshape(EXPERTS, split, SLOTS, width).transpose(1, 0, 2, 3).reshape(pieces)

    records = []
    before = None
    for l in range(LAYERS):
        first = l == 0
        gather = fast and first
        if first:
            arrays = [("image", patches), ("whole", enter)]
        else:
            arrays = [("image", before[0]), ("image", before[1]), ("whole", before[2])]
        arrays += [
            ("smem", image_valid),
            ("image", col_form),
            ("image", row_form),
            ("any", qkv_rows) if gather else ("whole", gathered[l][0]),
            ("any", proj_rows) if gather else ("whole", gathered[l][1]),
            (l, biases),
            ("whole", moves[l]),
            ("whole", backs[l]),
            (l, norm_gain),
            (l, norm_bias),
            (l, routers),
        ]
        if gather:
            arrays += [("any", core_up), ("any", down_rows)]
        outs = [("image", token, f32)]
        if not first:
            outs.append(("image", token, f32))
        outs += [
            ("image", token, f32),
            ("image", token, bf16),
            ("image", (images, IMGROWS, 1), f32),
            ("whole", buffer_shape, bf16),
            ("image", token, bf16),
            ("image", (images, 2 * width, IMGROWS), bf16),
            ("image", token, bf16),
            ("image", (images, PAIRS * HEADS, WPAD, LANES), bf16),
            ("image", (images, width, IMGROWS), bf16),
            ("whole", (width, width), bf16),
        ]
        scratch = [pltpu.VMEM(buffer_shape, f32)]
        gathered_shapes = [(mp, *a.shape[1:]) for a in shards]
        if gather:
            outs.append(("whole", (3 * width, width), bf16))
            outs += [("any", shape, bf16) for shape in gathered_shapes[2:]]
            scratch += [pltpu.VMEM(shape, bf16) for shape in gathered_shapes[:2]] + WeightGather.scratch(4)
        results = list(
            image_call(
                functools.partial(attention_forward_kernel, first, l % 2 == 1, mp, gather),
                images, arrays, outs, scratch, f"attend_{l}", 3 * LAYERS + 1 if gather else None,
            )
        )
        if gather:
            gathered[l] = [results[-3], None] + results[-2:]
            results = results[:-3]
        carried = results.pop(0)
        if not first:
            records[-1]["expert_out"] = results.pop(0)
        middle, second_low, gate, buffer = results[:4]
        gather = fast and l < LAYERS - 1
        received, returned, up_eff, down_eff, *more = expert_call(
            functools.partial(expert_forward_kernel, dp, mp, l, gather),
            [buffer.reshape(EXPERTS, SLOTS, width)],
            [
                (block_rows, bf16),
                (block_rows, bf16),
                ((width, hidden), bf16),
                ((hidden, width), bf16),
            ],
            [
                pltpu.VMEM(block_rows, bf16),
                pltpu.VMEM((8, LANES) if fast else (width, hidden), f32),
                pltpu.VMEM(gathered_shapes[2], bf16),
                pltpu.VMEM(gathered_shapes[3], bf16),
                pltpu.VMEM((width, hidden), bf16),
                pltpu.VMEM((hidden, width), bf16),
                pltpu.SemaphoreType.DMA((4,)),
            ]
            + (WeightGather.scratch(4) if gather else []),
            dp, l, f"experts_{l}", 4 * dp * SLOTS * width * hidden,
            [gathered[l][2], gathered[l][3], residual_up, residual_down, *(shards if gather else ())],
            [(shape, bf16) for shape in gathered_shapes] if gather else (),
        )
        if gather:
            gathered[l + 1] = more
        returned = by_piece(returned)
        before = (middle, gate, returned)
        records.append(
            dict(
                carried=carried, middle=middle, second_low=second_low, gate=gate, saved=results[4:], received=received,
                up_eff=up_eff, down_eff=down_eff,
            )
        )

    top = records[-1]
    block_output, grad, logit_grad, router_part, buffer = image_call(
        turn_kernel,
        images,
        [
            ("image", before[0]),
            ("image", before[1]),
            ("whole", before[2]),
            ("image", cotangent),
            ("whole", enter),
            ("whole", leave),
            ("image", col_form),
            ("image", row_form),
            ("image", top["second_low"]),
            (LAYERS - 1, routers),
        ],
        [
            ("image", patches.shape, bf16),
            ("image", token, f32),
            ("image", (images, IMGROWS, LANES), f32),
            ("whole", (LANES, width), f32),
            ("whole", buffer_shape, bf16),
        ],
        [pltpu.VMEM(buffer_shape, f32)],
        "turn",
    )
    router_parts, tables, smalls = [None] * LAYERS, [None] * LAYERS, [None] * LAYERS
    residual_sums, shard_sums = [None] * LAYERS, [None] * LAYERS
    router_parts[LAYERS - 1] = router_part
    units, attn_units, mines = [None] * LAYERS, [None] * LAYERS, [None] * LAYERS
    for l in reversed(range(LAYERS)):
        rec = records[l]
        last = l == 0
        reduce = fast and l < LAYERS - 1
        arrays = [buffer.reshape(EXPERTS, SLOTS, width), rec["received"], rec["up_eff"], rec["down_eff"]]
        outs = [(block_rows, bf16)]
        scratch = [
            pltpu.VMEM(block_rows, bf16),
            pltpu.VMEM((dp, SLOTS, hidden), bf16),
            pltpu.VMEM((dp, SLOTS, hidden), f32),
            pltpu.VMEM((dp, SLOTS, hidden), bf16),
            pltpu.VMEM(block_rows, bf16),
        ]
        if fast:
            outs.append(((2, mp, width, width), bf16))
            scratch += [pltpu.VMEM((width, hidden), f32)] * 2
        else:
            outs += [((width, hidden), f32)] * 2
        if reduce:
            arrays += [mines[l + 1], attn_units[l + 1]]
            outs += [((2, mp, width, width), bf16), ((width, width), bf16)]
            scratch += RowSum.scratch(1, width) + RowGather.scratch(2)
        results = list(
            expert_call(
                functools.partial(expert_backward_kernel, dp, mp, fast, reduce), arrays, outs, scratch, dp, LAYERS + l,
                f"experts_back_{l}", 10 * dp * SLOTS * width * hidden,
            )
        )
        returned_grad = results.pop(0)
        if fast:
            units[l] = results.pop(0)
        else:
            residual_sums[l] = lax.psum(tuple(t.astype(bf16) for t in results[:2]), "mp")
        if reduce:
            full_above, mine_above = results
            shard_above = lax.psum(jnp.concatenate([mines[l + 1], mine_above[None]], 0), "dp")
        window_in, qk, v, probs, att, proj_full = rec["saved"]
        qkv_full = gathered[l][0].reshape(3 * width, width)
        arrays = [
            ("smem", image_valid),
            ("image", grad),
            ("whole", by_piece(returned_grad)),
            ("image", logit_grad),
            ("image", rec["middle"]),
            ("image", rec["carried"]),
            (l, routers),
            ("image", col_form),
            ("whole", moves[l]),
            ("whole", backs[l]),
            (l, norm_gain),
            ("whole", proj_full),
            ("whole", qkv_full),
            ("image", window_in),
            ("image", qk),
            ("image", v),
            ("image", probs),
            ("image", att),
        ]
        outs = [("image", patches.shape if last else token, f32)]
        scratch = [pltpu.VMEM((3 * width, (2 - images % 2) * IMGROWS), bf16)]
        if fast:
            arrays.append(("whole", units[l]))
            outs += [("whole", (mp, width, width), bf16), ("whole", (2, width, width), bf16)]
            scratch += [pltpu.VMEM((3 * width, width), f32), pltpu.VMEM((width, width), f32)]
        else:
            outs += [("whole", (3 * width, width), f32), ("whole", (width, width), f32)]
        outs += [("whole", (HEADS, WPAD, LANES), f32), ("whole", (8, width), f32)]
        if last:
            arrays.append(("whole", leave))
        else:
            below = records[l - 1]
            arrays += [
                ("image", row_form),
                ("image", below["expert_out"]),
                ("image", below["second_low"]),
                (l - 1, routers),
            ]
            outs += [
                ("image", (images, IMGROWS, LANES), f32),
                ("whole", (LANES, width), f32),
                ("whole", buffer_shape, bf16),
            ]
            scratch.append(pltpu.VMEM(buffer_shape, f32))
        if fast:
            scratch += RowSum.scratch(2, width)
        results = list(
            image_call(
                functools.partial(attention_backward_kernel, last, mp, fast),
                images, arrays, outs, scratch, f"attend_back_{l}", 2 * LAYERS + 1 + l if fast else None,
            )
        )
        grad = results.pop(0)
        if fast:
            attn_units[l], mines[l] = results[:2]
            results = results[2:]
        else:
            qkv_part, proj_part = results[:2]
            results = results[2:]
        tables[l], smalls[l] = results[:2]
        if not last:
            logit_grad, router_parts[l - 1], buffer = results[2:]
        if fast:
            continue
        attn = (
            lax.psum_scatter(qkv_part.astype(bf16), "mp", scatter_dimension=0, tiled=True),
            lax.psum_scatter(proj_part.T.astype(bf16), "mp", scatter_dimension=0, tiled=True),
        )
        up_sum, down_sum = residual_sums[l]
        if split > 1:
            begin = lax.axis_index("dp") % split * hidden
            empty = jnp.zeros((width, hidden_full), bf16)
            up_sum = lax.dynamic_update_slice_in_dim(empty, up_sum, begin, 1)
            down_sum = lax.dynamic_update_slice_in_dim(empty, down_sum, begin, 1)
        up_columns, down_columns = core_up.shape[-1], core_down.shape[-1]
        up_shard = lax.dynamic_slice_in_dim(up_sum, row_index * up_columns, up_columns, 1)
        down_shard = lax.dynamic_slice_in_dim(down_sum, row_index * down_columns, down_columns, 0)
        shard_sums[l] = lax.psum((attn[0], attn[1], up_shard, down_shard), "dp")

    entry_turned = (entries[:, None] == jnp.arange(OFFSETS)[None, :]).astype(f32)
    table_part = jnp.dot(
        jnp.stack(tables, 0).reshape(LAYERS * HEADS, WPAD * LANES), entry_turned, precision=highest
    )
    small_part = jnp.stack(smalls, 0)[:, :4]
    router_part = jnp.stack(router_parts, 0)[:, :EXPERTS]
    if fast:
        lines = jnp.concatenate(
            [
                jnp.pad(table_part, ((0, 0), (0, width - OFFSETS))),
                router_part.reshape(-1, width),
                small_part.reshape(-1, width),
            ],
            0,
        )
        count = -(-lines.shape[0] // 64) * 64
        full, closed, lines = closing_call(
            dp, mp, mines[0], attn_units[0], jnp.pad(lines, ((0, count - lines.shape[0]), (0, 0))), 2 * LAYERS
        )
        *attn_grads, core_up_grad, core_down_grad, residual_up_grad, residual_down_grad = format_call(
            [full, full_above], [closed, shard_above], qkv_weight.shape[-1]
        )
        attn_grads = [a.transpose(0, 2, 1) for a in attn_grads]
        core_grads = (core_up_grad, core_down_grad.transpose(0, 2, 1))
        at = LAYERS * HEADS
        table_sum = lines[:at, :OFFSETS]
        router_sum = lines[at : at + LAYERS * EXPERTS].reshape(LAYERS, EXPERTS, width)
        at += LAYERS * EXPERTS
        small_sum = lines[at : at + LAYERS * 4].reshape(LAYERS, 4, width)
    else:
        table_sum, small_sum, router_sum = lax.psum((table_part, small_part, router_part), ("dp", "mp"))

        def shard(k):
            return jnp.stack([shard_sums[l][k] for l in range(LAYERS)], 0).astype(f32)

        attn_grads = (shard(0).transpose(0, 2, 1), shard(1).transpose(0, 2, 1))
        core_grads = (shard(2), shard(3).transpose(0, 2, 1))
        residual_up_grad, residual_down_grad = (
            jnp.stack([residual_sums[l][k] for l in range(LAYERS)], 0).astype(f32) for k in range(2)
        )
        residual_up_grad = residual_up_grad[:, None]
        residual_down_grad = residual_down_grad.transpose(0, 2, 1)[:, None]

    return (
        block_output,
        grad,
        attn_grads[0],
        attn_grads[1],
        core_grads[0],
        core_grads[1],
        residual_up_grad,
        residual_down_grad,
        table_sum.reshape(LAYERS, HEADS, OFFSETS).transpose(0, 2, 1),
        router_sum.transpose(0, 2, 1),
        small_sum[:, 0:2],
        small_sum[:, 2:4],
    )


def solution(mesh):
    placed = (
        P(("dp", "mp"), None, None),
        P(None, None, "mp"),
        P(None, None, "mp"),
        P(None, None, "mp"),
        P(None, None, "mp"),
        P(None, "dp", None, None),
        P(None, "dp", None, None),
        P(),
        P(),
        P(),
        P(),
        P(("dp", "mp"), None, None),
        P(("dp", "mp")),
        P(("dp", "mp"), None),
        P(("dp", "mp"), None),
        P(("dp", "mp"), None, None),
    )
    return jax.shard_map(
        per_device,
        mesh=mesh,
        in_specs=placed,
        out_specs=(
            P(("dp", "mp"), None, None),
            P(("dp", "mp"), None, None),
            P(None, None, "mp"),
            P(None, None, "mp"),
            P(None, None, "mp"),
            P(None, None, "mp"),
            P(None, "dp", None, None),
            P(None, "dp", None, None),
            P(),
            P(),
            P(),
            P(),
        ),
        check_vma=False,
    )
```

```python
import functools

import jax
import jax.numpy as jnp
import numpy as np
from jax import lax
from jax.experimental import pallas as pl
from jax.experimental.pallas import tpu as pltpu
from jax.sharding import PartitionSpec as P

HEADS = 12
HEAD_DIM = 32
EXPERTS = 8
WINDOW = 7
GRID = 14
SHIFT = 3
LAYERS = 2
WINPOS = 49
OFFSETS = 169
CAP = 122

WPAD = 64
IMGROWS = 256
PATCHES = 196
SLOTS = 128
ROWS = EXPERTS * SLOTS
LANES = 128
GROUP = 4
PAIRS = 2
TABLE = 256

bf16 = jnp.bfloat16
f32 = jnp.float32
highest = lax.Precision.HIGHEST
norm_epsilon = 1e-05
mask_fill = -100.0
head_scale = HEAD_DIM ** (-0.5)
MESH = pl.DeviceIdType.MESH
MIB = 1024 * 1024


def nn(a, b):
    return lax.dot_general(a, b, (((1,), (0,)), ((), ())), preferred_element_type=f32)


def nt(a, b):
    return lax.dot_general(a, b, (((1,), (1,)), ((), ())), preferred_element_type=f32)


def tn(a, b):
    return lax.dot_general(a, b, (((0,), (0,)), ((), ())), preferred_element_type=f32)


def iota(shape, dim):
    return lax.broadcasted_iota(jnp.int32, shape, dim)


def onehot(flags):
    return jnp.where(flags, 1.0, 0.0).astype(bf16)


def natural_of_row(shifted):
    moved = SHIFT if shifted else 0
    blocks = GRID // WINDOW
    out = -np.ones(IMGROWS, np.int32)
    for window in range(blocks * blocks):
        for cell in range(WINPOS):
            row = (window // blocks * WINDOW + cell // WINDOW + moved) % GRID
            col = (window % blocks * WINDOW + cell % WINDOW + moved) % GRID
            out[window * WPAD + cell] = row * GRID + col
    return out


def key_base_of(key):
    return (2 * WINDOW) * (WINDOW - 1) - (key // WINDOW * (2 * WINDOW - 1) + key % WINDOW)


def enter_table():
    held = natural_of_row(False)
    return (held[:, None] == np.arange(PATCHES)[None, :]).astype(np.float32)


def move_table(shifted):
    first, second = natural_of_row(False), natural_of_row(shifted)
    same = (second[:, None] == first[None, :]) & (second[:, None] >= 0)
    return same.astype(np.float32)


def cell_entries():
    cell = np.arange(LANES) % WPAD
    return np.where(cell < WINPOS, cell // WINDOW * (2 * WINDOW - 1) + cell % WINDOW, -4 * TABLE).astype(np.int32)


def norm_parts(x):
    width = x.shape[-1]
    center = x - jnp.sum(x, -1, keepdims=True) * (1.0 / width)
    spread = jnp.sum(center * center, -1, keepdims=True) * (1.0 / width)
    rstd = lax.rsqrt(spread + norm_epsilon)
    return center * rstd, rstd


def norm_back(grad, gain, xhat, rstd):
    width = xhat.shape[-1]
    dxhat = grad * gain
    mean_one = jnp.sum(dxhat, -1, keepdims=True) * (1.0 / width)
    mean_two = jnp.sum(dxhat * xhat, -1, keepdims=True) * (1.0 / width)
    return rstd * (dxhat - mean_one - xhat * mean_two)


def split_two(x):
    high = x.astype(bf16)
    return high, (x - high.astype(f32)).astype(bf16)


def collect(pos_col, returned_ref):
    pick = onehot(pos_col == iota((pos_col.shape[0], ROWS), 1))
    out = nn(pick, returned_ref[0])
    for piece in range(1, returned_ref.shape[0]):
        out = out + nn(pick, returned_ref[piece])
    return out


def join(ref):
    return ref[...].reshape(ref.shape[0] * ref.shape[1], *ref.shape[2:])


def store(ref, rows):
    ref[...] = rows.reshape(ref.shape).astype(ref.dtype)


def per_image(function, count):
    return jnp.concatenate([function(i) for i in range(count)], 0)


def image_rows(i):
    return slice(i * IMGROWS, (i + 1) * IMGROWS)


def lay_positions(row_ref):
    return jnp.concatenate([row_ref[i, 0:1, :] for i in range(row_ref.shape[0])], 1)


def spread_rows(pos_row, rows_low):
    return nn(onehot(iota((ROWS, pos_row.shape[1]), 0) == pos_row), rows_low)


def route(second_low, router, pos_col):
    logits = nt(second_low, router)
    lane = iota(logits.shape, 1)
    logits = jnp.where(lane < EXPERTS, logits, -1e30)
    expo = jnp.exp(logits - jnp.max(logits, -1, keepdims=True))
    probs = expo / jnp.sum(expo, -1, keepdims=True)
    expert = jnp.where(pos_col >= 0, pos_col // SLOTS, -1)
    chosen = jnp.where(lane == expert, 1.0, 0.0)
    return probs, chosen, jnp.sum(probs * chosen, -1, keepdims=True)


def head_masks():
    rows = iota((LANES, LANES), 0) // HEAD_DIM
    return [onehot(rows == h) for h in range(GROUP)]


def lane_masks():
    lane = iota((WPAD, LANES), 1)
    return [onehot(lane < WPAD), onehot(lane >= WPAD)]


def key_base(key):
    return (2 * WINDOW) * (WINDOW - 1) - (key // WINDOW * (2 * WINDOW - 1) + lax.rem(key, WINDOW))


def form_bias(bias_ref, table_ref, entry_row):
    layers, heads = bias_ref.shape[:2]
    bias_ref[...] = jnp.where(iota(bias_ref.shape, 2) < WINPOS, 0.0, -1e30)
    table = table_ref[...]
    high = table.astype(bf16)
    mid, low = split_two(table - high.astype(f32))

    def step(key, carry):
        pick = onehot(iota((TABLE, LANES), 0) == entry_row + key_base(key))
        row = nn(high, pick) + nn(mid, pick) + nn(low, pick)
        for layer in range(layers):
            part = row[layer * heads : (layer + 1) * heads]
            bias_ref[layer, :, pl.ds(key, 1), :] = part.reshape(heads, 1, LANES)
        return carry

    lax.fori_loop(0, WINPOS, step, 0)


def table_grad(parts, entry_col):
    heads = parts[0].shape[0]

    def step(key, total):
        rows = jnp.concatenate([ref[:, pl.ds(key, 1), :].reshape(heads, LANES) for ref in parts], 0)
        pick = onehot(iota((LANES, TABLE), 1) == entry_col + key_base(key))
        high, low = split_two(rows)
        return total + nn(high, pick) + nn(low, pick)

    return lax.fori_loop(0, WINPOS, step, jnp.zeros((heads * len(parts), TABLE), f32))


def attention_forward_kernel(first, shifted, mp, gather, *refs):
    refs = list(refs)
    if first:
        patches_ref, enter_ref = refs[:2]
        refs = refs[2:]
    else:
        prev_ref, prev_gate_ref, returned_ref = refs[:3]
        refs = refs[3:]
    (
        valid_ref, col_ref, row_ref, qkv_ref, proj_ref, bias_ref, move_ref, back_ref, gain_ref, nbias_ref, router_ref,
    ) = refs[:11]
    gain_ref, nbias_ref, router_ref = (ref.at[0] for ref in (gain_ref, nbias_ref, router_ref))
    refs = refs[11:]
    if first:
        table_ref, entry_ref = bias_ref, refs.pop(0)
    if gather:
        core_up_ref, core_down_ref = refs[:2]
        refs = refs[2:]
    carried_ref = refs.pop(0)
    if first:
        biases_ref = refs.pop(0)
        bias_ref = biases_ref.at[0]
    else:
        expert_out_ref = refs.pop(0)
        bias_ref = bias_ref.at[0]
    middle_ref, second_ref, gate_ref, buffer_ref, window_ref, qk_ref, v_ref, probs_ref, att_ref, proj_full = refs[:10]
    refs = refs[10:]
    if gather:
        qkv_full = refs.pop(0)
        up_out, down_out = refs[:2]
        refs = refs[2:]
    total_ref = refs.pop(0)
    step = pl.program_id(0)
    final = pl.num_programs(0) - 1
    count, _, width = carried_ref.shape
    if gather:
        shards = [ref.at[0] for ref in (qkv_ref, proj_ref, core_up_ref, core_down_ref)]
        qkv_ref, proj_ref = refs[:2]
        moving = WeightGather(shards, [qkv_ref, proj_ref, up_out, down_out], refs[2:])

        @pl.when(step == 0)
        def _():
            pl.semaphore_wait(moving.row.greet(), 2)
            for k in (0, 1):
                moving.start(k)
            form_bias(biases_ref, table_ref, entry_ref[...])
            for k in (0, 1):
                moving.forward(k)
            for k in (2, 3):
                moving.start(k)
            for k in (0, 1):
                moving.arrive(k)

        @pl.when(step == final)
        def _():
            for k in (2, 3):
                moving.forward(k)

    @pl.when(step == 0)
    def _():
        if gather:
            qkv_full[...] = join(qkv_ref)
        elif first:
            form_bias(biases_ref, table_ref, entry_ref[...])
        proj_full[...] = join(proj_ref).astype(f32).T.astype(bf16)
        total_ref[...] = jnp.zeros(total_ref.shape, f32)

    pos_col = join(col_ref)[:, 0:1]
    if first:
        x = per_image(lambda i: nn(enter_ref[...], patches_ref[i]), count)
    else:
        expert_out = collect(pos_col, returned_ref)
        store(expert_out_ref, expert_out)
        x = join(prev_ref) + join(prev_gate_ref) * expert_out
    store(carried_ref, x)
    xhat, _ = norm_parts(x)
    normed = (xhat * gain_ref[0:1, :] + nbias_ref[0:1, :]).astype(bf16)
    window_in = per_image(lambda i: nn(move_ref[...], normed[image_rows(i)]), count).astype(bf16)
    store(window_ref, window_in)
    qkv = join(qkv_ref)
    turned = nt(qkv, window_in).astype(bf16)
    straight = nt(window_in, qkv[width:]).astype(bf16)
    for i in range(count):
        qk_ref[i] = turned[: 2 * width, image_rows(i)]
    store(v_ref, straight[:, width:])
    heads_rows = head_masks()
    halves = lane_masks()
    low_lane = iota((WPAD, LANES), 1) < WPAD
    if shifted:
        row_labels = [nt(row_ref[i].astype(f32).astype(bf16), move_ref[...]) for i in range(count)]
        col_labels = [nn(move_ref[...], col_ref[i].astype(f32).astype(bf16)) for i in range(count)]
    for pair in range(PAIRS * count):
        image, side = pair // PAIRS, pair % PAIRS
        across = slice(pair * LANES, (pair + 1) * LANES)
        within = slice(side * LANES, (side + 1) * LANES)
        if shifted:
            ahead = col_labels[image][side * LANES : side * LANES + WPAD, 1:2]
            behind = col_labels[image][side * LANES + WPAD : (side + 1) * LANES, 1:2]
            key_label = jnp.where(low_lane, ahead, behind)
            mask = jnp.where(key_label == row_labels[image][1:2, within], 0.0, mask_fill)
        for group in range(HEADS // GROUP):
            features = slice(group * LANES, (group + 1) * LANES)
            queries = turned[features, across]
            spread = jnp.concatenate([queries * heads_rows[h] for h in range(GROUP)], 1)
            raw = nn(straight[across, features], spread)
            for h in range(GROUP):
                head = group * GROUP + h
                part = raw[:, h * LANES : (h + 1) * LANES]
                scores = jnp.where(low_lane, part[:WPAD], part[WPAD:]) * head_scale + bias_ref[head]
                if shifted:
                    scores = scores + mask
                expo = jnp.exp(scores - jnp.max(scores, 0, keepdims=True))
                probs = (expo * (1.0 / jnp.sum(expo, 0, keepdims=True))).astype(bf16)
                probs_ref[image, side * HEADS + head] = probs
                both = jnp.concatenate([probs * halves[0], probs * halves[1]], 0)
                at = slice(head * HEAD_DIM, (head + 1) * HEAD_DIM)
                values = turned[2 * width + head * HEAD_DIM : 2 * width + (head + 1) * HEAD_DIM, across]
                att_ref[image, at, within] = nn(values, both).astype(bf16)
    attended = per_image(lambda i: nt(back_ref[...], att_ref[i]), count).astype(bf16)
    branch = nt(attended, join(proj_ref))
    middle = x + per_image(lambda i: valid_ref[step * count + i].astype(f32) * branch[image_rows(i)], count)
    store(middle_ref, middle)
    xhat, _ = norm_parts(middle)
    second_low = (xhat * gain_ref[1:2, :] + nbias_ref[1:2, :]).astype(bf16)
    store(second_ref, second_low)
    _, _, gate = route(second_low, router_ref[...], pos_col)
    store(gate_ref, gate)
    total_ref[...] += spread_rows(lay_positions(row_ref), second_low)

    @pl.when(step == final)
    def _():
        buffer_ref[...] = total_ref[...].astype(bf16)
        if gather:
            for k in (2, 3):
                moving.arrive(k)
            for k in range(4):
                moving.sent(k)


def image_spec(array_shape, count):
    rest = tuple(array_shape[1:])
    zeros = (0,) * len(rest)
    return pl.BlockSpec((count,) + rest, lambda i: (i,) + zeros)


def whole_spec(array_shape):
    zeros = (0,) * len(array_shape)
    return pl.BlockSpec(tuple(array_shape), lambda i: zeros)


def image_call(kernel, images, arrays, outs, scratch, name, collective_id=None):
    count = 2 - images % 2

    def spec(kind, shape):
        if isinstance(kind, int):
            rest = tuple(shape[1:])
            return pl.BlockSpec((1,) + rest, lambda i: (kind,) + (0,) * len(rest))
        if kind in ("smem", "any"):
            return pl.BlockSpec(memory_space=pltpu.SMEM if kind == "smem" else pl.ANY)
        return image_spec(shape, count) if kind == "image" else whole_spec(shape)

    return pl.pallas_call(
        kernel,
        grid=(images // count,),
        out_shape=[jax.ShapeDtypeStruct(shape, dtype) for _, shape, dtype in outs],
        in_specs=[spec(kind, array.shape) for kind, array in arrays],
        out_specs=[spec(kind, shape) for kind, shape, _ in outs],
        scratch_shapes=scratch,
        compiler_params=pltpu.CompilerParams(
            vmem_limit_bytes=56 * MIB,
            dimension_semantics=("arbitrary",),
            collective_id=collective_id,
            has_side_effects=collective_id is not None,
        ),
        name=name,
    )(*[array for _, array in arrays])


def send_part(g, expert_out, second_low, router, pos_col, pos_row, logit_ref, router_grad_ref, total_ref):
    probs, chosen, gate = route(second_low, router, pos_col)
    gate_grad = jnp.where(pos_col >= 0, jnp.sum(g * expert_out, -1, keepdims=True), 0.0)
    sent = (gate * g).astype(bf16)
    logit_grad = gate_grad * gate * (chosen - probs)
    store(logit_ref, logit_grad)
    high, low = split_two(logit_grad)
    router_grad_ref[...] += tn(high, second_low) + tn(low, second_low)
    total_ref[...] += spread_rows(pos_row, sent)


def turn_kernel(
    prev_ref, gate_ref, returned_ref, cotangent_ref, enter_ref, leave_ref, col_ref, row_ref, second_ref, router_ref,
    block_ref, grad_ref, logit_ref, router_grad_ref, buffer_ref, total_ref,
):
    step = pl.program_id(0)
    count = cotangent_ref.shape[0]

    @pl.when(step == 0)
    def _():
        total_ref[...] = jnp.zeros(total_ref.shape, f32)
        router_grad_ref[...] = jnp.zeros(router_grad_ref.shape, f32)

    pos_col = join(col_ref)[:, 0:1]
    expert_out = collect(pos_col, returned_ref)
    x = (join(prev_ref) + join(gate_ref) * expert_out).astype(bf16)
    for i in range(count):
        block_ref[i] = nn(leave_ref[...], x[image_rows(i)]).astype(bf16)
    g = per_image(lambda i: nn(enter_ref[...], cotangent_ref[i]), count)
    store(grad_ref, g)
    send_part(
        g, expert_out, join(second_ref), router_ref[0], pos_col, lay_positions(row_ref), logit_ref, router_grad_ref, total_ref
    )

    @pl.when(step == pl.num_programs(0) - 1)
    def _():
        buffer_ref[...] = total_ref[...].astype(bf16)


def attention_backward_kernel(last, dp, mp, fast, *refs):
    (
        valid_ref, grad_ref, returned_ref, logit_ref, middle_ref, carried_ref, router_ref, col_ref, move_ref, back_ref,
        gain_ref, proj_ref, qkv_ref, window_ref, qk_ref, v_ref, probs_ref, att_ref,
    ) = refs[:18]
    refs = refs[18:]
    refs = list(refs)
    if fast:
        units_ref = refs.pop(0)
    if last:
        leave_ref = refs.pop(0)
        if fast:
            table_above, small_above, router_above, router_here, entry_ref = refs[:5]
            refs = refs[5:]
    else:
        row_ref, expert_out_ref, second_ref, router_next_ref = refs[:4]
        refs = refs[4:]
    out_ref = refs.pop(0)
    closing = None
    if fast and last:
        full_ref, shard_ref, small_out = refs[:3]
        refs = refs[3:]
    else:
        if fast:
            unit_ref, mine_ref = refs[:2]
        else:
            qkv_grad_ref, proj_grad_ref = refs[:2]
        table_ref, small_ref = refs[2:4]
        refs = refs[4:]
    if not last:
        logit_out_ref, router_grad_ref, buffer_ref = refs[:3]
        refs = refs[3:]
    turned = refs.pop(0)
    if fast:
        qkv_grad_ref, proj_grad_ref = refs[:2]
        refs = refs[2:]
    if not last:
        total_ref = refs.pop(0)
    step = pl.program_id(0)
    final = pl.num_programs(0) - 1
    count, _, width = carried_ref.shape
    if fast:
        row = Row()
        if last:
            table_ref, small_ref, unit_ref, lines_ref, full_in, shard_in, small_in = refs[:7]
            closing = Closing(row, dp, units_ref, unit_ref, lines_ref, full_in, shard_in, small_in, refs[7:])
            sums = closing.sums
        else:
            sums = RowSum(
                row, [units_ref.at[k] for k in range(2)], refs[0], refs[1], refs[2],
                [mine_ref.at[k] for k in range(2)], refs[3:7],
            )

        @pl.when(step == 0)
        def _():
            if last:
                closing.greet()
            else:
                pl.semaphore_wait(row.greet(), 2)
            for k in range(2):
                sums.start(k)

    if closing:

        @pl.when(step == final)
        def _():
            closing.take(0)

    @pl.when(step == 0)
    def _():
        qkv_grad_ref[...] = jnp.zeros(qkv_grad_ref.shape, f32)
        proj_grad_ref[...] = jnp.zeros(proj_grad_ref.shape, f32)
        table_ref[...] = jnp.zeros(table_ref.shape, f32)
        small_ref[...] = jnp.zeros(small_ref.shape, f32)
        if not last:
            total_ref[...] = jnp.zeros(total_ref.shape, f32)
            router_grad_ref[...] = jnp.zeros(router_grad_ref.shape, f32)

    pos_col = join(col_ref)[:, 0:1]
    g = join(grad_ref)
    high, low = split_two(join(logit_ref))
    gain_ref, router = gain_ref.at[0], router_ref[0]
    normed_grad = collect(pos_col, returned_ref) + nn(high, router) + nn(low, router)
    xhat, rstd = norm_parts(join(middle_ref))
    small_ref[1:2, :] += jnp.sum(normed_grad * xhat, 0, keepdims=True)
    small_ref[3:4, :] += jnp.sum(normed_grad, 0, keepdims=True)
    middle_grad = g + norm_back(normed_grad, gain_ref[1:2, :], xhat, rstd)

    def branch_part(i):
        low_part = (valid_ref[step * count + i].astype(f32) * middle_grad[image_rows(i)]).astype(bf16)
        return nn(move_ref[...], low_part)

    branch_grad = per_image(branch_part, count).astype(bf16)
    for i in range(count):
        proj_grad_ref[...] += nn(att_ref[i], branch_grad[image_rows(i)])
    att_grad = nt(proj_ref[...], branch_grad).astype(bf16)
    if fast:

        @pl.when(step == 0)
        def _():
            for k in range(2):
                sums.middle(k)

        if closing:

            @pl.when(step == final)
            def _():
                closing.take(1)

    heads_rows = head_masks()
    halves = lane_masks()
    low_lane = iota((WPAD, LANES), 1) < WPAD
    for pair in range(PAIRS * count):
        image, side = pair // PAIRS, pair % PAIRS
        across = slice(pair * LANES, (pair + 1) * LANES)
        within = slice(side * LANES, (side + 1) * LANES)
        for group in range(HEADS // GROUP):
            features = slice(group * LANES, (group + 1) * LANES)
            grads = att_grad[features, across]
            spread = jnp.concatenate([grads * heads_rows[h] for h in range(GROUP)], 1)
            raw = nn(v_ref[image, within, features], spread)
            for h in range(GROUP):
                head = group * GROUP + h
                at = slice(head * HEAD_DIM, (head + 1) * HEAD_DIM)
                below = slice(width + head * HEAD_DIM, width + (head + 1) * HEAD_DIM)
                lowest = slice(2 * width + head * HEAD_DIM, 2 * width + (head + 1) * HEAD_DIM)
                part = raw[:, h * LANES : (h + 1) * LANES]
                probs_grad = jnp.where(low_lane, part[:WPAD], part[WPAD:])
                probs_low = probs_ref[image, side * HEADS + head]
                probs = probs_low.astype(f32)
                weighted = probs * probs_grad
                scores_grad = weighted - probs * jnp.sum(weighted, 0, keepdims=True)
                table_ref[head] += scores_grad
                scores_low = scores_grad.astype(bf16)
                both = jnp.concatenate([scores_low * halves[0], scores_low * halves[1]], 0)
                probs_both = jnp.concatenate([probs_low * halves[0], probs_low * halves[1]], 0)
                turned[at, across] = (nn(qk_ref[image, below, within], both) * head_scale).astype(bf16)
                turned[below, across] = (nt(qk_ref[image, at, within], both) * head_scale).astype(bf16)
                turned[lowest, across] = nt(att_grad[at, across], probs_both).astype(bf16)
    qkv_grad_ref[...] += nn(turned[...], join(window_ref))
    if fast:

        @pl.when(step == final)
        def _():
            columns, rows = 3 * width // mp, width // mp
            proj_turned = proj_grad_ref[...].T
            for place in range(mp):
                q = quarter_at(place, mp)
                unit_ref[place, :columns] = qkv_grad_ref[q * columns : (q + 1) * columns].astype(bf16)
                unit_ref[place, columns:] = proj_turned[q * rows : (q + 1) * rows].astype(bf16)
            if closing:
                closing.open()

    mixed_grad = per_image(lambda i: nt(back_ref[...], turned[:, image_rows(i)]), count).astype(bf16)
    first_grad = nn(mixed_grad, qkv_ref[...])
    xhat, rstd = norm_parts(join(carried_ref))
    small_ref[0:1, :] += jnp.sum(first_grad * xhat, 0, keepdims=True)
    small_ref[2:3, :] += jnp.sum(first_grad, 0, keepdims=True)
    out = middle_grad + norm_back(first_grad, gain_ref[0:1, :], xhat, rstd)
    if closing:

        @pl.when(step == final)
        def _():
            closing.attend()

    if last:
        top = out.astype(bf16)
        rest = out - top.astype(f32)
        mid, low = split_two(rest)
        leave = leave_ref[...]
        for i in range(count):
            at = image_rows(i)
            out_ref[i] = nn(leave, top[at]) + nn(leave, mid[at]) + nn(leave, low[at])
    else:
        store(out_ref, out)
        send_part(
            out, join(expert_out_ref), join(second_ref), router_next_ref[0], pos_col, lay_positions(row_ref), logit_out_ref,
            router_grad_ref, total_ref,
        )

    @pl.when(step == final)
    def _():
        if not last:
            buffer_ref[...] = total_ref[...].astype(bf16)
        if closing:
            heads = 2 * HEADS
            lines_ref[...] = jnp.zeros(lines_ref.shape, f32)
            lines_ref[:heads, :TABLE] = table_grad([table_ref, table_above], entry_ref[...])
            lines_ref[heads : heads + EXPERTS] = router_here[:EXPERTS]
            lines_ref[heads + EXPERTS : heads + 2 * EXPERTS] = router_above[:EXPERTS]
            lines_ref[heads + 2 * EXPERTS : heads + 2 * EXPERTS + 8] = small_ref[...]
            lines_ref[heads + 2 * EXPERTS + 8 : heads + 2 * EXPERTS + 16] = small_above[...]
            closing.finish()
            full_ref[...] = full_in[...]
            shard_ref[...] = shard_in[...]
            small_out[...] = small_in[...]
        elif fast:
            for k in range(2):
                sums.end(k)
                sums.finish(k)


def quarter_at(place, mp):
    return place % (mp // 2) * 2 + place // (mp // 2)


def add_up(*parts):
    total = parts[0].astype(f32)
    for part in parts[1:]:
        total = total + part.astype(f32)
    return total


def to_row(source, target, sems, k, row):
    return pltpu.make_async_remote_copy(
        src_ref=source,
        dst_ref=target,
        send_sem=sems[0].at[k],
        recv_sem=sems[1].at[k],
        device_id={"mp": row},
        device_id_type=MESH,
    )


class Row:
    def __init__(self):
        row = lax.axis_index("mp")
        self.row, self.core, self.y = row, lax.rem(row, 2), lax.div(row, 2)
        self.sibling, self.across = row + 1 - 2 * self.core, row + 2 - 4 * self.y
        self.place = self.core * 2 + self.y
        self.place_across = self.core * 2 + 1 - self.y

    def greet(self):
        barrier = pltpu.get_barrier_semaphore()
        for row in (self.sibling, self.across):
            pl.semaphore_signal(barrier, inc=1, device_id={"mp": row}, device_id_type=MESH)
        return barrier


class RowSum:
    semaphores = 4

    def __init__(self, row, units, core_in, y_out, y_in, mine, sems):
        self.row, self.units, self.mine = row, units, mine
        self.core_in, self.y_out, self.y_in = core_in, y_out, y_in
        self.sems = (sems[:2], sems[2:])

    def pair(self, k):
        theirs = self.units[k].at[pl.ds(2 * (1 - self.row.core), 2)]
        return to_row(theirs, self.core_in.at[k], self.sems[0], k, self.row.sibling)

    def cross(self, k):
        return to_row(self.y_out.at[k], self.y_in.at[k], self.sems[1], k, self.row.across)

    def start(self, k):
        self.pair(k).start()

    def middle(self, k):
        self.pair(k).wait_recv()
        other = 1 - self.row.y
        mixed = add_up(self.units[k][self.row.core * 2 + other], self.core_in[k, other])
        self.y_out[k] = mixed.astype(bf16)
        self.cross(k).start()

    def end(self, k):
        self.cross(k).wait_recv()
        self.mine[k][...] = add_up(
            self.units[k][self.row.place], self.core_in[k, self.row.y], self.y_in[k]
        ).astype(bf16)

    def finish(self, k):
        self.pair(k).wait_send()
        self.cross(k).wait_send()

    @classmethod
    def scratch(cls, count, width):
        return [
            pltpu.VMEM((count, 2, width, width), bf16),
            pltpu.VMEM((count, width, width), bf16),
            pltpu.VMEM((count, width, width), bf16),
        ] + [pltpu.SemaphoreType.DMA((count,))] * cls.semaphores


class RowGather:
    semaphores = 6

    def __init__(self, row, sources, fulls, slot, slot_across, sems):
        self.row, self.sources, self.fulls = row, sources, fulls
        self.slot, self.slot_across = slot, slot_across
        self.sems = (sems[:2], sems[2:4], sems[4:])

    def over(self, k):
        return to_row(self.sources[k], self.fulls[k].at[self.slot], self.sems[0], k, self.row.across)

    def near(self, k):
        return to_row(self.sources[k], self.fulls[k].at[self.slot], self.sems[1], k, self.row.sibling)

    def onward(self, k):
        block = self.fulls[k].at[self.slot_across]
        return to_row(block, block, self.sems[2], k, self.row.sibling)

    def start(self, k):
        self.over(k).start()
        self.near(k).start()

    def forward(self, k):
        self.over(k).wait_recv()
        self.onward(k).start()

    def arrive(self, k):
        self.near(k).wait_recv()
        self.onward(k).wait_recv()

    def sent(self, k):
        self.over(k).wait_send()
        self.near(k).wait_send()
        self.onward(k).wait_send()

    @classmethod
    def scratch(cls, count):
        return [pltpu.SemaphoreType.DMA((count,))] * cls.semaphores


class WeightGather(RowGather):
    def __init__(self, shards, fulls, sems):
        row = Row()
        super().__init__(row, shards, fulls, row.row, row.across, sems[:6])
        self.own_sem = sems[6]

    def own(self, k):
        return pltpu.make_async_copy(self.sources[k], self.fulls[k].at[self.slot], self.own_sem.at[k])

    def start(self, k):
        super().start(k)
        self.own(k).start()

    def arrive(self, k):
        super().arrive(k)
        self.own(k).wait()

    @classmethod
    def scratch(cls, count):
        return super().scratch(count) + [pltpu.SemaphoreType.DMA((count,))]


class Closing:
    lines = 64

    def __init__(self, row, dp, units_ref, attn_ref, lines_ref, full_ref, shard_ref, small_out, refs):
        self.row, self.lines_ref = row, lines_ref
        core_in, y_out, y_in = refs[:3]
        mine, x_in, half, z_in, self.s_core, self.s_one, self.s_y, s_mine, s_x, s_half, s_z = refs[7:18]
        self.sums = RowSum(
            row, [units_ref.at[0], units_ref.at[1], attn_ref], core_in, y_out, y_in, [mine.at[k] for k in range(3)], refs[3:7]
        )
        self.gather = RowGather(
            row, [mine.at[k] for k in range(2)], [full_ref.at[k] for k in range(2)], row.place, row.place_across, refs[18:24]
        )
        (s0, s1, s2, s3, self.x0, self.x1, self.z0, self.z1, self.w0, self.w1, self.v0, self.v1) = refs[24:]
        self.s_pair = to_row(lines_ref, self.s_core, (s0, s1), 0, row.sibling)
        self.s_cross = to_row(self.s_one, self.s_y, (s2, s3), 0, row.across)
        self.mine, self.full, self.s_mine = mine, full_ref, s_mine
        me = lax.axis_index("dp")
        self.x, self.z, self.deep = lax.rem(me, 2), lax.div(me, 2), dp // 2
        self.partner = me + 1 - 2 * self.x
        self.total = [mine.at[k] for k in range(3)] + [s_mine]
        self.arrived = [x_in.at[k] for k in range(3)] + [s_x]
        self.halves = [half.at[k] for k in range(3)] + [s_half]
        self.slots = [z_in.at[k] for k in range(3)] + [s_z]
        self.result = [shard_ref.at[k] for k in range(3)] + [small_out]

    def greet(self):
        barrier = self.row.greet()
        pl.semaphore_signal(barrier, inc=1, device_id={"dp": self.partner}, device_id_type=MESH)
        for off in range(1, self.deep):
            peer = lax.rem(self.z + off, self.deep) * 2 + self.x
            pl.semaphore_signal(barrier, inc=1, device_id={"dp": peer}, device_id_type=MESH)
        pl.semaphore_wait(barrier, 3 + self.deep - 1)

    def cut(self, k):
        height = self.total[k].shape[0] // 2
        return height, height // self.deep

    def over_x(self, k):
        height, _ = self.cut(k)
        away = self.total[k].at[pl.ds(pl.multiple_of((1 - self.x) * height, height), height)]
        return to_peer(away, self.arrived[k], self.x0.at[k], self.x1.at[k], self.partner)

    def over_z(self, k, off):
        _, piece = self.cut(k)
        to = lax.rem(self.z + off, self.deep)
        part = self.halves[k].at[pl.ds(pl.multiple_of(to * piece, piece), piece)]
        return to_peer(part, self.slots[k].at[off], self.z0.at[k, off], self.z1.at[k, off], to * 2 + self.x)

    def own_piece(self, k):
        height, piece = self.cut(k)
        return self.result[k].at[pl.ds(pl.multiple_of(self.x * height + self.z * piece, piece), piece)]

    def own_half(self, k):
        height, _ = self.cut(k)
        return self.result[k].at[pl.ds(pl.multiple_of(self.x * height, height), height)]

    def back_z(self, k, off):
        to = lax.rem(self.z + off, self.deep)
        return to_peer(self.own_piece(k), self.own_piece(k), self.w0.at[k, off], self.w1.at[k, off], to * 2 + self.x)

    def back_x(self, k):
        return to_peer(self.own_half(k), self.own_half(k), self.v0.at[k], self.v1.at[k], self.partner)

    def halve(self, k):
        self.over_x(k).wait_recv()
        height, _ = self.cut(k)
        keep = self.total[k][pl.ds(pl.multiple_of(self.x * height, height), height)]
        self.halves[k][...] = add_up(keep, self.arrived[k][...]).astype(self.halves[k].dtype)
        for off in range(1, self.deep):
            self.over_z(k, off).start()

    def quarter(self, k):
        for off in range(1, self.deep):
            self.over_z(k, off).wait_recv()
        _, piece = self.cut(k)
        keep = self.halves[k][pl.ds(pl.multiple_of(self.z * piece, piece), piece)]
        total = add_up(keep, *[self.slots[k][off] for off in range(1, self.deep)])
        self.own_piece(k)[...] = total.astype(self.result[k].dtype)
        for off in range(1, self.deep):
            self.back_z(k, off).start()

    def widen(self, k):
        for off in range(1, self.deep):
            self.back_z(k, off).wait_recv()
        self.back_x(k).start()

    def take(self, k):
        self.sums.end(k)
        self.over_x(k).start()

    def open(self):
        self.sums.start(2)
        for k in range(2):
            self.halve(k)

    def attend(self):
        self.sums.middle(2)
        for k in range(2):
            self.gather.start(k)
            self.full[k, self.row.place] = self.mine[k]
        for k in range(2):
            self.quarter(k)

    def finish(self):
        self.s_pair.start()
        self.sums.end(2)
        self.over_x(2).start()
        self.s_pair.wait_recv()
        self.s_one[...] = self.lines_ref[...] + self.s_core[...]
        self.s_cross.start()
        for k in range(2):
            self.widen(k)
        self.halve(2)
        self.s_cross.wait_recv()
        self.s_mine[...] = self.s_one[...] + self.s_y[...]
        self.over_x(3).start()
        self.quarter(2)
        self.halve(3)
        self.gather.forward(0)
        self.widen(2)
        self.quarter(3)
        self.gather.forward(1)
        self.widen(3)
        self.s_pair.wait_send()
        self.s_cross.wait_send()
        for k in range(3):
            self.sums.finish(k)
        for k in range(2):
            self.gather.arrive(k)
            self.gather.sent(k)
        for k in range(4):
            self.over_x(k).wait_send()
            for off in range(1, self.deep):
                self.over_z(k, off).wait_send()
                self.back_z(k, off).wait_send()
            self.back_x(k).wait()

    @classmethod
    def scratch(cls, dp, width):
        deep = dp // 2
        dma = pltpu.SemaphoreType.DMA
        lines = cls.lines
        flat = pltpu.VMEM((lines, width), f32)
        return (
            RowSum.scratch(3, width)
            + [
                pltpu.VMEM((3, width, width), bf16),
                pltpu.VMEM((3, width // 2, width), bf16),
                pltpu.VMEM((3, width // 2, width), bf16),
                pltpu.VMEM((3, deep, width // dp, width), bf16),
                flat, flat, flat, flat,
                pltpu.VMEM((lines // 2, width), f32),
                pltpu.VMEM((lines // 2, width), f32),
                pltpu.VMEM((deep, lines // dp, width), f32),
            ]
            + RowGather.scratch(2)
            + [dma((1,))] * 4
            + [dma((4,)), dma((4,))]
            + [dma((4, deep))] * 4
            + [dma((4,)), dma((4,))]
        )


def format_kernel(columns, *refs):
    count = 2
    qkv_out, proj_out, core_up_out, core_down_out, up_out, down_out = refs[-6:]
    closed, experts_above, attn_above = refs[2:5]
    shards = ([closed.at[k] for k in range(3)], [experts_above.at[0], experts_above.at[1], attn_above])

    def form(full, shard):
        mp, width = full.shape[1], full.shape[2]
        rows = width // mp
        qkv_out[0] = shard[2][:columns].astype(f32)
        proj_out[0] = shard[2][columns:].astype(f32)
        core_up_out[0] = shard[0][...].astype(f32)
        for place in range(mp):
            q = quarter_at(place, mp)
            up_out[0, 0, :, q * width : (q + 1) * width] = full[0, place].astype(f32)
        for chunk in range(mp):
            at = slice(chunk * width, (chunk + 1) * width)
            core_down_out[0, :, at] = shard[1][chunk * rows : (chunk + 1) * rows].astype(f32)
            block = [None] * mp
            for place in range(mp):
                block[quarter_at(place, mp)] = full[1, place, chunk * rows : (chunk + 1) * rows].astype(f32)
            down_out[0, 0, at, :] = jnp.concatenate(block, 0).T

    for layer in range(count):
        pl.when(pl.program_id(0) == layer)(functools.partial(form, refs[layer], shards[layer]))


def format_call(fulls, shards, columns):
    layers = len(fulls)
    _, mp, width, _ = fulls[0].shape
    hidden = mp * width
    shapes = [
        (layers, columns, width),
        (layers, width - columns, width),
        (layers, width, width),
        (layers, width // mp, hidden),
        (layers, 1, width, hidden),
        (layers, 1, hidden, width),
    ]
    return pl.pallas_call(
        functools.partial(format_kernel, columns),
        grid=(layers,),
        out_shape=[jax.ShapeDtypeStruct(shape, f32) for shape in shapes],
        in_specs=[whole_spec(a.shape) for a in (*fulls, *shards)],
        out_specs=[image_spec(shape, 1) for shape in shapes],
        compiler_params=pltpu.CompilerParams(vmem_limit_bytes=56 * MIB),
        name="format",
    )(*fulls, *shards)


def greet(dp, me, rows=()):
    barrier = pltpu.get_barrier_semaphore()
    for row in rows:
        pl.semaphore_signal(barrier, inc=1, device_id={"mp": row}, device_id_type=MESH)

    def signal(off, carry):
        pl.semaphore_signal(barrier, inc=1, device_id={"dp": lax.rem(me + off, dp)}, device_id_type=MESH)
        return carry

    lax.fori_loop(1, dp, signal, 0)
    pl.semaphore_wait(barrier, dp - 1 + len(rows))


def to_peer(source, target, send_sem, recv_sem, peer):
    return pltpu.make_async_remote_copy(
        src_ref=source,
        dst_ref=target,
        send_sem=send_sem,
        recv_sem=recv_sem,
        device_id={"dp": peer},
        device_id_type=MESH,
    )


def gelu_parts(h):
    root = np.float32(np.sqrt(2.0 / np.pi))
    square = h * h
    t = jnp.tanh(root * h * (1.0 + 0.044715 * square))
    half = 0.5 * (1.0 + t)
    slope = half + 0.5 * h * (1.0 - t * t) * root * (1.0 + 3 * 0.044715 * square)
    return h * half, slope


def expert_forward_kernel(dp, mp, layer, gather, *refs):
    refs = list(refs)
    buffer_ref, up_any, down_any, rup_any, rdown_any = refs[:5]
    refs = refs[5:]
    if gather:
        shards = [ref.at[layer + 1] for ref in refs[:4]]
        refs = refs[4:]
    recv_ref, returned_ref, up_eff, down_eff = refs[:4]
    refs = refs[4:]
    if gather:
        fulls = refs[:4]
        refs = refs[4:]
    part, core, up_ref, down_ref, rup_ref, rdown_ref, local = refs[:7]
    refs = refs[7:]
    moving = WeightGather(shards, fulls, refs[:7]) if gather else None
    send_one, recv_one, send_two, recv_two = refs[-4:]
    split = dp // EXPERTS
    me = lax.axis_index("dp")
    loads = [
        pltpu.make_async_copy(source, target, local.at[k])
        for k, (source, target) in enumerate(
            [
                (up_any, up_ref),
                (rup_any.at[layer, 0], rup_ref),
                (down_any, down_ref),
                (rdown_any.at[layer, 0], rdown_ref),
            ]
        )
    ]
    for load in loads:
        load.start()
    greet(dp, me, (moving.row.sibling, moving.row.across) if gather else ())

    def first(off):
        peer = lax.rem(me + off, dp)
        return to_peer(
            buffer_ref.at[lax.div(peer, split)], recv_ref.at[me], send_one.at[off], recv_one.at[off], peer
        )

    def second(off):
        source = lax.rem(me + dp - off, dp)
        return to_peer(part.at[source], returned_ref.at[me], send_two.at[off], recv_two.at[off], source)

    def start_first(off, carry):
        first(off).start()
        return carry

    lax.fori_loop(1, dp, start_first, 0)
    if gather:
        for k in range(4):
            moving.start(k)
    recv_ref[me] = buffer_ref[lax.div(me, split)]
    hidden = up_eff.shape[1]
    columns = up_ref.shape[-1]
    loads[0].wait()
    loads[1].wait()
    if split == 1 and columns % LANES == 0:
        for m in range(mp):
            at = slice(m * columns, (m + 1) * columns)
            up_eff[:, at] = (up_ref[m].astype(f32) + rup_ref[:, at].astype(f32)).astype(bf16)
    else:
        core[...] = rup_ref[...].astype(f32)
        begin = lax.rem(me, split) * hidden
        for m in range(mp):
            put = onehot(iota((columns, hidden), 0) + m * columns == iota((columns, hidden), 1) + begin)
            core[...] += nn(up_ref[m], put)
        up_eff[...] = core[...].astype(bf16)
    begin = pl.multiple_of(lax.rem(me, split) * hidden, LANES)
    loads[2].wait()
    loads[3].wait()
    core_part = down_ref[:, :, pl.ds(begin, hidden)].reshape(down_eff.shape[1], hidden)
    down_eff[...] = (core_part.astype(f32).T + rdown_ref[...].astype(f32)).astype(bf16)

    def work(source):
        hidden_pre = nn(recv_ref[source], up_eff[...])
        hidden_low = gelu_parts(hidden_pre)[0].astype(bf16)
        return nn(hidden_low, down_eff[...]).astype(bf16)

    returned_ref[me] = work(me)

    def step(off, carry):
        source = lax.rem(me + dp - off, dp)
        first(off).wait_recv()
        part[source] = work(source)
        second(off).start()
        return carry

    lax.fori_loop(1, dp, step, 0)
    if gather:
        for k in range(4):
            moving.forward(k)

    def finish(off, carry):
        first(off).wait_send()
        second(off).wait()
        return carry

    lax.fori_loop(1, dp, finish, 0)
    if gather:
        for k in range(4):
            moving.arrive(k)
            moving.sent(k)


def expert_backward_kernel(dp, mp, fast, reduce, *refs):
    refs = list(refs)
    buffer_ref, recv_ref, up_ref, down_ref = refs[:4]
    refs = refs[4:]
    if reduce:
        given_ref, attn_ref = refs[:2]
        refs = refs[2:]
    returned_ref = refs.pop(0)
    if fast:
        units_ref = refs.pop(0)
    else:
        up_term, down_term = refs[:2]
        refs = refs[2:]
    if reduce:
        full_ref, mine_ref = refs[:2]
        refs = refs[2:]
    grads, hidden_low, slope, pre, part = refs[:5]
    refs = refs[5:]
    if fast:
        up_term, down_term = refs[:2]
        refs = refs[2:]
    row = Row() if reduce else None
    if reduce:
        core_in, y_out, y_in = refs[:3]
        sums = RowSum(row, [attn_ref], core_in, y_out, y_in, [mine_ref], refs[3:7])
        gather = RowGather(
            row, [given_ref.at[k] for k in range(2)], [full_ref.at[k] for k in range(2)], row.place, row.place_across,
            refs[7:13],
        )
        refs = refs[13:]
    send_one, recv_one, send_two, recv_two = refs
    split = dp // EXPERTS
    me = lax.axis_index("dp")
    greet(dp, me, (row.sibling, row.across) if reduce else ())

    def first(off):
        peer = lax.rem(me + off, dp)
        return to_peer(buffer_ref.at[lax.div(peer, split)], grads.at[me], send_one.at[off], recv_one.at[off], peer)

    def second(off):
        source = lax.rem(me + dp - off, dp)
        return to_peer(part.at[source], returned_ref.at[me], send_two.at[off], recv_two.at[off], source)

    def start_first(off, carry):
        first(off).start()
        return carry

    lax.fori_loop(1, dp, start_first, 0)
    if reduce:
        sums.start(0)
        for k in range(2):
            gather.start(k)
    grads[me] = buffer_ref[lax.div(me, split)]

    def again(source, carry):
        value, rate = gelu_parts(nn(recv_ref[source], up_ref[...]))
        hidden_low[source] = value.astype(bf16)
        slope[source] = rate
        return carry

    lax.fori_loop(0, dp, again, 0)
    if reduce:
        sums.middle(0)
        for k in range(2):
            full_ref[k, row.place] = given_ref[k]

    def work(source):
        hidden_grad = nt(grads[source], down_ref[...])
        pre_grad = (slope[source] * hidden_grad).astype(bf16)
        pre[source] = pre_grad
        return nt(pre_grad, up_ref[...]).astype(bf16)

    returned_ref[me] = work(me)

    def step(off, carry):
        source = lax.rem(me + dp - off, dp)
        first(off).wait_recv()
        part[source] = work(source)
        second(off).start()
        return carry

    lax.fori_loop(1, dp, step, 0)
    if reduce:
        for k in range(2):
            gather.forward(k)
        sums.end(0)
    up_term[...] = jnp.zeros(up_term.shape, f32)
    down_term[...] = jnp.zeros(down_term.shape, f32)

    def terms(block, carry):
        up_term[...] += tn(recv_ref[block], pre[block])
        down_term[...] += tn(grads[block], hidden_low[block])
        return carry

    lax.fori_loop(0, dp, terms, 0)
    if fast:
        width = up_term.shape[0]
        height = width // mp
        for place in range(mp):
            q = quarter_at(place, mp)
            units_ref[0, place] = up_term[:, q * width : (q + 1) * width].astype(bf16)
            for chunk in range(mp):
                block = down_term[q * height : (q + 1) * height, chunk * width : (chunk + 1) * width]
                units_ref[1, place, chunk * height : (chunk + 1) * height] = block.astype(bf16)

    def finish(off, carry):
        first(off).wait_send()
        second(off).wait()
        return carry

    lax.fori_loop(1, dp, finish, 0)
    if reduce:
        sums.finish(0)
        for k in range(2):
            gather.arrive(k)
            gather.sent(k)


def expert_call(kernel, arrays, outs, scratch, dp, collective_id, name, flops, anys=(), any_outs=()):
    sems = [pltpu.SemaphoreType.DMA((dp,))] * 4
    vmem, anywhere = pl.BlockSpec(memory_space=pltpu.VMEM), pl.BlockSpec(memory_space=pl.ANY)
    return pl.pallas_call(
        kernel,
        out_shape=[jax.ShapeDtypeStruct(shape, dtype) for shape, dtype in (*outs, *any_outs)],
        in_specs=[vmem] * len(arrays) + [anywhere] * len(anys),
        out_specs=[vmem] * len(outs) + [anywhere] * len(any_outs),
        scratch_shapes=scratch + sems,
        compiler_params=pltpu.CompilerParams(
            vmem_limit_bytes=56 * MIB, collective_id=collective_id, has_side_effects=True
        ),
        cost_estimate=pl.CostEstimate(flops=flops, bytes_accessed=20 * MIB, transcendentals=0),
        name=name,
    )(*arrays, *anys)


def by_windows(grid):
    images, kinds = grid.shape[:2]
    blocks = GRID // WINDOW
    grid = grid.reshape(images, kinds, blocks, WINDOW, blocks, WINDOW).transpose(0, 1, 2, 4, 3, 5)
    grid = grid.reshape(images, kinds, blocks * blocks, WINPOS)
    grid = jnp.pad(grid, ((0, 0), (0, 0), (0, 0), (0, WPAD - WINPOS)), constant_values=-1)
    return grid.reshape(images, kinds, IMGROWS)


def per_device(
    patches,
    qkv_weight,
    proj_weight,
    core_up,
    core_down,
    residual_up,
    residual_down,
    position_bias,
    router_weight,
    norm_gain,
    norm_bias,
    cotangent,
    image_valid,
    expert_index,
    slot_index,
    region_id,
):
    dp, mp = lax.axis_size("dp"), lax.axis_size("mp")
    images, _, width = patches.shape
    split = dp // EXPERTS
    hidden = residual_up.shape[-1]
    hidden_full = core_up.shape[-1] * mp
    row_index = lax.axis_index("mp")

    fast = split == 1 and dp == 8 and mp == 4 and hidden == mp * width
    qkv_rows, proj_rows, down_rows = (a.transpose(0, 2, 1) for a in (qkv_weight, proj_weight, core_down))
    shards = (qkv_rows, proj_rows, core_up, down_rows)
    gathered = [[None] * len(shards)] * LAYERS
    if not fast:
        gathered = [[lax.all_gather(a[l], "mp", axis=0, tiled=False) for a in shards] for l in range(LAYERS)]

    position = jnp.where(slot_index >= 0, expert_index * SLOTS + slot_index, -1)
    row_form = by_windows(jnp.stack([position.reshape(images, GRID, GRID), region_id], 1))
    col_form = row_form.transpose(0, 2, 1)
    enter = jnp.asarray(enter_table(), bf16)
    leave = jnp.asarray(enter_table().T, bf16)
    moves = [jnp.asarray(move_table(l % 2 == 1), bf16) for l in range(LAYERS)]
    backs = [jnp.asarray(move_table(l % 2 == 1).T, bf16) for l in range(LAYERS)]
    table_rows = position_bias.transpose(0, 2, 1).reshape(LAYERS * HEADS, OFFSETS)
    table_rows = jnp.pad(table_rows, ((0, 0), (0, TABLE - OFFSETS)))
    entry_row, entry_col = jnp.asarray(cell_entries()[None, :]), jnp.asarray(cell_entries()[:, None])
    routers = jnp.pad(router_weight.transpose(0, 2, 1), ((0, 0), (0, LANES - EXPERTS), (0, 0)))

    token = (images, IMGROWS, width)
    buffer_shape = (ROWS, width)
    block_rows = (dp, SLOTS, width)
    pieces = (split, ROWS, width)

    def by_piece(returned):
        return returned.reshape(EXPERTS, split, SLOTS, width).transpose(1, 0, 2, 3).reshape(pieces)

    records = []
    before = None
    for l in range(LAYERS):
        first = l == 0
        gather = fast and first
        if first:
            arrays = [("image", patches), ("whole", enter)]
        else:
            arrays = [("image", before[0]), ("image", before[1]), ("whole", before[2])]
        arrays += [
            ("smem", image_valid),
            ("image", col_form),
            ("image", row_form),
            ("any", qkv_rows) if gather else ("whole", gathered[l][0]),
            ("any", proj_rows) if gather else ("whole", gathered[l][1]),
            ("whole", table_rows) if first else (l, biases),
            ("whole", moves[l]),
            ("whole", backs[l]),
            (l, norm_gain),
            (l, norm_bias),
            (l, routers),
        ]
        if first:
            arrays.append(("whole", entry_row))
        if gather:
            arrays += [("any", core_up), ("any", down_rows)]
        outs = [("image", token, f32)]
        if first:
            outs.append(("whole", (LAYERS, HEADS, WPAD, LANES), f32))
        else:
            outs.append(("image", token, f32))
        outs += [
            ("image", token, f32),
            ("image", token, bf16),
            ("image", (images, IMGROWS, 1), f32),
            ("whole", buffer_shape, bf16),
            ("image", token, bf16),
            ("image", (images, 2 * width, IMGROWS), bf16),
            ("image", token, bf16),
            ("image", (images, PAIRS * HEADS, WPAD, LANES), bf16),
            ("image", (images, width, IMGROWS), bf16),
            ("whole", (width, width), bf16),
        ]
        scratch = [pltpu.VMEM(buffer_shape, f32)]
        gathered_shapes = [(mp, *a.shape[1:]) for a in shards]
        if gather:
            outs.append(("whole", (3 * width, width), bf16))
            outs += [("any", shape, bf16) for shape in gathered_shapes[2:]]
            scratch += [pltpu.VMEM(shape, bf16) for shape in gathered_shapes[:2]] + WeightGather.scratch(4)
        results = list(
            image_call(
                functools.partial(attention_forward_kernel, first, l % 2 == 1, mp, gather),
                images, arrays, outs, scratch, f"attend_{l}", 3 * LAYERS + 1 if gather else None,
            )
        )
        if gather:
            gathered[l] = [results[-3], None] + results[-2:]
            results = results[:-3]
        carried = results.pop(0)
        if first:
            biases = results.pop(0)
        else:
            records[-1]["expert_out"] = results.pop(0)
        middle, second_low, gate, buffer = results[:4]
        gather = fast and l < LAYERS - 1
        received, returned, up_eff, down_eff, *more = expert_call(
            functools.partial(expert_forward_kernel, dp, mp, l, gather),
            [buffer.reshape(EXPERTS, SLOTS, width)],
            [
                (block_rows, bf16),
                (block_rows, bf16),
                ((width, hidden), bf16),
                ((hidden, width), bf16),
            ],
            [
                pltpu.VMEM(block_rows, bf16),
                pltpu.VMEM((8, LANES) if fast else (width, hidden), f32),
                pltpu.VMEM(gathered_shapes[2], bf16),
                pltpu.VMEM(gathered_shapes[3], bf16),
                pltpu.VMEM((width, hidden), bf16),
                pltpu.VMEM((hidden, width), bf16),
                pltpu.SemaphoreType.DMA((4,)),
            ]
            + (WeightGather.scratch(4) if gather else []),
            dp, l, f"experts_{l}", 4 * dp * SLOTS * width * hidden,
            [gathered[l][2], gathered[l][3], residual_up, residual_down, *(shards if gather else ())],
            [(shape, bf16) for shape in gathered_shapes] if gather else (),
        )
        if gather:
            gathered[l + 1] = more
        returned = by_piece(returned)
        before = (middle, gate, returned)
        records.append(
            dict(
                carried=carried, middle=middle, second_low=second_low, gate=gate, saved=results[4:], received=received,
                up_eff=up_eff, down_eff=down_eff,
            )
        )

    top = records[-1]
    block_output, grad, logit_grad, router_part, buffer = image_call(
        turn_kernel,
        images,
        [
            ("image", before[0]),
            ("image", before[1]),
            ("whole", before[2]),
            ("image", cotangent),
            ("whole", enter),
            ("whole", leave),
            ("image", col_form),
            ("image", row_form),
            ("image", top["second_low"]),
            (LAYERS - 1, routers),
        ],
        [
            ("image", patches.shape, bf16),
            ("image", token, f32),
            ("image", (images, IMGROWS, LANES), f32),
            ("whole", (LANES, width), f32),
            ("whole", buffer_shape, bf16),
        ],
        [pltpu.VMEM(buffer_shape, f32)],
        "turn",
    )
    router_parts, tables, smalls = [None] * LAYERS, [None] * LAYERS, [None] * LAYERS
    residual_sums, shard_sums = [None] * LAYERS, [None] * LAYERS
    router_parts[LAYERS - 1] = router_part
    units, attn_units, mines = [None] * LAYERS, [None] * LAYERS, [None] * LAYERS
    for l in reversed(range(LAYERS)):
        rec = records[l]
        last = l == 0
        reduce = fast and l < LAYERS - 1
        arrays = [buffer.reshape(EXPERTS, SLOTS, width), rec["received"], rec["up_eff"], rec["down_eff"]]
        outs = [(block_rows, bf16)]
        scratch = [
            pltpu.VMEM(block_rows, bf16),
            pltpu.VMEM((dp, SLOTS, hidden), bf16),
            pltpu.VMEM((dp, SLOTS, hidden), f32),
            pltpu.VMEM((dp, SLOTS, hidden), bf16),
            pltpu.VMEM(block_rows, bf16),
        ]
        if fast:
            outs.append(((2, mp, width, width), bf16))
            scratch += [pltpu.VMEM((width, hidden), f32)] * 2
        else:
            outs += [((width, hidden), f32)] * 2
        if reduce:
            arrays += [mines[l + 1], attn_units[l + 1]]
            outs += [((2, mp, width, width), bf16), ((width, width), bf16)]
            scratch += RowSum.scratch(1, width) + RowGather.scratch(2)
        results = list(
            expert_call(
                functools.partial(expert_backward_kernel, dp, mp, fast, reduce), arrays, outs, scratch, dp, LAYERS + l,
                f"experts_back_{l}", 10 * dp * SLOTS * width * hidden,
            )
        )
        returned_grad = results.pop(0)
        if fast:
            units[l] = results.pop(0)
        else:
            residual_sums[l] = lax.psum(tuple(t.astype(bf16) for t in results[:2]), "mp")
        if reduce:
            full_above, mine_above = results
            shard_above = lax.psum((mines[l + 1], mine_above), "dp")
        window_in, qk, v, probs, att, proj_full = rec["saved"]
        qkv_full = gathered[l][0].reshape(3 * width, width)
        arrays = [
            ("smem", image_valid),
            ("image", grad),
            ("whole", by_piece(returned_grad)),
            ("image", logit_grad),
            ("image", rec["middle"]),
            ("image", rec["carried"]),
            (l, routers),
            ("image", col_form),
            ("whole", moves[l]),
            ("whole", backs[l]),
            (l, norm_gain),
            ("whole", proj_full),
            ("whole", qkv_full),
            ("image", window_in),
            ("image", qk),
            ("image", v),
            ("image", probs),
            ("image", att),
        ]
        outs = [("image", patches.shape if last else token, f32)]
        scratch = [pltpu.VMEM((3 * width, (2 - images % 2) * IMGROWS), bf16)]
        closes = fast and last
        table_shape, small_shape = (HEADS, WPAD, LANES), (8, width)
        if fast:
            arrays.append(("whole", units[l]))
            scratch += [pltpu.VMEM((3 * width, width), f32), pltpu.VMEM((width, width), f32)]
        if closes:
            outs += [
                ("whole", (2, mp, width, width), bf16),
                ("whole", (3, width, width), bf16),
                ("whole", (Closing.lines, width), f32),
            ]
        else:
            if fast:
                outs += [("whole", (mp, width, width), bf16), ("whole", (2, width, width), bf16)]
            else:
                outs += [("whole", (3 * width, width), f32), ("whole", (width, width), f32)]
            outs += [("whole", table_shape, f32), ("whole", small_shape, f32)]
        if last:
            arrays.append(("whole", leave))
            if fast:
                arrays += [
                    ("whole", a) for a in (tables[1], smalls[1], router_parts[1], router_parts[0], entry_col)
                ]
        else:
            below = records[l - 1]
            arrays += [
                ("image", row_form),
                ("image", below["expert_out"]),
                ("image", below["second_low"]),
                (l - 1, routers),
            ]
            outs += [
                ("image", (images, IMGROWS, LANES), f32),
                ("whole", (LANES, width), f32),
                ("whole", buffer_shape, bf16),
            ]
            scratch.append(pltpu.VMEM(buffer_shape, f32))
        if closes:
            scratch += [
                pltpu.VMEM(table_shape, f32),
                pltpu.VMEM(small_shape, f32),
                pltpu.VMEM((mp, width, width), bf16),
                pltpu.VMEM((Closing.lines, width), f32),
                pltpu.VMEM((2, mp, width, width), bf16),
                pltpu.VMEM((3, width, width), bf16),
                pltpu.VMEM((Closing.lines, width), f32),
            ] + Closing.scratch(dp, width)
        elif fast:
            scratch += RowSum.scratch(2, width)
        results = list(
            image_call(
                functools.partial(attention_backward_kernel, last, dp, mp, fast),
                images, arrays, outs, scratch, f"attend_back_{l}", 2 * LAYERS + 1 + l if fast else None,
            )
        )
        grad = results.pop(0)
        if closes:
            full, closed, lines = results
            continue
        if fast:
            attn_units[l], mines[l] = results[:2]
        else:
            qkv_part, proj_part = results[:2]
        tables[l], smalls[l] = results[2:4]
        if not last:
            logit_grad, router_parts[l - 1], buffer = results[4:]
        if fast:
            continue
        attn = (
            lax.psum_scatter(qkv_part.astype(bf16), "mp", scatter_dimension=0, tiled=True),
            lax.psum_scatter(proj_part.T.astype(bf16), "mp", scatter_dimension=0, tiled=True),
        )
        up_sum, down_sum = residual_sums[l]
        if split > 1:
            begin = lax.axis_index("dp") % split * hidden
            empty = jnp.zeros((width, hidden_full), bf16)
            up_sum = lax.dynamic_update_slice_in_dim(empty, up_sum, begin, 1)
            down_sum = lax.dynamic_update_slice_in_dim(empty, down_sum, begin, 1)
        up_columns, down_columns = core_up.shape[-1], core_down.shape[-1]
        up_shard = lax.dynamic_slice_in_dim(up_sum, row_index * up_columns, up_columns, 1)
        down_shard = lax.dynamic_slice_in_dim(down_sum, row_index * down_columns, down_columns, 0)
        shard_sums[l] = lax.psum((attn[0], attn[1], up_shard, down_shard), "dp")

    if fast:
        *attn_grads, core_up_grad, core_down_grad, residual_up_grad, residual_down_grad = format_call(
            [full, full_above], [closed, *shard_above], qkv_weight.shape[-1]
        )
        attn_grads = [a.transpose(0, 2, 1) for a in attn_grads]
        core_grads = (core_up_grad, core_down_grad.transpose(0, 2, 1))
        at = LAYERS * HEADS
        table_sum = lines[:at, :OFFSETS]
        router_sum = lines[at : at + LAYERS * EXPERTS].reshape(LAYERS, EXPERTS, width)
        at += LAYERS * EXPERTS
        small_sum = lines[at : at + LAYERS * 8].reshape(LAYERS, 8, width)[:, :4]
    else:
        entry = cell_entries()[None, :] + np.array([key_base_of(key) for key in range(WPAD)])[:, None]
        entry = jnp.asarray(np.where(np.arange(WPAD)[:, None] < WINPOS, entry, -1).reshape(-1))
        entry_turned = (entry[:, None] == jnp.arange(OFFSETS)[None, :]).astype(f32)
        table_part = jnp.dot(
            jnp.stack(tables, 0).reshape(LAYERS * HEADS, WPAD * LANES), entry_turned, precision=highest
        )
        small_part = jnp.stack(smalls, 0)[:, :4]
        router_part = jnp.stack(router_parts, 0)[:, :EXPERTS]
        table_sum, small_sum, router_sum = lax.psum((table_part, small_part, router_part), ("dp", "mp"))

        def shard(k):
            return jnp.stack([shard_sums[l][k] for l in range(LAYERS)], 0).astype(f32)

        attn_grads = (shard(0).transpose(0, 2, 1), shard(1).transpose(0, 2, 1))
        core_grads = (shard(2), shard(3).transpose(0, 2, 1))
        residual_up_grad, residual_down_grad = (
            jnp.stack([residual_sums[l][k] for l in range(LAYERS)], 0).astype(f32) for k in range(2)
        )
        residual_up_grad = residual_up_grad[:, None]
        residual_down_grad = residual_down_grad.transpose(0, 2, 1)[:, None]

    return (
        block_output,
        grad,
        attn_grads[0],
        attn_grads[1],
        core_grads[0],
        core_grads[1],
        residual_up_grad,
        residual_down_grad,
        table_sum.reshape(LAYERS, HEADS, OFFSETS).transpose(0, 2, 1),
        router_sum.transpose(0, 2, 1),
        small_sum[:, 0:2],
        small_sum[:, 2:4],
    )


def solution(mesh):
    placed = (
        P(("dp", "mp"), None, None),
        P(None, None, "mp"),
        P(None, None, "mp"),
        P(None, None, "mp"),
        P(None, None, "mp"),
        P(None, "dp", None, None),
        P(None, "dp", None, None),
        P(),
        P(),
        P(),
        P(),
        P(("dp", "mp"), None, None),
        P(("dp", "mp")),
        P(("dp", "mp"), None),
        P(("dp", "mp"), None),
        P(("dp", "mp"), None, None),
    )
    return jax.shard_map(
        per_device,
        mesh=mesh,
        in_specs=placed,
        out_specs=(
            P(("dp", "mp"), None, None),
            P(("dp", "mp"), None, None),
            P(None, None, "mp"),
            P(None, None, "mp"),
            P(None, None, "mp"),
            P(None, None, "mp"),
            P(None, "dp", None, None),
            P(None, "dp", None, None),
            P(),
            P(),
            P(),
            P(),
        ),
        check_vma=False,
    )
```

```python
import functools

import jax
import jax.numpy as jnp
import numpy as np
from jax import lax
from jax.experimental import pallas as pl
from jax.experimental.pallas import tpu as pltpu
from jax.sharding import PartitionSpec as P

HEADS = 12
HEAD_DIM = 32
EXPERTS = 8
WINDOW = 7
GRID = 14
SHIFT = 3
LAYERS = 2
WINPOS = 49
OFFSETS = 169
CAP = 122

WPAD = 64
IMGROWS = 256
PATCHES = 196
SLOTS = 128
ROWS = EXPERTS * SLOTS
LANES = 128
GROUP = 4
PAIRS = 2
TABLE = 256

bf16 = jnp.bfloat16
f32 = jnp.float32
highest = lax.Precision.HIGHEST
norm_epsilon = 1e-05
mask_fill = -100.0
head_scale = HEAD_DIM ** (-0.5)
MESH = pl.DeviceIdType.MESH
MIB = 1024 * 1024


def nn(a, b):
    return lax.dot_general(a, b, (((1,), (0,)), ((), ())), preferred_element_type=f32)


def nt(a, b):
    return lax.dot_general(a, b, (((1,), (1,)), ((), ())), preferred_element_type=f32)


def tn(a, b):
    return lax.dot_general(a, b, (((0,), (0,)), ((), ())), preferred_element_type=f32)


def iota(shape, dim):
    return lax.broadcasted_iota(jnp.int32, shape, dim)


def onehot(flags):
    return jnp.where(flags, 1.0, 0.0).astype(bf16)


def natural_of_row(shifted):
    moved = SHIFT if shifted else 0
    blocks = GRID // WINDOW
    out = -np.ones(IMGROWS, np.int32)
    for window in range(blocks * blocks):
        for cell in range(WINPOS):
            row = (window // blocks * WINDOW + cell // WINDOW + moved) % GRID
            col = (window % blocks * WINDOW + cell % WINDOW + moved) % GRID
            out[window * WPAD + cell] = row * GRID + col
    return out


def key_base_of(key):
    return (2 * WINDOW) * (WINDOW - 1) - (key // WINDOW * (2 * WINDOW - 1) + key % WINDOW)


def enter_table():
    held = natural_of_row(False)
    return (held[:, None] == np.arange(PATCHES)[None, :]).astype(np.float32)


def move_table(shifted):
    first, second = natural_of_row(False), natural_of_row(shifted)
    same = (second[:, None] == first[None, :]) & (second[:, None] >= 0)
    return same.astype(np.float32)


def cell_entries():
    cell = np.arange(LANES) % WPAD
    return np.where(cell < WINPOS, cell // WINDOW * (2 * WINDOW - 1) + cell % WINDOW, -4 * TABLE).astype(np.int32)


def norm_parts(x):
    width = x.shape[-1]
    center = x - jnp.sum(x, -1, keepdims=True) * (1.0 / width)
    spread = jnp.sum(center * center, -1, keepdims=True) * (1.0 / width)
    rstd = lax.rsqrt(spread + norm_epsilon)
    return center * rstd, rstd


def norm_back(grad, gain, xhat, rstd):
    width = xhat.shape[-1]
    dxhat = grad * gain
    mean_one = jnp.sum(dxhat, -1, keepdims=True) * (1.0 / width)
    mean_two = jnp.sum(dxhat * xhat, -1, keepdims=True) * (1.0 / width)
    return rstd * (dxhat - mean_one - xhat * mean_two)


def split_two(x):
    high = x.astype(bf16)
    return high, (x - high.astype(f32)).astype(bf16)


def collect(pos_col, returned_ref):
    pick = onehot(pos_col == iota((pos_col.shape[0], ROWS), 1))
    out = nn(pick, returned_ref[0])
    for piece in range(1, returned_ref.shape[0]):
        out = out + nn(pick, returned_ref[piece])
    return out


def join(ref):
    return ref[...].reshape(ref.shape[0] * ref.shape[1], *ref.shape[2:])


def store(ref, rows):
    ref[...] = rows.reshape(ref.shape).astype(ref.dtype)


def per_image(function, count):
    return jnp.concatenate([function(i) for i in range(count)], 0)


def image_rows(i):
    return slice(i * IMGROWS, (i + 1) * IMGROWS)


def lay_positions(row_ref):
    return jnp.concatenate([row_ref[i, 0:1, :] for i in range(row_ref.shape[0])], 1)


def spread_rows(pos_row, rows_low):
    return nn(onehot(iota((ROWS, pos_row.shape[1]), 0) == pos_row), rows_low)


def route(second_low, router, pos_col):
    logits = nt(second_low, router)
    lane = iota(logits.shape, 1)
    logits = jnp.where(lane < EXPERTS, logits, -1e30)
    expo = jnp.exp(logits - jnp.max(logits, -1, keepdims=True))
    probs = expo / jnp.sum(expo, -1, keepdims=True)
    expert = jnp.where(pos_col >= 0, pos_col // SLOTS, -1)
    chosen = jnp.where(lane == expert, 1.0, 0.0)
    return probs, chosen, jnp.sum(probs * chosen, -1, keepdims=True)


def head_masks():
    rows = iota((LANES, LANES), 0) // HEAD_DIM
    return [onehot(rows == h) for h in range(GROUP)]


def lane_masks():
    lane = iota((WPAD, LANES), 1)
    return [onehot(lane < WPAD), onehot(lane >= WPAD)]


def key_base(key):
    return (2 * WINDOW) * (WINDOW - 1) - (key // WINDOW * (2 * WINDOW - 1) + lax.rem(key, WINDOW))


def form_bias(bias_ref, table_ref, entry_row):
    layers, heads = bias_ref.shape[:2]
    bias_ref[...] = jnp.where(iota(bias_ref.shape, 2) < WINPOS, 0.0, -1e30)
    table = table_ref[...]
    high = table.astype(bf16)
    mid, low = split_two(table - high.astype(f32))

    def step(key, carry):
        pick = onehot(iota((TABLE, LANES), 0) == entry_row + key_base(key))
        row = nn(high, pick) + nn(mid, pick) + nn(low, pick)
        for layer in range(layers):
            part = row[layer * heads : (layer + 1) * heads]
            bias_ref[layer, :, pl.ds(key, 1), :] = part.reshape(heads, 1, LANES)
        return carry

    lax.fori_loop(0, WINPOS, step, 0)


def table_grad(parts, entry_col):
    heads = parts[0].shape[0]

    def step(key, total):
        rows = jnp.concatenate([ref[:, pl.ds(key, 1), :].reshape(heads, LANES) for ref in parts], 0)
        pick = onehot(iota((LANES, TABLE), 1) == entry_col + key_base(key))
        high, low = split_two(rows)
        return total + nn(high, pick) + nn(low, pick)

    return lax.fori_loop(0, WINPOS, step, jnp.zeros((heads * len(parts), TABLE), f32))


def attention_forward_kernel(first, shifted, mp, gather, *refs):
    refs = list(refs)
    if first:
        patches_ref, enter_ref = refs[:2]
        refs = refs[2:]
    else:
        prev_ref, prev_gate_ref, returned_ref = refs[:3]
        refs = refs[3:]
    (
        valid_ref, col_ref, row_ref, qkv_ref, proj_ref, bias_ref, move_ref, back_ref, gain_ref, nbias_ref, router_ref,
    ) = refs[:11]
    gain_ref, nbias_ref, router_ref = (ref.at[0] for ref in (gain_ref, nbias_ref, router_ref))
    refs = refs[11:]
    if first:
        table_ref, entry_ref = bias_ref, refs.pop(0)
    if gather:
        core_up_ref, core_down_ref = refs[:2]
        refs = refs[2:]
    carried_ref = refs.pop(0)
    if first:
        biases_ref = refs.pop(0)
        bias_ref = biases_ref.at[0]
    else:
        expert_out_ref = refs.pop(0)
        bias_ref = bias_ref.at[0]
    middle_ref, second_ref, gate_ref, buffer_ref, window_ref, qk_ref, v_ref, probs_ref, att_ref, proj_full = refs[:10]
    refs = refs[10:]
    if gather:
        qkv_full = refs.pop(0)
        up_out, down_out = refs[:2]
        refs = refs[2:]
    total_ref = refs.pop(0)
    step = pl.program_id(0)
    final = pl.num_programs(0) - 1
    count, _, width = carried_ref.shape
    if gather:
        shards = [ref.at[0] for ref in (qkv_ref, proj_ref, core_up_ref, core_down_ref)]
        qkv_ref, proj_ref = refs[:2]
        moving = WeightGather(shards, [qkv_ref, proj_ref, up_out, down_out], refs[2:])

        @pl.when(step == 0)
        def _():
            pl.semaphore_wait(moving.row.greet(), 2)
            for k in (0, 1):
                moving.start(k)
            form_bias(biases_ref, table_ref, entry_ref[...])

        @pl.when(step == final)
        def _():
            for k in (2, 3):
                moving.forward(k)

    pos_col = join(col_ref)[:, 0:1]
    if first:
        x = per_image(lambda i: nn(enter_ref[...], patches_ref[i]), count)
    else:
        expert_out = collect(pos_col, returned_ref)
        store(expert_out_ref, expert_out)
        x = join(prev_ref) + join(prev_gate_ref) * expert_out
    store(carried_ref, x)
    xhat, _ = norm_parts(x)
    normed = (xhat * gain_ref[0:1, :] + nbias_ref[0:1, :]).astype(bf16)
    window_in = per_image(lambda i: nn(move_ref[...], normed[image_rows(i)]), count).astype(bf16)
    store(window_ref, window_in)

    @pl.when(step == 0)
    def _():
        if gather:
            for k in (0, 1):
                moving.forward(k)
            for k in (2, 3):
                moving.start(k)
            for k in (0, 1):
                moving.arrive(k)
            qkv_full[...] = join(qkv_ref)
        elif first:
            form_bias(biases_ref, table_ref, entry_ref[...])
        proj_full[...] = join(proj_ref).astype(f32).T.astype(bf16)
        total_ref[...] = jnp.zeros(total_ref.shape, f32)

    qkv = join(qkv_ref)
    turned = nt(qkv, window_in).astype(bf16)
    straight = nt(window_in, qkv[width:]).astype(bf16)
    for i in range(count):
        qk_ref[i] = turned[: 2 * width, image_rows(i)]
    store(v_ref, straight[:, width:])
    heads_rows = head_masks()
    halves = lane_masks()
    low_lane = iota((WPAD, LANES), 1) < WPAD
    if shifted:
        row_labels = [nt(row_ref[i].astype(f32).astype(bf16), move_ref[...]) for i in range(count)]
        col_labels = [nn(move_ref[...], col_ref[i].astype(f32).astype(bf16)) for i in range(count)]
    for pair in range(PAIRS * count):
        image, side = pair // PAIRS, pair % PAIRS
        across = slice(pair * LANES, (pair + 1) * LANES)
        within = slice(side * LANES, (side + 1) * LANES)
        if shifted:
            ahead = col_labels[image][side * LANES : side * LANES + WPAD, 1:2]
            behind = col_labels[image][side * LANES + WPAD : (side + 1) * LANES, 1:2]
            key_label = jnp.where(low_lane, ahead, behind)
            mask = jnp.where(key_label == row_labels[image][1:2, within], 0.0, mask_fill)
        for group in range(HEADS // GROUP):
            features = slice(group * LANES, (group + 1) * LANES)
            queries = turned[features, across]
            spread = jnp.concatenate([queries * heads_rows[h] for h in range(GROUP)], 1)
            raw = nn(straight[across, features], spread)
            for h in range(GROUP):
                head = group * GROUP + h
                part = raw[:, h * LANES : (h + 1) * LANES]
                scores = jnp.where(low_lane, part[:WPAD], part[WPAD:]) * head_scale + bias_ref[head]
                if shifted:
                    scores = scores + mask
                expo = jnp.exp(scores - jnp.max(scores, 0, keepdims=True))
                probs = (expo * (1.0 / jnp.sum(expo, 0, keepdims=True))).astype(bf16)
                probs_ref[image, side * HEADS + head] = probs
                both = jnp.concatenate([probs * halves[0], probs * halves[1]], 0)
                at = slice(head * HEAD_DIM, (head + 1) * HEAD_DIM)
                values = turned[2 * width + head * HEAD_DIM : 2 * width + (head + 1) * HEAD_DIM, across]
                att_ref[image, at, within] = nn(values, both).astype(bf16)
    attended = per_image(lambda i: nt(back_ref[...], att_ref[i]), count).astype(bf16)
    branch = nt(attended, join(proj_ref))
    middle = x + per_image(lambda i: valid_ref[step * count + i].astype(f32) * branch[image_rows(i)], count)
    store(middle_ref, middle)
    xhat, _ = norm_parts(middle)
    second_low = (xhat * gain_ref[1:2, :] + nbias_ref[1:2, :]).astype(bf16)
    store(second_ref, second_low)
    _, _, gate = route(second_low, router_ref[...], pos_col)
    store(gate_ref, gate)
    total_ref[...] += spread_rows(lay_positions(row_ref), second_low)

    @pl.when(step == final)
    def _():
        buffer_ref[...] = total_ref[...].astype(bf16)
        if gather:
            for k in (2, 3):
                moving.arrive(k)
            for k in range(4):
                moving.sent(k)


def image_spec(array_shape, count):
    rest = tuple(array_shape[1:])
    zeros = (0,) * len(rest)
    return pl.BlockSpec((count,) + rest, lambda i: (i,) + zeros)


def whole_spec(array_shape):
    zeros = (0,) * len(array_shape)
    return pl.BlockSpec(tuple(array_shape), lambda i: zeros)


def image_call(kernel, images, arrays, outs, scratch, name, collective_id=None):
    count = 2 - images % 2

    def spec(kind, shape):
        if isinstance(kind, int):
            rest = tuple(shape[1:])
            return pl.BlockSpec((1,) + rest, lambda i: (kind,) + (0,) * len(rest))
        if kind in ("smem", "any"):
            return pl.BlockSpec(memory_space=pltpu.SMEM if kind == "smem" else pl.ANY)
        return image_spec(shape, count) if kind == "image" else whole_spec(shape)

    return pl.pallas_call(
        kernel,
        grid=(images // count,),
        out_shape=[jax.ShapeDtypeStruct(shape, dtype) for _, shape, dtype in outs],
        in_specs=[spec(kind, array.shape) for kind, array in arrays],
        out_specs=[spec(kind, shape) for kind, shape, _ in outs],
        scratch_shapes=scratch,
        compiler_params=pltpu.CompilerParams(
            vmem_limit_bytes=56 * MIB,
            dimension_semantics=("arbitrary",),
            collective_id=collective_id,
            has_side_effects=collective_id is not None,
        ),
        name=name,
    )(*[array for _, array in arrays])


def send_part(g, expert_out, second_low, router, pos_col, pos_row, logit_ref, router_grad_ref, total_ref):
    probs, chosen, gate = route(second_low, router, pos_col)
    gate_grad = jnp.where(pos_col >= 0, jnp.sum(g * expert_out, -1, keepdims=True), 0.0)
    sent = (gate * g).astype(bf16)
    logit_grad = gate_grad * gate * (chosen - probs)
    store(logit_ref, logit_grad)
    high, low = split_two(logit_grad)
    router_grad_ref[...] += tn(high, second_low) + tn(low, second_low)
    total_ref[...] += spread_rows(pos_row, sent)


def turn_kernel(
    prev_ref, gate_ref, returned_ref, cotangent_ref, enter_ref, leave_ref, col_ref, row_ref, second_ref, router_ref,
    block_ref, grad_ref, logit_ref, router_grad_ref, buffer_ref, total_ref,
):
    step = pl.program_id(0)
    count = cotangent_ref.shape[0]

    @pl.when(step == 0)
    def _():
        total_ref[...] = jnp.zeros(total_ref.shape, f32)
        router_grad_ref[...] = jnp.zeros(router_grad_ref.shape, f32)

    pos_col = join(col_ref)[:, 0:1]
    expert_out = collect(pos_col, returned_ref)
    x = (join(prev_ref) + join(gate_ref) * expert_out).astype(bf16)
    for i in range(count):
        block_ref[i] = nn(leave_ref[...], x[image_rows(i)]).astype(bf16)
    g = per_image(lambda i: nn(enter_ref[...], cotangent_ref[i]), count)
    store(grad_ref, g)
    send_part(
        g, expert_out, join(second_ref), router_ref[0], pos_col, lay_positions(row_ref), logit_ref, router_grad_ref, total_ref
    )

    @pl.when(step == pl.num_programs(0) - 1)
    def _():
        buffer_ref[...] = total_ref[...].astype(bf16)


def attention_backward_kernel(last, dp, mp, fast, *refs):
    (
        valid_ref, grad_ref, returned_ref, logit_ref, middle_ref, carried_ref, router_ref, col_ref, move_ref, back_ref,
        gain_ref, proj_ref, qkv_ref, window_ref, qk_ref, v_ref, probs_ref, att_ref,
    ) = refs[:18]
    refs = refs[18:]
    refs = list(refs)
    if fast:
        units_ref = refs.pop(0)
    if last:
        leave_ref = refs.pop(0)
        if fast:
            table_above, small_above, router_above, router_here, entry_ref, halves_above, attn_above = refs[:7]
            refs = refs[7:]
    else:
        row_ref, expert_out_ref, second_ref, router_next_ref = refs[:4]
        refs = refs[4:]
    out_ref = refs.pop(0)
    closing = None
    if fast and last:
        results, refs = refs[:4], refs[4:]
    else:
        if fast:
            halves_ref = refs.pop(0)
            unit_ref, mine_ref = refs[:2]
        else:
            qkv_grad_ref, proj_grad_ref = refs[:2]
        table_ref, small_ref = refs[2:4]
        refs = refs[4:]
    if not last:
        logit_out_ref, router_grad_ref, buffer_ref = refs[:3]
        refs = refs[3:]
    turned = refs.pop(0)
    if fast:
        qkv_grad_ref, proj_grad_ref = refs[:2]
        refs = refs[2:]
    if not last:
        total_ref = refs.pop(0)
    step = pl.program_id(0)
    final = pl.num_programs(0) - 1
    count, _, width = carried_ref.shape
    if fast:
        row = Row()
        if last:
            table_ref, small_ref, unit_ref, lines_ref = refs[:4]
            landing, refs = refs[4:8], refs[8:]
            closing = Closing(row, dp, units_ref, unit_ref, lines_ref, halves_above, attn_above, landing, refs)
        else:
            sums = RowSum(row, blocks(units_ref), refs[0], refs[1], refs[2], blocks(mine_ref), refs[3:7])
            across_x = DeepSum(
                dp, blocks(mine_ref), blocks(refs[7]), blocks(halves_ref), [None] * 2, [None] * 2, refs[8:10] * 4
            )

        def take(k):
            if closing:
                closing.take(k)
            else:
                sums.end(k)
                across_x.over_x(k).start()

        @pl.when(step == 0)
        def _():
            if closing:
                closing.enter()
            else:
                barrier = row.greet()
                pl.semaphore_wait(barrier, 2 + across_x.greet(barrier, False))
                for k in range(2):
                    sums.start(k)

        pl.when(step == final)(functools.partial(take, 0))

    @pl.when(step == 0)
    def _():
        qkv_grad_ref[...] = jnp.zeros(qkv_grad_ref.shape, f32)
        proj_grad_ref[...] = jnp.zeros(proj_grad_ref.shape, f32)
        table_ref[...] = jnp.zeros(table_ref.shape, f32)
        small_ref[...] = jnp.zeros(small_ref.shape, f32)
        if not last:
            total_ref[...] = jnp.zeros(total_ref.shape, f32)
            router_grad_ref[...] = jnp.zeros(router_grad_ref.shape, f32)

    pos_col = join(col_ref)[:, 0:1]
    g = join(grad_ref)
    high, low = split_two(join(logit_ref))
    gain_ref, router = gain_ref.at[0], router_ref[0]
    normed_grad = collect(pos_col, returned_ref) + nn(high, router) + nn(low, router)
    xhat, rstd = norm_parts(join(middle_ref))
    small_ref[1:2, :] += jnp.sum(normed_grad * xhat, 0, keepdims=True)
    small_ref[3:4, :] += jnp.sum(normed_grad, 0, keepdims=True)
    middle_grad = g + norm_back(normed_grad, gain_ref[1:2, :], xhat, rstd)

    def branch_part(i):
        low_part = (valid_ref[step * count + i].astype(f32) * middle_grad[image_rows(i)]).astype(bf16)
        return nn(move_ref[...], low_part)

    branch_grad = per_image(branch_part, count).astype(bf16)
    for i in range(count):
        proj_grad_ref[...] += nn(att_ref[i], branch_grad[image_rows(i)])
    att_grad = nt(proj_ref[...], branch_grad).astype(bf16)
    if fast:

        @pl.when(step == 0)
        def _():
            if closing:
                closing.early()
            else:
                for k in range(2):
                    sums.middle(k)

        pl.when(step == final)(functools.partial(take, 1))

    heads_rows = head_masks()
    halves = lane_masks()
    low_lane = iota((WPAD, LANES), 1) < WPAD
    for pair in range(PAIRS * count):
        image, side = pair // PAIRS, pair % PAIRS
        across = slice(pair * LANES, (pair + 1) * LANES)
        within = slice(side * LANES, (side + 1) * LANES)
        for group in range(HEADS // GROUP):
            features = slice(group * LANES, (group + 1) * LANES)
            grads = att_grad[features, across]
            spread = jnp.concatenate([grads * heads_rows[h] for h in range(GROUP)], 1)
            raw = nn(v_ref[image, within, features], spread)
            for h in range(GROUP):
                head = group * GROUP + h
                at = slice(head * HEAD_DIM, (head + 1) * HEAD_DIM)
                below = slice(width + head * HEAD_DIM, width + (head + 1) * HEAD_DIM)
                lowest = slice(2 * width + head * HEAD_DIM, 2 * width + (head + 1) * HEAD_DIM)
                part = raw[:, h * LANES : (h + 1) * LANES]
                probs_grad = jnp.where(low_lane, part[:WPAD], part[WPAD:])
                probs_low = probs_ref[image, side * HEADS + head]
                probs = probs_low.astype(f32)
                weighted = probs * probs_grad
                scores_grad = weighted - probs * jnp.sum(weighted, 0, keepdims=True)
                table_ref[head] += scores_grad
                scores_low = scores_grad.astype(bf16)
                both = jnp.concatenate([scores_low * halves[0], scores_low * halves[1]], 0)
                probs_both = jnp.concatenate([probs_low * halves[0], probs_low * halves[1]], 0)
                turned[at, across] = (nn(qk_ref[image, below, within], both) * head_scale).astype(bf16)
                turned[below, across] = (nt(qk_ref[image, at, within], both) * head_scale).astype(bf16)
                turned[lowest, across] = nt(att_grad[at, across], probs_both).astype(bf16)
    qkv_grad_ref[...] += nn(turned[...], join(window_ref))
    if fast:

        @pl.when(step == final)
        def _():
            columns, rows = 3 * width // mp, width // mp
            proj_turned = proj_grad_ref[...].T
            for place in range(mp):
                q = quarter_at(place, mp)
                unit_ref[place, :columns] = qkv_grad_ref[q * columns : (q + 1) * columns].astype(bf16)
                unit_ref[place, columns:] = proj_turned[q * rows : (q + 1) * rows].astype(bf16)
            if closing:
                closing.open()

    mixed_grad = per_image(lambda i: nt(back_ref[...], turned[:, image_rows(i)]), count).astype(bf16)
    first_grad = nn(mixed_grad, qkv_ref[...])
    xhat, rstd = norm_parts(join(carried_ref))
    small_ref[0:1, :] += jnp.sum(first_grad * xhat, 0, keepdims=True)
    small_ref[2:3, :] += jnp.sum(first_grad, 0, keepdims=True)
    out = middle_grad + norm_back(first_grad, gain_ref[0:1, :], xhat, rstd)
    if closing:

        @pl.when(step == final)
        def _():
            closing.attend()

    if last:
        top = out.astype(bf16)
        rest = out - top.astype(f32)
        mid, low = split_two(rest)
        leave = leave_ref[...]
        for i in range(count):
            at = image_rows(i)
            out_ref[i] = nn(leave, top[at]) + nn(leave, mid[at]) + nn(leave, low[at])
    else:
        store(out_ref, out)
        send_part(
            out, join(expert_out_ref), join(second_ref), router_next_ref[0], pos_col, lay_positions(row_ref), logit_out_ref,
            router_grad_ref, total_ref,
        )

    @pl.when(step == final)
    def _():
        if not last:
            buffer_ref[...] = total_ref[...].astype(bf16)
        if closing:
            heads = 2 * HEADS
            lines_ref[...] = jnp.zeros(lines_ref.shape, f32)
            lines_ref[:heads, :TABLE] = table_grad([table_ref, table_above], entry_ref[...])
            lines_ref[heads : heads + EXPERTS] = router_here[:EXPERTS]
            lines_ref[heads + EXPERTS : heads + 2 * EXPERTS] = router_above[:EXPERTS]
            lines_ref[heads + 2 * EXPERTS : heads + 2 * EXPERTS + 8] = small_ref[...]
            lines_ref[heads + 2 * EXPERTS + 8 : heads + 2 * EXPERTS + 16] = small_above[...]
            closing.finish()
            for out, landed in zip(results, landing):
                out[...] = landed[...]
        elif fast:
            for k in range(2):
                across_x.halve(k)
                across_x.over_x(k).wait_send()
                sums.finish(k)


def quarter_at(place, mp):
    return place % (mp // 2) * 2 + place // (mp // 2)


def add_up(*parts):
    total = parts[0].astype(f32)
    for part in parts[1:]:
        total = total + part.astype(f32)
    return total


def to_row(source, target, sems, k, row):
    return pltpu.make_async_remote_copy(
        src_ref=source,
        dst_ref=target,
        send_sem=sems[0].at[k],
        recv_sem=sems[1].at[k],
        device_id={"mp": row},
        device_id_type=MESH,
    )


class Row:
    def __init__(self):
        row = lax.axis_index("mp")
        self.row, self.core, self.y = row, lax.rem(row, 2), lax.div(row, 2)
        self.sibling, self.across = row + 1 - 2 * self.core, row + 2 - 4 * self.y
        self.place = self.core * 2 + self.y
        self.place_across = self.core * 2 + 1 - self.y

    def greet(self):
        barrier = pltpu.get_barrier_semaphore()
        for row in (self.sibling, self.across):
            pl.semaphore_signal(barrier, inc=1, device_id={"mp": row}, device_id_type=MESH)
        return barrier


class RowSum:
    semaphores = 4

    def __init__(self, row, units, core_in, y_out, y_in, mine, sems):
        self.row, self.units, self.mine = row, units, mine
        self.core_in, self.y_out, self.y_in = core_in, y_out, y_in
        self.sems = (sems[:2], sems[2:])

    def pair(self, k):
        theirs = self.units[k].at[pl.ds(2 * (1 - self.row.core), 2)]
        return to_row(theirs, self.core_in.at[k], self.sems[0], k, self.row.sibling)

    def cross(self, k):
        return to_row(self.y_out.at[k], self.y_in.at[k], self.sems[1], k, self.row.across)

    def start(self, k):
        self.pair(k).start()

    def middle(self, k):
        self.pair(k).wait_recv()
        other = 1 - self.row.y
        mixed = add_up(self.units[k][self.row.core * 2 + other], self.core_in[k, other])
        self.y_out[k] = mixed.astype(bf16)
        self.cross(k).start()

    def end(self, k):
        self.cross(k).wait_recv()
        self.mine[k][...] = add_up(
            self.units[k][self.row.place], self.core_in[k, self.row.y], self.y_in[k]
        ).astype(bf16)

    def finish(self, k):
        self.pair(k).wait_send()
        self.cross(k).wait_send()

    @classmethod
    def scratch(cls, count, width):
        return [
            pltpu.VMEM((count, 2, width, width), bf16),
            pltpu.VMEM((count, width, width), bf16),
            pltpu.VMEM((count, width, width), bf16),
        ] + [pltpu.SemaphoreType.DMA((count,))] * cls.semaphores


class RowGather:
    semaphores = 6

    def __init__(self, row, sources, fulls, slot, slot_across, sems):
        self.row, self.sources, self.fulls = row, sources, fulls
        self.slot, self.slot_across = slot, slot_across
        self.sems = (sems[:2], sems[2:4], sems[4:])

    def over(self, k):
        return to_row(self.sources[k], self.fulls[k].at[self.slot], self.sems[0], k, self.row.across)

    def near(self, k):
        return to_row(self.sources[k], self.fulls[k].at[self.slot], self.sems[1], k, self.row.sibling)

    def onward(self, k):
        block = self.fulls[k].at[self.slot_across]
        return to_row(block, block, self.sems[2], k, self.row.sibling)

    def start(self, k):
        self.over(k).start()
        self.near(k).start()

    def forward(self, k):
        self.over(k).wait_recv()
        self.onward(k).start()

    def arrive(self, k):
        self.near(k).wait_recv()
        self.onward(k).wait_recv()

    def sent(self, k):
        self.over(k).wait_send()
        self.near(k).wait_send()
        self.onward(k).wait_send()

    @classmethod
    def scratch(cls, count):
        return [pltpu.SemaphoreType.DMA((count,))] * cls.semaphores


class WeightGather(RowGather):
    def __init__(self, shards, fulls, sems):
        row = Row()
        super().__init__(row, shards, fulls, row.row, row.across, sems[:6])
        self.own_sem = sems[6]

    def own(self, k):
        return pltpu.make_async_copy(self.sources[k], self.fulls[k].at[self.slot], self.own_sem.at[k])

    def start(self, k):
        super().start(k)
        self.own(k).start()

    def arrive(self, k):
        super().arrive(k)
        self.own(k).wait()

    @classmethod
    def scratch(cls, count):
        return super().scratch(count) + [pltpu.SemaphoreType.DMA((count,))]


class DeepSum:
    def __init__(self, dp, total, arrived, halves, slots, result, sems):
        self.total, self.arrived, self.halves, self.slots, self.result = total, arrived, halves, slots, result
        self.x_sems, self.z_sems, self.z_back, self.x_back = (sems[2 * k : 2 * k + 2] for k in range(4))
        me = lax.axis_index("dp")
        self.x, self.z, self.deep = lax.rem(me, 2), lax.div(me, 2), dp // 2
        self.partner = me + 1 - 2 * self.x

    def greet(self, barrier, whole=True):
        pl.semaphore_signal(barrier, inc=1, device_id={"dp": self.partner}, device_id_type=MESH)
        if not whole:
            return 1
        for off in range(1, self.deep):
            peer = lax.rem(self.z + off, self.deep) * 2 + self.x
            pl.semaphore_signal(barrier, inc=1, device_id={"dp": peer}, device_id_type=MESH)
        return self.deep

    def cut(self, k):
        height = self.halves[k].shape[0]
        return height, height // self.deep

    def over_x(self, k):
        height, _ = self.cut(k)
        away = self.total[k].at[pl.ds(pl.multiple_of((1 - self.x) * height, height), height)]
        return to_peer(away, self.arrived[k], self.x_sems[0].at[k], self.x_sems[1].at[k], self.partner)

    def over_z(self, k, off):
        _, piece = self.cut(k)
        to = lax.rem(self.z + off, self.deep)
        part = self.halves[k].at[pl.ds(pl.multiple_of(to * piece, piece), piece)]
        sems = [sem.at[k, off] for sem in self.z_sems]
        return to_peer(part, self.slots[k].at[off], *sems, to * 2 + self.x)

    def own_piece(self, k):
        height, piece = self.cut(k)
        return self.result[k].at[pl.ds(pl.multiple_of(self.x * height + self.z * piece, piece), piece)]

    def own_half(self, k):
        height, _ = self.cut(k)
        return self.result[k].at[pl.ds(pl.multiple_of(self.x * height, height), height)]

    def back_z(self, k, off):
        to = lax.rem(self.z + off, self.deep)
        sems = [sem.at[k, off] for sem in self.z_back]
        return to_peer(self.own_piece(k), self.own_piece(k), *sems, to * 2 + self.x)

    def back_x(self, k):
        return to_peer(self.own_half(k), self.own_half(k), self.x_back[0].at[k], self.x_back[1].at[k], self.partner)

    def halve(self, k):
        self.over_x(k).wait_recv()
        height, _ = self.cut(k)
        keep = self.total[k][pl.ds(pl.multiple_of(self.x * height, height), height)]
        self.halves[k][...] = add_up(keep, self.arrived[k][...]).astype(self.halves[k].dtype)

    def deepen(self, k):
        for off in range(1, self.deep):
            self.over_z(k, off).start()

    def quarter(self, k):
        for off in range(1, self.deep):
            self.over_z(k, off).wait_recv()
        _, piece = self.cut(k)
        keep = self.halves[k][pl.ds(pl.multiple_of(self.z * piece, piece), piece)]
        total = add_up(keep, *[self.slots[k][off] for off in range(1, self.deep)])
        self.own_piece(k)[...] = total.astype(self.result[k].dtype)
        for off in range(1, self.deep):
            self.back_z(k, off).start()

    def widen(self, k):
        for off in range(1, self.deep):
            self.back_z(k, off).wait_recv()
        self.back_x(k).start()

    def finish(self, k, halved=True):
        if halved:
            self.over_x(k).wait_send()
        for off in range(1, self.deep):
            self.over_z(k, off).wait_send()
            self.back_z(k, off).wait_send()
        self.back_x(k).wait()

    @staticmethod
    def semaphores(dp, count):
        one, many = pltpu.SemaphoreType.DMA((count,)), pltpu.SemaphoreType.DMA((count, dp // 2))
        return [one, one, many, many, many, many, one, one]


def blocks(ref):
    return [ref.at[k] for k in range(ref.shape[0])]


class Closing:
    lines = 64

    def __init__(self, row, dp, units_ref, attn_ref, lines_ref, halves_above, attn_above, results, refs):
        self.row, self.lines_ref = row, lines_ref
        self.full, shard, small, above = results
        core_in, y_out, y_in = refs[:3]
        mine, x_in, half, z_in, self.s_core, self.s_one, self.s_y, self.s_mine, s_x, s_half, s_z = refs[7:18]
        x_above, half_above, z_above = refs[18:21]
        refs_sems, refs = refs[3:7], refs[21:]
        self.mine = mine
        self.sums = RowSum(row, blocks(units_ref) + [attn_ref], core_in, y_out, y_in, blocks(mine), refs_sems)
        self.gather = RowGather(
            row, [mine.at[k] for k in range(2)], blocks(self.full), row.place, row.place_across, refs[:6]
        )
        self.s_pair = to_row(lines_ref, self.s_core, refs[6:8], 0, row.sibling)
        self.s_cross = to_row(self.s_one, self.s_y, refs[8:10], 0, row.across)
        self.here = DeepSum(
            dp, blocks(mine) + [self.s_mine], blocks(x_in) + [s_x], blocks(half) + [s_half], blocks(z_in) + [s_z],
            blocks(shard) + [small], refs[10:18],
        )
        self.above = DeepSum(
            dp, [None, None, attn_above], [None, None, x_above], blocks(halves_above) + [half_above], blocks(z_above),
            blocks(above), refs[18:26],
        )

    def enter(self):
        barrier = self.row.greet()
        pl.semaphore_wait(barrier, 2 + self.here.greet(barrier))
        for k in range(2):
            self.sums.start(k)
        for k in range(2):
            self.above.deepen(k)
        self.above.over_x(2).start()

    def early(self):
        for k in range(2):
            self.sums.middle(k)
        self.above.halve(2)
        self.above.deepen(2)
        for k in range(2):
            self.above.quarter(k)

    def take(self, k):
        self.sums.end(k)
        self.here.over_x(k).start()
        if k == 0:
            for j in range(2):
                self.above.widen(j)
            self.above.quarter(2)
        else:
            self.above.widen(2)

    def open(self):
        self.sums.start(2)
        for k in range(2):
            self.here.halve(k)
            self.here.deepen(k)

    def attend(self):
        self.sums.middle(2)
        for k in range(2):
            self.gather.start(k)
            self.full[k, self.row.place] = self.mine[k]
        for k in range(2):
            self.here.quarter(k)

    def finish(self):
        here = self.here
        self.s_pair.start()
        self.sums.end(2)
        here.over_x(2).start()
        self.s_pair.wait_recv()
        self.s_one[...] = self.lines_ref[...] + self.s_core[...]
        self.s_cross.start()
        for k in range(2):
            here.widen(k)
        here.halve(2)
        here.deepen(2)
        self.s_cross.wait_recv()
        self.s_mine[...] = self.s_one[...] + self.s_y[...]
        here.over_x(3).start()
        here.quarter(2)
        here.halve(3)
        here.deepen(3)
        self.gather.forward(0)
        here.widen(2)
        here.quarter(3)
        self.gather.forward(1)
        here.widen(3)
        self.s_pair.wait_send()
        self.s_cross.wait_send()
        for k in range(3):
            self.sums.finish(k)
            self.above.finish(k, k == 2)
        for k in range(2):
            self.gather.arrive(k)
            self.gather.sent(k)
        for k in range(4):
            here.finish(k)

    @classmethod
    def scratch(cls, dp, width):
        deep = dp // 2
        lines = cls.lines
        flat, half_flat = pltpu.VMEM((lines, width), f32), pltpu.VMEM((lines // 2, width), f32)
        half, slots = (width // 2, width), (3, deep, width // dp, width)
        return (
            RowSum.scratch(3, width)
            + [
                pltpu.VMEM((3, width, width), bf16),
                pltpu.VMEM((3, *half), bf16),
                pltpu.VMEM((3, *half), bf16),
                pltpu.VMEM(slots, bf16),
                flat, flat, flat, flat, half_flat, half_flat,
                pltpu.VMEM((deep, lines // dp, width), f32),
                pltpu.VMEM(half, bf16),
                pltpu.VMEM(half, bf16),
                pltpu.VMEM(slots, bf16),
            ]
            + RowGather.scratch(2)
            + [pltpu.SemaphoreType.DMA((1,))] * 4
            + DeepSum.semaphores(dp, 4)
            + DeepSum.semaphores(dp, 3)
        )


def format_kernel(columns, *refs):
    layers = len(refs[:-6]) // 3
    qkv_out, proj_out, core_up_out, core_down_out, up_out, down_out = refs[-6:]

    def form(ups, downs, shard):
        mp, rows = downs.shape[1], downs.shape[2]
        up_out[0, 0] = ups[0, 0].astype(f32)
        down_out[0, 0] = jnp.concatenate(
            [downs[0, q % 2 * (mp // 2) + q // 2].astype(f32) for q in range(mp)], 0
        ).T
        core_down_out[0] = shard[1, pl.ds(pl.multiple_of(pl.program_id(1) * rows, rows), rows)].astype(f32)

        @pl.when(pl.program_id(1) == 0)
        def _():
            qkv_out[0] = shard[2, :columns].astype(f32)
            proj_out[0] = shard[2, columns:].astype(f32)
            core_up_out[0] = shard[0].astype(f32)

    for layer in range(layers):
        pl.when(pl.program_id(0) == layer)(functools.partial(form, *refs[3 * layer : 3 * layer + 3]))


def format_call(fulls, shards, columns):
    layers = len(fulls)
    _, mp, width, _ = fulls[0].shape
    hidden, rows = mp * width, width // mp
    outs = [
        ((layers, columns, width), None),
        ((layers, width - columns, width), None),
        ((layers, width, width), None),
        ((layers, rows, hidden), pl.BlockSpec((1, rows, width), lambda i, j: (i, 0, j))),
        ((layers, 1, width, hidden), pl.BlockSpec((1, 1, width, width), lambda i, j: (i, 0, 0, j))),
        ((layers, 1, hidden, width), pl.BlockSpec((1, 1, width, width), lambda i, j: (i, 0, j, 0))),
    ]

    def by_layer(shape):
        return pl.BlockSpec((1, *shape[1:]), lambda i, j: (i, 0, 0))

    def chunk(layer, i, j):
        return jnp.where(i == layer, j, jnp.where(i < layer, 0, mp - 1))

    def place(q):
        return lax.rem(q, 2) * (mp // 2) + lax.div(q, 2)

    specs, arrays = [], []
    for layer in range(layers):
        specs += [
            pl.BlockSpec((1, 1, width, width), lambda i, j, at=layer: (0, place(chunk(at, i, j)), 0, 0)),
            pl.BlockSpec((1, mp, rows, width), lambda i, j, at=layer: (1, 0, chunk(at, i, j), 0)),
            pl.BlockSpec((3, width, width), lambda i, j: (0, 0, 0)),
        ]
        arrays += [fulls[layer], fulls[layer], shards[layer]]
    return pl.pallas_call(
        functools.partial(format_kernel, columns),
        grid=(layers, mp),
        out_shape=[jax.ShapeDtypeStruct(shape, f32) for shape, _ in outs],
        in_specs=specs,
        out_specs=[spec or by_layer(shape) for shape, spec in outs],
        compiler_params=pltpu.CompilerParams(vmem_limit_bytes=40 * MIB),
        name="format",
    )(*arrays)


def greet(dp, me, rows=()):
    barrier = pltpu.get_barrier_semaphore()
    for row in rows:
        pl.semaphore_signal(barrier, inc=1, device_id={"mp": row}, device_id_type=MESH)

    def signal(off, carry):
        pl.semaphore_signal(barrier, inc=1, device_id={"dp": lax.rem(me + off, dp)}, device_id_type=MESH)
        return carry

    lax.fori_loop(1, dp, signal, 0)
    pl.semaphore_wait(barrier, dp - 1 + len(rows))


def to_peer(source, target, send_sem, recv_sem, peer):
    return pltpu.make_async_remote_copy(
        src_ref=source,
        dst_ref=target,
        send_sem=send_sem,
        recv_sem=recv_sem,
        device_id={"dp": peer},
        device_id_type=MESH,
    )


def gelu_parts(h):
    root = np.float32(np.sqrt(2.0 / np.pi))
    square = h * h
    t = jnp.tanh(root * h * (1.0 + 0.044715 * square))
    half = 0.5 * (1.0 + t)
    slope = half + 0.5 * h * (1.0 - t * t) * root * (1.0 + 3 * 0.044715 * square)
    return h * half, slope


def expert_forward_kernel(dp, mp, layer, gather, *refs):
    refs = list(refs)
    buffer_ref, up_any, down_any, rup_any, rdown_any = refs[:5]
    refs = refs[5:]
    if gather:
        shards = [ref.at[layer + 1] for ref in refs[:4]]
        refs = refs[4:]
    recv_ref, returned_ref, up_eff, down_eff = refs[:4]
    refs = refs[4:]
    if gather:
        fulls = refs[:4]
        refs = refs[4:]
    part, core, up_ref, down_ref, rup_ref, rdown_ref, local = refs[:7]
    refs = refs[7:]
    moving = WeightGather(shards, fulls, refs[:7]) if gather else None
    send_one, recv_one, send_two, recv_two = refs[-4:]
    split = dp // EXPERTS
    me = lax.axis_index("dp")
    loads = [
        pltpu.make_async_copy(source, target, local.at[k])
        for k, (source, target) in enumerate(
            [
                (up_any, up_ref),
                (rup_any.at[layer, 0], rup_ref),
                (down_any, down_ref),
                (rdown_any.at[layer, 0], rdown_ref),
            ]
        )
    ]
    for load in loads:
        load.start()
    greet(dp, me, (moving.row.sibling, moving.row.across) if gather else ())

    def first(off):
        peer = lax.rem(me + off, dp)
        return to_peer(
            buffer_ref.at[lax.div(peer, split)], recv_ref.at[me], send_one.at[off], recv_one.at[off], peer
        )

    def second(off):
        source = lax.rem(me + dp - off, dp)
        return to_peer(part.at[source], returned_ref.at[me], send_two.at[off], recv_two.at[off], source)

    def start_first(off, carry):
        first(off).start()
        return carry

    lax.fori_loop(1, dp, start_first, 0)
    if gather:
        for k in range(4):
            moving.start(k)
    recv_ref[me] = buffer_ref[lax.div(me, split)]
    hidden = up_eff.shape[1]
    columns = up_ref.shape[-1]
    loads[0].wait()
    loads[1].wait()
    if split == 1 and columns % LANES == 0:
        for m in range(mp):
            at = slice(m * columns, (m + 1) * columns)
            up_eff[:, at] = (up_ref[m].astype(f32) + rup_ref[:, at].astype(f32)).astype(bf16)
    else:
        core[...] = rup_ref[...].astype(f32)
        begin = lax.rem(me, split) * hidden
        for m in range(mp):
            put = onehot(iota((columns, hidden), 0) + m * columns == iota((columns, hidden), 1) + begin)
            core[...] += nn(up_ref[m], put)
        up_eff[...] = core[...].astype(bf16)
    begin = pl.multiple_of(lax.rem(me, split) * hidden, LANES)
    loads[2].wait()
    loads[3].wait()
    core_part = down_ref[:, :, pl.ds(begin, hidden)].reshape(down_eff.shape[1], hidden)
    down_eff[...] = (core_part.astype(f32).T + rdown_ref[...].astype(f32)).astype(bf16)

    def work(source):
        hidden_pre = nn(recv_ref[source], up_eff[...])
        hidden_low = gelu_parts(hidden_pre)[0].astype(bf16)
        return nn(hidden_low, down_eff[...]).astype(bf16)

    returned_ref[me] = work(me)

    def step(off, carry):
        source = lax.rem(me + dp - off, dp)
        first(off).wait_recv()
        part[source] = work(source)
        second(off).start()
        return carry

    lax.fori_loop(1, dp, step, 0)
    if gather:
        for k in range(4):
            moving.forward(k)

    def finish(off, carry):
        first(off).wait_send()
        second(off).wait()
        return carry

    lax.fori_loop(1, dp, finish, 0)
    if gather:
        for k in range(4):
            moving.arrive(k)
            moving.sent(k)


def expert_backward_kernel(dp, mp, fast, reduce, *refs):
    refs = list(refs)
    buffer_ref, recv_ref, up_ref, down_ref = refs[:4]
    refs = refs[4:]
    if reduce:
        given_ref, attn_ref = refs[:2]
        refs = refs[2:]
    returned_ref = refs.pop(0)
    if fast:
        units_ref = refs.pop(0)
    else:
        up_term, down_term = refs[:2]
        refs = refs[2:]
    if reduce:
        full_ref, mine_ref = refs[:2]
        refs = refs[2:]
    grads, hidden_low, slope, pre, part = refs[:5]
    refs = refs[5:]
    if fast:
        up_term, down_term = refs[:2]
        refs = refs[2:]
    row = Row() if reduce else None
    if reduce:
        core_in, y_out, y_in = refs[:3]
        sums = RowSum(row, [attn_ref], core_in, y_out, y_in, [mine_ref], refs[3:7])
        gather = RowGather(
            row, [given_ref.at[k] for k in range(2)], [full_ref.at[k] for k in range(2)], row.place, row.place_across,
            refs[7:13],
        )
        refs = refs[13:]
    send_one, recv_one, send_two, recv_two = refs
    split = dp // EXPERTS
    me = lax.axis_index("dp")
    greet(dp, me, (row.sibling, row.across) if reduce else ())

    def first(off):
        peer = lax.rem(me + off, dp)
        return to_peer(buffer_ref.at[lax.div(peer, split)], grads.at[me], send_one.at[off], recv_one.at[off], peer)

    def second(off):
        source = lax.rem(me + dp - off, dp)
        return to_peer(part.at[source], returned_ref.at[me], send_two.at[off], recv_two.at[off], source)

    def start_first(off, carry):
        first(off).start()
        return carry

    lax.fori_loop(1, dp, start_first, 0)
    if reduce:
        sums.start(0)
        for k in range(2):
            gather.start(k)
    grads[me] = buffer_ref[lax.div(me, split)]

    def again(source, carry):
        value, rate = gelu_parts(nn(recv_ref[source], up_ref[...]))
        hidden_low[source] = value.astype(bf16)
        slope[source] = rate
        return carry

    lax.fori_loop(0, dp, again, 0)
    if reduce:
        sums.middle(0)
        for k in range(2):
            full_ref[k, row.place] = given_ref[k]

    def work(source):
        hidden_grad = nt(grads[source], down_ref[...])
        pre_grad = (slope[source] * hidden_grad).astype(bf16)
        pre[source] = pre_grad
        return nt(pre_grad, up_ref[...]).astype(bf16)

    returned_ref[me] = work(me)

    def step(off, carry):
        source = lax.rem(me + dp - off, dp)
        first(off).wait_recv()
        part[source] = work(source)
        second(off).start()
        return carry

    lax.fori_loop(1, dp, step, 0)
    if reduce:
        for k in range(2):
            gather.forward(k)
        sums.end(0)
    up_term[...] = jnp.zeros(up_term.shape, f32)
    down_term[...] = jnp.zeros(down_term.shape, f32)

    def terms(block, carry):
        up_term[...] += tn(recv_ref[block], pre[block])
        down_term[...] += tn(grads[block], hidden_low[block])
        return carry

    lax.fori_loop(0, dp, terms, 0)
    if fast:
        width = up_term.shape[0]
        height = width // mp
        for place in range(mp):
            q = quarter_at(place, mp)
            units_ref[0, place] = up_term[:, q * width : (q + 1) * width].astype(bf16)
            for chunk in range(mp):
                block = down_term[q * height : (q + 1) * height, chunk * width : (chunk + 1) * width]
                units_ref[1, place, chunk * height : (chunk + 1) * height] = block.astype(bf16)

    def finish(off, carry):
        first(off).wait_send()
        second(off).wait()
        return carry

    lax.fori_loop(1, dp, finish, 0)
    if reduce:
        sums.finish(0)
        for k in range(2):
            gather.arrive(k)
            gather.sent(k)


def expert_call(kernel, arrays, outs, scratch, dp, collective_id, name, flops, anys=(), any_outs=()):
    sems = [pltpu.SemaphoreType.DMA((dp,))] * 4
    vmem, anywhere = pl.BlockSpec(memory_space=pltpu.VMEM), pl.BlockSpec(memory_space=pl.ANY)
    return pl.pallas_call(
        kernel,
        out_shape=[jax.ShapeDtypeStruct(shape, dtype) for shape, dtype in (*outs, *any_outs)],
        in_specs=[vmem] * len(arrays) + [anywhere] * len(anys),
        out_specs=[vmem] * len(outs) + [anywhere] * len(any_outs),
        scratch_shapes=scratch + sems,
        compiler_params=pltpu.CompilerParams(
            vmem_limit_bytes=56 * MIB, collective_id=collective_id, has_side_effects=True
        ),
        cost_estimate=pl.CostEstimate(flops=flops, bytes_accessed=20 * MIB, transcendentals=0),
        name=name,
    )(*arrays, *anys)


def by_windows(grid):
    images, kinds = grid.shape[:2]
    blocks = GRID // WINDOW
    grid = grid.reshape(images, kinds, blocks, WINDOW, blocks, WINDOW).transpose(0, 1, 2, 4, 3, 5)
    grid = grid.reshape(images, kinds, blocks * blocks, WINPOS)
    grid = jnp.pad(grid, ((0, 0), (0, 0), (0, 0), (0, WPAD - WINPOS)), constant_values=-1)
    return grid.reshape(images, kinds, IMGROWS)


def per_device(
    patches,
    qkv_weight,
    proj_weight,
    core_up,
    core_down,
    residual_up,
    residual_down,
    position_bias,
    router_weight,
    norm_gain,
    norm_bias,
    cotangent,
    image_valid,
    expert_index,
    slot_index,
    region_id,
):
    dp, mp = lax.axis_size("dp"), lax.axis_size("mp")
    images, _, width = patches.shape
    split = dp // EXPERTS
    hidden = residual_up.shape[-1]
    hidden_full = core_up.shape[-1] * mp
    row_index = lax.axis_index("mp")

    fast = split == 1 and dp == 8 and mp == 4 and hidden == mp * width
    qkv_rows, proj_rows, down_rows = (a.transpose(0, 2, 1) for a in (qkv_weight, proj_weight, core_down))
    shards = (qkv_rows, proj_rows, core_up, down_rows)
    gathered = [[None] * len(shards)] * LAYERS
    if not fast:
        gathered = [[lax.all_gather(a[l], "mp", axis=0, tiled=False) for a in shards] for l in range(LAYERS)]

    position = jnp.where(slot_index >= 0, expert_index * SLOTS + slot_index, -1)
    row_form = by_windows(jnp.stack([position.reshape(images, GRID, GRID), region_id], 1))
    col_form = row_form.transpose(0, 2, 1)
    enter = jnp.asarray(enter_table(), bf16)
    leave = jnp.asarray(enter_table().T, bf16)
    moves = [jnp.asarray(move_table(l % 2 == 1), bf16) for l in range(LAYERS)]
    backs = [jnp.asarray(move_table(l % 2 == 1).T, bf16) for l in range(LAYERS)]
    table_rows = position_bias.transpose(0, 2, 1).reshape(LAYERS * HEADS, OFFSETS)
    table_rows = jnp.pad(table_rows, ((0, 0), (0, TABLE - OFFSETS)))
    entry_row, entry_col = jnp.asarray(cell_entries()[None, :]), jnp.asarray(cell_entries()[:, None])
    routers = jnp.pad(router_weight.transpose(0, 2, 1), ((0, 0), (0, LANES - EXPERTS), (0, 0)))

    token = (images, IMGROWS, width)
    buffer_shape = (ROWS, width)
    block_rows = (dp, SLOTS, width)
    pieces = (split, ROWS, width)

    def by_piece(returned):
        return returned.reshape(EXPERTS, split, SLOTS, width).transpose(1, 0, 2, 3).reshape(pieces)

    records = []
    before = None
    for l in range(LAYERS):
        first = l == 0
        gather = fast and first
        if first:
            arrays = [("image", patches), ("whole", enter)]
        else:
            arrays = [("image", before[0]), ("image", before[1]), ("whole", before[2])]
        arrays += [
            ("smem", image_valid),
            ("image", col_form),
            ("image", row_form),
            ("any", qkv_rows) if gather else ("whole", gathered[l][0]),
            ("any", proj_rows) if gather else ("whole", gathered[l][1]),
            ("whole", table_rows) if first else (l, biases),
            ("whole", moves[l]),
            ("whole", backs[l]),
            (l, norm_gain),
            (l, norm_bias),
            (l, routers),
        ]
        if first:
            arrays.append(("whole", entry_row))
        if gather:
            arrays += [("any", core_up), ("any", down_rows)]
        outs = [("image", token, f32)]
        if first:
            outs.append(("whole", (LAYERS, HEADS, WPAD, LANES), f32))
        else:
            outs.append(("image", token, f32))
        outs += [
            ("image", token, f32),
            ("image", token, bf16),
            ("image", (images, IMGROWS, 1), f32),
            ("whole", buffer_shape, bf16),
            ("image", token, bf16),
            ("image", (images, 2 * width, IMGROWS), bf16),
            ("image", token, bf16),
            ("image", (images, PAIRS * HEADS, WPAD, LANES), bf16),
            ("image", (images, width, IMGROWS), bf16),
            ("whole", (width, width), bf16),
        ]
        scratch = [pltpu.VMEM(buffer_shape, f32)]
        gathered_shapes = [(mp, *a.shape[1:]) for a in shards]
        if gather:
            outs.append(("whole", (3 * width, width), bf16))
            outs += [("any", shape, bf16) for shape in gathered_shapes[2:]]
            scratch += [pltpu.VMEM(shape, bf16) for shape in gathered_shapes[:2]] + WeightGather.scratch(4)
        results = list(
            image_call(
                functools.partial(attention_forward_kernel, first, l % 2 == 1, mp, gather),
                images, arrays, outs, scratch, f"attend_{l}", 3 * LAYERS + 1 if gather else None,
            )
        )
        if gather:
            gathered[l] = [results[-3], None] + results[-2:]
            results = results[:-3]
        carried = results.pop(0)
        if first:
            biases = results.pop(0)
        else:
            records[-1]["expert_out"] = results.pop(0)
        middle, second_low, gate, buffer = results[:4]
        gather = fast and l < LAYERS - 1
        received, returned, up_eff, down_eff, *more = expert_call(
            functools.partial(expert_forward_kernel, dp, mp, l, gather),
            [buffer.reshape(EXPERTS, SLOTS, width)],
            [
                (block_rows, bf16),
                (block_rows, bf16),
                ((width, hidden), bf16),
                ((hidden, width), bf16),
            ],
            [
                pltpu.VMEM(block_rows, bf16),
                pltpu.VMEM((8, LANES) if fast else (width, hidden), f32),
                pltpu.VMEM(gathered_shapes[2], bf16),
                pltpu.VMEM(gathered_shapes[3], bf16),
                pltpu.VMEM((width, hidden), bf16),
                pltpu.VMEM((hidden, width), bf16),
                pltpu.SemaphoreType.DMA((4,)),
            ]
            + (WeightGather.scratch(4) if gather else []),
            dp, l, f"experts_{l}", 4 * dp * SLOTS * width * hidden,
            [gathered[l][2], gathered[l][3], residual_up, residual_down, *(shards if gather else ())],
            [(shape, bf16) for shape in gathered_shapes] if gather else (),
        )
        if gather:
            gathered[l + 1] = more
        returned = by_piece(returned)
        before = (middle, gate, returned)
        records.append(
            dict(
                carried=carried, middle=middle, second_low=second_low, gate=gate, saved=results[4:], received=received,
                up_eff=up_eff, down_eff=down_eff,
            )
        )

    top = records[-1]
    block_output, grad, logit_grad, router_part, buffer = image_call(
        turn_kernel,
        images,
        [
            ("image", before[0]),
            ("image", before[1]),
            ("whole", before[2]),
            ("image", cotangent),
            ("whole", enter),
            ("whole", leave),
            ("image", col_form),
            ("image", row_form),
            ("image", top["second_low"]),
            (LAYERS - 1, routers),
        ],
        [
            ("image", patches.shape, bf16),
            ("image", token, f32),
            ("image", (images, IMGROWS, LANES), f32),
            ("whole", (LANES, width), f32),
            ("whole", buffer_shape, bf16),
        ],
        [pltpu.VMEM(buffer_shape, f32)],
        "turn",
    )
    router_parts, tables, smalls = [None] * LAYERS, [None] * LAYERS, [None] * LAYERS
    residual_sums, shard_sums = [None] * LAYERS, [None] * LAYERS
    router_parts[LAYERS - 1] = router_part
    units, attn_units, mines = [None] * LAYERS, [None] * LAYERS, [None] * LAYERS
    for l in reversed(range(LAYERS)):
        rec = records[l]
        last = l == 0
        reduce = fast and l < LAYERS - 1
        arrays = [buffer.reshape(EXPERTS, SLOTS, width), rec["received"], rec["up_eff"], rec["down_eff"]]
        outs = [(block_rows, bf16)]
        scratch = [
            pltpu.VMEM(block_rows, bf16),
            pltpu.VMEM((dp, SLOTS, hidden), bf16),
            pltpu.VMEM((dp, SLOTS, hidden), f32),
            pltpu.VMEM((dp, SLOTS, hidden), bf16),
            pltpu.VMEM(block_rows, bf16),
        ]
        if fast:
            outs.append(((2, mp, width, width), bf16))
            scratch += [pltpu.VMEM((width, hidden), f32)] * 2
        else:
            outs += [((width, hidden), f32)] * 2
        if reduce:
            arrays += [mines[l + 1], attn_units[l + 1]]
            outs += [((2, mp, width, width), bf16), ((width, width), bf16)]
            scratch += RowSum.scratch(1, width) + RowGather.scratch(2)
        results = list(
            expert_call(
                functools.partial(expert_backward_kernel, dp, mp, fast, reduce), arrays, outs, scratch, dp, LAYERS + l,
                f"experts_back_{l}", 10 * dp * SLOTS * width * hidden,
            )
        )
        returned_grad = results.pop(0)
        if fast:
            units[l] = results.pop(0)
        else:
            residual_sums[l] = lax.psum(tuple(t.astype(bf16) for t in results[:2]), "mp")
        if reduce:
            full_above, mine_above = results
        window_in, qk, v, probs, att, proj_full = rec["saved"]
        qkv_full = gathered[l][0].reshape(3 * width, width)
        arrays = [
            ("smem", image_valid),
            ("image", grad),
            ("whole", by_piece(returned_grad)),
            ("image", logit_grad),
            ("image", rec["middle"]),
            ("image", rec["carried"]),
            (l, routers),
            ("image", col_form),
            ("whole", moves[l]),
            ("whole", backs[l]),
            (l, norm_gain),
            ("whole", proj_full),
            ("whole", qkv_full),
            ("image", window_in),
            ("image", qk),
            ("image", v),
            ("image", probs),
            ("image", att),
        ]
        outs = [("image", patches.shape if last else token, f32)]
        scratch = [pltpu.VMEM((3 * width, (2 - images % 2) * IMGROWS), bf16)]
        closes = fast and last
        table_shape, small_shape = (HEADS, WPAD, LANES), (8, width)
        if fast:
            arrays.append(("whole", units[l]))
            scratch += [pltpu.VMEM((3 * width, width), f32), pltpu.VMEM((width, width), f32)]
        if closes:
            outs += [
                ("whole", (2, mp, width, width), bf16),
                ("whole", (3, width, width), bf16),
                ("whole", (Closing.lines, width), f32),
                ("whole", (3, width, width), bf16),
            ]
        else:
            if fast:
                outs += [
                    ("whole", (2, width // 2, width), bf16),
                    ("whole", (mp, width, width), bf16),
                    ("whole", (2, width, width), bf16),
                ]
            else:
                outs += [("whole", (3 * width, width), f32), ("whole", (width, width), f32)]
            outs += [("whole", table_shape, f32), ("whole", small_shape, f32)]
        if last:
            arrays.append(("whole", leave))
            if fast:
                arrays += [
                    ("whole", a)
                    for a in (
                        tables[1], smalls[1], router_parts[1], router_parts[0], entry_col, halves_above, mine_above,
                    )
                ]
        else:
            below = records[l - 1]
            arrays += [
                ("image", row_form),
                ("image", below["expert_out"]),
                ("image", below["second_low"]),
                (l - 1, routers),
            ]
            outs += [
                ("image", (images, IMGROWS, LANES), f32),
                ("whole", (LANES, width), f32),
                ("whole", buffer_shape, bf16),
            ]
            scratch.append(pltpu.VMEM(buffer_shape, f32))
        if closes:
            scratch += [
                pltpu.VMEM(table_shape, f32),
                pltpu.VMEM(small_shape, f32),
                pltpu.VMEM((mp, width, width), bf16),
                pltpu.VMEM((Closing.lines, width), f32),
            ]
            scratch += [pltpu.VMEM(shape, dtype) for _, shape, dtype in outs[1:5]] + Closing.scratch(dp, width)
        elif fast:
            scratch += RowSum.scratch(2, width) + [pltpu.VMEM((2, width // 2, width), bf16)]
            scratch += [pltpu.SemaphoreType.DMA((2,))] * 2
        results = list(
            image_call(
                functools.partial(attention_backward_kernel, last, dp, mp, fast),
                images, arrays, outs, scratch, f"attend_back_{l}", 2 * LAYERS + 1 + l if fast else None,
            )
        )
        grad = results.pop(0)
        if closes:
            full, closed, lines, shard_above = results
            continue
        if fast:
            halves_above = results.pop(0)
            attn_units[l], mines[l] = results[:2]
        else:
            qkv_part, proj_part = results[:2]
        tables[l], smalls[l] = results[2:4]
        if not last:
            logit_grad, router_parts[l - 1], buffer = results[4:]
        if fast:
            continue
        attn = (
            lax.psum_scatter(qkv_part.astype(bf16), "mp", scatter_dimension=0, tiled=True),
            lax.psum_scatter(proj_part.T.astype(bf16), "mp", scatter_dimension=0, tiled=True),
        )
        up_sum, down_sum = residual_sums[l]
        if split > 1:
            begin = lax.axis_index("dp") % split * hidden
            empty = jnp.zeros((width, hidden_full), bf16)
            up_sum = lax.dynamic_update_slice_in_dim(empty, up_sum, begin, 1)
            down_sum = lax.dynamic_update_slice_in_dim(empty, down_sum, begin, 1)
        up_columns, down_columns = core_up.shape[-1], core_down.shape[-1]
        up_shard = lax.dynamic_slice_in_dim(up_sum, row_index * up_columns, up_columns, 1)
        down_shard = lax.dynamic_slice_in_dim(down_sum, row_index * down_columns, down_columns, 0)
        shard_sums[l] = lax.psum((attn[0], attn[1], up_shard, down_shard), "dp")

    if fast:
        *attn_grads, core_up_grad, core_down_grad, residual_up_grad, residual_down_grad = format_call(
            [full, full_above], [closed, shard_above], qkv_weight.shape[-1]
        )
        attn_grads = [a.transpose(0, 2, 1) for a in attn_grads]
        core_grads = (core_up_grad, core_down_grad.transpose(0, 2, 1))
        at = LAYERS * HEADS
        table_sum = lines[:at, :OFFSETS]
        router_sum = lines[at : at + LAYERS * EXPERTS].reshape(LAYERS, EXPERTS, width)
        at += LAYERS * EXPERTS
        small_sum = lines[at : at + LAYERS * 8].reshape(LAYERS, 8, width)[:, :4]
    else:
        entry = cell_entries()[None, :] + np.array([key_base_of(key) for key in range(WPAD)])[:, None]
        entry = jnp.asarray(np.where(np.arange(WPAD)[:, None] < WINPOS, entry, -1).reshape(-1))
        entry_turned = (entry[:, None] == jnp.arange(OFFSETS)[None, :]).astype(f32)
        table_part = jnp.dot(
            jnp.stack(tables, 0).reshape(LAYERS * HEADS, WPAD * LANES), entry_turned, precision=highest
        )
        small_part = jnp.stack(smalls, 0)[:, :4]
        router_part = jnp.stack(router_parts, 0)[:, :EXPERTS]
        table_sum, small_sum, router_sum = lax.psum((table_part, small_part, router_part), ("dp", "mp"))

        def shard(k):
            return jnp.stack([shard_sums[l][k] for l in range(LAYERS)], 0).astype(f32)

        attn_grads = (shard(0).transpose(0, 2, 1), shard(1).transpose(0, 2, 1))
        core_grads = (shard(2), shard(3).transpose(0, 2, 1))
        residual_up_grad, residual_down_grad = (
            jnp.stack([residual_sums[l][k] for l in range(LAYERS)], 0).astype(f32) for k in range(2)
        )
        residual_up_grad = residual_up_grad[:, None]
        residual_down_grad = residual_down_grad.transpose(0, 2, 1)[:, None]

    return (
        block_output,
        grad,
        attn_grads[0],
        attn_grads[1],
        core_grads[0],
        core_grads[1],
        residual_up_grad,
        residual_down_grad,
        table_sum.reshape(LAYERS, HEADS, OFFSETS).transpose(0, 2, 1),
        router_sum.transpose(0, 2, 1),
        small_sum[:, 0:2],
        small_sum[:, 2:4],
    )


def solution(mesh):
    placed = (
        P(("dp", "mp"), None, None),
        P(None, None, "mp"),
        P(None, None, "mp"),
        P(None, None, "mp"),
        P(None, None, "mp"),
        P(None, "dp", None, None),
        P(None, "dp", None, None),
        P(),
        P(),
        P(),
        P(),
        P(("dp", "mp"), None, None),
        P(("dp", "mp")),
        P(("dp", "mp"), None),
        P(("dp", "mp"), None),
        P(("dp", "mp"), None, None),
    )
    return jax.shard_map(
        per_device,
        mesh=mesh,
        in_specs=placed,
        out_specs=(
            P(("dp", "mp"), None, None),
            P(("dp", "mp"), None, None),
            P(None, None, "mp"),
            P(None, None, "mp"),
            P(None, None, "mp"),
            P(None, None, "mp"),
            P(None, "dp", None, None),
            P(None, "dp", None, None),
            P(),
            P(),
            P(),
            P(),
        ),
        check_vma=False,
    )
```

```python
import functools

import jax
import jax.numpy as jnp
import numpy as np
from jax import lax
from jax.experimental import pallas as pl
from jax.experimental.pallas import tpu as pltpu
from jax.sharding import PartitionSpec as P

HEADS = 12
HEAD_DIM = 32
EXPERTS = 8
WINDOW = 7
GRID = 14
SHIFT = 3
LAYERS = 2
WINPOS = 49
OFFSETS = 169
CAP = 122

WPAD = 64
IMGROWS = 256
PATCHES = 196
SLOTS = 128
ROWS = EXPERTS * SLOTS
LANES = 128
GROUP = 4
PAIRS = 2
TABLE = 256

bf16 = jnp.bfloat16
f32 = jnp.float32
highest = lax.Precision.HIGHEST
norm_epsilon = 1e-05
mask_fill = -100.0
head_scale = HEAD_DIM ** (-0.5)
MESH = pl.DeviceIdType.MESH
MIB = 1024 * 1024


def nn(a, b):
    return lax.dot_general(a, b, (((1,), (0,)), ((), ())), preferred_element_type=f32)


def nt(a, b):
    return lax.dot_general(a, b, (((1,), (1,)), ((), ())), preferred_element_type=f32)


def tn(a, b):
    return lax.dot_general(a, b, (((0,), (0,)), ((), ())), preferred_element_type=f32)


def iota(shape, dim):
    return lax.broadcasted_iota(jnp.int32, shape, dim)


def onehot(flags):
    return jnp.where(flags, 1.0, 0.0).astype(bf16)


def natural_of_row(shifted):
    moved = SHIFT if shifted else 0
    blocks = GRID // WINDOW
    out = -np.ones(IMGROWS, np.int32)
    for window in range(blocks * blocks):
        for cell in range(WINPOS):
            row = (window // blocks * WINDOW + cell // WINDOW + moved) % GRID
            col = (window % blocks * WINDOW + cell % WINDOW + moved) % GRID
            out[window * WPAD + cell] = row * GRID + col
    return out


def key_base_of(key):
    return (2 * WINDOW) * (WINDOW - 1) - (key // WINDOW * (2 * WINDOW - 1) + key % WINDOW)


def enter_table():
    held = natural_of_row(False)
    return (held[:, None] == np.arange(PATCHES)[None, :]).astype(np.float32)


def move_table(shifted):
    first, second = natural_of_row(False), natural_of_row(shifted)
    same = (second[:, None] == first[None, :]) & (second[:, None] >= 0)
    return same.astype(np.float32)


def cell_entries():
    cell = np.arange(LANES) % WPAD
    return np.where(cell < WINPOS, cell // WINDOW * (2 * WINDOW - 1) + cell % WINDOW, -4 * TABLE).astype(np.int32)


def norm_parts(x):
    width = x.shape[-1]
    center = x - jnp.sum(x, -1, keepdims=True) * (1.0 / width)
    spread = jnp.sum(center * center, -1, keepdims=True) * (1.0 / width)
    rstd = lax.rsqrt(spread + norm_epsilon)
    return center * rstd, rstd


def norm_back(grad, gain, xhat, rstd):
    width = xhat.shape[-1]
    dxhat = grad * gain
    mean_one = jnp.sum(dxhat, -1, keepdims=True) * (1.0 / width)
    mean_two = jnp.sum(dxhat * xhat, -1, keepdims=True) * (1.0 / width)
    return rstd * (dxhat - mean_one - xhat * mean_two)


def split_two(x):
    high = x.astype(bf16)
    return high, (x - high.astype(f32)).astype(bf16)


def collect(pos_col, returned_ref):
    pick = onehot(pos_col == iota((pos_col.shape[0], ROWS), 1))
    out = nn(pick, returned_ref[0])
    for piece in range(1, returned_ref.shape[0]):
        out = out + nn(pick, returned_ref[piece])
    return out


def join(ref):
    return ref[...].reshape(ref.shape[0] * ref.shape[1], *ref.shape[2:])


def store(ref, rows):
    ref[...] = rows.reshape(ref.shape).astype(ref.dtype)


def per_image(function, count):
    return jnp.concatenate([function(i) for i in range(count)], 0)


def image_rows(i):
    return slice(i * IMGROWS, (i + 1) * IMGROWS)


def lay_positions(row_ref):
    return jnp.concatenate([row_ref[i, 0:1, :] for i in range(row_ref.shape[0])], 1)


def spread_rows(pos_row, rows_low):
    return nn(onehot(iota((ROWS, pos_row.shape[1]), 0) == pos_row), rows_low)


def route(second_low, router, pos_col):
    logits = nt(second_low, router)
    lane = iota(logits.shape, 1)
    logits = jnp.where(lane < EXPERTS, logits, -1e30)
    expo = jnp.exp(logits - jnp.max(logits, -1, keepdims=True))
    probs = expo / jnp.sum(expo, -1, keepdims=True)
    expert = jnp.where(pos_col >= 0, pos_col // SLOTS, -1)
    chosen = jnp.where(lane == expert, 1.0, 0.0)
    return probs, chosen, jnp.sum(probs * chosen, -1, keepdims=True)


def head_masks():
    rows = iota((LANES, LANES), 0) // HEAD_DIM
    return [onehot(rows == h) for h in range(GROUP)]


def lane_masks():
    lane = iota((WPAD, LANES), 1)
    return [onehot(lane < WPAD), onehot(lane >= WPAD)]


def keys_entry(cells, key_row, turned):
    parts = [cells + (key_base_of(col) - key_row * (2 * WINDOW - 1)) for col in range(WINDOW)]
    return jnp.concatenate(parts, 0 if turned else 1)


def form_bias(bias_ref, table_ref, entry_row):
    layers, heads = bias_ref.shape[:2]
    lines = layers * heads
    bias_ref[...] = jnp.where(iota(bias_ref.shape, 2) < WINPOS, 0.0, -1e30)
    table = table_ref[...]
    high = table.astype(bf16)
    mid, low = split_two(table - high.astype(f32))
    parts = jnp.concatenate([high.astype(f32), mid.astype(f32), low.astype(f32)], 0).astype(bf16)

    def step(key_row, carry):
        pick = onehot(iota((TABLE, WINDOW * LANES), 0) == keys_entry(entry_row, key_row, False))
        rows = nn(parts, pick)
        rows = rows[:lines] + rows[lines : 2 * lines] + rows[2 * lines :]
        for col in range(WINDOW):
            for layer in range(layers):
                part = rows[layer * heads : (layer + 1) * heads, col * LANES : (col + 1) * LANES]
                bias_ref[layer, :, pl.ds(key_row * WINDOW + col, 1), :] = part.reshape(heads, 1, LANES)
        return carry

    lax.fori_loop(0, WINDOW, step, 0)


def table_grad(parts, entry_col):
    heads = parts[0].shape[0]
    lines = heads * len(parts)

    def step(key_row, total):
        keys = [
            jnp.concatenate([ref[:, pl.ds(key_row * WINDOW + col, 1), :].reshape(heads, LANES) for ref in parts], 0)
            for col in range(WINDOW)
        ]
        rows = jnp.concatenate(keys, 1)
        high = rows.astype(bf16).astype(f32)
        both = jnp.concatenate([high, rows - high], 0).astype(bf16)
        entry = keys_entry(entry_col, key_row, True)
        out = nn(both, onehot(iota((WINDOW * LANES, TABLE), 1) == entry))
        return total + out[:lines] + out[lines:]

    return lax.fori_loop(0, WINDOW, step, jnp.zeros((lines, TABLE), f32))


def attention_forward_kernel(first, shifted, mp, gather, *refs):
    refs = list(refs)
    if first:
        patches_ref, enter_ref = refs[:2]
        refs = refs[2:]
    else:
        prev_ref, prev_gate_ref, returned_ref = refs[:3]
        refs = refs[3:]
    (
        valid_ref, col_ref, row_ref, qkv_ref, proj_ref, bias_ref, move_ref, back_ref, gain_ref, nbias_ref, router_ref,
    ) = refs[:11]
    gain_ref, nbias_ref, router_ref = (ref.at[0] for ref in (gain_ref, nbias_ref, router_ref))
    refs = refs[11:]
    if first:
        table_ref, entry_ref = bias_ref, refs.pop(0)
    if gather:
        core_up_ref, core_down_ref = refs[:2]
        refs = refs[2:]
    carried_ref = refs.pop(0)
    if first:
        biases_ref = refs.pop(0)
        bias_ref = biases_ref.at[0]
    else:
        expert_out_ref = refs.pop(0)
        bias_ref = bias_ref.at[0]
    middle_ref, second_ref, gate_ref, buffer_ref, window_ref, qk_ref, v_ref, probs_ref, att_ref, proj_full = refs[:10]
    refs = refs[10:]
    if gather:
        qkv_full = refs.pop(0)
        up_out, down_out = refs[:2]
        refs = refs[2:]
    total_ref = refs.pop(0)
    step = pl.program_id(0)
    final = pl.num_programs(0) - 1
    count, _, width = carried_ref.shape
    if gather:
        shards = [ref.at[0] for ref in (qkv_ref, proj_ref, core_up_ref, core_down_ref)]
        qkv_ref, proj_ref = refs[:2]
        moving = WeightGather(shards, [qkv_ref, proj_ref, up_out, down_out], refs[2:])

        @pl.when(step == 0)
        def _():
            pl.semaphore_wait(moving.row.greet(), 2)
            for k in (0, 1):
                moving.start(k)
            form_bias(biases_ref, table_ref, entry_ref[...])

        @pl.when(step == final)
        def _():
            for k in (2, 3):
                moving.forward(k)

    pos_col = join(col_ref)[:, 0:1]
    if first:
        x = per_image(lambda i: nn(enter_ref[...], patches_ref[i]), count)
    else:
        expert_out = collect(pos_col, returned_ref)
        store(expert_out_ref, expert_out)
        x = join(prev_ref) + join(prev_gate_ref) * expert_out
    store(carried_ref, x)
    xhat, _ = norm_parts(x)
    normed = (xhat * gain_ref[0:1, :] + nbias_ref[0:1, :]).astype(bf16)
    window_in = per_image(lambda i: nn(move_ref[...], normed[image_rows(i)]), count).astype(bf16)
    store(window_ref, window_in)

    @pl.when(step == 0)
    def _():
        if gather:
            for k in (0, 1):
                moving.forward(k)
            for k in (2, 3):
                moving.start(k)
            for k in (0, 1):
                moving.arrive(k)
            qkv_full[...] = join(qkv_ref)
        elif first:
            form_bias(biases_ref, table_ref, entry_ref[...])
        proj_full[...] = join(proj_ref).astype(f32).T.astype(bf16)
        total_ref[...] = jnp.zeros(total_ref.shape, f32)

    qkv = join(qkv_ref)
    turned = nt(qkv, window_in).astype(bf16)
    straight = nt(window_in, qkv[width:]).astype(bf16)
    for i in range(count):
        qk_ref[i] = turned[: 2 * width, image_rows(i)]
    store(v_ref, straight[:, width:])
    heads_rows = head_masks()
    halves = lane_masks()
    low_lane = iota((WPAD, LANES), 1) < WPAD
    if shifted:
        row_labels = [nt(row_ref[i].astype(f32).astype(bf16), move_ref[...]) for i in range(count)]
        col_labels = [nn(move_ref[...], col_ref[i].astype(f32).astype(bf16)) for i in range(count)]
    for pair in range(PAIRS * count):
        image, side = pair // PAIRS, pair % PAIRS
        across = slice(pair * LANES, (pair + 1) * LANES)
        within = slice(side * LANES, (side + 1) * LANES)
        if shifted:
            ahead = col_labels[image][side * LANES : side * LANES + WPAD, 1:2]
            behind = col_labels[image][side * LANES + WPAD : (side + 1) * LANES, 1:2]
            key_label = jnp.where(low_lane, ahead, behind)
            mask = jnp.where(key_label == row_labels[image][1:2, within], 0.0, mask_fill)
        for group in range(HEADS // GROUP):
            features = slice(group * LANES, (group + 1) * LANES)
            queries = turned[features, across]
            spread = jnp.concatenate([queries * heads_rows[h] for h in range(GROUP)], 1)
            raw = nn(straight[across, features], spread)
            for h in range(GROUP):
                head = group * GROUP + h
                part = raw[:, h * LANES : (h + 1) * LANES]
                scores = jnp.where(low_lane, part[:WPAD], part[WPAD:]) * head_scale + bias_ref[head]
                if shifted:
                    scores = scores + mask
                expo = jnp.exp(scores - jnp.max(scores, 0, keepdims=True))
                probs = (expo * (1.0 / jnp.sum(expo, 0, keepdims=True))).astype(bf16)
                probs_ref[image, side * HEADS + head] = probs
                both = jnp.concatenate([probs * halves[0], probs * halves[1]], 0)
                at = slice(head * HEAD_DIM, (head + 1) * HEAD_DIM)
                values = turned[2 * width + head * HEAD_DIM : 2 * width + (head + 1) * HEAD_DIM, across]
                att_ref[image, at, within] = nn(values, both).astype(bf16)
    attended = per_image(lambda i: nt(back_ref[...], att_ref[i]), count).astype(bf16)
    branch = nt(attended, join(proj_ref))
    middle = x + per_image(lambda i: valid_ref[step * count + i].astype(f32) * branch[image_rows(i)], count)
    store(middle_ref, middle)
    xhat, _ = norm_parts(middle)
    second_low = (xhat * gain_ref[1:2, :] + nbias_ref[1:2, :]).astype(bf16)
    store(second_ref, second_low)
    _, _, gate = route(second_low, router_ref[...], pos_col)
    store(gate_ref, gate)
    total_ref[...] += spread_rows(lay_positions(row_ref), second_low)

    @pl.when(step == final)
    def _():
        buffer_ref[...] = total_ref[...].astype(bf16)
        if gather:
            for k in (2, 3):
                moving.arrive(k)
            for k in range(4):
                moving.sent(k)


def image_spec(array_shape, count):
    rest = tuple(array_shape[1:])
    zeros = (0,) * len(rest)
    return pl.BlockSpec((count,) + rest, lambda i: (i,) + zeros)


def whole_spec(array_shape):
    zeros = (0,) * len(array_shape)
    return pl.BlockSpec(tuple(array_shape), lambda i: zeros)


def image_call(kernel, images, arrays, outs, scratch, name, collective_id=None):
    count = 2 - images % 2

    def spec(kind, shape):
        if isinstance(kind, int):
            rest = tuple(shape[1:])
            return pl.BlockSpec((1,) + rest, lambda i: (kind,) + (0,) * len(rest))
        if kind in ("smem", "any"):
            return pl.BlockSpec(memory_space=pltpu.SMEM if kind == "smem" else pl.ANY)
        return image_spec(shape, count) if kind == "image" else whole_spec(shape)

    return pl.pallas_call(
        kernel,
        grid=(images // count,),
        out_shape=[jax.ShapeDtypeStruct(shape, dtype) for _, shape, dtype in outs],
        in_specs=[spec(kind, array.shape) for kind, array in arrays],
        out_specs=[spec(kind, shape) for kind, shape, _ in outs],
        scratch_shapes=scratch,
        compiler_params=pltpu.CompilerParams(
            vmem_limit_bytes=56 * MIB,
            dimension_semantics=("arbitrary",),
            collective_id=collective_id,
            has_side_effects=collective_id is not None,
        ),
        name=name,
    )(*[array for _, array in arrays])


def send_part(g, expert_out, second_low, router, pos_col, pos_row, logit_ref, router_grad_ref, total_ref):
    probs, chosen, gate = route(second_low, router, pos_col)
    gate_grad = jnp.where(pos_col >= 0, jnp.sum(g * expert_out, -1, keepdims=True), 0.0)
    sent = (gate * g).astype(bf16)
    logit_grad = gate_grad * gate * (chosen - probs)
    store(logit_ref, logit_grad)
    high, low = split_two(logit_grad)
    router_grad_ref[...] += tn(high, second_low) + tn(low, second_low)
    total_ref[...] += spread_rows(pos_row, sent)


def turn_kernel(
    prev_ref, gate_ref, returned_ref, cotangent_ref, enter_ref, leave_ref, col_ref, row_ref, second_ref, router_ref,
    block_ref, grad_ref, logit_ref, router_grad_ref, buffer_ref, total_ref,
):
    step = pl.program_id(0)
    count = cotangent_ref.shape[0]

    @pl.when(step == 0)
    def _():
        total_ref[...] = jnp.zeros(total_ref.shape, f32)
        router_grad_ref[...] = jnp.zeros(router_grad_ref.shape, f32)

    pos_col = join(col_ref)[:, 0:1]
    expert_out = collect(pos_col, returned_ref)
    x = (join(prev_ref) + join(gate_ref) * expert_out).astype(bf16)
    for i in range(count):
        block_ref[i] = nn(leave_ref[...], x[image_rows(i)]).astype(bf16)
    g = per_image(lambda i: nn(enter_ref[...], cotangent_ref[i]), count)
    store(grad_ref, g)
    send_part(
        g, expert_out, join(second_ref), router_ref[0], pos_col, lay_positions(row_ref), logit_ref, router_grad_ref, total_ref
    )

    @pl.when(step == pl.num_programs(0) - 1)
    def _():
        buffer_ref[...] = total_ref[...].astype(bf16)


def attention_backward_kernel(last, dp, mp, fast, *refs):
    (
        valid_ref, grad_ref, returned_ref, logit_ref, middle_ref, carried_ref, router_ref, col_ref, move_ref, back_ref,
        gain_ref, proj_ref, qkv_ref, window_ref, qk_ref, v_ref, probs_ref, att_ref,
    ) = refs[:18]
    refs = refs[18:]
    refs = list(refs)
    if fast:
        units_ref = refs.pop(0)
    if last:
        leave_ref = refs.pop(0)
        if fast:
            table_above, small_above, router_above, router_here, entry_ref, half_above, down_above, attn_above = refs[:8]
            refs = refs[8:]
    else:
        row_ref, expert_out_ref, second_ref, router_next_ref = refs[:4]
        refs = refs[4:]
    out_ref = refs.pop(0)
    closing = None
    if fast and last:
        results, refs = refs[:4], refs[4:]
    else:
        if fast:
            halves_ref = refs.pop(0)
            unit_ref, mine_ref = refs[:2]
        else:
            qkv_grad_ref, proj_grad_ref = refs[:2]
        table_ref, small_ref = refs[2:4]
        refs = refs[4:]
    if not last:
        logit_out_ref, router_grad_ref, buffer_ref = refs[:3]
        refs = refs[3:]
    turned = refs.pop(0)
    if fast:
        qkv_grad_ref, proj_grad_ref = refs[:2]
        refs = refs[2:]
    if not last:
        total_ref = refs.pop(0)
    step = pl.program_id(0)
    final = pl.num_programs(0) - 1
    count, _, width = carried_ref.shape
    if fast:
        row = Row()
        if last:
            table_ref, small_ref, unit_ref, lines_ref = refs[:4]
            landing, refs = refs[4:8], refs[8:]
            above = (half_above, down_above.at[1], attn_above)
            closing = Closing(row, dp, units_ref, unit_ref, lines_ref, above, landing, refs)
        else:
            sums = RowSum(row, blocks(units_ref), refs[0], refs[1], refs[2], blocks(mine_ref), refs[3:7])
            across_x = DeepSum(dp, [mine_ref.at[0]], [refs[7]], [halves_ref], [None], [None], refs[8:10] * 4)

        def take(k):
            if closing:
                closing.take(k)
            else:
                sums.end(k)
                if k == 0:
                    across_x.over_x(k).start()

        @pl.when(step == 0)
        def _():
            if closing:
                closing.enter()
            else:
                barrier = row.greet()
                pl.semaphore_wait(barrier, 2 + across_x.greet(barrier, False))
                for k in range(2):
                    sums.start(k)

    @pl.when(step == 0)
    def _():
        qkv_grad_ref[...] = jnp.zeros(qkv_grad_ref.shape, f32)
        proj_grad_ref[...] = jnp.zeros(proj_grad_ref.shape, f32)
        table_ref[...] = jnp.zeros(table_ref.shape, f32)
        small_ref[...] = jnp.zeros(small_ref.shape, f32)
        if not last:
            total_ref[...] = jnp.zeros(total_ref.shape, f32)
            router_grad_ref[...] = jnp.zeros(router_grad_ref.shape, f32)

    pos_col = join(col_ref)[:, 0:1]
    g = join(grad_ref)
    high, low = split_two(join(logit_ref))
    gain_ref, router = gain_ref.at[0], router_ref[0]
    normed_grad = collect(pos_col, returned_ref) + nn(high, router) + nn(low, router)
    xhat, rstd = norm_parts(join(middle_ref))
    small_ref[1:2, :] += jnp.sum(normed_grad * xhat, 0, keepdims=True)
    small_ref[3:4, :] += jnp.sum(normed_grad, 0, keepdims=True)
    middle_grad = g + norm_back(normed_grad, gain_ref[1:2, :], xhat, rstd)

    def branch_part(i):
        low_part = (valid_ref[step * count + i].astype(f32) * middle_grad[image_rows(i)]).astype(bf16)
        return nn(move_ref[...], low_part)

    branch_grad = per_image(branch_part, count).astype(bf16)
    for i in range(count):
        proj_grad_ref[...] += nn(att_ref[i], branch_grad[image_rows(i)])
    att_grad = nt(proj_ref[...], branch_grad).astype(bf16)
    if fast:

        @pl.when(step == 0)
        def _():
            if closing:
                closing.early()
            else:
                for k in range(2):
                    sums.middle(k)

        pl.when(step == final)(functools.partial(take, 0))

    heads_rows = head_masks()
    halves = lane_masks()
    low_lane = iota((WPAD, LANES), 1) < WPAD
    for pair in range(PAIRS * count):
        image, side = pair // PAIRS, pair % PAIRS
        across = slice(pair * LANES, (pair + 1) * LANES)
        within = slice(side * LANES, (side + 1) * LANES)
        for group in range(HEADS // GROUP):
            features = slice(group * LANES, (group + 1) * LANES)
            grads = att_grad[features, across]
            spread = jnp.concatenate([grads * heads_rows[h] for h in range(GROUP)], 1)
            raw = nn(v_ref[image, within, features], spread)
            for h in range(GROUP):
                head = group * GROUP + h
                at = slice(head * HEAD_DIM, (head + 1) * HEAD_DIM)
                below = slice(width + head * HEAD_DIM, width + (head + 1) * HEAD_DIM)
                lowest = slice(2 * width + head * HEAD_DIM, 2 * width + (head + 1) * HEAD_DIM)
                part = raw[:, h * LANES : (h + 1) * LANES]
                probs_grad = jnp.where(low_lane, part[:WPAD], part[WPAD:])
                probs_low = probs_ref[image, side * HEADS + head]
                probs = probs_low.astype(f32)
                weighted = probs * probs_grad
                scores_grad = weighted - probs * jnp.sum(weighted, 0, keepdims=True)
                table_ref[head] += scores_grad
                scores_low = scores_grad.astype(bf16)
                both = jnp.concatenate([scores_low * halves[0], scores_low * halves[1]], 0)
                probs_both = jnp.concatenate([probs_low * halves[0], probs_low * halves[1]], 0)
                turned[at, across] = (nn(qk_ref[image, below, within], both) * head_scale).astype(bf16)
                turned[below, across] = (nt(qk_ref[image, at, within], both) * head_scale).astype(bf16)
                turned[lowest, across] = nt(att_grad[at, across], probs_both).astype(bf16)
    qkv_grad_ref[...] += nn(turned[...], join(window_ref))
    if fast:

        @pl.when(step == final)
        def _():
            columns, rows = 3 * width // mp, width // mp
            proj_turned = proj_grad_ref[...].T
            for place in range(mp):
                q = quarter_at(place, mp)
                unit_ref[place, :columns] = qkv_grad_ref[q * columns : (q + 1) * columns].astype(bf16)
                unit_ref[place, columns:] = proj_turned[q * rows : (q + 1) * rows].astype(bf16)
            take(1)
            if closing:
                closing.open()

    mixed_grad = per_image(lambda i: nt(back_ref[...], turned[:, image_rows(i)]), count).astype(bf16)
    first_grad = nn(mixed_grad, qkv_ref[...])
    xhat, rstd = norm_parts(join(carried_ref))
    small_ref[0:1, :] += jnp.sum(first_grad * xhat, 0, keepdims=True)
    small_ref[2:3, :] += jnp.sum(first_grad, 0, keepdims=True)
    out = middle_grad + norm_back(first_grad, gain_ref[0:1, :], xhat, rstd)
    if closing:

        @pl.when(step == final)
        def _():
            closing.attend()

    if last:
        top = out.astype(bf16)
        rest = out - top.astype(f32)
        mid, low = split_two(rest)
        leave = leave_ref[...]
        for i in range(count):
            at = image_rows(i)
            out_ref[i] = nn(leave, top[at]) + nn(leave, mid[at]) + nn(leave, low[at])
    else:
        store(out_ref, out)
        send_part(
            out, join(expert_out_ref), join(second_ref), router_next_ref[0], pos_col, lay_positions(row_ref), logit_out_ref,
            router_grad_ref, total_ref,
        )

    @pl.when(step == final)
    def _():
        if not last:
            buffer_ref[...] = total_ref[...].astype(bf16)
        if closing:
            heads = 2 * HEADS
            lines_ref[...] = jnp.zeros(lines_ref.shape, f32)
            lines_ref[:heads, :TABLE] = table_grad([table_ref, table_above], entry_ref[...])
            lines_ref[heads : heads + EXPERTS] = router_here[:EXPERTS]
            lines_ref[heads + EXPERTS : heads + 2 * EXPERTS] = router_above[:EXPERTS]
            lines_ref[heads + 2 * EXPERTS : heads + 2 * EXPERTS + 8] = small_ref[...]
            lines_ref[heads + 2 * EXPERTS + 8 : heads + 2 * EXPERTS + 16] = small_above[...]
            closing.finish()
            for out, landed in zip(results, landing):
                out[...] = landed[...]
        elif fast:
            across_x.halve(0)
            across_x.over_x(0).wait_send()
            for k in range(2):
                sums.finish(k)


def quarter_at(place, mp):
    return place % (mp // 2) * 2 + place // (mp // 2)


def add_up(*parts):
    total = parts[0].astype(f32)
    for part in parts[1:]:
        total = total + part.astype(f32)
    return total


def to_row(source, target, sems, k, row):
    return pltpu.make_async_remote_copy(
        src_ref=source,
        dst_ref=target,
        send_sem=sems[0].at[k],
        recv_sem=sems[1].at[k],
        device_id={"mp": row},
        device_id_type=MESH,
    )


class Row:
    def __init__(self):
        row = lax.axis_index("mp")
        self.row, self.core, self.y = row, lax.rem(row, 2), lax.div(row, 2)
        self.sibling, self.across = row + 1 - 2 * self.core, row + 2 - 4 * self.y
        self.place = self.core * 2 + self.y
        self.place_across = self.core * 2 + 1 - self.y

    def greet(self):
        barrier = pltpu.get_barrier_semaphore()
        for row in (self.sibling, self.across):
            pl.semaphore_signal(barrier, inc=1, device_id={"mp": row}, device_id_type=MESH)
        return barrier


class RowSum:
    semaphores = 4

    def __init__(self, row, units, core_in, y_out, y_in, mine, sems):
        self.row, self.units, self.mine = row, units, mine
        self.core_in, self.y_out, self.y_in = core_in, y_out, y_in
        self.sems = (sems[:2], sems[2:])

    def pair(self, k):
        theirs = self.units[k].at[pl.ds(2 * (1 - self.row.core), 2)]
        return to_row(theirs, self.core_in.at[k], self.sems[0], k, self.row.sibling)

    def cross(self, k):
        return to_row(self.y_out.at[k], self.y_in.at[k], self.sems[1], k, self.row.across)

    def start(self, k):
        self.pair(k).start()

    def middle(self, k):
        self.pair(k).wait_recv()
        other = 1 - self.row.y
        mixed = add_up(self.units[k][self.row.core * 2 + other], self.core_in[k, other])
        self.y_out[k] = mixed.astype(bf16)
        self.cross(k).start()

    def end(self, k):
        self.cross(k).wait_recv()
        self.mine[k][...] = add_up(
            self.units[k][self.row.place], self.core_in[k, self.row.y], self.y_in[k]
        ).astype(bf16)

    def finish(self, k):
        self.pair(k).wait_send()
        self.cross(k).wait_send()

    @classmethod
    def scratch(cls, count, width):
        return [
            pltpu.VMEM((count, 2, width, width), bf16),
            pltpu.VMEM((count, width, width), bf16),
            pltpu.VMEM((count, width, width), bf16),
        ] + [pltpu.SemaphoreType.DMA((count,))] * cls.semaphores


class RowGather:
    semaphores = 6

    def __init__(self, row, sources, fulls, slot, slot_across, sems):
        self.row, self.sources, self.fulls = row, sources, fulls
        self.slot, self.slot_across = slot, slot_across
        self.sems = (sems[:2], sems[2:4], sems[4:])

    def over(self, k):
        return to_row(self.sources[k], self.fulls[k].at[self.slot], self.sems[0], k, self.row.across)

    def near(self, k):
        return to_row(self.sources[k], self.fulls[k].at[self.slot], self.sems[1], k, self.row.sibling)

    def onward(self, k):
        block = self.fulls[k].at[self.slot_across]
        return to_row(block, block, self.sems[2], k, self.row.sibling)

    def start(self, k):
        self.over(k).start()
        self.near(k).start()

    def forward(self, k):
        self.over(k).wait_recv()
        self.onward(k).start()

    def arrive(self, k):
        self.near(k).wait_recv()
        self.onward(k).wait_recv()

    def sent(self, k):
        self.over(k).wait_send()
        self.near(k).wait_send()
        self.onward(k).wait_send()

    @classmethod
    def scratch(cls, count):
        return [pltpu.SemaphoreType.DMA((count,))] * cls.semaphores


class WeightGather(RowGather):
    def __init__(self, shards, fulls, sems):
        row = Row()
        super().__init__(row, shards, fulls, row.row, row.across, sems[:6])
        self.own_sem = sems[6]

    def own(self, k):
        return pltpu.make_async_copy(self.sources[k], self.fulls[k].at[self.slot], self.own_sem.at[k])

    def start(self, k):
        super().start(k)
        self.own(k).start()

    def arrive(self, k):
        super().arrive(k)
        self.own(k).wait()

    @classmethod
    def scratch(cls, count):
        return super().scratch(count) + [pltpu.SemaphoreType.DMA((count,))]


class DeepSum:
    def __init__(self, dp, total, arrived, halves, slots, result, sems):
        self.total, self.arrived, self.halves, self.slots, self.result = total, arrived, halves, slots, result
        self.x_sems, self.z_sems, self.z_back, self.x_back = (sems[2 * k : 2 * k + 2] for k in range(4))
        me = lax.axis_index("dp")
        self.x, self.z, self.deep = lax.rem(me, 2), lax.div(me, 2), dp // 2
        self.partner = me + 1 - 2 * self.x

    def greet(self, barrier, whole=True):
        pl.semaphore_signal(barrier, inc=1, device_id={"dp": self.partner}, device_id_type=MESH)
        if not whole:
            return 1
        for off in range(1, self.deep):
            peer = lax.rem(self.z + off, self.deep) * 2 + self.x
            pl.semaphore_signal(barrier, inc=1, device_id={"dp": peer}, device_id_type=MESH)
        return self.deep

    def cut(self, k):
        height = self.halves[k].shape[0]
        return height, height // self.deep

    def over_x(self, k):
        height, _ = self.cut(k)
        away = self.total[k].at[pl.ds(pl.multiple_of((1 - self.x) * height, height), height)]
        return to_peer(away, self.arrived[k], self.x_sems[0].at[k], self.x_sems[1].at[k], self.partner)

    def over_z(self, k, off):
        _, piece = self.cut(k)
        to = lax.rem(self.z + off, self.deep)
        part = self.halves[k].at[pl.ds(pl.multiple_of(to * piece, piece), piece)]
        sems = [sem.at[k, off] for sem in self.z_sems]
        return to_peer(part, self.slots[k].at[off], *sems, to * 2 + self.x)

    def own_piece(self, k):
        height, piece = self.cut(k)
        return self.result[k].at[pl.ds(pl.multiple_of(self.x * height + self.z * piece, piece), piece)]

    def own_half(self, k):
        height, _ = self.cut(k)
        return self.result[k].at[pl.ds(pl.multiple_of(self.x * height, height), height)]

    def back_z(self, k, off):
        to = lax.rem(self.z + off, self.deep)
        sems = [sem.at[k, off] for sem in self.z_back]
        return to_peer(self.own_piece(k), self.own_piece(k), *sems, to * 2 + self.x)

    def back_x(self, k):
        return to_peer(self.own_half(k), self.own_half(k), self.x_back[0].at[k], self.x_back[1].at[k], self.partner)

    def halve(self, k):
        self.over_x(k).wait_recv()
        height, _ = self.cut(k)
        keep = self.total[k][pl.ds(pl.multiple_of(self.x * height, height), height)]
        self.halves[k][...] = add_up(keep, self.arrived[k][...]).astype(self.halves[k].dtype)

    def deepen(self, k):
        for off in range(1, self.deep):
            self.over_z(k, off).start()

    def quarter(self, k):
        for off in range(1, self.deep):
            self.over_z(k, off).wait_recv()
        _, piece = self.cut(k)
        keep = self.halves[k][pl.ds(pl.multiple_of(self.z * piece, piece), piece)]
        total = add_up(keep, *[self.slots[k][off] for off in range(1, self.deep)])
        self.own_piece(k)[...] = total.astype(self.result[k].dtype)
        for off in range(1, self.deep):
            self.back_z(k, off).start()

    def widen(self, k):
        for off in range(1, self.deep):
            self.back_z(k, off).wait_recv()
        self.back_x(k).start()

    def finish(self, k, halved=True):
        if halved:
            self.over_x(k).wait_send()
        for off in range(1, self.deep):
            self.over_z(k, off).wait_send()
            self.back_z(k, off).wait_send()
        self.back_x(k).wait()

    @staticmethod
    def semaphores(dp, count):
        one, many = pltpu.SemaphoreType.DMA((count,)), pltpu.SemaphoreType.DMA((count, dp // 2))
        return [one, one, many, many, many, many, one, one]


def blocks(ref):
    return [ref.at[k] for k in range(ref.shape[0])]


class Closing:
    lines = 64

    def __init__(self, row, dp, units_ref, attn_ref, lines_ref, given, results, refs):
        self.row, self.lines_ref = row, lines_ref
        self.full, shard, small, above = results
        core_in, y_out, y_in = refs[:3]
        mine, x_in, half, z_in, self.s_core, self.s_one, self.s_y, self.s_mine, s_x, s_half, s_z = refs[7:18]
        x_above, half_above, z_above = refs[18:21]
        refs_sems, refs = refs[3:7], refs[21:]
        self.mine = mine
        self.sums = RowSum(row, blocks(units_ref) + [attn_ref], core_in, y_out, y_in, blocks(mine), refs_sems)
        self.gather = RowGather(
            row, [mine.at[k] for k in range(2)], blocks(self.full), row.place, row.place_across, refs[:6]
        )
        self.s_pair = to_row(lines_ref, self.s_core, refs[6:8], 0, row.sibling)
        self.s_cross = to_row(self.s_one, self.s_y, refs[8:10], 0, row.across)
        self.here = DeepSum(
            dp, blocks(mine) + [self.s_mine], blocks(x_in) + [s_x], blocks(half) + [s_half], blocks(z_in) + [s_z],
            blocks(shard) + [small], refs[10:18],
        )
        self.above = DeepSum(
            dp, [None, *given[1:]], [None] + blocks(x_above), [given[0]] + blocks(half_above), blocks(z_above), blocks(above),
            refs[18:26],
        )

    def enter(self):
        barrier = self.row.greet()
        pl.semaphore_wait(barrier, 2 + self.here.greet(barrier))
        for k in range(2):
            self.sums.start(k)
        self.above.deepen(0)
        for k in (1, 2):
            self.above.over_x(k).start()

    def early(self):
        for k in range(2):
            self.sums.middle(k)
        for k in (1, 2):
            self.above.halve(k)
            self.above.deepen(k)
        self.above.quarter(0)

    def take(self, k):
        self.sums.end(k)
        self.here.over_x(k).start()
        if k == 0:
            self.above.widen(0)
            for j in (1, 2):
                self.above.quarter(j)
        else:
            for j in (1, 2):
                self.above.widen(j)

    def open(self):
        self.sums.start(2)
        for k in range(2):
            self.here.halve(k)
            self.here.deepen(k)

    def attend(self):
        self.sums.middle(2)
        for k in range(2):
            self.gather.start(k)
            self.full[k, self.row.place] = self.mine[k]
        for k in range(2):
            self.here.quarter(k)

    def finish(self):
        here = self.here
        self.s_pair.start()
        self.sums.end(2)
        here.over_x(2).start()
        self.s_pair.wait_recv()
        self.s_one[...] = self.lines_ref[...] + self.s_core[...]
        self.s_cross.start()
        for k in range(2):
            here.widen(k)
        here.halve(2)
        here.deepen(2)
        self.s_cross.wait_recv()
        self.s_mine[...] = self.s_one[...] + self.s_y[...]
        here.over_x(3).start()
        here.quarter(2)
        here.halve(3)
        here.deepen(3)
        self.gather.forward(0)
        here.widen(2)
        here.quarter(3)
        self.gather.forward(1)
        here.widen(3)
        self.s_pair.wait_send()
        self.s_cross.wait_send()
        for k in range(3):
            self.sums.finish(k)
            self.above.finish(k, k > 0)
        for k in range(2):
            self.gather.arrive(k)
            self.gather.sent(k)
        for k in range(4):
            here.finish(k)

    @classmethod
    def scratch(cls, dp, width):
        deep = dp // 2
        lines = cls.lines
        flat, half_flat = pltpu.VMEM((lines, width), f32), pltpu.VMEM((lines // 2, width), f32)
        half, slots = (width // 2, width), (3, deep, width // dp, width)
        return (
            RowSum.scratch(3, width)
            + [
                pltpu.VMEM((3, width, width), bf16),
                pltpu.VMEM((3, *half), bf16),
                pltpu.VMEM((3, *half), bf16),
                pltpu.VMEM(slots, bf16),
                flat, flat, flat, flat, half_flat, half_flat,
                pltpu.VMEM((deep, lines // dp, width), f32),
                pltpu.VMEM((2, *half), bf16),
                pltpu.VMEM((2, *half), bf16),
                pltpu.VMEM(slots, bf16),
            ]
            + RowGather.scratch(2)
            + [pltpu.SemaphoreType.DMA((1,))] * 4
            + DeepSum.semaphores(dp, 4)
            + DeepSum.semaphores(dp, 3)
        )


def format_kernel(columns, *refs):
    layers = len(refs[:-6]) // 3
    qkv_out, proj_out, core_up_out, core_down_out, up_out, down_out = refs[-6:]

    def form(ups, downs, shard):
        mp, rows = downs.shape[1], downs.shape[2]
        up_out[0, 0] = ups[0, 0].astype(f32)
        down_out[0, 0] = jnp.concatenate(
            [downs[0, q % 2 * (mp // 2) + q // 2].astype(f32) for q in range(mp)], 0
        ).T
        core_down_out[0] = shard[1, pl.ds(pl.multiple_of(pl.program_id(1) * rows, rows), rows)].astype(f32)

        @pl.when(pl.program_id(1) == 0)
        def _():
            qkv_out[0] = shard[2, :columns].astype(f32)
            proj_out[0] = shard[2, columns:].astype(f32)
            core_up_out[0] = shard[0].astype(f32)

    for layer in range(layers):
        pl.when(pl.program_id(0) == layer)(functools.partial(form, *refs[3 * layer : 3 * layer + 3]))


def format_call(fulls, shards, columns):
    layers = len(fulls)
    _, mp, width, _ = fulls[0].shape
    hidden, rows = mp * width, width // mp
    outs = [
        ((layers, columns, width), None),
        ((layers, width - columns, width), None),
        ((layers, width, width), None),
        ((layers, rows, hidden), pl.BlockSpec((1, rows, width), lambda i, j: (i, 0, j))),
        ((layers, 1, width, hidden), pl.BlockSpec((1, 1, width, width), lambda i, j: (i, 0, 0, j))),
        ((layers, 1, hidden, width), pl.BlockSpec((1, 1, width, width), lambda i, j: (i, 0, j, 0))),
    ]

    def by_layer(shape):
        return pl.BlockSpec((1, *shape[1:]), lambda i, j: (i, 0, 0))

    def chunk(layer, i, j):
        return jnp.where(i == layer, j, jnp.where(i < layer, 0, mp - 1))

    def place(q):
        return lax.rem(q, 2) * (mp // 2) + lax.div(q, 2)

    specs, arrays = [], []
    for layer in range(layers):
        specs += [
            pl.BlockSpec((1, 1, width, width), lambda i, j, at=layer: (0, place(chunk(at, i, j)), 0, 0)),
            pl.BlockSpec((1, mp, rows, width), lambda i, j, at=layer: (1, 0, chunk(at, i, j), 0)),
            pl.BlockSpec((3, width, width), lambda i, j: (0, 0, 0)),
        ]
        arrays += [fulls[layer], fulls[layer], shards[layer]]
    return pl.pallas_call(
        functools.partial(format_kernel, columns),
        grid=(layers, mp),
        out_shape=[jax.ShapeDtypeStruct(shape, f32) for shape, _ in outs],
        in_specs=specs,
        out_specs=[spec or by_layer(shape) for shape, spec in outs],
        compiler_params=pltpu.CompilerParams(vmem_limit_bytes=40 * MIB),
        name="format",
    )(*arrays)


def greet(dp, me, rows=()):
    barrier = pltpu.get_barrier_semaphore()
    for row in rows:
        pl.semaphore_signal(barrier, inc=1, device_id={"mp": row}, device_id_type=MESH)

    def signal(off, carry):
        pl.semaphore_signal(barrier, inc=1, device_id={"dp": lax.rem(me + off, dp)}, device_id_type=MESH)
        return carry

    lax.fori_loop(1, dp, signal, 0)
    pl.semaphore_wait(barrier, dp - 1 + len(rows))


def to_peer(source, target, send_sem, recv_sem, peer):
    return pltpu.make_async_remote_copy(
        src_ref=source,
        dst_ref=target,
        send_sem=send_sem,
        recv_sem=recv_sem,
        device_id={"dp": peer},
        device_id_type=MESH,
    )


def gelu_parts(h):
    root = np.float32(np.sqrt(2.0 / np.pi))
    square = h * h
    t = jnp.tanh(root * h * (1.0 + 0.044715 * square))
    half = 0.5 * (1.0 + t)
    slope = half + 0.5 * h * (1.0 - t * t) * root * (1.0 + 3 * 0.044715 * square)
    return h * half, slope


def expert_forward_kernel(dp, mp, layer, gather, *refs):
    refs = list(refs)
    buffer_ref, up_any, down_any, rup_any, rdown_any = refs[:5]
    refs = refs[5:]
    if gather:
        shards = [ref.at[layer + 1] for ref in refs[:4]]
        refs = refs[4:]
    recv_ref, returned_ref, up_eff, down_eff = refs[:4]
    refs = refs[4:]
    if gather:
        fulls = refs[:4]
        refs = refs[4:]
    part, core, up_ref, down_ref, rup_ref, rdown_ref, local = refs[:7]
    refs = refs[7:]
    moving = WeightGather(shards, fulls, refs[:7]) if gather else None
    send_one, recv_one, send_two, recv_two = refs[-4:]
    split = dp // EXPERTS
    me = lax.axis_index("dp")
    loads = [
        pltpu.make_async_copy(source, target, local.at[k])
        for k, (source, target) in enumerate(
            [
                (up_any, up_ref),
                (rup_any.at[layer, 0], rup_ref),
                (down_any, down_ref),
                (rdown_any.at[layer, 0], rdown_ref),
            ]
        )
    ]
    for load in loads:
        load.start()
    greet(dp, me, (moving.row.sibling, moving.row.across) if gather else ())

    def first(off):
        peer = lax.rem(me + off, dp)
        return to_peer(
            buffer_ref.at[lax.div(peer, split)], recv_ref.at[me], send_one.at[off], recv_one.at[off], peer
        )

    def second(off):
        source = lax.rem(me + dp - off, dp)
        return to_peer(part.at[source], returned_ref.at[me], send_two.at[off], recv_two.at[off], source)

    def start_first(off, carry):
        first(off).start()
        return carry

    lax.fori_loop(1, dp, start_first, 0)
    if gather:
        for k in range(4):
            moving.start(k)
    recv_ref[me] = buffer_ref[lax.div(me, split)]
    hidden = up_eff.shape[1]
    columns = up_ref.shape[-1]
    loads[0].wait()
    loads[1].wait()
    if split == 1 and columns % LANES == 0:
        for m in range(mp):
            at = slice(m * columns, (m + 1) * columns)
            up_eff[:, at] = (up_ref[m].astype(f32) + rup_ref[:, at].astype(f32)).astype(bf16)
    else:
        core[...] = rup_ref[...].astype(f32)
        begin = lax.rem(me, split) * hidden
        for m in range(mp):
            put = onehot(iota((columns, hidden), 0) + m * columns == iota((columns, hidden), 1) + begin)
            core[...] += nn(up_ref[m], put)
        up_eff[...] = core[...].astype(bf16)
    begin = pl.multiple_of(lax.rem(me, split) * hidden, LANES)
    loads[2].wait()
    loads[3].wait()
    core_part = down_ref[:, :, pl.ds(begin, hidden)].reshape(down_eff.shape[1], hidden)
    down_eff[...] = (core_part.astype(f32).T + rdown_ref[...].astype(f32)).astype(bf16)

    def work(source):
        hidden_pre = nn(recv_ref[source], up_eff[...])
        hidden_low = gelu_parts(hidden_pre)[0].astype(bf16)
        return nn(hidden_low, down_eff[...]).astype(bf16)

    returned_ref[me] = work(me)

    def step(off, carry):
        source = lax.rem(me + dp - off, dp)
        first(off).wait_recv()
        part[source] = work(source)
        second(off).start()
        return carry

    lax.fori_loop(1, dp, step, 0)
    if gather:
        for k in range(4):
            moving.forward(k)

    def finish(off, carry):
        first(off).wait_send()
        second(off).wait()
        return carry

    lax.fori_loop(1, dp, finish, 0)
    if gather:
        for k in range(4):
            moving.arrive(k)
            moving.sent(k)


def expert_backward_kernel(dp, mp, fast, reduce, *refs):
    refs = list(refs)
    buffer_ref, recv_ref, up_ref, down_ref = refs[:4]
    refs = refs[4:]
    if reduce:
        given_ref, attn_ref = refs[:2]
        refs = refs[2:]
    returned_ref = refs.pop(0)
    if fast:
        units_ref = refs.pop(0)
    else:
        up_term, down_term = refs[:2]
        refs = refs[2:]
    if reduce:
        full_ref, mine_ref = refs[:2]
        refs = refs[2:]
    grads, hidden_low, slope, pre, part = refs[:5]
    refs = refs[5:]
    if fast:
        up_term, down_term = refs[:2]
        refs = refs[2:]
    row = Row() if reduce else None
    if reduce:
        core_in, y_out, y_in = refs[:3]
        sums = RowSum(row, [attn_ref], core_in, y_out, y_in, [mine_ref], refs[3:7])
        gather = RowGather(
            row, [given_ref.at[k] for k in range(2)], [full_ref.at[k] for k in range(2)], row.place, row.place_across,
            refs[7:13],
        )
        refs = refs[13:]
    send_one, recv_one, send_two, recv_two = refs
    split = dp // EXPERTS
    me = lax.axis_index("dp")
    greet(dp, me, (row.sibling, row.across) if reduce else ())

    def first(off):
        peer = lax.rem(me + off, dp)
        return to_peer(buffer_ref.at[lax.div(peer, split)], grads.at[me], send_one.at[off], recv_one.at[off], peer)

    def second(off):
        source = lax.rem(me + dp - off, dp)
        return to_peer(part.at[source], returned_ref.at[me], send_two.at[off], recv_two.at[off], source)

    def start_first(off, carry):
        first(off).start()
        return carry

    lax.fori_loop(1, dp, start_first, 0)
    if reduce:
        sums.start(0)
        for k in range(2):
            gather.start(k)
    grads[me] = buffer_ref[lax.div(me, split)]

    def again(source, carry):
        value, rate = gelu_parts(nn(recv_ref[source], up_ref[...]))
        hidden_low[source] = value.astype(bf16)
        slope[source] = rate
        return carry

    lax.fori_loop(0, dp, again, 0)
    if reduce:
        sums.middle(0)
        for k in range(2):
            full_ref[k, row.place] = given_ref[k]

    def work(source):
        hidden_grad = nt(grads[source], down_ref[...])
        pre_grad = (slope[source] * hidden_grad).astype(bf16)
        pre[source] = pre_grad
        return nt(pre_grad, up_ref[...]).astype(bf16)

    returned_ref[me] = work(me)

    def step(off, carry):
        source = lax.rem(me + dp - off, dp)
        first(off).wait_recv()
        part[source] = work(source)
        second(off).start()
        return carry

    lax.fori_loop(1, dp, step, 0)
    if reduce:
        for k in range(2):
            gather.forward(k)
        sums.end(0)
    up_term[...] = jnp.zeros(up_term.shape, f32)
    down_term[...] = jnp.zeros(down_term.shape, f32)

    def terms(block, carry):
        up_term[...] += tn(recv_ref[block], pre[block])
        down_term[...] += tn(grads[block], hidden_low[block])
        return carry

    lax.fori_loop(0, dp, terms, 0)
    if fast:
        width = up_term.shape[0]
        height = width // mp
        for place in range(mp):
            q = quarter_at(place, mp)
            units_ref[0, place] = up_term[:, q * width : (q + 1) * width].astype(bf16)
            for chunk in range(mp):
                block = down_term[q * height : (q + 1) * height, chunk * width : (chunk + 1) * width]
                units_ref[1, place, chunk * height : (chunk + 1) * height] = block.astype(bf16)

    def finish(off, carry):
        first(off).wait_send()
        second(off).wait()
        return carry

    lax.fori_loop(1, dp, finish, 0)
    if reduce:
        sums.finish(0)
        for k in range(2):
            gather.arrive(k)
            gather.sent(k)


def expert_call(kernel, arrays, outs, scratch, dp, collective_id, name, flops, anys=(), any_outs=()):
    sems = [pltpu.SemaphoreType.DMA((dp,))] * 4
    vmem, anywhere = pl.BlockSpec(memory_space=pltpu.VMEM), pl.BlockSpec(memory_space=pl.ANY)
    return pl.pallas_call(
        kernel,
        out_shape=[jax.ShapeDtypeStruct(shape, dtype) for shape, dtype in (*outs, *any_outs)],
        in_specs=[vmem] * len(arrays) + [anywhere] * len(anys),
        out_specs=[vmem] * len(outs) + [anywhere] * len(any_outs),
        scratch_shapes=scratch + sems,
        compiler_params=pltpu.CompilerParams(
            vmem_limit_bytes=56 * MIB, collective_id=collective_id, has_side_effects=True
        ),
        cost_estimate=pl.CostEstimate(flops=flops, bytes_accessed=20 * MIB, transcendentals=0),
        name=name,
    )(*arrays, *anys)


def by_windows(grid):
    images, kinds = grid.shape[:2]
    blocks = GRID // WINDOW
    grid = grid.reshape(images, kinds, blocks, WINDOW, blocks, WINDOW).transpose(0, 1, 2, 4, 3, 5)
    grid = grid.reshape(images, kinds, blocks * blocks, WINPOS)
    grid = jnp.pad(grid, ((0, 0), (0, 0), (0, 0), (0, WPAD - WINPOS)), constant_values=-1)
    return grid.reshape(images, kinds, IMGROWS)


def per_device(
    patches,
    qkv_weight,
    proj_weight,
    core_up,
    core_down,
    residual_up,
    residual_down,
    position_bias,
    router_weight,
    norm_gain,
    norm_bias,
    cotangent,
    image_valid,
    expert_index,
    slot_index,
    region_id,
):
    dp, mp = lax.axis_size("dp"), lax.axis_size("mp")
    images, _, width = patches.shape
    split = dp // EXPERTS
    hidden = residual_up.shape[-1]
    hidden_full = core_up.shape[-1] * mp
    row_index = lax.axis_index("mp")

    fast = split == 1 and dp == 8 and mp == 4 and hidden == mp * width
    qkv_rows, proj_rows, down_rows = (a.transpose(0, 2, 1) for a in (qkv_weight, proj_weight, core_down))
    shards = (qkv_rows, proj_rows, core_up, down_rows)
    gathered = [[None] * len(shards)] * LAYERS
    if not fast:
        gathered = [[lax.all_gather(a[l], "mp", axis=0, tiled=False) for a in shards] for l in range(LAYERS)]

    position = jnp.where(slot_index >= 0, expert_index * SLOTS + slot_index, -1)
    row_form = by_windows(jnp.stack([position.reshape(images, GRID, GRID), region_id], 1))
    col_form = row_form.transpose(0, 2, 1)
    enter = jnp.asarray(enter_table(), bf16)
    leave = jnp.asarray(enter_table().T, bf16)
    moves = [jnp.asarray(move_table(l % 2 == 1), bf16) for l in range(LAYERS)]
    backs = [jnp.asarray(move_table(l % 2 == 1).T, bf16) for l in range(LAYERS)]
    table_rows = position_bias.transpose(0, 2, 1).reshape(LAYERS * HEADS, OFFSETS)
    table_rows = jnp.pad(table_rows, ((0, 0), (0, TABLE - OFFSETS)))
    entry_row, entry_col = jnp.asarray(cell_entries()[None, :]), jnp.asarray(cell_entries()[:, None])
    routers = jnp.pad(router_weight.transpose(0, 2, 1), ((0, 0), (0, LANES - EXPERTS), (0, 0)))

    token = (images, IMGROWS, width)
    buffer_shape = (ROWS, width)
    block_rows = (dp, SLOTS, width)
    pieces = (split, ROWS, width)

    def by_piece(returned):
        return returned.reshape(EXPERTS, split, SLOTS, width).transpose(1, 0, 2, 3).reshape(pieces)

    records = []
    before = None
    for l in range(LAYERS):
        first = l == 0
        gather = fast and first
        if first:
            arrays = [("image", patches), ("whole", enter)]
        else:
            arrays = [("image", before[0]), ("image", before[1]), ("whole", before[2])]
        arrays += [
            ("smem", image_valid),
            ("image", col_form),
            ("image", row_form),
            ("any", qkv_rows) if gather else ("whole", gathered[l][0]),
            ("any", proj_rows) if gather else ("whole", gathered[l][1]),
            ("whole", table_rows) if first else (l, biases),
            ("whole", moves[l]),
            ("whole", backs[l]),
            (l, norm_gain),
            (l, norm_bias),
            (l, routers),
        ]
        if first:
            arrays.append(("whole", entry_row))
        if gather:
            arrays += [("any", core_up), ("any", down_rows)]
        outs = [("image", token, f32)]
        if first:
            outs.append(("whole", (LAYERS, HEADS, WPAD, LANES), f32))
        else:
            outs.append(("image", token, f32))
        outs += [
            ("image", token, f32),
            ("image", token, bf16),
            ("image", (images, IMGROWS, 1), f32),
            ("whole", buffer_shape, bf16),
            ("image", token, bf16),
            ("image", (images, 2 * width, IMGROWS), bf16),
            ("image", token, bf16),
            ("image", (images, PAIRS * HEADS, WPAD, LANES), bf16),
            ("image", (images, width, IMGROWS), bf16),
            ("whole", (width, width), bf16),
        ]
        scratch = [pltpu.VMEM(buffer_shape, f32)]
        gathered_shapes = [(mp, *a.shape[1:]) for a in shards]
        if gather:
            outs.append(("whole", (3 * width, width), bf16))
            outs += [("any", shape, bf16) for shape in gathered_shapes[2:]]
            scratch += [pltpu.VMEM(shape, bf16) for shape in gathered_shapes[:2]] + WeightGather.scratch(4)
        results = list(
            image_call(
                functools.partial(attention_forward_kernel, first, l % 2 == 1, mp, gather),
                images, arrays, outs, scratch, f"attend_{l}", 3 * LAYERS + 1 if gather else None,
            )
        )
        if gather:
            gathered[l] = [results[-3], None] + results[-2:]
            results = results[:-3]
        carried = results.pop(0)
        if first:
            biases = results.pop(0)
        else:
            records[-1]["expert_out"] = results.pop(0)
        middle, second_low, gate, buffer = results[:4]
        gather = fast and l < LAYERS - 1
        received, returned, up_eff, down_eff, *more = expert_call(
            functools.partial(expert_forward_kernel, dp, mp, l, gather),
            [buffer.reshape(EXPERTS, SLOTS, width)],
            [
                (block_rows, bf16),
                (block_rows, bf16),
                ((width, hidden), bf16),
                ((hidden, width), bf16),
            ],
            [
                pltpu.VMEM(block_rows, bf16),
                pltpu.VMEM((8, LANES) if fast else (width, hidden), f32),
                pltpu.VMEM(gathered_shapes[2], bf16),
                pltpu.VMEM(gathered_shapes[3], bf16),
                pltpu.VMEM((width, hidden), bf16),
                pltpu.VMEM((hidden, width), bf16),
                pltpu.SemaphoreType.DMA((4,)),
            ]
            + (WeightGather.scratch(4) if gather else []),
            dp, l, f"experts_{l}", 4 * dp * SLOTS * width * hidden,
            [gathered[l][2], gathered[l][3], residual_up, residual_down, *(shards if gather else ())],
            [(shape, bf16) for shape in gathered_shapes] if gather else (),
        )
        if gather:
            gathered[l + 1] = more
        returned = by_piece(returned)
        before = (middle, gate, returned)
        records.append(
            dict(
                carried=carried, middle=middle, second_low=second_low, gate=gate, saved=results[4:], received=received,
                up_eff=up_eff, down_eff=down_eff,
            )
        )

    top = records[-1]
    block_output, grad, logit_grad, router_part, buffer = image_call(
        turn_kernel,
        images,
        [
            ("image", before[0]),
            ("image", before[1]),
            ("whole", before[2]),
            ("image", cotangent),
            ("whole", enter),
            ("whole", leave),
            ("image", col_form),
            ("image", row_form),
            ("image", top["second_low"]),
            (LAYERS - 1, routers),
        ],
        [
            ("image", patches.shape, bf16),
            ("image", token, f32),
            ("image", (images, IMGROWS, LANES), f32),
            ("whole", (LANES, width), f32),
            ("whole", buffer_shape, bf16),
        ],
        [pltpu.VMEM(buffer_shape, f32)],
        "turn",
    )
    router_parts, tables, smalls = [None] * LAYERS, [None] * LAYERS, [None] * LAYERS
    residual_sums, shard_sums = [None] * LAYERS, [None] * LAYERS
    router_parts[LAYERS - 1] = router_part
    units, attn_units, mines = [None] * LAYERS, [None] * LAYERS, [None] * LAYERS
    for l in reversed(range(LAYERS)):
        rec = records[l]
        last = l == 0
        reduce = fast and l < LAYERS - 1
        arrays = [buffer.reshape(EXPERTS, SLOTS, width), rec["received"], rec["up_eff"], rec["down_eff"]]
        outs = [(block_rows, bf16)]
        scratch = [
            pltpu.VMEM(block_rows, bf16),
            pltpu.VMEM((dp, SLOTS, hidden), bf16),
            pltpu.VMEM((dp, SLOTS, hidden), f32),
            pltpu.VMEM((dp, SLOTS, hidden), bf16),
            pltpu.VMEM(block_rows, bf16),
        ]
        if fast:
            outs.append(((2, mp, width, width), bf16))
            scratch += [pltpu.VMEM((width, hidden), f32)] * 2
        else:
            outs += [((width, hidden), f32)] * 2
        if reduce:
            arrays += [mines[l + 1], attn_units[l + 1]]
            outs += [((2, mp, width, width), bf16), ((width, width), bf16)]
            scratch += RowSum.scratch(1, width) + RowGather.scratch(2)
        results = list(
            expert_call(
                functools.partial(expert_backward_kernel, dp, mp, fast, reduce), arrays, outs, scratch, dp, LAYERS + l,
                f"experts_back_{l}", 10 * dp * SLOTS * width * hidden,
            )
        )
        returned_grad = results.pop(0)
        if fast:
            units[l] = results.pop(0)
        else:
            residual_sums[l] = lax.psum(tuple(t.astype(bf16) for t in results[:2]), "mp")
        if reduce:
            full_above, mine_above = results
        window_in, qk, v, probs, att, proj_full = rec["saved"]
        qkv_full = gathered[l][0].reshape(3 * width, width)
        arrays = [
            ("smem", image_valid),
            ("image", grad),
            ("whole", by_piece(returned_grad)),
            ("image", logit_grad),
            ("image", rec["middle"]),
            ("image", rec["carried"]),
            (l, routers),
            ("image", col_form),
            ("whole", moves[l]),
            ("whole", backs[l]),
            (l, norm_gain),
            ("whole", proj_full),
            ("whole", qkv_full),
            ("image", window_in),
            ("image", qk),
            ("image", v),
            ("image", probs),
            ("image", att),
        ]
        outs = [("image", patches.shape if last else token, f32)]
        scratch = [pltpu.VMEM((3 * width, (2 - images % 2) * IMGROWS), bf16)]
        closes = fast and last
        table_shape, small_shape = (HEADS, WPAD, LANES), (8, width)
        if fast:
            arrays.append(("whole", units[l]))
            scratch += [pltpu.VMEM((3 * width, width), f32), pltpu.VMEM((width, width), f32)]
        if closes:
            outs += [
                ("whole", (2, mp, width, width), bf16),
                ("whole", (3, width, width), bf16),
                ("whole", (Closing.lines, width), f32),
                ("whole", (3, width, width), bf16),
            ]
        else:
            if fast:
                outs += [
                    ("whole", (width // 2, width), bf16),
                    ("whole", (mp, width, width), bf16),
                    ("whole", (2, width, width), bf16),
                ]
            else:
                outs += [("whole", (3 * width, width), f32), ("whole", (width, width), f32)]
            outs += [("whole", table_shape, f32), ("whole", small_shape, f32)]
        if last:
            arrays.append(("whole", leave))
            if fast:
                arrays += [
                    ("whole", a)
                    for a in (
                        tables[1], smalls[1], router_parts[1], router_parts[0], entry_col, halves_above, mines[1],
                        mine_above,
                    )
                ]
        else:
            below = records[l - 1]
            arrays += [
                ("image", row_form),
                ("image", below["expert_out"]),
                ("image", below["second_low"]),
                (l - 1, routers),
            ]
            outs += [
                ("image", (images, IMGROWS, LANES), f32),
                ("whole", (LANES, width), f32),
                ("whole", buffer_shape, bf16),
            ]
            scratch.append(pltpu.VMEM(buffer_shape, f32))
        if closes:
            scratch += [
                pltpu.VMEM(table_shape, f32),
                pltpu.VMEM(small_shape, f32),
                pltpu.VMEM((mp, width, width), bf16),
                pltpu.VMEM((Closing.lines, width), f32),
            ]
            scratch += [pltpu.VMEM(shape, dtype) for _, shape, dtype in outs[1:5]] + Closing.scratch(dp, width)
        elif fast:
            scratch += RowSum.scratch(2, width) + [pltpu.VMEM((width // 2, width), bf16)]
            scratch += [pltpu.SemaphoreType.DMA((1,))] * 2
        results = list(
            image_call(
                functools.partial(attention_backward_kernel, last, dp, mp, fast),
                images, arrays, outs, scratch, f"attend_back_{l}", 2 * LAYERS + 1 + l if fast else None,
            )
        )
        grad = results.pop(0)
        if closes:
            full, closed, lines, shard_above = results
            continue
        if fast:
            halves_above = results.pop(0)
            attn_units[l], mines[l] = results[:2]
        else:
            qkv_part, proj_part = results[:2]
        tables[l], smalls[l] = results[2:4]
        if not last:
            logit_grad, router_parts[l - 1], buffer = results[4:]
        if fast:
            continue
        attn = (
            lax.psum_scatter(qkv_part.astype(bf16), "mp", scatter_dimension=0, tiled=True),
            lax.psum_scatter(proj_part.T.astype(bf16), "mp", scatter_dimension=0, tiled=True),
        )
        up_sum, down_sum = residual_sums[l]
        if split > 1:
            begin = lax.axis_index("dp") % split * hidden
            empty = jnp.zeros((width, hidden_full), bf16)
            up_sum = lax.dynamic_update_slice_in_dim(empty, up_sum, begin, 1)
            down_sum = lax.dynamic_update_slice_in_dim(empty, down_sum, begin, 1)
        up_columns, down_columns = core_up.shape[-1], core_down.shape[-1]
        up_shard = lax.dynamic_slice_in_dim(up_sum, row_index * up_columns, up_columns, 1)
        down_shard = lax.dynamic_slice_in_dim(down_sum, row_index * down_columns, down_columns, 0)
        shard_sums[l] = lax.psum((attn[0], attn[1], up_shard, down_shard), "dp")

    if fast:
        *attn_grads, core_up_grad, core_down_grad, residual_up_grad, residual_down_grad = format_call(
            [full, full_above], [closed, shard_above], qkv_weight.shape[-1]
        )
        attn_grads = [a.transpose(0, 2, 1) for a in attn_grads]
        core_grads = (core_up_grad, core_down_grad.transpose(0, 2, 1))
        at = LAYERS * HEADS
        table_sum = lines[:at, :OFFSETS]
        router_sum = lines[at : at + LAYERS * EXPERTS].reshape(LAYERS, EXPERTS, width)
        at += LAYERS * EXPERTS
        small_sum = lines[at : at + LAYERS * 8].reshape(LAYERS, 8, width)[:, :4]
    else:
        entry = cell_entries()[None, :] + np.array([key_base_of(key) for key in range(WPAD)])[:, None]
        entry = jnp.asarray(np.where(np.arange(WPAD)[:, None] < WINPOS, entry, -1).reshape(-1))
        entry_turned = (entry[:, None] == jnp.arange(OFFSETS)[None, :]).astype(f32)
        table_part = jnp.dot(
            jnp.stack(tables, 0).reshape(LAYERS * HEADS, WPAD * LANES), entry_turned, precision=highest
        )
        small_part = jnp.stack(smalls, 0)[:, :4]
        router_part = jnp.stack(router_parts, 0)[:, :EXPERTS]
        table_sum, small_sum, router_sum = lax.psum((table_part, small_part, router_part), ("dp", "mp"))

        def shard(k):
            return jnp.stack([shard_sums[l][k] for l in range(LAYERS)], 0).astype(f32)

        attn_grads = (shard(0).transpose(0, 2, 1), shard(1).transpose(0, 2, 1))
        core_grads = (shard(2), shard(3).transpose(0, 2, 1))
        residual_up_grad, residual_down_grad = (
            jnp.stack([residual_sums[l][k] for l in range(LAYERS)], 0).astype(f32) for k in range(2)
        )
        residual_up_grad = residual_up_grad[:, None]
        residual_down_grad = residual_down_grad.transpose(0, 2, 1)[:, None]

    return (
        block_output,
        grad,
        attn_grads[0],
        attn_grads[1],
        core_grads[0],
        core_grads[1],
        residual_up_grad,
        residual_down_grad,
        table_sum.reshape(LAYERS, HEADS, OFFSETS).transpose(0, 2, 1),
        router_sum.transpose(0, 2, 1),
        small_sum[:, 0:2],
        small_sum[:, 2:4],
    )


def solution(mesh):
    placed = (
        P(("dp", "mp"), None, None),
        P(None, None, "mp"),
        P(None, None, "mp"),
        P(None, None, "mp"),
        P(None, None, "mp"),
        P(None, "dp", None, None),
        P(None, "dp", None, None),
        P(),
        P(),
        P(),
        P(),
        P(("dp", "mp"), None, None),
        P(("dp", "mp")),
        P(("dp", "mp"), None),
        P(("dp", "mp"), None),
        P(("dp", "mp"), None, None),
    )
    return jax.shard_map(
        per_device,
        mesh=mesh,
        in_specs=placed,
        out_specs=(
            P(("dp", "mp"), None, None),
            P(("dp", "mp"), None, None),
            P(None, None, "mp"),
            P(None, None, "mp"),
            P(None, None, "mp"),
            P(None, None, "mp"),
            P(None, "dp", None, None),
            P(None, "dp", None, None),
            P(),
            P(),
            P(),
            P(),
        ),
        check_vma=False,
    )
```

```python
import functools

import jax
import jax.numpy as jnp
import numpy as np
from jax import lax
from jax.experimental import pallas as pl
from jax.experimental.pallas import tpu as pltpu
from jax.sharding import PartitionSpec as P

HEADS = 12
HEAD_DIM = 32
EXPERTS = 8
WINDOW = 7
GRID = 14
SHIFT = 3
LAYERS = 2
WINPOS = 49
OFFSETS = 169
CAP = 122

WPAD = 64
IMGROWS = 256
PATCHES = 196
SLOTS = 128
ROWS = EXPERTS * SLOTS
LANES = 128
GROUP = 4
PAIRS = 2
TABLE = 256

bf16 = jnp.bfloat16
f32 = jnp.float32
highest = lax.Precision.HIGHEST
norm_epsilon = 1e-05
mask_fill = -100.0
head_scale = HEAD_DIM ** (-0.5)
MESH = pl.DeviceIdType.MESH
MIB = 1024 * 1024


def nn(a, b):
    return lax.dot_general(a, b, (((1,), (0,)), ((), ())), preferred_element_type=f32)


def nt(a, b):
    return lax.dot_general(a, b, (((1,), (1,)), ((), ())), preferred_element_type=f32)


def tn(a, b):
    return lax.dot_general(a, b, (((0,), (0,)), ((), ())), preferred_element_type=f32)


def iota(shape, dim):
    return lax.broadcasted_iota(jnp.int32, shape, dim)


def onehot(flags):
    return jnp.where(flags, 1.0, 0.0).astype(bf16)


def natural_of_row(shifted):
    moved = SHIFT if shifted else 0
    blocks = GRID // WINDOW
    out = -np.ones(IMGROWS, np.int32)
    for window in range(blocks * blocks):
        for cell in range(WINPOS):
            row = (window // blocks * WINDOW + cell // WINDOW + moved) % GRID
            col = (window % blocks * WINDOW + cell % WINDOW + moved) % GRID
            out[window * WPAD + cell] = row * GRID + col
    return out


def key_base_of(key):
    return (2 * WINDOW) * (WINDOW - 1) - (key // WINDOW * (2 * WINDOW - 1) + key % WINDOW)


def enter_table():
    held = natural_of_row(False)
    return (held[:, None] == np.arange(PATCHES)[None, :]).astype(np.float32)


def move_table(shifted):
    first, second = natural_of_row(False), natural_of_row(shifted)
    same = (second[:, None] == first[None, :]) & (second[:, None] >= 0)
    return same.astype(np.float32)


def cell_entries():
    cell = np.arange(LANES) % WPAD
    return np.where(cell < WINPOS, cell // WINDOW * (2 * WINDOW - 1) + cell % WINDOW, -4 * TABLE).astype(np.int32)


def norm_parts(x):
    width = x.shape[-1]
    center = x - jnp.sum(x, -1, keepdims=True) * (1.0 / width)
    spread = jnp.sum(center * center, -1, keepdims=True) * (1.0 / width)
    rstd = lax.rsqrt(spread + norm_epsilon)
    return center * rstd, rstd


def norm_back(grad, gain, xhat, rstd):
    width = xhat.shape[-1]
    dxhat = grad * gain
    mean_one = jnp.sum(dxhat, -1, keepdims=True) * (1.0 / width)
    mean_two = jnp.sum(dxhat * xhat, -1, keepdims=True) * (1.0 / width)
    return rstd * (dxhat - mean_one - xhat * mean_two)


def split_two(x):
    high = x.astype(bf16)
    return high, (x - high.astype(f32)).astype(bf16)


def collect(pos_col, returned_ref):
    pick = onehot(pos_col == iota((pos_col.shape[0], ROWS), 1))
    out = nn(pick, returned_ref[0])
    for piece in range(1, returned_ref.shape[0]):
        out = out + nn(pick, returned_ref[piece])
    return out


def join(ref):
    return ref[...].reshape(ref.shape[0] * ref.shape[1], *ref.shape[2:])


def store(ref, rows):
    ref[...] = rows.reshape(ref.shape).astype(ref.dtype)


def per_image(function, count):
    return jnp.concatenate([function(i) for i in range(count)], 0)


def image_rows(i):
    return slice(i * IMGROWS, (i + 1) * IMGROWS)


def lay_positions(row_ref):
    return jnp.concatenate([row_ref[i, 0:1, :] for i in range(row_ref.shape[0])], 1)


def spread_rows(pos_row, rows_low):
    return nn(onehot(iota((ROWS, pos_row.shape[1]), 0) == pos_row), rows_low)


def route(second_low, router, pos_col):
    logits = nt(second_low, router)
    lane = iota(logits.shape, 1)
    logits = jnp.where(lane < EXPERTS, logits, -1e30)
    expo = jnp.exp(logits - jnp.max(logits, -1, keepdims=True))
    probs = expo / jnp.sum(expo, -1, keepdims=True)
    expert = jnp.where(pos_col >= 0, pos_col // SLOTS, -1)
    chosen = jnp.where(lane == expert, 1.0, 0.0)
    return probs, chosen, jnp.sum(probs * chosen, -1, keepdims=True)


def head_masks():
    rows = iota((LANES, LANES), 0) // HEAD_DIM
    return [onehot(rows == h) for h in range(GROUP)]


def lane_masks():
    lane = iota((WPAD, LANES), 1)
    return [onehot(lane < WPAD), onehot(lane >= WPAD)]


def keys_entry(cells, key_row, turned):
    parts = [cells + (key_base_of(col) - key_row * (2 * WINDOW - 1)) for col in range(WINDOW)]
    return jnp.concatenate(parts, 0 if turned else 1)


def form_bias(bias_ref, table_ref, entry_row):
    layers, heads = bias_ref.shape[:2]
    lines = layers * heads
    bias_ref[...] = jnp.where(iota(bias_ref.shape, 2) < WINPOS, 0.0, -1e30)
    table = table_ref[...]
    high = table.astype(bf16)
    mid, low = split_two(table - high.astype(f32))
    parts = jnp.concatenate([high.astype(f32), mid.astype(f32), low.astype(f32)], 0).astype(bf16)

    def step(key_row, carry):
        pick = onehot(iota((TABLE, WINDOW * LANES), 0) == keys_entry(entry_row, key_row, False))
        rows = nn(parts, pick)
        rows = rows[:lines] + rows[lines : 2 * lines] + rows[2 * lines :]
        for col in range(WINDOW):
            for layer in range(layers):
                part = rows[layer * heads : (layer + 1) * heads, col * LANES : (col + 1) * LANES]
                bias_ref[layer, :, pl.ds(key_row * WINDOW + col, 1), :] = part.reshape(heads, 1, LANES)
        return carry

    lax.fori_loop(0, WINDOW, step, 0)


def table_grad(parts, entry_col):
    heads = parts[0].shape[0]
    lines = heads * len(parts)

    def step(key_row, total):
        keys = [
            jnp.concatenate([ref[:, pl.ds(key_row * WINDOW + col, 1), :].reshape(heads, LANES) for ref in parts], 0)
            for col in range(WINDOW)
        ]
        rows = jnp.concatenate(keys, 1)
        high = rows.astype(bf16).astype(f32)
        both = jnp.concatenate([high, rows - high], 0).astype(bf16)
        entry = keys_entry(entry_col, key_row, True)
        out = nn(both, onehot(iota((WINDOW * LANES, TABLE), 1) == entry))
        return total + out[:lines] + out[lines:]

    return lax.fori_loop(0, WINDOW, step, jnp.zeros((lines, TABLE), f32))


def attention_forward_kernel(first, shifted, mp, gather, *refs):
    refs = list(refs)
    if first:
        patches_ref, enter_ref = refs[:2]
        refs = refs[2:]
    else:
        prev_ref, prev_gate_ref, returned_ref = refs[:3]
        refs = refs[3:]
    (
        valid_ref, col_ref, row_ref, qkv_ref, proj_ref, bias_ref, move_ref, back_ref, gain_ref, nbias_ref, router_ref,
    ) = refs[:11]
    gain_ref, nbias_ref, router_ref = (ref.at[0] for ref in (gain_ref, nbias_ref, router_ref))
    refs = refs[11:]
    if first:
        table_ref, entry_ref = bias_ref, refs.pop(0)
    if gather:
        core_up_ref, core_down_ref = refs[:2]
        refs = refs[2:]
    carried_ref = refs.pop(0)
    if first:
        biases_ref = refs.pop(0)
        bias_ref = biases_ref.at[0]
    else:
        expert_out_ref = refs.pop(0)
        bias_ref = bias_ref.at[0]
    middle_ref, second_ref, gate_ref, buffer_ref, window_ref, qk_ref, v_ref, probs_ref, att_ref, proj_full = refs[:10]
    refs = refs[10:]
    if gather:
        qkv_full = refs.pop(0)
        up_out, down_out = refs[:2]
        refs = refs[2:]
    total_ref = refs.pop(0)
    step = pl.program_id(0)
    final = pl.num_programs(0) - 1
    count, _, width = carried_ref.shape
    if gather:
        shards = [ref.at[0] for ref in (qkv_ref, proj_ref, core_up_ref, core_down_ref)]
        qkv_ref, proj_ref = refs[:2]
        moving = WeightGather(shards, [qkv_ref, proj_ref, up_out, down_out], refs[2:])

        @pl.when(step == 0)
        def _():
            pl.semaphore_wait(moving.row.greet(), 2)
            for k in (0, 1):
                moving.start(k)
            form_bias(biases_ref, table_ref, entry_ref[...])

    pos_col = join(col_ref)[:, 0:1]
    if first:
        x = per_image(lambda i: nn(enter_ref[...], patches_ref[i]), count)
    else:
        expert_out = collect(pos_col, returned_ref)
        store(expert_out_ref, expert_out)
        x = join(prev_ref) + join(prev_gate_ref) * expert_out
    store(carried_ref, x)
    xhat, _ = norm_parts(x)
    normed = (xhat * gain_ref[0:1, :] + nbias_ref[0:1, :]).astype(bf16)
    window_in = per_image(lambda i: nn(move_ref[...], normed[image_rows(i)]), count).astype(bf16)
    store(window_ref, window_in)

    @pl.when(step == 0)
    def _():
        if gather:
            for k in (0, 1):
                moving.forward(k)
            for k in (2, 3):
                moving.start(k)
            for k in (0, 1):
                moving.arrive(k)
            qkv_full[...] = join(qkv_ref)
        elif first:
            form_bias(biases_ref, table_ref, entry_ref[...])
        proj_full[...] = join(proj_ref).astype(f32).T.astype(bf16)
        total_ref[...] = jnp.zeros(total_ref.shape, f32)

    qkv = join(qkv_ref)
    turned = nt(qkv, window_in).astype(bf16)
    straight = nt(window_in, qkv[width:]).astype(bf16)
    for i in range(count):
        qk_ref[i] = turned[: 2 * width, image_rows(i)]
    store(v_ref, straight[:, width:])
    heads_rows = head_masks()
    halves = lane_masks()
    low_lane = iota((WPAD, LANES), 1) < WPAD
    if shifted:
        row_labels = [nt(row_ref[i].astype(f32).astype(bf16), move_ref[...]) for i in range(count)]
        col_labels = [nn(move_ref[...], col_ref[i].astype(f32).astype(bf16)) for i in range(count)]
    for pair in range(PAIRS * count):
        image, side = pair // PAIRS, pair % PAIRS
        across = slice(pair * LANES, (pair + 1) * LANES)
        within = slice(side * LANES, (side + 1) * LANES)
        if shifted:
            ahead = col_labels[image][side * LANES : side * LANES + WPAD, 1:2]
            behind = col_labels[image][side * LANES + WPAD : (side + 1) * LANES, 1:2]
            key_label = jnp.where(low_lane, ahead, behind)
            mask = jnp.where(key_label == row_labels[image][1:2, within], 0.0, mask_fill)
        for group in range(HEADS // GROUP):
            features = slice(group * LANES, (group + 1) * LANES)
            queries = turned[features, across]
            spread = jnp.concatenate([queries * heads_rows[h] for h in range(GROUP)], 1)
            raw = nn(straight[across, features], spread)
            for h in range(GROUP):
                head = group * GROUP + h
                part = raw[:, h * LANES : (h + 1) * LANES]
                scores = jnp.where(low_lane, part[:WPAD], part[WPAD:]) * head_scale + bias_ref[head]
                if shifted:
                    scores = scores + mask
                expo = jnp.exp(scores - jnp.max(scores, 0, keepdims=True))
                probs = (expo * (1.0 / jnp.sum(expo, 0, keepdims=True))).astype(bf16)
                probs_ref[image, side * HEADS + head] = probs
                both = jnp.concatenate([probs * halves[0], probs * halves[1]], 0)
                at = slice(head * HEAD_DIM, (head + 1) * HEAD_DIM)
                values = turned[2 * width + head * HEAD_DIM : 2 * width + (head + 1) * HEAD_DIM, across]
                att_ref[image, at, within] = nn(values, both).astype(bf16)
    attended = per_image(lambda i: nt(back_ref[...], att_ref[i]), count).astype(bf16)
    branch = nt(attended, join(proj_ref))
    middle = x + per_image(lambda i: valid_ref[step * count + i].astype(f32) * branch[image_rows(i)], count)
    store(middle_ref, middle)
    xhat, _ = norm_parts(middle)
    second_low = (xhat * gain_ref[1:2, :] + nbias_ref[1:2, :]).astype(bf16)
    store(second_ref, second_low)
    _, _, gate = route(second_low, router_ref[...], pos_col)
    store(gate_ref, gate)
    total_ref[...] += spread_rows(lay_positions(row_ref), second_low)

    @pl.when(step == final)
    def _():
        buffer_ref[...] = total_ref[...].astype(bf16)
        if gather:
            for k in (2, 3):
                moving.forward(k)
            for k in (2, 3):
                moving.arrive(k)
            for k in range(4):
                moving.sent(k)


def image_spec(array_shape, count):
    rest = tuple(array_shape[1:])
    zeros = (0,) * len(rest)
    return pl.BlockSpec((count,) + rest, lambda i: (i,) + zeros)


def whole_spec(array_shape):
    zeros = (0,) * len(array_shape)
    return pl.BlockSpec(tuple(array_shape), lambda i: zeros)


def image_call(kernel, images, arrays, outs, scratch, name, collective_id=None):
    count = 2 - images % 2

    def spec(kind, shape):
        if isinstance(kind, int):
            rest = tuple(shape[1:])
            return pl.BlockSpec((1,) + rest, lambda i: (kind,) + (0,) * len(rest))
        if kind in ("smem", "any"):
            return pl.BlockSpec(memory_space=pltpu.SMEM if kind == "smem" else pl.ANY)
        return image_spec(shape, count) if kind == "image" else whole_spec(shape)

    return pl.pallas_call(
        kernel,
        grid=(images // count,),
        out_shape=[jax.ShapeDtypeStruct(shape, dtype) for _, shape, dtype in outs],
        in_specs=[spec(kind, array.shape) for kind, array in arrays],
        out_specs=[spec(kind, shape) for kind, shape, _ in outs],
        scratch_shapes=scratch,
        compiler_params=pltpu.CompilerParams(
            vmem_limit_bytes=56 * MIB,
            dimension_semantics=("arbitrary",),
            collective_id=collective_id,
            has_side_effects=collective_id is not None,
        ),
        name=name,
    )(*[array for _, array in arrays])


def send_part(g, expert_out, second_low, router, pos_col, pos_row, logit_ref, router_grad_ref, total_ref):
    probs, chosen, gate = route(second_low, router, pos_col)
    gate_grad = jnp.where(pos_col >= 0, jnp.sum(g * expert_out, -1, keepdims=True), 0.0)
    sent = (gate * g).astype(bf16)
    logit_grad = gate_grad * gate * (chosen - probs)
    store(logit_ref, logit_grad)
    high, low = split_two(logit_grad)
    router_grad_ref[...] += tn(high, second_low) + tn(low, second_low)
    total_ref[...] += spread_rows(pos_row, sent)


def turn_kernel(
    prev_ref, gate_ref, returned_ref, cotangent_ref, enter_ref, leave_ref, col_ref, row_ref, second_ref, router_ref,
    block_ref, grad_ref, logit_ref, router_grad_ref, buffer_ref, total_ref,
):
    step = pl.program_id(0)
    count = cotangent_ref.shape[0]

    @pl.when(step == 0)
    def _():
        total_ref[...] = jnp.zeros(total_ref.shape, f32)
        router_grad_ref[...] = jnp.zeros(router_grad_ref.shape, f32)

    pos_col = join(col_ref)[:, 0:1]
    expert_out = collect(pos_col, returned_ref)
    x = (join(prev_ref) + join(gate_ref) * expert_out).astype(bf16)
    for i in range(count):
        block_ref[i] = nn(leave_ref[...], x[image_rows(i)]).astype(bf16)
    g = per_image(lambda i: nn(enter_ref[...], cotangent_ref[i]), count)
    store(grad_ref, g)
    send_part(
        g, expert_out, join(second_ref), router_ref[0], pos_col, lay_positions(row_ref), logit_ref, router_grad_ref, total_ref
    )

    @pl.when(step == pl.num_programs(0) - 1)
    def _():
        buffer_ref[...] = total_ref[...].astype(bf16)


def attention_backward_kernel(last, dp, mp, fast, *refs):
    (
        valid_ref, grad_ref, returned_ref, logit_ref, middle_ref, carried_ref, router_ref, col_ref, move_ref, back_ref,
        gain_ref, proj_ref, qkv_ref, window_ref, qk_ref, v_ref, probs_ref, att_ref,
    ) = refs[:18]
    refs = refs[18:]
    refs = list(refs)
    if fast:
        units_ref = refs.pop(0)
    if last:
        leave_ref = refs.pop(0)
        if fast:
            table_above, small_above, router_above, router_here, entry_ref, half_above, down_above, attn_above = refs[:8]
            refs = refs[8:]
    else:
        row_ref, expert_out_ref, second_ref, router_next_ref = refs[:4]
        refs = refs[4:]
    out_ref = refs.pop(0)
    closing = None
    if fast and last:
        results, refs = refs[:4], refs[4:]
    else:
        if fast:
            halves_ref = refs.pop(0)
            unit_ref, mine_ref = refs[:2]
        else:
            qkv_grad_ref, proj_grad_ref = refs[:2]
        table_ref, small_ref = refs[2:4]
        refs = refs[4:]
    if not last:
        logit_out_ref, router_grad_ref, buffer_ref = refs[:3]
        refs = refs[3:]
    turned = refs.pop(0)
    if fast:
        qkv_grad_ref, proj_grad_ref = refs[:2]
        refs = refs[2:]
    if not last:
        total_ref = refs.pop(0)
    step = pl.program_id(0)
    final = pl.num_programs(0) - 1
    count, _, width = carried_ref.shape
    if fast:
        row = Row()
        if last:
            table_ref, small_ref, unit_ref, lines_ref = refs[:4]
            landing, refs = refs[4:8], refs[8:]
            above = (half_above, down_above.at[1], attn_above)
            closing = Closing(row, dp, units_ref, unit_ref, lines_ref, above, landing, refs)
        else:
            sums = RowSum(row, blocks(units_ref), refs[0], refs[1], refs[2], blocks(mine_ref), refs[3:7])
            across_x = DeepSum(dp, [mine_ref.at[0]], [refs[7]], [halves_ref], [None], [None], refs[8:10] * 4)

        def take(k):
            if closing:
                closing.take(k)
            else:
                sums.end(k)
                if k == 0:
                    across_x.over_x(k).start()

        @pl.when(step == 0)
        def _():
            if closing:
                closing.enter()
            else:
                barrier = row.greet()
                pl.semaphore_wait(barrier, 2 + across_x.greet(barrier, False))
                for k in range(2):
                    sums.start(k)

    @pl.when(step == 0)
    def _():
        qkv_grad_ref[...] = jnp.zeros(qkv_grad_ref.shape, f32)
        proj_grad_ref[...] = jnp.zeros(proj_grad_ref.shape, f32)
        table_ref[...] = jnp.zeros(table_ref.shape, f32)
        small_ref[...] = jnp.zeros(small_ref.shape, f32)
        if not last:
            total_ref[...] = jnp.zeros(total_ref.shape, f32)
            router_grad_ref[...] = jnp.zeros(router_grad_ref.shape, f32)

    pos_col = join(col_ref)[:, 0:1]
    g = join(grad_ref)
    high, low = split_two(join(logit_ref))
    gain_ref, router = gain_ref.at[0], router_ref[0]
    normed_grad = collect(pos_col, returned_ref) + nn(high, router) + nn(low, router)
    xhat, rstd = norm_parts(join(middle_ref))
    small_ref[1:2, :] += jnp.sum(normed_grad * xhat, 0, keepdims=True)
    small_ref[3:4, :] += jnp.sum(normed_grad, 0, keepdims=True)
    middle_grad = g + norm_back(normed_grad, gain_ref[1:2, :], xhat, rstd)

    def branch_part(i):
        low_part = (valid_ref[step * count + i].astype(f32) * middle_grad[image_rows(i)]).astype(bf16)
        return nn(move_ref[...], low_part)

    branch_grad = per_image(branch_part, count).astype(bf16)
    for i in range(count):
        proj_grad_ref[...] += nn(att_ref[i], branch_grad[image_rows(i)])
    att_grad = nt(proj_ref[...], branch_grad).astype(bf16)
    if fast:

        @pl.when(step == 0)
        def _():
            if closing:
                closing.early()
            else:
                for k in range(2):
                    sums.middle(k)

        pl.when(step == final)(functools.partial(take, 0))

    heads_rows = head_masks()
    halves = lane_masks()
    low_lane = iota((WPAD, LANES), 1) < WPAD
    for pair in range(PAIRS * count):
        image, side = pair // PAIRS, pair % PAIRS
        across = slice(pair * LANES, (pair + 1) * LANES)
        within = slice(side * LANES, (side + 1) * LANES)
        for group in range(HEADS // GROUP):
            features = slice(group * LANES, (group + 1) * LANES)
            grads = att_grad[features, across]
            spread = jnp.concatenate([grads * heads_rows[h] for h in range(GROUP)], 1)
            raw = nn(v_ref[image, within, features], spread)
            for h in range(GROUP):
                head = group * GROUP + h
                at = slice(head * HEAD_DIM, (head + 1) * HEAD_DIM)
                below = slice(width + head * HEAD_DIM, width + (head + 1) * HEAD_DIM)
                lowest = slice(2 * width + head * HEAD_DIM, 2 * width + (head + 1) * HEAD_DIM)
                part = raw[:, h * LANES : (h + 1) * LANES]
                probs_grad = jnp.where(low_lane, part[:WPAD], part[WPAD:])
                probs_low = probs_ref[image, side * HEADS + head]
                probs = probs_low.astype(f32)
                weighted = probs * probs_grad
                scores_grad = weighted - probs * jnp.sum(weighted, 0, keepdims=True)
                table_ref[head] += scores_grad
                scores_low = scores_grad.astype(bf16)
                both = jnp.concatenate([scores_low * halves[0], scores_low * halves[1]], 0)
                probs_both = jnp.concatenate([probs_low * halves[0], probs_low * halves[1]], 0)
                turned[at, across] = (nn(qk_ref[image, below, within], both) * head_scale).astype(bf16)
                turned[below, across] = (nt(qk_ref[image, at, within], both) * head_scale).astype(bf16)
                turned[lowest, across] = nt(att_grad[at, across], probs_both).astype(bf16)
    qkv_grad_ref[...] += nn(turned[...], join(window_ref))
    if fast:

        @pl.when(step == final)
        def _():
            columns, rows = 3 * width // mp, width // mp
            proj_turned = proj_grad_ref[...].T
            for place in range(mp):
                q = quarter_at(place, mp)
                unit_ref[place, :columns] = qkv_grad_ref[q * columns : (q + 1) * columns].astype(bf16)
                unit_ref[place, columns:] = proj_turned[q * rows : (q + 1) * rows].astype(bf16)
            take(1)
            if closing:
                closing.open()

    mixed_grad = per_image(lambda i: nt(back_ref[...], turned[:, image_rows(i)]), count).astype(bf16)
    first_grad = nn(mixed_grad, qkv_ref[...])
    if closing:

        @pl.when(step == final)
        def _():
            closing.cross()

    xhat, rstd = norm_parts(join(carried_ref))
    small_ref[0:1, :] += jnp.sum(first_grad * xhat, 0, keepdims=True)
    small_ref[2:3, :] += jnp.sum(first_grad, 0, keepdims=True)
    out = middle_grad + norm_back(first_grad, gain_ref[0:1, :], xhat, rstd)
    if last:
        top = out.astype(bf16)
        rest = out - top.astype(f32)
        mid, low = split_two(rest)
        leave = leave_ref[...]
        for i in range(count):
            at = image_rows(i)
            out_ref[i] = nn(leave, top[at]) + nn(leave, mid[at]) + nn(leave, low[at])
    else:
        store(out_ref, out)
        send_part(
            out, join(expert_out_ref), join(second_ref), router_next_ref[0], pos_col, lay_positions(row_ref), logit_out_ref,
            router_grad_ref, total_ref,
        )

    @pl.when(step == final)
    def _():
        if not last:
            buffer_ref[...] = total_ref[...].astype(bf16)
        if closing:
            heads = 2 * HEADS
            lines_ref[...] = jnp.zeros(lines_ref.shape, f32)
            lines_ref[:heads, :TABLE] = table_grad([table_ref, table_above], entry_ref[...])
            lines_ref[heads : heads + EXPERTS] = router_here[:EXPERTS]
            lines_ref[heads + EXPERTS : heads + 2 * EXPERTS] = router_above[:EXPERTS]
            lines_ref[heads + 2 * EXPERTS : heads + 2 * EXPERTS + 8] = small_ref[...]
            lines_ref[heads + 2 * EXPERTS + 8 : heads + 2 * EXPERTS + 16] = small_above[...]
            closing.finish()
            for out, landed in zip(results, landing):
                out[...] = landed[...]
        elif fast:
            across_x.halve(0)
            across_x.over_x(0).wait_send()
            for k in range(2):
                sums.finish(k)


def quarter_at(place, mp):
    return place % (mp // 2) * 2 + place // (mp // 2)


def add_up(*parts):
    total = parts[0].astype(f32)
    for part in parts[1:]:
        total = total + part.astype(f32)
    return total


def to_row(source, target, sems, k, row):
    return pltpu.make_async_remote_copy(
        src_ref=source,
        dst_ref=target,
        send_sem=sems[0].at[k],
        recv_sem=sems[1].at[k],
        device_id={"mp": row},
        device_id_type=MESH,
    )


class Row:
    def __init__(self):
        row = lax.axis_index("mp")
        self.row, self.core, self.y = row, lax.rem(row, 2), lax.div(row, 2)
        self.sibling, self.across = row + 1 - 2 * self.core, row + 2 - 4 * self.y
        self.place = self.core * 2 + self.y
        self.place_across = self.core * 2 + 1 - self.y

    def greet(self):
        barrier = pltpu.get_barrier_semaphore()
        for row in (self.sibling, self.across):
            pl.semaphore_signal(barrier, inc=1, device_id={"mp": row}, device_id_type=MESH)
        return barrier


class RowSum:
    semaphores = 4

    def __init__(self, row, units, core_in, y_out, y_in, mine, sems):
        self.row, self.units, self.mine = row, units, mine
        self.core_in, self.y_out, self.y_in = core_in, y_out, y_in
        self.sems = (sems[:2], sems[2:])

    def pair(self, k):
        theirs = self.units[k].at[pl.ds(2 * (1 - self.row.core), 2)]
        return to_row(theirs, self.core_in.at[k], self.sems[0], k, self.row.sibling)

    def cross(self, k):
        return to_row(self.y_out.at[k], self.y_in.at[k], self.sems[1], k, self.row.across)

    def start(self, k):
        self.pair(k).start()

    def middle(self, k):
        self.pair(k).wait_recv()
        other = 1 - self.row.y
        mixed = add_up(self.units[k][self.row.core * 2 + other], self.core_in[k, other])
        self.y_out[k] = mixed.astype(bf16)
        self.cross(k).start()

    def end(self, k):
        self.cross(k).wait_recv()
        self.mine[k][...] = add_up(
            self.units[k][self.row.place], self.core_in[k, self.row.y], self.y_in[k]
        ).astype(bf16)

    def finish(self, k):
        self.pair(k).wait_send()
        self.cross(k).wait_send()

    @classmethod
    def scratch(cls, count, width):
        return [
            pltpu.VMEM((count, 2, width, width), bf16),
            pltpu.VMEM((count, width, width), bf16),
            pltpu.VMEM((count, width, width), bf16),
        ] + [pltpu.SemaphoreType.DMA((count,))] * cls.semaphores


class RowGather:
    semaphores = 6

    def __init__(self, row, sources, fulls, slot, slot_across, sems):
        self.row, self.sources, self.fulls = row, sources, fulls
        self.slot, self.slot_across = slot, slot_across
        self.sems = (sems[:2], sems[2:4], sems[4:])

    def over(self, k):
        return to_row(self.sources[k], self.fulls[k].at[self.slot], self.sems[0], k, self.row.across)

    def near(self, k):
        return to_row(self.sources[k], self.fulls[k].at[self.slot], self.sems[1], k, self.row.sibling)

    def onward(self, k):
        block = self.fulls[k].at[self.slot_across]
        return to_row(block, block, self.sems[2], k, self.row.sibling)

    def start(self, k):
        self.over(k).start()
        self.near(k).start()

    def forward(self, k):
        self.over(k).wait_recv()
        self.onward(k).start()

    def arrive(self, k):
        self.near(k).wait_recv()
        self.onward(k).wait_recv()

    def sent(self, k):
        self.over(k).wait_send()
        self.near(k).wait_send()
        self.onward(k).wait_send()

    @classmethod
    def scratch(cls, count):
        return [pltpu.SemaphoreType.DMA((count,))] * cls.semaphores


class WeightGather(RowGather):
    def __init__(self, shards, fulls, sems):
        row = Row()
        super().__init__(row, shards, fulls, row.row, row.across, sems[:6])
        self.own_sem = sems[6]

    def own(self, k):
        return pltpu.make_async_copy(self.sources[k], self.fulls[k].at[self.slot], self.own_sem.at[k])

    def start(self, k):
        super().start(k)
        self.own(k).start()

    def arrive(self, k):
        super().arrive(k)
        self.own(k).wait()

    @classmethod
    def scratch(cls, count):
        return super().scratch(count) + [pltpu.SemaphoreType.DMA((count,))]


class DeepSum:
    def __init__(self, dp, total, arrived, halves, slots, result, sems):
        self.total, self.arrived, self.halves, self.slots, self.result = total, arrived, halves, slots, result
        self.x_sems, self.z_sems, self.z_back, self.x_back = (sems[2 * k : 2 * k + 2] for k in range(4))
        me = lax.axis_index("dp")
        self.x, self.z, self.deep = lax.rem(me, 2), lax.div(me, 2), dp // 2
        self.partner = me + 1 - 2 * self.x

    def greet(self, barrier, whole=True):
        pl.semaphore_signal(barrier, inc=1, device_id={"dp": self.partner}, device_id_type=MESH)
        if not whole:
            return 1
        for off in range(1, self.deep):
            peer = lax.rem(self.z + off, self.deep) * 2 + self.x
            pl.semaphore_signal(barrier, inc=1, device_id={"dp": peer}, device_id_type=MESH)
        return self.deep

    def cut(self, k):
        height = self.halves[k].shape[0]
        return height, height // self.deep

    def over_x(self, k):
        height, _ = self.cut(k)
        away = self.total[k].at[pl.ds(pl.multiple_of((1 - self.x) * height, height), height)]
        return to_peer(away, self.arrived[k], self.x_sems[0].at[k], self.x_sems[1].at[k], self.partner)

    def over_z(self, k, off):
        _, piece = self.cut(k)
        to = lax.rem(self.z + off, self.deep)
        part = self.halves[k].at[pl.ds(pl.multiple_of(to * piece, piece), piece)]
        sems = [sem.at[k, off] for sem in self.z_sems]
        return to_peer(part, self.slots[k].at[off], *sems, to * 2 + self.x)

    def own_piece(self, k):
        height, piece = self.cut(k)
        return self.result[k].at[pl.ds(pl.multiple_of(self.x * height + self.z * piece, piece), piece)]

    def own_half(self, k):
        height, _ = self.cut(k)
        return self.result[k].at[pl.ds(pl.multiple_of(self.x * height, height), height)]

    def back_z(self, k, off):
        to = lax.rem(self.z + off, self.deep)
        sems = [sem.at[k, off] for sem in self.z_back]
        return to_peer(self.own_piece(k), self.own_piece(k), *sems, to * 2 + self.x)

    def back_x(self, k):
        return to_peer(self.own_half(k), self.own_half(k), self.x_back[0].at[k], self.x_back[1].at[k], self.partner)

    def halve(self, k):
        self.over_x(k).wait_recv()
        height, _ = self.cut(k)
        keep = self.total[k][pl.ds(pl.multiple_of(self.x * height, height), height)]
        self.halves[k][...] = add_up(keep, self.arrived[k][...]).astype(self.halves[k].dtype)

    def deepen(self, k):
        for off in range(1, self.deep):
            self.over_z(k, off).start()

    def quarter(self, k):
        for off in range(1, self.deep):
            self.over_z(k, off).wait_recv()
        _, piece = self.cut(k)
        keep = self.halves[k][pl.ds(pl.multiple_of(self.z * piece, piece), piece)]
        total = add_up(keep, *[self.slots[k][off] for off in range(1, self.deep)])
        self.own_piece(k)[...] = total.astype(self.result[k].dtype)
        for off in range(1, self.deep):
            self.back_z(k, off).start()

    def widen(self, k):
        for off in range(1, self.deep):
            self.back_z(k, off).wait_recv()
        self.back_x(k).start()

    def finish(self, k, halved=True):
        if halved:
            self.over_x(k).wait_send()
        for off in range(1, self.deep):
            self.over_z(k, off).wait_send()
            self.back_z(k, off).wait_send()
        self.back_x(k).wait()

    @staticmethod
    def semaphores(dp, count):
        one, many = pltpu.SemaphoreType.DMA((count,)), pltpu.SemaphoreType.DMA((count, dp // 2))
        return [one, one, many, many, many, many, one, one]


def blocks(ref):
    return [ref.at[k] for k in range(ref.shape[0])]


class Closing:
    lines = 64

    def __init__(self, row, dp, units_ref, attn_ref, lines_ref, given, results, refs):
        self.row, self.lines_ref = row, lines_ref
        self.full, shard, small, above = results
        core_in, y_out, y_in = refs[:3]
        mine, x_in, half, z_in, self.s_core, self.s_one, self.s_y, self.s_mine, s_x, s_half, s_z = refs[7:18]
        x_above, half_above, z_above = refs[18:21]
        refs_sems, refs = refs[3:7], refs[21:]
        self.mine = mine
        self.sums = RowSum(row, blocks(units_ref) + [attn_ref], core_in, y_out, y_in, blocks(mine), refs_sems)
        self.gather = RowGather(
            row, [mine.at[k] for k in range(2)], blocks(self.full), row.place, row.place_across, refs[:6]
        )
        self.s_pair = to_row(lines_ref, self.s_core, refs[6:8], 0, row.sibling)
        self.s_cross = to_row(self.s_one, self.s_y, refs[8:10], 0, row.across)
        self.here = DeepSum(
            dp, blocks(mine) + [self.s_mine], blocks(x_in) + [s_x], blocks(half) + [s_half], blocks(z_in) + [s_z],
            blocks(shard) + [small], refs[10:18],
        )
        self.above = DeepSum(
            dp, [None, *given[1:]], [None] + blocks(x_above), [given[0]] + blocks(half_above), blocks(z_above), blocks(above),
            refs[18:26],
        )

    def enter(self):
        barrier = self.row.greet()
        pl.semaphore_wait(barrier, 2 + self.here.greet(barrier))
        for k in range(2):
            self.sums.start(k)
        self.above.deepen(0)
        for k in (1, 2):
            self.above.over_x(k).start()

    def early(self):
        for k in range(2):
            self.sums.middle(k)
        for k in (1, 2):
            self.above.halve(k)
            self.above.deepen(k)
        self.above.quarter(0)

    def take(self, k):
        self.sums.end(k)
        self.here.over_x(k).start()
        if k == 0:
            self.above.widen(0)
            for j in (1, 2):
                self.above.quarter(j)
        else:
            for j in (1, 2):
                self.above.widen(j)

    def open(self):
        self.sums.start(2)
        for k in range(2):
            self.here.halve(k)
            self.here.deepen(k)

    def cross(self):
        self.sums.middle(2)
        for k in range(2):
            self.here.quarter(k)

    def finish(self):
        here = self.here
        self.s_pair.start()
        self.sums.end(2)
        here.over_x(2).start()
        self.s_pair.wait_recv()
        self.s_one[...] = self.lines_ref[...] + self.s_core[...]
        self.s_cross.start()
        for k in range(2):
            self.gather.start(k)
            here.widen(k)
            self.full[k, self.row.place] = self.mine[k]
        here.halve(2)
        here.deepen(2)
        self.s_cross.wait_recv()
        self.s_mine[...] = self.s_one[...] + self.s_y[...]
        here.over_x(3).start()
        here.quarter(2)
        here.halve(3)
        here.deepen(3)
        here.widen(2)
        self.gather.forward(0)
        here.quarter(3)
        here.widen(3)
        self.gather.forward(1)
        self.s_pair.wait_send()
        self.s_cross.wait_send()
        for k in range(3):
            self.sums.finish(k)
            self.above.finish(k, k > 0)
        for k in range(2):
            self.gather.arrive(k)
            self.gather.sent(k)
        for k in range(4):
            here.finish(k)

    @classmethod
    def scratch(cls, dp, width):
        deep = dp // 2
        lines = cls.lines
        flat, half_flat = pltpu.VMEM((lines, width), f32), pltpu.VMEM((lines // 2, width), f32)
        half, slots = (width // 2, width), (3, deep, width // dp, width)
        return (
            RowSum.scratch(3, width)
            + [
                pltpu.VMEM((3, width, width), bf16),
                pltpu.VMEM((3, *half), bf16),
                pltpu.VMEM((3, *half), bf16),
                pltpu.VMEM(slots, bf16),
                flat, flat, flat, flat, half_flat, half_flat,
                pltpu.VMEM((deep, lines // dp, width), f32),
                pltpu.VMEM((2, *half), bf16),
                pltpu.VMEM((2, *half), bf16),
                pltpu.VMEM(slots, bf16),
            ]
            + RowGather.scratch(2)
            + [pltpu.SemaphoreType.DMA((1,))] * 4
            + DeepSum.semaphores(dp, 4)
            + DeepSum.semaphores(dp, 3)
        )


def format_kernel(columns, *refs):
    layers = len(refs[:-6]) // 3
    qkv_out, proj_out, core_up_out, core_down_out, up_out, down_out = refs[-6:]

    def form(ups, downs, shard):
        mp, rows = downs.shape[1], downs.shape[2]
        up_out[0, 0] = ups[0, 0].astype(f32)
        down_out[0, 0] = jnp.concatenate(
            [downs[0, q % 2 * (mp // 2) + q // 2].astype(f32) for q in range(mp)], 0
        ).T
        core_down_out[0] = shard[1, pl.ds(pl.multiple_of(pl.program_id(1) * rows, rows), rows)].astype(f32)

        @pl.when(pl.program_id(1) == 0)
        def _():
            qkv_out[0] = shard[2, :columns].astype(f32)
            proj_out[0] = shard[2, columns:].astype(f32)
            core_up_out[0] = shard[0].astype(f32)

    for layer in range(layers):
        pl.when(pl.program_id(0) == layer)(functools.partial(form, *refs[3 * layer : 3 * layer + 3]))


def format_call(fulls, shards, columns):
    layers = len(fulls)
    _, mp, width, _ = fulls[0].shape
    hidden, rows = mp * width, width // mp
    outs = [
        ((layers, columns, width), None),
        ((layers, width - columns, width), None),
        ((layers, width, width), None),
        ((layers, rows, hidden), pl.BlockSpec((1, rows, width), lambda i, j: (i, 0, j))),
        ((layers, 1, width, hidden), pl.BlockSpec((1, 1, width, width), lambda i, j: (i, 0, 0, j))),
        ((layers, 1, hidden, width), pl.BlockSpec((1, 1, width, width), lambda i, j: (i, 0, j, 0))),
    ]

    def by_layer(shape):
        return pl.BlockSpec((1, *shape[1:]), lambda i, j: (i, 0, 0))

    def chunk(layer, i, j):
        return jnp.where(i == layer, j, jnp.where(i < layer, 0, mp - 1))

    def place(q):
        return lax.rem(q, 2) * (mp // 2) + lax.div(q, 2)

    specs, arrays = [], []
    for layer in range(layers):
        specs += [
            pl.BlockSpec((1, 1, width, width), lambda i, j, at=layer: (0, place(chunk(at, i, j)), 0, 0)),
            pl.BlockSpec((1, mp, rows, width), lambda i, j, at=layer: (1, 0, chunk(at, i, j), 0)),
            pl.BlockSpec((3, width, width), lambda i, j: (0, 0, 0)),
        ]
        arrays += [fulls[layer], fulls[layer], shards[layer]]
    return pl.pallas_call(
        functools.partial(format_kernel, columns),
        grid=(layers, mp),
        out_shape=[jax.ShapeDtypeStruct(shape, f32) for shape, _ in outs],
        in_specs=specs,
        out_specs=[spec or by_layer(shape) for shape, spec in outs],
        compiler_params=pltpu.CompilerParams(vmem_limit_bytes=56 * MIB),
        name="format",
    )(*arrays)


def greet(dp, me, rows=()):
    barrier = pltpu.get_barrier_semaphore()
    for row in rows:
        pl.semaphore_signal(barrier, inc=1, device_id={"mp": row}, device_id_type=MESH)

    def signal(off, carry):
        pl.semaphore_signal(barrier, inc=1, device_id={"dp": lax.rem(me + off, dp)}, device_id_type=MESH)
        return carry

    lax.fori_loop(1, dp, signal, 0)
    pl.semaphore_wait(barrier, dp - 1 + len(rows))


def partner_of(me, p, dp):
    out, bit = 0, 1
    while bit < dp:
        one, two = lax.rem(lax.div(me, bit), 2), lax.rem(lax.div(p, bit), 2)
        out = out + bit * (one + two - 2 * one * two)
        bit *= 2
    return out


def to_peer(source, target, send_sem, recv_sem, peer):
    return pltpu.make_async_remote_copy(
        src_ref=source,
        dst_ref=target,
        send_sem=send_sem,
        recv_sem=recv_sem,
        device_id={"dp": peer},
        device_id_type=MESH,
    )


def gelu_parts(h):
    root = np.float32(np.sqrt(2.0 / np.pi))
    square = h * h
    t = jnp.tanh(root * h * (1.0 + 0.044715 * square))
    half = 0.5 * (1.0 + t)
    slope = half + 0.5 * h * (1.0 - t * t) * root * (1.0 + 3 * 0.044715 * square)
    return h * half, slope


def expert_forward_kernel(dp, mp, layer, gather, *refs):
    refs = list(refs)
    buffer_ref, up_any, down_any, rup_any, rdown_any = refs[:5]
    refs = refs[5:]
    if gather:
        shards = [ref.at[layer + 1] for ref in refs[:4]]
        refs = refs[4:]
    recv_ref, returned_ref, up_eff, down_eff = refs[:4]
    refs = refs[4:]
    if gather:
        fulls = refs[:4]
        refs = refs[4:]
    part, core, up_ref, down_ref, rup_ref, rdown_ref, local = refs[:7]
    refs = refs[7:]
    moving = WeightGather(shards, fulls, refs[:7]) if gather else None
    send_one, recv_one, send_two, recv_two = refs[-4:]
    split = dp // EXPERTS
    me = lax.axis_index("dp")
    loads = [
        pltpu.make_async_copy(source, target, local.at[k])
        for k, (source, target) in enumerate(
            [
                (up_any, up_ref),
                (rup_any.at[layer, 0], rup_ref),
                (down_any, down_ref),
                (rdown_any.at[layer, 0], rdown_ref),
            ]
        )
    ]
    for load in loads:
        load.start()
    greet(dp, me, (moving.row.sibling, moving.row.across) if gather else ())

    def first(off):
        peer = partner_of(me, off, dp)
        return to_peer(
            buffer_ref.at[lax.div(peer, split)], recv_ref.at[me], send_one.at[off], recv_one.at[off], peer
        )

    def second(off):
        source = partner_of(me, off, dp)
        return to_peer(part.at[source], returned_ref.at[me], send_two.at[off], recv_two.at[off], source)

    def start_first(off, carry):
        first(dp - off).start()
        return carry

    lax.fori_loop(1, dp, start_first, 0)
    if gather:
        for k in range(4):
            moving.start(k)
    recv_ref[me] = buffer_ref[lax.div(me, split)]
    hidden = up_eff.shape[1]
    columns = up_ref.shape[-1]
    loads[0].wait()
    loads[1].wait()
    if split == 1 and columns % LANES == 0:
        for m in range(mp):
            at = slice(m * columns, (m + 1) * columns)
            up_eff[:, at] = (up_ref[m].astype(f32) + rup_ref[:, at].astype(f32)).astype(bf16)
    else:
        core[...] = rup_ref[...].astype(f32)
        begin = lax.rem(me, split) * hidden
        for m in range(mp):
            put = onehot(iota((columns, hidden), 0) + m * columns == iota((columns, hidden), 1) + begin)
            core[...] += nn(up_ref[m], put)
        up_eff[...] = core[...].astype(bf16)
    begin = pl.multiple_of(lax.rem(me, split) * hidden, LANES)
    loads[2].wait()
    loads[3].wait()
    core_part = down_ref[:, :, pl.ds(begin, hidden)].reshape(down_eff.shape[1], hidden)
    down_eff[...] = (core_part.astype(f32).T + rdown_ref[...].astype(f32)).astype(bf16)

    def work(source):
        hidden_pre = nn(recv_ref[source], up_eff[...])
        hidden_low = gelu_parts(hidden_pre)[0].astype(bf16)
        return nn(hidden_low, down_eff[...]).astype(bf16)

    returned_ref[me] = work(me)

    def step(off, carry):
        source = partner_of(me, off, dp)
        first(off).wait_recv()
        part[source] = work(source)
        second(off).start()
        return carry

    lax.fori_loop(1, dp, step, 0)
    if gather:
        for k in range(4):
            moving.forward(k)

    def finish(off, carry):
        first(off).wait_send()
        second(off).wait()
        return carry

    lax.fori_loop(1, dp, finish, 0)
    if gather:
        for k in range(4):
            moving.arrive(k)
            moving.sent(k)


def expert_backward_kernel(dp, mp, fast, reduce, *refs):
    refs = list(refs)
    buffer_ref, recv_ref, up_ref, down_ref = refs[:4]
    refs = refs[4:]
    if reduce:
        given_ref, attn_ref = refs[:2]
        refs = refs[2:]
    returned_ref = refs.pop(0)
    if fast:
        units_ref = refs.pop(0)
    else:
        up_term, down_term = refs[:2]
        refs = refs[2:]
    if reduce:
        full_ref, mine_ref = refs[:2]
        refs = refs[2:]
    grads, hidden_low, slope, pre, part = refs[:5]
    refs = refs[5:]
    if fast:
        up_term, down_term = refs[:2]
        refs = refs[2:]
    row = Row() if reduce else None
    if reduce:
        core_in, y_out, y_in = refs[:3]
        sums = RowSum(row, [attn_ref], core_in, y_out, y_in, [mine_ref], refs[3:7])
        gather = RowGather(
            row, [given_ref.at[k] for k in range(2)], [full_ref.at[k] for k in range(2)], row.place, row.place_across,
            refs[7:13],
        )
        refs = refs[13:]
    send_one, recv_one, send_two, recv_two = refs
    split = dp // EXPERTS
    me = lax.axis_index("dp")
    greet(dp, me, (row.sibling, row.across) if reduce else ())

    def first(off):
        peer = partner_of(me, off, dp)
        return to_peer(buffer_ref.at[lax.div(peer, split)], grads.at[me], send_one.at[off], recv_one.at[off], peer)

    def second(off):
        source = partner_of(me, off, dp)
        return to_peer(part.at[source], returned_ref.at[me], send_two.at[off], recv_two.at[off], source)

    def start_first(off, carry):
        first(dp - off).start()
        return carry

    lax.fori_loop(1, dp, start_first, 0)
    if reduce:
        sums.start(0)
        for k in range(2):
            gather.start(k)
    grads[me] = buffer_ref[lax.div(me, split)]

    def again(source, carry):
        value, rate = gelu_parts(nn(recv_ref[source], up_ref[...]))
        hidden_low[source] = value.astype(bf16)
        slope[source] = rate
        return carry

    lax.fori_loop(0, dp, again, 0)
    if reduce:
        sums.middle(0)
        for k in range(2):
            full_ref[k, row.place] = given_ref[k]

    def work(source):
        hidden_grad = nt(grads[source], down_ref[...])
        pre_grad = (slope[source] * hidden_grad).astype(bf16)
        pre[source] = pre_grad
        return nt(pre_grad, up_ref[...]).astype(bf16)

    returned_ref[me] = work(me)

    def step(off, carry):
        source = partner_of(me, off, dp)
        first(off).wait_recv()
        part[source] = work(source)
        second(off).start()
        return carry

    lax.fori_loop(1, dp, step, 0)
    if reduce:
        for k in range(2):
            gather.forward(k)
        sums.end(0)
    up_term[...] = jnp.zeros(up_term.shape, f32)
    down_term[...] = jnp.zeros(down_term.shape, f32)

    def terms(block, carry):
        up_term[...] += tn(recv_ref[block], pre[block])
        down_term[...] += tn(grads[block], hidden_low[block])
        return carry

    lax.fori_loop(0, dp, terms, 0)
    if fast:
        width = up_term.shape[0]
        height = width // mp
        for place in range(mp):
            q = quarter_at(place, mp)
            units_ref[0, place] = up_term[:, q * width : (q + 1) * width].astype(bf16)
            for chunk in range(mp):
                block = down_term[q * height : (q + 1) * height, chunk * width : (chunk + 1) * width]
                units_ref[1, place, chunk * height : (chunk + 1) * height] = block.astype(bf16)

    def finish(off, carry):
        first(off).wait_send()
        second(off).wait()
        return carry

    lax.fori_loop(1, dp, finish, 0)
    if reduce:
        sums.finish(0)
        for k in range(2):
            gather.arrive(k)
            gather.sent(k)


def expert_call(kernel, arrays, outs, scratch, dp, collective_id, name, flops, anys=(), any_outs=()):
    sems = [pltpu.SemaphoreType.DMA((dp,))] * 4
    vmem, anywhere = pl.BlockSpec(memory_space=pltpu.VMEM), pl.BlockSpec(memory_space=pl.ANY)
    return pl.pallas_call(
        kernel,
        out_shape=[jax.ShapeDtypeStruct(shape, dtype) for shape, dtype in (*outs, *any_outs)],
        in_specs=[vmem] * len(arrays) + [anywhere] * len(anys),
        out_specs=[vmem] * len(outs) + [anywhere] * len(any_outs),
        scratch_shapes=scratch + sems,
        compiler_params=pltpu.CompilerParams(
            vmem_limit_bytes=56 * MIB, collective_id=collective_id, has_side_effects=True
        ),
        cost_estimate=pl.CostEstimate(flops=flops, bytes_accessed=20 * MIB, transcendentals=0),
        name=name,
    )(*arrays, *anys)


def by_windows(grid):
    images, kinds = grid.shape[:2]
    blocks = GRID // WINDOW
    grid = grid.reshape(images, kinds, blocks, WINDOW, blocks, WINDOW).transpose(0, 1, 2, 4, 3, 5)
    grid = grid.reshape(images, kinds, blocks * blocks, WINPOS)
    grid = jnp.pad(grid, ((0, 0), (0, 0), (0, 0), (0, WPAD - WINPOS)), constant_values=-1)
    return grid.reshape(images, kinds, IMGROWS)


def per_device(
    patches,
    qkv_weight,
    proj_weight,
    core_up,
    core_down,
    residual_up,
    residual_down,
    position_bias,
    router_weight,
    norm_gain,
    norm_bias,
    cotangent,
    image_valid,
    expert_index,
    slot_index,
    region_id,
):
    dp, mp = lax.axis_size("dp"), lax.axis_size("mp")
    images, _, width = patches.shape
    split = dp // EXPERTS
    hidden = residual_up.shape[-1]
    hidden_full = core_up.shape[-1] * mp
    row_index = lax.axis_index("mp")

    fast = split == 1 and dp == 8 and mp == 4 and hidden == mp * width
    qkv_rows, proj_rows, down_rows = (a.transpose(0, 2, 1) for a in (qkv_weight, proj_weight, core_down))
    shards = (qkv_rows, proj_rows, core_up, down_rows)
    gathered = [[None] * len(shards)] * LAYERS
    if not fast:
        gathered = [[lax.all_gather(a[l], "mp", axis=0, tiled=False) for a in shards] for l in range(LAYERS)]

    position = jnp.where(slot_index >= 0, expert_index * SLOTS + slot_index, -1)
    row_form = by_windows(jnp.stack([position.reshape(images, GRID, GRID), region_id], 1))
    col_form = row_form.transpose(0, 2, 1)
    enter = jnp.asarray(enter_table(), bf16)
    leave = jnp.asarray(enter_table().T, bf16)
    moves = [jnp.asarray(move_table(l % 2 == 1), bf16) for l in range(LAYERS)]
    backs = [jnp.asarray(move_table(l % 2 == 1).T, bf16) for l in range(LAYERS)]
    table_rows = position_bias.transpose(0, 2, 1).reshape(LAYERS * HEADS, OFFSETS)
    table_rows = jnp.pad(table_rows, ((0, 0), (0, TABLE - OFFSETS)))
    entry_row, entry_col = jnp.asarray(cell_entries()[None, :]), jnp.asarray(cell_entries()[:, None])
    routers = jnp.pad(router_weight.transpose(0, 2, 1), ((0, 0), (0, LANES - EXPERTS), (0, 0)))

    token = (images, IMGROWS, width)
    buffer_shape = (ROWS, width)
    block_rows = (dp, SLOTS, width)
    pieces = (split, ROWS, width)

    def by_piece(returned):
        return returned.reshape(EXPERTS, split, SLOTS, width).transpose(1, 0, 2, 3).reshape(pieces)

    records = []
    before = None
    for l in range(LAYERS):
        first = l == 0
        gather = fast and first
        if first:
            arrays = [("image", patches), ("whole", enter)]
        else:
            arrays = [("image", before[0]), ("image", before[1]), ("whole", before[2])]
        arrays += [
            ("smem", image_valid),
            ("image", col_form),
            ("image", row_form),
            ("any", qkv_rows) if gather else ("whole", gathered[l][0]),
            ("any", proj_rows) if gather else ("whole", gathered[l][1]),
            ("whole", table_rows) if first else (l, biases),
            ("whole", moves[l]),
            ("whole", backs[l]),
            (l, norm_gain),
            (l, norm_bias),
            (l, routers),
        ]
        if first:
            arrays.append(("whole", entry_row))
        if gather:
            arrays += [("any", core_up), ("any", down_rows)]
        outs = [("image", token, f32)]
        if first:
            outs.append(("whole", (LAYERS, HEADS, WPAD, LANES), f32))
        else:
            outs.append(("image", token, f32))
        outs += [
            ("image", token, f32),
            ("image", token, bf16),
            ("image", (images, IMGROWS, 1), f32),
            ("whole", buffer_shape, bf16),
            ("image", token, bf16),
            ("image", (images, 2 * width, IMGROWS), bf16),
            ("image", token, bf16),
            ("image", (images, PAIRS * HEADS, WPAD, LANES), bf16),
            ("image", (images, width, IMGROWS), bf16),
            ("whole", (width, width), bf16),
        ]
        scratch = [pltpu.VMEM(buffer_shape, f32)]
        gathered_shapes = [(mp, *a.shape[1:]) for a in shards]
        if gather:
            outs.append(("whole", (3 * width, width), bf16))
            outs += [("any", shape, bf16) for shape in gathered_shapes[2:]]
            scratch += [pltpu.VMEM(shape, bf16) for shape in gathered_shapes[:2]] + WeightGather.scratch(4)
        results = list(
            image_call(
                functools.partial(attention_forward_kernel, first, l % 2 == 1, mp, gather),
                images, arrays, outs, scratch, f"attend_{l}", 3 * LAYERS + 1 if gather else None,
            )
        )
        if gather:
            gathered[l] = [results[-3], None] + results[-2:]
            results = results[:-3]
        carried = results.pop(0)
        if first:
            biases = results.pop(0)
        else:
            records[-1]["expert_out"] = results.pop(0)
        middle, second_low, gate, buffer = results[:4]
        gather = fast and l < LAYERS - 1
        received, returned, up_eff, down_eff, *more = expert_call(
            functools.partial(expert_forward_kernel, dp, mp, l, gather),
            [buffer.reshape(EXPERTS, SLOTS, width)],
            [
                (block_rows, bf16),
                (block_rows, bf16),
                ((width, hidden), bf16),
                ((hidden, width), bf16),
            ],
            [
                pltpu.VMEM(block_rows, bf16),
                pltpu.VMEM((8, LANES) if fast else (width, hidden), f32),
                pltpu.VMEM(gathered_shapes[2], bf16),
                pltpu.VMEM(gathered_shapes[3], bf16),
                pltpu.VMEM((width, hidden), bf16),
                pltpu.VMEM((hidden, width), bf16),
                pltpu.SemaphoreType.DMA((4,)),
            ]
            + (WeightGather.scratch(4) if gather else []),
            dp, l, f"experts_{l}", 4 * dp * SLOTS * width * hidden,
            [gathered[l][2], gathered[l][3], residual_up, residual_down, *(shards if gather else ())],
            [(shape, bf16) for shape in gathered_shapes] if gather else (),
        )
        if gather:
            gathered[l + 1] = more
        returned = by_piece(returned)
        before = (middle, gate, returned)
        records.append(
            dict(
                carried=carried, middle=middle, second_low=second_low, gate=gate, saved=results[4:], received=received,
                up_eff=up_eff, down_eff=down_eff,
            )
        )

    top = records[-1]
    block_output, grad, logit_grad, router_part, buffer = image_call(
        turn_kernel,
        images,
        [
            ("image", before[0]),
            ("image", before[1]),
            ("whole", before[2]),
            ("image", cotangent),
            ("whole", enter),
            ("whole", leave),
            ("image", col_form),
            ("image", row_form),
            ("image", top["second_low"]),
            (LAYERS - 1, routers),
        ],
        [
            ("image", patches.shape, bf16),
            ("image", token, f32),
            ("image", (images, IMGROWS, LANES), f32),
            ("whole", (LANES, width), f32),
            ("whole", buffer_shape, bf16),
        ],
        [pltpu.VMEM(buffer_shape, f32)],
        "turn",
    )
    router_parts, tables, smalls = [None] * LAYERS, [None] * LAYERS, [None] * LAYERS
    residual_sums, shard_sums = [None] * LAYERS, [None] * LAYERS
    router_parts[LAYERS - 1] = router_part
    units, attn_units, mines = [None] * LAYERS, [None] * LAYERS, [None] * LAYERS
    for l in reversed(range(LAYERS)):
        rec = records[l]
        last = l == 0
        reduce = fast and l < LAYERS - 1
        arrays = [buffer.reshape(EXPERTS, SLOTS, width), rec["received"], rec["up_eff"], rec["down_eff"]]
        outs = [(block_rows, bf16)]
        scratch = [
            pltpu.VMEM(block_rows, bf16),
            pltpu.VMEM((dp, SLOTS, hidden), bf16),
            pltpu.VMEM((dp, SLOTS, hidden), f32),
            pltpu.VMEM((dp, SLOTS, hidden), bf16),
            pltpu.VMEM(block_rows, bf16),
        ]
        if fast:
            outs.append(((2, mp, width, width), bf16))
            scratch += [pltpu.VMEM((width, hidden), f32)] * 2
        else:
            outs += [((width, hidden), f32)] * 2
        if reduce:
            arrays += [mines[l + 1], attn_units[l + 1]]
            outs += [((2, mp, width, width), bf16), ((width, width), bf16)]
            scratch += RowSum.scratch(1, width) + RowGather.scratch(2)
        results = list(
            expert_call(
                functools.partial(expert_backward_kernel, dp, mp, fast, reduce), arrays, outs, scratch, dp, LAYERS + l,
                f"experts_back_{l}", 10 * dp * SLOTS * width * hidden,
            )
        )
        returned_grad = results.pop(0)
        if fast:
            units[l] = results.pop(0)
        else:
            residual_sums[l] = lax.psum(tuple(t.astype(bf16) for t in results[:2]), "mp")
        if reduce:
            full_above, mine_above = results
        window_in, qk, v, probs, att, proj_full = rec["saved"]
        qkv_full = gathered[l][0].reshape(3 * width, width)
        arrays = [
            ("smem", image_valid),
            ("image", grad),
            ("whole", by_piece(returned_grad)),
            ("image", logit_grad),
            ("image", rec["middle"]),
            ("image", rec["carried"]),
            (l, routers),
            ("image", col_form),
            ("whole", moves[l]),
            ("whole", backs[l]),
            (l, norm_gain),
            ("whole", proj_full),
            ("whole", qkv_full),
            ("image", window_in),
            ("image", qk),
            ("image", v),
            ("image", probs),
            ("image", att),
        ]
        outs = [("image", patches.shape if last else token, f32)]
        scratch = [pltpu.VMEM((3 * width, (2 - images % 2) * IMGROWS), bf16)]
        closes = fast and last
        table_shape, small_shape = (HEADS, WPAD, LANES), (8, width)
        if fast:
            arrays.append(("whole", units[l]))
            scratch += [pltpu.VMEM((3 * width, width), f32), pltpu.VMEM((width, width), f32)]
        if closes:
            outs += [
                ("whole", (2, mp, width, width), bf16),
                ("whole", (3, width, width), bf16),
                ("whole", (Closing.lines, width), f32),
                ("whole", (3, width, width), bf16),
            ]
        else:
            if fast:
                outs += [
                    ("whole", (width // 2, width), bf16),
                    ("whole", (mp, width, width), bf16),
                    ("whole", (2, width, width), bf16),
                ]
            else:
                outs += [("whole", (3 * width, width), f32), ("whole", (width, width), f32)]
            outs += [("whole", table_shape, f32), ("whole", small_shape, f32)]
        if last:
            arrays.append(("whole", leave))
            if fast:
                arrays += [
                    ("whole", a)
                    for a in (
                        tables[1], smalls[1], router_parts[1], router_parts[0], entry_col, halves_above, mines[1],
                        mine_above,
                    )
                ]
        else:
            below = records[l - 1]
            arrays += [
                ("image", row_form),
                ("image", below["expert_out"]),
                ("image", below["second_low"]),
                (l - 1, routers),
            ]
            outs += [
                ("image", (images, IMGROWS, LANES), f32),
                ("whole", (LANES, width), f32),
                ("whole", buffer_shape, bf16),
            ]
            scratch.append(pltpu.VMEM(buffer_shape, f32))
        if closes:
            scratch += [
                pltpu.VMEM(table_shape, f32),
                pltpu.VMEM(small_shape, f32),
                pltpu.VMEM((mp, width, width), bf16),
                pltpu.VMEM((Closing.lines, width), f32),
            ]
            scratch += [pltpu.VMEM(shape, dtype) for _, shape, dtype in outs[1:5]] + Closing.scratch(dp, width)
        elif fast:
            scratch += RowSum.scratch(2, width) + [pltpu.VMEM((width // 2, width), bf16)]
            scratch += [pltpu.SemaphoreType.DMA((1,))] * 2
        results = list(
            image_call(
                functools.partial(attention_backward_kernel, last, dp, mp, fast),
                images, arrays, outs, scratch, f"attend_back_{l}", 2 * LAYERS + 1 + l if fast else None,
            )
        )
        grad = results.pop(0)
        if closes:
            full, closed, lines, shard_above = results
            continue
        if fast:
            halves_above = results.pop(0)
            attn_units[l], mines[l] = results[:2]
        else:
            qkv_part, proj_part = results[:2]
        tables[l], smalls[l] = results[2:4]
        if not last:
            logit_grad, router_parts[l - 1], buffer = results[4:]
        if fast:
            continue
        attn = (
            lax.psum_scatter(qkv_part.astype(bf16), "mp", scatter_dimension=0, tiled=True),
            lax.psum_scatter(proj_part.T.astype(bf16), "mp", scatter_dimension=0, tiled=True),
        )
        up_sum, down_sum = residual_sums[l]
        if split > 1:
            begin = lax.axis_index("dp") % split * hidden
            empty = jnp.zeros((width, hidden_full), bf16)
            up_sum = lax.dynamic_update_slice_in_dim(empty, up_sum, begin, 1)
            down_sum = lax.dynamic_update_slice_in_dim(empty, down_sum, begin, 1)
        up_columns, down_columns = core_up.shape[-1], core_down.shape[-1]
        up_shard = lax.dynamic_slice_in_dim(up_sum, row_index * up_columns, up_columns, 1)
        down_shard = lax.dynamic_slice_in_dim(down_sum, row_index * down_columns, down_columns, 0)
        shard_sums[l] = lax.psum((attn[0], attn[1], up_shard, down_shard), "dp")

    if fast:
        *attn_grads, core_up_grad, core_down_grad, residual_up_grad, residual_down_grad = format_call(
            [full, full_above], [closed, shard_above], qkv_weight.shape[-1]
        )
        attn_grads = [a.transpose(0, 2, 1) for a in attn_grads]
        core_grads = (core_up_grad, core_down_grad.transpose(0, 2, 1))
        at = LAYERS * HEADS
        table_sum = lines[:at, :OFFSETS]
        router_sum = lines[at : at + LAYERS * EXPERTS].reshape(LAYERS, EXPERTS, width)
        at += LAYERS * EXPERTS
        small_sum = lines[at : at + LAYERS * 8].reshape(LAYERS, 8, width)[:, :4]
    else:
        entry = cell_entries()[None, :] + np.array([key_base_of(key) for key in range(WPAD)])[:, None]
        entry = jnp.asarray(np.where(np.arange(WPAD)[:, None] < WINPOS, entry, -1).reshape(-1))
        entry_turned = (entry[:, None] == jnp.arange(OFFSETS)[None, :]).astype(f32)
        table_part = jnp.dot(
            jnp.stack(tables, 0).reshape(LAYERS * HEADS, WPAD * LANES), entry_turned, precision=highest
        )
        small_part = jnp.stack(smalls, 0)[:, :4]
        router_part = jnp.stack(router_parts, 0)[:, :EXPERTS]
        table_sum, small_sum, router_sum = lax.psum((table_part, small_part, router_part), ("dp", "mp"))

        def shard(k):
            return jnp.stack([shard_sums[l][k] for l in range(LAYERS)], 0).astype(f32)

        attn_grads = (shard(0).transpose(0, 2, 1), shard(1).transpose(0, 2, 1))
        core_grads = (shard(2), shard(3).transpose(0, 2, 1))
        residual_up_grad, residual_down_grad = (
            jnp.stack([residual_sums[l][k] for l in range(LAYERS)], 0).astype(f32) for k in range(2)
        )
        residual_up_grad = residual_up_grad[:, None]
        residual_down_grad = residual_down_grad.transpose(0, 2, 1)[:, None]

    return (
        block_output,
        grad,
        attn_grads[0],
        attn_grads[1],
        core_grads[0],
        core_grads[1],
        residual_up_grad,
        residual_down_grad,
        table_sum.reshape(LAYERS, HEADS, OFFSETS).transpose(0, 2, 1),
        router_sum.transpose(0, 2, 1),
        small_sum[:, 0:2],
        small_sum[:, 2:4],
    )


def solution(mesh):
    placed = (
        P(("dp", "mp"), None, None),
        P(None, None, "mp"),
        P(None, None, "mp"),
        P(None, None, "mp"),
        P(None, None, "mp"),
        P(None, "dp", None, None),
        P(None, "dp", None, None),
        P(),
        P(),
        P(),
        P(),
        P(("dp", "mp"), None, None),
        P(("dp", "mp")),
        P(("dp", "mp"), None),
        P(("dp", "mp"), None),
        P(("dp", "mp"), None, None),
    )
    return jax.shard_map(
        per_device,
        mesh=mesh,
        in_specs=placed,
        out_specs=(
            P(("dp", "mp"), None, None),
            P(("dp", "mp"), None, None),
            P(None, None, "mp"),
            P(None, None, "mp"),
            P(None, None, "mp"),
            P(None, None, "mp"),
            P(None, "dp", None, None),
            P(None, "dp", None, None),
            P(),
            P(),
            P(),
            P(),
        ),
        check_vma=False,
    )
```

```python
import functools

import jax
import jax.numpy as jnp
import numpy as np
from jax import lax
from jax.experimental import pallas as pl
from jax.experimental.pallas import tpu as pltpu
from jax.sharding import PartitionSpec as P

HEADS = 12
HEAD_DIM = 32
EXPERTS = 8
WINDOW = 7
GRID = 14
SHIFT = 3
LAYERS = 2
WINPOS = 49
OFFSETS = 169
CAP = 122

WPAD = 64
IMGROWS = 256
PATCHES = 196
SLOTS = 128
ROWS = EXPERTS * SLOTS
LANES = 128
GROUP = 4
PAIRS = 2
TABLE = 256

bf16 = jnp.bfloat16
f32 = jnp.float32
highest = lax.Precision.HIGHEST
norm_epsilon = 1e-05
mask_fill = -100.0
head_scale = HEAD_DIM ** (-0.5)
MESH = pl.DeviceIdType.MESH
MIB = 1024 * 1024


def nn(a, b):
    return lax.dot_general(a, b, (((1,), (0,)), ((), ())), preferred_element_type=f32)


def nt(a, b):
    return lax.dot_general(a, b, (((1,), (1,)), ((), ())), preferred_element_type=f32)


def tn(a, b):
    return lax.dot_general(a, b, (((0,), (0,)), ((), ())), preferred_element_type=f32)


def iota(shape, dim):
    return lax.broadcasted_iota(jnp.int32, shape, dim)


def onehot(flags):
    return jnp.where(flags, 1.0, 0.0).astype(bf16)


def natural_of_row(shifted):
    moved = SHIFT if shifted else 0
    blocks = GRID // WINDOW
    out = -np.ones(IMGROWS, np.int32)
    for window in range(blocks * blocks):
        for cell in range(WINPOS):
            row = (window // blocks * WINDOW + cell // WINDOW + moved) % GRID
            col = (window % blocks * WINDOW + cell % WINDOW + moved) % GRID
            out[window * WPAD + cell] = row * GRID + col
    return out


def key_base_of(key):
    return (2 * WINDOW) * (WINDOW - 1) - (key // WINDOW * (2 * WINDOW - 1) + key % WINDOW)


def enter_table():
    held = natural_of_row(False)
    return (held[:, None] == np.arange(PATCHES)[None, :]).astype(np.float32)


def move_table(shifted):
    first, second = natural_of_row(False), natural_of_row(shifted)
    same = (second[:, None] == first[None, :]) & (second[:, None] >= 0)
    return same.astype(np.float32)


def cell_entries():
    cell = np.arange(LANES) % WPAD
    return np.where(cell < WINPOS, cell // WINDOW * (2 * WINDOW - 1) + cell % WINDOW, -4 * TABLE).astype(np.int32)


def norm_parts(x):
    width = x.shape[-1]
    center = x - jnp.sum(x, -1, keepdims=True) * (1.0 / width)
    spread = jnp.sum(center * center, -1, keepdims=True) * (1.0 / width)
    rstd = lax.rsqrt(spread + norm_epsilon)
    return center * rstd, rstd


def norm_back(grad, gain, xhat, rstd):
    width = xhat.shape[-1]
    dxhat = grad * gain
    mean_one = jnp.sum(dxhat, -1, keepdims=True) * (1.0 / width)
    mean_two = jnp.sum(dxhat * xhat, -1, keepdims=True) * (1.0 / width)
    return rstd * (dxhat - mean_one - xhat * mean_two)


def split_two(x):
    high = x.astype(bf16)
    return high, (x - high.astype(f32)).astype(bf16)


def collect(pos_col, returned_ref):
    pick = onehot(pos_col == iota((pos_col.shape[0], ROWS), 1))
    out = nn(pick, returned_ref[0])
    for piece in range(1, returned_ref.shape[0]):
        out = out + nn(pick, returned_ref[piece])
    return out


def join(ref):
    return ref[...].reshape(ref.shape[0] * ref.shape[1], *ref.shape[2:])


def store(ref, rows):
    ref[...] = rows.reshape(ref.shape).astype(ref.dtype)


def per_image(function, count):
    return jnp.concatenate([function(i) for i in range(count)], 0)


def image_rows(i):
    return slice(i * IMGROWS, (i + 1) * IMGROWS)


def lay_positions(row_ref):
    return jnp.concatenate([row_ref[i, 0:1, :] for i in range(row_ref.shape[0])], 1)


def spread_rows(pos_row, rows_low):
    return nn(onehot(iota((ROWS, pos_row.shape[1]), 0) == pos_row), rows_low)


def route(second_low, router, pos_col):
    logits = nt(second_low, router)
    lane = iota(logits.shape, 1)
    logits = jnp.where(lane < EXPERTS, logits, -1e30)
    expo = jnp.exp(logits - jnp.max(logits, -1, keepdims=True))
    probs = expo / jnp.sum(expo, -1, keepdims=True)
    expert = jnp.where(pos_col >= 0, pos_col // SLOTS, -1)
    chosen = jnp.where(lane == expert, 1.0, 0.0)
    return probs, chosen, jnp.sum(probs * chosen, -1, keepdims=True)


def head_masks():
    rows = iota((LANES, LANES), 0) // HEAD_DIM
    return [onehot(rows == h) for h in range(GROUP)]


def lane_masks():
    lane = iota((WPAD, LANES), 1)
    return [onehot(lane < WPAD), onehot(lane >= WPAD)]


def keys_entry(cells, key_row, turned):
    parts = [cells + (key_base_of(col) - key_row * (2 * WINDOW - 1)) for col in range(WINDOW)]
    return jnp.concatenate(parts, 0 if turned else 1)


def form_bias(bias_ref, table_ref, entry_row):
    layers, heads = bias_ref.shape[:2]
    lines = layers * heads
    bias_ref[...] = jnp.where(iota(bias_ref.shape, 2) < WINPOS, 0.0, -1e30)
    table = table_ref[...]
    high = table.astype(bf16)
    mid, low = split_two(table - high.astype(f32))
    parts = jnp.concatenate([high.astype(f32), mid.astype(f32), low.astype(f32)], 0).astype(bf16)

    def step(key_row, carry):
        pick = onehot(iota((TABLE, WINDOW * LANES), 0) == keys_entry(entry_row, key_row, False))
        rows = nn(parts, pick)
        rows = rows[:lines] + rows[lines : 2 * lines] + rows[2 * lines :]
        for col in range(WINDOW):
            for layer in range(layers):
                part = rows[layer * heads : (layer + 1) * heads, col * LANES : (col + 1) * LANES]
                bias_ref[layer, :, pl.ds(key_row * WINDOW + col, 1), :] = part.reshape(heads, 1, LANES)
        return carry

    lax.fori_loop(0, WINDOW, step, 0)


def table_grad(parts, entry_col):
    heads = parts[0].shape[0]
    lines = heads * len(parts)

    def step(key_row, total):
        keys = [
            jnp.concatenate([ref[:, pl.ds(key_row * WINDOW + col, 1), :].reshape(heads, LANES) for ref in parts], 0)
            for col in range(WINDOW)
        ]
        rows = jnp.concatenate(keys, 1)
        high = rows.astype(bf16).astype(f32)
        both = jnp.concatenate([high, rows - high], 0).astype(bf16)
        entry = keys_entry(entry_col, key_row, True)
        out = nn(both, onehot(iota((WINDOW * LANES, TABLE), 1) == entry))
        return total + out[:lines] + out[lines:]

    return lax.fori_loop(0, WINDOW, step, jnp.zeros((lines, TABLE), f32))


def attention_forward_kernel(first, shifted, mp, gather, *refs):
    refs = list(refs)
    if first:
        patches_ref, enter_ref = refs[:2]
        refs = refs[2:]
    else:
        prev_ref, prev_gate_ref, returned_ref = refs[:3]
        refs = refs[3:]
    (
        valid_ref, col_ref, row_ref, qkv_ref, proj_ref, bias_ref, move_ref, back_ref, gain_ref, nbias_ref, router_ref,
    ) = refs[:11]
    gain_ref, nbias_ref, router_ref = (ref.at[0] for ref in (gain_ref, nbias_ref, router_ref))
    refs = refs[11:]
    if first:
        table_ref, entry_ref = bias_ref, refs.pop(0)
    if gather:
        core_up_ref, core_down_ref = refs[:2]
        refs = refs[2:]
    carried_ref = refs.pop(0)
    if first:
        biases_ref = refs.pop(0)
        bias_ref = biases_ref.at[0]
    else:
        expert_out_ref = refs.pop(0)
        bias_ref = bias_ref.at[0]
    middle_ref, second_ref, gate_ref, buffer_ref, window_ref, qk_ref, v_ref, probs_ref, att_ref, proj_full = refs[:10]
    refs = refs[10:]
    if gather:
        qkv_full = refs.pop(0)
        up_out, down_out = refs[:2]
        refs = refs[2:]
    total_ref = refs.pop(0)
    step = pl.program_id(0)
    final = pl.num_programs(0) - 1
    count, _, width = carried_ref.shape
    if gather:
        shards = [ref.at[0] for ref in (qkv_ref, proj_ref, core_up_ref, core_down_ref)]
        qkv_ref, proj_ref = refs[:2]
        moving = WeightGather(shards, [qkv_ref, proj_ref, up_out, down_out], refs[2:])

        @pl.when(step == 0)
        def _():
            pl.semaphore_wait(moving.row.greet(), 2)
            for k in (0, 1):
                moving.start(k)
            form_bias(biases_ref, table_ref, entry_ref[...])

    pos_col = join(col_ref)[:, 0:1]
    if first:
        x = per_image(lambda i: nn(enter_ref[...], patches_ref[i]), count)
    else:
        expert_out = collect(pos_col, returned_ref)
        store(expert_out_ref, expert_out)
        x = join(prev_ref) + join(prev_gate_ref) * expert_out
    store(carried_ref, x)
    xhat, _ = norm_parts(x)
    normed = (xhat * gain_ref[0:1, :] + nbias_ref[0:1, :]).astype(bf16)
    window_in = per_image(lambda i: nn(move_ref[...], normed[image_rows(i)]), count).astype(bf16)
    store(window_ref, window_in)

    @pl.when(step == 0)
    def _():
        if gather:
            for k in (0, 1):
                moving.forward(k)
            for k in (2, 3):
                moving.start(k)
            for k in (0, 1):
                moving.arrive(k)
            qkv_full[...] = join(qkv_ref)
        elif first:
            form_bias(biases_ref, table_ref, entry_ref[...])
        proj_full[...] = join(proj_ref).astype(f32).T.astype(bf16)
        total_ref[...] = jnp.zeros(total_ref.shape, f32)

    qkv = join(qkv_ref)
    turned = nt(qkv, window_in).astype(bf16)
    straight = nt(window_in, qkv[width:]).astype(bf16)
    for i in range(count):
        qk_ref[i] = turned[: 2 * width, image_rows(i)]
    store(v_ref, straight[:, width:])
    heads_rows = head_masks()
    halves = lane_masks()
    low_lane = iota((WPAD, LANES), 1) < WPAD
    if shifted:
        row_labels = [nt(row_ref[i].astype(f32).astype(bf16), move_ref[...]) for i in range(count)]
        col_labels = [nn(move_ref[...], col_ref[i].astype(f32).astype(bf16)) for i in range(count)]
    for pair in range(PAIRS * count):
        image, side = pair // PAIRS, pair % PAIRS
        across = slice(pair * LANES, (pair + 1) * LANES)
        within = slice(side * LANES, (side + 1) * LANES)
        if shifted:
            ahead = col_labels[image][side * LANES : side * LANES + WPAD, 1:2]
            behind = col_labels[image][side * LANES + WPAD : (side + 1) * LANES, 1:2]
            key_label = jnp.where(low_lane, ahead, behind)
            mask = jnp.where(key_label == row_labels[image][1:2, within], 0.0, mask_fill)
        for group in range(HEADS // GROUP):
            features = slice(group * LANES, (group + 1) * LANES)
            queries = turned[features, across]
            spread = jnp.concatenate([queries * heads_rows[h] for h in range(GROUP)], 1)
            raw = nn(straight[across, features], spread)
            for h in range(GROUP):
                head = group * GROUP + h
                part = raw[:, h * LANES : (h + 1) * LANES]
                scores = jnp.where(low_lane, part[:WPAD], part[WPAD:]) * head_scale + bias_ref[head]
                if shifted:
                    scores = scores + mask
                expo = jnp.exp(scores - jnp.max(scores, 0, keepdims=True))
                probs = (expo * (1.0 / jnp.sum(expo, 0, keepdims=True))).astype(bf16)
                probs_ref[image, side * HEADS + head] = probs
                both = jnp.concatenate([probs * halves[0], probs * halves[1]], 0)
                at = slice(head * HEAD_DIM, (head + 1) * HEAD_DIM)
                values = turned[2 * width + head * HEAD_DIM : 2 * width + (head + 1) * HEAD_DIM, across]
                att_ref[image, at, within] = nn(values, both).astype(bf16)
    attended = per_image(lambda i: nt(back_ref[...], att_ref[i]), count).astype(bf16)
    branch = nt(attended, join(proj_ref))
    middle = x + per_image(lambda i: valid_ref[step * count + i].astype(f32) * branch[image_rows(i)], count)
    store(middle_ref, middle)
    xhat, _ = norm_parts(middle)
    second_low = (xhat * gain_ref[1:2, :] + nbias_ref[1:2, :]).astype(bf16)
    store(second_ref, second_low)
    _, _, gate = route(second_low, router_ref[...], pos_col)
    store(gate_ref, gate)
    total_ref[...] += spread_rows(lay_positions(row_ref), second_low)

    @pl.when(step == final)
    def _():
        buffer_ref[...] = total_ref[...].astype(bf16)
        if gather:
            for k in (2, 3):
                moving.forward(k)
            for k in (2, 3):
                moving.arrive(k)
            for k in range(4):
                moving.sent(k)


def image_spec(array_shape, count):
    rest = tuple(array_shape[1:])
    zeros = (0,) * len(rest)
    return pl.BlockSpec((count,) + rest, lambda i: (i,) + zeros)


def whole_spec(array_shape):
    zeros = (0,) * len(array_shape)
    return pl.BlockSpec(tuple(array_shape), lambda i: zeros)


def image_call(kernel, images, arrays, outs, scratch, name, collective_id=None):
    count = 2 - images % 2

    def spec(kind, shape):
        if isinstance(kind, int):
            rest = tuple(shape[1:])
            return pl.BlockSpec((1,) + rest, lambda i: (kind,) + (0,) * len(rest))
        if kind in ("smem", "any"):
            return pl.BlockSpec(memory_space=pltpu.SMEM if kind == "smem" else pl.ANY)
        return image_spec(shape, count) if kind == "image" else whole_spec(shape)

    return pl.pallas_call(
        kernel,
        grid=(images // count,),
        out_shape=[jax.ShapeDtypeStruct(shape, dtype) for _, shape, dtype in outs],
        in_specs=[spec(kind, array.shape) for kind, array in arrays],
        out_specs=[spec(kind, shape) for kind, shape, _ in outs],
        scratch_shapes=scratch,
        compiler_params=pltpu.CompilerParams(
            vmem_limit_bytes=56 * MIB,
            dimension_semantics=("arbitrary",),
            collective_id=collective_id,
            has_side_effects=collective_id is not None,
        ),
        name=name,
    )(*[array for _, array in arrays])


def send_part(g, expert_out, second_low, router, pos_col, pos_row, logit_ref, router_grad_ref, total_ref):
    probs, chosen, gate = route(second_low, router, pos_col)
    gate_grad = jnp.where(pos_col >= 0, jnp.sum(g * expert_out, -1, keepdims=True), 0.0)
    sent = (gate * g).astype(bf16)
    logit_grad = gate_grad * gate * (chosen - probs)
    store(logit_ref, logit_grad)
    high, low = split_two(logit_grad)
    router_grad_ref[...] += tn(high, second_low) + tn(low, second_low)
    total_ref[...] += spread_rows(pos_row, sent)


def turn_kernel(
    prev_ref, gate_ref, returned_ref, cotangent_ref, enter_ref, leave_ref, col_ref, row_ref, second_ref, router_ref,
    block_ref, grad_ref, logit_ref, router_grad_ref, buffer_ref, total_ref,
):
    step = pl.program_id(0)
    count = cotangent_ref.shape[0]

    @pl.when(step == 0)
    def _():
        total_ref[...] = jnp.zeros(total_ref.shape, f32)
        router_grad_ref[...] = jnp.zeros(router_grad_ref.shape, f32)

    pos_col = join(col_ref)[:, 0:1]
    expert_out = collect(pos_col, returned_ref)
    x = (join(prev_ref) + join(gate_ref) * expert_out).astype(bf16)
    for i in range(count):
        block_ref[i] = nn(leave_ref[...], x[image_rows(i)]).astype(bf16)
    g = per_image(lambda i: nn(enter_ref[...], cotangent_ref[i]), count)
    store(grad_ref, g)
    send_part(
        g, expert_out, join(second_ref), router_ref[0], pos_col, lay_positions(row_ref), logit_ref, router_grad_ref, total_ref
    )

    @pl.when(step == pl.num_programs(0) - 1)
    def _():
        buffer_ref[...] = total_ref[...].astype(bf16)


def attention_backward_kernel(last, dp, mp, fast, *refs):
    (
        valid_ref, grad_ref, returned_ref, logit_ref, middle_ref, carried_ref, router_ref, col_ref, move_ref, back_ref,
        gain_ref, proj_ref, qkv_ref, window_ref, qk_ref, v_ref, probs_ref, att_ref,
    ) = refs[:18]
    refs = refs[18:]
    refs = list(refs)
    if fast:
        units_ref = refs.pop(0)
    if last:
        leave_ref = refs.pop(0)
        if fast:
            table_above, small_above, router_above, router_here, entry_ref, half_above, down_above, attn_above = refs[:8]
            refs = refs[8:]
    else:
        row_ref, expert_out_ref, second_ref, router_next_ref = refs[:4]
        refs = refs[4:]
    out_ref = refs.pop(0)
    closing = None
    if fast and last:
        results, refs = refs[:4], refs[4:]
    else:
        if fast:
            halves_ref = refs.pop(0)
            unit_ref, mine_ref = refs[:2]
        else:
            qkv_grad_ref, proj_grad_ref = refs[:2]
        table_ref, small_ref = refs[2:4]
        refs = refs[4:]
    if not last:
        logit_out_ref, router_grad_ref, buffer_ref = refs[:3]
        refs = refs[3:]
    turned = refs.pop(0)
    if fast:
        qkv_grad_ref, proj_grad_ref = refs[:2]
        refs = refs[2:]
    if not last:
        total_ref = refs.pop(0)
    step = pl.program_id(0)
    final = pl.num_programs(0) - 1
    count, _, width = carried_ref.shape
    if fast:
        row = Row()
        if last:
            table_ref, small_ref, unit_ref, lines_ref = refs[:4]
            landing, refs = refs[4:8], refs[8:]
            above = (half_above, down_above.at[1], attn_above)
            closing = Closing(row, dp, units_ref, unit_ref, lines_ref, above, landing, refs)
        else:
            sums = RowSum(row, blocks(units_ref), refs[0], refs[1], refs[2], blocks(mine_ref), refs[3:7])
            across_x = DeepSum(dp, [mine_ref.at[0]], [refs[7]], [halves_ref], [None], [None], refs[8:10] * 4)

        def take(k):
            if closing:
                closing.take(k)
            else:
                sums.end(k)
                if k == 0:
                    across_x.over_x(k).start()

        @pl.when(step == 0)
        def _():
            if closing:
                closing.enter()
            else:
                barrier = row.greet()
                pl.semaphore_wait(barrier, 2 + across_x.greet(barrier, False))
                for k in range(2):
                    sums.start(k)

    @pl.when(step == 0)
    def _():
        qkv_grad_ref[...] = jnp.zeros(qkv_grad_ref.shape, f32)
        proj_grad_ref[...] = jnp.zeros(proj_grad_ref.shape, f32)
        table_ref[...] = jnp.zeros(table_ref.shape, f32)
        small_ref[...] = jnp.zeros(small_ref.shape, f32)
        if not last:
            total_ref[...] = jnp.zeros(total_ref.shape, f32)
            router_grad_ref[...] = jnp.zeros(router_grad_ref.shape, f32)

    pos_col = join(col_ref)[:, 0:1]
    g = join(grad_ref)
    high, low = split_two(join(logit_ref))
    gain_ref, router = gain_ref.at[0], router_ref[0]
    normed_grad = collect(pos_col, returned_ref) + nn(high, router) + nn(low, router)
    xhat, rstd = norm_parts(join(middle_ref))
    small_ref[1:2, :] += jnp.sum(normed_grad * xhat, 0, keepdims=True)
    small_ref[3:4, :] += jnp.sum(normed_grad, 0, keepdims=True)
    middle_grad = g + norm_back(normed_grad, gain_ref[1:2, :], xhat, rstd)

    def branch_part(i):
        low_part = (valid_ref[step * count + i].astype(f32) * middle_grad[image_rows(i)]).astype(bf16)
        return nn(move_ref[...], low_part)

    branch_grad = per_image(branch_part, count).astype(bf16)
    for i in range(count):
        proj_grad_ref[...] += nn(att_ref[i], branch_grad[image_rows(i)])
    att_grad = nt(proj_ref[...], branch_grad).astype(bf16)
    if fast:

        @pl.when(step == 0)
        def _():
            if closing:
                closing.early()
            else:
                for k in range(2):
                    sums.middle(k)

        pl.when(step == final)(functools.partial(take, 0))

    heads_rows = head_masks()
    halves = lane_masks()
    low_lane = iota((WPAD, LANES), 1) < WPAD
    for pair in range(PAIRS * count):
        image, side = pair // PAIRS, pair % PAIRS
        across = slice(pair * LANES, (pair + 1) * LANES)
        within = slice(side * LANES, (side + 1) * LANES)
        for group in range(HEADS // GROUP):
            features = slice(group * LANES, (group + 1) * LANES)
            grads = att_grad[features, across]
            spread = jnp.concatenate([grads * heads_rows[h] for h in range(GROUP)], 1)
            raw = nn(v_ref[image, within, features], spread)
            for h in range(GROUP):
                head = group * GROUP + h
                at = slice(head * HEAD_DIM, (head + 1) * HEAD_DIM)
                below = slice(width + head * HEAD_DIM, width + (head + 1) * HEAD_DIM)
                lowest = slice(2 * width + head * HEAD_DIM, 2 * width + (head + 1) * HEAD_DIM)
                part = raw[:, h * LANES : (h + 1) * LANES]
                probs_grad = jnp.where(low_lane, part[:WPAD], part[WPAD:])
                probs_low = probs_ref[image, side * HEADS + head]
                probs = probs_low.astype(f32)
                weighted = probs * probs_grad
                scores_grad = weighted - probs * jnp.sum(weighted, 0, keepdims=True)
                table_ref[head] += scores_grad
                scores_low = scores_grad.astype(bf16)
                both = jnp.concatenate([scores_low * halves[0], scores_low * halves[1]], 0)
                probs_both = jnp.concatenate([probs_low * halves[0], probs_low * halves[1]], 0)
                turned[at, across] = (nn(qk_ref[image, below, within], both) * head_scale).astype(bf16)
                turned[below, across] = (nt(qk_ref[image, at, within], both) * head_scale).astype(bf16)
                turned[lowest, across] = nt(att_grad[at, across], probs_both).astype(bf16)
    qkv_grad_ref[...] += nn(turned[...], join(window_ref))
    if fast:

        @pl.when(step == final)
        def _():
            columns, rows = 3 * width // mp, width // mp
            proj_turned = proj_grad_ref[...].T
            for place in range(mp):
                q = quarter_at(place, mp)
                unit_ref[place, :columns] = qkv_grad_ref[q * columns : (q + 1) * columns].astype(bf16)
                unit_ref[place, columns:] = proj_turned[q * rows : (q + 1) * rows].astype(bf16)
            if closing:
                closing.open()
            take(1)
            if closing:
                heads = 2 * HEADS
                lines_ref[...] = jnp.zeros(lines_ref.shape, f32)
                lines_ref[:heads, :TABLE] = table_grad([table_ref, table_above], entry_ref[...])

    mixed_grad = per_image(lambda i: nt(back_ref[...], turned[:, image_rows(i)]), count).astype(bf16)
    first_grad = nn(mixed_grad, qkv_ref[...])
    if closing:

        @pl.when(step == final)
        def _():
            closing.cross()

    xhat, rstd = norm_parts(join(carried_ref))
    small_ref[0:1, :] += jnp.sum(first_grad * xhat, 0, keepdims=True)
    small_ref[2:3, :] += jnp.sum(first_grad, 0, keepdims=True)
    if closing:

        @pl.when(step == final)
        def _():
            heads = 2 * HEADS
            lines_ref[heads : heads + EXPERTS] = router_here[:EXPERTS]
            lines_ref[heads + EXPERTS : heads + 2 * EXPERTS] = router_above[:EXPERTS]
            lines_ref[heads + 2 * EXPERTS : heads + 2 * EXPERTS + 8] = small_ref[...]
            lines_ref[heads + 2 * EXPERTS + 8 : heads + 2 * EXPERTS + 16] = small_above[...]
            closing.send_lines()

    out = middle_grad + norm_back(first_grad, gain_ref[0:1, :], xhat, rstd)
    if last:
        top = out.astype(bf16)
        rest = out - top.astype(f32)
        mid, low = split_two(rest)
        leave = leave_ref[...]
        for i in range(count):
            at = image_rows(i)
            out_ref[i] = nn(leave, top[at]) + nn(leave, mid[at]) + nn(leave, low[at])
    else:
        store(out_ref, out)
        send_part(
            out, join(expert_out_ref), join(second_ref), router_next_ref[0], pos_col, lay_positions(row_ref), logit_out_ref,
            router_grad_ref, total_ref,
        )

    @pl.when(step == final)
    def _():
        if not last:
            buffer_ref[...] = total_ref[...].astype(bf16)
        if closing:
            closing.finish()
            for out, landed in zip(results, landing):
                out[...] = landed[...]
        elif fast:
            across_x.halve(0)
            across_x.over_x(0).wait_send()
            for k in range(2):
                sums.finish(k)


def quarter_at(place, mp):
    return place % (mp // 2) * 2 + place // (mp // 2)


def add_up(*parts):
    total = parts[0].astype(f32)
    for part in parts[1:]:
        total = total + part.astype(f32)
    return total


def to_row(source, target, sems, k, row):
    return pltpu.make_async_remote_copy(
        src_ref=source,
        dst_ref=target,
        send_sem=sems[0].at[k],
        recv_sem=sems[1].at[k],
        device_id={"mp": row},
        device_id_type=MESH,
    )


class Row:
    def __init__(self):
        row = lax.axis_index("mp")
        self.row, self.core, self.y = row, lax.rem(row, 2), lax.div(row, 2)
        self.sibling, self.across = row + 1 - 2 * self.core, row + 2 - 4 * self.y
        self.place = self.core * 2 + self.y
        self.place_across = self.core * 2 + 1 - self.y

    def greet(self):
        barrier = pltpu.get_barrier_semaphore()
        for row in (self.sibling, self.across):
            pl.semaphore_signal(barrier, inc=1, device_id={"mp": row}, device_id_type=MESH)
        return barrier


class RowSum:
    semaphores = 4

    def __init__(self, row, units, core_in, y_out, y_in, mine, sems):
        self.row, self.units, self.mine = row, units, mine
        self.core_in, self.y_out, self.y_in = core_in, y_out, y_in
        self.sems = (sems[:2], sems[2:])

    def pair(self, k):
        theirs = self.units[k].at[pl.ds(2 * (1 - self.row.core), 2)]
        return to_row(theirs, self.core_in.at[k], self.sems[0], k, self.row.sibling)

    def cross(self, k):
        return to_row(self.y_out.at[k], self.y_in.at[k], self.sems[1], k, self.row.across)

    def start(self, k):
        self.pair(k).start()

    def middle(self, k):
        self.pair(k).wait_recv()
        other = 1 - self.row.y
        mixed = add_up(self.units[k][self.row.core * 2 + other], self.core_in[k, other])
        self.y_out[k] = mixed.astype(bf16)
        self.cross(k).start()

    def end(self, k):
        self.cross(k).wait_recv()
        self.mine[k][...] = add_up(
            self.units[k][self.row.place], self.core_in[k, self.row.y], self.y_in[k]
        ).astype(bf16)

    def finish(self, k):
        self.pair(k).wait_send()
        self.cross(k).wait_send()

    @classmethod
    def scratch(cls, count, width):
        return [
            pltpu.VMEM((count, 2, width, width), bf16),
            pltpu.VMEM((count, width, width), bf16),
            pltpu.VMEM((count, width, width), bf16),
        ] + [pltpu.SemaphoreType.DMA((count,))] * cls.semaphores


class RowGather:
    semaphores = 6

    def __init__(self, row, sources, fulls, slot, slot_across, sems):
        self.row, self.sources, self.fulls = row, sources, fulls
        self.slot, self.slot_across = slot, slot_across
        self.sems = (sems[:2], sems[2:4], sems[4:])

    def over(self, k):
        return to_row(self.sources[k], self.fulls[k].at[self.slot], self.sems[0], k, self.row.across)

    def near(self, k):
        return to_row(self.sources[k], self.fulls[k].at[self.slot], self.sems[1], k, self.row.sibling)

    def onward(self, k):
        block = self.fulls[k].at[self.slot_across]
        return to_row(block, block, self.sems[2], k, self.row.sibling)

    def start(self, k):
        self.over(k).start()
        self.near(k).start()

    def forward(self, k):
        self.over(k).wait_recv()
        self.onward(k).start()

    def arrive(self, k):
        self.near(k).wait_recv()
        self.onward(k).wait_recv()

    def sent(self, k):
        self.over(k).wait_send()
        self.near(k).wait_send()
        self.onward(k).wait_send()

    @classmethod
    def scratch(cls, count):
        return [pltpu.SemaphoreType.DMA((count,))] * cls.semaphores


class WeightGather(RowGather):
    def __init__(self, shards, fulls, sems):
        row = Row()
        super().__init__(row, shards, fulls, row.row, row.across, sems[:6])
        self.own_sem = sems[6]

    def own(self, k):
        return pltpu.make_async_copy(self.sources[k], self.fulls[k].at[self.slot], self.own_sem.at[k])

    def start(self, k):
        super().start(k)
        self.own(k).start()

    def arrive(self, k):
        super().arrive(k)
        self.own(k).wait()

    @classmethod
    def scratch(cls, count):
        return super().scratch(count) + [pltpu.SemaphoreType.DMA((count,))]


class DeepSum:
    def __init__(self, dp, total, arrived, halves, slots, result, sems):
        self.total, self.arrived, self.halves, self.slots, self.result = total, arrived, halves, slots, result
        self.x_sems, self.z_sems, self.z_back, self.x_back = (sems[2 * k : 2 * k + 2] for k in range(4))
        me = lax.axis_index("dp")
        self.x, self.z, self.deep = lax.rem(me, 2), lax.div(me, 2), dp // 2
        self.partner = me + 1 - 2 * self.x

    def greet(self, barrier, whole=True):
        pl.semaphore_signal(barrier, inc=1, device_id={"dp": self.partner}, device_id_type=MESH)
        if not whole:
            return 1
        for off in range(1, self.deep):
            peer = lax.rem(self.z + off, self.deep) * 2 + self.x
            pl.semaphore_signal(barrier, inc=1, device_id={"dp": peer}, device_id_type=MESH)
        return self.deep

    def cut(self, k):
        height = self.halves[k].shape[0]
        return height, height // self.deep

    def over_x(self, k):
        height, _ = self.cut(k)
        away = self.total[k].at[pl.ds(pl.multiple_of((1 - self.x) * height, height), height)]
        return to_peer(away, self.arrived[k], self.x_sems[0].at[k], self.x_sems[1].at[k], self.partner)

    def over_z(self, k, off):
        _, piece = self.cut(k)
        to = lax.rem(self.z + off, self.deep)
        part = self.halves[k].at[pl.ds(pl.multiple_of(to * piece, piece), piece)]
        sems = [sem.at[k, off] for sem in self.z_sems]
        return to_peer(part, self.slots[k].at[off], *sems, to * 2 + self.x)

    def own_piece(self, k):
        height, piece = self.cut(k)
        return self.result[k].at[pl.ds(pl.multiple_of(self.x * height + self.z * piece, piece), piece)]

    def own_half(self, k):
        height, _ = self.cut(k)
        return self.result[k].at[pl.ds(pl.multiple_of(self.x * height, height), height)]

    def back_z(self, k, off):
        to = lax.rem(self.z + off, self.deep)
        sems = [sem.at[k, off] for sem in self.z_back]
        return to_peer(self.own_piece(k), self.own_piece(k), *sems, to * 2 + self.x)

    def back_x(self, k):
        return to_peer(self.own_half(k), self.own_half(k), self.x_back[0].at[k], self.x_back[1].at[k], self.partner)

    def halve(self, k):
        self.over_x(k).wait_recv()
        height, _ = self.cut(k)
        keep = self.total[k][pl.ds(pl.multiple_of(self.x * height, height), height)]
        self.halves[k][...] = add_up(keep, self.arrived[k][...]).astype(self.halves[k].dtype)

    def deepen(self, k):
        for off in range(1, self.deep):
            self.over_z(k, off).start()

    def quarter(self, k):
        for off in range(1, self.deep):
            self.over_z(k, off).wait_recv()
        _, piece = self.cut(k)
        keep = self.halves[k][pl.ds(pl.multiple_of(self.z * piece, piece), piece)]
        total = add_up(keep, *[self.slots[k][off] for off in range(1, self.deep)])
        self.own_piece(k)[...] = total.astype(self.result[k].dtype)
        for off in range(1, self.deep):
            self.back_z(k, off).start()

    def widen(self, k):
        for off in range(1, self.deep):
            self.back_z(k, off).wait_recv()
        self.back_x(k).start()

    def finish(self, k, halved=True):
        if halved:
            self.over_x(k).wait_send()
        for off in range(1, self.deep):
            self.over_z(k, off).wait_send()
            self.back_z(k, off).wait_send()
        self.back_x(k).wait()

    @staticmethod
    def semaphores(dp, count):
        one, many = pltpu.SemaphoreType.DMA((count,)), pltpu.SemaphoreType.DMA((count, dp // 2))
        return [one, one, many, many, many, many, one, one]


def blocks(ref):
    return [ref.at[k] for k in range(ref.shape[0])]


class WideSum:
    def __init__(self, dp, total, slots, result, sems):
        self.dp, self.total, self.slots, self.result, self.sems = dp, total, slots, result, sems
        self.me = lax.axis_index("dp")

    def piece(self, ref, at):
        size = ref.shape[0] // self.dp
        return ref.at[pl.ds(pl.multiple_of(at * size, size), size)]

    def out(self, k, p):
        peer = partner_of(self.me, p, self.dp)
        sems = self.sems[0].at[k, p], self.sems[1].at[k, p]
        return to_peer(self.piece(self.total[k], peer), self.slots[k].at[p], *sems, peer)

    def back(self, k, p):
        mine = self.piece(self.result[k], self.me)
        sems = self.sems[2].at[k, p], self.sems[3].at[k, p]
        return to_peer(mine, mine, *sems, partner_of(self.me, p, self.dp))

    def start(self, k):
        for p in range(self.dp - 1, 0, -1):
            self.out(k, p).start()

    def middle(self, k):
        for p in range(1, self.dp):
            self.out(k, p).wait_recv()
        total = add_up(self.piece(self.total[k], self.me)[...], *[self.slots[k][p] for p in range(1, self.dp)])
        self.piece(self.result[k], self.me)[...] = total.astype(self.result[k].dtype)
        for p in range(self.dp - 1, 0, -1):
            self.back(k, p).start()

    def finish(self, k):
        for p in range(1, self.dp):
            self.out(k, p).wait_send()
            self.back(k, p).wait()

    @staticmethod
    def semaphores(dp, count):
        return [pltpu.SemaphoreType.DMA((count, dp))] * 4


class Closing:
    lines = 64

    def __init__(self, row, dp, units_ref, attn_ref, lines_ref, given, results, refs):
        self.row, self.lines_ref, self.dp = row, lines_ref, dp
        self.full, shard, small, above = results
        core_in, y_out, y_in = refs[:3]
        mine, x_in, half, z_in, self.s_core, self.s_one, self.s_y, self.s_mine, s_slots, wide_in = refs[7:17]
        x_above, half_above, z_above = refs[17:20]
        refs_sems, refs = refs[3:7], refs[20:]
        self.mine = mine
        self.sums = RowSum(row, blocks(units_ref) + [attn_ref], core_in, y_out, y_in, blocks(mine), refs_sems)
        self.gather = RowGather(
            row, [mine.at[k] for k in range(2)], blocks(self.full), row.place, row.place_across, refs[:6]
        )
        self.s_pair = to_row(lines_ref, self.s_core, refs[6:8], 0, row.sibling)
        self.s_cross = to_row(self.s_one, self.s_y, refs[8:10], 0, row.across)
        self.here = DeepSum(
            dp, [mine.at[0], mine.at[1]], blocks(x_in), blocks(half), blocks(z_in), [shard.at[0], shard.at[1]], refs[10:18]
        )
        self.above = DeepSum(
            dp, [None, *given[1:]], [None] + blocks(x_above), [given[0]] + blocks(half_above), blocks(z_above), blocks(above),
            refs[18:26],
        )
        self.wide = WideSum(dp, [mine.at[2], self.s_mine], [wide_in, s_slots], [shard.at[2], small], refs[26:30])

    def enter(self):
        greet(self.dp, lax.axis_index("dp"), (self.row.sibling, self.row.across))
        for k in range(2):
            self.sums.start(k)
        self.above.deepen(0)
        for k in (1, 2):
            self.above.over_x(k).start()

    def early(self):
        for k in range(2):
            self.sums.middle(k)
        for k in (1, 2):
            self.above.halve(k)
            self.above.deepen(k)
        self.above.quarter(0)

    def take(self, k):
        self.sums.end(k)
        self.here.over_x(k).start()
        if k == 0:
            self.above.widen(0)
            for j in (1, 2):
                self.above.quarter(j)
        else:
            for j in (1, 2):
                self.above.widen(j)

    def open(self):
        self.sums.start(2)

    def cross(self):
        self.sums.middle(2)
        for k in range(2):
            self.here.halve(k)
            self.here.deepen(k)

    def send_lines(self):
        self.s_pair.start()
        for k in range(2):
            self.here.quarter(k)
        self.s_pair.wait_recv()
        self.s_one[...] = self.lines_ref[...] + self.s_core[...]
        self.s_cross.start()

    def finish(self):
        self.sums.end(2)
        self.wide.start(0)
        self.s_cross.wait_recv()
        self.s_mine[...] = self.s_one[...] + self.s_y[...]
        self.wide.start(1)
        for k in range(2):
            self.gather.start(k)
            self.full[k, self.row.place] = self.mine[k]
        self.wide.middle(0)
        self.wide.middle(1)
        for k in range(2):
            self.here.widen(k)
        for k in range(2):
            self.gather.forward(k)
        self.s_pair.wait_send()
        self.s_cross.wait_send()
        for k in range(3):
            self.sums.finish(k)
            self.above.finish(k, k > 0)
        for k in range(2):
            self.here.finish(k)
            self.wide.finish(k)
            self.gather.arrive(k)
            self.gather.sent(k)

    @classmethod
    def scratch(cls, dp, width):
        deep = dp // 2
        lines = cls.lines
        flat = pltpu.VMEM((lines, width), f32)
        half, slots = (width // 2, width), (deep, width // dp, width)
        return (
            RowSum.scratch(3, width)
            + [
                pltpu.VMEM((3, width, width), bf16),
                pltpu.VMEM((2, *half), bf16),
                pltpu.VMEM((2, *half), bf16),
                pltpu.VMEM((2, *slots), bf16),
                flat, flat, flat, flat,
                pltpu.VMEM((dp, lines // dp, width), f32),
                pltpu.VMEM((dp, width // dp, width), bf16),
                pltpu.VMEM((2, *half), bf16),
                pltpu.VMEM((2, *half), bf16),
                pltpu.VMEM((3, *slots), bf16),
            ]
            + RowGather.scratch(2)
            + [pltpu.SemaphoreType.DMA((1,))] * 4
            + DeepSum.semaphores(dp, 2)
            + DeepSum.semaphores(dp, 3)
            + WideSum.semaphores(dp, 2)
        )


def format_kernel(columns, *refs):
    layers = len(refs[:-6]) // 3
    qkv_out, proj_out, core_up_out, core_down_out, up_out, down_out = refs[-6:]

    def form(ups, downs, shard):
        mp, rows = downs.shape[1], downs.shape[2]
        up_out[0, 0] = ups[0, 0].astype(f32)
        down_out[0, 0] = jnp.concatenate(
            [downs[0, q % 2 * (mp // 2) + q // 2].astype(f32) for q in range(mp)], 0
        ).T
        core_down_out[0] = shard[1, pl.ds(pl.multiple_of(pl.program_id(1) * rows, rows), rows)].astype(f32)

        @pl.when(pl.program_id(1) == 0)
        def _():
            qkv_out[0] = shard[2, :columns].astype(f32)
            proj_out[0] = shard[2, columns:].astype(f32)
            core_up_out[0] = shard[0].astype(f32)

    for layer in range(layers):
        pl.when(pl.program_id(0) == layer)(functools.partial(form, *refs[3 * layer : 3 * layer + 3]))


def format_call(fulls, shards, columns):
    layers = len(fulls)
    _, mp, width, _ = fulls[0].shape
    hidden, rows = mp * width, width // mp
    outs = [
        ((layers, columns, width), None),
        ((layers, width - columns, width), None),
        ((layers, width, width), None),
        ((layers, rows, hidden), pl.BlockSpec((1, rows, width), lambda i, j: (i, 0, j))),
        ((layers, 1, width, hidden), pl.BlockSpec((1, 1, width, width), lambda i, j: (i, 0, 0, j))),
        ((layers, 1, hidden, width), pl.BlockSpec((1, 1, width, width), lambda i, j: (i, 0, j, 0))),
    ]

    def by_layer(shape):
        return pl.BlockSpec((1, *shape[1:]), lambda i, j: (i, 0, 0))

    def chunk(layer, i, j):
        return jnp.where(i == layer, j, jnp.where(i < layer, 0, mp - 1))

    def place(q):
        return lax.rem(q, 2) * (mp // 2) + lax.div(q, 2)

    specs, arrays = [], []
    for layer in range(layers):
        specs += [
            pl.BlockSpec((1, 1, width, width), lambda i, j, at=layer: (0, place(chunk(at, i, j)), 0, 0)),
            pl.BlockSpec((1, mp, rows, width), lambda i, j, at=layer: (1, 0, chunk(at, i, j), 0)),
            pl.BlockSpec((3, width, width), lambda i, j: (0, 0, 0)),
        ]
        arrays += [fulls[layer], fulls[layer], shards[layer]]
    return pl.pallas_call(
        functools.partial(format_kernel, columns),
        grid=(layers, mp),
        out_shape=[jax.ShapeDtypeStruct(shape, f32) for shape, _ in outs],
        in_specs=specs,
        out_specs=[spec or by_layer(shape) for shape, spec in outs],
        compiler_params=pltpu.CompilerParams(vmem_limit_bytes=56 * MIB),
        name="format",
    )(*arrays)


def greet(dp, me, rows=()):
    barrier = pltpu.get_barrier_semaphore()
    for row in rows:
        pl.semaphore_signal(barrier, inc=1, device_id={"mp": row}, device_id_type=MESH)

    def signal(off, carry):
        pl.semaphore_signal(barrier, inc=1, device_id={"dp": lax.rem(me + off, dp)}, device_id_type=MESH)
        return carry

    lax.fori_loop(1, dp, signal, 0)
    pl.semaphore_wait(barrier, dp - 1 + len(rows))


def partner_of(me, p, dp):
    out, bit = 0, 1
    while bit < dp:
        one, two = lax.rem(lax.div(me, bit), 2), lax.rem(lax.div(p, bit), 2)
        out = out + bit * (one + two - 2 * one * two)
        bit *= 2
    return out


def to_peer(source, target, send_sem, recv_sem, peer):
    return pltpu.make_async_remote_copy(
        src_ref=source,
        dst_ref=target,
        send_sem=send_sem,
        recv_sem=recv_sem,
        device_id={"dp": peer},
        device_id_type=MESH,
    )


def gelu_parts(h):
    root = np.float32(np.sqrt(2.0 / np.pi))
    square = h * h
    t = jnp.tanh(root * h * (1.0 + 0.044715 * square))
    half = 0.5 * (1.0 + t)
    slope = half + 0.5 * h * (1.0 - t * t) * root * (1.0 + 3 * 0.044715 * square)
    return h * half, slope


def expert_forward_kernel(dp, mp, layer, gather, *refs):
    refs = list(refs)
    buffer_ref, up_any, down_any, rup_any, rdown_any = refs[:5]
    refs = refs[5:]
    if gather:
        shards = [ref.at[layer + 1] for ref in refs[:4]]
        refs = refs[4:]
    recv_ref, returned_ref, up_eff, down_eff = refs[:4]
    refs = refs[4:]
    if gather:
        fulls = refs[:4]
        refs = refs[4:]
    part, core, up_ref, down_ref, rup_ref, rdown_ref, local = refs[:7]
    refs = refs[7:]
    moving = WeightGather(shards, fulls, refs[:7]) if gather else None
    send_one, recv_one, send_two, recv_two = refs[-4:]
    split = dp // EXPERTS
    me = lax.axis_index("dp")
    loads = [
        pltpu.make_async_copy(source, target, local.at[k])
        for k, (source, target) in enumerate(
            [
                (up_any, up_ref),
                (rup_any.at[layer, 0], rup_ref),
                (down_any, down_ref),
                (rdown_any.at[layer, 0], rdown_ref),
            ]
        )
    ]
    for load in loads:
        load.start()
    greet(dp, me, (moving.row.sibling, moving.row.across) if gather else ())

    def first(off):
        peer = partner_of(me, off, dp)
        return to_peer(
            buffer_ref.at[lax.div(peer, split)], recv_ref.at[me], send_one.at[off], recv_one.at[off], peer
        )

    def second(off):
        source = partner_of(me, off, dp)
        return to_peer(part.at[source], returned_ref.at[me], send_two.at[off], recv_two.at[off], source)

    def start_first(off, carry):
        first(dp - off).start()
        return carry

    lax.fori_loop(1, dp, start_first, 0)
    if gather:
        for k in range(4):
            moving.start(k)
    recv_ref[me] = buffer_ref[lax.div(me, split)]
    hidden = up_eff.shape[1]
    columns = up_ref.shape[-1]
    loads[0].wait()
    loads[1].wait()
    if split == 1 and columns % LANES == 0:
        for m in range(mp):
            at = slice(m * columns, (m + 1) * columns)
            up_eff[:, at] = (up_ref[m].astype(f32) + rup_ref[:, at].astype(f32)).astype(bf16)
    else:
        core[...] = rup_ref[...].astype(f32)
        begin = lax.rem(me, split) * hidden
        for m in range(mp):
            put = onehot(iota((columns, hidden), 0) + m * columns == iota((columns, hidden), 1) + begin)
            core[...] += nn(up_ref[m], put)
        up_eff[...] = core[...].astype(bf16)
    begin = pl.multiple_of(lax.rem(me, split) * hidden, LANES)
    loads[2].wait()
    loads[3].wait()
    core_part = down_ref[:, :, pl.ds(begin, hidden)].reshape(down_eff.shape[1], hidden)
    down_eff[...] = (core_part.astype(f32).T + rdown_ref[...].astype(f32)).astype(bf16)

    def work(source):
        hidden_pre = nn(recv_ref[source], up_eff[...])
        hidden_low = gelu_parts(hidden_pre)[0].astype(bf16)
        return nn(hidden_low, down_eff[...]).astype(bf16)

    returned_ref[me] = work(me)

    def step(off, carry):
        source = partner_of(me, off, dp)
        first(off).wait_recv()
        part[source] = work(source)
        second(off).start()
        return carry

    lax.fori_loop(1, dp, step, 0)
    if gather:
        for k in range(4):
            moving.forward(k)

    def finish(off, carry):
        first(off).wait_send()
        second(off).wait()
        return carry

    lax.fori_loop(1, dp, finish, 0)
    if gather:
        for k in range(4):
            moving.arrive(k)
            moving.sent(k)


def expert_backward_kernel(dp, mp, fast, reduce, *refs):
    refs = list(refs)
    buffer_ref, recv_ref, up_ref, down_ref = refs[:4]
    refs = refs[4:]
    if reduce:
        given_ref, attn_ref = refs[:2]
        refs = refs[2:]
    returned_ref = refs.pop(0)
    if fast:
        units_ref = refs.pop(0)
    else:
        up_term, down_term = refs[:2]
        refs = refs[2:]
    if reduce:
        full_ref, mine_ref = refs[:2]
        refs = refs[2:]
    grads, hidden_low, slope, pre, part = refs[:5]
    refs = refs[5:]
    if fast:
        up_term, down_term = refs[:2]
        refs = refs[2:]
    row = Row() if reduce else None
    if reduce:
        core_in, y_out, y_in = refs[:3]
        sums = RowSum(row, [attn_ref], core_in, y_out, y_in, [mine_ref], refs[3:7])
        gather = RowGather(
            row, [given_ref.at[k] for k in range(2)], [full_ref.at[k] for k in range(2)], row.place, row.place_across,
            refs[7:13],
        )
        refs = refs[13:]
    send_one, recv_one, send_two, recv_two = refs
    split = dp // EXPERTS
    me = lax.axis_index("dp")
    greet(dp, me, (row.sibling, row.across) if reduce else ())

    def first(off):
        peer = partner_of(me, off, dp)
        return to_peer(buffer_ref.at[lax.div(peer, split)], grads.at[me], send_one.at[off], recv_one.at[off], peer)

    def second(off):
        source = partner_of(me, off, dp)
        return to_peer(part.at[source], returned_ref.at[me], send_two.at[off], recv_two.at[off], source)

    def start_first(off, carry):
        first(dp - off).start()
        return carry

    lax.fori_loop(1, dp, start_first, 0)
    if reduce:
        sums.start(0)
        for k in range(2):
            gather.start(k)
    grads[me] = buffer_ref[lax.div(me, split)]

    def again(source, carry):
        value, rate = gelu_parts(nn(recv_ref[source], up_ref[...]))
        hidden_low[source] = value.astype(bf16)
        slope[source] = rate
        return carry

    lax.fori_loop(0, dp, again, 0)
    if reduce:
        sums.middle(0)
        for k in range(2):
            full_ref[k, row.place] = given_ref[k]

    def work(source):
        hidden_grad = nt(grads[source], down_ref[...])
        pre_grad = (slope[source] * hidden_grad).astype(bf16)
        pre[source] = pre_grad
        return nt(pre_grad, up_ref[...]).astype(bf16)

    returned_ref[me] = work(me)

    def step(off, carry):
        source = partner_of(me, off, dp)
        first(off).wait_recv()
        part[source] = work(source)
        second(off).start()
        return carry

    lax.fori_loop(1, dp, step, 0)
    if reduce:
        for k in range(2):
            gather.forward(k)
        sums.end(0)
    up_term[...] = jnp.zeros(up_term.shape, f32)
    down_term[...] = jnp.zeros(down_term.shape, f32)

    def terms(block, carry):
        up_term[...] += tn(recv_ref[block], pre[block])
        down_term[...] += tn(grads[block], hidden_low[block])
        return carry

    lax.fori_loop(0, dp, terms, 0)
    if fast:
        width = up_term.shape[0]
        height = width // mp
        for place in range(mp):
            q = quarter_at(place, mp)
            units_ref[0, place] = up_term[:, q * width : (q + 1) * width].astype(bf16)
            for chunk in range(mp):
                block = down_term[q * height : (q + 1) * height, chunk * width : (chunk + 1) * width]
                units_ref[1, place, chunk * height : (chunk + 1) * height] = block.astype(bf16)

    def finish(off, carry):
        first(off).wait_send()
        second(off).wait()
        return carry

    lax.fori_loop(1, dp, finish, 0)
    if reduce:
        sums.finish(0)
        for k in range(2):
            gather.arrive(k)
            gather.sent(k)


def expert_call(kernel, arrays, outs, scratch, dp, collective_id, name, flops, anys=(), any_outs=()):
    sems = [pltpu.SemaphoreType.DMA((dp,))] * 4
    vmem, anywhere = pl.BlockSpec(memory_space=pltpu.VMEM), pl.BlockSpec(memory_space=pl.ANY)
    return pl.pallas_call(
        kernel,
        out_shape=[jax.ShapeDtypeStruct(shape, dtype) for shape, dtype in (*outs, *any_outs)],
        in_specs=[vmem] * len(arrays) + [anywhere] * len(anys),
        out_specs=[vmem] * len(outs) + [anywhere] * len(any_outs),
        scratch_shapes=scratch + sems,
        compiler_params=pltpu.CompilerParams(
            vmem_limit_bytes=56 * MIB, collective_id=collective_id, has_side_effects=True
        ),
        cost_estimate=pl.CostEstimate(flops=flops, bytes_accessed=20 * MIB, transcendentals=0),
        name=name,
    )(*arrays, *anys)


def by_windows(grid):
    images, kinds = grid.shape[:2]
    blocks = GRID // WINDOW
    grid = grid.reshape(images, kinds, blocks, WINDOW, blocks, WINDOW).transpose(0, 1, 2, 4, 3, 5)
    grid = grid.reshape(images, kinds, blocks * blocks, WINPOS)
    grid = jnp.pad(grid, ((0, 0), (0, 0), (0, 0), (0, WPAD - WINPOS)), constant_values=-1)
    return grid.reshape(images, kinds, IMGROWS)


def per_device(
    patches,
    qkv_weight,
    proj_weight,
    core_up,
    core_down,
    residual_up,
    residual_down,
    position_bias,
    router_weight,
    norm_gain,
    norm_bias,
    cotangent,
    image_valid,
    expert_index,
    slot_index,
    region_id,
):
    dp, mp = lax.axis_size("dp"), lax.axis_size("mp")
    images, _, width = patches.shape
    split = dp // EXPERTS
    hidden = residual_up.shape[-1]
    hidden_full = core_up.shape[-1] * mp
    row_index = lax.axis_index("mp")

    fast = split == 1 and dp == 8 and mp == 4 and hidden == mp * width
    qkv_rows, proj_rows, down_rows = (a.transpose(0, 2, 1) for a in (qkv_weight, proj_weight, core_down))
    shards = (qkv_rows, proj_rows, core_up, down_rows)
    gathered = [[None] * len(shards)] * LAYERS
    if not fast:
        gathered = [[lax.all_gather(a[l], "mp", axis=0, tiled=False) for a in shards] for l in range(LAYERS)]

    position = jnp.where(slot_index >= 0, expert_index * SLOTS + slot_index, -1)
    row_form = by_windows(jnp.stack([position.reshape(images, GRID, GRID), region_id], 1))
    col_form = row_form.transpose(0, 2, 1)
    enter = jnp.asarray(enter_table(), bf16)
    leave = jnp.asarray(enter_table().T, bf16)
    moves = [jnp.asarray(move_table(l % 2 == 1), bf16) for l in range(LAYERS)]
    backs = [jnp.asarray(move_table(l % 2 == 1).T, bf16) for l in range(LAYERS)]
    table_rows = position_bias.transpose(0, 2, 1).reshape(LAYERS * HEADS, OFFSETS)
    table_rows = jnp.pad(table_rows, ((0, 0), (0, TABLE - OFFSETS)))
    entry_row, entry_col = jnp.asarray(cell_entries()[None, :]), jnp.asarray(cell_entries()[:, None])
    routers = jnp.pad(router_weight.transpose(0, 2, 1), ((0, 0), (0, LANES - EXPERTS), (0, 0)))

    token = (images, IMGROWS, width)
    buffer_shape = (ROWS, width)
    block_rows = (dp, SLOTS, width)
    pieces = (split, ROWS, width)

    def by_piece(returned):
        return returned.reshape(EXPERTS, split, SLOTS, width).transpose(1, 0, 2, 3).reshape(pieces)

    records = []
    before = None
    for l in range(LAYERS):
        first = l == 0
        gather = fast and first
        if first:
            arrays = [("image", patches), ("whole", enter)]
        else:
            arrays = [("image", before[0]), ("image", before[1]), ("whole", before[2])]
        arrays += [
            ("smem", image_valid),
            ("image", col_form),
            ("image", row_form),
            ("any", qkv_rows) if gather else ("whole", gathered[l][0]),
            ("any", proj_rows) if gather else ("whole", gathered[l][1]),
            ("whole", table_rows) if first else (l, biases),
            ("whole", moves[l]),
            ("whole", backs[l]),
            (l, norm_gain),
            (l, norm_bias),
            (l, routers),
        ]
        if first:
            arrays.append(("whole", entry_row))
        if gather:
            arrays += [("any", core_up), ("any", down_rows)]
        outs = [("image", token, f32)]
        if first:
            outs.append(("whole", (LAYERS, HEADS, WPAD, LANES), f32))
        else:
            outs.append(("image", token, f32))
        outs += [
            ("image", token, f32),
            ("image", token, bf16),
            ("image", (images, IMGROWS, 1), f32),
            ("whole", buffer_shape, bf16),
            ("image", token, bf16),
            ("image", (images, 2 * width, IMGROWS), bf16),
            ("image", token, bf16),
            ("image", (images, PAIRS * HEADS, WPAD, LANES), bf16),
            ("image", (images, width, IMGROWS), bf16),
            ("whole", (width, width), bf16),
        ]
        scratch = [pltpu.VMEM(buffer_shape, f32)]
        gathered_shapes = [(mp, *a.shape[1:]) for a in shards]
        if gather:
            outs.append(("whole", (3 * width, width), bf16))
            outs += [("any", shape, bf16) for shape in gathered_shapes[2:]]
            scratch += [pltpu.VMEM(shape, bf16) for shape in gathered_shapes[:2]] + WeightGather.scratch(4)
        results = list(
            image_call(
                functools.partial(attention_forward_kernel, first, l % 2 == 1, mp, gather),
                images, arrays, outs, scratch, f"attend_{l}", 3 * LAYERS + 1 if gather else None,
            )
        )
        if gather:
            gathered[l] = [results[-3], None] + results[-2:]
            results = results[:-3]
        carried = results.pop(0)
        if first:
            biases = results.pop(0)
        else:
            records[-1]["expert_out"] = results.pop(0)
        middle, second_low, gate, buffer = results[:4]
        gather = fast and l < LAYERS - 1
        received, returned, up_eff, down_eff, *more = expert_call(
            functools.partial(expert_forward_kernel, dp, mp, l, gather),
            [buffer.reshape(EXPERTS, SLOTS, width)],
            [
                (block_rows, bf16),
                (block_rows, bf16),
                ((width, hidden), bf16),
                ((hidden, width), bf16),
            ],
            [
                pltpu.VMEM(block_rows, bf16),
                pltpu.VMEM((8, LANES) if fast else (width, hidden), f32),
                pltpu.VMEM(gathered_shapes[2], bf16),
                pltpu.VMEM(gathered_shapes[3], bf16),
                pltpu.VMEM((width, hidden), bf16),
                pltpu.VMEM((hidden, width), bf16),
                pltpu.SemaphoreType.DMA((4,)),
            ]
            + (WeightGather.scratch(4) if gather else []),
            dp, l, f"experts_{l}", 4 * dp * SLOTS * width * hidden,
            [gathered[l][2], gathered[l][3], residual_up, residual_down, *(shards if gather else ())],
            [(shape, bf16) for shape in gathered_shapes] if gather else (),
        )
        if gather:
            gathered[l + 1] = more
        returned = by_piece(returned)
        before = (middle, gate, returned)
        records.append(
            dict(
                carried=carried, middle=middle, second_low=second_low, gate=gate, saved=results[4:], received=received,
                up_eff=up_eff, down_eff=down_eff,
            )
        )

    top = records[-1]
    block_output, grad, logit_grad, router_part, buffer = image_call(
        turn_kernel,
        images,
        [
            ("image", before[0]),
            ("image", before[1]),
            ("whole", before[2]),
            ("image", cotangent),
            ("whole", enter),
            ("whole", leave),
            ("image", col_form),
            ("image", row_form),
            ("image", top["second_low"]),
            (LAYERS - 1, routers),
        ],
        [
            ("image", patches.shape, bf16),
            ("image", token, f32),
            ("image", (images, IMGROWS, LANES), f32),
            ("whole", (LANES, width), f32),
            ("whole", buffer_shape, bf16),
        ],
        [pltpu.VMEM(buffer_shape, f32)],
        "turn",
    )
    router_parts, tables, smalls = [None] * LAYERS, [None] * LAYERS, [None] * LAYERS
    residual_sums, shard_sums = [None] * LAYERS, [None] * LAYERS
    router_parts[LAYERS - 1] = router_part
    units, attn_units, mines = [None] * LAYERS, [None] * LAYERS, [None] * LAYERS
    for l in reversed(range(LAYERS)):
        rec = records[l]
        last = l == 0
        reduce = fast and l < LAYERS - 1
        arrays = [buffer.reshape(EXPERTS, SLOTS, width), rec["received"], rec["up_eff"], rec["down_eff"]]
        outs = [(block_rows, bf16)]
        scratch = [
            pltpu.VMEM(block_rows, bf16),
            pltpu.VMEM((dp, SLOTS, hidden), bf16),
            pltpu.VMEM((dp, SLOTS, hidden), f32),
            pltpu.VMEM((dp, SLOTS, hidden), bf16),
            pltpu.VMEM(block_rows, bf16),
        ]
        if fast:
            outs.append(((2, mp, width, width), bf16))
            scratch += [pltpu.VMEM((width, hidden), f32)] * 2
        else:
            outs += [((width, hidden), f32)] * 2
        if reduce:
            arrays += [mines[l + 1], attn_units[l + 1]]
            outs += [((2, mp, width, width), bf16), ((width, width), bf16)]
            scratch += RowSum.scratch(1, width) + RowGather.scratch(2)
        results = list(
            expert_call(
                functools.partial(expert_backward_kernel, dp, mp, fast, reduce), arrays, outs, scratch, dp, LAYERS + l,
                f"experts_back_{l}", 10 * dp * SLOTS * width * hidden,
            )
        )
        returned_grad = results.pop(0)
        if fast:
            units[l] = results.pop(0)
        else:
            residual_sums[l] = lax.psum(tuple(t.astype(bf16) for t in results[:2]), "mp")
        if reduce:
            full_above, mine_above = results
        window_in, qk, v, probs, att, proj_full = rec["saved"]
        qkv_full = gathered[l][0].reshape(3 * width, width)
        arrays = [
            ("smem", image_valid),
            ("image", grad),
            ("whole", by_piece(returned_grad)),
            ("image", logit_grad),
            ("image", rec["middle"]),
            ("image", rec["carried"]),
            (l, routers),
            ("image", col_form),
            ("whole", moves[l]),
            ("whole", backs[l]),
            (l, norm_gain),
            ("whole", proj_full),
            ("whole", qkv_full),
            ("image", window_in),
            ("image", qk),
            ("image", v),
            ("image", probs),
            ("image", att),
        ]
        outs = [("image", patches.shape if last else token, f32)]
        scratch = [pltpu.VMEM((3 * width, (2 - images % 2) * IMGROWS), bf16)]
        closes = fast and last
        table_shape, small_shape = (HEADS, WPAD, LANES), (8, width)
        if fast:
            arrays.append(("whole", units[l]))
            scratch += [pltpu.VMEM((3 * width, width), f32), pltpu.VMEM((width, width), f32)]
        if closes:
            outs += [
                ("whole", (2, mp, width, width), bf16),
                ("whole", (3, width, width), bf16),
                ("whole", (Closing.lines, width), f32),
                ("whole", (3, width, width), bf16),
            ]
        else:
            if fast:
                outs += [
                    ("whole", (width // 2, width), bf16),
                    ("whole", (mp, width, width), bf16),
                    ("whole", (2, width, width), bf16),
                ]
            else:
                outs += [("whole", (3 * width, width), f32), ("whole", (width, width), f32)]
            outs += [("whole", table_shape, f32), ("whole", small_shape, f32)]
        if last:
            arrays.append(("whole", leave))
            if fast:
                arrays += [
                    ("whole", a)
                    for a in (
                        tables[1], smalls[1], router_parts[1], router_parts[0], entry_col, halves_above, mines[1],
                        mine_above,
                    )
                ]
        else:
            below = records[l - 1]
            arrays += [
                ("image", row_form),
                ("image", below["expert_out"]),
                ("image", below["second_low"]),
                (l - 1, routers),
            ]
            outs += [
                ("image", (images, IMGROWS, LANES), f32),
                ("whole", (LANES, width), f32),
                ("whole", buffer_shape, bf16),
            ]
            scratch.append(pltpu.VMEM(buffer_shape, f32))
        if closes:
            scratch += [
                pltpu.VMEM(table_shape, f32),
                pltpu.VMEM(small_shape, f32),
                pltpu.VMEM((mp, width, width), bf16),
                pltpu.VMEM((Closing.lines, width), f32),
            ]
            scratch += [pltpu.VMEM(shape, dtype) for _, shape, dtype in outs[1:5]] + Closing.scratch(dp, width)
        elif fast:
            scratch += RowSum.scratch(2, width) + [pltpu.VMEM((width // 2, width), bf16)]
            scratch += [pltpu.SemaphoreType.DMA((1,))] * 2
        results = list(
            image_call(
                functools.partial(attention_backward_kernel, last, dp, mp, fast),
                images, arrays, outs, scratch, f"attend_back_{l}", 2 * LAYERS + 1 + l if fast else None,
            )
        )
        grad = results.pop(0)
        if closes:
            full, closed, lines, shard_above = results
            continue
        if fast:
            halves_above = results.pop(0)
            attn_units[l], mines[l] = results[:2]
        else:
            qkv_part, proj_part = results[:2]
        tables[l], smalls[l] = results[2:4]
        if not last:
            logit_grad, router_parts[l - 1], buffer = results[4:]
        if fast:
            continue
        attn = (
            lax.psum_scatter(qkv_part.astype(bf16), "mp", scatter_dimension=0, tiled=True),
            lax.psum_scatter(proj_part.T.astype(bf16), "mp", scatter_dimension=0, tiled=True),
        )
        up_sum, down_sum = residual_sums[l]
        if split > 1:
            begin = lax.axis_index("dp") % split * hidden
            empty = jnp.zeros((width, hidden_full), bf16)
            up_sum = lax.dynamic_update_slice_in_dim(empty, up_sum, begin, 1)
            down_sum = lax.dynamic_update_slice_in_dim(empty, down_sum, begin, 1)
        up_columns, down_columns = core_up.shape[-1], core_down.shape[-1]
        up_shard = lax.dynamic_slice_in_dim(up_sum, row_index * up_columns, up_columns, 1)
        down_shard = lax.dynamic_slice_in_dim(down_sum, row_index * down_columns, down_columns, 0)
        shard_sums[l] = lax.psum((attn[0], attn[1], up_shard, down_shard), "dp")

    if fast:
        *attn_grads, core_up_grad, core_down_grad, residual_up_grad, residual_down_grad = format_call(
            [full, full_above], [closed, shard_above], qkv_weight.shape[-1]
        )
        attn_grads = [a.transpose(0, 2, 1) for a in attn_grads]
        core_grads = (core_up_grad, core_down_grad.transpose(0, 2, 1))
        at = LAYERS * HEADS
        table_sum = lines[:at, :OFFSETS]
        router_sum = lines[at : at + LAYERS * EXPERTS].reshape(LAYERS, EXPERTS, width)
        at += LAYERS * EXPERTS
        small_sum = lines[at : at + LAYERS * 8].reshape(LAYERS, 8, width)[:, :4]
    else:
        entry = cell_entries()[None, :] + np.array([key_base_of(key) for key in range(WPAD)])[:, None]
        entry = jnp.asarray(np.where(np.arange(WPAD)[:, None] < WINPOS, entry, -1).reshape(-1))
        entry_turned = (entry[:, None] == jnp.arange(OFFSETS)[None, :]).astype(f32)
        table_part = jnp.dot(
            jnp.stack(tables, 0).reshape(LAYERS * HEADS, WPAD * LANES), entry_turned, precision=highest
        )
        small_part = jnp.stack(smalls, 0)[:, :4]
        router_part = jnp.stack(router_parts, 0)[:, :EXPERTS]
        table_sum, small_sum, router_sum = lax.psum((table_part, small_part, router_part), ("dp", "mp"))

        def shard(k):
            return jnp.stack([shard_sums[l][k] for l in range(LAYERS)], 0).astype(f32)

        attn_grads = (shard(0).transpose(0, 2, 1), shard(1).transpose(0, 2, 1))
        core_grads = (shard(2), shard(3).transpose(0, 2, 1))
        residual_up_grad, residual_down_grad = (
            jnp.stack([residual_sums[l][k] for l in range(LAYERS)], 0).astype(f32) for k in range(2)
        )
        residual_up_grad = residual_up_grad[:, None]
        residual_down_grad = residual_down_grad.transpose(0, 2, 1)[:, None]

    return (
        block_output,
        grad,
        attn_grads[0],
        attn_grads[1],
        core_grads[0],
        core_grads[1],
        residual_up_grad,
        residual_down_grad,
        table_sum.reshape(LAYERS, HEADS, OFFSETS).transpose(0, 2, 1),
        router_sum.transpose(0, 2, 1),
        small_sum[:, 0:2],
        small_sum[:, 2:4],
    )


def solution(mesh):
    placed = (
        P(("dp", "mp"), None, None),
        P(None, None, "mp"),
        P(None, None, "mp"),
        P(None, None, "mp"),
        P(None, None, "mp"),
        P(None, "dp", None, None),
        P(None, "dp", None, None),
        P(),
        P(),
        P(),
        P(),
        P(("dp", "mp"), None, None),
        P(("dp", "mp")),
        P(("dp", "mp"), None),
        P(("dp", "mp"), None),
        P(("dp", "mp"), None, None),
    )
    return jax.shard_map(
        per_device,
        mesh=mesh,
        in_specs=placed,
        out_specs=(
            P(("dp", "mp"), None, None),
            P(("dp", "mp"), None, None),
            P(None, None, "mp"),
            P(None, None, "mp"),
            P(None, None, "mp"),
            P(None, None, "mp"),
            P(None, "dp", None, None),
            P(None, "dp", None, None),
            P(),
            P(),
            P(),
            P(),
        ),
        check_vma=False,
    )
```

```python
import functools

import jax
import jax.numpy as jnp
import numpy as np
from jax import lax
from jax.experimental import pallas as pl
from jax.experimental.pallas import tpu as pltpu
from jax.sharding import PartitionSpec as P

HEADS = 12
HEAD_DIM = 32
EXPERTS = 8
WINDOW = 7
GRID = 14
SHIFT = 3
LAYERS = 2
WINPOS = 49
OFFSETS = 169
CAP = 122

WPAD = 64
IMGROWS = 256
PATCHES = 196
SLOTS = 128
ROWS = EXPERTS * SLOTS
LANES = 128
GROUP = 4
PAIRS = 2
TABLE = 256

bf16 = jnp.bfloat16
f32 = jnp.float32
highest = lax.Precision.HIGHEST
norm_epsilon = 1e-05
mask_fill = -100.0
head_scale = HEAD_DIM ** (-0.5)
MESH = pl.DeviceIdType.MESH
MIB = 1024 * 1024


def nn(a, b):
    return lax.dot_general(a, b, (((1,), (0,)), ((), ())), preferred_element_type=f32)


def nt(a, b):
    return lax.dot_general(a, b, (((1,), (1,)), ((), ())), preferred_element_type=f32)


def tn(a, b):
    return lax.dot_general(a, b, (((0,), (0,)), ((), ())), preferred_element_type=f32)


def iota(shape, dim):
    return lax.broadcasted_iota(jnp.int32, shape, dim)


def onehot(flags):
    return jnp.where(flags, 1.0, 0.0).astype(bf16)


def natural_of_row(shifted):
    moved = SHIFT if shifted else 0
    blocks = GRID // WINDOW
    out = -np.ones(IMGROWS, np.int32)
    for window in range(blocks * blocks):
        for cell in range(WINPOS):
            row = (window // blocks * WINDOW + cell // WINDOW + moved) % GRID
            col = (window % blocks * WINDOW + cell % WINDOW + moved) % GRID
            out[window * WPAD + cell] = row * GRID + col
    return out


def key_base_of(key):
    return (2 * WINDOW) * (WINDOW - 1) - (key // WINDOW * (2 * WINDOW - 1) + key % WINDOW)


def enter_table():
    held = natural_of_row(False)
    return (held[:, None] == np.arange(PATCHES)[None, :]).astype(np.float32)


def move_table(shifted):
    first, second = natural_of_row(False), natural_of_row(shifted)
    same = (second[:, None] == first[None, :]) & (second[:, None] >= 0)
    return same.astype(np.float32)


def cell_entries():
    cell = np.arange(LANES) % WPAD
    return np.where(cell < WINPOS, cell // WINDOW * (2 * WINDOW - 1) + cell % WINDOW, -4 * TABLE).astype(np.int32)


def norm_parts(x):
    width = x.shape[-1]
    center = x - jnp.sum(x, -1, keepdims=True) * (1.0 / width)
    spread = jnp.sum(center * center, -1, keepdims=True) * (1.0 / width)
    rstd = lax.rsqrt(spread + norm_epsilon)
    return center * rstd, rstd


def norm_back(grad, gain, xhat, rstd):
    width = xhat.shape[-1]
    dxhat = grad * gain
    mean_one = jnp.sum(dxhat, -1, keepdims=True) * (1.0 / width)
    mean_two = jnp.sum(dxhat * xhat, -1, keepdims=True) * (1.0 / width)
    return rstd * (dxhat - mean_one - xhat * mean_two)


def turn_blocks(x):
    size = x.shape[0]
    same = onehot(iota((size, size), 0) == iota((size, size), 1))
    return jnp.concatenate([nt(same, x[:, at : at + size]) for at in range(0, x.shape[1], size)], 0)


def split_two(x):
    high = x.astype(bf16)
    return high, (x - high.astype(f32)).astype(bf16)


def collect(pos_col, returned_ref):
    pick = onehot(pos_col == iota((pos_col.shape[0], ROWS), 1))
    out = nn(pick, returned_ref[0])
    for piece in range(1, returned_ref.shape[0]):
        out = out + nn(pick, returned_ref[piece])
    return out


def join(ref):
    return ref[...].reshape(ref.shape[0] * ref.shape[1], *ref.shape[2:])


def store(ref, rows):
    ref[...] = rows.reshape(ref.shape).astype(ref.dtype)


def per_image(function, count):
    return jnp.concatenate([function(i) for i in range(count)], 0)


def image_rows(i):
    return slice(i * IMGROWS, (i + 1) * IMGROWS)


def lay_positions(row_ref):
    return jnp.concatenate([row_ref[i, 0:1, :] for i in range(row_ref.shape[0])], 1)


def spread_rows(pos_row, rows_low):
    return nn(onehot(iota((ROWS, pos_row.shape[1]), 0) == pos_row), rows_low)


def route(second_low, router, pos_col):
    logits = nt(second_low, router)
    lane = iota(logits.shape, 1)
    logits = jnp.where(lane < EXPERTS, logits, -1e30)
    expo = jnp.exp(logits - jnp.max(logits, -1, keepdims=True))
    probs = expo / jnp.sum(expo, -1, keepdims=True)
    expert = jnp.where(pos_col >= 0, pos_col // SLOTS, -1)
    chosen = jnp.where(lane == expert, 1.0, 0.0)
    return probs, chosen, jnp.sum(probs * chosen, -1, keepdims=True)


def head_masks():
    rows = iota((LANES, LANES), 0) // HEAD_DIM
    return [onehot(rows == h) for h in range(GROUP)]


def lane_masks():
    lane = iota((WPAD, LANES), 1)
    return [onehot(lane < WPAD), onehot(lane >= WPAD)]


def keys_entry(cells, key_row, turned):
    parts = [cells + (key_base_of(col) - key_row * (2 * WINDOW - 1)) for col in range(WINDOW)]
    return jnp.concatenate(parts, 0 if turned else 1)


def form_bias(bias_ref, table_ref, entry_row):
    layers, heads = bias_ref.shape[:2]
    lines = layers * heads
    bias_ref[...] = jnp.where(iota(bias_ref.shape, 2) < WINPOS, 0.0, -1e30)
    table = table_ref[...]
    high = table.astype(bf16)
    mid, low = split_two(table - high.astype(f32))
    parts = jnp.concatenate([high.astype(f32), mid.astype(f32), low.astype(f32)], 0).astype(bf16)

    def step(key_row, carry):
        pick = onehot(iota((TABLE, WINDOW * LANES), 0) == keys_entry(entry_row, key_row, False))
        rows = nn(parts, pick)
        rows = rows[:lines] + rows[lines : 2 * lines] + rows[2 * lines :]
        for col in range(WINDOW):
            for layer in range(layers):
                part = rows[layer * heads : (layer + 1) * heads, col * LANES : (col + 1) * LANES]
                bias_ref[layer, :, pl.ds(key_row * WINDOW + col, 1), :] = part.reshape(heads, 1, LANES)
        return carry

    lax.fori_loop(0, WINDOW, step, 0)


def table_grad(parts, entry_col):
    heads = parts[0].shape[0]
    lines = heads * len(parts)

    def step(key_row, total):
        keys = [
            jnp.concatenate([ref[:, pl.ds(key_row * WINDOW + col, 1), :].reshape(heads, LANES) for ref in parts], 0)
            for col in range(WINDOW)
        ]
        rows = jnp.concatenate(keys, 1)
        high = rows.astype(bf16).astype(f32)
        both = jnp.concatenate([high, rows - high], 0).astype(bf16)
        entry = keys_entry(entry_col, key_row, True)
        out = nn(both, onehot(iota((WINDOW * LANES, TABLE), 1) == entry))
        return total + out[:lines] + out[lines:]

    return lax.fori_loop(0, WINDOW, step, jnp.zeros((lines, TABLE), f32))


def attention_forward_kernel(first, shifted, mp, gather, *refs):
    refs = list(refs)
    if first:
        patches_ref, enter_ref = refs[:2]
        refs = refs[2:]
    else:
        prev_ref, prev_gate_ref, returned_ref = refs[:3]
        refs = refs[3:]
    (
        valid_ref, col_ref, row_ref, qkv_ref, proj_ref, bias_ref, move_ref, back_ref, gain_ref, nbias_ref, router_ref,
    ) = refs[:11]
    gain_ref, nbias_ref, router_ref = (ref.at[0] for ref in (gain_ref, nbias_ref, router_ref))
    refs = refs[11:]
    if first:
        table_ref, entry_ref = bias_ref, refs.pop(0)
    if gather:
        core_up_ref, core_down_ref = refs[:2]
        refs = refs[2:]
    carried_ref = refs.pop(0)
    if first:
        biases_ref = refs.pop(0)
        bias_ref = biases_ref.at[0]
    else:
        expert_out_ref = refs.pop(0)
        bias_ref = bias_ref.at[0]
    middle_ref, second_ref, gate_ref, buffer_ref, window_ref, qk_ref, v_ref, probs_ref, att_ref, proj_full = refs[:10]
    refs = refs[10:]
    if gather:
        qkv_full = refs.pop(0)
        up_out, down_out = refs[:2]
        refs = refs[2:]
    total_ref = refs.pop(0)
    step = pl.program_id(0)
    final = pl.num_programs(0) - 1
    count, _, width = carried_ref.shape
    if gather:
        shards = [ref.at[0] for ref in (qkv_ref, proj_ref, core_up_ref, core_down_ref)]
        qkv_ref, proj_ref = refs[:2]
        moving = WeightGather(shards, [qkv_ref, proj_ref, up_out, down_out], refs[2:])

        @pl.when(step == 0)
        def _():
            pl.semaphore_wait(moving.row.greet(), 2)
            for k in (0, 1):
                moving.start(k)
            form_bias(biases_ref, table_ref, entry_ref[...])

    pos_col = join(col_ref)[:, 0:1]
    if first:
        x = per_image(lambda i: nn(enter_ref[...], patches_ref[i]), count)
    else:
        expert_out = collect(pos_col, returned_ref)
        store(expert_out_ref, expert_out)
        x = join(prev_ref) + join(prev_gate_ref) * expert_out
    store(carried_ref, x)
    xhat, _ = norm_parts(x)
    normed = (xhat * gain_ref[0:1, :] + nbias_ref[0:1, :]).astype(bf16)
    window_in = per_image(lambda i: nn(move_ref[...], normed[image_rows(i)]), count).astype(bf16)
    store(window_ref, window_in)

    @pl.when(step == 0)
    def _():
        if gather:
            for k in (0, 1):
                moving.forward(k)
            for k in (2, 3):
                moving.start(k)
            for k in (0, 1):
                moving.arrive(k)
            qkv_full[...] = join(qkv_ref)
        elif first:
            form_bias(biases_ref, table_ref, entry_ref[...])
        proj_full[...] = turn_blocks(join(proj_ref)).astype(bf16)
        total_ref[...] = jnp.zeros(total_ref.shape, f32)

    qkv = join(qkv_ref)
    turned = nt(qkv, window_in).astype(bf16)
    straight = nt(window_in, qkv[width:]).astype(bf16)
    for i in range(count):
        qk_ref[i] = turned[: 2 * width, image_rows(i)]
    store(v_ref, straight[:, width:])
    heads_rows = head_masks()
    halves = lane_masks()
    low_lane = iota((WPAD, LANES), 1) < WPAD
    if shifted:
        row_labels = [nt(row_ref[i].astype(f32).astype(bf16), move_ref[...]) for i in range(count)]
        col_labels = [nn(move_ref[...], col_ref[i].astype(f32).astype(bf16)) for i in range(count)]
    for pair in range(PAIRS * count):
        image, side = pair // PAIRS, pair % PAIRS
        across = slice(pair * LANES, (pair + 1) * LANES)
        within = slice(side * LANES, (side + 1) * LANES)
        if shifted:
            ahead = col_labels[image][side * LANES : side * LANES + WPAD, 1:2]
            behind = col_labels[image][side * LANES + WPAD : (side + 1) * LANES, 1:2]
            key_label = jnp.where(low_lane, ahead, behind)
            mask = jnp.where(key_label == row_labels[image][1:2, within], 0.0, mask_fill)
        for group in range(HEADS // GROUP):
            features = slice(group * LANES, (group + 1) * LANES)
            queries = turned[features, across]
            spread = jnp.concatenate([queries * heads_rows[h] for h in range(GROUP)], 1)
            raw = nn(straight[across, features], spread)
            for h in range(GROUP):
                head = group * GROUP + h
                part = raw[:, h * LANES : (h + 1) * LANES]
                scores = jnp.where(low_lane, part[:WPAD], part[WPAD:]) * head_scale + bias_ref[head]
                if shifted:
                    scores = scores + mask
                expo = jnp.exp(scores - jnp.max(scores, 0, keepdims=True))
                probs = (expo * (1.0 / jnp.sum(expo, 0, keepdims=True))).astype(bf16)
                probs_ref[image, side * HEADS + head] = probs
                both = jnp.concatenate([probs * halves[0], probs * halves[1]], 0)
                at = slice(head * HEAD_DIM, (head + 1) * HEAD_DIM)
                values = turned[2 * width + head * HEAD_DIM : 2 * width + (head + 1) * HEAD_DIM, across]
                att_ref[image, at, within] = nn(values, both).astype(bf16)
    attended = per_image(lambda i: nt(back_ref[...], att_ref[i]), count).astype(bf16)
    branch = nt(attended, join(proj_ref))
    middle = x + per_image(lambda i: valid_ref[step * count + i].astype(f32) * branch[image_rows(i)], count)
    store(middle_ref, middle)
    xhat, _ = norm_parts(middle)
    second_low = (xhat * gain_ref[1:2, :] + nbias_ref[1:2, :]).astype(bf16)
    store(second_ref, second_low)
    _, _, gate = route(second_low, router_ref[...], pos_col)
    store(gate_ref, gate)
    total_ref[...] += spread_rows(lay_positions(row_ref), second_low)

    @pl.when(step == final)
    def _():
        buffer_ref[...] = total_ref[...].astype(bf16)
        if gather:
            for k in (2, 3):
                moving.forward(k)
            for k in (2, 3):
                moving.arrive(k)
            for k in range(4):
                moving.sent(k)


def image_spec(array_shape, count):
    rest = tuple(array_shape[1:])
    zeros = (0,) * len(rest)
    return pl.BlockSpec((count,) + rest, lambda i: (i,) + zeros)


def whole_spec(array_shape):
    zeros = (0,) * len(array_shape)
    return pl.BlockSpec(tuple(array_shape), lambda i: zeros)


def image_call(kernel, images, arrays, outs, scratch, name, collective_id=None):
    count = 2 - images % 2

    def spec(kind, shape):
        if isinstance(kind, int):
            rest = tuple(shape[1:])
            return pl.BlockSpec((1,) + rest, lambda i: (kind,) + (0,) * len(rest))
        if kind in ("smem", "any"):
            return pl.BlockSpec(memory_space=pltpu.SMEM if kind == "smem" else pl.ANY)
        return image_spec(shape, count) if kind == "image" else whole_spec(shape)

    return pl.pallas_call(
        kernel,
        grid=(images // count,),
        out_shape=[jax.ShapeDtypeStruct(shape, dtype) for _, shape, dtype in outs],
        in_specs=[spec(kind, array.shape) for kind, array in arrays],
        out_specs=[spec(kind, shape) for kind, shape, _ in outs],
        scratch_shapes=scratch,
        compiler_params=pltpu.CompilerParams(
            vmem_limit_bytes=56 * MIB,
            dimension_semantics=("arbitrary",),
            collective_id=collective_id,
            has_side_effects=collective_id is not None,
        ),
        name=name,
    )(*[array for _, array in arrays])


def send_part(g, expert_out, second_low, router, pos_col, pos_row, logit_ref, router_grad_ref, total_ref):
    probs, chosen, gate = route(second_low, router, pos_col)
    gate_grad = jnp.where(pos_col >= 0, jnp.sum(g * expert_out, -1, keepdims=True), 0.0)
    sent = (gate * g).astype(bf16)
    logit_grad = gate_grad * gate * (chosen - probs)
    store(logit_ref, logit_grad)
    high, low = split_two(logit_grad)
    router_grad_ref[...] += tn(high, second_low) + tn(low, second_low)
    total_ref[...] += spread_rows(pos_row, sent)


def turn_kernel(
    prev_ref, gate_ref, returned_ref, cotangent_ref, enter_ref, leave_ref, col_ref, row_ref, second_ref, router_ref,
    block_ref, grad_ref, logit_ref, router_grad_ref, buffer_ref, total_ref,
):
    step = pl.program_id(0)
    count = cotangent_ref.shape[0]

    @pl.when(step == 0)
    def _():
        total_ref[...] = jnp.zeros(total_ref.shape, f32)
        router_grad_ref[...] = jnp.zeros(router_grad_ref.shape, f32)

    pos_col = join(col_ref)[:, 0:1]
    expert_out = collect(pos_col, returned_ref)
    x = (join(prev_ref) + join(gate_ref) * expert_out).astype(bf16)
    for i in range(count):
        block_ref[i] = nn(leave_ref[...], x[image_rows(i)]).astype(bf16)
    g = per_image(lambda i: nn(enter_ref[...], cotangent_ref[i]), count)
    store(grad_ref, g)
    send_part(
        g, expert_out, join(second_ref), router_ref[0], pos_col, lay_positions(row_ref), logit_ref, router_grad_ref, total_ref
    )

    @pl.when(step == pl.num_programs(0) - 1)
    def _():
        buffer_ref[...] = total_ref[...].astype(bf16)


def attention_backward_kernel(last, dp, mp, fast, *refs):
    (
        valid_ref, grad_ref, returned_ref, logit_ref, middle_ref, carried_ref, router_ref, col_ref, move_ref, back_ref,
        gain_ref, proj_ref, qkv_ref, window_ref, qk_ref, v_ref, probs_ref, att_ref,
    ) = refs[:18]
    refs = refs[18:]
    refs = list(refs)
    if fast:
        units_ref = refs.pop(0)
    if last:
        leave_ref = refs.pop(0)
        if fast:
            table_above, small_above, router_above, router_here, entry_ref, half_above, down_above, attn_above = refs[:8]
            refs = refs[8:]
    else:
        row_ref, expert_out_ref, second_ref, router_next_ref = refs[:4]
        refs = refs[4:]
    out_ref = refs.pop(0)
    closing = None
    if fast and last:
        results, refs = refs[:4], refs[4:]
    else:
        if fast:
            halves_ref = refs.pop(0)
            unit_ref, mine_ref = refs[:2]
        else:
            qkv_grad_ref, proj_grad_ref = refs[:2]
        table_ref, small_ref = refs[2:4]
        refs = refs[4:]
    if not last:
        logit_out_ref, router_grad_ref, buffer_ref = refs[:3]
        refs = refs[3:]
    turned = refs.pop(0)
    if fast:
        qkv_grad_ref, proj_grad_ref = refs[:2]
        refs = refs[2:]
    if not last:
        total_ref = refs.pop(0)
    step = pl.program_id(0)
    final = pl.num_programs(0) - 1
    count, _, width = carried_ref.shape
    if fast:
        row = Row()
        if last:
            table_ref, small_ref, unit_ref, lines_ref = refs[:4]
            landing, refs = refs[4:8], refs[8:]
            above = (half_above, down_above.at[1], attn_above)
            closing = Closing(row, dp, units_ref, unit_ref, lines_ref, above, landing, refs)
            sums = closing.sums
        else:
            sums = RowSum(row, blocks(units_ref), refs[0], refs[1], refs[2], blocks(mine_ref), refs[3:7])
            across_x = DeepSum(dp, [mine_ref.at[0]], [refs[7]], [halves_ref], [None], [None], refs[8:10] * 4)

        def take(k):
            if closing:
                closing.take(k)
            else:
                sums.end(k)
                if k == 0:
                    across_x.over_x(k).start()

        @pl.when(step == 0)
        def _():
            if closing:
                closing.enter()
            else:
                barrier = row.greet()
                pl.semaphore_wait(barrier, 2 + across_x.greet(barrier, False))
                for k in range(2):
                    sums.start(k)

    @pl.when(step == 0)
    def _():
        qkv_grad_ref[...] = jnp.zeros(qkv_grad_ref.shape, f32)
        proj_grad_ref[...] = jnp.zeros(proj_grad_ref.shape, f32)
        table_ref[...] = jnp.zeros(table_ref.shape, f32)
        small_ref[...] = jnp.zeros(small_ref.shape, f32)
        if not last:
            total_ref[...] = jnp.zeros(total_ref.shape, f32)
            router_grad_ref[...] = jnp.zeros(router_grad_ref.shape, f32)

    pos_col = join(col_ref)[:, 0:1]
    g = join(grad_ref)
    high, low = split_two(join(logit_ref))
    gain_ref, router = gain_ref.at[0], router_ref[0]
    normed_grad = collect(pos_col, returned_ref) + nn(high, router) + nn(low, router)
    xhat, rstd = norm_parts(join(middle_ref))
    small_ref[1:2, :] += jnp.sum(normed_grad * xhat, 0, keepdims=True)
    small_ref[3:4, :] += jnp.sum(normed_grad, 0, keepdims=True)
    middle_grad = g + norm_back(normed_grad, gain_ref[1:2, :], xhat, rstd)

    if fast:

        @pl.when(step == 0)
        def _():
            for k in range(2):
                sums.middle(k)

    def branch_part(i):
        low_part = (valid_ref[step * count + i].astype(f32) * middle_grad[image_rows(i)]).astype(bf16)
        return nn(move_ref[...], low_part)

    branch_grad = per_image(branch_part, count).astype(bf16)
    for i in range(count):
        proj_grad_ref[...] += nn(att_ref[i], branch_grad[image_rows(i)])
    att_grad = nt(proj_ref[...], branch_grad).astype(bf16)
    if fast:

        @pl.when(step == 0)
        def _():
            if closing:
                closing.early()

        pl.when(step == final)(functools.partial(take, 0))

    heads_rows = head_masks()
    halves = lane_masks()
    low_lane = iota((WPAD, LANES), 1) < WPAD
    for pair in range(PAIRS * count):
        image, side = pair // PAIRS, pair % PAIRS
        across = slice(pair * LANES, (pair + 1) * LANES)
        within = slice(side * LANES, (side + 1) * LANES)
        for group in range(HEADS // GROUP):
            features = slice(group * LANES, (group + 1) * LANES)
            grads = att_grad[features, across]
            spread = jnp.concatenate([grads * heads_rows[h] for h in range(GROUP)], 1)
            raw = nn(v_ref[image, within, features], spread)
            for h in range(GROUP):
                head = group * GROUP + h
                at = slice(head * HEAD_DIM, (head + 1) * HEAD_DIM)
                below = slice(width + head * HEAD_DIM, width + (head + 1) * HEAD_DIM)
                lowest = slice(2 * width + head * HEAD_DIM, 2 * width + (head + 1) * HEAD_DIM)
                part = raw[:, h * LANES : (h + 1) * LANES]
                probs_grad = jnp.where(low_lane, part[:WPAD], part[WPAD:])
                probs_low = probs_ref[image, side * HEADS + head]
                probs = probs_low.astype(f32)
                weighted = probs * probs_grad
                scores_grad = weighted - probs * jnp.sum(weighted, 0, keepdims=True)
                table_ref[head] += scores_grad
                scores_low = scores_grad.astype(bf16)
                both = jnp.concatenate([scores_low * halves[0], scores_low * halves[1]], 0)
                probs_both = jnp.concatenate([probs_low * halves[0], probs_low * halves[1]], 0)
                turned[at, across] = (nn(qk_ref[image, below, within], both) * head_scale).astype(bf16)
                turned[below, across] = (nt(qk_ref[image, at, within], both) * head_scale).astype(bf16)
                turned[lowest, across] = nt(att_grad[at, across], probs_both).astype(bf16)
    qkv_grad_ref[...] += nn(turned[...], join(window_ref))
    if fast:

        @pl.when(step == final)
        def _():
            columns, rows = 3 * width // mp, width // mp
            proj_turned = turn_blocks(proj_grad_ref[...].astype(bf16)).astype(bf16)
            for place in range(mp):
                q = quarter_at(place, mp)
                unit_ref[place, :columns] = qkv_grad_ref[q * columns : (q + 1) * columns].astype(bf16)
                unit_ref[place, columns:] = proj_turned[q * rows : (q + 1) * rows]
            if closing:
                closing.open()
            take(1)
            if closing:
                heads = 2 * HEADS
                lines_ref[...] = jnp.zeros(lines_ref.shape, f32)
                lines_ref[:heads, :TABLE] = table_grad([table_ref, table_above], entry_ref[...])

    mixed_grad = per_image(lambda i: nt(back_ref[...], turned[:, image_rows(i)]), count).astype(bf16)
    first_grad = nn(mixed_grad, qkv_ref[...])
    if closing:

        @pl.when(step == final)
        def _():
            closing.cross()

    xhat, rstd = norm_parts(join(carried_ref))
    small_ref[0:1, :] += jnp.sum(first_grad * xhat, 0, keepdims=True)
    small_ref[2:3, :] += jnp.sum(first_grad, 0, keepdims=True)
    if closing:

        @pl.when(step == final)
        def _():
            heads = 2 * HEADS
            lines_ref[heads : heads + EXPERTS] = router_here[:EXPERTS]
            lines_ref[heads + EXPERTS : heads + 2 * EXPERTS] = router_above[:EXPERTS]
            lines_ref[heads + 2 * EXPERTS : heads + 2 * EXPERTS + 8] = small_ref[...]
            lines_ref[heads + 2 * EXPERTS + 8 : heads + 2 * EXPERTS + 16] = small_above[...]
            closing.send_lines()

    out = middle_grad + norm_back(first_grad, gain_ref[0:1, :], xhat, rstd)
    if last:
        top = out.astype(bf16)
        rest = out - top.astype(f32)
        mid, low = split_two(rest)
        leave = leave_ref[...]
        for i in range(count):
            at = image_rows(i)
            out_ref[i] = nn(leave, top[at]) + nn(leave, mid[at]) + nn(leave, low[at])
    else:
        store(out_ref, out)
        send_part(
            out, join(expert_out_ref), join(second_ref), router_next_ref[0], pos_col, lay_positions(row_ref), logit_out_ref,
            router_grad_ref, total_ref,
        )

    @pl.when(step == final)
    def _():
        if not last:
            buffer_ref[...] = total_ref[...].astype(bf16)
        if closing:
            closing.finish()
            for out, landed in zip(results, landing):
                out[...] = landed[...]
        elif fast:
            across_x.halve(0)
            across_x.over_x(0).wait_send()
            for k in range(2):
                sums.finish(k)


def quarter_at(place, mp):
    return place % (mp // 2) * 2 + place // (mp // 2)


def add_up(*parts):
    total = parts[0].astype(f32)
    for part in parts[1:]:
        total = total + part.astype(f32)
    return total


def to_row(source, target, sems, k, row):
    return pltpu.make_async_remote_copy(
        src_ref=source,
        dst_ref=target,
        send_sem=sems[0].at[k],
        recv_sem=sems[1].at[k],
        device_id={"mp": row},
        device_id_type=MESH,
    )


class Row:
    def __init__(self):
        row = lax.axis_index("mp")
        self.row, self.core, self.y = row, lax.rem(row, 2), lax.div(row, 2)
        self.sibling, self.across = row + 1 - 2 * self.core, row + 2 - 4 * self.y
        self.place = self.core * 2 + self.y
        self.place_across = self.core * 2 + 1 - self.y

    def greet(self):
        barrier = pltpu.get_barrier_semaphore()
        for row in (self.sibling, self.across):
            pl.semaphore_signal(barrier, inc=1, device_id={"mp": row}, device_id_type=MESH)
        return barrier


class RowSum:
    semaphores = 4

    def __init__(self, row, units, core_in, y_out, y_in, mine, sems):
        self.row, self.units, self.mine = row, units, mine
        self.core_in, self.y_out, self.y_in = core_in, y_out, y_in
        self.sems = (sems[:2], sems[2:])

    def pair(self, k):
        theirs = self.units[k].at[pl.ds(2 * (1 - self.row.core), 2)]
        return to_row(theirs, self.core_in.at[k], self.sems[0], k, self.row.sibling)

    def cross(self, k):
        return to_row(self.y_out.at[k], self.y_in.at[k], self.sems[1], k, self.row.across)

    def start(self, k):
        self.pair(k).start()

    def middle(self, k):
        self.pair(k).wait_recv()
        other = 1 - self.row.y
        mixed = add_up(self.units[k][self.row.core * 2 + other], self.core_in[k, other])
        self.y_out[k] = mixed.astype(bf16)
        self.cross(k).start()

    def end(self, k):
        self.cross(k).wait_recv()
        self.mine[k][...] = add_up(
            self.units[k][self.row.place], self.core_in[k, self.row.y], self.y_in[k]
        ).astype(bf16)

    def finish(self, k):
        self.pair(k).wait_send()
        self.cross(k).wait_send()

    @classmethod
    def scratch(cls, count, width):
        return [
            pltpu.VMEM((count, 2, width, width), bf16),
            pltpu.VMEM((count, width, width), bf16),
            pltpu.VMEM((count, width, width), bf16),
        ] + [pltpu.SemaphoreType.DMA((count,))] * cls.semaphores


class RowGather:
    semaphores = 6

    def __init__(self, row, sources, fulls, slot, slot_across, sems):
        self.row, self.sources, self.fulls = row, sources, fulls
        self.slot, self.slot_across = slot, slot_across
        self.sems = (sems[:2], sems[2:4], sems[4:])

    def over(self, k):
        return to_row(self.sources[k], self.fulls[k].at[self.slot], self.sems[0], k, self.row.across)

    def near(self, k):
        return to_row(self.sources[k], self.fulls[k].at[self.slot], self.sems[1], k, self.row.sibling)

    def onward(self, k):
        block = self.fulls[k].at[self.slot_across]
        return to_row(block, block, self.sems[2], k, self.row.sibling)

    def start(self, k):
        self.over(k).start()
        self.near(k).start()

    def forward(self, k):
        self.over(k).wait_recv()
        self.onward(k).start()

    def arrive(self, k):
        self.near(k).wait_recv()
        self.onward(k).wait_recv()

    def sent(self, k):
        self.over(k).wait_send()
        self.near(k).wait_send()
        self.onward(k).wait_send()

    @classmethod
    def scratch(cls, count):
        return [pltpu.SemaphoreType.DMA((count,))] * cls.semaphores


class WeightGather(RowGather):
    def __init__(self, shards, fulls, sems):
        row = Row()
        super().__init__(row, shards, fulls, row.row, row.across, sems[:6])
        self.own_sem = sems[6]

    def own(self, k):
        return pltpu.make_async_copy(self.sources[k], self.fulls[k].at[self.slot], self.own_sem.at[k])

    def start(self, k):
        super().start(k)
        self.own(k).start()

    def arrive(self, k):
        super().arrive(k)
        self.own(k).wait()

    @classmethod
    def scratch(cls, count):
        return super().scratch(count) + [pltpu.SemaphoreType.DMA((count,))]


class DeepSum:
    def __init__(self, dp, total, arrived, halves, slots, result, sems):
        self.total, self.arrived, self.halves, self.slots, self.result = total, arrived, halves, slots, result
        self.x_sems, self.z_sems, self.z_back, self.x_back = (sems[2 * k : 2 * k + 2] for k in range(4))
        me = lax.axis_index("dp")
        self.x, self.z, self.deep = lax.rem(me, 2), lax.div(me, 2), dp // 2
        self.partner = me + 1 - 2 * self.x

    def greet(self, barrier, whole=True):
        pl.semaphore_signal(barrier, inc=1, device_id={"dp": self.partner}, device_id_type=MESH)
        if not whole:
            return 1
        for off in range(1, self.deep):
            peer = lax.rem(self.z + off, self.deep) * 2 + self.x
            pl.semaphore_signal(barrier, inc=1, device_id={"dp": peer}, device_id_type=MESH)
        return self.deep

    def cut(self, k):
        height = self.halves[k].shape[0]
        return height, height // self.deep

    def over_x(self, k):
        height, _ = self.cut(k)
        away = self.total[k].at[pl.ds(pl.multiple_of((1 - self.x) * height, height), height)]
        return to_peer(away, self.arrived[k], self.x_sems[0].at[k], self.x_sems[1].at[k], self.partner)

    def over_z(self, k, off):
        _, piece = self.cut(k)
        to = lax.rem(self.z + off, self.deep)
        part = self.halves[k].at[pl.ds(pl.multiple_of(to * piece, piece), piece)]
        sems = [sem.at[k, off] for sem in self.z_sems]
        return to_peer(part, self.slots[k].at[off], *sems, to * 2 + self.x)

    def own_piece(self, k):
        height, piece = self.cut(k)
        return self.result[k].at[pl.ds(pl.multiple_of(self.x * height + self.z * piece, piece), piece)]

    def own_half(self, k):
        height, _ = self.cut(k)
        return self.result[k].at[pl.ds(pl.multiple_of(self.x * height, height), height)]

    def back_z(self, k, off):
        to = lax.rem(self.z + off, self.deep)
        sems = [sem.at[k, off] for sem in self.z_back]
        return to_peer(self.own_piece(k), self.own_piece(k), *sems, to * 2 + self.x)

    def back_x(self, k):
        return to_peer(self.own_half(k), self.own_half(k), self.x_back[0].at[k], self.x_back[1].at[k], self.partner)

    def halve(self, k):
        self.over_x(k).wait_recv()
        height, _ = self.cut(k)
        keep = self.total[k][pl.ds(pl.multiple_of(self.x * height, height), height)]
        self.halves[k][...] = add_up(keep, self.arrived[k][...]).astype(self.halves[k].dtype)

    def deepen(self, k):
        for off in range(1, self.deep):
            self.over_z(k, off).start()

    def quarter(self, k):
        for off in range(1, self.deep):
            self.over_z(k, off).wait_recv()
        _, piece = self.cut(k)
        keep = self.halves[k][pl.ds(pl.multiple_of(self.z * piece, piece), piece)]
        total = add_up(keep, *[self.slots[k][off] for off in range(1, self.deep)])
        self.own_piece(k)[...] = total.astype(self.result[k].dtype)
        for off in range(1, self.deep):
            self.back_z(k, off).start()

    def widen(self, k):
        for off in range(1, self.deep):
            self.back_z(k, off).wait_recv()
        self.back_x(k).start()

    def finish(self, k, halved=True):
        if halved:
            self.over_x(k).wait_send()
        for off in range(1, self.deep):
            self.over_z(k, off).wait_send()
            self.back_z(k, off).wait_send()
        self.back_x(k).wait()

    @staticmethod
    def semaphores(dp, count):
        one, many = pltpu.SemaphoreType.DMA((count,)), pltpu.SemaphoreType.DMA((count, dp // 2))
        return [one, one, many, many, many, many, one, one]


def blocks(ref):
    return [ref.at[k] for k in range(ref.shape[0])]


class WideSum:
    def __init__(self, dp, total, slots, result, sems):
        self.dp, self.total, self.slots, self.result, self.sems = dp, total, slots, result, sems
        self.me = lax.axis_index("dp")

    def piece(self, ref, at):
        size = ref.shape[0] // self.dp
        return ref.at[pl.ds(pl.multiple_of(at * size, size), size)]

    def out(self, k, p):
        peer = partner_of(self.me, p, self.dp)
        sems = self.sems[0].at[k, p], self.sems[1].at[k, p]
        return to_peer(self.piece(self.total[k], peer), self.slots[k].at[p], *sems, peer)

    def back(self, k, p):
        mine = self.piece(self.result[k], self.me)
        sems = self.sems[2].at[k, p], self.sems[3].at[k, p]
        return to_peer(mine, mine, *sems, partner_of(self.me, p, self.dp))

    def start(self, k):
        for p in range(self.dp - 1, 0, -1):
            self.out(k, p).start()

    def middle(self, k):
        for p in range(1, self.dp):
            self.out(k, p).wait_recv()
        total = add_up(self.piece(self.total[k], self.me)[...], *[self.slots[k][p] for p in range(1, self.dp)])
        self.piece(self.result[k], self.me)[...] = total.astype(self.result[k].dtype)
        for p in range(self.dp - 1, 0, -1):
            self.back(k, p).start()

    def finish(self, k):
        for p in range(1, self.dp):
            self.out(k, p).wait_send()
            self.back(k, p).wait()

    @staticmethod
    def semaphores(dp, count):
        return [pltpu.SemaphoreType.DMA((count, dp))] * 4


class Closing:
    lines = 64

    def __init__(self, row, dp, units_ref, attn_ref, lines_ref, given, results, refs):
        self.row, self.lines_ref, self.dp = row, lines_ref, dp
        self.full, shard, small, above = results
        core_in, y_out, y_in = refs[:3]
        mine, x_in, half, z_in, self.s_core, self.s_one, self.s_y, self.s_mine, s_slots, wide_in = refs[7:17]
        x_above, half_above, z_above = refs[17:20]
        refs_sems, refs = refs[3:7], refs[20:]
        self.mine = mine
        self.sums = RowSum(row, blocks(units_ref) + [attn_ref], core_in, y_out, y_in, blocks(mine), refs_sems)
        self.gather = RowGather(
            row, [mine.at[k] for k in range(2)], blocks(self.full), row.place, row.place_across, refs[:6]
        )
        self.s_pair = to_row(lines_ref, self.s_core, refs[6:8], 0, row.sibling)
        self.s_cross = to_row(self.s_one, self.s_y, refs[8:10], 0, row.across)
        self.here = DeepSum(
            dp, [mine.at[0], mine.at[1]], blocks(x_in), blocks(half), blocks(z_in), [shard.at[0], shard.at[1]], refs[10:18]
        )
        self.above = DeepSum(
            dp, [None, *given[1:]], [None] + blocks(x_above), [given[0]] + blocks(half_above), blocks(z_above), blocks(above),
            refs[18:26],
        )
        self.wide = WideSum(dp, [mine.at[2], self.s_mine], [wide_in, s_slots], [shard.at[2], small], refs[26:30])

    def enter(self):
        greet(self.dp, lax.axis_index("dp"), (self.row.sibling, self.row.across))
        for k in range(2):
            self.sums.start(k)
        self.above.deepen(0)
        for k in (1, 2):
            self.above.over_x(k).start()

    def early(self):
        for k in (1, 2):
            self.above.halve(k)
            self.above.deepen(k)
        self.above.quarter(0)

    def take(self, k):
        self.sums.end(k)
        self.here.over_x(k).start()
        self.gather.start(k)
        self.full[k, self.row.place] = self.mine[k]
        if k == 0:
            self.above.widen(0)
            for j in (1, 2):
                self.above.quarter(j)
        else:
            for j in (1, 2):
                self.above.widen(j)

    def open(self):
        self.sums.start(2)

    def cross(self):
        self.sums.middle(2)
        for k in range(2):
            self.here.halve(k)
            self.here.deepen(k)
        self.gather.forward(0)

    def send_lines(self):
        self.s_pair.start()
        for k in range(2):
            self.here.quarter(k)
        self.s_pair.wait_recv()
        self.s_one[...] = self.lines_ref[...] + self.s_core[...]
        self.s_cross.start()

    def finish(self):
        self.sums.end(2)
        self.wide.start(0)
        self.s_cross.wait_recv()
        self.s_mine[...] = self.s_one[...] + self.s_y[...]
        self.wide.start(1)
        self.gather.forward(1)
        for k in range(2):
            self.here.widen(k)
        self.wide.middle(0)
        self.wide.middle(1)
        self.s_pair.wait_send()
        self.s_cross.wait_send()
        for k in range(3):
            self.sums.finish(k)
            self.above.finish(k, k > 0)
        for k in range(2):
            self.here.finish(k)
            self.wide.finish(k)
            self.gather.arrive(k)
            self.gather.sent(k)

    @classmethod
    def scratch(cls, dp, width):
        deep = dp // 2
        lines = cls.lines
        flat = pltpu.VMEM((lines, width), f32)
        half, slots = (width // 2, width), (deep, width // dp, width)
        return (
            RowSum.scratch(3, width)
            + [
                pltpu.VMEM((3, width, width), bf16),
                pltpu.VMEM((2, *half), bf16),
                pltpu.VMEM((2, *half), bf16),
                pltpu.VMEM((2, *slots), bf16),
                flat, flat, flat, flat,
                pltpu.VMEM((dp, lines // dp, width), f32),
                pltpu.VMEM((dp, width // dp, width), bf16),
                pltpu.VMEM((2, *half), bf16),
                pltpu.VMEM((2, *half), bf16),
                pltpu.VMEM((3, *slots), bf16),
            ]
            + RowGather.scratch(2)
            + [pltpu.SemaphoreType.DMA((1,))] * 4
            + DeepSum.semaphores(dp, 2)
            + DeepSum.semaphores(dp, 3)
            + WideSum.semaphores(dp, 2)
        )


def format_kernel(columns, *refs):
    layers = len(refs[:-6]) // 3
    qkv_out, proj_out, core_up_out, core_down_out, up_out, down_out = refs[-6:]

    def form(ups, downs, shard):
        mp, rows = downs.shape[1], downs.shape[2]
        up_out[0, 0] = ups[0, 0].astype(f32)
        down_out[0, 0] = turn_blocks(
            jnp.concatenate([downs[0, q % 2 * (mp // 2) + q // 2] for q in range(mp)], 0)
        )
        core_down_out[0] = shard[1, pl.ds(pl.multiple_of(pl.program_id(1) * rows, rows), rows)].astype(f32)

        @pl.when(pl.program_id(1) == 0)
        def _():
            qkv_out[0] = shard[2, :columns].astype(f32)
            proj_out[0] = shard[2, columns:].astype(f32)
            core_up_out[0] = shard[0].astype(f32)

    for layer in range(layers):
        pl.when(pl.program_id(0) == layer)(functools.partial(form, *refs[3 * layer : 3 * layer + 3]))


def format_call(fulls, shards, columns):
    layers = len(fulls)
    _, mp, width, _ = fulls[0].shape
    hidden, rows = mp * width, width // mp
    outs = [
        ((layers, columns, width), None),
        ((layers, width - columns, width), None),
        ((layers, width, width), None),
        ((layers, rows, hidden), pl.BlockSpec((1, rows, width), lambda i, j: (i, 0, j))),
        ((layers, 1, width, hidden), pl.BlockSpec((1, 1, width, width), lambda i, j: (i, 0, 0, j))),
        ((layers, 1, hidden, width), pl.BlockSpec((1, 1, width, width), lambda i, j: (i, 0, j, 0))),
    ]

    def by_layer(shape):
        return pl.BlockSpec((1, *shape[1:]), lambda i, j: (i, 0, 0))

    def chunk(layer, i, j):
        return jnp.where(i == layer, j, jnp.where(i < layer, 0, mp - 1))

    def place(q):
        return lax.rem(q, 2) * (mp // 2) + lax.div(q, 2)

    specs, arrays = [], []
    for layer in range(layers):
        specs += [
            pl.BlockSpec((1, 1, width, width), lambda i, j, at=layer: (0, place(chunk(at, i, j)), 0, 0)),
            pl.BlockSpec((1, mp, rows, width), lambda i, j, at=layer: (1, 0, chunk(at, i, j), 0)),
            pl.BlockSpec((3, width, width), lambda i, j: (0, 0, 0)),
        ]
        arrays += [fulls[layer], fulls[layer], shards[layer]]
    return pl.pallas_call(
        functools.partial(format_kernel, columns),
        grid=(layers, mp),
        out_shape=[jax.ShapeDtypeStruct(shape, f32) for shape, _ in outs],
        in_specs=specs,
        out_specs=[spec or by_layer(shape) for shape, spec in outs],
        compiler_params=pltpu.CompilerParams(vmem_limit_bytes=56 * MIB),
        name="format",
    )(*arrays)


def greet(dp, me, rows=()):
    barrier = pltpu.get_barrier_semaphore()
    for row in rows:
        pl.semaphore_signal(barrier, inc=1, device_id={"mp": row}, device_id_type=MESH)

    def signal(off, carry):
        pl.semaphore_signal(barrier, inc=1, device_id={"dp": lax.rem(me + off, dp)}, device_id_type=MESH)
        return carry

    lax.fori_loop(1, dp, signal, 0)
    pl.semaphore_wait(barrier, dp - 1 + len(rows))


def partner_of(me, p, dp):
    out, bit = 0, 1
    while bit < dp:
        one, two = lax.rem(lax.div(me, bit), 2), lax.rem(lax.div(p, bit), 2)
        out = out + bit * (one + two - 2 * one * two)
        bit *= 2
    return out


def to_peer(source, target, send_sem, recv_sem, peer):
    return pltpu.make_async_remote_copy(
        src_ref=source,
        dst_ref=target,
        send_sem=send_sem,
        recv_sem=recv_sem,
        device_id={"dp": peer},
        device_id_type=MESH,
    )


def gelu_parts(h):
    root = np.float32(np.sqrt(2.0 / np.pi))
    square = h * h
    t = jnp.tanh(root * h * (1.0 + 0.044715 * square))
    half = 0.5 * (1.0 + t)
    slope = half + 0.5 * h * (1.0 - t * t) * root * (1.0 + 3 * 0.044715 * square)
    return h * half, slope


def expert_forward_kernel(dp, mp, layer, gather, *refs):
    refs = list(refs)
    buffer_ref, up_any, down_any, rup_any, rdown_any = refs[:5]
    refs = refs[5:]
    if gather:
        shards = [ref.at[layer + 1] for ref in refs[:4]]
        refs = refs[4:]
    recv_ref, returned_ref, up_eff, down_eff = refs[:4]
    refs = refs[4:]
    if gather:
        fulls = refs[:4]
        refs = refs[4:]
    part, core, up_ref, down_ref, rup_ref, rdown_ref, local = refs[:7]
    refs = refs[7:]
    moving = WeightGather(shards, fulls, refs[:7]) if gather else None
    send_one, recv_one, send_two, recv_two = refs[-4:]
    split = dp // EXPERTS
    me = lax.axis_index("dp")
    loads = [
        pltpu.make_async_copy(source, target, local.at[k])
        for k, (source, target) in enumerate(
            [
                (up_any, up_ref),
                (rup_any.at[layer, 0], rup_ref),
                (down_any, down_ref),
                (rdown_any.at[layer, 0], rdown_ref),
            ]
        )
    ]
    for load in loads:
        load.start()
    greet(dp, me, (moving.row.sibling, moving.row.across) if gather else ())

    def first(off):
        peer = partner_of(me, off, dp)
        return to_peer(
            buffer_ref.at[lax.div(peer, split)], recv_ref.at[me], send_one.at[off], recv_one.at[off], peer
        )

    def second(off):
        source = partner_of(me, off, dp)
        return to_peer(part.at[source], returned_ref.at[me], send_two.at[off], recv_two.at[off], source)

    def start_first(off, carry):
        first(dp - off).start()
        return carry

    lax.fori_loop(1, dp, start_first, 0)
    if gather:
        for k in range(4):
            moving.start(k)
    recv_ref[me] = buffer_ref[lax.div(me, split)]
    hidden = up_eff.shape[1]
    columns = up_ref.shape[-1]
    loads[0].wait()
    loads[1].wait()
    if split == 1 and columns % LANES == 0:
        for m in range(mp):
            at = slice(m * columns, (m + 1) * columns)
            up_eff[:, at] = (up_ref[m].astype(f32) + rup_ref[:, at].astype(f32)).astype(bf16)
    else:
        core[...] = rup_ref[...].astype(f32)
        begin = lax.rem(me, split) * hidden
        for m in range(mp):
            put = onehot(iota((columns, hidden), 0) + m * columns == iota((columns, hidden), 1) + begin)
            core[...] += nn(up_ref[m], put)
        up_eff[...] = core[...].astype(bf16)
    begin = pl.multiple_of(lax.rem(me, split) * hidden, LANES)
    loads[2].wait()
    loads[3].wait()
    core_part = down_ref[:, :, pl.ds(begin, hidden)].reshape(down_eff.shape[1], hidden)
    down_eff[...] = (turn_blocks(core_part) + rdown_ref[...].astype(f32)).astype(bf16)

    def work(source):
        hidden_pre = nn(recv_ref[source], up_eff[...])
        hidden_low = gelu_parts(hidden_pre)[0].astype(bf16)
        return nn(hidden_low, down_eff[...]).astype(bf16)

    returned_ref[me] = work(me)

    def step(off, carry):
        source = partner_of(me, off, dp)
        first(off).wait_recv()
        part[source] = work(source)
        second(off).start()
        return carry

    lax.fori_loop(1, dp, step, 0)
    if gather:
        for k in range(4):
            moving.forward(k)

    def finish(off, carry):
        first(off).wait_send()
        second(off).wait()
        return carry

    lax.fori_loop(1, dp, finish, 0)
    if gather:
        for k in range(4):
            moving.arrive(k)
            moving.sent(k)


def expert_backward_kernel(dp, mp, fast, reduce, *refs):
    refs = list(refs)
    buffer_ref, recv_ref, up_ref, down_ref = refs[:4]
    refs = refs[4:]
    if reduce:
        given_ref, attn_ref = refs[:2]
        refs = refs[2:]
    returned_ref = refs.pop(0)
    if fast:
        units_ref = refs.pop(0)
    else:
        up_term, down_term = refs[:2]
        refs = refs[2:]
    if reduce:
        full_ref, mine_ref = refs[:2]
        refs = refs[2:]
    grads, hidden_low, slope, pre, part = refs[:5]
    refs = refs[5:]
    if fast:
        up_term, down_term = refs[:2]
        refs = refs[2:]
    row = Row() if reduce else None
    if reduce:
        core_in, y_out, y_in = refs[:3]
        sums = RowSum(row, [attn_ref], core_in, y_out, y_in, [mine_ref], refs[3:7])
        gather = RowGather(
            row, [given_ref.at[k] for k in range(2)], [full_ref.at[k] for k in range(2)], row.place, row.place_across,
            refs[7:13],
        )
        refs = refs[13:]
    send_one, recv_one, send_two, recv_two = refs
    split = dp // EXPERTS
    me = lax.axis_index("dp")
    greet(dp, me, (row.sibling, row.across) if reduce else ())

    def first(off):
        peer = partner_of(me, off, dp)
        return to_peer(buffer_ref.at[lax.div(peer, split)], grads.at[me], send_one.at[off], recv_one.at[off], peer)

    def second(off):
        source = partner_of(me, off, dp)
        return to_peer(part.at[source], returned_ref.at[me], send_two.at[off], recv_two.at[off], source)

    def start_first(off, carry):
        first(dp - off).start()
        return carry

    lax.fori_loop(1, dp, start_first, 0)
    if reduce:
        sums.start(0)
        for k in range(2):
            gather.start(k)
    grads[me] = buffer_ref[lax.div(me, split)]

    def again(source, carry):
        value, rate = gelu_parts(nn(recv_ref[source], up_ref[...]))
        hidden_low[source] = value.astype(bf16)
        slope[source] = rate
        return carry

    lax.fori_loop(0, dp, again, 0)
    if reduce:
        sums.middle(0)
        for k in range(2):
            full_ref[k, row.place] = given_ref[k]

    def work(source):
        hidden_grad = nt(grads[source], down_ref[...])
        pre_grad = (slope[source] * hidden_grad).astype(bf16)
        pre[source] = pre_grad
        return nt(pre_grad, up_ref[...]).astype(bf16)

    returned_ref[me] = work(me)

    def step(off, carry):
        source = partner_of(me, off, dp)
        first(off).wait_recv()
        part[source] = work(source)
        second(off).start()
        return carry

    lax.fori_loop(1, dp, step, 0)
    if reduce:
        for k in range(2):
            gather.forward(k)
        sums.end(0)
    up_term[...] = jnp.zeros(up_term.shape, f32)
    down_term[...] = jnp.zeros(down_term.shape, f32)

    def terms(block, carry):
        up_term[...] += tn(recv_ref[block], pre[block])
        down_term[...] += tn(grads[block], hidden_low[block])
        return carry

    lax.fori_loop(0, dp, terms, 0)
    if fast:
        width = up_term.shape[0]
        height = width // mp
        for place in range(mp):
            q = quarter_at(place, mp)
            units_ref[0, place] = up_term[:, q * width : (q + 1) * width].astype(bf16)
            for chunk in range(mp):
                block = down_term[q * height : (q + 1) * height, chunk * width : (chunk + 1) * width]
                units_ref[1, place, chunk * height : (chunk + 1) * height] = block.astype(bf16)

    def finish(off, carry):
        first(off).wait_send()
        second(off).wait()
        return carry

    lax.fori_loop(1, dp, finish, 0)
    if reduce:
        sums.finish(0)
        for k in range(2):
            gather.arrive(k)
            gather.sent(k)


def expert_call(kernel, arrays, outs, scratch, dp, collective_id, name, flops, anys=(), any_outs=()):
    sems = [pltpu.SemaphoreType.DMA((dp,))] * 4
    vmem, anywhere = pl.BlockSpec(memory_space=pltpu.VMEM), pl.BlockSpec(memory_space=pl.ANY)
    return pl.pallas_call(
        kernel,
        out_shape=[jax.ShapeDtypeStruct(shape, dtype) for shape, dtype in (*outs, *any_outs)],
        in_specs=[vmem] * len(arrays) + [anywhere] * len(anys),
        out_specs=[vmem] * len(outs) + [anywhere] * len(any_outs),
        scratch_shapes=scratch + sems,
        compiler_params=pltpu.CompilerParams(
            vmem_limit_bytes=56 * MIB, collective_id=collective_id, has_side_effects=True
        ),
        cost_estimate=pl.CostEstimate(flops=flops, bytes_accessed=20 * MIB, transcendentals=0),
        name=name,
    )(*arrays, *anys)


def by_windows(grid):
    images, kinds = grid.shape[:2]
    blocks = GRID // WINDOW
    grid = grid.reshape(images, kinds, blocks, WINDOW, blocks, WINDOW).transpose(0, 1, 2, 4, 3, 5)
    grid = grid.reshape(images, kinds, blocks * blocks, WINPOS)
    grid = jnp.pad(grid, ((0, 0), (0, 0), (0, 0), (0, WPAD - WINPOS)), constant_values=-1)
    return grid.reshape(images, kinds, IMGROWS)


def per_device(
    patches,
    qkv_weight,
    proj_weight,
    core_up,
    core_down,
    residual_up,
    residual_down,
    position_bias,
    router_weight,
    norm_gain,
    norm_bias,
    cotangent,
    image_valid,
    expert_index,
    slot_index,
    region_id,
):
    dp, mp = lax.axis_size("dp"), lax.axis_size("mp")
    images, _, width = patches.shape
    split = dp // EXPERTS
    hidden = residual_up.shape[-1]
    hidden_full = core_up.shape[-1] * mp
    row_index = lax.axis_index("mp")

    fast = split == 1 and dp == 8 and mp == 4 and hidden == mp * width
    qkv_rows, proj_rows, down_rows = (a.transpose(0, 2, 1) for a in (qkv_weight, proj_weight, core_down))
    shards = (qkv_rows, proj_rows, core_up, down_rows)
    gathered = [[None] * len(shards)] * LAYERS
    if not fast:
        gathered = [[lax.all_gather(a[l], "mp", axis=0, tiled=False) for a in shards] for l in range(LAYERS)]

    position = jnp.where(slot_index >= 0, expert_index * SLOTS + slot_index, -1)
    row_form = by_windows(jnp.stack([position.reshape(images, GRID, GRID), region_id], 1))
    col_form = row_form.transpose(0, 2, 1)
    enter = jnp.asarray(enter_table(), bf16)
    leave = jnp.asarray(enter_table().T, bf16)
    moves = [jnp.asarray(move_table(l % 2 == 1), bf16) for l in range(LAYERS)]
    backs = [jnp.asarray(move_table(l % 2 == 1).T, bf16) for l in range(LAYERS)]
    table_rows = position_bias.transpose(0, 2, 1).reshape(LAYERS * HEADS, OFFSETS)
    table_rows = jnp.pad(table_rows, ((0, 0), (0, TABLE - OFFSETS)))
    entry_row, entry_col = jnp.asarray(cell_entries()[None, :]), jnp.asarray(cell_entries()[:, None])
    routers = jnp.pad(router_weight.transpose(0, 2, 1), ((0, 0), (0, LANES - EXPERTS), (0, 0)))

    token = (images, IMGROWS, width)
    buffer_shape = (ROWS, width)
    block_rows = (dp, SLOTS, width)
    pieces = (split, ROWS, width)

    def by_piece(returned):
        return returned.reshape(EXPERTS, split, SLOTS, width).transpose(1, 0, 2, 3).reshape(pieces)

    records = []
    before = None
    for l in range(LAYERS):
        first = l == 0
        gather = fast and first
        if first:
            arrays = [("image", patches), ("whole", enter)]
        else:
            arrays = [("image", before[0]), ("image", before[1]), ("whole", before[2])]
        arrays += [
            ("smem", image_valid),
            ("image", col_form),
            ("image", row_form),
            ("any", qkv_rows) if gather else ("whole", gathered[l][0]),
            ("any", proj_rows) if gather else ("whole", gathered[l][1]),
            ("whole", table_rows) if first else (l, biases),
            ("whole", moves[l]),
            ("whole", backs[l]),
            (l, norm_gain),
            (l, norm_bias),
            (l, routers),
        ]
        if first:
            arrays.append(("whole", entry_row))
        if gather:
            arrays += [("any", core_up), ("any", down_rows)]
        outs = [("image", token, f32)]
        if first:
            outs.append(("whole", (LAYERS, HEADS, WPAD, LANES), f32))
        else:
            outs.append(("image", token, f32))
        outs += [
            ("image", token, f32),
            ("image", token, bf16),
            ("image", (images, IMGROWS, 1), f32),
            ("whole", buffer_shape, bf16),
            ("image", token, bf16),
            ("image", (images, 2 * width, IMGROWS), bf16),
            ("image", token, bf16),
            ("image", (images, PAIRS * HEADS, WPAD, LANES), bf16),
            ("image", (images, width, IMGROWS), bf16),
            ("whole", (width, width), bf16),
        ]
        scratch = [pltpu.VMEM(buffer_shape, f32)]
        gathered_shapes = [(mp, *a.shape[1:]) for a in shards]
        if gather:
            outs.append(("whole", (3 * width, width), bf16))
            outs += [("any", shape, bf16) for shape in gathered_shapes[2:]]
            scratch += [pltpu.VMEM(shape, bf16) for shape in gathered_shapes[:2]] + WeightGather.scratch(4)
        results = list(
            image_call(
                functools.partial(attention_forward_kernel, first, l % 2 == 1, mp, gather),
                images, arrays, outs, scratch, f"attend_{l}", 3 * LAYERS + 1 if gather else None,
            )
        )
        if gather:
            gathered[l] = [results[-3], None] + results[-2:]
            results = results[:-3]
        carried = results.pop(0)
        if first:
            biases = results.pop(0)
        else:
            records[-1]["expert_out"] = results.pop(0)
        middle, second_low, gate, buffer = results[:4]
        gather = fast and l < LAYERS - 1
        received, returned, up_eff, down_eff, *more = expert_call(
            functools.partial(expert_forward_kernel, dp, mp, l, gather),
            [buffer.reshape(EXPERTS, SLOTS, width)],
            [
                (block_rows, bf16),
                (block_rows, bf16),
                ((width, hidden), bf16),
                ((hidden, width), bf16),
            ],
            [
                pltpu.VMEM(block_rows, bf16),
                pltpu.VMEM((8, LANES) if fast else (width, hidden), f32),
                pltpu.VMEM(gathered_shapes[2], bf16),
                pltpu.VMEM(gathered_shapes[3], bf16),
                pltpu.VMEM((width, hidden), bf16),
                pltpu.VMEM((hidden, width), bf16),
                pltpu.SemaphoreType.DMA((4,)),
            ]
            + (WeightGather.scratch(4) if gather else []),
            dp, l, f"experts_{l}", 4 * dp * SLOTS * width * hidden,
            [gathered[l][2], gathered[l][3], residual_up, residual_down, *(shards if gather else ())],
            [(shape, bf16) for shape in gathered_shapes] if gather else (),
        )
        if gather:
            gathered[l + 1] = more
        returned = by_piece(returned)
        before = (middle, gate, returned)
        records.append(
            dict(
                carried=carried, middle=middle, second_low=second_low, gate=gate, saved=results[4:], received=received,
                up_eff=up_eff, down_eff=down_eff,
            )
        )

    top = records[-1]
    block_output, grad, logit_grad, router_part, buffer = image_call(
        turn_kernel,
        images,
        [
            ("image", before[0]),
            ("image", before[1]),
            ("whole", before[2]),
            ("image", cotangent),
            ("whole", enter),
            ("whole", leave),
            ("image", col_form),
            ("image", row_form),
            ("image", top["second_low"]),
            (LAYERS - 1, routers),
        ],
        [
            ("image", patches.shape, bf16),
            ("image", token, f32),
            ("image", (images, IMGROWS, LANES), f32),
            ("whole", (LANES, width), f32),
            ("whole", buffer_shape, bf16),
        ],
        [pltpu.VMEM(buffer_shape, f32)],
        "turn",
    )
    router_parts, tables, smalls = [None] * LAYERS, [None] * LAYERS, [None] * LAYERS
    residual_sums, shard_sums = [None] * LAYERS, [None] * LAYERS
    router_parts[LAYERS - 1] = router_part
    units, attn_units, mines = [None] * LAYERS, [None] * LAYERS, [None] * LAYERS
    for l in reversed(range(LAYERS)):
        rec = records[l]
        last = l == 0
        reduce = fast and l < LAYERS - 1
        arrays = [buffer.reshape(EXPERTS, SLOTS, width), rec["received"], rec["up_eff"], rec["down_eff"]]
        outs = [(block_rows, bf16)]
        scratch = [
            pltpu.VMEM(block_rows, bf16),
            pltpu.VMEM((dp, SLOTS, hidden), bf16),
            pltpu.VMEM((dp, SLOTS, hidden), f32),
            pltpu.VMEM((dp, SLOTS, hidden), bf16),
            pltpu.VMEM(block_rows, bf16),
        ]
        if fast:
            outs.append(((2, mp, width, width), bf16))
            scratch += [pltpu.VMEM((width, hidden), f32)] * 2
        else:
            outs += [((width, hidden), f32)] * 2
        if reduce:
            arrays += [mines[l + 1], attn_units[l + 1]]
            outs += [((2, mp, width, width), bf16), ((width, width), bf16)]
            scratch += RowSum.scratch(1, width) + RowGather.scratch(2)
        results = list(
            expert_call(
                functools.partial(expert_backward_kernel, dp, mp, fast, reduce), arrays, outs, scratch, dp, LAYERS + l,
                f"experts_back_{l}", 10 * dp * SLOTS * width * hidden,
            )
        )
        returned_grad = results.pop(0)
        if fast:
            units[l] = results.pop(0)
        else:
            residual_sums[l] = lax.psum(tuple(t.astype(bf16) for t in results[:2]), "mp")
        if reduce:
            full_above, mine_above = results
        window_in, qk, v, probs, att, proj_full = rec["saved"]
        qkv_full = gathered[l][0].reshape(3 * width, width)
        arrays = [
            ("smem", image_valid),
            ("image", grad),
            ("whole", by_piece(returned_grad)),
            ("image", logit_grad),
            ("image", rec["middle"]),
            ("image", rec["carried"]),
            (l, routers),
            ("image", col_form),
            ("whole", moves[l]),
            ("whole", backs[l]),
            (l, norm_gain),
            ("whole", proj_full),
            ("whole", qkv_full),
            ("image", window_in),
            ("image", qk),
            ("image", v),
            ("image", probs),
            ("image", att),
        ]
        outs = [("image", patches.shape if last else token, f32)]
        scratch = [pltpu.VMEM((3 * width, (2 - images % 2) * IMGROWS), bf16)]
        closes = fast and last
        table_shape, small_shape = (HEADS, WPAD, LANES), (8, width)
        if fast:
            arrays.append(("whole", units[l]))
            scratch += [pltpu.VMEM((3 * width, width), f32), pltpu.VMEM((width, width), f32)]
        if closes:
            outs += [
                ("whole", (2, mp, width, width), bf16),
                ("whole", (3, width, width), bf16),
                ("whole", (Closing.lines, width), f32),
                ("whole", (3, width, width), bf16),
            ]
        else:
            if fast:
                outs += [
                    ("whole", (width // 2, width), bf16),
                    ("whole", (mp, width, width), bf16),
                    ("whole", (2, width, width), bf16),
                ]
            else:
                outs += [("whole", (3 * width, width), f32), ("whole", (width, width), f32)]
            outs += [("whole", table_shape, f32), ("whole", small_shape, f32)]
        if last:
            arrays.append(("whole", leave))
            if fast:
                arrays += [
                    ("whole", a)
                    for a in (
                        tables[1], smalls[1], router_parts[1], router_parts[0], entry_col, halves_above, mines[1],
                        mine_above,
                    )
                ]
        else:
            below = records[l - 1]
            arrays += [
                ("image", row_form),
                ("image", below["expert_out"]),
                ("image", below["second_low"]),
                (l - 1, routers),
            ]
            outs += [
                ("image", (images, IMGROWS, LANES), f32),
                ("whole", (LANES, width), f32),
                ("whole", buffer_shape, bf16),
            ]
            scratch.append(pltpu.VMEM(buffer_shape, f32))
        if closes:
            scratch += [
                pltpu.VMEM(table_shape, f32),
                pltpu.VMEM(small_shape, f32),
                pltpu.VMEM((mp, width, width), bf16),
                pltpu.VMEM((Closing.lines, width), f32),
            ]
            scratch += [pltpu.VMEM(shape, dtype) for _, shape, dtype in outs[1:5]] + Closing.scratch(dp, width)
        elif fast:
            scratch += RowSum.scratch(2, width) + [pltpu.VMEM((width // 2, width), bf16)]
            scratch += [pltpu.SemaphoreType.DMA((1,))] * 2
        results = list(
            image_call(
                functools.partial(attention_backward_kernel, last, dp, mp, fast),
                images, arrays, outs, scratch, f"attend_back_{l}", 2 * LAYERS + 1 + l if fast else None,
            )
        )
        grad = results.pop(0)
        if closes:
            full, closed, lines, shard_above = results
            continue
        if fast:
            halves_above = results.pop(0)
            attn_units[l], mines[l] = results[:2]
        else:
            qkv_part, proj_part = results[:2]
        tables[l], smalls[l] = results[2:4]
        if not last:
            logit_grad, router_parts[l - 1], buffer = results[4:]
        if fast:
            continue
        attn = (
            lax.psum_scatter(qkv_part.astype(bf16), "mp", scatter_dimension=0, tiled=True),
            lax.psum_scatter(proj_part.T.astype(bf16), "mp", scatter_dimension=0, tiled=True),
        )
        up_sum, down_sum = residual_sums[l]
        if split > 1:
            begin = lax.axis_index("dp") % split * hidden
            empty = jnp.zeros((width, hidden_full), bf16)
            up_sum = lax.dynamic_update_slice_in_dim(empty, up_sum, begin, 1)
            down_sum = lax.dynamic_update_slice_in_dim(empty, down_sum, begin, 1)
        up_columns, down_columns = core_up.shape[-1], core_down.shape[-1]
        up_shard = lax.dynamic_slice_in_dim(up_sum, row_index * up_columns, up_columns, 1)
        down_shard = lax.dynamic_slice_in_dim(down_sum, row_index * down_columns, down_columns, 0)
        shard_sums[l] = lax.psum((attn[0], attn[1], up_shard, down_shard), "dp")

    if fast:
        *attn_grads, core_up_grad, core_down_grad, residual_up_grad, residual_down_grad = format_call(
            [full, full_above], [closed, shard_above], qkv_weight.shape[-1]
        )
        attn_grads = [a.transpose(0, 2, 1) for a in attn_grads]
        core_grads = (core_up_grad, core_down_grad.transpose(0, 2, 1))
        at = LAYERS * HEADS
        table_sum = lines[:at, :OFFSETS]
        router_sum = lines[at : at + LAYERS * EXPERTS].reshape(LAYERS, EXPERTS, width)
        at += LAYERS * EXPERTS
        small_sum = lines[at : at + LAYERS * 8].reshape(LAYERS, 8, width)[:, :4]
    else:
        entry = cell_entries()[None, :] + np.array([key_base_of(key) for key in range(WPAD)])[:, None]
        entry = jnp.asarray(np.where(np.arange(WPAD)[:, None] < WINPOS, entry, -1).reshape(-1))
        entry_turned = (entry[:, None] == jnp.arange(OFFSETS)[None, :]).astype(f32)
        table_part = jnp.dot(
            jnp.stack(tables, 0).reshape(LAYERS * HEADS, WPAD * LANES), entry_turned, precision=highest
        )
        small_part = jnp.stack(smalls, 0)[:, :4]
        router_part = jnp.stack(router_parts, 0)[:, :EXPERTS]
        table_sum, small_sum, router_sum = lax.psum((table_part, small_part, router_part), ("dp", "mp"))

        def shard(k):
            return jnp.stack([shard_sums[l][k] for l in range(LAYERS)], 0).astype(f32)

        attn_grads = (shard(0).transpose(0, 2, 1), shard(1).transpose(0, 2, 1))
        core_grads = (shard(2), shard(3).transpose(0, 2, 1))
        residual_up_grad, residual_down_grad = (
            jnp.stack([residual_sums[l][k] for l in range(LAYERS)], 0).astype(f32) for k in range(2)
        )
        residual_up_grad = residual_up_grad[:, None]
        residual_down_grad = residual_down_grad.transpose(0, 2, 1)[:, None]

    return (
        block_output,
        grad,
        attn_grads[0],
        attn_grads[1],
        core_grads[0],
        core_grads[1],
        residual_up_grad,
        residual_down_grad,
        table_sum.reshape(LAYERS, HEADS, OFFSETS).transpose(0, 2, 1),
        router_sum.transpose(0, 2, 1),
        small_sum[:, 0:2],
        small_sum[:, 2:4],
    )


def solution(mesh):
    placed = (
        P(("dp", "mp"), None, None),
        P(None, None, "mp"),
        P(None, None, "mp"),
        P(None, None, "mp"),
        P(None, None, "mp"),
        P(None, "dp", None, None),
        P(None, "dp", None, None),
        P(),
        P(),
        P(),
        P(),
        P(("dp", "mp"), None, None),
        P(("dp", "mp")),
        P(("dp", "mp"), None),
        P(("dp", "mp"), None),
        P(("dp", "mp"), None, None),
    )
    return jax.shard_map(
        per_device,
        mesh=mesh,
        in_specs=placed,
        out_specs=(
            P(("dp", "mp"), None, None),
            P(("dp", "mp"), None, None),
            P(None, None, "mp"),
            P(None, None, "mp"),
            P(None, None, "mp"),
            P(None, None, "mp"),
            P(None, "dp", None, None),
            P(None, "dp", None, None),
            P(),
            P(),
            P(),
            P(),
        ),
        check_vma=False,
    )
```

```python
import functools

import jax
import jax.numpy as jnp
import numpy as np
from jax import lax
from jax.experimental import pallas as pl
from jax.experimental.pallas import tpu as pltpu
from jax.sharding import PartitionSpec as P

HEADS = 12
HEAD_DIM = 32
EXPERTS = 8
WINDOW = 7
GRID = 14
SHIFT = 3
LAYERS = 2
WINPOS = 49
OFFSETS = 169
CAP = 122

WPAD = 64
IMGROWS = 256
PATCHES = 196
SLOTS = 128
ROWS = EXPERTS * SLOTS
LANES = 128
GROUP = 4
PAIRS = 2
TABLE = 256

bf16 = jnp.bfloat16
f32 = jnp.float32
highest = lax.Precision.HIGHEST
norm_epsilon = 1e-05
mask_fill = -100.0
head_scale = HEAD_DIM ** (-0.5)
MESH = pl.DeviceIdType.MESH
MIB = 1024 * 1024


def nn(a, b):
    return lax.dot_general(a, b, (((1,), (0,)), ((), ())), preferred_element_type=f32)


def nt(a, b):
    return lax.dot_general(a, b, (((1,), (1,)), ((), ())), preferred_element_type=f32)


def tn(a, b):
    return lax.dot_general(a, b, (((0,), (0,)), ((), ())), preferred_element_type=f32)


def iota(shape, dim):
    return lax.broadcasted_iota(jnp.int32, shape, dim)


def onehot(flags):
    return jnp.where(flags, 1.0, 0.0).astype(bf16)


def natural_of_row(shifted):
    moved = SHIFT if shifted else 0
    blocks = GRID // WINDOW
    out = -np.ones(IMGROWS, np.int32)
    for window in range(blocks * blocks):
        for cell in range(WINPOS):
            row = (window // blocks * WINDOW + cell // WINDOW + moved) % GRID
            col = (window % blocks * WINDOW + cell % WINDOW + moved) % GRID
            out[window * WPAD + cell] = row * GRID + col
    return out


def key_base_of(key):
    return (2 * WINDOW) * (WINDOW - 1) - (key // WINDOW * (2 * WINDOW - 1) + key % WINDOW)


def enter_table():
    held = natural_of_row(False)
    return (held[:, None] == np.arange(PATCHES)[None, :]).astype(np.float32)


def move_table(shifted):
    first, second = natural_of_row(False), natural_of_row(shifted)
    same = (second[:, None] == first[None, :]) & (second[:, None] >= 0)
    return same.astype(np.float32)


def cell_entries():
    cell = np.arange(LANES) % WPAD
    return np.where(cell < WINPOS, cell // WINDOW * (2 * WINDOW - 1) + cell % WINDOW, -4 * TABLE).astype(np.int32)


def norm_parts(x):
    width = x.shape[-1]
    center = x - jnp.sum(x, -1, keepdims=True) * (1.0 / width)
    spread = jnp.sum(center * center, -1, keepdims=True) * (1.0 / width)
    rstd = lax.rsqrt(spread + norm_epsilon)
    return center * rstd, rstd


def norm_back(grad, gain, xhat, rstd):
    width = xhat.shape[-1]
    dxhat = grad * gain
    mean_one = jnp.sum(dxhat, -1, keepdims=True) * (1.0 / width)
    mean_two = jnp.sum(dxhat * xhat, -1, keepdims=True) * (1.0 / width)
    return rstd * (dxhat - mean_one - xhat * mean_two)


def turn_blocks(x):
    size = x.shape[0]
    same = onehot(iota((size, size), 0) == iota((size, size), 1))
    return jnp.concatenate([nt(same, x[:, at : at + size]) for at in range(0, x.shape[1], size)], 0)


def split_two(x):
    high = x.astype(bf16)
    return high, (x - high.astype(f32)).astype(bf16)


def collect(pos_col, returned_ref):
    pick = onehot(pos_col == iota((pos_col.shape[0], ROWS), 1))
    out = nn(pick, returned_ref[0])
    for piece in range(1, returned_ref.shape[0]):
        out = out + nn(pick, returned_ref[piece])
    return out


def join(ref):
    return ref[...].reshape(ref.shape[0] * ref.shape[1], *ref.shape[2:])


def store(ref, rows):
    ref[...] = rows.reshape(ref.shape).astype(ref.dtype)


def per_image(function, count):
    return jnp.concatenate([function(i) for i in range(count)], 0)


def image_rows(i):
    return slice(i * IMGROWS, (i + 1) * IMGROWS)


def lay_positions(row_ref):
    return jnp.concatenate([row_ref[i, 0:1, :] for i in range(row_ref.shape[0])], 1)


def spread_rows(pos_row, rows_low):
    return nn(onehot(iota((ROWS, pos_row.shape[1]), 0) == pos_row), rows_low)


def route(second_low, router, pos_col):
    logits = nt(second_low, router)
    lane = iota(logits.shape, 1)
    logits = jnp.where(lane < EXPERTS, logits, -1e30)
    expo = jnp.exp(logits - jnp.max(logits, -1, keepdims=True))
    probs = expo / jnp.sum(expo, -1, keepdims=True)
    expert = jnp.where(pos_col >= 0, pos_col // SLOTS, -1)
    chosen = jnp.where(lane == expert, 1.0, 0.0)
    return probs, chosen, jnp.sum(probs * chosen, -1, keepdims=True)


def head_masks():
    rows = iota((LANES, LANES), 0) // HEAD_DIM
    return [onehot(rows == h) for h in range(GROUP)]


def lane_masks():
    lane = iota((WPAD, LANES), 1)
    return [onehot(lane < WPAD), onehot(lane >= WPAD)]


def keys_entry(cells, key_row, turned):
    parts = [cells + (key_base_of(col) - key_row * (2 * WINDOW - 1)) for col in range(WINDOW)]
    return jnp.concatenate(parts, 0 if turned else 1)


def form_bias(bias_ref, table_ref, entry_row):
    layers, heads = bias_ref.shape[:2]
    lines = layers * heads
    bias_ref[...] = jnp.where(iota(bias_ref.shape, 2) < WINPOS, 0.0, -1e30)
    table = table_ref[...]
    high = table.astype(bf16)
    mid, low = split_two(table - high.astype(f32))
    parts = jnp.concatenate([high.astype(f32), mid.astype(f32), low.astype(f32)], 0).astype(bf16)

    def step(key_row, carry):
        pick = onehot(iota((TABLE, WINDOW * LANES), 0) == keys_entry(entry_row, key_row, False))
        rows = nn(parts, pick)
        rows = rows[:lines] + rows[lines : 2 * lines] + rows[2 * lines :]
        for col in range(WINDOW):
            for layer in range(layers):
                part = rows[layer * heads : (layer + 1) * heads, col * LANES : (col + 1) * LANES]
                bias_ref[layer, :, pl.ds(key_row * WINDOW + col, 1), :] = part.reshape(heads, 1, LANES)
        return carry

    lax.fori_loop(0, WINDOW, step, 0)


def table_grad(parts, entry_col):
    heads = parts[0].shape[0]
    lines = heads * len(parts)

    def step(key_row, total):
        keys = [
            jnp.concatenate([ref[:, pl.ds(key_row * WINDOW + col, 1), :].reshape(heads, LANES) for ref in parts], 0)
            for col in range(WINDOW)
        ]
        rows = jnp.concatenate(keys, 1)
        high = rows.astype(bf16).astype(f32)
        both = jnp.concatenate([high, rows - high], 0).astype(bf16)
        entry = keys_entry(entry_col, key_row, True)
        out = nn(both, onehot(iota((WINDOW * LANES, TABLE), 1) == entry))
        return total + out[:lines] + out[lines:]

    return lax.fori_loop(0, WINDOW, step, jnp.zeros((lines, TABLE), f32))


def attention_forward_kernel(first, shifted, mp, gather, *refs):
    refs = list(refs)
    if first:
        patches_ref, enter_ref = refs[:2]
        refs = refs[2:]
    else:
        prev_ref, prev_gate_ref, returned_ref = refs[:3]
        refs = refs[3:]
    (
        valid_ref, col_ref, row_ref, qkv_ref, proj_ref, bias_ref, move_ref, back_ref, gain_ref, nbias_ref, router_ref,
    ) = refs[:11]
    gain_ref, nbias_ref, router_ref = (ref.at[0] for ref in (gain_ref, nbias_ref, router_ref))
    refs = refs[11:]
    if first:
        table_ref, entry_ref = bias_ref, refs.pop(0)
    if gather:
        core_up_ref, core_down_ref = refs[:2]
        refs = refs[2:]
    carried_ref = refs.pop(0)
    if first:
        biases_ref = refs.pop(0)
        bias_ref = biases_ref.at[0]
    else:
        expert_out_ref = refs.pop(0)
        bias_ref = bias_ref.at[0]
    middle_ref, second_ref, gate_ref, buffer_ref, window_ref, qk_ref, v_ref, probs_ref, att_ref, proj_full = refs[:10]
    refs = refs[10:]
    if gather:
        qkv_full = refs.pop(0)
        up_out, down_out = refs[:2]
        refs = refs[2:]
    total_ref = refs.pop(0)
    step = pl.program_id(0)
    final = pl.num_programs(0) - 1
    count, _, width = carried_ref.shape
    if gather:
        shards = [ref.at[0] for ref in (qkv_ref, proj_ref, core_up_ref, core_down_ref)]
        qkv_ref, proj_ref = refs[:2]
        moving = WeightGather(shards, [qkv_ref, proj_ref, up_out, down_out], refs[2:])

        @pl.when(step == 0)
        def _():
            pl.semaphore_wait(moving.row.greet(), 2)
            for k in (0, 1):
                moving.start(k)
            form_bias(biases_ref, table_ref, entry_ref[...])

    pos_col = join(col_ref)[:, 0:1]
    if first:
        x = per_image(lambda i: nn(enter_ref[...], patches_ref[i]), count)
    else:
        expert_out = collect(pos_col, returned_ref)
        store(expert_out_ref, expert_out)
        x = join(prev_ref) + join(prev_gate_ref) * expert_out
    store(carried_ref, x)
    xhat, _ = norm_parts(x)
    normed = (xhat * gain_ref[0:1, :] + nbias_ref[0:1, :]).astype(bf16)
    window_in = per_image(lambda i: nn(move_ref[...], normed[image_rows(i)]), count).astype(bf16)
    store(window_ref, window_in)

    @pl.when(step == 0)
    def _():
        if gather:
            for k in (0, 1):
                moving.forward(k)
            for k in (2, 3):
                moving.start(k)
            for k in (0, 1):
                moving.arrive(k)
            qkv_full[...] = join(qkv_ref)
        elif first:
            form_bias(biases_ref, table_ref, entry_ref[...])
        proj_full[...] = turn_blocks(join(proj_ref)).astype(bf16)
        total_ref[...] = jnp.zeros(total_ref.shape, f32)

    qkv = join(qkv_ref)
    turned = nt(qkv, window_in).astype(bf16)
    straight = nt(window_in, qkv[width:]).astype(bf16)
    for i in range(count):
        qk_ref[i] = turned[: 2 * width, image_rows(i)]
    store(v_ref, straight[:, width:])
    heads_rows = head_masks()
    halves = lane_masks()
    low_lane = iota((WPAD, LANES), 1) < WPAD
    if shifted:
        row_labels = [nt(row_ref[i].astype(f32).astype(bf16), move_ref[...]) for i in range(count)]
        col_labels = [nn(move_ref[...], col_ref[i].astype(f32).astype(bf16)) for i in range(count)]
    for pair in range(PAIRS * count):
        image, side = pair // PAIRS, pair % PAIRS
        across = slice(pair * LANES, (pair + 1) * LANES)
        within = slice(side * LANES, (side + 1) * LANES)
        if shifted:
            ahead = col_labels[image][side * LANES : side * LANES + WPAD, 1:2]
            behind = col_labels[image][side * LANES + WPAD : (side + 1) * LANES, 1:2]
            key_label = jnp.where(low_lane, ahead, behind)
            mask = jnp.where(key_label == row_labels[image][1:2, within], 0.0, mask_fill)
        for group in range(HEADS // GROUP):
            features = slice(group * LANES, (group + 1) * LANES)
            queries = turned[features, across]
            spread = jnp.concatenate([queries * heads_rows[h] for h in range(GROUP)], 1)
            raw = nn(straight[across, features], spread)
            for h in range(GROUP):
                head = group * GROUP + h
                part = raw[:, h * LANES : (h + 1) * LANES]
                scores = jnp.where(low_lane, part[:WPAD], part[WPAD:]) * head_scale + bias_ref[head]
                if shifted:
                    scores = scores + mask
                expo = jnp.exp(scores - jnp.max(scores, 0, keepdims=True))
                probs = (expo * (1.0 / jnp.sum(expo, 0, keepdims=True))).astype(bf16)
                probs_ref[image, side * HEADS + head] = probs
                both = jnp.concatenate([probs * halves[0], probs * halves[1]], 0)
                at = slice(head * HEAD_DIM, (head + 1) * HEAD_DIM)
                values = turned[2 * width + head * HEAD_DIM : 2 * width + (head + 1) * HEAD_DIM, across]
                att_ref[image, at, within] = nn(values, both).astype(bf16)
    attended = per_image(lambda i: nt(back_ref[...], att_ref[i]), count).astype(bf16)
    branch = nt(attended, join(proj_ref))
    middle = x + per_image(lambda i: valid_ref[step * count + i].astype(f32) * branch[image_rows(i)], count)
    store(middle_ref, middle)
    xhat, _ = norm_parts(middle)
    second_low = (xhat * gain_ref[1:2, :] + nbias_ref[1:2, :]).astype(bf16)
    store(second_ref, second_low)
    _, _, gate = route(second_low, router_ref[...], pos_col)
    store(gate_ref, gate)
    total_ref[...] += spread_rows(lay_positions(row_ref), second_low)

    @pl.when(step == final)
    def _():
        buffer_ref[...] = total_ref[...].astype(bf16)
        if gather:
            for k in (2, 3):
                moving.forward(k)
            for k in (2, 3):
                moving.arrive(k)
            for k in range(4):
                moving.sent(k)


def image_spec(array_shape, count):
    rest = tuple(array_shape[1:])
    zeros = (0,) * len(rest)
    return pl.BlockSpec((count,) + rest, lambda i: (i,) + zeros)


def whole_spec(array_shape):
    zeros = (0,) * len(array_shape)
    return pl.BlockSpec(tuple(array_shape), lambda i: zeros)


def image_call(kernel, images, arrays, outs, scratch, name, collective_id=None):
    count = 2 - images % 2

    def spec(kind, shape):
        if isinstance(kind, int):
            rest = tuple(shape[1:])
            return pl.BlockSpec((1,) + rest, lambda i: (kind,) + (0,) * len(rest))
        if kind in ("smem", "any"):
            return pl.BlockSpec(memory_space=pltpu.SMEM if kind == "smem" else pl.ANY)
        return image_spec(shape, count) if kind == "image" else whole_spec(shape)

    return pl.pallas_call(
        kernel,
        grid=(images // count,),
        out_shape=[jax.ShapeDtypeStruct(shape, dtype) for _, shape, dtype in outs],
        in_specs=[spec(kind, array.shape) for kind, array in arrays],
        out_specs=[spec(kind, shape) for kind, shape, _ in outs],
        scratch_shapes=scratch,
        compiler_params=pltpu.CompilerParams(
            vmem_limit_bytes=56 * MIB,
            dimension_semantics=("arbitrary",),
            collective_id=collective_id,
            has_side_effects=collective_id is not None,
        ),
        name=name,
    )(*[array for _, array in arrays])


def send_part(g, expert_out, second_low, router, pos_col, pos_row, logit_ref, router_grad_ref, total_ref):
    probs, chosen, gate = route(second_low, router, pos_col)
    gate_grad = jnp.where(pos_col >= 0, jnp.sum(g * expert_out, -1, keepdims=True), 0.0)
    sent = (gate * g).astype(bf16)
    logit_grad = gate_grad * gate * (chosen - probs)
    store(logit_ref, logit_grad)
    high, low = split_two(logit_grad)
    router_grad_ref[...] += tn(high, second_low) + tn(low, second_low)
    total_ref[...] += spread_rows(pos_row, sent)


def turn_kernel(
    prev_ref, gate_ref, returned_ref, cotangent_ref, enter_ref, leave_ref, col_ref, row_ref, second_ref, router_ref,
    block_ref, grad_ref, logit_ref, router_grad_ref, buffer_ref, total_ref,
):
    step = pl.program_id(0)
    count = cotangent_ref.shape[0]

    @pl.when(step == 0)
    def _():
        total_ref[...] = jnp.zeros(total_ref.shape, f32)
        router_grad_ref[...] = jnp.zeros(router_grad_ref.shape, f32)

    pos_col = join(col_ref)[:, 0:1]
    expert_out = collect(pos_col, returned_ref)
    x = (join(prev_ref) + join(gate_ref) * expert_out).astype(bf16)
    for i in range(count):
        block_ref[i] = nn(leave_ref[...], x[image_rows(i)]).astype(bf16)
    g = per_image(lambda i: nn(enter_ref[...], cotangent_ref[i]), count)
    store(grad_ref, g)
    send_part(
        g, expert_out, join(second_ref), router_ref[0], pos_col, lay_positions(row_ref), logit_ref, router_grad_ref, total_ref
    )

    @pl.when(step == pl.num_programs(0) - 1)
    def _():
        buffer_ref[...] = total_ref[...].astype(bf16)


def attention_backward_kernel(last, dp, mp, fast, *refs):
    (
        valid_ref, grad_ref, returned_ref, logit_ref, middle_ref, carried_ref, router_ref, col_ref, move_ref, back_ref,
        gain_ref, proj_ref, qkv_ref, window_ref, qk_ref, v_ref, probs_ref, att_ref,
    ) = refs[:18]
    refs = refs[18:]
    refs = list(refs)
    if fast:
        units_ref = refs.pop(0)
    if last:
        leave_ref = refs.pop(0)
        if fast:
            table_above, small_above, router_above, router_here, entry_ref, half_above, down_above, attn_above = refs[:8]
            refs = refs[8:]
    else:
        row_ref, expert_out_ref, second_ref, router_next_ref = refs[:4]
        refs = refs[4:]
    out_ref = refs.pop(0)
    closing = None
    if fast and last:
        results, refs = refs[:4], refs[4:]
    else:
        if fast:
            halves_ref = refs.pop(0)
            unit_ref, mine_ref = refs[:2]
        else:
            qkv_grad_ref, proj_grad_ref = refs[:2]
        table_ref, small_ref = refs[2:4]
        refs = refs[4:]
    if not last:
        logit_out_ref, router_grad_ref, buffer_ref = refs[:3]
        refs = refs[3:]
    turned = refs.pop(0)
    if fast:
        qkv_grad_ref, proj_grad_ref = refs[:2]
        refs = refs[2:]
    if not last:
        total_ref = refs.pop(0)
    step = pl.program_id(0)
    final = pl.num_programs(0) - 1
    count, _, width = carried_ref.shape
    if fast:
        row = Row()
        if last:
            table_ref, small_ref, unit_ref, lines_ref = refs[:4]
            landing, refs = refs[4:8], refs[8:]
            above = (half_above, down_above.at[1], attn_above)
            closing = Closing(row, dp, units_ref, unit_ref, lines_ref, above, landing, refs)
            sums = closing.sums
        else:
            sums = RowSum(row, blocks(units_ref), refs[0], refs[1], refs[2], blocks(mine_ref), refs[3:7])
            across_x = DeepSum(dp, [mine_ref.at[0]], [refs[7]], [halves_ref], [None], [None], refs[8:10] * 4)

        def take(k):
            if closing:
                closing.take(k)
            else:
                sums.end(k)
                if k == 0:
                    across_x.over_x(k).start()

        @pl.when(step == 0)
        def _():
            if closing:
                closing.enter()
            else:
                barrier = row.greet()
                pl.semaphore_wait(barrier, 2 + across_x.greet(barrier, False))
                for k in range(2):
                    sums.start(k)

    @pl.when(step == 0)
    def _():
        qkv_grad_ref[...] = jnp.zeros(qkv_grad_ref.shape, f32)
        proj_grad_ref[...] = jnp.zeros(proj_grad_ref.shape, f32)
        table_ref[...] = jnp.zeros(table_ref.shape, f32)
        small_ref[...] = jnp.zeros(small_ref.shape, f32)
        if not last:
            total_ref[...] = jnp.zeros(total_ref.shape, f32)
            router_grad_ref[...] = jnp.zeros(router_grad_ref.shape, f32)

    pos_col = join(col_ref)[:, 0:1]
    g = join(grad_ref)
    high, low = split_two(join(logit_ref))
    gain_ref, router = gain_ref.at[0], router_ref[0]
    normed_grad = collect(pos_col, returned_ref) + nn(high, router) + nn(low, router)
    xhat, rstd = norm_parts(join(middle_ref))
    small_ref[1:2, :] += jnp.sum(normed_grad * xhat, 0, keepdims=True)
    small_ref[3:4, :] += jnp.sum(normed_grad, 0, keepdims=True)
    middle_grad = g + norm_back(normed_grad, gain_ref[1:2, :], xhat, rstd)

    if fast:

        @pl.when(step == 0)
        def _():
            for k in range(2):
                sums.middle(k)

    def branch_part(i):
        low_part = (valid_ref[step * count + i].astype(f32) * middle_grad[image_rows(i)]).astype(bf16)
        return nn(move_ref[...], low_part)

    branch_grad = per_image(branch_part, count).astype(bf16)
    for i in range(count):
        proj_grad_ref[...] += nn(att_ref[i], branch_grad[image_rows(i)])
    att_grad = nt(proj_ref[...], branch_grad).astype(bf16)
    if fast:

        @pl.when(step == 0)
        def _():
            if closing:
                closing.early()

        pl.when(step == final)(functools.partial(take, 0))

    heads_rows = head_masks()
    halves = lane_masks()
    low_lane = iota((WPAD, LANES), 1) < WPAD
    for pair in range(PAIRS * count):
        image, side = pair // PAIRS, pair % PAIRS
        across = slice(pair * LANES, (pair + 1) * LANES)
        within = slice(side * LANES, (side + 1) * LANES)
        for group in range(HEADS // GROUP):
            features = slice(group * LANES, (group + 1) * LANES)
            grads = att_grad[features, across]
            spread = jnp.concatenate([grads * heads_rows[h] for h in range(GROUP)], 1)
            raw = nn(v_ref[image, within, features], spread)
            for h in range(GROUP):
                head = group * GROUP + h
                at = slice(head * HEAD_DIM, (head + 1) * HEAD_DIM)
                below = slice(width + head * HEAD_DIM, width + (head + 1) * HEAD_DIM)
                lowest = slice(2 * width + head * HEAD_DIM, 2 * width + (head + 1) * HEAD_DIM)
                part = raw[:, h * LANES : (h + 1) * LANES]
                probs_grad = jnp.where(low_lane, part[:WPAD], part[WPAD:])
                probs_low = probs_ref[image, side * HEADS + head]
                probs = probs_low.astype(f32)
                weighted = probs * probs_grad
                scores_grad = weighted - probs * jnp.sum(weighted, 0, keepdims=True)
                table_ref[head] += scores_grad
                scores_low = scores_grad.astype(bf16)
                both = jnp.concatenate([scores_low * halves[0], scores_low * halves[1]], 0)
                probs_both = jnp.concatenate([probs_low * halves[0], probs_low * halves[1]], 0)
                turned[at, across] = (nn(qk_ref[image, below, within], both) * head_scale).astype(bf16)
                turned[below, across] = (nt(qk_ref[image, at, within], both) * head_scale).astype(bf16)
                turned[lowest, across] = nt(att_grad[at, across], probs_both).astype(bf16)
    qkv_grad_ref[...] += nn(turned[...], join(window_ref))
    if fast:

        @pl.when(step == final)
        def _():
            columns, rows = 3 * width // mp, width // mp
            proj_turned = turn_blocks(proj_grad_ref[...].astype(bf16)).astype(bf16)
            for place in range(mp):
                q = quarter_at(place, mp)
                unit_ref[place, :columns] = qkv_grad_ref[q * columns : (q + 1) * columns].astype(bf16)
                unit_ref[place, columns:] = proj_turned[q * rows : (q + 1) * rows]
            if closing:
                closing.open()
            take(1)
            if closing:
                heads = 2 * HEADS
                lines_ref[...] = jnp.zeros(lines_ref.shape, f32)
                lines_ref[:heads, :TABLE] = table_grad([table_ref, table_above], entry_ref[...])

    mixed_grad = per_image(lambda i: nt(back_ref[...], turned[:, image_rows(i)]), count).astype(bf16)
    first_grad = nn(mixed_grad, qkv_ref[...])
    if closing:

        @pl.when(step == final)
        def _():
            closing.cross()

    xhat, rstd = norm_parts(join(carried_ref))
    small_ref[0:1, :] += jnp.sum(first_grad * xhat, 0, keepdims=True)
    small_ref[2:3, :] += jnp.sum(first_grad, 0, keepdims=True)
    if closing:

        @pl.when(step == final)
        def _():
            heads = 2 * HEADS
            lines_ref[heads : heads + EXPERTS] = router_here[:EXPERTS]
            lines_ref[heads + EXPERTS : heads + 2 * EXPERTS] = router_above[:EXPERTS]
            lines_ref[heads + 2 * EXPERTS : heads + 2 * EXPERTS + 8] = small_ref[...]
            lines_ref[heads + 2 * EXPERTS + 8 : heads + 2 * EXPERTS + 16] = small_above[...]
            closing.send_lines()

    out = middle_grad + norm_back(first_grad, gain_ref[0:1, :], xhat, rstd)
    if last:
        top = out.astype(bf16)
        rest = out - top.astype(f32)
        mid, low = split_two(rest)
        leave = leave_ref[...]
        for i in range(count):
            at = image_rows(i)
            out_ref[i] = nn(leave, top[at]) + nn(leave, mid[at]) + nn(leave, low[at])
    else:
        store(out_ref, out)
        send_part(
            out, join(expert_out_ref), join(second_ref), router_next_ref[0], pos_col, lay_positions(row_ref), logit_out_ref,
            router_grad_ref, total_ref,
        )

    @pl.when(step == final)
    def _():
        if not last:
            buffer_ref[...] = total_ref[...].astype(bf16)
        if closing:
            closing.finish()
            for out, landed in zip(results, landing):
                out[...] = landed[...]
        elif fast:
            across_x.halve(0)
            across_x.over_x(0).wait_send()
            for k in range(2):
                sums.finish(k)


def quarter_at(place, mp):
    return place % (mp // 2) * 2 + place // (mp // 2)


def add_up(*parts):
    total = parts[0].astype(f32)
    for part in parts[1:]:
        total = total + part.astype(f32)
    return total


class Copies:
    def __init__(self, source, target, send_sem, recv_sem, device):
        self.source, self.target = source, target
        self.how = dict(send_sem=send_sem, recv_sem=recv_sem, device_id=device, device_id_type=MESH)
        whole = pltpu.make_async_remote_copy(src_ref=source, dst_ref=target, **self.how)
        self.wait_send, self.wait_recv = whole.wait_send, whole.wait_recv

    def start(self):
        shape = self.source.shape
        rows = shape[-2]
        parts = max(n for n in (1, 2, 3, 4) if rows % (16 * n) == 0)
        size = rows // parts
        leads = [(lead,) for lead in range(shape[0])] if len(shape) == 3 else [()]
        for lead in leads:
            for part in range(parts):
                at = (*lead, pl.ds(part * size, size))
                pltpu.make_async_remote_copy(
                    src_ref=self.source.at[at], dst_ref=self.target.at[at], **self.how
                ).start()

    def wait(self):
        self.wait_send()
        self.wait_recv()


def to_row(source, target, sems, k, row):
    return Copies(source, target, sems[0].at[k], sems[1].at[k], {"mp": row})


class Row:
    def __init__(self):
        row = lax.axis_index("mp")
        self.row, self.core, self.y = row, lax.rem(row, 2), lax.div(row, 2)
        self.sibling, self.across = row + 1 - 2 * self.core, row + 2 - 4 * self.y
        self.place = self.core * 2 + self.y
        self.place_across = self.core * 2 + 1 - self.y

    def greet(self):
        barrier = pltpu.get_barrier_semaphore()
        for row in (self.sibling, self.across):
            pl.semaphore_signal(barrier, inc=1, device_id={"mp": row}, device_id_type=MESH)
        return barrier


class RowSum:
    semaphores = 4

    def __init__(self, row, units, core_in, y_out, y_in, mine, sems):
        self.row, self.units, self.mine = row, units, mine
        self.core_in, self.y_out, self.y_in = core_in, y_out, y_in
        self.sems = (sems[:2], sems[2:])

    def pair(self, k):
        theirs = self.units[k].at[pl.ds(2 * (1 - self.row.core), 2)]
        return to_row(theirs, self.core_in.at[k], self.sems[0], k, self.row.sibling)

    def cross(self, k):
        return to_row(self.y_out.at[k], self.y_in.at[k], self.sems[1], k, self.row.across)

    def start(self, k):
        self.pair(k).start()

    def middle(self, k):
        self.pair(k).wait_recv()
        other = 1 - self.row.y
        mixed = add_up(self.units[k][self.row.core * 2 + other], self.core_in[k, other])
        self.y_out[k] = mixed.astype(bf16)
        self.cross(k).start()

    def end(self, k):
        self.cross(k).wait_recv()
        self.mine[k][...] = add_up(
            self.units[k][self.row.place], self.core_in[k, self.row.y], self.y_in[k]
        ).astype(bf16)

    def finish(self, k):
        self.pair(k).wait_send()
        self.cross(k).wait_send()

    @classmethod
    def scratch(cls, count, width):
        return [
            pltpu.VMEM((count, 2, width, width), bf16),
            pltpu.VMEM((count, width, width), bf16),
            pltpu.VMEM((count, width, width), bf16),
        ] + [pltpu.SemaphoreType.DMA((count,))] * cls.semaphores


class RowGather:
    semaphores = 6

    def __init__(self, row, sources, fulls, slot, slot_across, sems):
        self.row, self.sources, self.fulls = row, sources, fulls
        self.slot, self.slot_across = slot, slot_across
        self.sems = (sems[:2], sems[2:4], sems[4:])

    def over(self, k):
        return to_row(self.sources[k], self.fulls[k].at[self.slot], self.sems[0], k, self.row.across)

    def near(self, k):
        return to_row(self.sources[k], self.fulls[k].at[self.slot], self.sems[1], k, self.row.sibling)

    def onward(self, k):
        block = self.fulls[k].at[self.slot_across]
        return to_row(block, block, self.sems[2], k, self.row.sibling)

    def start(self, k):
        self.over(k).start()
        self.near(k).start()

    def forward(self, k):
        self.over(k).wait_recv()
        self.onward(k).start()

    def arrive(self, k):
        self.near(k).wait_recv()
        self.onward(k).wait_recv()

    def sent(self, k):
        self.over(k).wait_send()
        self.near(k).wait_send()
        self.onward(k).wait_send()

    @classmethod
    def scratch(cls, count):
        return [pltpu.SemaphoreType.DMA((count,))] * cls.semaphores


class WeightGather(RowGather):
    def __init__(self, shards, fulls, sems):
        row = Row()
        super().__init__(row, shards, fulls, row.row, row.across, sems[:6])
        self.own_sem = sems[6]

    def own(self, k):
        return pltpu.make_async_copy(self.sources[k], self.fulls[k].at[self.slot], self.own_sem.at[k])

    def start(self, k):
        super().start(k)
        self.own(k).start()

    def arrive(self, k):
        super().arrive(k)
        self.own(k).wait()

    @classmethod
    def scratch(cls, count):
        return super().scratch(count) + [pltpu.SemaphoreType.DMA((count,))]


class DeepSum:
    def __init__(self, dp, total, arrived, halves, slots, result, sems):
        self.total, self.arrived, self.halves, self.slots, self.result = total, arrived, halves, slots, result
        self.x_sems, self.z_sems, self.z_back, self.x_back = (sems[2 * k : 2 * k + 2] for k in range(4))
        me = lax.axis_index("dp")
        self.x, self.z, self.deep = lax.rem(me, 2), lax.div(me, 2), dp // 2
        self.partner = me + 1 - 2 * self.x

    def greet(self, barrier, whole=True):
        pl.semaphore_signal(barrier, inc=1, device_id={"dp": self.partner}, device_id_type=MESH)
        if not whole:
            return 1
        for off in range(1, self.deep):
            peer = lax.rem(self.z + off, self.deep) * 2 + self.x
            pl.semaphore_signal(barrier, inc=1, device_id={"dp": peer}, device_id_type=MESH)
        return self.deep

    def cut(self, k):
        height = self.halves[k].shape[0]
        return height, height // self.deep

    def over_x(self, k):
        height, _ = self.cut(k)
        away = self.total[k].at[pl.ds(pl.multiple_of((1 - self.x) * height, height), height)]
        return Copies(away, self.arrived[k], self.x_sems[0].at[k], self.x_sems[1].at[k], {"dp": self.partner})

    def over_z(self, k, off):
        _, piece = self.cut(k)
        to = lax.rem(self.z + off, self.deep)
        part = self.halves[k].at[pl.ds(pl.multiple_of(to * piece, piece), piece)]
        sems = [sem.at[k, off] for sem in self.z_sems]
        return to_peer(part, self.slots[k].at[off], *sems, to * 2 + self.x)

    def own_piece(self, k):
        height, piece = self.cut(k)
        return self.result[k].at[pl.ds(pl.multiple_of(self.x * height + self.z * piece, piece), piece)]

    def own_half(self, k):
        height, _ = self.cut(k)
        return self.result[k].at[pl.ds(pl.multiple_of(self.x * height, height), height)]

    def back_z(self, k, off):
        to = lax.rem(self.z + off, self.deep)
        sems = [sem.at[k, off] for sem in self.z_back]
        return to_peer(self.own_piece(k), self.own_piece(k), *sems, to * 2 + self.x)

    def back_x(self, k):
        half = self.own_half(k)
        return Copies(half, half, self.x_back[0].at[k], self.x_back[1].at[k], {"dp": self.partner})

    def halve(self, k):
        self.over_x(k).wait_recv()
        height, _ = self.cut(k)
        keep = self.total[k][pl.ds(pl.multiple_of(self.x * height, height), height)]
        self.halves[k][...] = add_up(keep, self.arrived[k][...]).astype(self.halves[k].dtype)

    def deepen(self, k):
        for off in range(1, self.deep):
            self.over_z(k, off).start()

    def quarter(self, k):
        for off in range(1, self.deep):
            self.over_z(k, off).wait_recv()
        _, piece = self.cut(k)
        keep = self.halves[k][pl.ds(pl.multiple_of(self.z * piece, piece), piece)]
        total = add_up(keep, *[self.slots[k][off] for off in range(1, self.deep)])
        self.own_piece(k)[...] = total.astype(self.result[k].dtype)
        for off in range(1, self.deep):
            self.back_z(k, off).start()

    def widen(self, k):
        for off in range(1, self.deep):
            self.back_z(k, off).wait_recv()
        self.back_x(k).start()

    def finish(self, k, halved=True):
        if halved:
            self.over_x(k).wait_send()
        for off in range(1, self.deep):
            self.over_z(k, off).wait_send()
            self.back_z(k, off).wait_send()
        self.back_x(k).wait()

    @staticmethod
    def semaphores(dp, count):
        one, many = pltpu.SemaphoreType.DMA((count,)), pltpu.SemaphoreType.DMA((count, dp // 2))
        return [one, one, many, many, many, many, one, one]


def blocks(ref):
    return [ref.at[k] for k in range(ref.shape[0])]


class WideSum:
    def __init__(self, dp, total, slots, result, sems):
        self.dp, self.total, self.slots, self.result, self.sems = dp, total, slots, result, sems
        self.me = lax.axis_index("dp")

    def piece(self, ref, at):
        size = ref.shape[0] // self.dp
        return ref.at[pl.ds(pl.multiple_of(at * size, size), size)]

    def out(self, k, p):
        peer = partner_of(self.me, p, self.dp)
        sems = self.sems[0].at[k, p], self.sems[1].at[k, p]
        return to_peer(self.piece(self.total[k], peer), self.slots[k].at[p], *sems, peer)

    def back(self, k, p):
        mine = self.piece(self.result[k], self.me)
        sems = self.sems[2].at[k, p], self.sems[3].at[k, p]
        return to_peer(mine, mine, *sems, partner_of(self.me, p, self.dp))

    def start(self, k):
        for p in range(self.dp - 1, 0, -1):
            self.out(k, p).start()

    def middle(self, k):
        for p in range(1, self.dp):
            self.out(k, p).wait_recv()
        total = add_up(self.piece(self.total[k], self.me)[...], *[self.slots[k][p] for p in range(1, self.dp)])
        self.piece(self.result[k], self.me)[...] = total.astype(self.result[k].dtype)
        for p in range(self.dp - 1, 0, -1):
            self.back(k, p).start()

    def finish(self, k):
        for p in range(1, self.dp):
            self.out(k, p).wait_send()
            self.back(k, p).wait()

    @staticmethod
    def semaphores(dp, count):
        return [pltpu.SemaphoreType.DMA((count, dp))] * 4


class Closing:
    lines = 64

    def __init__(self, row, dp, units_ref, attn_ref, lines_ref, given, results, refs):
        self.row, self.lines_ref, self.dp = row, lines_ref, dp
        self.full, shard, small, above = results
        core_in, y_out, y_in = refs[:3]
        mine, x_in, half, z_in, self.s_core, self.s_one, self.s_y, self.s_mine, s_slots, wide_in = refs[7:17]
        x_above, half_above, z_above = refs[17:20]
        refs_sems, refs = refs[3:7], refs[20:]
        self.mine = mine
        self.sums = RowSum(row, blocks(units_ref) + [attn_ref], core_in, y_out, y_in, blocks(mine), refs_sems)
        self.gather = RowGather(
            row, [mine.at[k] for k in range(2)], blocks(self.full), row.place, row.place_across, refs[:6]
        )
        self.s_pair = to_row(lines_ref, self.s_core, refs[6:8], 0, row.sibling)
        self.s_cross = to_row(self.s_one, self.s_y, refs[8:10], 0, row.across)
        self.here = DeepSum(
            dp, [mine.at[0], mine.at[1]], blocks(x_in), blocks(half), blocks(z_in), [shard.at[0], shard.at[1]], refs[10:18]
        )
        self.above = DeepSum(
            dp, [None, *given[1:]], [None] + blocks(x_above), [given[0]] + blocks(half_above), blocks(z_above), blocks(above),
            refs[18:26],
        )
        self.wide = WideSum(dp, [mine.at[2], self.s_mine], [wide_in, s_slots], [shard.at[2], small], refs[26:30])

    def enter(self):
        greet(self.dp, lax.axis_index("dp"), (self.row.sibling, self.row.across))
        for k in range(2):
            self.sums.start(k)
        self.above.deepen(0)
        for k in (1, 2):
            self.above.over_x(k).start()

    def early(self):
        for k in (1, 2):
            self.above.halve(k)
            self.above.deepen(k)
        self.above.quarter(0)

    def take(self, k):
        self.sums.end(k)
        self.here.over_x(k).start()
        self.gather.start(k)
        self.full[k, self.row.place] = self.mine[k]
        if k == 0:
            self.above.widen(0)
            for j in (1, 2):
                self.above.quarter(j)
        else:
            for j in (1, 2):
                self.above.widen(j)

    def open(self):
        self.sums.start(2)

    def cross(self):
        self.sums.middle(2)
        for k in range(2):
            self.here.halve(k)
            self.here.deepen(k)
        self.gather.forward(0)

    def send_lines(self):
        self.s_pair.start()
        for k in range(2):
            self.here.quarter(k)
        self.s_pair.wait_recv()
        self.s_one[...] = self.lines_ref[...] + self.s_core[...]
        self.s_cross.start()

    def finish(self):
        self.sums.end(2)
        self.wide.start(0)
        self.s_cross.wait_recv()
        self.s_mine[...] = self.s_one[...] + self.s_y[...]
        self.wide.start(1)
        self.gather.forward(1)
        for k in range(2):
            self.here.widen(k)
        self.wide.middle(0)
        self.wide.middle(1)
        self.s_pair.wait_send()
        self.s_cross.wait_send()
        for k in range(3):
            self.sums.finish(k)
            self.above.finish(k, k > 0)
        for k in range(2):
            self.here.finish(k)
            self.wide.finish(k)
            self.gather.arrive(k)
            self.gather.sent(k)

    @classmethod
    def scratch(cls, dp, width):
        deep = dp // 2
        lines = cls.lines
        flat = pltpu.VMEM((lines, width), f32)
        half, slots = (width // 2, width), (deep, width // dp, width)
        return (
            RowSum.scratch(3, width)
            + [
                pltpu.VMEM((3, width, width), bf16),
                pltpu.VMEM((2, *half), bf16),
                pltpu.VMEM((2, *half), bf16),
                pltpu.VMEM((2, *slots), bf16),
                flat, flat, flat, flat,
                pltpu.VMEM((dp, lines // dp, width), f32),
                pltpu.VMEM((dp, width // dp, width), bf16),
                pltpu.VMEM((2, *half), bf16),
                pltpu.VMEM((2, *half), bf16),
                pltpu.VMEM((3, *slots), bf16),
            ]
            + RowGather.scratch(2)
            + [pltpu.SemaphoreType.DMA((1,))] * 4
            + DeepSum.semaphores(dp, 2)
            + DeepSum.semaphores(dp, 3)
            + WideSum.semaphores(dp, 2)
        )


def format_kernel(columns, *refs):
    count = (len(refs) - 6) // 2
    qkv_out, proj_out, core_up_out, core_down_out, up_out, down_out = refs[2 * count :]

    def form(full, shard):
        mp, width = full.shape[1], full.shape[2]
        rows = width // mp
        qkv_out[0] = shard[2, :columns].astype(f32)
        proj_out[0] = shard[2, columns:].astype(f32)
        core_up_out[0] = shard[0].astype(f32)
        for place in range(mp):
            q = quarter_at(place, mp)
            up_out[0, 0, :, q * width : (q + 1) * width] = full[0, place].astype(f32)
        for chunk in range(mp):
            at = slice(chunk * width, (chunk + 1) * width)
            core_down_out[0, :, at] = shard[1, chunk * rows : (chunk + 1) * rows].astype(f32)
            block = [None] * mp
            for place in range(mp):
                block[quarter_at(place, mp)] = full[1, place, chunk * rows : (chunk + 1) * rows]
            down_out[0, 0, at, :] = turn_blocks(jnp.concatenate(block, 0))

    for layer in range(count):
        pl.when(pl.program_id(0) == layer)(functools.partial(form, refs[layer], refs[count + layer]))


def format_call(fulls, shards, columns):
    layers = len(fulls)
    _, mp, width, _ = fulls[0].shape
    hidden = mp * width
    shapes = [
        (layers, columns, width),
        (layers, width - columns, width),
        (layers, width, width),
        (layers, width // mp, hidden),
        (layers, 1, width, hidden),
        (layers, 1, hidden, width),
    ]
    return pl.pallas_call(
        functools.partial(format_kernel, columns),
        grid=(layers,),
        out_shape=[jax.ShapeDtypeStruct(shape, f32) for shape in shapes],
        in_specs=[whole_spec(a.shape) for a in (*fulls, *shards)],
        out_specs=[image_spec(shape, 1) for shape in shapes],
        compiler_params=pltpu.CompilerParams(vmem_limit_bytes=56 * MIB),
        name="format",
    )(*fulls, *shards)


def greet(dp, me, rows=()):
    barrier = pltpu.get_barrier_semaphore()
    for row in rows:
        pl.semaphore_signal(barrier, inc=1, device_id={"mp": row}, device_id_type=MESH)

    def signal(off, carry):
        pl.semaphore_signal(barrier, inc=1, device_id={"dp": lax.rem(me + off, dp)}, device_id_type=MESH)
        return carry

    lax.fori_loop(1, dp, signal, 0)
    pl.semaphore_wait(barrier, dp - 1 + len(rows))


def partner_of(me, p, dp):
    out, bit = 0, 1
    while bit < dp:
        one, two = lax.rem(lax.div(me, bit), 2), lax.rem(lax.div(p, bit), 2)
        out = out + bit * (one + two - 2 * one * two)
        bit *= 2
    return out


def to_peer(source, target, send_sem, recv_sem, peer):
    return pltpu.make_async_remote_copy(
        src_ref=source,
        dst_ref=target,
        send_sem=send_sem,
        recv_sem=recv_sem,
        device_id={"dp": peer},
        device_id_type=MESH,
    )


def gelu_parts(h):
    root = np.float32(np.sqrt(2.0 / np.pi))
    square = h * h
    t = jnp.tanh(root * h * (1.0 + 0.044715 * square))
    half = 0.5 * (1.0 + t)
    slope = half + 0.5 * h * (1.0 - t * t) * root * (1.0 + 3 * 0.044715 * square)
    return h * half, slope


def expert_forward_kernel(dp, mp, layer, gather, *refs):
    refs = list(refs)
    buffer_ref, up_any, down_any, rup_any, rdown_any = refs[:5]
    refs = refs[5:]
    if gather:
        shards = [ref.at[layer + 1] for ref in refs[:4]]
        refs = refs[4:]
    recv_ref, returned_ref, up_eff, down_eff = refs[:4]
    refs = refs[4:]
    if gather:
        fulls = refs[:4]
        refs = refs[4:]
    part, core, up_ref, down_ref, rup_ref, rdown_ref, local = refs[:7]
    refs = refs[7:]
    moving = WeightGather(shards, fulls, refs[:7]) if gather else None
    send_one, recv_one, send_two, recv_two = refs[-4:]
    split = dp // EXPERTS
    me = lax.axis_index("dp")
    loads = [
        pltpu.make_async_copy(source, target, local.at[k])
        for k, (source, target) in enumerate(
            [
                (up_any, up_ref),
                (rup_any.at[layer, 0], rup_ref),
                (down_any, down_ref),
                (rdown_any.at[layer, 0], rdown_ref),
            ]
        )
    ]
    for load in loads:
        load.start()
    greet(dp, me, (moving.row.sibling, moving.row.across) if gather else ())

    def first(off):
        peer = partner_of(me, off, dp)
        return to_peer(
            buffer_ref.at[lax.div(peer, split)], recv_ref.at[me], send_one.at[off], recv_one.at[off], peer
        )

    def second(off):
        source = partner_of(me, off, dp)
        return to_peer(part.at[source], returned_ref.at[me], send_two.at[off], recv_two.at[off], source)

    def start_first(off, carry):
        first(dp - off).start()
        return carry

    lax.fori_loop(1, dp, start_first, 0)
    if gather:
        for k in range(4):
            moving.start(k)
    recv_ref[me] = buffer_ref[lax.div(me, split)]
    hidden = up_eff.shape[1]
    columns = up_ref.shape[-1]
    loads[0].wait()
    loads[1].wait()
    if split == 1 and columns % LANES == 0:
        for m in range(mp):
            at = slice(m * columns, (m + 1) * columns)
            up_eff[:, at] = (up_ref[m].astype(f32) + rup_ref[:, at].astype(f32)).astype(bf16)
    else:
        core[...] = rup_ref[...].astype(f32)
        begin = lax.rem(me, split) * hidden
        for m in range(mp):
            put = onehot(iota((columns, hidden), 0) + m * columns == iota((columns, hidden), 1) + begin)
            core[...] += nn(up_ref[m], put)
        up_eff[...] = core[...].astype(bf16)
    begin = pl.multiple_of(lax.rem(me, split) * hidden, LANES)
    loads[2].wait()
    loads[3].wait()
    core_part = down_ref[:, :, pl.ds(begin, hidden)].reshape(down_eff.shape[1], hidden)
    down_eff[...] = (turn_blocks(core_part) + rdown_ref[...].astype(f32)).astype(bf16)

    def work(source):
        hidden_pre = nn(recv_ref[source], up_eff[...])
        hidden_low = gelu_parts(hidden_pre)[0].astype(bf16)
        return nn(hidden_low, down_eff[...]).astype(bf16)

    returned_ref[me] = work(me)

    def step(off, carry):
        source = partner_of(me, off, dp)
        first(off).wait_recv()
        part[source] = work(source)
        second(off).start()
        return carry

    lax.fori_loop(1, dp, step, 0)
    if gather:
        for k in range(4):
            moving.forward(k)

    def finish(off, carry):
        first(off).wait_send()
        second(off).wait()
        return carry

    lax.fori_loop(1, dp, finish, 0)
    if gather:
        for k in range(4):
            moving.arrive(k)
            moving.sent(k)


def expert_backward_kernel(dp, mp, fast, reduce, *refs):
    refs = list(refs)
    buffer_ref, recv_ref, up_ref, down_ref = refs[:4]
    refs = refs[4:]
    if reduce:
        given_ref, attn_ref = refs[:2]
        refs = refs[2:]
    returned_ref = refs.pop(0)
    if fast:
        units_ref = refs.pop(0)
    else:
        up_term, down_term = refs[:2]
        refs = refs[2:]
    if reduce:
        full_ref, mine_ref = refs[:2]
        refs = refs[2:]
    grads, hidden_low, slope, pre, part = refs[:5]
    refs = refs[5:]
    if fast:
        up_term, down_term = refs[:2]
        refs = refs[2:]
    row = Row() if reduce else None
    if reduce:
        core_in, y_out, y_in = refs[:3]
        sums = RowSum(row, [attn_ref], core_in, y_out, y_in, [mine_ref], refs[3:7])
        gather = RowGather(
            row, [given_ref.at[k] for k in range(2)], [full_ref.at[k] for k in range(2)], row.place, row.place_across,
            refs[7:13],
        )
        refs = refs[13:]
    send_one, recv_one, send_two, recv_two = refs
    split = dp // EXPERTS
    me = lax.axis_index("dp")
    greet(dp, me, (row.sibling, row.across) if reduce else ())

    def first(off):
        peer = partner_of(me, off, dp)
        return to_peer(buffer_ref.at[lax.div(peer, split)], grads.at[me], send_one.at[off], recv_one.at[off], peer)

    def second(off):
        source = partner_of(me, off, dp)
        return to_peer(part.at[source], returned_ref.at[me], send_two.at[off], recv_two.at[off], source)

    def start_first(off, carry):
        first(dp - off).start()
        return carry

    lax.fori_loop(1, dp, start_first, 0)
    if reduce:
        sums.start(0)
        for k in range(2):
            gather.start(k)
    grads[me] = buffer_ref[lax.div(me, split)]

    def again(source, carry):
        value, rate = gelu_parts(nn(recv_ref[source], up_ref[...]))
        hidden_low[source] = value.astype(bf16)
        slope[source] = rate
        return carry

    lax.fori_loop(0, dp, again, 0)
    if reduce:
        sums.middle(0)
        for k in range(2):
            full_ref[k, row.place] = given_ref[k]

    def work(source):
        hidden_grad = nt(grads[source], down_ref[...])
        pre_grad = (slope[source] * hidden_grad).astype(bf16)
        pre[source] = pre_grad
        return nt(pre_grad, up_ref[...]).astype(bf16)

    returned_ref[me] = work(me)

    def step(off, carry):
        source = partner_of(me, off, dp)
        first(off).wait_recv()
        part[source] = work(source)
        second(off).start()
        return carry

    lax.fori_loop(1, dp, step, 0)
    if reduce:
        for k in range(2):
            gather.forward(k)
        sums.end(0)
    up_term[...] = jnp.zeros(up_term.shape, f32)
    down_term[...] = jnp.zeros(down_term.shape, f32)

    def terms(block, carry):
        up_term[...] += tn(recv_ref[block], pre[block])
        down_term[...] += tn(grads[block], hidden_low[block])
        return carry

    lax.fori_loop(0, dp, terms, 0)
    if fast:
        width = up_term.shape[0]
        height = width // mp
        for place in range(mp):
            q = quarter_at(place, mp)
            units_ref[0, place] = up_term[:, q * width : (q + 1) * width].astype(bf16)
            for chunk in range(mp):
                block = down_term[q * height : (q + 1) * height, chunk * width : (chunk + 1) * width]
                units_ref[1, place, chunk * height : (chunk + 1) * height] = block.astype(bf16)

    def finish(off, carry):
        first(off).wait_send()
        second(off).wait()
        return carry

    lax.fori_loop(1, dp, finish, 0)
    if reduce:
        sums.finish(0)
        for k in range(2):
            gather.arrive(k)
            gather.sent(k)


def expert_call(kernel, arrays, outs, scratch, dp, collective_id, name, flops, anys=(), any_outs=()):
    sems = [pltpu.SemaphoreType.DMA((dp,))] * 4
    vmem, anywhere = pl.BlockSpec(memory_space=pltpu.VMEM), pl.BlockSpec(memory_space=pl.ANY)
    return pl.pallas_call(
        kernel,
        out_shape=[jax.ShapeDtypeStruct(shape, dtype) for shape, dtype in (*outs, *any_outs)],
        in_specs=[vmem] * len(arrays) + [anywhere] * len(anys),
        out_specs=[vmem] * len(outs) + [anywhere] * len(any_outs),
        scratch_shapes=scratch + sems,
        compiler_params=pltpu.CompilerParams(
            vmem_limit_bytes=56 * MIB, collective_id=collective_id, has_side_effects=True
        ),
        cost_estimate=pl.CostEstimate(flops=flops, bytes_accessed=20 * MIB, transcendentals=0),
        name=name,
    )(*arrays, *anys)


def by_windows(grid):
    images, kinds = grid.shape[:2]
    blocks = GRID // WINDOW
    grid = grid.reshape(images, kinds, blocks, WINDOW, blocks, WINDOW).transpose(0, 1, 2, 4, 3, 5)
    grid = grid.reshape(images, kinds, blocks * blocks, WINPOS)
    grid = jnp.pad(grid, ((0, 0), (0, 0), (0, 0), (0, WPAD - WINPOS)), constant_values=-1)
    return grid.reshape(images, kinds, IMGROWS)


def per_device(
    patches,
    qkv_weight,
    proj_weight,
    core_up,
    core_down,
    residual_up,
    residual_down,
    position_bias,
    router_weight,
    norm_gain,
    norm_bias,
    cotangent,
    image_valid,
    expert_index,
    slot_index,
    region_id,
):
    dp, mp = lax.axis_size("dp"), lax.axis_size("mp")
    images, _, width = patches.shape
    split = dp // EXPERTS
    hidden = residual_up.shape[-1]
    hidden_full = core_up.shape[-1] * mp
    row_index = lax.axis_index("mp")

    fast = split == 1 and dp == 8 and mp == 4 and hidden == mp * width
    qkv_rows, proj_rows, down_rows = (a.transpose(0, 2, 1) for a in (qkv_weight, proj_weight, core_down))
    shards = (qkv_rows, proj_rows, core_up, down_rows)
    gathered = [[None] * len(shards)] * LAYERS
    if not fast:
        gathered = [[lax.all_gather(a[l], "mp", axis=0, tiled=False) for a in shards] for l in range(LAYERS)]

    position = jnp.where(slot_index >= 0, expert_index * SLOTS + slot_index, -1)
    row_form = by_windows(jnp.stack([position.reshape(images, GRID, GRID), region_id], 1))
    col_form = row_form.transpose(0, 2, 1)
    enter = jnp.asarray(enter_table(), bf16)
    leave = jnp.asarray(enter_table().T, bf16)
    moves = [jnp.asarray(move_table(l % 2 == 1), bf16) for l in range(LAYERS)]
    backs = [jnp.asarray(move_table(l % 2 == 1).T, bf16) for l in range(LAYERS)]
    table_rows = position_bias.transpose(0, 2, 1).reshape(LAYERS * HEADS, OFFSETS)
    table_rows = jnp.pad(table_rows, ((0, 0), (0, TABLE - OFFSETS)))
    entry_row, entry_col = jnp.asarray(cell_entries()[None, :]), jnp.asarray(cell_entries()[:, None])
    routers = jnp.pad(router_weight.transpose(0, 2, 1), ((0, 0), (0, LANES - EXPERTS), (0, 0)))

    token = (images, IMGROWS, width)
    buffer_shape = (ROWS, width)
    block_rows = (dp, SLOTS, width)
    pieces = (split, ROWS, width)

    def by_piece(returned):
        return returned.reshape(EXPERTS, split, SLOTS, width).transpose(1, 0, 2, 3).reshape(pieces)

    records = []
    before = None
    for l in range(LAYERS):
        first = l == 0
        gather = fast and first
        if first:
            arrays = [("image", patches), ("whole", enter)]
        else:
            arrays = [("image", before[0]), ("image", before[1]), ("whole", before[2])]
        arrays += [
            ("smem", image_valid),
            ("image", col_form),
            ("image", row_form),
            ("any", qkv_rows) if gather else ("whole", gathered[l][0]),
            ("any", proj_rows) if gather else ("whole", gathered[l][1]),
            ("whole", table_rows) if first else (l, biases),
            ("whole", moves[l]),
            ("whole", backs[l]),
            (l, norm_gain),
            (l, norm_bias),
            (l, routers),
        ]
        if first:
            arrays.append(("whole", entry_row))
        if gather:
            arrays += [("any", core_up), ("any", down_rows)]
        outs = [("image", token, f32)]
        if first:
            outs.append(("whole", (LAYERS, HEADS, WPAD, LANES), f32))
        else:
            outs.append(("image", token, f32))
        outs += [
            ("image", token, f32),
            ("image", token, bf16),
            ("image", (images, IMGROWS, 1), f32),
            ("whole", buffer_shape, bf16),
            ("image", token, bf16),
            ("image", (images, 2 * width, IMGROWS), bf16),
            ("image", token, bf16),
            ("image", (images, PAIRS * HEADS, WPAD, LANES), bf16),
            ("image", (images, width, IMGROWS), bf16),
            ("whole", (width, width), bf16),
        ]
        scratch = [pltpu.VMEM(buffer_shape, f32)]
        gathered_shapes = [(mp, *a.shape[1:]) for a in shards]
        if gather:
            outs.append(("whole", (3 * width, width), bf16))
            outs += [("any", shape, bf16) for shape in gathered_shapes[2:]]
            scratch += [pltpu.VMEM(shape, bf16) for shape in gathered_shapes[:2]] + WeightGather.scratch(4)
        results = list(
            image_call(
                functools.partial(attention_forward_kernel, first, l % 2 == 1, mp, gather),
                images, arrays, outs, scratch, f"attend_{l}", 3 * LAYERS + 1 if gather else None,
            )
        )
        if gather:
            gathered[l] = [results[-3], None] + results[-2:]
            results = results[:-3]
        carried = results.pop(0)
        if first:
            biases = results.pop(0)
        else:
            records[-1]["expert_out"] = results.pop(0)
        middle, second_low, gate, buffer = results[:4]
        gather = fast and l < LAYERS - 1
        received, returned, up_eff, down_eff, *more = expert_call(
            functools.partial(expert_forward_kernel, dp, mp, l, gather),
            [buffer.reshape(EXPERTS, SLOTS, width)],
            [
                (block_rows, bf16),
                (block_rows, bf16),
                ((width, hidden), bf16),
                ((hidden, width), bf16),
            ],
            [
                pltpu.VMEM(block_rows, bf16),
                pltpu.VMEM((8, LANES) if fast else (width, hidden), f32),
                pltpu.VMEM(gathered_shapes[2], bf16),
                pltpu.VMEM(gathered_shapes[3], bf16),
                pltpu.VMEM((width, hidden), bf16),
                pltpu.VMEM((hidden, width), bf16),
                pltpu.SemaphoreType.DMA((4,)),
            ]
            + (WeightGather.scratch(4) if gather else []),
            dp, l, f"experts_{l}", 4 * dp * SLOTS * width * hidden,
            [gathered[l][2], gathered[l][3], residual_up, residual_down, *(shards if gather else ())],
            [(shape, bf16) for shape in gathered_shapes] if gather else (),
        )
        if gather:
            gathered[l + 1] = more
        returned = by_piece(returned)
        before = (middle, gate, returned)
        records.append(
            dict(
                carried=carried, middle=middle, second_low=second_low, gate=gate, saved=results[4:], received=received,
                up_eff=up_eff, down_eff=down_eff,
            )
        )

    top = records[-1]
    block_output, grad, logit_grad, router_part, buffer = image_call(
        turn_kernel,
        images,
        [
            ("image", before[0]),
            ("image", before[1]),
            ("whole", before[2]),
            ("image", cotangent),
            ("whole", enter),
            ("whole", leave),
            ("image", col_form),
            ("image", row_form),
            ("image", top["second_low"]),
            (LAYERS - 1, routers),
        ],
        [
            ("image", patches.shape, bf16),
            ("image", token, f32),
            ("image", (images, IMGROWS, LANES), f32),
            ("whole", (LANES, width), f32),
            ("whole", buffer_shape, bf16),
        ],
        [pltpu.VMEM(buffer_shape, f32)],
        "turn",
    )
    router_parts, tables, smalls = [None] * LAYERS, [None] * LAYERS, [None] * LAYERS
    residual_sums, shard_sums = [None] * LAYERS, [None] * LAYERS
    router_parts[LAYERS - 1] = router_part
    units, attn_units, mines = [None] * LAYERS, [None] * LAYERS, [None] * LAYERS
    for l in reversed(range(LAYERS)):
        rec = records[l]
        last = l == 0
        reduce = fast and l < LAYERS - 1
        arrays = [buffer.reshape(EXPERTS, SLOTS, width), rec["received"], rec["up_eff"], rec["down_eff"]]
        outs = [(block_rows, bf16)]
        scratch = [
            pltpu.VMEM(block_rows, bf16),
            pltpu.VMEM((dp, SLOTS, hidden), bf16),
            pltpu.VMEM((dp, SLOTS, hidden), f32),
            pltpu.VMEM((dp, SLOTS, hidden), bf16),
            pltpu.VMEM(block_rows, bf16),
        ]
        if fast:
            outs.append(((2, mp, width, width), bf16))
            scratch += [pltpu.VMEM((width, hidden), f32)] * 2
        else:
            outs += [((width, hidden), f32)] * 2
        if reduce:
            arrays += [mines[l + 1], attn_units[l + 1]]
            outs += [((2, mp, width, width), bf16), ((width, width), bf16)]
            scratch += RowSum.scratch(1, width) + RowGather.scratch(2)
        results = list(
            expert_call(
                functools.partial(expert_backward_kernel, dp, mp, fast, reduce), arrays, outs, scratch, dp, LAYERS + l,
                f"experts_back_{l}", 10 * dp * SLOTS * width * hidden,
            )
        )
        returned_grad = results.pop(0)
        if fast:
            units[l] = results.pop(0)
        else:
            residual_sums[l] = lax.psum(tuple(t.astype(bf16) for t in results[:2]), "mp")
        if reduce:
            full_above, mine_above = results
        window_in, qk, v, probs, att, proj_full = rec["saved"]
        qkv_full = gathered[l][0].reshape(3 * width, width)
        arrays = [
            ("smem", image_valid),
            ("image", grad),
            ("whole", by_piece(returned_grad)),
            ("image", logit_grad),
            ("image", rec["middle"]),
            ("image", rec["carried"]),
            (l, routers),
            ("image", col_form),
            ("whole", moves[l]),
            ("whole", backs[l]),
            (l, norm_gain),
            ("whole", proj_full),
            ("whole", qkv_full),
            ("image", window_in),
            ("image", qk),
            ("image", v),
            ("image", probs),
            ("image", att),
        ]
        outs = [("image", patches.shape if last else token, f32)]
        scratch = [pltpu.VMEM((3 * width, (2 - images % 2) * IMGROWS), bf16)]
        closes = fast and last
        table_shape, small_shape = (HEADS, WPAD, LANES), (8, width)
        if fast:
            arrays.append(("whole", units[l]))
            scratch += [pltpu.VMEM((3 * width, width), f32), pltpu.VMEM((width, width), f32)]
        if closes:
            outs += [
                ("whole", (2, mp, width, width), bf16),
                ("whole", (3, width, width), bf16),
                ("whole", (Closing.lines, width), f32),
                ("whole", (3, width, width), bf16),
            ]
        else:
            if fast:
                outs += [
                    ("whole", (width // 2, width), bf16),
                    ("whole", (mp, width, width), bf16),
                    ("whole", (2, width, width), bf16),
                ]
            else:
                outs += [("whole", (3 * width, width), f32), ("whole", (width, width), f32)]
            outs += [("whole", table_shape, f32), ("whole", small_shape, f32)]
        if last:
            arrays.append(("whole", leave))
            if fast:
                arrays += [
                    ("whole", a)
                    for a in (
                        tables[1], smalls[1], router_parts[1], router_parts[0], entry_col, halves_above, mines[1],
                        mine_above,
                    )
                ]
        else:
            below = records[l - 1]
            arrays += [
                ("image", row_form),
                ("image", below["expert_out"]),
                ("image", below["second_low"]),
                (l - 1, routers),
            ]
            outs += [
                ("image", (images, IMGROWS, LANES), f32),
                ("whole", (LANES, width), f32),
                ("whole", buffer_shape, bf16),
            ]
            scratch.append(pltpu.VMEM(buffer_shape, f32))
        if closes:
            scratch += [
                pltpu.VMEM(table_shape, f32),
                pltpu.VMEM(small_shape, f32),
                pltpu.VMEM((mp, width, width), bf16),
                pltpu.VMEM((Closing.lines, width), f32),
            ]
            scratch += [pltpu.VMEM(shape, dtype) for _, shape, dtype in outs[1:5]] + Closing.scratch(dp, width)
        elif fast:
            scratch += RowSum.scratch(2, width) + [pltpu.VMEM((width // 2, width), bf16)]
            scratch += [pltpu.SemaphoreType.DMA((1,))] * 2
        results = list(
            image_call(
                functools.partial(attention_backward_kernel, last, dp, mp, fast),
                images, arrays, outs, scratch, f"attend_back_{l}", 2 * LAYERS + 1 + l if fast else None,
            )
        )
        grad = results.pop(0)
        if closes:
            full, closed, lines, shard_above = results
            continue
        if fast:
            halves_above = results.pop(0)
            attn_units[l], mines[l] = results[:2]
        else:
            qkv_part, proj_part = results[:2]
        tables[l], smalls[l] = results[2:4]
        if not last:
            logit_grad, router_parts[l - 1], buffer = results[4:]
        if fast:
            continue
        attn = (
            lax.psum_scatter(qkv_part.astype(bf16), "mp", scatter_dimension=0, tiled=True),
            lax.psum_scatter(proj_part.T.astype(bf16), "mp", scatter_dimension=0, tiled=True),
        )
        up_sum, down_sum = residual_sums[l]
        if split > 1:
            begin = lax.axis_index("dp") % split * hidden
            empty = jnp.zeros((width, hidden_full), bf16)
            up_sum = lax.dynamic_update_slice_in_dim(empty, up_sum, begin, 1)
            down_sum = lax.dynamic_update_slice_in_dim(empty, down_sum, begin, 1)
        up_columns, down_columns = core_up.shape[-1], core_down.shape[-1]
        up_shard = lax.dynamic_slice_in_dim(up_sum, row_index * up_columns, up_columns, 1)
        down_shard = lax.dynamic_slice_in_dim(down_sum, row_index * down_columns, down_columns, 0)
        shard_sums[l] = lax.psum((attn[0], attn[1], up_shard, down_shard), "dp")

    if fast:
        *attn_grads, core_up_grad, core_down_grad, residual_up_grad, residual_down_grad = format_call(
            [full, full_above], [closed, shard_above], qkv_weight.shape[-1]
        )
        attn_grads = [a.transpose(0, 2, 1) for a in attn_grads]
        core_grads = (core_up_grad, core_down_grad.transpose(0, 2, 1))
        at = LAYERS * HEADS
        table_sum = lines[:at, :OFFSETS]
        router_sum = lines[at : at + LAYERS * EXPERTS].reshape(LAYERS, EXPERTS, width)
        at += LAYERS * EXPERTS
        small_sum = lines[at : at + LAYERS * 8].reshape(LAYERS, 8, width)[:, :4]
    else:
        entry = cell_entries()[None, :] + np.array([key_base_of(key) for key in range(WPAD)])[:, None]
        entry = jnp.asarray(np.where(np.arange(WPAD)[:, None] < WINPOS, entry, -1).reshape(-1))
        entry_turned = (entry[:, None] == jnp.arange(OFFSETS)[None, :]).astype(f32)
        table_part = jnp.dot(
            jnp.stack(tables, 0).reshape(LAYERS * HEADS, WPAD * LANES), entry_turned, precision=highest
        )
        small_part = jnp.stack(smalls, 0)[:, :4]
        router_part = jnp.stack(router_parts, 0)[:, :EXPERTS]
        table_sum, small_sum, router_sum = lax.psum((table_part, small_part, router_part), ("dp", "mp"))

        def shard(k):
            return jnp.stack([shard_sums[l][k] for l in range(LAYERS)], 0).astype(f32)

        attn_grads = (shard(0).transpose(0, 2, 1), shard(1).transpose(0, 2, 1))
        core_grads = (shard(2), shard(3).transpose(0, 2, 1))
        residual_up_grad, residual_down_grad = (
            jnp.stack([residual_sums[l][k] for l in range(LAYERS)], 0).astype(f32) for k in range(2)
        )
        residual_up_grad = residual_up_grad[:, None]
        residual_down_grad = residual_down_grad.transpose(0, 2, 1)[:, None]

    return (
        block_output,
        grad,
        attn_grads[0],
        attn_grads[1],
        core_grads[0],
        core_grads[1],
        residual_up_grad,
        residual_down_grad,
        table_sum.reshape(LAYERS, HEADS, OFFSETS).transpose(0, 2, 1),
        router_sum.transpose(0, 2, 1),
        small_sum[:, 0:2],
        small_sum[:, 2:4],
    )


def solution(mesh):
    placed = (
        P(("dp", "mp"), None, None),
        P(None, None, "mp"),
        P(None, None, "mp"),
        P(None, None, "mp"),
        P(None, None, "mp"),
        P(None, "dp", None, None),
        P(None, "dp", None, None),
        P(),
        P(),
        P(),
        P(),
        P(("dp", "mp"), None, None),
        P(("dp", "mp")),
        P(("dp", "mp"), None),
        P(("dp", "mp"), None),
        P(("dp", "mp"), None, None),
    )
    return jax.shard_map(
        per_device,
        mesh=mesh,
        in_specs=placed,
        out_specs=(
            P(("dp", "mp"), None, None),
            P(("dp", "mp"), None, None),
            P(None, None, "mp"),
            P(None, None, "mp"),
            P(None, None, "mp"),
            P(None, None, "mp"),
            P(None, "dp", None, None),
            P(None, "dp", None, None),
            P(),
            P(),
            P(),
            P(),
        ),
        check_vma=False,
    )
```

```python
import functools

import jax
import jax.numpy as jnp
import numpy as np
from jax import lax
from jax.experimental import pallas as pl
from jax.experimental.pallas import tpu as pltpu
from jax.sharding import PartitionSpec as P

HEADS = 12
HEAD_DIM = 32
EXPERTS = 8
WINDOW = 7
GRID = 14
SHIFT = 3
LAYERS = 2
WINPOS = 49
OFFSETS = 169
CAP = 122

WPAD = 64
IMGROWS = 256
PATCHES = 196
SLOTS = 128
ROWS = EXPERTS * SLOTS
LANES = 128
GROUP = 4
PAIRS = 2
TABLE = 256

bf16 = jnp.bfloat16
f32 = jnp.float32
highest = lax.Precision.HIGHEST
norm_epsilon = 1e-05
mask_fill = -100.0
head_scale = HEAD_DIM ** (-0.5)
MESH = pl.DeviceIdType.MESH
MIB = 1024 * 1024


def nn(a, b):
    return lax.dot_general(a, b, (((1,), (0,)), ((), ())), preferred_element_type=f32)


def nt(a, b):
    return lax.dot_general(a, b, (((1,), (1,)), ((), ())), preferred_element_type=f32)


def tn(a, b):
    return lax.dot_general(a, b, (((0,), (0,)), ((), ())), preferred_element_type=f32)


def iota(shape, dim):
    return lax.broadcasted_iota(jnp.int32, shape, dim)


def onehot(flags):
    return jnp.where(flags, 1.0, 0.0).astype(bf16)


def natural_of_row(shifted):
    moved = SHIFT if shifted else 0
    blocks = GRID // WINDOW
    out = -np.ones(IMGROWS, np.int32)
    for window in range(blocks * blocks):
        for cell in range(WINPOS):
            row = (window // blocks * WINDOW + cell // WINDOW + moved) % GRID
            col = (window % blocks * WINDOW + cell % WINDOW + moved) % GRID
            out[window * WPAD + cell] = row * GRID + col
    return out


def key_base_of(key):
    return (2 * WINDOW) * (WINDOW - 1) - (key // WINDOW * (2 * WINDOW - 1) + key % WINDOW)


def enter_table():
    held = natural_of_row(False)
    return (held[:, None] == np.arange(PATCHES)[None, :]).astype(np.float32)


def move_table(shifted):
    first, second = natural_of_row(False), natural_of_row(shifted)
    same = (second[:, None] == first[None, :]) & (second[:, None] >= 0)
    return same.astype(np.float32)


def cell_entries():
    cell = np.arange(LANES) % WPAD
    return np.where(cell < WINPOS, cell // WINDOW * (2 * WINDOW - 1) + cell % WINDOW, -4 * TABLE).astype(np.int32)


def norm_parts(x):
    width = x.shape[-1]
    center = x - jnp.sum(x, -1, keepdims=True) * (1.0 / width)
    spread = jnp.sum(center * center, -1, keepdims=True) * (1.0 / width)
    rstd = lax.rsqrt(spread + norm_epsilon)
    return center * rstd, rstd


def norm_back(grad, gain, xhat, rstd):
    width = xhat.shape[-1]
    dxhat = grad * gain
    mean_one = jnp.sum(dxhat, -1, keepdims=True) * (1.0 / width)
    mean_two = jnp.sum(dxhat * xhat, -1, keepdims=True) * (1.0 / width)
    return rstd * (dxhat - mean_one - xhat * mean_two)


def turn_blocks(x):
    size = x.shape[0]
    same = onehot(iota((size, size), 0) == iota((size, size), 1))
    return jnp.concatenate([nt(same, x[:, at : at + size]) for at in range(0, x.shape[1], size)], 0)


def split_two(x):
    high = x.astype(bf16)
    return high, (x - high.astype(f32)).astype(bf16)


def collect(pos_col, returned_ref):
    pick = onehot(pos_col == iota((pos_col.shape[0], ROWS), 1))
    out = nn(pick, returned_ref[0])
    for piece in range(1, returned_ref.shape[0]):
        out = out + nn(pick, returned_ref[piece])
    return out


def join(ref):
    return ref[...].reshape(ref.shape[0] * ref.shape[1], *ref.shape[2:])


def store(ref, rows):
    ref[...] = rows.reshape(ref.shape).astype(ref.dtype)


def per_image(function, count):
    return jnp.concatenate([function(i) for i in range(count)], 0)


def image_rows(i):
    return slice(i * IMGROWS, (i + 1) * IMGROWS)


def lay_positions(row_ref):
    return jnp.concatenate([row_ref[i, 0:1, :] for i in range(row_ref.shape[0])], 1)


def spread_rows(pos_row, rows_low):
    return nn(onehot(iota((ROWS, pos_row.shape[1]), 0) == pos_row), rows_low)


def route(second_low, router, pos_col):
    logits = nt(second_low, router)
    lane = iota(logits.shape, 1)
    logits = jnp.where(lane < EXPERTS, logits, -1e30)
    expo = jnp.exp(logits - jnp.max(logits, -1, keepdims=True))
    probs = expo / jnp.sum(expo, -1, keepdims=True)
    expert = jnp.where(pos_col >= 0, pos_col // SLOTS, -1)
    chosen = jnp.where(lane == expert, 1.0, 0.0)
    return probs, chosen, jnp.sum(probs * chosen, -1, keepdims=True)


def head_masks():
    rows = iota((LANES, LANES), 0) // HEAD_DIM
    return [onehot(rows == h) for h in range(GROUP)]


def lane_masks():
    lane = iota((WPAD, LANES), 1)
    return [onehot(lane < WPAD), onehot(lane >= WPAD)]


def keys_entry(cells, key_row, turned):
    parts = [cells + (key_base_of(col) - key_row * (2 * WINDOW - 1)) for col in range(WINDOW)]
    return jnp.concatenate(parts, 0 if turned else 1)


def form_bias(bias_ref, table_ref, entry_row):
    layers, heads = bias_ref.shape[:2]
    lines = layers * heads
    bias_ref[...] = jnp.where(iota(bias_ref.shape, 2) < WINPOS, 0.0, -1e30)
    table = table_ref[...]
    high = table.astype(bf16)
    mid, low = split_two(table - high.astype(f32))
    parts = jnp.concatenate([high.astype(f32), mid.astype(f32), low.astype(f32)], 0).astype(bf16)

    def step(key_row, carry):
        pick = onehot(iota((TABLE, WINDOW * LANES), 0) == keys_entry(entry_row, key_row, False))
        rows = nn(parts, pick)
        rows = rows[:lines] + rows[lines : 2 * lines] + rows[2 * lines :]
        for col in range(WINDOW):
            for layer in range(layers):
                part = rows[layer * heads : (layer + 1) * heads, col * LANES : (col + 1) * LANES]
                bias_ref[layer, :, pl.ds(key_row * WINDOW + col, 1), :] = part.reshape(heads, 1, LANES)
        return carry

    lax.fori_loop(0, WINDOW, step, 0)


def table_grad(parts, entry_col):
    heads = parts[0].shape[0]
    lines = heads * len(parts)

    def step(key_row, total):
        keys = [
            jnp.concatenate([ref[:, pl.ds(key_row * WINDOW + col, 1), :].reshape(heads, LANES) for ref in parts], 0)
            for col in range(WINDOW)
        ]
        rows = jnp.concatenate(keys, 1)
        high = rows.astype(bf16).astype(f32)
        both = jnp.concatenate([high, rows - high], 0).astype(bf16)
        entry = keys_entry(entry_col, key_row, True)
        out = nn(both, onehot(iota((WINDOW * LANES, TABLE), 1) == entry))
        return total + out[:lines] + out[lines:]

    return lax.fori_loop(0, WINDOW, step, jnp.zeros((lines, TABLE), f32))


def attention_forward_kernel(first, shifted, mp, gather, *refs):
    refs = list(refs)
    if first:
        patches_ref, enter_ref = refs[:2]
        refs = refs[2:]
    else:
        prev_ref, prev_gate_ref, returned_ref = refs[:3]
        refs = refs[3:]
    (
        valid_ref, col_ref, row_ref, qkv_ref, proj_ref, bias_ref, move_ref, back_ref, gain_ref, nbias_ref, router_ref,
    ) = refs[:11]
    gain_ref, nbias_ref, router_ref = (ref.at[0] for ref in (gain_ref, nbias_ref, router_ref))
    refs = refs[11:]
    if first:
        table_ref, entry_ref = bias_ref, refs.pop(0)
    if gather:
        core_up_ref, core_down_ref = refs[:2]
        refs = refs[2:]
    carried_ref = refs.pop(0)
    if first:
        biases_ref = refs.pop(0)
        bias_ref = biases_ref.at[0]
    else:
        expert_out_ref = refs.pop(0)
        bias_ref = bias_ref.at[0]
    middle_ref, second_ref, gate_ref, buffer_ref, window_ref, qk_ref, v_ref, probs_ref, att_ref, proj_full = refs[:10]
    refs = refs[10:]
    if gather:
        qkv_full = refs.pop(0)
        up_out, down_out = refs[:2]
        refs = refs[2:]
    total_ref = refs.pop(0)
    step = pl.program_id(0)
    final = pl.num_programs(0) - 1
    count, _, width = carried_ref.shape
    if gather:
        shards = [ref.at[0] for ref in (qkv_ref, proj_ref, core_up_ref, core_down_ref)]
        qkv_ref, proj_ref = refs[:2]
        moving = WeightGather(shards, [qkv_ref, proj_ref, up_out, down_out], refs[2:])

        @pl.when(step == 0)
        def _():
            pl.semaphore_wait(moving.row.greet(), 2)
            for k in (0, 1):
                moving.start(k)
            form_bias(biases_ref, table_ref, entry_ref[...])

    pos_col = join(col_ref)[:, 0:1]
    if first:
        x = per_image(lambda i: nn(enter_ref[...], patches_ref[i]), count)
    else:
        expert_out = collect(pos_col, returned_ref)
        store(expert_out_ref, expert_out)
        x = join(prev_ref) + join(prev_gate_ref) * expert_out
    store(carried_ref, x)
    xhat, _ = norm_parts(x)
    normed = (xhat * gain_ref[0:1, :] + nbias_ref[0:1, :]).astype(bf16)
    window_in = per_image(lambda i: nn(move_ref[...], normed[image_rows(i)]), count).astype(bf16)
    store(window_ref, window_in)

    @pl.when(step == 0)
    def _():
        if gather:
            for k in (0, 1):
                moving.forward(k)
            for k in (2, 3):
                moving.start(k)
            for k in (0, 1):
                moving.arrive(k)
            qkv_full[...] = join(qkv_ref)
        elif first:
            form_bias(biases_ref, table_ref, entry_ref[...])
        proj_full[...] = turn_blocks(join(proj_ref)).astype(bf16)
        total_ref[...] = jnp.zeros(total_ref.shape, f32)

    qkv = join(qkv_ref)
    turned = nt(qkv, window_in).astype(bf16)
    straight = nt(window_in, qkv[width:]).astype(bf16)
    for i in range(count):
        qk_ref[i] = turned[: 2 * width, image_rows(i)]
    store(v_ref, straight[:, width:])
    heads_rows = head_masks()
    halves = lane_masks()
    low_lane = iota((WPAD, LANES), 1) < WPAD
    if shifted:
        row_labels = [nt(row_ref[i].astype(f32).astype(bf16), move_ref[...]) for i in range(count)]
        col_labels = [nn(move_ref[...], col_ref[i].astype(f32).astype(bf16)) for i in range(count)]
    for pair in range(PAIRS * count):
        image, side = pair // PAIRS, pair % PAIRS
        across = slice(pair * LANES, (pair + 1) * LANES)
        within = slice(side * LANES, (side + 1) * LANES)
        if shifted:
            ahead = col_labels[image][side * LANES : side * LANES + WPAD, 1:2]
            behind = col_labels[image][side * LANES + WPAD : (side + 1) * LANES, 1:2]
            key_label = jnp.where(low_lane, ahead, behind)
            mask = jnp.where(key_label == row_labels[image][1:2, within], 0.0, mask_fill)
        for group in range(HEADS // GROUP):
            features = slice(group * LANES, (group + 1) * LANES)
            queries = turned[features, across]
            spread = jnp.concatenate([queries * heads_rows[h] for h in range(GROUP)], 1)
            raw = nn(straight[across, features], spread)
            for h in range(GROUP):
                head = group * GROUP + h
                part = raw[:, h * LANES : (h + 1) * LANES]
                scores = jnp.where(low_lane, part[:WPAD], part[WPAD:]) * head_scale + bias_ref[head]
                if shifted:
                    scores = scores + mask
                expo = jnp.exp(scores - jnp.max(scores, 0, keepdims=True))
                probs = (expo * (1.0 / jnp.sum(expo, 0, keepdims=True))).astype(bf16)
                probs_ref[image, side * HEADS + head] = probs
                both = jnp.concatenate([probs * halves[0], probs * halves[1]], 0)
                at = slice(head * HEAD_DIM, (head + 1) * HEAD_DIM)
                values = turned[2 * width + head * HEAD_DIM : 2 * width + (head + 1) * HEAD_DIM, across]
                att_ref[image, at, within] = nn(values, both).astype(bf16)
    attended = per_image(lambda i: nt(back_ref[...], att_ref[i]), count).astype(bf16)
    branch = nt(attended, join(proj_ref))
    middle = x + per_image(lambda i: valid_ref[step * count + i].astype(f32) * branch[image_rows(i)], count)
    store(middle_ref, middle)
    xhat, _ = norm_parts(middle)
    second_low = (xhat * gain_ref[1:2, :] + nbias_ref[1:2, :]).astype(bf16)
    store(second_ref, second_low)
    _, _, gate = route(second_low, router_ref[...], pos_col)
    store(gate_ref, gate)
    total_ref[...] += spread_rows(lay_positions(row_ref), second_low)

    @pl.when(step == final)
    def _():
        buffer_ref[...] = total_ref[...].astype(bf16)
        if gather:
            for k in (2, 3):
                moving.forward(k)
            for k in (2, 3):
                moving.arrive(k)
            for k in range(4):
                moving.sent(k)


def image_spec(array_shape, count):
    rest = tuple(array_shape[1:])
    zeros = (0,) * len(rest)
    return pl.BlockSpec((count,) + rest, lambda i: (i,) + zeros)


def whole_spec(array_shape):
    zeros = (0,) * len(array_shape)
    return pl.BlockSpec(tuple(array_shape), lambda i: zeros)


def image_call(kernel, images, arrays, outs, scratch, name, collective_id=None):
    count = 2 - images % 2

    def spec(kind, shape):
        if isinstance(kind, int):
            rest = tuple(shape[1:])
            return pl.BlockSpec((1,) + rest, lambda i: (kind,) + (0,) * len(rest))
        if kind in ("smem", "any"):
            return pl.BlockSpec(memory_space=pltpu.SMEM if kind == "smem" else pl.ANY)
        return image_spec(shape, count) if kind == "image" else whole_spec(shape)

    return pl.pallas_call(
        kernel,
        grid=(images // count,),
        out_shape=[jax.ShapeDtypeStruct(shape, dtype) for _, shape, dtype in outs],
        in_specs=[spec(kind, array.shape) for kind, array in arrays],
        out_specs=[spec(kind, shape) for kind, shape, _ in outs],
        scratch_shapes=scratch,
        compiler_params=pltpu.CompilerParams(
            vmem_limit_bytes=56 * MIB,
            dimension_semantics=("arbitrary",),
            collective_id=collective_id,
            has_side_effects=collective_id is not None,
        ),
        name=name,
    )(*[array for _, array in arrays])


def send_part(g, expert_out, second_low, router, pos_col, pos_row, logit_ref, router_grad_ref, total_ref):
    probs, chosen, gate = route(second_low, router, pos_col)
    gate_grad = jnp.where(pos_col >= 0, jnp.sum(g * expert_out, -1, keepdims=True), 0.0)
    sent = (gate * g).astype(bf16)
    logit_grad = gate_grad * gate * (chosen - probs)
    store(logit_ref, logit_grad)
    high, low = split_two(logit_grad)
    router_grad_ref[...] += tn(high, second_low) + tn(low, second_low)
    total_ref[...] += spread_rows(pos_row, sent)


def turn_kernel(
    prev_ref, gate_ref, returned_ref, cotangent_ref, enter_ref, leave_ref, col_ref, row_ref, second_ref, router_ref,
    block_ref, grad_ref, logit_ref, router_grad_ref, buffer_ref, total_ref,
):
    step = pl.program_id(0)
    count = cotangent_ref.shape[0]

    @pl.when(step == 0)
    def _():
        total_ref[...] = jnp.zeros(total_ref.shape, f32)
        router_grad_ref[...] = jnp.zeros(router_grad_ref.shape, f32)

    pos_col = join(col_ref)[:, 0:1]
    expert_out = collect(pos_col, returned_ref)
    x = (join(prev_ref) + join(gate_ref) * expert_out).astype(bf16)
    for i in range(count):
        block_ref[i] = nn(leave_ref[...], x[image_rows(i)]).astype(bf16)
    g = per_image(lambda i: nn(enter_ref[...], cotangent_ref[i]), count)
    store(grad_ref, g)
    send_part(
        g, expert_out, join(second_ref), router_ref[0], pos_col, lay_positions(row_ref), logit_ref, router_grad_ref, total_ref
    )

    @pl.when(step == pl.num_programs(0) - 1)
    def _():
        buffer_ref[...] = total_ref[...].astype(bf16)


def attention_backward_kernel(last, dp, mp, fast, *refs):
    (
        valid_ref, grad_ref, returned_ref, logit_ref, middle_ref, carried_ref, router_ref, col_ref, move_ref, back_ref,
        gain_ref, proj_ref, qkv_ref, window_ref, qk_ref, v_ref, probs_ref, att_ref,
    ) = refs[:18]
    refs = refs[18:]
    refs = list(refs)
    if fast:
        units_ref = refs.pop(0)
    if last:
        leave_ref = refs.pop(0)
        if fast:
            table_above, small_above, router_above, router_here, entry_ref, half_above, down_above, attn_above = refs[:8]
            refs = refs[8:]
    else:
        row_ref, expert_out_ref, second_ref, router_next_ref = refs[:4]
        refs = refs[4:]
    out_ref = refs.pop(0)
    closing = None
    if fast and last:
        results, refs = refs[:4], refs[4:]
    else:
        if fast:
            halves_ref = refs.pop(0)
            unit_ref, mine_ref = refs[:2]
        else:
            qkv_grad_ref, proj_grad_ref = refs[:2]
        table_ref, small_ref = refs[2:4]
        refs = refs[4:]
    if not last:
        logit_out_ref, router_grad_ref, buffer_ref = refs[:3]
        refs = refs[3:]
    turned = refs.pop(0)
    if fast:
        qkv_grad_ref, proj_grad_ref = refs[:2]
        refs = refs[2:]
    if not last:
        total_ref = refs.pop(0)
    step = pl.program_id(0)
    final = pl.num_programs(0) - 1
    count, _, width = carried_ref.shape
    if fast:
        row = Row()
        if last:
            table_ref, small_ref, unit_ref, lines_ref = refs[:4]
            landing, refs = refs[4:8], refs[8:]
            above = (half_above, down_above.at[1], attn_above)
            closing = Closing(row, dp, units_ref, unit_ref, lines_ref, above, landing, refs)
            sums = closing.sums
        else:
            sums = RowSum(row, blocks(units_ref), refs[0], refs[1], refs[2], blocks(mine_ref), refs[3:7])
            across_x = DeepSum(dp, [mine_ref.at[0]], [refs[7]], [halves_ref], [None], [None], refs[8:10] * 4)

        def take(k):
            if closing:
                closing.take(k)
            else:
                sums.end(k)
                if k == 0:
                    across_x.over_x(k).start()

        @pl.when(step == 0)
        def _():
            if closing:
                closing.enter()
            else:
                barrier = row.greet()
                pl.semaphore_wait(barrier, 2 + across_x.greet(barrier, False))
                for k in range(2):
                    sums.start(k)

    @pl.when(step == 0)
    def _():
        qkv_grad_ref[...] = jnp.zeros(qkv_grad_ref.shape, f32)
        proj_grad_ref[...] = jnp.zeros(proj_grad_ref.shape, f32)
        table_ref[...] = jnp.zeros(table_ref.shape, f32)
        small_ref[...] = jnp.zeros(small_ref.shape, f32)
        if not last:
            total_ref[...] = jnp.zeros(total_ref.shape, f32)
            router_grad_ref[...] = jnp.zeros(router_grad_ref.shape, f32)

    pos_col = join(col_ref)[:, 0:1]
    g = join(grad_ref)
    high, low = split_two(join(logit_ref))
    gain_ref, router = gain_ref.at[0], router_ref[0]
    normed_grad = collect(pos_col, returned_ref) + nn(high, router) + nn(low, router)
    xhat, rstd = norm_parts(join(middle_ref))
    small_ref[1:2, :] += jnp.sum(normed_grad * xhat, 0, keepdims=True)
    small_ref[3:4, :] += jnp.sum(normed_grad, 0, keepdims=True)
    middle_grad = g + norm_back(normed_grad, gain_ref[1:2, :], xhat, rstd)

    if fast:

        @pl.when(step == 0)
        def _():
            for k in range(2):
                sums.middle(k)

    def branch_part(i):
        low_part = (valid_ref[step * count + i].astype(f32) * middle_grad[image_rows(i)]).astype(bf16)
        return nn(move_ref[...], low_part)

    branch_grad = per_image(branch_part, count).astype(bf16)
    for i in range(count):
        proj_grad_ref[...] += nn(att_ref[i], branch_grad[image_rows(i)])
    att_grad = nt(proj_ref[...], branch_grad).astype(bf16)
    if fast:

        @pl.when(step == 0)
        def _():
            if closing:
                closing.early()

        pl.when(step == final)(functools.partial(take, 0))

    heads_rows = head_masks()
    halves = lane_masks()
    low_lane = iota((WPAD, LANES), 1) < WPAD
    for pair in range(PAIRS * count):
        image, side = pair // PAIRS, pair % PAIRS
        across = slice(pair * LANES, (pair + 1) * LANES)
        within = slice(side * LANES, (side + 1) * LANES)
        for group in range(HEADS // GROUP):
            features = slice(group * LANES, (group + 1) * LANES)
            grads = att_grad[features, across]
            spread = jnp.concatenate([grads * heads_rows[h] for h in range(GROUP)], 1)
            raw = nn(v_ref[image, within, features], spread)
            for h in range(GROUP):
                head = group * GROUP + h
                at = slice(head * HEAD_DIM, (head + 1) * HEAD_DIM)
                below = slice(width + head * HEAD_DIM, width + (head + 1) * HEAD_DIM)
                lowest = slice(2 * width + head * HEAD_DIM, 2 * width + (head + 1) * HEAD_DIM)
                part = raw[:, h * LANES : (h + 1) * LANES]
                probs_grad = jnp.where(low_lane, part[:WPAD], part[WPAD:])
                probs_low = probs_ref[image, side * HEADS + head]
                probs = probs_low.astype(f32)
                weighted = probs * probs_grad
                scores_grad = weighted - probs * jnp.sum(weighted, 0, keepdims=True)
                table_ref[head] += scores_grad
                scores_low = scores_grad.astype(bf16)
                both = jnp.concatenate([scores_low * halves[0], scores_low * halves[1]], 0)
                probs_both = jnp.concatenate([probs_low * halves[0], probs_low * halves[1]], 0)
                turned[at, across] = (nn(qk_ref[image, below, within], both) * head_scale).astype(bf16)
                turned[below, across] = (nt(qk_ref[image, at, within], both) * head_scale).astype(bf16)
                turned[lowest, across] = nt(att_grad[at, across], probs_both).astype(bf16)
    qkv_grad_ref[...] += nn(turned[...], join(window_ref))
    if fast:

        @pl.when(step == final)
        def _():
            columns, rows = 3 * width // mp, width // mp
            proj_turned = turn_blocks(proj_grad_ref[...].astype(bf16)).astype(bf16)
            for place in range(mp):
                q = quarter_at(place, mp)
                unit_ref[place, :columns] = qkv_grad_ref[q * columns : (q + 1) * columns].astype(bf16)
                unit_ref[place, columns:] = proj_turned[q * rows : (q + 1) * rows]
            if closing:
                closing.open()
            take(1)
            if closing:
                heads = 2 * HEADS
                lines_ref[...] = jnp.zeros(lines_ref.shape, f32)
                lines_ref[:heads, :TABLE] = table_grad([table_ref, table_above], entry_ref[...])

    mixed_grad = per_image(lambda i: nt(back_ref[...], turned[:, image_rows(i)]), count).astype(bf16)
    first_grad = nn(mixed_grad, qkv_ref[...])
    if closing:

        @pl.when(step == final)
        def _():
            closing.cross()

    xhat, rstd = norm_parts(join(carried_ref))
    small_ref[0:1, :] += jnp.sum(first_grad * xhat, 0, keepdims=True)
    small_ref[2:3, :] += jnp.sum(first_grad, 0, keepdims=True)
    if closing:

        @pl.when(step == final)
        def _():
            heads = 2 * HEADS
            lines_ref[heads : heads + EXPERTS] = router_here[:EXPERTS]
            lines_ref[heads + EXPERTS : heads + 2 * EXPERTS] = router_above[:EXPERTS]
            lines_ref[heads + 2 * EXPERTS : heads + 2 * EXPERTS + 8] = small_ref[...]
            lines_ref[heads + 2 * EXPERTS + 8 : heads + 2 * EXPERTS + 16] = small_above[...]
            closing.send_lines()

    out = middle_grad + norm_back(first_grad, gain_ref[0:1, :], xhat, rstd)
    if last:
        top = out.astype(bf16)
        rest = out - top.astype(f32)
        mid, low = split_two(rest)
        leave = leave_ref[...]
        for i in range(count):
            at = image_rows(i)
            out_ref[i] = nn(leave, top[at]) + nn(leave, mid[at]) + nn(leave, low[at])
    else:
        store(out_ref, out)
        send_part(
            out, join(expert_out_ref), join(second_ref), router_next_ref[0], pos_col, lay_positions(row_ref), logit_out_ref,
            router_grad_ref, total_ref,
        )

    @pl.when(step == final)
    def _():
        if not last:
            buffer_ref[...] = total_ref[...].astype(bf16)
        if closing:
            closing.finish()
            for out, landed in zip(results, landing):
                out[...] = landed[...]
        elif fast:
            across_x.halve(0)
            across_x.over_x(0).wait_send()
            for k in range(2):
                sums.finish(k)


def quarter_at(place, mp):
    return place % (mp // 2) * 2 + place // (mp // 2)


def add_up(*parts):
    total = parts[0].astype(f32)
    for part in parts[1:]:
        total = total + part.astype(f32)
    return total


class Copies:
    def __init__(self, source, target, send_sem, recv_sem, device):
        self.source, self.target = source, target
        self.how = dict(send_sem=send_sem, recv_sem=recv_sem, device_id=device, device_id_type=MESH)
        whole = pltpu.make_async_remote_copy(src_ref=source, dst_ref=target, **self.how)
        self.wait_send, self.wait_recv = whole.wait_send, whole.wait_recv

    def start(self):
        shape = self.source.shape
        rows = shape[-2]
        parts = max([n for n in (2, 3, 4) if rows % (16 * n) == 0], default=1)
        size = rows // parts
        leads = [(lead,) for lead in range(shape[0])] if len(shape) == 3 else [()]
        for lead in leads:
            for part in range(parts):
                at = (*lead, pl.ds(part * size, size))
                pltpu.make_async_remote_copy(
                    src_ref=self.source.at[at], dst_ref=self.target.at[at], **self.how
                ).start()

    def wait(self):
        self.wait_send()
        self.wait_recv()


def to_row(source, target, sems, k, row):
    return Copies(source, target, sems[0].at[k], sems[1].at[k], {"mp": row})


class Row:
    def __init__(self):
        row = lax.axis_index("mp")
        self.row, self.core, self.y = row, lax.rem(row, 2), lax.div(row, 2)
        self.sibling, self.across = row + 1 - 2 * self.core, row + 2 - 4 * self.y
        self.place = self.core * 2 + self.y
        self.place_across = self.core * 2 + 1 - self.y

    def greet(self):
        barrier = pltpu.get_barrier_semaphore()
        for row in (self.sibling, self.across):
            pl.semaphore_signal(barrier, inc=1, device_id={"mp": row}, device_id_type=MESH)
        return barrier


class RowSum:
    semaphores = 4

    def __init__(self, row, units, core_in, y_out, y_in, mine, sems):
        self.row, self.units, self.mine = row, units, mine
        self.core_in, self.y_out, self.y_in = core_in, y_out, y_in
        self.sems = (sems[:2], sems[2:])

    def pair(self, k):
        theirs = self.units[k].at[pl.ds(2 * (1 - self.row.core), 2)]
        return to_row(theirs, self.core_in.at[k], self.sems[0], k, self.row.sibling)

    def cross(self, k):
        return to_row(self.y_out.at[k], self.y_in.at[k], self.sems[1], k, self.row.across)

    def start(self, k):
        self.pair(k).start()

    def middle(self, k):
        self.pair(k).wait_recv()
        other = 1 - self.row.y
        mixed = add_up(self.units[k][self.row.core * 2 + other], self.core_in[k, other])
        self.y_out[k] = mixed.astype(bf16)
        self.cross(k).start()

    def end(self, k):
        self.cross(k).wait_recv()
        self.mine[k][...] = add_up(
            self.units[k][self.row.place], self.core_in[k, self.row.y], self.y_in[k]
        ).astype(bf16)

    def finish(self, k):
        self.pair(k).wait_send()
        self.cross(k).wait_send()

    @classmethod
    def scratch(cls, count, width):
        return [
            pltpu.VMEM((count, 2, width, width), bf16),
            pltpu.VMEM((count, width, width), bf16),
            pltpu.VMEM((count, width, width), bf16),
        ] + [pltpu.SemaphoreType.DMA((count,))] * cls.semaphores


class RowGather:
    semaphores = 6

    def __init__(self, row, sources, fulls, slot, slot_across, sems):
        self.row, self.sources, self.fulls = row, sources, fulls
        self.slot, self.slot_across = slot, slot_across
        self.sems = (sems[:2], sems[2:4], sems[4:])

    def over(self, k):
        return to_row(self.sources[k], self.fulls[k].at[self.slot], self.sems[0], k, self.row.across)

    def near(self, k):
        return to_row(self.sources[k], self.fulls[k].at[self.slot], self.sems[1], k, self.row.sibling)

    def onward(self, k):
        block = self.fulls[k].at[self.slot_across]
        return to_row(block, block, self.sems[2], k, self.row.sibling)

    def start(self, k):
        self.over(k).start()
        self.near(k).start()

    def forward(self, k):
        self.over(k).wait_recv()
        self.onward(k).start()

    def arrive(self, k):
        self.near(k).wait_recv()
        self.onward(k).wait_recv()

    def sent(self, k):
        self.over(k).wait_send()
        self.near(k).wait_send()
        self.onward(k).wait_send()

    @classmethod
    def scratch(cls, count):
        return [pltpu.SemaphoreType.DMA((count,))] * cls.semaphores


class WeightGather(RowGather):
    def __init__(self, shards, fulls, sems):
        row = Row()
        super().__init__(row, shards, fulls, row.row, row.across, sems[:6])
        self.own_sem = sems[6]

    def own(self, k):
        return pltpu.make_async_copy(self.sources[k], self.fulls[k].at[self.slot], self.own_sem.at[k])

    def start(self, k):
        super().start(k)
        self.own(k).start()

    def arrive(self, k):
        super().arrive(k)
        self.own(k).wait()

    @classmethod
    def scratch(cls, count):
        return super().scratch(count) + [pltpu.SemaphoreType.DMA((count,))]


class DeepSum:
    def __init__(self, dp, total, arrived, halves, slots, result, sems):
        self.total, self.arrived, self.halves, self.slots, self.result = total, arrived, halves, slots, result
        self.x_sems, self.z_sems, self.z_back, self.x_back = (sems[2 * k : 2 * k + 2] for k in range(4))
        me = lax.axis_index("dp")
        self.x, self.z, self.deep = lax.rem(me, 2), lax.div(me, 2), dp // 2
        self.partner = me + 1 - 2 * self.x

    def greet(self, barrier, whole=True):
        pl.semaphore_signal(barrier, inc=1, device_id={"dp": self.partner}, device_id_type=MESH)
        if not whole:
            return 1
        for off in range(1, self.deep):
            peer = lax.rem(self.z + off, self.deep) * 2 + self.x
            pl.semaphore_signal(barrier, inc=1, device_id={"dp": peer}, device_id_type=MESH)
        return self.deep

    def cut(self, k):
        height = self.halves[k].shape[0]
        return height, height // self.deep

    def begin(self, k):
        self.over_x(k).start()

    def over_x(self, k):
        height, _ = self.cut(k)
        away = self.total[k].at[pl.ds(pl.multiple_of((1 - self.x) * height, height), height)]
        return Copies(away, self.arrived[k], self.x_sems[0].at[k], self.x_sems[1].at[k], {"dp": self.partner})

    def over_z(self, k, off):
        _, piece = self.cut(k)
        to = lax.rem(self.z + off, self.deep)
        part = self.halves[k].at[pl.ds(pl.multiple_of(to * piece, piece), piece)]
        sems = [sem.at[k, off] for sem in self.z_sems]
        return to_peer(part, self.slots[k].at[off], *sems, to * 2 + self.x)

    def own_piece(self, k):
        height, piece = self.cut(k)
        return self.result[k].at[pl.ds(pl.multiple_of(self.x * height + self.z * piece, piece), piece)]

    def own_half(self, k):
        height, _ = self.cut(k)
        return self.result[k].at[pl.ds(pl.multiple_of(self.x * height, height), height)]

    def back_z(self, k, off):
        to = lax.rem(self.z + off, self.deep)
        sems = [sem.at[k, off] for sem in self.z_back]
        return to_peer(self.own_piece(k), self.own_piece(k), *sems, to * 2 + self.x)

    def back_x(self, k):
        half = self.own_half(k)
        return Copies(half, half, self.x_back[0].at[k], self.x_back[1].at[k], {"dp": self.partner})

    def halve(self, k):
        self.over_x(k).wait_recv()
        height, _ = self.cut(k)
        keep = self.total[k][pl.ds(pl.multiple_of(self.x * height, height), height)]
        self.halves[k][...] = add_up(keep, self.arrived[k][...]).astype(self.halves[k].dtype)

    def deepen(self, k):
        for off in range(1, self.deep):
            self.over_z(k, off).start()

    def quarter(self, k):
        for off in range(1, self.deep):
            self.over_z(k, off).wait_recv()
        _, piece = self.cut(k)
        keep = self.halves[k][pl.ds(pl.multiple_of(self.z * piece, piece), piece)]
        total = add_up(keep, *[self.slots[k][off] for off in range(1, self.deep)])
        self.own_piece(k)[...] = total.astype(self.result[k].dtype)
        for off in range(1, self.deep):
            self.back_z(k, off).start()

    def widen(self, k):
        for off in range(1, self.deep):
            self.back_z(k, off).wait_recv()
        self.back_x(k).start()

    def finish(self, k, halved=True):
        if halved:
            self.over_x(k).wait_send()
        for off in range(1, self.deep):
            self.over_z(k, off).wait_send()
            self.back_z(k, off).wait_send()
        self.back_x(k).wait()

    @staticmethod
    def semaphores(dp, count):
        one, many = pltpu.SemaphoreType.DMA((count,)), pltpu.SemaphoreType.DMA((count, dp // 2))
        return [one, one, many, many, many, many, one, one]


class DeepFirst(DeepSum):
    def cut(self, k):
        height = self.halves[k].shape[0]
        return height, height // 2

    def over_z(self, k, off):
        height, _ = self.cut(k)
        to = lax.rem(self.z + off, self.deep)
        part = self.total[k].at[pl.ds(pl.multiple_of(to * height, height), height)]
        sems = [sem.at[k, off] for sem in self.z_sems]
        return to_peer(part, self.slots[k].at[off], *sems, to * 2 + self.x)

    def over_x(self, k):
        _, piece = self.cut(k)
        away = self.halves[k].at[pl.ds(pl.multiple_of((1 - self.x) * piece, piece), piece)]
        return to_peer(away, self.arrived[k], self.x_sems[0].at[k], self.x_sems[1].at[k], self.partner)

    def own_piece(self, k):
        height, piece = self.cut(k)
        return self.result[k].at[pl.ds(pl.multiple_of(self.z * height + self.x * piece, piece), piece)]

    def own_half(self, k):
        height, _ = self.cut(k)
        return self.result[k].at[pl.ds(pl.multiple_of(self.z * height, height), height)]

    def back_x(self, k):
        piece = self.own_piece(k)
        return to_peer(piece, piece, self.x_back[0].at[k], self.x_back[1].at[k], self.partner)

    def back_z(self, k, off):
        to = lax.rem(self.z + off, self.deep)
        sems = [sem.at[k, off] for sem in self.z_back]
        return to_peer(self.own_half(k), self.own_half(k), *sems, to * 2 + self.x)

    def begin(self, k):
        for off in range(1, self.deep):
            self.over_z(k, off).start()

    def halve(self, k):
        for off in range(1, self.deep):
            self.over_z(k, off).wait_recv()
        height, _ = self.cut(k)
        keep = self.total[k][pl.ds(pl.multiple_of(self.z * height, height), height)]
        total = add_up(keep, *[self.slots[k][off] for off in range(1, self.deep)])
        self.halves[k][...] = total.astype(self.halves[k].dtype)

    def deepen(self, k):
        self.over_x(k).start()

    def quarter(self, k):
        self.over_x(k).wait_recv()
        _, piece = self.cut(k)
        keep = self.halves[k][pl.ds(pl.multiple_of(self.x * piece, piece), piece)]
        self.own_piece(k)[...] = add_up(keep, self.arrived[k][...]).astype(self.result[k].dtype)
        self.back_x(k).start()

    def widen(self, k):
        self.back_x(k).wait_recv()
        for off in range(1, self.deep):
            self.back_z(k, off).start()

    def finish(self, k, halved=True):
        self.over_x(k).wait_send()
        self.back_x(k).wait_send()
        for off in range(1, self.deep):
            self.over_z(k, off).wait_send()
            self.back_z(k, off).wait_send()
            self.back_z(k, off).wait_recv()


def blocks(ref):
    return [ref.at[k] for k in range(ref.shape[0])]


class WideSum:
    def __init__(self, dp, row, total, slots, kept, crossed, result, sems):
        self.dp, self.row, self.total, self.slots = dp, row, total, slots
        self.kept, self.crossed, self.result, self.sems = kept, crossed, result, sems
        self.me = lax.axis_index("dp")

    def rows(self, k, at):
        size = self.result[k].shape[0] // self.dp
        return pl.ds(pl.multiple_of(at * size, size), size)

    def out(self, k, p):
        peer = partner_of(self.me, p, self.dp)
        sems = self.sems[0].at[k, p], self.sems[1].at[k, p]
        source = self.total[k]
        lead = (pl.ds(0, source.shape[0]),) if len(source.shape) == 3 else ()
        return to_peer(source.at[(*lead, self.rows(k, peer))], self.slots[k].at[p], *sems, peer)

    def cross(self, k):
        return to_row(self.kept[k], self.crossed[k], self.sems[4:6], k, self.row.across)

    def back(self, k, p):
        mine = self.result[k].at[self.rows(k, self.me)]
        sems = self.sems[2].at[k, p], self.sems[3].at[k, p]
        return to_peer(mine, mine, *sems, partner_of(self.me, p, self.dp))

    def start(self, k):
        for p in range(self.dp - 1, 0, -1):
            self.out(k, p).start()

    def sum_up(self, k, side):
        if side is None:
            parts = [self.total[k][self.rows(k, self.me)]] + [self.slots[k][p] for p in range(1, self.dp)]
        else:
            parts = [self.total[k][side, self.rows(k, self.me)]] + [self.slots[k][p, side] for p in range(1, self.dp)]
        return add_up(*parts)

    def middle(self, k):
        for p in range(1, self.dp):
            self.out(k, p).wait_recv()
        side = 1 - self.row.y if len(self.total[k].shape) == 3 else None
        self.kept[k][...] = self.sum_up(k, side).astype(self.kept[k].dtype)
        self.cross(k).start()

    def end(self, k):
        self.cross(k).wait_recv()
        if len(self.total[k].shape) == 3:
            own = self.sum_up(k, self.row.y)
        else:
            own = self.kept[k][...]
        self.result[k].at[self.rows(k, self.me)][...] = add_up(own, self.crossed[k][...]).astype(self.result[k].dtype)
        for p in range(self.dp - 1, 0, -1):
            self.back(k, p).start()

    def finish(self, k):
        self.cross(k).wait_send()
        for p in range(1, self.dp):
            self.out(k, p).wait_send()
            self.back(k, p).wait()

    @staticmethod
    def semaphores(dp, count):
        return [pltpu.SemaphoreType.DMA((count, dp))] * 4 + [pltpu.SemaphoreType.DMA((count,))] * 2


class Closing:
    lines = 64

    def __init__(self, row, dp, units_ref, attn_ref, lines_ref, given, results, refs):
        self.row, self.lines_ref, self.dp, self.attn = row, lines_ref, dp, attn_ref
        self.full, shard, small, above = results
        core_in, y_out, y_in = refs[:3]
        row_sems, refs = refs[3:7], refs[7:]
        mine, self.a_core, self.a_one, self.s_core, self.s_one = refs[:5]
        a_slots, s_slots, a_kept, s_kept, a_crossed, s_crossed = refs[5:11]
        x_in, x_half, x_slots, z_in, z_half, z_slots = refs[11:17]
        gather_sems, pair_sems, refs = refs[17:23], refs[23:25], refs[25:]
        self.mine = mine
        self.sums = RowSum(row, blocks(units_ref), core_in, y_out, y_in, blocks(mine), row_sems)
        self.gather = RowGather(row, blocks(mine), blocks(self.full), row.place, row.place_across, gather_sems)
        self.a_pair = to_row(attn_ref.at[pl.ds(2 * (1 - row.core), 2)], self.a_core, pair_sems, 0, row.sibling)
        self.s_pair = to_row(lines_ref, self.s_core, pair_sems, 1, row.sibling)
        over_x = DeepSum(
            dp, [mine.at[0], None, given[2]], [x_in.at[0], None, x_in.at[1]], [x_half.at[0], given[0], x_half.at[1]],
            blocks(x_slots), [shard.at[0], above.at[0], above.at[2]], refs[:8],
        )
        over_z = DeepFirst(
            dp, [mine.at[1], given[1]], blocks(z_in), blocks(z_half), blocks(z_slots), [shard.at[1], above.at[1]], refs[8:16]
        )
        self.here = [(over_x, 0), (over_z, 0)]
        self.above = [(over_x, 1), (over_z, 1), (over_x, 2)]
        self.wide = WideSum(
            dp, row, [self.a_one, self.s_one], [a_slots, s_slots], [a_kept, s_kept], [a_crossed, s_crossed],
            [shard.at[2], small], refs[16:22],
        )

    @staticmethod
    def each(units, *steps):
        for step in steps:
            for owner, k in units:
                getattr(owner, step)(k)

    def enter(self):
        greet(self.dp, lax.axis_index("dp"), (self.row.sibling, self.row.across))
        for k in range(2):
            self.sums.start(k)
        self.each(self.above[:1], "deepen")
        self.each(self.above[1:], "begin")

    def early(self):
        for unit in self.above[1:]:
            self.each([unit], "halve", "deepen")
        self.each(self.above[:1], "quarter")

    def take(self, k):
        self.sums.end(k)
        self.each(self.here[k : k + 1], "begin")
        self.gather.start(k)
        self.full[k, self.row.place] = self.mine[k]
        if k == 0:
            self.each(self.above[:1], "widen")
            self.each(self.above[1:], "quarter")
        else:
            self.each(self.above[1:], "widen")

    def open(self):
        self.a_pair.start()

    def cross(self):
        self.a_pair.wait_recv()
        for side in range(2):
            own = self.attn[self.row.core * 2 + side]
            self.a_one[side] = add_up(own, self.a_core[side]).astype(bf16)
        self.wide.start(0)
        for unit in self.here:
            self.each([unit], "halve", "deepen")
        self.gather.forward(0)

    def send_lines(self):
        self.s_pair.start()
        self.each(self.here, "quarter")
        self.s_pair.wait_recv()
        self.s_one[...] = self.lines_ref[...] + self.s_core[...]
        self.wide.start(1)

    def finish(self):
        self.wide.middle(0)
        self.wide.middle(1)
        self.each(self.here, "widen")
        self.wide.end(0)
        self.wide.end(1)
        self.gather.forward(1)
        self.a_pair.wait_send()
        self.s_pair.wait_send()
        for k in range(2):
            self.sums.finish(k)
            self.wide.finish(k)
        for owner, k in self.here + self.above[1:]:
            owner.finish(k)
        self.above[0][0].finish(self.above[0][1], False)
        for k in range(2):
            self.gather.arrive(k)
            self.gather.sent(k)

    @classmethod
    def scratch(cls, dp, width):
        deep, lines = dp // 2, cls.lines
        flat = pltpu.VMEM((lines, width), f32)
        half, deep_part, piece = width // 2, width // deep, width // dp

        def low(*shape):
            return pltpu.VMEM((*shape, width), bf16)

        return (
            RowSum.scratch(2, width)
            + [
                low(2, width),
                low(2, width),
                low(2, width),
                flat,
                flat,
                low(dp, 2, piece),
                pltpu.VMEM((dp, lines // dp, width), f32),
                low(piece),
                pltpu.VMEM((lines // dp, width), f32),
                low(piece),
                pltpu.VMEM((lines // dp, width), f32),
                low(2, half),
                low(2, half),
                low(3, deep, piece),
                low(2, piece),
                low(2, deep_part),
                low(2, deep, deep_part),
            ]
            + RowGather.scratch(2)
            + [pltpu.SemaphoreType.DMA((2,))] * 2
            + DeepSum.semaphores(dp, 3)
            + DeepSum.semaphores(dp, 2)
            + WideSum.semaphores(dp, 2)
        )


def format_kernel(columns, *refs):
    count = (len(refs) - 6) // 2
    qkv_out, proj_out, core_up_out, core_down_out, up_out, down_out = refs[2 * count :]

    def form(full, shard):
        mp, width = full.shape[1], full.shape[2]
        rows = width // mp
        qkv_out[0] = shard[2, :columns].astype(f32)
        proj_out[0] = shard[2, columns:].astype(f32)
        core_up_out[0] = shard[0].astype(f32)
        for place in range(mp):
            q = quarter_at(place, mp)
            up_out[0, 0, :, q * width : (q + 1) * width] = full[0, place].astype(f32)
        for chunk in range(mp):
            at = slice(chunk * width, (chunk + 1) * width)
            core_down_out[0, :, at] = shard[1, chunk * rows : (chunk + 1) * rows].astype(f32)
            block = [None] * mp
            for place in range(mp):
                block[quarter_at(place, mp)] = full[1, place, chunk * rows : (chunk + 1) * rows]
            down_out[0, 0, at, :] = turn_blocks(jnp.concatenate(block, 0))

    for layer in range(count):
        pl.when(pl.program_id(0) == layer)(functools.partial(form, refs[layer], refs[count + layer]))


def format_call(fulls, shards, columns):
    layers = len(fulls)
    _, mp, width, _ = fulls[0].shape
    hidden = mp * width
    shapes = [
        (layers, columns, width),
        (layers, width - columns, width),
        (layers, width, width),
        (layers, width // mp, hidden),
        (layers, 1, width, hidden),
        (layers, 1, hidden, width),
    ]
    return pl.pallas_call(
        functools.partial(format_kernel, columns),
        grid=(layers,),
        out_shape=[jax.ShapeDtypeStruct(shape, f32) for shape in shapes],
        in_specs=[whole_spec(a.shape) for a in (*fulls, *shards)],
        out_specs=[image_spec(shape, 1) for shape in shapes],
        compiler_params=pltpu.CompilerParams(vmem_limit_bytes=56 * MIB),
        name="format",
    )(*fulls, *shards)


def greet(dp, me, rows=()):
    barrier = pltpu.get_barrier_semaphore()
    for row in rows:
        pl.semaphore_signal(barrier, inc=1, device_id={"mp": row}, device_id_type=MESH)

    def signal(off, carry):
        pl.semaphore_signal(barrier, inc=1, device_id={"dp": lax.rem(me + off, dp)}, device_id_type=MESH)
        return carry

    lax.fori_loop(1, dp, signal, 0)
    pl.semaphore_wait(barrier, dp - 1 + len(rows))


def partner_of(me, p, dp):
    out, bit = 0, 1
    while bit < dp:
        one, two = lax.rem(lax.div(me, bit), 2), lax.rem(lax.div(p, bit), 2)
        out = out + bit * (one + two - 2 * one * two)
        bit *= 2
    return out


def to_peer(source, target, send_sem, recv_sem, peer):
    return pltpu.make_async_remote_copy(
        src_ref=source,
        dst_ref=target,
        send_sem=send_sem,
        recv_sem=recv_sem,
        device_id={"dp": peer},
        device_id_type=MESH,
    )


def gelu_parts(h):
    root = np.float32(np.sqrt(2.0 / np.pi))
    square = h * h
    t = jnp.tanh(root * h * (1.0 + 0.044715 * square))
    half = 0.5 * (1.0 + t)
    slope = half + 0.5 * h * (1.0 - t * t) * root * (1.0 + 3 * 0.044715 * square)
    return h * half, slope


def expert_forward_kernel(dp, mp, layer, gather, *refs):
    refs = list(refs)
    buffer_ref, up_any, down_any, rup_any, rdown_any = refs[:5]
    refs = refs[5:]
    if gather:
        shards = [ref.at[layer + 1] for ref in refs[:4]]
        refs = refs[4:]
    recv_ref, returned_ref, up_eff, down_eff = refs[:4]
    refs = refs[4:]
    if gather:
        fulls = refs[:4]
        refs = refs[4:]
    part, core, up_ref, down_ref, rup_ref, rdown_ref, local = refs[:7]
    refs = refs[7:]
    moving = WeightGather(shards, fulls, refs[:7]) if gather else None
    send_one, recv_one, send_two, recv_two = refs[-4:]
    split = dp // EXPERTS
    me = lax.axis_index("dp")
    loads = [
        pltpu.make_async_copy(source, target, local.at[k])
        for k, (source, target) in enumerate(
            [
                (up_any, up_ref),
                (rup_any.at[layer, 0], rup_ref),
                (down_any, down_ref),
                (rdown_any.at[layer, 0], rdown_ref),
            ]
        )
    ]
    for load in loads:
        load.start()
    greet(dp, me, (moving.row.sibling, moving.row.across) if gather else ())

    def first(off):
        peer = partner_of(me, off, dp)
        return to_peer(
            buffer_ref.at[lax.div(peer, split)], recv_ref.at[me], send_one.at[off], recv_one.at[off], peer
        )

    def second(off):
        source = partner_of(me, off, dp)
        return to_peer(part.at[source], returned_ref.at[me], send_two.at[off], recv_two.at[off], source)

    def start_first(off, carry):
        first(dp - off).start()
        return carry

    lax.fori_loop(1, dp, start_first, 0)
    if gather:
        for k in range(4):
            moving.start(k)
    recv_ref[me] = buffer_ref[lax.div(me, split)]
    hidden = up_eff.shape[1]
    columns = up_ref.shape[-1]
    loads[0].wait()
    loads[1].wait()
    if split == 1 and columns % LANES == 0:
        for m in range(mp):
            at = slice(m * columns, (m + 1) * columns)
            up_eff[:, at] = (up_ref[m].astype(f32) + rup_ref[:, at].astype(f32)).astype(bf16)
    else:
        core[...] = rup_ref[...].astype(f32)
        begin = lax.rem(me, split) * hidden
        for m in range(mp):
            put = onehot(iota((columns, hidden), 0) + m * columns == iota((columns, hidden), 1) + begin)
            core[...] += nn(up_ref[m], put)
        up_eff[...] = core[...].astype(bf16)
    begin = pl.multiple_of(lax.rem(me, split) * hidden, LANES)
    loads[2].wait()
    loads[3].wait()
    core_part = down_ref[:, :, pl.ds(begin, hidden)].reshape(down_eff.shape[1], hidden)
    down_eff[...] = (turn_blocks(core_part) + rdown_ref[...].astype(f32)).astype(bf16)

    def work(source):
        hidden_pre = nn(recv_ref[source], up_eff[...])
        hidden_low = gelu_parts(hidden_pre)[0].astype(bf16)
        return nn(hidden_low, down_eff[...]).astype(bf16)

    returned_ref[me] = work(me)

    def step(off, carry):
        source = partner_of(me, off, dp)
        first(off).wait_recv()
        part[source] = work(source)
        second(off).start()
        return carry

    lax.fori_loop(1, dp, step, 0)
    if gather:
        for k in range(4):
            moving.forward(k)

    def finish(off, carry):
        first(off).wait_send()
        second(off).wait()
        return carry

    lax.fori_loop(1, dp, finish, 0)
    if gather:
        for k in range(4):
            moving.arrive(k)
            moving.sent(k)


def expert_backward_kernel(dp, mp, fast, reduce, *refs):
    refs = list(refs)
    buffer_ref, recv_ref, up_ref, down_ref = refs[:4]
    refs = refs[4:]
    if reduce:
        given_ref, attn_ref = refs[:2]
        refs = refs[2:]
    returned_ref = refs.pop(0)
    if fast:
        units_ref = refs.pop(0)
    else:
        up_term, down_term = refs[:2]
        refs = refs[2:]
    if reduce:
        full_ref, mine_ref = refs[:2]
        refs = refs[2:]
    grads, hidden_low, slope, pre, part = refs[:5]
    refs = refs[5:]
    if fast:
        up_term, down_term = refs[:2]
        refs = refs[2:]
    row = Row() if reduce else None
    if reduce:
        core_in, y_out, y_in = refs[:3]
        sums = RowSum(row, [attn_ref], core_in, y_out, y_in, [mine_ref], refs[3:7])
        gather = RowGather(
            row, [given_ref.at[k] for k in range(2)], [full_ref.at[k] for k in range(2)], row.place, row.place_across,
            refs[7:13],
        )
        refs = refs[13:]
    send_one, recv_one, send_two, recv_two = refs
    split = dp // EXPERTS
    me = lax.axis_index("dp")
    greet(dp, me, (row.sibling, row.across) if reduce else ())

    def first(off):
        peer = partner_of(me, off, dp)
        return to_peer(buffer_ref.at[lax.div(peer, split)], grads.at[me], send_one.at[off], recv_one.at[off], peer)

    def second(off):
        source = partner_of(me, off, dp)
        return to_peer(part.at[source], returned_ref.at[me], send_two.at[off], recv_two.at[off], source)

    def start_first(off, carry):
        first(dp - off).start()
        return carry

    lax.fori_loop(1, dp, start_first, 0)
    if reduce:
        sums.start(0)
        for k in range(2):
            gather.start(k)
    grads[me] = buffer_ref[lax.div(me, split)]

    def again(source, carry):
        value, rate = gelu_parts(nn(recv_ref[source], up_ref[...]))
        hidden_low[source] = value.astype(bf16)
        slope[source] = rate
        return carry

    lax.fori_loop(0, dp, again, 0)
    if reduce:
        sums.middle(0)
        for k in range(2):
            full_ref[k, row.place] = given_ref[k]

    def work(source):
        hidden_grad = nt(grads[source], down_ref[...])
        pre_grad = (slope[source] * hidden_grad).astype(bf16)
        pre[source] = pre_grad
        return nt(pre_grad, up_ref[...]).astype(bf16)

    returned_ref[me] = work(me)

    def step(off, carry):
        source = partner_of(me, off, dp)
        first(off).wait_recv()
        part[source] = work(source)
        second(off).start()
        return carry

    lax.fori_loop(1, dp, step, 0)
    if reduce:
        for k in range(2):
            gather.forward(k)
        sums.end(0)
    up_term[...] = jnp.zeros(up_term.shape, f32)
    down_term[...] = jnp.zeros(down_term.shape, f32)

    def terms(block, carry):
        up_term[...] += tn(recv_ref[block], pre[block])
        down_term[...] += tn(grads[block], hidden_low[block])
        return carry

    lax.fori_loop(0, dp, terms, 0)
    if fast:
        width = up_term.shape[0]
        height = width // mp
        for place in range(mp):
            q = quarter_at(place, mp)
            units_ref[0, place] = up_term[:, q * width : (q + 1) * width].astype(bf16)
            for chunk in range(mp):
                block = down_term[q * height : (q + 1) * height, chunk * width : (chunk + 1) * width]
                units_ref[1, place, chunk * height : (chunk + 1) * height] = block.astype(bf16)

    def finish(off, carry):
        first(off).wait_send()
        second(off).wait()
        return carry

    lax.fori_loop(1, dp, finish, 0)
    if reduce:
        sums.finish(0)
        for k in range(2):
            gather.arrive(k)
            gather.sent(k)


def expert_call(kernel, arrays, outs, scratch, dp, collective_id, name, flops, anys=(), any_outs=()):
    sems = [pltpu.SemaphoreType.DMA((dp,))] * 4
    vmem, anywhere = pl.BlockSpec(memory_space=pltpu.VMEM), pl.BlockSpec(memory_space=pl.ANY)
    return pl.pallas_call(
        kernel,
        out_shape=[jax.ShapeDtypeStruct(shape, dtype) for shape, dtype in (*outs, *any_outs)],
        in_specs=[vmem] * len(arrays) + [anywhere] * len(anys),
        out_specs=[vmem] * len(outs) + [anywhere] * len(any_outs),
        scratch_shapes=scratch + sems,
        compiler_params=pltpu.CompilerParams(
            vmem_limit_bytes=56 * MIB, collective_id=collective_id, has_side_effects=True
        ),
        cost_estimate=pl.CostEstimate(flops=flops, bytes_accessed=20 * MIB, transcendentals=0),
        name=name,
    )(*arrays, *anys)


def by_windows(grid):
    images, kinds = grid.shape[:2]
    blocks = GRID // WINDOW
    grid = grid.reshape(images, kinds, blocks, WINDOW, blocks, WINDOW).transpose(0, 1, 2, 4, 3, 5)
    grid = grid.reshape(images, kinds, blocks * blocks, WINPOS)
    grid = jnp.pad(grid, ((0, 0), (0, 0), (0, 0), (0, WPAD - WINPOS)), constant_values=-1)
    return grid.reshape(images, kinds, IMGROWS)


def per_device(
    patches,
    qkv_weight,
    proj_weight,
    core_up,
    core_down,
    residual_up,
    residual_down,
    position_bias,
    router_weight,
    norm_gain,
    norm_bias,
    cotangent,
    image_valid,
    expert_index,
    slot_index,
    region_id,
):
    dp, mp = lax.axis_size("dp"), lax.axis_size("mp")
    images, _, width = patches.shape
    split = dp // EXPERTS
    hidden = residual_up.shape[-1]
    hidden_full = core_up.shape[-1] * mp
    row_index = lax.axis_index("mp")

    fast = split == 1 and dp == 8 and mp == 4 and hidden == mp * width
    qkv_rows, proj_rows, down_rows = (a.transpose(0, 2, 1) for a in (qkv_weight, proj_weight, core_down))
    shards = (qkv_rows, proj_rows, core_up, down_rows)
    gathered = [[None] * len(shards)] * LAYERS
    if not fast:
        gathered = [[lax.all_gather(a[l], "mp", axis=0, tiled=False) for a in shards] for l in range(LAYERS)]

    position = jnp.where(slot_index >= 0, expert_index * SLOTS + slot_index, -1)
    row_form = by_windows(jnp.stack([position.reshape(images, GRID, GRID), region_id], 1))
    col_form = row_form.transpose(0, 2, 1)
    enter = jnp.asarray(enter_table(), bf16)
    leave = jnp.asarray(enter_table().T, bf16)
    moves = [jnp.asarray(move_table(l % 2 == 1), bf16) for l in range(LAYERS)]
    backs = [jnp.asarray(move_table(l % 2 == 1).T, bf16) for l in range(LAYERS)]
    table_rows = position_bias.transpose(0, 2, 1).reshape(LAYERS * HEADS, OFFSETS)
    table_rows = jnp.pad(table_rows, ((0, 0), (0, TABLE - OFFSETS)))
    entry_row, entry_col = jnp.asarray(cell_entries()[None, :]), jnp.asarray(cell_entries()[:, None])
    routers = jnp.pad(router_weight.transpose(0, 2, 1), ((0, 0), (0, LANES - EXPERTS), (0, 0)))

    token = (images, IMGROWS, width)
    buffer_shape = (ROWS, width)
    block_rows = (dp, SLOTS, width)
    pieces = (split, ROWS, width)

    def by_piece(returned):
        return returned.reshape(EXPERTS, split, SLOTS, width).transpose(1, 0, 2, 3).reshape(pieces)

    records = []
    before = None
    for l in range(LAYERS):
        first = l == 0
        gather = fast and first
        if first:
            arrays = [("image", patches), ("whole", enter)]
        else:
            arrays = [("image", before[0]), ("image", before[1]), ("whole", before[2])]
        arrays += [
            ("smem", image_valid),
            ("image", col_form),
            ("image", row_form),
            ("any", qkv_rows) if gather else ("whole", gathered[l][0]),
            ("any", proj_rows) if gather else ("whole", gathered[l][1]),
            ("whole", table_rows) if first else (l, biases),
            ("whole", moves[l]),
            ("whole", backs[l]),
            (l, norm_gain),
            (l, norm_bias),
            (l, routers),
        ]
        if first:
            arrays.append(("whole", entry_row))
        if gather:
            arrays += [("any", core_up), ("any", down_rows)]
        outs = [("image", token, f32)]
        if first:
            outs.append(("whole", (LAYERS, HEADS, WPAD, LANES), f32))
        else:
            outs.append(("image", token, f32))
        outs += [
            ("image", token, f32),
            ("image", token, bf16),
            ("image", (images, IMGROWS, 1), f32),
            ("whole", buffer_shape, bf16),
            ("image", token, bf16),
            ("image", (images, 2 * width, IMGROWS), bf16),
            ("image", token, bf16),
            ("image", (images, PAIRS * HEADS, WPAD, LANES), bf16),
            ("image", (images, width, IMGROWS), bf16),
            ("whole", (width, width), bf16),
        ]
        scratch = [pltpu.VMEM(buffer_shape, f32)]
        gathered_shapes = [(mp, *a.shape[1:]) for a in shards]
        if gather:
            outs.append(("whole", (3 * width, width), bf16))
            outs += [("any", shape, bf16) for shape in gathered_shapes[2:]]
            scratch += [pltpu.VMEM(shape, bf16) for shape in gathered_shapes[:2]] + WeightGather.scratch(4)
        results = list(
            image_call(
                functools.partial(attention_forward_kernel, first, l % 2 == 1, mp, gather),
                images, arrays, outs, scratch, f"attend_{l}", 3 * LAYERS + 1 if gather else None,
            )
        )
        if gather:
            gathered[l] = [results[-3], None] + results[-2:]
            results = results[:-3]
        carried = results.pop(0)
        if first:
            biases = results.pop(0)
        else:
            records[-1]["expert_out"] = results.pop(0)
        middle, second_low, gate, buffer = results[:4]
        gather = fast and l < LAYERS - 1
        received, returned, up_eff, down_eff, *more = expert_call(
            functools.partial(expert_forward_kernel, dp, mp, l, gather),
            [buffer.reshape(EXPERTS, SLOTS, width)],
            [
                (block_rows, bf16),
                (block_rows, bf16),
                ((width, hidden), bf16),
                ((hidden, width), bf16),
            ],
            [
                pltpu.VMEM(block_rows, bf16),
                pltpu.VMEM((8, LANES) if fast else (width, hidden), f32),
                pltpu.VMEM(gathered_shapes[2], bf16),
                pltpu.VMEM(gathered_shapes[3], bf16),
                pltpu.VMEM((width, hidden), bf16),
                pltpu.VMEM((hidden, width), bf16),
                pltpu.SemaphoreType.DMA((4,)),
            ]
            + (WeightGather.scratch(4) if gather else []),
            dp, l, f"experts_{l}", 4 * dp * SLOTS * width * hidden,
            [gathered[l][2], gathered[l][3], residual_up, residual_down, *(shards if gather else ())],
            [(shape, bf16) for shape in gathered_shapes] if gather else (),
        )
        if gather:
            gathered[l + 1] = more
        returned = by_piece(returned)
        before = (middle, gate, returned)
        records.append(
            dict(
                carried=carried, middle=middle, second_low=second_low, gate=gate, saved=results[4:], received=received,
                up_eff=up_eff, down_eff=down_eff,
            )
        )

    top = records[-1]
    block_output, grad, logit_grad, router_part, buffer = image_call(
        turn_kernel,
        images,
        [
            ("image", before[0]),
            ("image", before[1]),
            ("whole", before[2]),
            ("image", cotangent),
            ("whole", enter),
            ("whole", leave),
            ("image", col_form),
            ("image", row_form),
            ("image", top["second_low"]),
            (LAYERS - 1, routers),
        ],
        [
            ("image", patches.shape, bf16),
            ("image", token, f32),
            ("image", (images, IMGROWS, LANES), f32),
            ("whole", (LANES, width), f32),
            ("whole", buffer_shape, bf16),
        ],
        [pltpu.VMEM(buffer_shape, f32)],
        "turn",
    )
    router_parts, tables, smalls = [None] * LAYERS, [None] * LAYERS, [None] * LAYERS
    residual_sums, shard_sums = [None] * LAYERS, [None] * LAYERS
    router_parts[LAYERS - 1] = router_part
    units, attn_units, mines = [None] * LAYERS, [None] * LAYERS, [None] * LAYERS
    for l in reversed(range(LAYERS)):
        rec = records[l]
        last = l == 0
        reduce = fast and l < LAYERS - 1
        arrays = [buffer.reshape(EXPERTS, SLOTS, width), rec["received"], rec["up_eff"], rec["down_eff"]]
        outs = [(block_rows, bf16)]
        scratch = [
            pltpu.VMEM(block_rows, bf16),
            pltpu.VMEM((dp, SLOTS, hidden), bf16),
            pltpu.VMEM((dp, SLOTS, hidden), f32),
            pltpu.VMEM((dp, SLOTS, hidden), bf16),
            pltpu.VMEM(block_rows, bf16),
        ]
        if fast:
            outs.append(((2, mp, width, width), bf16))
            scratch += [pltpu.VMEM((width, hidden), f32)] * 2
        else:
            outs += [((width, hidden), f32)] * 2
        if reduce:
            arrays += [mines[l + 1], attn_units[l + 1]]
            outs += [((2, mp, width, width), bf16), ((width, width), bf16)]
            scratch += RowSum.scratch(1, width) + RowGather.scratch(2)
        results = list(
            expert_call(
                functools.partial(expert_backward_kernel, dp, mp, fast, reduce), arrays, outs, scratch, dp, LAYERS + l,
                f"experts_back_{l}", 10 * dp * SLOTS * width * hidden,
            )
        )
        returned_grad = results.pop(0)
        if fast:
            units[l] = results.pop(0)
        else:
            residual_sums[l] = lax.psum(tuple(t.astype(bf16) for t in results[:2]), "mp")
        if reduce:
            full_above, mine_above = results
        window_in, qk, v, probs, att, proj_full = rec["saved"]
        qkv_full = gathered[l][0].reshape(3 * width, width)
        arrays = [
            ("smem", image_valid),
            ("image", grad),
            ("whole", by_piece(returned_grad)),
            ("image", logit_grad),
            ("image", rec["middle"]),
            ("image", rec["carried"]),
            (l, routers),
            ("image", col_form),
            ("whole", moves[l]),
            ("whole", backs[l]),
            (l, norm_gain),
            ("whole", proj_full),
            ("whole", qkv_full),
            ("image", window_in),
            ("image", qk),
            ("image", v),
            ("image", probs),
            ("image", att),
        ]
        outs = [("image", patches.shape if last else token, f32)]
        scratch = [pltpu.VMEM((3 * width, (2 - images % 2) * IMGROWS), bf16)]
        closes = fast and last
        table_shape, small_shape = (HEADS, WPAD, LANES), (8, width)
        if fast:
            arrays.append(("whole", units[l]))
            scratch += [pltpu.VMEM((3 * width, width), f32), pltpu.VMEM((width, width), f32)]
        if closes:
            outs += [
                ("whole", (2, mp, width, width), bf16),
                ("whole", (3, width, width), bf16),
                ("whole", (Closing.lines, width), f32),
                ("whole", (3, width, width), bf16),
            ]
        else:
            if fast:
                outs += [
                    ("whole", (width // 2, width), bf16),
                    ("whole", (mp, width, width), bf16),
                    ("whole", (2, width, width), bf16),
                ]
            else:
                outs += [("whole", (3 * width, width), f32), ("whole", (width, width), f32)]
            outs += [("whole", table_shape, f32), ("whole", small_shape, f32)]
        if last:
            arrays.append(("whole", leave))
            if fast:
                arrays += [
                    ("whole", a)
                    for a in (
                        tables[1], smalls[1], router_parts[1], router_parts[0], entry_col, halves_above, mines[1],
                        mine_above,
                    )
                ]
        else:
            below = records[l - 1]
            arrays += [
                ("image", row_form),
                ("image", below["expert_out"]),
                ("image", below["second_low"]),
                (l - 1, routers),
            ]
            outs += [
                ("image", (images, IMGROWS, LANES), f32),
                ("whole", (LANES, width), f32),
                ("whole", buffer_shape, bf16),
            ]
            scratch.append(pltpu.VMEM(buffer_shape, f32))
        if closes:
            scratch += [
                pltpu.VMEM(table_shape, f32),
                pltpu.VMEM(small_shape, f32),
                pltpu.VMEM((mp, width, width), bf16),
                pltpu.VMEM((Closing.lines, width), f32),
            ]
            scratch += [pltpu.VMEM(shape, dtype) for _, shape, dtype in outs[1:5]] + Closing.scratch(dp, width)
        elif fast:
            scratch += RowSum.scratch(2, width) + [pltpu.VMEM((width // 2, width), bf16)]
            scratch += [pltpu.SemaphoreType.DMA((1,))] * 2
        results = list(
            image_call(
                functools.partial(attention_backward_kernel, last, dp, mp, fast),
                images, arrays, outs, scratch, f"attend_back_{l}", 2 * LAYERS + 1 + l if fast else None,
            )
        )
        grad = results.pop(0)
        if closes:
            full, closed, lines, shard_above = results
            continue
        if fast:
            halves_above = results.pop(0)
            attn_units[l], mines[l] = results[:2]
        else:
            qkv_part, proj_part = results[:2]
        tables[l], smalls[l] = results[2:4]
        if not last:
            logit_grad, router_parts[l - 1], buffer = results[4:]
        if fast:
            continue
        attn = (
            lax.psum_scatter(qkv_part.astype(bf16), "mp", scatter_dimension=0, tiled=True),
            lax.psum_scatter(proj_part.T.astype(bf16), "mp", scatter_dimension=0, tiled=True),
        )
        up_sum, down_sum = residual_sums[l]
        if split > 1:
            begin = lax.axis_index("dp") % split * hidden
            empty = jnp.zeros((width, hidden_full), bf16)
            up_sum = lax.dynamic_update_slice_in_dim(empty, up_sum, begin, 1)
            down_sum = lax.dynamic_update_slice_in_dim(empty, down_sum, begin, 1)
        up_columns, down_columns = core_up.shape[-1], core_down.shape[-1]
        up_shard = lax.dynamic_slice_in_dim(up_sum, row_index * up_columns, up_columns, 1)
        down_shard = lax.dynamic_slice_in_dim(down_sum, row_index * down_columns, down_columns, 0)
        shard_sums[l] = lax.psum((attn[0], attn[1], up_shard, down_shard), "dp")

    if fast:
        *attn_grads, core_up_grad, core_down_grad, residual_up_grad, residual_down_grad = format_call(
            [full, full_above], [closed, shard_above], qkv_weight.shape[-1]
        )
        attn_grads = [a.transpose(0, 2, 1) for a in attn_grads]
        core_grads = (core_up_grad, core_down_grad.transpose(0, 2, 1))
        at = LAYERS * HEADS
        table_sum = lines[:at, :OFFSETS]
        router_sum = lines[at : at + LAYERS * EXPERTS].reshape(LAYERS, EXPERTS, width)
        at += LAYERS * EXPERTS
        small_sum = lines[at : at + LAYERS * 8].reshape(LAYERS, 8, width)[:, :4]
    else:
        entry = cell_entries()[None, :] + np.array([key_base_of(key) for key in range(WPAD)])[:, None]
        entry = jnp.asarray(np.where(np.arange(WPAD)[:, None] < WINPOS, entry, -1).reshape(-1))
        entry_turned = (entry[:, None] == jnp.arange(OFFSETS)[None, :]).astype(f32)
        table_part = jnp.dot(
            jnp.stack(tables, 0).reshape(LAYERS * HEADS, WPAD * LANES), entry_turned, precision=highest
        )
        small_part = jnp.stack(smalls, 0)[:, :4]
        router_part = jnp.stack(router_parts, 0)[:, :EXPERTS]
        table_sum, small_sum, router_sum = lax.psum((table_part, small_part, router_part), ("dp", "mp"))

        def shard(k):
            return jnp.stack([shard_sums[l][k] for l in range(LAYERS)], 0).astype(f32)

        attn_grads = (shard(0).transpose(0, 2, 1), shard(1).transpose(0, 2, 1))
        core_grads = (shard(2), shard(3).transpose(0, 2, 1))
        residual_up_grad, residual_down_grad = (
            jnp.stack([residual_sums[l][k] for l in range(LAYERS)], 0).astype(f32) for k in range(2)
        )
        residual_up_grad = residual_up_grad[:, None]
        residual_down_grad = residual_down_grad.transpose(0, 2, 1)[:, None]

    return (
        block_output,
        grad,
        attn_grads[0],
        attn_grads[1],
        core_grads[0],
        core_grads[1],
        residual_up_grad,
        residual_down_grad,
        table_sum.reshape(LAYERS, HEADS, OFFSETS).transpose(0, 2, 1),
        router_sum.transpose(0, 2, 1),
        small_sum[:, 0:2],
        small_sum[:, 2:4],
    )


def solution(mesh):
    placed = (
        P(("dp", "mp"), None, None),
        P(None, None, "mp"),
        P(None, None, "mp"),
        P(None, None, "mp"),
        P(None, None, "mp"),
        P(None, "dp", None, None),
        P(None, "dp", None, None),
        P(),
        P(),
        P(),
        P(),
        P(("dp", "mp"), None, None),
        P(("dp", "mp")),
        P(("dp", "mp"), None),
        P(("dp", "mp"), None),
        P(("dp", "mp"), None, None),
    )
    return jax.shard_map(
        per_device,
        mesh=mesh,
        in_specs=placed,
        out_specs=(
            P(("dp", "mp"), None, None),
            P(("dp", "mp"), None, None),
            P(None, None, "mp"),
            P(None, None, "mp"),
            P(None, None, "mp"),
            P(None, None, "mp"),
            P(None, "dp", None, None),
            P(None, "dp", None, None),
            P(),
            P(),
            P(),
            P(),
        ),
        check_vma=False,
    )
```

```python
import functools

import jax
import jax.numpy as jnp
import numpy as np
from jax import lax
from jax.experimental import pallas as pl
from jax.experimental.pallas import tpu as pltpu
from jax.sharding import PartitionSpec as P

HEADS = 12
HEAD_DIM = 32
EXPERTS = 8
WINDOW = 7
GRID = 14
SHIFT = 3
LAYERS = 2
WINPOS = 49
OFFSETS = 169
CAP = 122

WPAD = 64
IMGROWS = 256
PATCHES = 196
SLOTS = 128
ROWS = EXPERTS * SLOTS
LANES = 128
GROUP = 4
PAIRS = 2
TABLE = 256

bf16 = jnp.bfloat16
f32 = jnp.float32
highest = lax.Precision.HIGHEST
norm_epsilon = 1e-05
mask_fill = -100.0
head_scale = HEAD_DIM ** (-0.5)
MESH = pl.DeviceIdType.MESH
MIB = 1024 * 1024


def nn(a, b):
    return lax.dot_general(a, b, (((1,), (0,)), ((), ())), preferred_element_type=f32)


def nt(a, b):
    return lax.dot_general(a, b, (((1,), (1,)), ((), ())), preferred_element_type=f32)


def tn(a, b):
    return lax.dot_general(a, b, (((0,), (0,)), ((), ())), preferred_element_type=f32)


def iota(shape, dim):
    return lax.broadcasted_iota(jnp.int32, shape, dim)


def onehot(flags):
    return jnp.where(flags, 1.0, 0.0).astype(bf16)


def natural_of_row(shifted):
    moved = SHIFT if shifted else 0
    blocks = GRID // WINDOW
    out = -np.ones(IMGROWS, np.int32)
    for window in range(blocks * blocks):
        for cell in range(WINPOS):
            row = (window // blocks * WINDOW + cell // WINDOW + moved) % GRID
            col = (window % blocks * WINDOW + cell % WINDOW + moved) % GRID
            out[window * WPAD + cell] = row * GRID + col
    return out


def key_base_of(key):
    return (2 * WINDOW) * (WINDOW - 1) - (key // WINDOW * (2 * WINDOW - 1) + key % WINDOW)


def enter_table():
    held = natural_of_row(False)
    return (held[:, None] == np.arange(PATCHES)[None, :]).astype(np.float32)


def move_table(shifted):
    first, second = natural_of_row(False), natural_of_row(shifted)
    same = (second[:, None] == first[None, :]) & (second[:, None] >= 0)
    return same.astype(np.float32)


def cell_entries():
    cell = np.arange(LANES) % WPAD
    return np.where(cell < WINPOS, cell // WINDOW * (2 * WINDOW - 1) + cell % WINDOW, -4 * TABLE).astype(np.int32)


def norm_parts(x):
    width = x.shape[-1]
    center = x - jnp.sum(x, -1, keepdims=True) * (1.0 / width)
    spread = jnp.sum(center * center, -1, keepdims=True) * (1.0 / width)
    rstd = lax.rsqrt(spread + norm_epsilon)
    return center * rstd, rstd


def norm_back(grad, gain, xhat, rstd):
    width = xhat.shape[-1]
    dxhat = grad * gain
    mean_one = jnp.sum(dxhat, -1, keepdims=True) * (1.0 / width)
    mean_two = jnp.sum(dxhat * xhat, -1, keepdims=True) * (1.0 / width)
    return rstd * (dxhat - mean_one - xhat * mean_two)


def turn_blocks(x):
    size = x.shape[0]
    same = onehot(iota((size, size), 0) == iota((size, size), 1))
    return jnp.concatenate([nt(same, x[:, at : at + size]) for at in range(0, x.shape[1], size)], 0)


def split_two(x):
    high = x.astype(bf16)
    return high, (x - high.astype(f32)).astype(bf16)


def collect(pos_col, returned_ref):
    pick = onehot(pos_col == iota((pos_col.shape[0], ROWS), 1))
    out = nn(pick, returned_ref[0])
    for piece in range(1, returned_ref.shape[0]):
        out = out + nn(pick, returned_ref[piece])
    return out


def join(ref):
    return ref[...].reshape(ref.shape[0] * ref.shape[1], *ref.shape[2:])


def store(ref, rows):
    ref[...] = rows.reshape(ref.shape).astype(ref.dtype)


def per_image(function, count):
    return jnp.concatenate([function(i) for i in range(count)], 0)


def image_rows(i):
    return slice(i * IMGROWS, (i + 1) * IMGROWS)


def lay_positions(row_ref):
    return jnp.concatenate([row_ref[i, 0:1, :] for i in range(row_ref.shape[0])], 1)


def spread_rows(pos_row, rows_low):
    return nn(onehot(iota((ROWS, pos_row.shape[1]), 0) == pos_row), rows_low)


def route(second_low, router, pos_col):
    logits = nt(second_low, router)
    lane = iota(logits.shape, 1)
    logits = jnp.where(lane < EXPERTS, logits, -1e30)
    expo = jnp.exp(logits - jnp.max(logits, -1, keepdims=True))
    probs = expo / jnp.sum(expo, -1, keepdims=True)
    expert = jnp.where(pos_col >= 0, pos_col // SLOTS, -1)
    chosen = jnp.where(lane == expert, 1.0, 0.0)
    return probs, chosen, jnp.sum(probs * chosen, -1, keepdims=True)


def head_masks():
    rows = iota((LANES, LANES), 0) // HEAD_DIM
    return [onehot(rows == h) for h in range(GROUP)]


def lane_masks():
    lane = iota((WPAD, LANES), 1)
    return [onehot(lane < WPAD), onehot(lane >= WPAD)]


def keys_entry(cells, key_row, turned):
    parts = [cells + (key_base_of(col) - key_row * (2 * WINDOW - 1)) for col in range(WINDOW)]
    return jnp.concatenate(parts, 0 if turned else 1)


def form_bias(bias_ref, table_ref, entry_row):
    layers, heads = bias_ref.shape[:2]
    lines = layers * heads
    bias_ref[...] = jnp.where(iota(bias_ref.shape, 2) < WINPOS, 0.0, -1e30)
    table = table_ref[...]
    high = table.astype(bf16)
    mid, low = split_two(table - high.astype(f32))
    parts = jnp.concatenate([high.astype(f32), mid.astype(f32), low.astype(f32)], 0).astype(bf16)

    def step(key_row, carry):
        pick = onehot(iota((TABLE, WINDOW * LANES), 0) == keys_entry(entry_row, key_row, False))
        rows = nn(parts, pick)
        rows = rows[:lines] + rows[lines : 2 * lines] + rows[2 * lines :]
        for col in range(WINDOW):
            for layer in range(layers):
                part = rows[layer * heads : (layer + 1) * heads, col * LANES : (col + 1) * LANES]
                bias_ref[layer, :, pl.ds(key_row * WINDOW + col, 1), :] = part.reshape(heads, 1, LANES)
        return carry

    lax.fori_loop(0, WINDOW, step, 0)


def table_grad(parts, entry_col):
    heads = parts[0].shape[0]
    lines = heads * len(parts)

    def step(key_row, total):
        keys = [
            jnp.concatenate([ref[:, pl.ds(key_row * WINDOW + col, 1), :].reshape(heads, LANES) for ref in parts], 0)
            for col in range(WINDOW)
        ]
        rows = jnp.concatenate(keys, 1)
        high = rows.astype(bf16).astype(f32)
        both = jnp.concatenate([high, rows - high], 0).astype(bf16)
        entry = keys_entry(entry_col, key_row, True)
        out = nn(both, onehot(iota((WINDOW * LANES, TABLE), 1) == entry))
        return total + out[:lines] + out[lines:]

    return lax.fori_loop(0, WINDOW, step, jnp.zeros((lines, TABLE), f32))


def attention_forward_kernel(first, shifted, mp, gather, *refs):
    refs = list(refs)
    if first:
        patches_ref, enter_ref = refs[:2]
        refs = refs[2:]
    else:
        prev_ref, prev_gate_ref, returned_ref = refs[:3]
        refs = refs[3:]
    (
        valid_ref, col_ref, row_ref, qkv_ref, proj_ref, bias_ref, move_ref, back_ref, gain_ref, nbias_ref, router_ref,
    ) = refs[:11]
    gain_ref, nbias_ref, router_ref = (ref.at[0] for ref in (gain_ref, nbias_ref, router_ref))
    refs = refs[11:]
    if first:
        table_ref, entry_ref = bias_ref, refs.pop(0)
    if gather:
        core_up_ref, core_down_ref = refs[:2]
        refs = refs[2:]
    carried_ref = refs.pop(0)
    if first:
        biases_ref = refs.pop(0)
        bias_ref = biases_ref.at[0]
    else:
        expert_out_ref = refs.pop(0)
        bias_ref = bias_ref.at[0]
    middle_ref, second_ref, gate_ref, buffer_ref, window_ref, qk_ref, v_ref, probs_ref, att_ref, proj_full = refs[:10]
    refs = refs[10:]
    if gather:
        qkv_full = refs.pop(0)
        up_out, down_out = refs[:2]
        refs = refs[2:]
    total_ref = refs.pop(0)
    step = pl.program_id(0)
    final = pl.num_programs(0) - 1
    count, _, width = carried_ref.shape
    if gather:
        shards = [ref.at[0] for ref in (qkv_ref, proj_ref, core_up_ref, core_down_ref)]
        qkv_ref, proj_ref = refs[:2]
        moving = WeightGather(shards, [qkv_ref, proj_ref, up_out, down_out], refs[2:])

        @pl.when(step == 0)
        def _():
            pl.semaphore_wait(moving.row.greet(), 2)
            for k in (0, 1):
                moving.start(k)
            form_bias(biases_ref, table_ref, entry_ref[...])

    pos_col = join(col_ref)[:, 0:1]
    if first:
        x = per_image(lambda i: nn(enter_ref[...], patches_ref[i]), count)
    else:
        expert_out = collect(pos_col, returned_ref)
        store(expert_out_ref, expert_out)
        x = join(prev_ref) + join(prev_gate_ref) * expert_out
    store(carried_ref, x)
    xhat, _ = norm_parts(x)
    normed = (xhat * gain_ref[0:1, :] + nbias_ref[0:1, :]).astype(bf16)
    window_in = per_image(lambda i: nn(move_ref[...], normed[image_rows(i)]), count).astype(bf16)
    store(window_ref, window_in)

    @pl.when(step == 0)
    def _():
        if gather:
            for k in (0, 1):
                moving.forward(k)
            for k in (2, 3):
                moving.start(k)
            for k in (0, 1):
                moving.arrive(k)
            qkv_full[...] = join(qkv_ref)
        elif first:
            form_bias(biases_ref, table_ref, entry_ref[...])
        proj_full[...] = turn_blocks(join(proj_ref)).astype(bf16)
        total_ref[...] = jnp.zeros(total_ref.shape, f32)

    qkv = join(qkv_ref)
    turned = nt(qkv, window_in).astype(bf16)
    straight = nt(window_in, qkv[width:]).astype(bf16)
    for i in range(count):
        qk_ref[i] = turned[: 2 * width, image_rows(i)]
    store(v_ref, straight[:, width:])
    heads_rows = head_masks()
    halves = lane_masks()
    low_lane = iota((WPAD, LANES), 1) < WPAD
    if shifted:
        row_labels = [nt(row_ref[i].astype(f32).astype(bf16), move_ref[...]) for i in range(count)]
        col_labels = [nn(move_ref[...], col_ref[i].astype(f32).astype(bf16)) for i in range(count)]
    for pair in range(PAIRS * count):
        image, side = pair // PAIRS, pair % PAIRS
        across = slice(pair * LANES, (pair + 1) * LANES)
        within = slice(side * LANES, (side + 1) * LANES)
        if shifted:
            ahead = col_labels[image][side * LANES : side * LANES + WPAD, 1:2]
            behind = col_labels[image][side * LANES + WPAD : (side + 1) * LANES, 1:2]
            key_label = jnp.where(low_lane, ahead, behind)
            mask = jnp.where(key_label == row_labels[image][1:2, within], 0.0, mask_fill)
        for group in range(HEADS // GROUP):
            features = slice(group * LANES, (group + 1) * LANES)
            queries = turned[features, across]
            spread = jnp.concatenate([queries * heads_rows[h] for h in range(GROUP)], 1)
            raw = nn(straight[across, features], spread)
            for h in range(GROUP):
                head = group * GROUP + h
                part = raw[:, h * LANES : (h + 1) * LANES]
                scores = jnp.where(low_lane, part[:WPAD], part[WPAD:]) * head_scale + bias_ref[head]
                if shifted:
                    scores = scores + mask
                expo = jnp.exp(scores - jnp.max(scores, 0, keepdims=True))
                probs = (expo * (1.0 / jnp.sum(expo, 0, keepdims=True))).astype(bf16)
                probs_ref[image, side * HEADS + head] = probs
                both = jnp.concatenate([probs * halves[0], probs * halves[1]], 0)
                at = slice(head * HEAD_DIM, (head + 1) * HEAD_DIM)
                values = turned[2 * width + head * HEAD_DIM : 2 * width + (head + 1) * HEAD_DIM, across]
                att_ref[image, at, within] = nn(values, both).astype(bf16)
    attended = per_image(lambda i: nt(back_ref[...], att_ref[i]), count).astype(bf16)
    branch = nt(attended, join(proj_ref))
    middle = x + per_image(lambda i: valid_ref[step * count + i].astype(f32) * branch[image_rows(i)], count)
    store(middle_ref, middle)
    xhat, _ = norm_parts(middle)
    second_low = (xhat * gain_ref[1:2, :] + nbias_ref[1:2, :]).astype(bf16)
    store(second_ref, second_low)
    _, _, gate = route(second_low, router_ref[...], pos_col)
    store(gate_ref, gate)
    total_ref[...] += spread_rows(lay_positions(row_ref), second_low)

    @pl.when(step == final)
    def _():
        buffer_ref[...] = total_ref[...].astype(bf16)
        if gather:
            for k in (2, 3):
                moving.forward(k)
            for k in (2, 3):
                moving.arrive(k)
            for k in range(4):
                moving.sent(k)


def image_spec(array_shape, count):
    rest = tuple(array_shape[1:])
    zeros = (0,) * len(rest)
    return pl.BlockSpec((count,) + rest, lambda i: (i,) + zeros)


def whole_spec(array_shape):
    zeros = (0,) * len(array_shape)
    return pl.BlockSpec(tuple(array_shape), lambda i: zeros)


def image_call(kernel, images, arrays, outs, scratch, name, collective_id=None):
    count = 2 - images % 2

    def spec(kind, shape):
        if isinstance(kind, int):
            rest = tuple(shape[1:])
            return pl.BlockSpec((1,) + rest, lambda i: (kind,) + (0,) * len(rest))
        if kind in ("smem", "any"):
            return pl.BlockSpec(memory_space=pltpu.SMEM if kind == "smem" else pl.ANY)
        return image_spec(shape, count) if kind == "image" else whole_spec(shape)

    return pl.pallas_call(
        kernel,
        grid=(images // count,),
        out_shape=[jax.ShapeDtypeStruct(shape, dtype) for _, shape, dtype in outs],
        in_specs=[spec(kind, array.shape) for kind, array in arrays],
        out_specs=[spec(kind, shape) for kind, shape, _ in outs],
        scratch_shapes=scratch,
        compiler_params=pltpu.CompilerParams(
            vmem_limit_bytes=56 * MIB,
            dimension_semantics=("arbitrary",),
            collective_id=collective_id,
            has_side_effects=collective_id is not None,
        ),
        name=name,
    )(*[array for _, array in arrays])


def send_part(g, expert_out, second_low, router, pos_col, pos_row, logit_ref, router_grad_ref, total_ref):
    probs, chosen, gate = route(second_low, router, pos_col)
    gate_grad = jnp.where(pos_col >= 0, jnp.sum(g * expert_out, -1, keepdims=True), 0.0)
    sent = (gate * g).astype(bf16)
    logit_grad = gate_grad * gate * (chosen - probs)
    store(logit_ref, logit_grad)
    high, low = split_two(logit_grad)
    router_grad_ref[...] += tn(high, second_low) + tn(low, second_low)
    total_ref[...] += spread_rows(pos_row, sent)


def turn_kernel(
    prev_ref, gate_ref, returned_ref, cotangent_ref, enter_ref, leave_ref, col_ref, row_ref, second_ref, router_ref,
    block_ref, grad_ref, logit_ref, router_grad_ref, buffer_ref, total_ref,
):
    step = pl.program_id(0)
    count = cotangent_ref.shape[0]

    @pl.when(step == 0)
    def _():
        total_ref[...] = jnp.zeros(total_ref.shape, f32)
        router_grad_ref[...] = jnp.zeros(router_grad_ref.shape, f32)

    pos_col = join(col_ref)[:, 0:1]
    expert_out = collect(pos_col, returned_ref)
    x = (join(prev_ref) + join(gate_ref) * expert_out).astype(bf16)
    for i in range(count):
        block_ref[i] = nn(leave_ref[...], x[image_rows(i)]).astype(bf16)
    g = per_image(lambda i: nn(enter_ref[...], cotangent_ref[i]), count)
    store(grad_ref, g)
    send_part(
        g, expert_out, join(second_ref), router_ref[0], pos_col, lay_positions(row_ref), logit_ref, router_grad_ref, total_ref
    )

    @pl.when(step == pl.num_programs(0) - 1)
    def _():
        buffer_ref[...] = total_ref[...].astype(bf16)


def attention_backward_kernel(last, dp, mp, fast, *refs):
    (
        valid_ref, grad_ref, returned_ref, logit_ref, middle_ref, carried_ref, router_ref, col_ref, move_ref, back_ref,
        gain_ref, proj_ref, qkv_ref, window_ref, qk_ref, v_ref, probs_ref, att_ref,
    ) = refs[:18]
    refs = refs[18:]
    refs = list(refs)
    if fast:
        units_ref = refs.pop(0)
    if last:
        leave_ref = refs.pop(0)
        if fast:
            table_above, small_above, router_above, router_here, entry_ref, half_above, down_above, attn_above = refs[:8]
            refs = refs[8:]
    else:
        row_ref, expert_out_ref, second_ref, router_next_ref = refs[:4]
        refs = refs[4:]
    out_ref = refs.pop(0)
    closing = None
    if fast and last:
        results, refs = refs[:4], refs[4:]
    else:
        if fast:
            halves_ref = refs.pop(0)
            unit_ref, mine_ref = refs[:2]
        else:
            qkv_grad_ref, proj_grad_ref = refs[:2]
        table_ref, small_ref = refs[2:4]
        refs = refs[4:]
    if not last:
        logit_out_ref, router_grad_ref, buffer_ref = refs[:3]
        refs = refs[3:]
    turned = refs.pop(0)
    if fast:
        qkv_grad_ref, proj_grad_ref = refs[:2]
        refs = refs[2:]
    if not last:
        total_ref = refs.pop(0)
    step = pl.program_id(0)
    final = pl.num_programs(0) - 1
    count, _, width = carried_ref.shape
    if fast:
        row = Row()
        if last:
            table_ref, small_ref, unit_ref, lines_ref = refs[:4]
            landing, refs = refs[4:8], refs[8:]
            above = (half_above, down_above.at[1], attn_above)
            closing = Closing(row, dp, units_ref, unit_ref, lines_ref, above, landing, refs)
            sums = closing.sums
        else:
            sums = RowSum(row, blocks(units_ref), refs[0], refs[1], refs[2], blocks(mine_ref), refs[3:7])
            across_x = DeepSum(dp, [mine_ref.at[0]], [refs[7]], [halves_ref], [None], [None], refs[8:10] * 4)

        def take(k):
            if closing:
                closing.take(k)
            else:
                sums.end(k)
                if k == 0:
                    across_x.over_x(k).start()

        @pl.when(step == 0)
        def _():
            if closing:
                closing.enter()
            else:
                barrier = row.greet()
                pl.semaphore_wait(barrier, 2 + across_x.greet(barrier, False))
                for k in range(2):
                    sums.start(k)

    @pl.when(step == 0)
    def _():
        qkv_grad_ref[...] = jnp.zeros(qkv_grad_ref.shape, f32)
        proj_grad_ref[...] = jnp.zeros(proj_grad_ref.shape, f32)
        table_ref[...] = jnp.zeros(table_ref.shape, f32)
        small_ref[...] = jnp.zeros(small_ref.shape, f32)
        if not last:
            total_ref[...] = jnp.zeros(total_ref.shape, f32)
            router_grad_ref[...] = jnp.zeros(router_grad_ref.shape, f32)

    pos_col = join(col_ref)[:, 0:1]
    g = join(grad_ref)
    high, low = split_two(join(logit_ref))
    gain_ref, router = gain_ref.at[0], router_ref[0]
    normed_grad = collect(pos_col, returned_ref) + nn(high, router) + nn(low, router)
    xhat, rstd = norm_parts(join(middle_ref))
    small_ref[1:2, :] += jnp.sum(normed_grad * xhat, 0, keepdims=True)
    small_ref[3:4, :] += jnp.sum(normed_grad, 0, keepdims=True)
    middle_grad = g + norm_back(normed_grad, gain_ref[1:2, :], xhat, rstd)

    if fast:

        @pl.when(step == 0)
        def _():
            for k in range(2):
                sums.middle(k)

    def branch_part(i):
        low_part = (valid_ref[step * count + i].astype(f32) * middle_grad[image_rows(i)]).astype(bf16)
        return nn(move_ref[...], low_part)

    branch_grad = per_image(branch_part, count).astype(bf16)
    for i in range(count):
        proj_grad_ref[...] += nn(att_ref[i], branch_grad[image_rows(i)])
    att_grad = nt(proj_ref[...], branch_grad).astype(bf16)
    if fast:

        @pl.when(step == 0)
        def _():
            if closing:
                closing.early()

        pl.when(step == final)(functools.partial(take, 0))

    heads_rows = head_masks()
    halves = lane_masks()
    low_lane = iota((WPAD, LANES), 1) < WPAD
    for pair in range(PAIRS * count):
        image, side = pair // PAIRS, pair % PAIRS
        across = slice(pair * LANES, (pair + 1) * LANES)
        within = slice(side * LANES, (side + 1) * LANES)
        for group in range(HEADS // GROUP):
            features = slice(group * LANES, (group + 1) * LANES)
            grads = att_grad[features, across]
            spread = jnp.concatenate([grads * heads_rows[h] for h in range(GROUP)], 1)
            raw = nn(v_ref[image, within, features], spread)
            for h in range(GROUP):
                head = group * GROUP + h
                at = slice(head * HEAD_DIM, (head + 1) * HEAD_DIM)
                below = slice(width + head * HEAD_DIM, width + (head + 1) * HEAD_DIM)
                lowest = slice(2 * width + head * HEAD_DIM, 2 * width + (head + 1) * HEAD_DIM)
                part = raw[:, h * LANES : (h + 1) * LANES]
                probs_grad = jnp.where(low_lane, part[:WPAD], part[WPAD:])
                probs_low = probs_ref[image, side * HEADS + head]
                probs = probs_low.astype(f32)
                weighted = probs * probs_grad
                scores_grad = weighted - probs * jnp.sum(weighted, 0, keepdims=True)
                table_ref[head] += scores_grad
                scores_low = scores_grad.astype(bf16)
                both = jnp.concatenate([scores_low * halves[0], scores_low * halves[1]], 0)
                probs_both = jnp.concatenate([probs_low * halves[0], probs_low * halves[1]], 0)
                turned[at, across] = (nn(qk_ref[image, below, within], both) * head_scale).astype(bf16)
                turned[below, across] = (nt(qk_ref[image, at, within], both) * head_scale).astype(bf16)
                turned[lowest, across] = nt(att_grad[at, across], probs_both).astype(bf16)
    qkv_grad_ref[...] += nn(turned[...], join(window_ref))
    if fast:

        @pl.when(step == final)
        def _():
            columns, rows = 3 * width // mp, width // mp
            proj_turned = turn_blocks(proj_grad_ref[...].astype(bf16)).astype(bf16)
            for place in range(mp):
                q = quarter_at(place, mp)
                unit_ref[place, :columns] = qkv_grad_ref[q * columns : (q + 1) * columns].astype(bf16)
                unit_ref[place, columns:] = proj_turned[q * rows : (q + 1) * rows]
            if closing:
                closing.open()
            take(1)
            if closing:
                heads = 2 * HEADS
                lines_ref[...] = jnp.zeros(lines_ref.shape, f32)
                lines_ref[:heads, :TABLE] = table_grad([table_ref, table_above], entry_ref[...])

    mixed_grad = per_image(lambda i: nt(back_ref[...], turned[:, image_rows(i)]), count).astype(bf16)
    first_grad = nn(mixed_grad, qkv_ref[...])
    if closing:

        @pl.when(step == final)
        def _():
            closing.cross()

    xhat, rstd = norm_parts(join(carried_ref))
    small_ref[0:1, :] += jnp.sum(first_grad * xhat, 0, keepdims=True)
    small_ref[2:3, :] += jnp.sum(first_grad, 0, keepdims=True)
    if closing:

        @pl.when(step == final)
        def _():
            heads = 2 * HEADS
            lines_ref[heads : heads + EXPERTS] = router_here[:EXPERTS]
            lines_ref[heads + EXPERTS : heads + 2 * EXPERTS] = router_above[:EXPERTS]
            lines_ref[heads + 2 * EXPERTS : heads + 2 * EXPERTS + 8] = small_ref[...]
            lines_ref[heads + 2 * EXPERTS + 8 : heads + 2 * EXPERTS + 16] = small_above[...]
            closing.send_lines()

    out = middle_grad + norm_back(first_grad, gain_ref[0:1, :], xhat, rstd)
    if last:
        top = out.astype(bf16)
        rest = out - top.astype(f32)
        mid, low = split_two(rest)
        leave = leave_ref[...]
        for i in range(count):
            at = image_rows(i)
            out_ref[i] = nn(leave, top[at]) + nn(leave, mid[at]) + nn(leave, low[at])
    else:
        store(out_ref, out)
        send_part(
            out, join(expert_out_ref), join(second_ref), router_next_ref[0], pos_col, lay_positions(row_ref), logit_out_ref,
            router_grad_ref, total_ref,
        )

    @pl.when(step == final)
    def _():
        if not last:
            buffer_ref[...] = total_ref[...].astype(bf16)
        if closing:
            closing.finish()
            for out, landed in zip(results, landing):
                out[...] = landed[...]
        elif fast:
            across_x.halve(0)
            across_x.over_x(0).wait_send()
            for k in range(2):
                sums.finish(k)


def quarter_at(place, mp):
    return place % (mp // 2) * 2 + place // (mp // 2)


def add_up(*parts):
    total = parts[0].astype(f32)
    for part in parts[1:]:
        total = total + part.astype(f32)
    return total


class Copies:
    def __init__(self, source, target, send_sem, recv_sem, device):
        self.source, self.target = source, target
        self.how = dict(send_sem=send_sem, recv_sem=recv_sem, device_id=device, device_id_type=MESH)
        whole = pltpu.make_async_remote_copy(src_ref=source, dst_ref=target, **self.how)
        self.wait_send, self.wait_recv = whole.wait_send, whole.wait_recv

    def start(self):
        shape = self.source.shape
        rows = shape[-2]
        parts = max(n for n in (1, 2, 3, 4) if rows % (16 * n) == 0)
        size = rows // parts
        leads = [(lead,) for lead in range(shape[0])] if len(shape) == 3 else [()]
        for lead in leads:
            for part in range(parts):
                at = (*lead, pl.ds(part * size, size))
                pltpu.make_async_remote_copy(
                    src_ref=self.source.at[at], dst_ref=self.target.at[at], **self.how
                ).start()

    def wait(self):
        self.wait_send()
        self.wait_recv()


def to_row(source, target, sems, k, row):
    return Copies(source, target, sems[0].at[k], sems[1].at[k], {"mp": row})


class Row:
    def __init__(self):
        row = lax.axis_index("mp")
        self.row, self.core, self.y = row, lax.rem(row, 2), lax.div(row, 2)
        self.sibling, self.across = row + 1 - 2 * self.core, row + 2 - 4 * self.y
        self.place = self.core * 2 + self.y
        self.place_across = self.core * 2 + 1 - self.y

    def greet(self):
        barrier = pltpu.get_barrier_semaphore()
        for row in (self.sibling, self.across):
            pl.semaphore_signal(barrier, inc=1, device_id={"mp": row}, device_id_type=MESH)
        return barrier


class RowSum:
    semaphores = 4

    def __init__(self, row, units, core_in, y_out, y_in, mine, sems):
        self.row, self.units, self.mine = row, units, mine
        self.core_in, self.y_out, self.y_in = core_in, y_out, y_in
        self.sems = (sems[:2], sems[2:])

    def pair(self, k):
        theirs = self.units[k].at[pl.ds(2 * (1 - self.row.core), 2)]
        return to_row(theirs, self.core_in.at[k], self.sems[0], k, self.row.sibling)

    def cross(self, k):
        return to_row(self.y_out.at[k], self.y_in.at[k], self.sems[1], k, self.row.across)

    def start(self, k):
        self.pair(k).start()

    def middle(self, k):
        self.pair(k).wait_recv()
        other = 1 - self.row.y
        mixed = add_up(self.units[k][self.row.core * 2 + other], self.core_in[k, other])
        self.y_out[k] = mixed.astype(bf16)
        self.cross(k).start()

    def end(self, k):
        self.cross(k).wait_recv()
        self.mine[k][...] = add_up(
            self.units[k][self.row.place], self.core_in[k, self.row.y], self.y_in[k]
        ).astype(bf16)

    def finish(self, k):
        self.pair(k).wait_send()
        self.cross(k).wait_send()

    @classmethod
    def scratch(cls, count, width):
        return [
            pltpu.VMEM((count, 2, width, width), bf16),
            pltpu.VMEM((count, width, width), bf16),
            pltpu.VMEM((count, width, width), bf16),
        ] + [pltpu.SemaphoreType.DMA((count,))] * cls.semaphores


class RowGather:
    semaphores = 6

    def __init__(self, row, sources, fulls, slot, slot_across, sems):
        self.row, self.sources, self.fulls = row, sources, fulls
        self.slot, self.slot_across = slot, slot_across
        self.sems = (sems[:2], sems[2:4], sems[4:])

    def over(self, k):
        return to_row(self.sources[k], self.fulls[k].at[self.slot], self.sems[0], k, self.row.across)

    def near(self, k):
        return to_row(self.sources[k], self.fulls[k].at[self.slot], self.sems[1], k, self.row.sibling)

    def onward(self, k):
        block = self.fulls[k].at[self.slot_across]
        return to_row(block, block, self.sems[2], k, self.row.sibling)

    def start(self, k):
        self.over(k).start()
        self.near(k).start()

    def forward(self, k):
        self.over(k).wait_recv()
        self.onward(k).start()

    def arrive(self, k):
        self.near(k).wait_recv()
        self.onward(k).wait_recv()

    def sent(self, k):
        self.over(k).wait_send()
        self.near(k).wait_send()
        self.onward(k).wait_send()

    @classmethod
    def scratch(cls, count):
        return [pltpu.SemaphoreType.DMA((count,))] * cls.semaphores


class WeightGather(RowGather):
    def __init__(self, shards, fulls, sems):
        row = Row()
        super().__init__(row, shards, fulls, row.row, row.across, sems[:6])
        self.own_sem = sems[6]

    def own(self, k):
        return pltpu.make_async_copy(self.sources[k], self.fulls[k].at[self.slot], self.own_sem.at[k])

    def start(self, k):
        super().start(k)
        self.own(k).start()

    def arrive(self, k):
        super().arrive(k)
        self.own(k).wait()

    @classmethod
    def scratch(cls, count):
        return super().scratch(count) + [pltpu.SemaphoreType.DMA((count,))]


class DeepSum:
    def __init__(self, dp, total, arrived, halves, slots, result, sems):
        self.total, self.arrived, self.halves, self.slots, self.result = total, arrived, halves, slots, result
        self.x_sems, self.z_sems, self.z_back, self.x_back = (sems[2 * k : 2 * k + 2] for k in range(4))
        me = lax.axis_index("dp")
        self.x, self.z, self.deep = lax.rem(me, 2), lax.div(me, 2), dp // 2
        self.partner = me + 1 - 2 * self.x

    def greet(self, barrier, whole=True):
        pl.semaphore_signal(barrier, inc=1, device_id={"dp": self.partner}, device_id_type=MESH)
        if not whole:
            return 1
        for off in range(1, self.deep):
            peer = lax.rem(self.z + off, self.deep) * 2 + self.x
            pl.semaphore_signal(barrier, inc=1, device_id={"dp": peer}, device_id_type=MESH)
        return self.deep

    def cut(self, k):
        height = self.halves[k].shape[0]
        return height, height // self.deep

    def over_x(self, k):
        height, _ = self.cut(k)
        away = self.total[k].at[pl.ds(pl.multiple_of((1 - self.x) * height, height), height)]
        return Copies(away, self.arrived[k], self.x_sems[0].at[k], self.x_sems[1].at[k], {"dp": self.partner})

    def over_z(self, k, off):
        _, piece = self.cut(k)
        to = lax.rem(self.z + off, self.deep)
        part = self.halves[k].at[pl.ds(pl.multiple_of(to * piece, piece), piece)]
        sems = [sem.at[k, off] for sem in self.z_sems]
        return to_peer(part, self.slots[k].at[off], *sems, to * 2 + self.x)

    def own_piece(self, k):
        height, piece = self.cut(k)
        return self.result[k].at[pl.ds(pl.multiple_of(self.x * height + self.z * piece, piece), piece)]

    def own_half(self, k):
        height, _ = self.cut(k)
        return self.result[k].at[pl.ds(pl.multiple_of(self.x * height, height), height)]

    def back_z(self, k, off):
        to = lax.rem(self.z + off, self.deep)
        sems = [sem.at[k, off] for sem in self.z_back]
        return to_peer(self.own_piece(k), self.own_piece(k), *sems, to * 2 + self.x)

    def back_x(self, k):
        half = self.own_half(k)
        return Copies(half, half, self.x_back[0].at[k], self.x_back[1].at[k], {"dp": self.partner})

    def halve(self, k):
        self.over_x(k).wait_recv()
        height, _ = self.cut(k)
        keep = self.total[k][pl.ds(pl.multiple_of(self.x * height, height), height)]
        self.halves[k][...] = add_up(keep, self.arrived[k][...]).astype(self.halves[k].dtype)

    def deepen(self, k):
        for off in range(1, self.deep):
            self.over_z(k, off).start()

    def quarter(self, k):
        for off in range(1, self.deep):
            self.over_z(k, off).wait_recv()
        _, piece = self.cut(k)
        keep = self.halves[k][pl.ds(pl.multiple_of(self.z * piece, piece), piece)]
        total = add_up(keep, *[self.slots[k][off] for off in range(1, self.deep)])
        self.own_piece(k)[...] = total.astype(self.result[k].dtype)
        for off in range(1, self.deep):
            self.back_z(k, off).start()

    def widen(self, k):
        for off in range(1, self.deep):
            self.back_z(k, off).wait_recv()
        self.back_x(k).start()

    def finish(self, k, halved=True):
        if halved:
            self.over_x(k).wait_send()
        for off in range(1, self.deep):
            self.over_z(k, off).wait_send()
            self.back_z(k, off).wait_send()
        self.back_x(k).wait()

    @staticmethod
    def semaphores(dp, count):
        one, many = pltpu.SemaphoreType.DMA((count,)), pltpu.SemaphoreType.DMA((count, dp // 2))
        return [one, one, many, many, many, many, one, one]


def blocks(ref):
    return [ref.at[k] for k in range(ref.shape[0])]


class WideSum:
    def __init__(self, dp, total, slots, result, sems):
        self.dp, self.total, self.slots, self.result, self.sems = dp, total, slots, result, sems
        self.me = lax.axis_index("dp")

    def piece(self, ref, at):
        size = ref.shape[0] // self.dp
        return ref.at[pl.ds(pl.multiple_of(at * size, size), size)]

    def out(self, k, p):
        peer = partner_of(self.me, p, self.dp)
        sems = self.sems[0].at[k, p], self.sems[1].at[k, p]
        return to_peer(self.piece(self.total[k], peer), self.slots[k].at[p], *sems, peer)

    def back(self, k, p):
        mine = self.piece(self.result[k], self.me)
        sems = self.sems[2].at[k, p], self.sems[3].at[k, p]
        return to_peer(mine, mine, *sems, partner_of(self.me, p, self.dp))

    def start(self, k):
        for p in range(self.dp - 1, 0, -1):
            self.out(k, p).start()

    def middle(self, k):
        for p in range(1, self.dp):
            self.out(k, p).wait_recv()
        total = add_up(self.piece(self.total[k], self.me)[...], *[self.slots[k][p] for p in range(1, self.dp)])
        self.piece(self.result[k], self.me)[...] = total.astype(self.result[k].dtype)
        for p in range(self.dp - 1, 0, -1):
            self.back(k, p).start()

    def finish(self, k):
        for p in range(1, self.dp):
            self.out(k, p).wait_send()
            self.back(k, p).wait()

    @staticmethod
    def semaphores(dp, count):
        return [pltpu.SemaphoreType.DMA((count, dp))] * 4


class HalvingSum:
    def __init__(self, total, result, refs, given=None):
        me = lax.axis_index("dp")
        self.bits = (lax.rem(me, 2), lax.rem(lax.div(me, 2), 2), lax.div(me, 4))
        self.partners = [me + (1 << s) * (1 - 2 * self.bits[s]) for s in range(3)]
        self.result = result
        self.arrived = refs[:3]
        self.held = [total, given if given is not None else refs[3], refs[4]]
        self.sems = refs[5:9]
        self.first = 0 if given is None else 1

    def size(self, step):
        return self.result.shape[0] >> (step + 1)

    def rows(self, step):
        base = sum(self.bits[s] * self.size(s) for s in range(step + 1))
        return self.result.at[pl.ds(pl.multiple_of(base, self.size(step)), self.size(step))]

    def part(self, step, bit):
        size = self.size(step)
        return self.held[step].at[pl.ds(pl.multiple_of(bit * size, size), size)]

    def down(self, step):
        away = self.part(step, 1 - self.bits[step])
        return to_peer(away, self.arrived[step], self.sems[0].at[step], self.sems[1].at[step], self.partners[step])

    def up(self, step):
        rows = self.rows(step)
        return to_peer(rows, rows, self.sems[2].at[step], self.sems[3].at[step], self.partners[step])

    def begin(self):
        self.down(self.first).start()

    def add(self, step):
        self.down(step).wait_recv()
        target = self.rows(2) if step == 2 else self.held[step + 1]
        keep = self.part(step, self.bits[step])[...]
        target[...] = add_up(keep, self.arrived[step][...]).astype(self.result.dtype)

    def halve(self):
        self.add(0)
        self.down(1).start()

    def quarter(self):
        self.add(1)
        self.down(2).start()

    def eighth(self):
        self.add(2)
        self.up(2).start()

    def widen(self):
        self.up(2).wait_recv()
        self.up(1).start()

    def wider(self):
        self.up(1).wait_recv()
        self.up(0).start()

    def finish(self):
        for step in range(self.first, 3):
            self.down(step).wait_send()
        for step in (2, 1):
            self.up(step).wait_send()
        self.up(0).wait_send()
        self.up(0).wait_recv()

    @staticmethod
    def scratch(width):
        half = [pltpu.VMEM((width >> step, width), bf16) for step in (1, 2, 3)]
        return half + half[:2] + [pltpu.SemaphoreType.DMA((3,))] * 4


def every(units, *steps):
    for step in steps:
        for unit in units:
            getattr(unit, step)()


class Closing:
    lines = 64

    def __init__(self, row, dp, units_ref, attn_ref, lines_ref, given, results, refs):
        self.row, self.lines_ref, self.dp = row, lines_ref, dp
        self.full, shard, small, above = results
        core_in, y_out, y_in = refs[:3]
        row_sems, refs = refs[3:7], refs[7:]
        mine, self.s_core, self.s_one, self.s_y, self.s_mine, s_slots = refs[:6]
        refs = refs[6:]
        self.mine = mine
        self.sums = RowSum(row, blocks(units_ref) + [attn_ref], core_in, y_out, y_in, blocks(mine), row_sems)
        self.gather = RowGather(
            row, [mine.at[k] for k in range(2)], blocks(self.full), row.place, row.place_across, refs[:6]
        )
        self.s_pair = to_row(lines_ref, self.s_core, refs[6:8], 0, row.sibling)
        self.s_cross = to_row(self.s_one, self.s_y, refs[8:10], 0, row.across)
        self.wide = WideSum(dp, [self.s_mine], [s_slots], [small], refs[10:14])
        refs = refs[14:]
        self.here = [HalvingSum(mine.at[k], shard.at[k], refs[9 * k : 9 * k + 9]) for k in range(3)]
        refs = refs[27:]
        self.above = [
            HalvingSum(given[k] if k else None, above.at[k], refs[9 * k : 9 * k + 9], None if k else given[0])
            for k in range(3)
        ]

    def enter(self):
        greet(self.dp, lax.axis_index("dp"), (self.row.sibling, self.row.across))
        for k in range(2):
            self.sums.start(k)
        every(self.above, "begin")

    def early(self):
        every(self.above[1:], "halve")
        every(self.above[:1], "quarter")

    def take(self, k):
        self.sums.end(k)
        self.here[k].begin()
        self.gather.start(k)
        self.full[k, self.row.place] = self.mine[k]
        if k == 0:
            every(self.above[:1], "eighth")
            every(self.above[1:], "quarter")
        else:
            every(self.above[:1], "widen")
            every(self.above[1:], "eighth")

    def open(self):
        self.sums.start(2)

    def cross(self):
        self.sums.middle(2)
        every(self.here[:2], "halve")
        every(self.above[1:], "widen")
        every(self.above[:1], "wider")
        self.gather.forward(0)

    def send_lines(self):
        self.s_pair.start()
        every(self.here[:2], "quarter")
        every(self.above[1:], "wider")
        self.s_pair.wait_recv()
        self.s_one[...] = self.lines_ref[...] + self.s_core[...]
        self.s_cross.start()

    def finish(self):
        attn = self.here[2:]
        self.sums.end(2)
        every(attn, "begin")
        self.s_cross.wait_recv()
        self.s_mine[...] = self.s_one[...] + self.s_y[...]
        self.wide.start(0)
        every(self.here[:2], "eighth")
        every(attn, "halve")
        self.gather.forward(1)
        self.wide.middle(0)
        every(attn, "quarter")
        every(self.here[:2], "widen")
        every(attn, "eighth")
        every(self.here[:2], "wider")
        every(attn, "widen", "wider")
        self.s_pair.wait_send()
        self.s_cross.wait_send()
        self.wide.finish(0)
        for k in range(3):
            self.sums.finish(k)
        every(self.above + self.here, "finish")
        for k in range(2):
            self.gather.arrive(k)
            self.gather.sent(k)

    @classmethod
    def scratch(cls, dp, width):
        lines = cls.lines
        flat = pltpu.VMEM((lines, width), f32)
        scratch = (
            RowSum.scratch(3, width)
            + [pltpu.VMEM((3, width, width), bf16), flat, flat, flat, flat, pltpu.VMEM((dp, lines // dp, width), f32)]
            + RowGather.scratch(2)
            + [pltpu.SemaphoreType.DMA((1,))] * 4
            + WideSum.semaphores(dp, 1)
        )
        for _ in range(6):
            scratch = scratch + HalvingSum.scratch(width)
        return scratch


def format_kernel(columns, *refs):
    count = (len(refs) - 6) // 2
    qkv_out, proj_out, core_up_out, core_down_out, up_out, down_out = refs[2 * count :]

    def form(full, shard):
        mp, width = full.shape[1], full.shape[2]
        rows = width // mp
        qkv_out[0] = shard[2, :columns].astype(f32)
        proj_out[0] = shard[2, columns:].astype(f32)
        core_up_out[0] = shard[0].astype(f32)
        for place in range(mp):
            q = quarter_at(place, mp)
            up_out[0, 0, :, q * width : (q + 1) * width] = full[0, place].astype(f32)
        for chunk in range(mp):
            at = slice(chunk * width, (chunk + 1) * width)
            core_down_out[0, :, at] = shard[1, chunk * rows : (chunk + 1) * rows].astype(f32)
            block = [None] * mp
            for place in range(mp):
                block[quarter_at(place, mp)] = full[1, place, chunk * rows : (chunk + 1) * rows]
            down_out[0, 0, at, :] = turn_blocks(jnp.concatenate(block, 0))

    for layer in range(count):
        pl.when(pl.program_id(0) == layer)(functools.partial(form, refs[layer], refs[count + layer]))


def format_call(fulls, shards, columns):
    layers = len(fulls)
    _, mp, width, _ = fulls[0].shape
    hidden = mp * width
    shapes = [
        (layers, columns, width),
        (layers, width - columns, width),
        (layers, width, width),
        (layers, width // mp, hidden),
        (layers, 1, width, hidden),
        (layers, 1, hidden, width),
    ]
    return pl.pallas_call(
        functools.partial(format_kernel, columns),
        grid=(layers,),
        out_shape=[jax.ShapeDtypeStruct(shape, f32) for shape in shapes],
        in_specs=[whole_spec(a.shape) for a in (*fulls, *shards)],
        out_specs=[image_spec(shape, 1) for shape in shapes],
        compiler_params=pltpu.CompilerParams(vmem_limit_bytes=56 * MIB),
        name="format",
    )(*fulls, *shards)


def greet(dp, me, rows=()):
    barrier = pltpu.get_barrier_semaphore()
    for row in rows:
        pl.semaphore_signal(barrier, inc=1, device_id={"mp": row}, device_id_type=MESH)

    def signal(off, carry):
        pl.semaphore_signal(barrier, inc=1, device_id={"dp": lax.rem(me + off, dp)}, device_id_type=MESH)
        return carry

    lax.fori_loop(1, dp, signal, 0)
    pl.semaphore_wait(barrier, dp - 1 + len(rows))


def partner_of(me, p, dp):
    out, bit = 0, 1
    while bit < dp:
        one, two = lax.rem(lax.div(me, bit), 2), lax.rem(lax.div(p, bit), 2)
        out = out + bit * (one + two - 2 * one * two)
        bit *= 2
    return out


def to_peer(source, target, send_sem, recv_sem, peer):
    return pltpu.make_async_remote_copy(
        src_ref=source,
        dst_ref=target,
        send_sem=send_sem,
        recv_sem=recv_sem,
        device_id={"dp": peer},
        device_id_type=MESH,
    )


def gelu_parts(h):
    root = np.float32(np.sqrt(2.0 / np.pi))
    square = h * h
    t = jnp.tanh(root * h * (1.0 + 0.044715 * square))
    half = 0.5 * (1.0 + t)
    slope = half + 0.5 * h * (1.0 - t * t) * root * (1.0 + 3 * 0.044715 * square)
    return h * half, slope


def expert_forward_kernel(dp, mp, layer, gather, *refs):
    refs = list(refs)
    buffer_ref, up_any, down_any, rup_any, rdown_any = refs[:5]
    refs = refs[5:]
    if gather:
        shards = [ref.at[layer + 1] for ref in refs[:4]]
        refs = refs[4:]
    recv_ref, returned_ref, up_eff, down_eff = refs[:4]
    refs = refs[4:]
    if gather:
        fulls = refs[:4]
        refs = refs[4:]
    part, core, up_ref, down_ref, rup_ref, rdown_ref, local = refs[:7]
    refs = refs[7:]
    moving = WeightGather(shards, fulls, refs[:7]) if gather else None
    send_one, recv_one, send_two, recv_two = refs[-4:]
    split = dp // EXPERTS
    me = lax.axis_index("dp")
    loads = [
        pltpu.make_async_copy(source, target, local.at[k])
        for k, (source, target) in enumerate(
            [
                (up_any, up_ref),
                (rup_any.at[layer, 0], rup_ref),
                (down_any, down_ref),
                (rdown_any.at[layer, 0], rdown_ref),
            ]
        )
    ]
    for load in loads:
        load.start()
    greet(dp, me, (moving.row.sibling, moving.row.across) if gather else ())

    def first(off):
        peer = partner_of(me, off, dp)
        return to_peer(
            buffer_ref.at[lax.div(peer, split)], recv_ref.at[me], send_one.at[off], recv_one.at[off], peer
        )

    def second(off):
        source = partner_of(me, off, dp)
        return to_peer(part.at[source], returned_ref.at[me], send_two.at[off], recv_two.at[off], source)

    def start_first(off, carry):
        first(dp - off).start()
        return carry

    lax.fori_loop(1, dp, start_first, 0)
    if gather:
        for k in range(4):
            moving.start(k)
    recv_ref[me] = buffer_ref[lax.div(me, split)]
    hidden = up_eff.shape[1]
    columns = up_ref.shape[-1]
    loads[0].wait()
    loads[1].wait()
    if split == 1 and columns % LANES == 0:
        for m in range(mp):
            at = slice(m * columns, (m + 1) * columns)
            up_eff[:, at] = (up_ref[m].astype(f32) + rup_ref[:, at].astype(f32)).astype(bf16)
    else:
        core[...] = rup_ref[...].astype(f32)
        begin = lax.rem(me, split) * hidden
        for m in range(mp):
            put = onehot(iota((columns, hidden), 0) + m * columns == iota((columns, hidden), 1) + begin)
            core[...] += nn(up_ref[m], put)
        up_eff[...] = core[...].astype(bf16)
    begin = pl.multiple_of(lax.rem(me, split) * hidden, LANES)
    loads[2].wait()
    loads[3].wait()
    core_part = down_ref[:, :, pl.ds(begin, hidden)].reshape(down_eff.shape[1], hidden)
    down_eff[...] = (turn_blocks(core_part) + rdown_ref[...].astype(f32)).astype(bf16)

    def work(source):
        hidden_pre = nn(recv_ref[source], up_eff[...])
        hidden_low = gelu_parts(hidden_pre)[0].astype(bf16)
        return nn(hidden_low, down_eff[...]).astype(bf16)

    returned_ref[me] = work(me)

    def step(off, carry):
        source = partner_of(me, off, dp)
        first(off).wait_recv()
        part[source] = work(source)
        second(off).start()
        return carry

    lax.fori_loop(1, dp, step, 0)
    if gather:
        for k in range(4):
            moving.forward(k)

    def finish(off, carry):
        first(off).wait_send()
        second(off).wait()
        return carry

    lax.fori_loop(1, dp, finish, 0)
    if gather:
        for k in range(4):
            moving.arrive(k)
            moving.sent(k)


def expert_backward_kernel(dp, mp, fast, reduce, *refs):
    refs = list(refs)
    buffer_ref, recv_ref, up_ref, down_ref = refs[:4]
    refs = refs[4:]
    if reduce:
        given_ref, attn_ref = refs[:2]
        refs = refs[2:]
    returned_ref = refs.pop(0)
    if fast:
        units_ref = refs.pop(0)
    else:
        up_term, down_term = refs[:2]
        refs = refs[2:]
    if reduce:
        full_ref, mine_ref = refs[:2]
        refs = refs[2:]
    grads, hidden_low, slope, pre, part = refs[:5]
    refs = refs[5:]
    if fast:
        up_term, down_term = refs[:2]
        refs = refs[2:]
    row = Row() if reduce else None
    if reduce:
        core_in, y_out, y_in = refs[:3]
        sums = RowSum(row, [attn_ref], core_in, y_out, y_in, [mine_ref], refs[3:7])
        gather = RowGather(
            row, [given_ref.at[k] for k in range(2)], [full_ref.at[k] for k in range(2)], row.place, row.place_across,
            refs[7:13],
        )
        refs = refs[13:]
    send_one, recv_one, send_two, recv_two = refs
    split = dp // EXPERTS
    me = lax.axis_index("dp")
    greet(dp, me, (row.sibling, row.across) if reduce else ())

    def first(off):
        peer = partner_of(me, off, dp)
        return to_peer(buffer_ref.at[lax.div(peer, split)], grads.at[me], send_one.at[off], recv_one.at[off], peer)

    def second(off):
        source = partner_of(me, off, dp)
        return to_peer(part.at[source], returned_ref.at[me], send_two.at[off], recv_two.at[off], source)

    def start_first(off, carry):
        first(dp - off).start()
        return carry

    lax.fori_loop(1, dp, start_first, 0)
    if reduce:
        sums.start(0)
        for k in range(2):
            gather.start(k)
    grads[me] = buffer_ref[lax.div(me, split)]

    def again(source, carry):
        value, rate = gelu_parts(nn(recv_ref[source], up_ref[...]))
        hidden_low[source] = value.astype(bf16)
        slope[source] = rate
        return carry

    lax.fori_loop(0, dp, again, 0)
    if reduce:
        sums.middle(0)
        for k in range(2):
            full_ref[k, row.place] = given_ref[k]

    def work(source):
        hidden_grad = nt(grads[source], down_ref[...])
        pre_grad = (slope[source] * hidden_grad).astype(bf16)
        pre[source] = pre_grad
        return nt(pre_grad, up_ref[...]).astype(bf16)

    returned_ref[me] = work(me)

    def step(off, carry):
        source = partner_of(me, off, dp)
        first(off).wait_recv()
        part[source] = work(source)
        second(off).start()
        return carry

    lax.fori_loop(1, dp, step, 0)
    if reduce:
        for k in range(2):
            gather.forward(k)
        sums.end(0)
    up_term[...] = jnp.zeros(up_term.shape, f32)
    down_term[...] = jnp.zeros(down_term.shape, f32)

    def terms(block, carry):
        up_term[...] += tn(recv_ref[block], pre[block])
        down_term[...] += tn(grads[block], hidden_low[block])
        return carry

    lax.fori_loop(0, dp, terms, 0)
    if fast:
        width = up_term.shape[0]
        height = width // mp
        for place in range(mp):
            q = quarter_at(place, mp)
            units_ref[0, place] = up_term[:, q * width : (q + 1) * width].astype(bf16)
            for chunk in range(mp):
                block = down_term[q * height : (q + 1) * height, chunk * width : (chunk + 1) * width]
                units_ref[1, place, chunk * height : (chunk + 1) * height] = block.astype(bf16)

    def finish(off, carry):
        first(off).wait_send()
        second(off).wait()
        return carry

    lax.fori_loop(1, dp, finish, 0)
    if reduce:
        sums.finish(0)
        for k in range(2):
            gather.arrive(k)
            gather.sent(k)


def expert_call(kernel, arrays, outs, scratch, dp, collective_id, name, flops, anys=(), any_outs=()):
    sems = [pltpu.SemaphoreType.DMA((dp,))] * 4
    vmem, anywhere = pl.BlockSpec(memory_space=pltpu.VMEM), pl.BlockSpec(memory_space=pl.ANY)
    return pl.pallas_call(
        kernel,
        out_shape=[jax.ShapeDtypeStruct(shape, dtype) for shape, dtype in (*outs, *any_outs)],
        in_specs=[vmem] * len(arrays) + [anywhere] * len(anys),
        out_specs=[vmem] * len(outs) + [anywhere] * len(any_outs),
        scratch_shapes=scratch + sems,
        compiler_params=pltpu.CompilerParams(
            vmem_limit_bytes=56 * MIB, collective_id=collective_id, has_side_effects=True
        ),
        cost_estimate=pl.CostEstimate(flops=flops, bytes_accessed=20 * MIB, transcendentals=0),
        name=name,
    )(*arrays, *anys)


def by_windows(grid):
    images, kinds = grid.shape[:2]
    blocks = GRID // WINDOW
    grid = grid.reshape(images, kinds, blocks, WINDOW, blocks, WINDOW).transpose(0, 1, 2, 4, 3, 5)
    grid = grid.reshape(images, kinds, blocks * blocks, WINPOS)
    grid = jnp.pad(grid, ((0, 0), (0, 0), (0, 0), (0, WPAD - WINPOS)), constant_values=-1)
    return grid.reshape(images, kinds, IMGROWS)


def per_device(
    patches,
    qkv_weight,
    proj_weight,
    core_up,
    core_down,
    residual_up,
    residual_down,
    position_bias,
    router_weight,
    norm_gain,
    norm_bias,
    cotangent,
    image_valid,
    expert_index,
    slot_index,
    region_id,
):
    dp, mp = lax.axis_size("dp"), lax.axis_size("mp")
    images, _, width = patches.shape
    split = dp // EXPERTS
    hidden = residual_up.shape[-1]
    hidden_full = core_up.shape[-1] * mp
    row_index = lax.axis_index("mp")

    fast = split == 1 and dp == 8 and mp == 4 and hidden == mp * width
    qkv_rows, proj_rows, down_rows = (a.transpose(0, 2, 1) for a in (qkv_weight, proj_weight, core_down))
    shards = (qkv_rows, proj_rows, core_up, down_rows)
    gathered = [[None] * len(shards)] * LAYERS
    if not fast:
        gathered = [[lax.all_gather(a[l], "mp", axis=0, tiled=False) for a in shards] for l in range(LAYERS)]

    position = jnp.where(slot_index >= 0, expert_index * SLOTS + slot_index, -1)
    row_form = by_windows(jnp.stack([position.reshape(images, GRID, GRID), region_id], 1))
    col_form = row_form.transpose(0, 2, 1)
    enter = jnp.asarray(enter_table(), bf16)
    leave = jnp.asarray(enter_table().T, bf16)
    moves = [jnp.asarray(move_table(l % 2 == 1), bf16) for l in range(LAYERS)]
    backs = [jnp.asarray(move_table(l % 2 == 1).T, bf16) for l in range(LAYERS)]
    table_rows = position_bias.transpose(0, 2, 1).reshape(LAYERS * HEADS, OFFSETS)
    table_rows = jnp.pad(table_rows, ((0, 0), (0, TABLE - OFFSETS)))
    entry_row, entry_col = jnp.asarray(cell_entries()[None, :]), jnp.asarray(cell_entries()[:, None])
    routers = jnp.pad(router_weight.transpose(0, 2, 1), ((0, 0), (0, LANES - EXPERTS), (0, 0)))

    token = (images, IMGROWS, width)
    buffer_shape = (ROWS, width)
    block_rows = (dp, SLOTS, width)
    pieces = (split, ROWS, width)

    def by_piece(returned):
        return returned.reshape(EXPERTS, split, SLOTS, width).transpose(1, 0, 2, 3).reshape(pieces)

    records = []
    before = None
    for l in range(LAYERS):
        first = l == 0
        gather = fast and first
        if first:
            arrays = [("image", patches), ("whole", enter)]
        else:
            arrays = [("image", before[0]), ("image", before[1]), ("whole", before[2])]
        arrays += [
            ("smem", image_valid),
            ("image", col_form),
            ("image", row_form),
            ("any", qkv_rows) if gather else ("whole", gathered[l][0]),
            ("any", proj_rows) if gather else ("whole", gathered[l][1]),
            ("whole", table_rows) if first else (l, biases),
            ("whole", moves[l]),
            ("whole", backs[l]),
            (l, norm_gain),
            (l, norm_bias),
            (l, routers),
        ]
        if first:
            arrays.append(("whole", entry_row))
        if gather:
            arrays += [("any", core_up), ("any", down_rows)]
        outs = [("image", token, f32)]
        if first:
            outs.append(("whole", (LAYERS, HEADS, WPAD, LANES), f32))
        else:
            outs.append(("image", token, f32))
        outs += [
            ("image", token, f32),
            ("image", token, bf16),
            ("image", (images, IMGROWS, 1), f32),
            ("whole", buffer_shape, bf16),
            ("image", token, bf16),
            ("image", (images, 2 * width, IMGROWS), bf16),
            ("image", token, bf16),
            ("image", (images, PAIRS * HEADS, WPAD, LANES), bf16),
            ("image", (images, width, IMGROWS), bf16),
            ("whole", (width, width), bf16),
        ]
        scratch = [pltpu.VMEM(buffer_shape, f32)]
        gathered_shapes = [(mp, *a.shape[1:]) for a in shards]
        if gather:
            outs.append(("whole", (3 * width, width), bf16))
            outs += [("any", shape, bf16) for shape in gathered_shapes[2:]]
            scratch += [pltpu.VMEM(shape, bf16) for shape in gathered_shapes[:2]] + WeightGather.scratch(4)
        results = list(
            image_call(
                functools.partial(attention_forward_kernel, first, l % 2 == 1, mp, gather),
                images, arrays, outs, scratch, f"attend_{l}", 3 * LAYERS + 1 if gather else None,
            )
        )
        if gather:
            gathered[l] = [results[-3], None] + results[-2:]
            results = results[:-3]
        carried = results.pop(0)
        if first:
            biases = results.pop(0)
        else:
            records[-1]["expert_out"] = results.pop(0)
        middle, second_low, gate, buffer = results[:4]
        gather = fast and l < LAYERS - 1
        received, returned, up_eff, down_eff, *more = expert_call(
            functools.partial(expert_forward_kernel, dp, mp, l, gather),
            [buffer.reshape(EXPERTS, SLOTS, width)],
            [
                (block_rows, bf16),
                (block_rows, bf16),
                ((width, hidden), bf16),
                ((hidden, width), bf16),
            ],
            [
                pltpu.VMEM(block_rows, bf16),
                pltpu.VMEM((8, LANES) if fast else (width, hidden), f32),
                pltpu.VMEM(gathered_shapes[2], bf16),
                pltpu.VMEM(gathered_shapes[3], bf16),
                pltpu.VMEM((width, hidden), bf16),
                pltpu.VMEM((hidden, width), bf16),
                pltpu.SemaphoreType.DMA((4,)),
            ]
            + (WeightGather.scratch(4) if gather else []),
            dp, l, f"experts_{l}", 4 * dp * SLOTS * width * hidden,
            [gathered[l][2], gathered[l][3], residual_up, residual_down, *(shards if gather else ())],
            [(shape, bf16) for shape in gathered_shapes] if gather else (),
        )
        if gather:
            gathered[l + 1] = more
        returned = by_piece(returned)
        before = (middle, gate, returned)
        records.append(
            dict(
                carried=carried, middle=middle, second_low=second_low, gate=gate, saved=results[4:], received=received,
                up_eff=up_eff, down_eff=down_eff,
            )
        )

    top = records[-1]
    block_output, grad, logit_grad, router_part, buffer = image_call(
        turn_kernel,
        images,
        [
            ("image", before[0]),
            ("image", before[1]),
            ("whole", before[2]),
            ("image", cotangent),
            ("whole", enter),
            ("whole", leave),
            ("image", col_form),
            ("image", row_form),
            ("image", top["second_low"]),
            (LAYERS - 1, routers),
        ],
        [
            ("image", patches.shape, bf16),
            ("image", token, f32),
            ("image", (images, IMGROWS, LANES), f32),
            ("whole", (LANES, width), f32),
            ("whole", buffer_shape, bf16),
        ],
        [pltpu.VMEM(buffer_shape, f32)],
        "turn",
    )
    router_parts, tables, smalls = [None] * LAYERS, [None] * LAYERS, [None] * LAYERS
    residual_sums, shard_sums = [None] * LAYERS, [None] * LAYERS
    router_parts[LAYERS - 1] = router_part
    units, attn_units, mines = [None] * LAYERS, [None] * LAYERS, [None] * LAYERS
    for l in reversed(range(LAYERS)):
        rec = records[l]
        last = l == 0
        reduce = fast and l < LAYERS - 1
        arrays = [buffer.reshape(EXPERTS, SLOTS, width), rec["received"], rec["up_eff"], rec["down_eff"]]
        outs = [(block_rows, bf16)]
        scratch = [
            pltpu.VMEM(block_rows, bf16),
            pltpu.VMEM((dp, SLOTS, hidden), bf16),
            pltpu.VMEM((dp, SLOTS, hidden), f32),
            pltpu.VMEM((dp, SLOTS, hidden), bf16),
            pltpu.VMEM(block_rows, bf16),
        ]
        if fast:
            outs.append(((2, mp, width, width), bf16))
            scratch += [pltpu.VMEM((width, hidden), f32)] * 2
        else:
            outs += [((width, hidden), f32)] * 2
        if reduce:
            arrays += [mines[l + 1], attn_units[l + 1]]
            outs += [((2, mp, width, width), bf16), ((width, width), bf16)]
            scratch += RowSum.scratch(1, width) + RowGather.scratch(2)
        results = list(
            expert_call(
                functools.partial(expert_backward_kernel, dp, mp, fast, reduce), arrays, outs, scratch, dp, LAYERS + l,
                f"experts_back_{l}", 10 * dp * SLOTS * width * hidden,
            )
        )
        returned_grad = results.pop(0)
        if fast:
            units[l] = results.pop(0)
        else:
            residual_sums[l] = lax.psum(tuple(t.astype(bf16) for t in results[:2]), "mp")
        if reduce:
            full_above, mine_above = results
        window_in, qk, v, probs, att, proj_full = rec["saved"]
        qkv_full = gathered[l][0].reshape(3 * width, width)
        arrays = [
            ("smem", image_valid),
            ("image", grad),
            ("whole", by_piece(returned_grad)),
            ("image", logit_grad),
            ("image", rec["middle"]),
            ("image", rec["carried"]),
            (l, routers),
            ("image", col_form),
            ("whole", moves[l]),
            ("whole", backs[l]),
            (l, norm_gain),
            ("whole", proj_full),
            ("whole", qkv_full),
            ("image", window_in),
            ("image", qk),
            ("image", v),
            ("image", probs),
            ("image", att),
        ]
        outs = [("image", patches.shape if last else token, f32)]
        scratch = [pltpu.VMEM((3 * width, (2 - images % 2) * IMGROWS), bf16)]
        closes = fast and last
        table_shape, small_shape = (HEADS, WPAD, LANES), (8, width)
        if fast:
            arrays.append(("whole", units[l]))
            scratch += [pltpu.VMEM((3 * width, width), f32), pltpu.VMEM((width, width), f32)]
        if closes:
            outs += [
                ("whole", (2, mp, width, width), bf16),
                ("whole", (3, width, width), bf16),
                ("whole", (Closing.lines, width), f32),
                ("whole", (3, width, width), bf16),
            ]
        else:
            if fast:
                outs += [
                    ("whole", (width // 2, width), bf16),
                    ("whole", (mp, width, width), bf16),
                    ("whole", (2, width, width), bf16),
                ]
            else:
                outs += [("whole", (3 * width, width), f32), ("whole", (width, width), f32)]
            outs += [("whole", table_shape, f32), ("whole", small_shape, f32)]
        if last:
            arrays.append(("whole", leave))
            if fast:
                arrays += [
                    ("whole", a)
                    for a in (
                        tables[1], smalls[1], router_parts[1], router_parts[0], entry_col, halves_above, mines[1],
                        mine_above,
                    )
                ]
        else:
            below = records[l - 1]
            arrays += [
                ("image", row_form),
                ("image", below["expert_out"]),
                ("image", below["second_low"]),
                (l - 1, routers),
            ]
            outs += [
                ("image", (images, IMGROWS, LANES), f32),
                ("whole", (LANES, width), f32),
                ("whole", buffer_shape, bf16),
            ]
            scratch.append(pltpu.VMEM(buffer_shape, f32))
        if closes:
            scratch += [
                pltpu.VMEM(table_shape, f32),
                pltpu.VMEM(small_shape, f32),
                pltpu.VMEM((mp, width, width), bf16),
                pltpu.VMEM((Closing.lines, width), f32),
            ]
            scratch += [pltpu.VMEM(shape, dtype) for _, shape, dtype in outs[1:5]] + Closing.scratch(dp, width)
        elif fast:
            scratch += RowSum.scratch(2, width) + [pltpu.VMEM((width // 2, width), bf16)]
            scratch += [pltpu.SemaphoreType.DMA((1,))] * 2
        results = list(
            image_call(
                functools.partial(attention_backward_kernel, last, dp, mp, fast),
                images, arrays, outs, scratch, f"attend_back_{l}", 2 * LAYERS + 1 + l if fast else None,
            )
        )
        grad = results.pop(0)
        if closes:
            full, closed, lines, shard_above = results
            continue
        if fast:
            halves_above = results.pop(0)
            attn_units[l], mines[l] = results[:2]
        else:
            qkv_part, proj_part = results[:2]
        tables[l], smalls[l] = results[2:4]
        if not last:
            logit_grad, router_parts[l - 1], buffer = results[4:]
        if fast:
            continue
        attn = (
            lax.psum_scatter(qkv_part.astype(bf16), "mp", scatter_dimension=0, tiled=True),
            lax.psum_scatter(proj_part.T.astype(bf16), "mp", scatter_dimension=0, tiled=True),
        )
        up_sum, down_sum = residual_sums[l]
        if split > 1:
            begin = lax.axis_index("dp") % split * hidden
            empty = jnp.zeros((width, hidden_full), bf16)
            up_sum = lax.dynamic_update_slice_in_dim(empty, up_sum, begin, 1)
            down_sum = lax.dynamic_update_slice_in_dim(empty, down_sum, begin, 1)
        up_columns, down_columns = core_up.shape[-1], core_down.shape[-1]
        up_shard = lax.dynamic_slice_in_dim(up_sum, row_index * up_columns, up_columns, 1)
        down_shard = lax.dynamic_slice_in_dim(down_sum, row_index * down_columns, down_columns, 0)
        shard_sums[l] = lax.psum((attn[0], attn[1], up_shard, down_shard), "dp")

    if fast:
        *attn_grads, core_up_grad, core_down_grad, residual_up_grad, residual_down_grad = format_call(
            [full, full_above], [closed, shard_above], qkv_weight.shape[-1]
        )
        attn_grads = [a.transpose(0, 2, 1) for a in attn_grads]
        core_grads = (core_up_grad, core_down_grad.transpose(0, 2, 1))
        at = LAYERS * HEADS
        table_sum = lines[:at, :OFFSETS]
        router_sum = lines[at : at + LAYERS * EXPERTS].reshape(LAYERS, EXPERTS, width)
        at += LAYERS * EXPERTS
        small_sum = lines[at : at + LAYERS * 8].reshape(LAYERS, 8, width)[:, :4]
    else:
        entry = cell_entries()[None, :] + np.array([key_base_of(key) for key in range(WPAD)])[:, None]
        entry = jnp.asarray(np.where(np.arange(WPAD)[:, None] < WINPOS, entry, -1).reshape(-1))
        entry_turned = (entry[:, None] == jnp.arange(OFFSETS)[None, :]).astype(f32)
        table_part = jnp.dot(
            jnp.stack(tables, 0).reshape(LAYERS * HEADS, WPAD * LANES), entry_turned, precision=highest
        )
        small_part = jnp.stack(smalls, 0)[:, :4]
        router_part = jnp.stack(router_parts, 0)[:, :EXPERTS]
        table_sum, small_sum, router_sum = lax.psum((table_part, small_part, router_part), ("dp", "mp"))

        def shard(k):
            return jnp.stack([shard_sums[l][k] for l in range(LAYERS)], 0).astype(f32)

        attn_grads = (shard(0).transpose(0, 2, 1), shard(1).transpose(0, 2, 1))
        core_grads = (shard(2), shard(3).transpose(0, 2, 1))
        residual_up_grad, residual_down_grad = (
            jnp.stack([residual_sums[l][k] for l in range(LAYERS)], 0).astype(f32) for k in range(2)
        )
        residual_up_grad = residual_up_grad[:, None]
        residual_down_grad = residual_down_grad.transpose(0, 2, 1)[:, None]

    return (
        block_output,
        grad,
        attn_grads[0],
        attn_grads[1],
        core_grads[0],
        core_grads[1],
        residual_up_grad,
        residual_down_grad,
        table_sum.reshape(LAYERS, HEADS, OFFSETS).transpose(0, 2, 1),
        router_sum.transpose(0, 2, 1),
        small_sum[:, 0:2],
        small_sum[:, 2:4],
    )


def solution(mesh):
    placed = (
        P(("dp", "mp"), None, None),
        P(None, None, "mp"),
        P(None, None, "mp"),
        P(None, None, "mp"),
        P(None, None, "mp"),
        P(None, "dp", None, None),
        P(None, "dp", None, None),
        P(),
        P(),
        P(),
        P(),
        P(("dp", "mp"), None, None),
        P(("dp", "mp")),
        P(("dp", "mp"), None),
        P(("dp", "mp"), None),
        P(("dp", "mp"), None, None),
    )
    return jax.shard_map(
        per_device,
        mesh=mesh,
        in_specs=placed,
        out_specs=(
            P(("dp", "mp"), None, None),
            P(("dp", "mp"), None, None),
            P(None, None, "mp"),
            P(None, None, "mp"),
            P(None, None, "mp"),
            P(None, None, "mp"),
            P(None, "dp", None, None),
            P(None, "dp", None, None),
            P(),
            P(),
            P(),
            P(),
        ),
        check_vma=False,
    )
```

```python
import functools

import jax
import jax.numpy as jnp
import numpy as np
from jax import lax
from jax.experimental import pallas as pl
from jax.experimental.pallas import tpu as pltpu
from jax.sharding import PartitionSpec as P

HEADS = 12
HEAD_DIM = 32
EXPERTS = 8
WINDOW = 7
GRID = 14
SHIFT = 3
LAYERS = 2
WINPOS = 49
OFFSETS = 169
CAP = 122

WPAD = 64
IMGROWS = 256
PATCHES = 196
SLOTS = 128
ROWS = EXPERTS * SLOTS
LANES = 128
GROUP = 4
PAIRS = 2
TABLE = 256

bf16 = jnp.bfloat16
f32 = jnp.float32
highest = lax.Precision.HIGHEST
norm_epsilon = 1e-05
mask_fill = -100.0
head_scale = HEAD_DIM ** (-0.5)
MESH = pl.DeviceIdType.MESH
MIB = 1024 * 1024


def nn(a, b):
    return lax.dot_general(a, b, (((1,), (0,)), ((), ())), preferred_element_type=f32)


def nt(a, b):
    return lax.dot_general(a, b, (((1,), (1,)), ((), ())), preferred_element_type=f32)


def tn(a, b):
    return lax.dot_general(a, b, (((0,), (0,)), ((), ())), preferred_element_type=f32)


def iota(shape, dim):
    return lax.broadcasted_iota(jnp.int32, shape, dim)


def onehot(flags):
    return jnp.where(flags, 1.0, 0.0).astype(bf16)


def natural_of_row(shifted):
    moved = SHIFT if shifted else 0
    blocks = GRID // WINDOW
    out = -np.ones(IMGROWS, np.int32)
    for window in range(blocks * blocks):
        for cell in range(WINPOS):
            row = (window // blocks * WINDOW + cell // WINDOW + moved) % GRID
            col = (window % blocks * WINDOW + cell % WINDOW + moved) % GRID
            out[window * WPAD + cell] = row * GRID + col
    return out


def key_base_of(key):
    return (2 * WINDOW) * (WINDOW - 1) - (key // WINDOW * (2 * WINDOW - 1) + key % WINDOW)


def enter_table():
    held = natural_of_row(False)
    return (held[:, None] == np.arange(PATCHES)[None, :]).astype(np.float32)


def move_table(shifted):
    first, second = natural_of_row(False), natural_of_row(shifted)
    same = (second[:, None] == first[None, :]) & (second[:, None] >= 0)
    return same.astype(np.float32)


def cell_entries():
    cell = np.arange(LANES) % WPAD
    return np.where(cell < WINPOS, cell // WINDOW * (2 * WINDOW - 1) + cell % WINDOW, -4 * TABLE).astype(np.int32)


def norm_parts(x):
    width = x.shape[-1]
    center = x - jnp.sum(x, -1, keepdims=True) * (1.0 / width)
    spread = jnp.sum(center * center, -1, keepdims=True) * (1.0 / width)
    rstd = lax.rsqrt(spread + norm_epsilon)
    return center * rstd, rstd


def norm_back(grad, gain, xhat, rstd):
    width = xhat.shape[-1]
    dxhat = grad * gain
    mean_one = jnp.sum(dxhat, -1, keepdims=True) * (1.0 / width)
    mean_two = jnp.sum(dxhat * xhat, -1, keepdims=True) * (1.0 / width)
    return rstd * (dxhat - mean_one - xhat * mean_two)


def turn_blocks(x):
    size = x.shape[0]
    same = onehot(iota((size, size), 0) == iota((size, size), 1))
    return jnp.concatenate([nt(same, x[:, at : at + size]) for at in range(0, x.shape[1], size)], 0)


def split_two(x):
    high = x.astype(bf16)
    return high, (x - high.astype(f32)).astype(bf16)


def collect(pos_col, returned_ref):
    pick = onehot(pos_col == iota((pos_col.shape[0], ROWS), 1))
    out = nn(pick, returned_ref[0])
    for piece in range(1, returned_ref.shape[0]):
        out = out + nn(pick, returned_ref[piece])
    return out


def join(ref):
    return ref[...].reshape(ref.shape[0] * ref.shape[1], *ref.shape[2:])


def store(ref, rows):
    ref[...] = rows.reshape(ref.shape).astype(ref.dtype)


def per_image(function, count):
    return jnp.concatenate([function(i) for i in range(count)], 0)


def image_rows(i):
    return slice(i * IMGROWS, (i + 1) * IMGROWS)


def lay_positions(row_ref):
    return jnp.concatenate([row_ref[i, 0:1, :] for i in range(row_ref.shape[0])], 1)


def spread_rows(pos_row, rows_low):
    return nn(onehot(iota((ROWS, pos_row.shape[1]), 0) == pos_row), rows_low)


def route(second_low, router, pos_col):
    logits = nt(second_low, router)
    lane = iota(logits.shape, 1)
    logits = jnp.where(lane < EXPERTS, logits, -1e30)
    expo = jnp.exp(logits - jnp.max(logits, -1, keepdims=True))
    probs = expo / jnp.sum(expo, -1, keepdims=True)
    expert = jnp.where(pos_col >= 0, pos_col // SLOTS, -1)
    chosen = jnp.where(lane == expert, 1.0, 0.0)
    return probs, chosen, jnp.sum(probs * chosen, -1, keepdims=True)


def head_masks():
    rows = iota((LANES, LANES), 0) // HEAD_DIM
    return [onehot(rows == h) for h in range(GROUP)]


def lane_masks():
    lane = iota((WPAD, LANES), 1)
    return [onehot(lane < WPAD), onehot(lane >= WPAD)]


def keys_entry(cells, key_row, turned):
    parts = [cells + (key_base_of(col) - key_row * (2 * WINDOW - 1)) for col in range(WINDOW)]
    return jnp.concatenate(parts, 0 if turned else 1)


def form_bias(bias_ref, table_ref, entry_row):
    layers, heads = bias_ref.shape[:2]
    lines = layers * heads
    bias_ref[...] = jnp.where(iota(bias_ref.shape, 2) < WINPOS, 0.0, -1e30)
    table = table_ref[...]
    high = table.astype(bf16)
    mid, low = split_two(table - high.astype(f32))
    parts = jnp.concatenate([high.astype(f32), mid.astype(f32), low.astype(f32)], 0).astype(bf16)

    def step(key_row, carry):
        pick = onehot(iota((TABLE, WINDOW * LANES), 0) == keys_entry(entry_row, key_row, False))
        rows = nn(parts, pick)
        rows = rows[:lines] + rows[lines : 2 * lines] + rows[2 * lines :]
        for col in range(WINDOW):
            for layer in range(layers):
                part = rows[layer * heads : (layer + 1) * heads, col * LANES : (col + 1) * LANES]
                bias_ref[layer, :, pl.ds(key_row * WINDOW + col, 1), :] = part.reshape(heads, 1, LANES)
        return carry

    lax.fori_loop(0, WINDOW, step, 0)


def table_grad(parts, entry_col):
    heads = parts[0].shape[0]
    lines = heads * len(parts)

    def step(key_row, total):
        keys = [
            jnp.concatenate([ref[:, pl.ds(key_row * WINDOW + col, 1), :].reshape(heads, LANES) for ref in parts], 0)
            for col in range(WINDOW)
        ]
        rows = jnp.concatenate(keys, 1)
        high = rows.astype(bf16).astype(f32)
        both = jnp.concatenate([high, rows - high], 0).astype(bf16)
        entry = keys_entry(entry_col, key_row, True)
        out = nn(both, onehot(iota((WINDOW * LANES, TABLE), 1) == entry))
        return total + out[:lines] + out[lines:]

    return lax.fori_loop(0, WINDOW, step, jnp.zeros((lines, TABLE), f32))


def attention_forward_kernel(first, shifted, mp, gather, *refs):
    refs = list(refs)
    if first:
        patches_ref, enter_ref = refs[:2]
        refs = refs[2:]
    else:
        prev_ref, prev_gate_ref, returned_ref = refs[:3]
        refs = refs[3:]
    (
        valid_ref, col_ref, row_ref, qkv_ref, proj_ref, bias_ref, move_ref, back_ref, gain_ref, nbias_ref, router_ref,
    ) = refs[:11]
    gain_ref, nbias_ref, router_ref = (ref.at[0] for ref in (gain_ref, nbias_ref, router_ref))
    refs = refs[11:]
    if first:
        table_ref, entry_ref = bias_ref, refs.pop(0)
    if gather:
        core_up_ref, core_down_ref = refs[:2]
        refs = refs[2:]
    carried_ref = refs.pop(0)
    if first:
        biases_ref = refs.pop(0)
        bias_ref = biases_ref.at[0]
    else:
        expert_out_ref = refs.pop(0)
        bias_ref = bias_ref.at[0]
    middle_ref, second_ref, gate_ref, buffer_ref, window_ref, qk_ref, v_ref, probs_ref, att_ref, proj_full = refs[:10]
    refs = refs[10:]
    if gather:
        qkv_full = refs.pop(0)
        up_out, down_out = refs[:2]
        refs = refs[2:]
    total_ref = refs.pop(0)
    step = pl.program_id(0)
    final = pl.num_programs(0) - 1
    count, _, width = carried_ref.shape
    if gather:
        shards = [ref.at[0] for ref in (qkv_ref, proj_ref, core_up_ref, core_down_ref)]
        qkv_ref, proj_ref = refs[:2]
        moving = WeightGather(shards, [qkv_ref, proj_ref, up_out, down_out], refs[2:])

        @pl.when(step == 0)
        def _():
            pl.semaphore_wait(moving.row.greet(), 2)
            for k in (0, 1):
                moving.start(k)
            form_bias(biases_ref, table_ref, entry_ref[...])

    pos_col = join(col_ref)[:, 0:1]
    if first:
        x = per_image(lambda i: nn(enter_ref[...], patches_ref[i]), count)
    else:
        expert_out = collect(pos_col, returned_ref)
        store(expert_out_ref, expert_out)
        x = join(prev_ref) + join(prev_gate_ref) * expert_out
    store(carried_ref, x)
    xhat, _ = norm_parts(x)
    normed = (xhat * gain_ref[0:1, :] + nbias_ref[0:1, :]).astype(bf16)
    window_in = per_image(lambda i: nn(move_ref[...], normed[image_rows(i)]), count).astype(bf16)
    store(window_ref, window_in)

    @pl.when(step == 0)
    def _():
        if gather:
            for k in (0, 1):
                moving.forward(k)
            for k in (2, 3):
                moving.start(k)
            for k in (0, 1):
                moving.arrive(k)
            qkv_full[...] = join(qkv_ref)
        elif first:
            form_bias(biases_ref, table_ref, entry_ref[...])
        proj_full[...] = join(proj_ref).astype(f32).T.astype(bf16)
        total_ref[...] = jnp.zeros(total_ref.shape, f32)

    qkv = join(qkv_ref)
    turned = nt(qkv, window_in).astype(bf16)
    straight = nt(window_in, qkv[width:]).astype(bf16)
    for i in range(count):
        qk_ref[i] = turned[: 2 * width, image_rows(i)]
    store(v_ref, straight[:, width:])
    heads_rows = head_masks()
    halves = lane_masks()
    low_lane = iota((WPAD, LANES), 1) < WPAD
    if shifted:
        row_labels = [nt(row_ref[i].astype(f32).astype(bf16), move_ref[...]) for i in range(count)]
        col_labels = [nn(move_ref[...], col_ref[i].astype(f32).astype(bf16)) for i in range(count)]
    for pair in range(PAIRS * count):
        image, side = pair // PAIRS, pair % PAIRS
        across = slice(pair * LANES, (pair + 1) * LANES)
        within = slice(side * LANES, (side + 1) * LANES)
        if shifted:
            ahead = col_labels[image][side * LANES : side * LANES + WPAD, 1:2]
            behind = col_labels[image][side * LANES + WPAD : (side + 1) * LANES, 1:2]
            key_label = jnp.where(low_lane, ahead, behind)
            mask = jnp.where(key_label == row_labels[image][1:2, within], 0.0, mask_fill)
        for group in range(HEADS // GROUP):
            features = slice(group * LANES, (group + 1) * LANES)
            queries = turned[features, across]
            spread = jnp.concatenate([queries * heads_rows[h] for h in range(GROUP)], 1)
            raw = nn(straight[across, features], spread)
            for h in range(GROUP):
                head = group * GROUP + h
                part = raw[:, h * LANES : (h + 1) * LANES]
                scores = jnp.where(low_lane, part[:WPAD], part[WPAD:]) * head_scale + bias_ref[head]
                if shifted:
                    scores = scores + mask
                expo = jnp.exp(scores - jnp.max(scores, 0, keepdims=True))
                probs = (expo * (1.0 / jnp.sum(expo, 0, keepdims=True))).astype(bf16)
                probs_ref[image, side * HEADS + head] = probs
                both = jnp.concatenate([probs * halves[0], probs * halves[1]], 0)
                at = slice(head * HEAD_DIM, (head + 1) * HEAD_DIM)
                values = turned[2 * width + head * HEAD_DIM : 2 * width + (head + 1) * HEAD_DIM, across]
                att_ref[image, at, within] = nn(values, both).astype(bf16)
    attended = per_image(lambda i: nt(back_ref[...], att_ref[i]), count).astype(bf16)
    branch = nt(attended, join(proj_ref))
    middle = x + per_image(lambda i: valid_ref[step * count + i].astype(f32) * branch[image_rows(i)], count)
    store(middle_ref, middle)
    xhat, _ = norm_parts(middle)
    second_low = (xhat * gain_ref[1:2, :] + nbias_ref[1:2, :]).astype(bf16)
    store(second_ref, second_low)
    _, _, gate = route(second_low, router_ref[...], pos_col)
    store(gate_ref, gate)
    total_ref[...] += spread_rows(lay_positions(row_ref), second_low)

    @pl.when(step == final)
    def _():
        buffer_ref[...] = total_ref[...].astype(bf16)
        if gather:
            for k in (2, 3):
                moving.forward(k)
            for k in (2, 3):
                moving.arrive(k)
            for k in range(4):
                moving.sent(k)


def image_spec(array_shape, count):
    rest = tuple(array_shape[1:])
    zeros = (0,) * len(rest)
    return pl.BlockSpec((count,) + rest, lambda i: (i,) + zeros)


def whole_spec(array_shape):
    zeros = (0,) * len(array_shape)
    return pl.BlockSpec(tuple(array_shape), lambda i: zeros)


def image_call(kernel, images, arrays, outs, scratch, name, collective_id=None):
    count = 2 - images % 2

    def spec(kind, shape):
        if isinstance(kind, int):
            rest = tuple(shape[1:])
            return pl.BlockSpec((1,) + rest, lambda i: (kind,) + (0,) * len(rest))
        if kind in ("smem", "any"):
            return pl.BlockSpec(memory_space=pltpu.SMEM if kind == "smem" else pl.ANY)
        return image_spec(shape, count) if kind == "image" else whole_spec(shape)

    return pl.pallas_call(
        kernel,
        grid=(images // count,),
        out_shape=[jax.ShapeDtypeStruct(shape, dtype) for _, shape, dtype in outs],
        in_specs=[spec(kind, array.shape) for kind, array in arrays],
        out_specs=[spec(kind, shape) for kind, shape, _ in outs],
        scratch_shapes=scratch,
        compiler_params=pltpu.CompilerParams(
            vmem_limit_bytes=44 * MIB,
            dimension_semantics=("arbitrary",),
            collective_id=collective_id,
            has_side_effects=collective_id is not None,
        ),
        name=name,
    )(*[array for _, array in arrays])


def send_part(g, expert_out, second_low, router, pos_col, pos_row, logit_ref, router_grad_ref, total_ref):
    probs, chosen, gate = route(second_low, router, pos_col)
    gate_grad = jnp.where(pos_col >= 0, jnp.sum(g * expert_out, -1, keepdims=True), 0.0)
    sent = (gate * g).astype(bf16)
    logit_grad = gate_grad * gate * (chosen - probs)
    store(logit_ref, logit_grad)
    high, low = split_two(logit_grad)
    router_grad_ref[...] += tn(high, second_low) + tn(low, second_low)
    total_ref[...] += spread_rows(pos_row, sent)


def turn_kernel(
    prev_ref, gate_ref, returned_ref, cotangent_ref, enter_ref, leave_ref, col_ref, row_ref, second_ref, router_ref,
    block_ref, grad_ref, logit_ref, router_grad_ref, buffer_ref, total_ref,
):
    step = pl.program_id(0)
    count = cotangent_ref.shape[0]

    @pl.when(step == 0)
    def _():
        total_ref[...] = jnp.zeros(total_ref.shape, f32)
        router_grad_ref[...] = jnp.zeros(router_grad_ref.shape, f32)

    pos_col = join(col_ref)[:, 0:1]
    expert_out = collect(pos_col, returned_ref)
    x = (join(prev_ref) + join(gate_ref) * expert_out).astype(bf16)
    for i in range(count):
        block_ref[i] = nn(leave_ref[...], x[image_rows(i)]).astype(bf16)
    g = per_image(lambda i: nn(enter_ref[...], cotangent_ref[i]), count)
    store(grad_ref, g)
    send_part(
        g, expert_out, join(second_ref), router_ref[0], pos_col, lay_positions(row_ref), logit_ref, router_grad_ref, total_ref
    )

    @pl.when(step == pl.num_programs(0) - 1)
    def _():
        buffer_ref[...] = total_ref[...].astype(bf16)


def attention_backward_kernel(last, dp, mp, fast, *refs):
    (
        valid_ref, grad_ref, returned_ref, logit_ref, middle_ref, carried_ref, router_ref, col_ref, move_ref, back_ref,
        gain_ref, proj_ref, qkv_ref, window_ref, qk_ref, v_ref, probs_ref, att_ref,
    ) = refs[:18]
    refs = refs[18:]
    refs = list(refs)
    if fast:
        units_ref = refs.pop(0)
    if last:
        leave_ref = refs.pop(0)
        if fast:
            table_above, small_above, router_above, router_here, entry_ref, half_above, down_above, attn_above = refs[:8]
            refs = refs[8:]
    else:
        row_ref, expert_out_ref, second_ref, router_next_ref = refs[:4]
        refs = refs[4:]
    out_ref = refs.pop(0)
    closing = None
    if fast and last:
        results, refs = refs[:4], refs[4:]
    else:
        if fast:
            halves_ref = refs.pop(0)
            unit_ref, mine_ref = refs[:2]
        else:
            qkv_grad_ref, proj_grad_ref = refs[:2]
        table_ref, small_ref = refs[2:4]
        refs = refs[4:]
    if not last:
        logit_out_ref, router_grad_ref, buffer_ref = refs[:3]
        refs = refs[3:]
    turned = refs.pop(0)
    if fast:
        qkv_grad_ref, proj_grad_ref = refs[:2]
        refs = refs[2:]
    if not last:
        total_ref = refs.pop(0)
    step = pl.program_id(0)
    final = pl.num_programs(0) - 1
    count, _, width = carried_ref.shape
    if fast:
        row = Row()
        if last:
            table_ref, small_ref, unit_ref, lines_ref = refs[:4]
            landing, refs = refs[4:8], refs[8:]
            above = (half_above, down_above.at[1], attn_above)
            closing = Closing(row, dp, units_ref, unit_ref, lines_ref, above, landing, refs)
        else:
            sums = RowSum(row, blocks(units_ref), refs[0], refs[1], refs[2], blocks(mine_ref), refs[3:7])
            across_x = DeepSum(dp, [mine_ref.at[0]], [refs[7]], [halves_ref], [None], [None], refs[8:10] * 4)

        def take(k):
            if closing:
                closing.take(k)
            else:
                sums.end(k)
                if k == 0:
                    across_x.over_x(k).start()

        @pl.when(step == 0)
        def _():
            if closing:
                closing.enter()
            else:
                barrier = row.greet()
                pl.semaphore_wait(barrier, 2 + across_x.greet(barrier, False))
                for k in range(2):
                    sums.start(k)

    @pl.when(step == 0)
    def _():
        qkv_grad_ref[...] = jnp.zeros(qkv_grad_ref.shape, f32)
        proj_grad_ref[...] = jnp.zeros(proj_grad_ref.shape, f32)
        table_ref[...] = jnp.zeros(table_ref.shape, f32)
        small_ref[...] = jnp.zeros(small_ref.shape, f32)
        if not last:
            total_ref[...] = jnp.zeros(total_ref.shape, f32)
            router_grad_ref[...] = jnp.zeros(router_grad_ref.shape, f32)

    pos_col = join(col_ref)[:, 0:1]
    g = join(grad_ref)
    high, low = split_two(join(logit_ref))
    gain_ref, router = gain_ref.at[0], router_ref[0]
    normed_grad = collect(pos_col, returned_ref) + nn(high, router) + nn(low, router)
    xhat, rstd = norm_parts(join(middle_ref))
    small_ref[1:2, :] += jnp.sum(normed_grad * xhat, 0, keepdims=True)
    small_ref[3:4, :] += jnp.sum(normed_grad, 0, keepdims=True)
    middle_grad = g + norm_back(normed_grad, gain_ref[1:2, :], xhat, rstd)

    def branch_part(i):
        low_part = (valid_ref[step * count + i].astype(f32) * middle_grad[image_rows(i)]).astype(bf16)
        return nn(move_ref[...], low_part)

    branch_grad = per_image(branch_part, count).astype(bf16)
    for i in range(count):
        proj_grad_ref[...] += nn(att_ref[i], branch_grad[image_rows(i)])
    att_grad = nt(proj_ref[...], branch_grad).astype(bf16)
    if fast:

        @pl.when(step == 0)
        def _():
            if closing:
                closing.early()
            else:
                for k in range(2):
                    sums.middle(k)

        pl.when(step == final)(functools.partial(take, 0))

    heads_rows = head_masks()
    halves = lane_masks()
    low_lane = iota((WPAD, LANES), 1) < WPAD
    for pair in range(PAIRS * count):
        image, side = pair // PAIRS, pair % PAIRS
        across = slice(pair * LANES, (pair + 1) * LANES)
        within = slice(side * LANES, (side + 1) * LANES)
        for group in range(HEADS // GROUP):
            features = slice(group * LANES, (group + 1) * LANES)
            grads = att_grad[features, across]
            spread = jnp.concatenate([grads * heads_rows[h] for h in range(GROUP)], 1)
            raw = nn(v_ref[image, within, features], spread)
            for h in range(GROUP):
                head = group * GROUP + h
                at = slice(head * HEAD_DIM, (head + 1) * HEAD_DIM)
                below = slice(width + head * HEAD_DIM, width + (head + 1) * HEAD_DIM)
                lowest = slice(2 * width + head * HEAD_DIM, 2 * width + (head + 1) * HEAD_DIM)
                part = raw[:, h * LANES : (h + 1) * LANES]
                probs_grad = jnp.where(low_lane, part[:WPAD], part[WPAD:])
                probs_low = probs_ref[image, side * HEADS + head]
                probs = probs_low.astype(f32)
                weighted = probs * probs_grad
                scores_grad = weighted - probs * jnp.sum(weighted, 0, keepdims=True)
                table_ref[head] += scores_grad
                scores_low = scores_grad.astype(bf16)
                both = jnp.concatenate([scores_low * halves[0], scores_low * halves[1]], 0)
                probs_both = jnp.concatenate([probs_low * halves[0], probs_low * halves[1]], 0)
                turned[at, across] = (nn(qk_ref[image, below, within], both) * head_scale).astype(bf16)
                turned[below, across] = (nt(qk_ref[image, at, within], both) * head_scale).astype(bf16)
                turned[lowest, across] = nt(att_grad[at, across], probs_both).astype(bf16)
    qkv_grad_ref[...] += nn(turned[...], join(window_ref))
    if fast:

        @pl.when(step == final)
        def _():
            columns, rows = 3 * width // mp, width // mp
            proj_turned = proj_grad_ref[...].T
            for place in range(mp):
                q = quarter_at(place, mp)
                unit_ref[place, :columns] = qkv_grad_ref[q * columns : (q + 1) * columns].astype(bf16)
                unit_ref[place, columns:] = proj_turned[q * rows : (q + 1) * rows].astype(bf16)
            if closing:
                closing.open()
            take(1)
            if closing:
                heads = 2 * HEADS
                lines_ref[...] = jnp.zeros(lines_ref.shape, f32)
                lines_ref[:heads, :TABLE] = table_grad([table_ref, table_above], entry_ref[...])

    mixed_grad = per_image(lambda i: nt(back_ref[...], turned[:, image_rows(i)]), count).astype(bf16)
    first_grad = nn(mixed_grad, qkv_ref[...])
    if closing:

        @pl.when(step == final)
        def _():
            closing.cross()

    xhat, rstd = norm_parts(join(carried_ref))
    small_ref[0:1, :] += jnp.sum(first_grad * xhat, 0, keepdims=True)
    small_ref[2:3, :] += jnp.sum(first_grad, 0, keepdims=True)
    if closing:

        @pl.when(step == final)
        def _():
            heads = 2 * HEADS
            lines_ref[heads : heads + EXPERTS] = router_here[:EXPERTS]
            lines_ref[heads + EXPERTS : heads + 2 * EXPERTS] = router_above[:EXPERTS]
            lines_ref[heads + 2 * EXPERTS : heads + 2 * EXPERTS + 8] = small_ref[...]
            lines_ref[heads + 2 * EXPERTS + 8 : heads + 2 * EXPERTS + 16] = small_above[...]
            closing.send_lines()

    out = middle_grad + norm_back(first_grad, gain_ref[0:1, :], xhat, rstd)
    if last:
        top = out.astype(bf16)
        rest = out - top.astype(f32)
        mid, low = split_two(rest)
        leave = leave_ref[...]
        for i in range(count):
            at = image_rows(i)
            out_ref[i] = nn(leave, top[at]) + nn(leave, mid[at]) + nn(leave, low[at])
    else:
        store(out_ref, out)
        send_part(
            out, join(expert_out_ref), join(second_ref), router_next_ref[0], pos_col, lay_positions(row_ref), logit_out_ref,
            router_grad_ref, total_ref,
        )

    @pl.when(step == final)
    def _():
        if not last:
            buffer_ref[...] = total_ref[...].astype(bf16)
        if closing:
            closing.finish()
            for out, landed in zip(results, landing):
                out[...] = landed[...]
        elif fast:
            across_x.halve(0)
            across_x.over_x(0).wait_send()
            for k in range(2):
                sums.finish(k)


def quarter_at(place, mp):
    return place % (mp // 2) * 2 + place // (mp // 2)


def add_up(*parts):
    total = parts[0].astype(f32)
    for part in parts[1:]:
        total = total + part.astype(f32)
    return total


def to_row(source, target, sems, k, row):
    return pltpu.make_async_remote_copy(
        src_ref=source,
        dst_ref=target,
        send_sem=sems[0].at[k],
        recv_sem=sems[1].at[k],
        device_id={"mp": row},
        device_id_type=MESH,
    )


class Row:
    def __init__(self):
        row = lax.axis_index("mp")
        self.row, self.core, self.y = row, lax.rem(row, 2), lax.div(row, 2)
        self.sibling, self.across = row + 1 - 2 * self.core, row + 2 - 4 * self.y
        self.place = self.core * 2 + self.y
        self.place_across = self.core * 2 + 1 - self.y

    def greet(self):
        barrier = pltpu.get_barrier_semaphore()
        for row in (self.sibling, self.across):
            pl.semaphore_signal(barrier, inc=1, device_id={"mp": row}, device_id_type=MESH)
        return barrier


class RowSum:
    semaphores = 4

    def __init__(self, row, units, core_in, y_out, y_in, mine, sems):
        self.row, self.units, self.mine = row, units, mine
        self.core_in, self.y_out, self.y_in = core_in, y_out, y_in
        self.sems = (sems[:2], sems[2:])

    def pair(self, k):
        theirs = self.units[k].at[pl.ds(2 * (1 - self.row.core), 2)]
        return to_row(theirs, self.core_in.at[k], self.sems[0], k, self.row.sibling)

    def cross(self, k):
        return to_row(self.y_out.at[k], self.y_in.at[k], self.sems[1], k, self.row.across)

    def start(self, k):
        self.pair(k).start()

    def middle(self, k):
        self.pair(k).wait_recv()
        other = 1 - self.row.y
        mixed = add_up(self.units[k][self.row.core * 2 + other], self.core_in[k, other])
        self.y_out[k] = mixed.astype(bf16)
        self.cross(k).start()

    def end(self, k):
        self.cross(k).wait_recv()
        self.mine[k][...] = add_up(
            self.units[k][self.row.place], self.core_in[k, self.row.y], self.y_in[k]
        ).astype(bf16)

    def finish(self, k):
        self.pair(k).wait_send()
        self.cross(k).wait_send()

    @classmethod
    def scratch(cls, count, width):
        return [
            pltpu.VMEM((count, 2, width, width), bf16),
            pltpu.VMEM((count, width, width), bf16),
            pltpu.VMEM((count, width, width), bf16),
        ] + [pltpu.SemaphoreType.DMA((count,))] * cls.semaphores


class RowGather:
    semaphores = 6

    def __init__(self, row, sources, fulls, slot, slot_across, sems):
        self.row, self.sources, self.fulls = row, sources, fulls
        self.slot, self.slot_across = slot, slot_across
        self.sems = (sems[:2], sems[2:4], sems[4:])

    def over(self, k):
        return to_row(self.sources[k], self.fulls[k].at[self.slot], self.sems[0], k, self.row.across)

    def near(self, k):
        return to_row(self.sources[k], self.fulls[k].at[self.slot], self.sems[1], k, self.row.sibling)

    def onward(self, k):
        block = self.fulls[k].at[self.slot_across]
        return to_row(block, block, self.sems[2], k, self.row.sibling)

    def start(self, k):
        self.over(k).start()
        self.near(k).start()

    def forward(self, k):
        self.over(k).wait_recv()
        self.onward(k).start()

    def arrive(self, k):
        self.near(k).wait_recv()
        self.onward(k).wait_recv()

    def sent(self, k):
        self.over(k).wait_send()
        self.near(k).wait_send()
        self.onward(k).wait_send()

    @classmethod
    def scratch(cls, count):
        return [pltpu.SemaphoreType.DMA((count,))] * cls.semaphores


class WeightGather(RowGather):
    def __init__(self, shards, fulls, sems):
        row = Row()
        super().__init__(row, shards, fulls, row.row, row.across, sems[:6])
        self.own_sem = sems[6]

    def own(self, k):
        return pltpu.make_async_copy(self.sources[k], self.fulls[k].at[self.slot], self.own_sem.at[k])

    def start(self, k):
        super().start(k)
        self.own(k).start()

    def arrive(self, k):
        super().arrive(k)
        self.own(k).wait()

    @classmethod
    def scratch(cls, count):
        return super().scratch(count) + [pltpu.SemaphoreType.DMA((count,))]


class DeepSum:
    def __init__(self, dp, total, arrived, halves, slots, result, sems):
        self.total, self.arrived, self.halves, self.slots, self.result = total, arrived, halves, slots, result
        self.x_sems, self.z_sems, self.z_back, self.x_back = (sems[2 * k : 2 * k + 2] for k in range(4))
        me = lax.axis_index("dp")
        self.x, self.z, self.deep = lax.rem(me, 2), lax.div(me, 2), dp // 2
        self.partner = me + 1 - 2 * self.x

    def greet(self, barrier, whole=True):
        pl.semaphore_signal(barrier, inc=1, device_id={"dp": self.partner}, device_id_type=MESH)
        if not whole:
            return 1
        for off in range(1, self.deep):
            peer = lax.rem(self.z + off, self.deep) * 2 + self.x
            pl.semaphore_signal(barrier, inc=1, device_id={"dp": peer}, device_id_type=MESH)
        return self.deep

    def cut(self, k):
        height = self.halves[k].shape[0]
        return height, height // self.deep

    def over_x(self, k):
        height, _ = self.cut(k)
        away = self.total[k].at[pl.ds(pl.multiple_of((1 - self.x) * height, height), height)]
        return to_peer(away, self.arrived[k], self.x_sems[0].at[k], self.x_sems[1].at[k], self.partner)

    def over_z(self, k, off):
        _, piece = self.cut(k)
        to = lax.rem(self.z + off, self.deep)
        part = self.halves[k].at[pl.ds(pl.multiple_of(to * piece, piece), piece)]
        sems = [sem.at[k, off] for sem in self.z_sems]
        return to_peer(part, self.slots[k].at[off], *sems, to * 2 + self.x)

    def own_piece(self, k):
        height, piece = self.cut(k)
        return self.result[k].at[pl.ds(pl.multiple_of(self.x * height + self.z * piece, piece), piece)]

    def own_half(self, k):
        height, _ = self.cut(k)
        return self.result[k].at[pl.ds(pl.multiple_of(self.x * height, height), height)]

    def back_z(self, k, off):
        to = lax.rem(self.z + off, self.deep)
        sems = [sem.at[k, off] for sem in self.z_back]
        return to_peer(self.own_piece(k), self.own_piece(k), *sems, to * 2 + self.x)

    def back_x(self, k):
        return to_peer(self.own_half(k), self.own_half(k), self.x_back[0].at[k], self.x_back[1].at[k], self.partner)

    def halve(self, k):
        self.over_x(k).wait_recv()
        height, _ = self.cut(k)
        keep = self.total[k][pl.ds(pl.multiple_of(self.x * height, height), height)]
        self.halves[k][...] = add_up(keep, self.arrived[k][...]).astype(self.halves[k].dtype)

    def deepen(self, k):
        for off in range(1, self.deep):
            self.over_z(k, off).start()

    def quarter(self, k):
        for off in range(1, self.deep):
            self.over_z(k, off).wait_recv()
        _, piece = self.cut(k)
        keep = self.halves[k][pl.ds(pl.multiple_of(self.z * piece, piece), piece)]
        total = add_up(keep, *[self.slots[k][off] for off in range(1, self.deep)])
        self.own_piece(k)[...] = total.astype(self.result[k].dtype)
        for off in range(1, self.deep):
            self.back_z(k, off).start()

    def widen(self, k):
        for off in range(1, self.deep):
            self.back_z(k, off).wait_recv()
        self.back_x(k).start()

    def finish(self, k, halved=True):
        if halved:
            self.over_x(k).wait_send()
        for off in range(1, self.deep):
            self.over_z(k, off).wait_send()
            self.back_z(k, off).wait_send()
        self.back_x(k).wait()

    @staticmethod
    def semaphores(dp, count):
        one, many = pltpu.SemaphoreType.DMA((count,)), pltpu.SemaphoreType.DMA((count, dp // 2))
        return [one, one, many, many, many, many, one, one]


def blocks(ref):
    return [ref.at[k] for k in range(ref.shape[0])]


class WideSum:
    def __init__(self, dp, total, slots, result, sems):
        self.dp, self.total, self.slots, self.result, self.sems = dp, total, slots, result, sems
        self.me = lax.axis_index("dp")

    def piece(self, ref, at):
        size = ref.shape[0] // self.dp
        return ref.at[pl.ds(pl.multiple_of(at * size, size), size)]

    def out(self, k, p):
        peer = partner_of(self.me, p, self.dp)
        sems = self.sems[0].at[k, p], self.sems[1].at[k, p]
        return to_peer(self.piece(self.total[k], peer), self.slots[k].at[p], *sems, peer)

    def back(self, k, p):
        mine = self.piece(self.result[k], self.me)
        sems = self.sems[2].at[k, p], self.sems[3].at[k, p]
        return to_peer(mine, mine, *sems, partner_of(self.me, p, self.dp))

    def start(self, k):
        for p in range(self.dp - 1, 0, -1):
            self.out(k, p).start()

    def middle(self, k):
        for p in range(1, self.dp):
            self.out(k, p).wait_recv()
        total = add_up(self.piece(self.total[k], self.me)[...], *[self.slots[k][p] for p in range(1, self.dp)])
        self.piece(self.result[k], self.me)[...] = total.astype(self.result[k].dtype)
        for p in range(self.dp - 1, 0, -1):
            self.back(k, p).start()

    def finish(self, k):
        for p in range(1, self.dp):
            self.out(k, p).wait_send()
            self.back(k, p).wait()

    @staticmethod
    def semaphores(dp, count):
        return [pltpu.SemaphoreType.DMA((count, dp))] * 4


class Closing:
    lines = 64

    def __init__(self, row, dp, units_ref, attn_ref, lines_ref, given, results, refs):
        self.row, self.lines_ref, self.dp = row, lines_ref, dp
        self.full, shard, small, above = results
        core_in, y_out, y_in = refs[:3]
        mine, x_in, half, z_in, self.s_core, self.s_one, self.s_y, self.s_mine, s_slots, wide_in = refs[7:17]
        x_above, half_above, z_above = refs[17:20]
        refs_sems, refs = refs[3:7], refs[20:]
        self.mine = mine
        self.sums = RowSum(row, blocks(units_ref) + [attn_ref], core_in, y_out, y_in, blocks(mine), refs_sems)
        self.gather = RowGather(
            row, [mine.at[k] for k in range(2)], blocks(self.full), row.place, row.place_across, refs[:6]
        )
        self.s_pair = to_row(lines_ref, self.s_core, refs[6:8], 0, row.sibling)
        self.s_cross = to_row(self.s_one, self.s_y, refs[8:10], 0, row.across)
        self.here = DeepSum(
            dp, [mine.at[0], mine.at[1]], blocks(x_in), blocks(half), blocks(z_in), [shard.at[0], shard.at[1]], refs[10:18]
        )
        self.above = DeepSum(
            dp, [None, *given[1:]], [None] + blocks(x_above), [given[0]] + blocks(half_above), blocks(z_above), blocks(above),
            refs[18:26],
        )
        self.wide = WideSum(dp, [mine.at[2], self.s_mine], [wide_in, s_slots], [shard.at[2], small], refs[26:30])

    def enter(self):
        greet(self.dp, lax.axis_index("dp"), (self.row.sibling, self.row.across))
        for k in range(2):
            self.sums.start(k)
        self.above.deepen(0)
        for k in (1, 2):
            self.above.over_x(k).start()

    def early(self):
        for k in range(2):
            self.sums.middle(k)
        for k in (1, 2):
            self.above.halve(k)
            self.above.deepen(k)
        self.above.quarter(0)

    def take(self, k):
        self.sums.end(k)
        self.here.over_x(k).start()
        if k == 0:
            self.above.widen(0)
            for j in (1, 2):
                self.above.quarter(j)
        else:
            for j in (1, 2):
                self.above.widen(j)

    def open(self):
        self.sums.start(2)

    def cross(self):
        self.sums.middle(2)
        for k in range(2):
            self.here.halve(k)
            self.here.deepen(k)

    def send_lines(self):
        self.s_pair.start()
        for k in range(2):
            self.here.quarter(k)
        self.s_pair.wait_recv()
        self.s_one[...] = self.lines_ref[...] + self.s_core[...]
        self.s_cross.start()

    def finish(self):
        self.sums.end(2)
        self.wide.start(0)
        self.s_cross.wait_recv()
        self.s_mine[...] = self.s_one[...] + self.s_y[...]
        self.wide.start(1)
        for k in range(2):
            self.gather.start(k)
            self.full[k, self.row.place] = self.mine[k]
        self.wide.middle(0)
        self.wide.middle(1)
        for k in range(2):
            self.here.widen(k)
        for k in range(2):
            self.gather.forward(k)
        self.s_pair.wait_send()
        self.s_cross.wait_send()
        for k in range(3):
            self.sums.finish(k)
            self.above.finish(k, k > 0)
        for k in range(2):
            self.here.finish(k)
            self.wide.finish(k)
            self.gather.arrive(k)
            self.gather.sent(k)

    @classmethod
    def scratch(cls, dp, width):
        deep = dp // 2
        lines = cls.lines
        flat = pltpu.VMEM((lines, width), f32)
        half, slots = (width // 2, width), (deep, width // dp, width)
        return (
            RowSum.scratch(3, width)
            + [
                pltpu.VMEM((3, width, width), bf16),
                pltpu.VMEM((2, *half), bf16),
                pltpu.VMEM((2, *half), bf16),
                pltpu.VMEM((2, *slots), bf16),
                flat, flat, flat, flat,
                pltpu.VMEM((dp, lines // dp, width), f32),
                pltpu.VMEM((dp, width // dp, width), bf16),
                pltpu.VMEM((2, *half), bf16),
                pltpu.VMEM((2, *half), bf16),
                pltpu.VMEM((3, *slots), bf16),
            ]
            + RowGather.scratch(2)
            + [pltpu.SemaphoreType.DMA((1,))] * 4
            + DeepSum.semaphores(dp, 2)
            + DeepSum.semaphores(dp, 3)
            + WideSum.semaphores(dp, 2)
        )


def format_kernel(columns, *refs):
    count = (len(refs) - 6) // 2
    qkv_out, proj_out, core_up_out, core_down_out, up_out, down_out = refs[2 * count :]

    def form(full, shard):
        mp, width = full.shape[1], full.shape[2]
        rows = width // mp
        qkv_out[0] = shard[2, :columns].astype(f32)
        proj_out[0] = shard[2, columns:].astype(f32)
        core_up_out[0] = shard[0].astype(f32)
        for place in range(mp):
            q = quarter_at(place, mp)
            up_out[0, 0, :, q * width : (q + 1) * width] = full[0, place].astype(f32)
        for chunk in range(mp):
            at = slice(chunk * width, (chunk + 1) * width)
            core_down_out[0, :, at] = shard[1, chunk * rows : (chunk + 1) * rows].astype(f32)
            block = [None] * mp
            for place in range(mp):
                block[quarter_at(place, mp)] = full[1, place, chunk * rows : (chunk + 1) * rows]
            down_out[0, 0, at, :] = turn_blocks(jnp.concatenate(block, 0))

    for layer in range(count):
        pl.when(pl.program_id(0) == layer)(functools.partial(form, refs[layer], refs[count + layer]))


def format_call(fulls, shards, columns):
    layers = len(fulls)
    _, mp, width, _ = fulls[0].shape
    hidden = mp * width
    shapes = [
        (layers, columns, width),
        (layers, width - columns, width),
        (layers, width, width),
        (layers, width // mp, hidden),
        (layers, 1, width, hidden),
        (layers, 1, hidden, width),
    ]
    return pl.pallas_call(
        functools.partial(format_kernel, columns),
        grid=(layers,),
        out_shape=[jax.ShapeDtypeStruct(shape, f32) for shape in shapes],
        in_specs=[whole_spec(a.shape) for a in (*fulls, *shards)],
        out_specs=[image_spec(shape, 1) for shape in shapes],
        compiler_params=pltpu.CompilerParams(vmem_limit_bytes=56 * MIB),
        name="format",
    )(*fulls, *shards)


def greet(dp, me, rows=()):
    barrier = pltpu.get_barrier_semaphore()
    for row in rows:
        pl.semaphore_signal(barrier, inc=1, device_id={"mp": row}, device_id_type=MESH)

    def signal(off, carry):
        pl.semaphore_signal(barrier, inc=1, device_id={"dp": lax.rem(me + off, dp)}, device_id_type=MESH)
        return carry

    lax.fori_loop(1, dp, signal, 0)
    pl.semaphore_wait(barrier, dp - 1 + len(rows))


def partner_of(me, p, dp):
    out, bit = 0, 1
    while bit < dp:
        one, two = lax.rem(lax.div(me, bit), 2), lax.rem(lax.div(p, bit), 2)
        out = out + bit * (one + two - 2 * one * two)
        bit *= 2
    return out


def to_peer(source, target, send_sem, recv_sem, peer):
    return pltpu.make_async_remote_copy(
        src_ref=source,
        dst_ref=target,
        send_sem=send_sem,
        recv_sem=recv_sem,
        device_id={"dp": peer},
        device_id_type=MESH,
    )


def gelu_parts(h):
    root = np.float32(np.sqrt(2.0 / np.pi))
    square = h * h
    t = jnp.tanh(root * h * (1.0 + 0.044715 * square))
    half = 0.5 * (1.0 + t)
    slope = half + 0.5 * h * (1.0 - t * t) * root * (1.0 + 3 * 0.044715 * square)
    return h * half, slope


def expert_forward_kernel(dp, mp, layer, gather, *refs):
    refs = list(refs)
    buffer_ref, up_any, down_any, rup_any, rdown_any = refs[:5]
    refs = refs[5:]
    if gather:
        shards = [ref.at[layer + 1] for ref in refs[:4]]
        refs = refs[4:]
    recv_ref, returned_ref, up_eff, down_eff = refs[:4]
    refs = refs[4:]
    if gather:
        fulls = refs[:4]
        refs = refs[4:]
    part, core, up_ref, down_ref, rup_ref, rdown_ref, local = refs[:7]
    refs = refs[7:]
    moving = WeightGather(shards, fulls, refs[:7]) if gather else None
    send_one, recv_one, send_two, recv_two = refs[-4:]
    split = dp // EXPERTS
    me = lax.axis_index("dp")
    loads = [
        pltpu.make_async_copy(source, target, local.at[k])
        for k, (source, target) in enumerate(
            [
                (up_any, up_ref),
                (rup_any.at[layer, 0], rup_ref),
                (down_any, down_ref),
                (rdown_any.at[layer, 0], rdown_ref),
            ]
        )
    ]
    for load in loads:
        load.start()
    greet(dp, me, (moving.row.sibling, moving.row.across) if gather else ())

    def first(off):
        peer = partner_of(me, off, dp)
        return to_peer(
            buffer_ref.at[lax.div(peer, split)], recv_ref.at[me], send_one.at[off], recv_one.at[off], peer
        )

    def second(off):
        source = partner_of(me, off, dp)
        return to_peer(part.at[source], returned_ref.at[me], send_two.at[off], recv_two.at[off], source)

    def start_first(off, carry):
        first(dp - off).start()
        return carry

    lax.fori_loop(1, dp, start_first, 0)
    if gather:
        for k in range(4):
            moving.start(k)
    recv_ref[me] = buffer_ref[lax.div(me, split)]
    hidden = up_eff.shape[1]
    columns = up_ref.shape[-1]
    loads[0].wait()
    loads[1].wait()
    if split == 1 and columns % LANES == 0:
        for m in range(mp):
            at = slice(m * columns, (m + 1) * columns)
            up_eff[:, at] = (up_ref[m].astype(f32) + rup_ref[:, at].astype(f32)).astype(bf16)
    else:
        core[...] = rup_ref[...].astype(f32)
        begin = lax.rem(me, split) * hidden
        for m in range(mp):
            put = onehot(iota((columns, hidden), 0) + m * columns == iota((columns, hidden), 1) + begin)
            core[...] += nn(up_ref[m], put)
        up_eff[...] = core[...].astype(bf16)
    begin = pl.multiple_of(lax.rem(me, split) * hidden, LANES)
    loads[2].wait()
    loads[3].wait()
    core_part = down_ref[:, :, pl.ds(begin, hidden)].reshape(down_eff.shape[1], hidden)
    down_eff[...] = (core_part.astype(f32).T + rdown_ref[...].astype(f32)).astype(bf16)

    def work(source):
        hidden_pre = nn(recv_ref[source], up_eff[...])
        hidden_low = gelu_parts(hidden_pre)[0].astype(bf16)
        return nn(hidden_low, down_eff[...]).astype(bf16)

    returned_ref[me] = work(me)

    def step(off, carry):
        source = partner_of(me, off, dp)
        first(off).wait_recv()
        part[source] = work(source)
        second(off).start()
        return carry

    lax.fori_loop(1, dp, step, 0)
    if gather:
        for k in range(4):
            moving.forward(k)

    def finish(off, carry):
        first(off).wait_send()
        second(off).wait()
        return carry

    lax.fori_loop(1, dp, finish, 0)
    if gather:
        for k in range(4):
            moving.arrive(k)
            moving.sent(k)


def expert_backward_kernel(dp, mp, fast, reduce, *refs):
    refs = list(refs)
    buffer_ref, recv_ref, up_ref, down_ref = refs[:4]
    refs = refs[4:]
    if reduce:
        given_ref, attn_ref = refs[:2]
        refs = refs[2:]
    returned_ref = refs.pop(0)
    if fast:
        units_ref = refs.pop(0)
    else:
        up_term, down_term = refs[:2]
        refs = refs[2:]
    if reduce:
        full_ref, mine_ref = refs[:2]
        refs = refs[2:]
    grads, hidden_low, slope, pre, part = refs[:5]
    refs = refs[5:]
    if fast:
        up_term, down_term = refs[:2]
        refs = refs[2:]
    row = Row() if reduce else None
    if reduce:
        core_in, y_out, y_in = refs[:3]
        sums = RowSum(row, [attn_ref], core_in, y_out, y_in, [mine_ref], refs[3:7])
        gather = RowGather(
            row, [given_ref.at[k] for k in range(2)], [full_ref.at[k] for k in range(2)], row.place, row.place_across,
            refs[7:13],
        )
        refs = refs[13:]
    send_one, recv_one, send_two, recv_two = refs
    split = dp // EXPERTS
    me = lax.axis_index("dp")
    greet(dp, me, (row.sibling, row.across) if reduce else ())

    def first(off):
        peer = partner_of(me, off, dp)
        return to_peer(buffer_ref.at[lax.div(peer, split)], grads.at[me], send_one.at[off], recv_one.at[off], peer)

    def second(off):
        source = partner_of(me, off, dp)
        return to_peer(part.at[source], returned_ref.at[me], send_two.at[off], recv_two.at[off], source)

    def start_first(off, carry):
        first(dp - off).start()
        return carry

    lax.fori_loop(1, dp, start_first, 0)
    if reduce:
        sums.start(0)
        for k in range(2):
            gather.start(k)
    grads[me] = buffer_ref[lax.div(me, split)]

    def again(source, carry):
        value, rate = gelu_parts(nn(recv_ref[source], up_ref[...]))
        hidden_low[source] = value.astype(bf16)
        slope[source] = rate
        return carry

    lax.fori_loop(0, dp, again, 0)
    if reduce:
        sums.middle(0)
        for k in range(2):
            full_ref[k, row.place] = given_ref[k]

    def work(source):
        hidden_grad = nt(grads[source], down_ref[...])
        pre_grad = (slope[source] * hidden_grad).astype(bf16)
        pre[source] = pre_grad
        return nt(pre_grad, up_ref[...]).astype(bf16)

    returned_ref[me] = work(me)

    def step(off, carry):
        source = partner_of(me, off, dp)
        first(off).wait_recv()
        part[source] = work(source)
        second(off).start()
        return carry

    lax.fori_loop(1, dp, step, 0)
    if reduce:
        for k in range(2):
            gather.forward(k)
        sums.end(0)
    up_term[...] = jnp.zeros(up_term.shape, f32)
    down_term[...] = jnp.zeros(down_term.shape, f32)

    def terms(block, carry):
        up_term[...] += tn(recv_ref[block], pre[block])
        down_term[...] += tn(grads[block], hidden_low[block])
        return carry

    lax.fori_loop(0, dp, terms, 0)
    if fast:
        width = up_term.shape[0]
        height = width // mp
        for place in range(mp):
            q = quarter_at(place, mp)
            units_ref[0, place] = up_term[:, q * width : (q + 1) * width].astype(bf16)
            for chunk in range(mp):
                block = down_term[q * height : (q + 1) * height, chunk * width : (chunk + 1) * width]
                units_ref[1, place, chunk * height : (chunk + 1) * height] = block.astype(bf16)

    def finish(off, carry):
        first(off).wait_send()
        second(off).wait()
        return carry

    lax.fori_loop(1, dp, finish, 0)
    if reduce:
        sums.finish(0)
        for k in range(2):
            gather.arrive(k)
            gather.sent(k)


def expert_call(kernel, arrays, outs, scratch, dp, collective_id, name, flops, anys=(), any_outs=()):
    sems = [pltpu.SemaphoreType.DMA((dp,))] * 4
    vmem, anywhere = pl.BlockSpec(memory_space=pltpu.VMEM), pl.BlockSpec(memory_space=pl.ANY)
    return pl.pallas_call(
        kernel,
        out_shape=[jax.ShapeDtypeStruct(shape, dtype) for shape, dtype in (*outs, *any_outs)],
        in_specs=[vmem] * len(arrays) + [anywhere] * len(anys),
        out_specs=[vmem] * len(outs) + [anywhere] * len(any_outs),
        scratch_shapes=scratch + sems,
        compiler_params=pltpu.CompilerParams(
            vmem_limit_bytes=44 * MIB, collective_id=collective_id, has_side_effects=True
        ),
        cost_estimate=pl.CostEstimate(flops=flops, bytes_accessed=20 * MIB, transcendentals=0),
        name=name,
    )(*arrays, *anys)


def by_windows(grid):
    images, kinds = grid.shape[:2]
    blocks = GRID // WINDOW
    grid = grid.reshape(images, kinds, blocks, WINDOW, blocks, WINDOW).transpose(0, 1, 2, 4, 3, 5)
    grid = grid.reshape(images, kinds, blocks * blocks, WINPOS)
    grid = jnp.pad(grid, ((0, 0), (0, 0), (0, 0), (0, WPAD - WINPOS)), constant_values=-1)
    return grid.reshape(images, kinds, IMGROWS)


def per_device(
    patches,
    qkv_weight,
    proj_weight,
    core_up,
    core_down,
    residual_up,
    residual_down,
    position_bias,
    router_weight,
    norm_gain,
    norm_bias,
    cotangent,
    image_valid,
    expert_index,
    slot_index,
    region_id,
):
    dp, mp = lax.axis_size("dp"), lax.axis_size("mp")
    images, _, width = patches.shape
    split = dp // EXPERTS
    hidden = residual_up.shape[-1]
    hidden_full = core_up.shape[-1] * mp
    row_index = lax.axis_index("mp")

    fast = split == 1 and dp == 8 and mp == 4 and hidden == mp * width
    qkv_rows, proj_rows, down_rows = (a.transpose(0, 2, 1) for a in (qkv_weight, proj_weight, core_down))
    shards = (qkv_rows, proj_rows, core_up, down_rows)
    gathered = [[None] * len(shards)] * LAYERS
    if not fast:
        gathered = [[lax.all_gather(a[l], "mp", axis=0, tiled=False) for a in shards] for l in range(LAYERS)]

    position = jnp.where(slot_index >= 0, expert_index * SLOTS + slot_index, -1)
    row_form = by_windows(jnp.stack([position.reshape(images, GRID, GRID), region_id], 1))
    col_form = row_form.transpose(0, 2, 1)
    enter = jnp.asarray(enter_table(), bf16)
    leave = jnp.asarray(enter_table().T, bf16)
    moves = [jnp.asarray(move_table(l % 2 == 1), bf16) for l in range(LAYERS)]
    backs = [jnp.asarray(move_table(l % 2 == 1).T, bf16) for l in range(LAYERS)]
    table_rows = position_bias.transpose(0, 2, 1).reshape(LAYERS * HEADS, OFFSETS)
    table_rows = jnp.pad(table_rows, ((0, 0), (0, TABLE - OFFSETS)))
    entry_row, entry_col = jnp.asarray(cell_entries()[None, :]), jnp.asarray(cell_entries()[:, None])
    routers = jnp.pad(router_weight.transpose(0, 2, 1), ((0, 0), (0, LANES - EXPERTS), (0, 0)))

    token = (images, IMGROWS, width)
    buffer_shape = (ROWS, width)
    block_rows = (dp, SLOTS, width)
    pieces = (split, ROWS, width)

    def by_piece(returned):
        return returned.reshape(EXPERTS, split, SLOTS, width).transpose(1, 0, 2, 3).reshape(pieces)

    records = []
    before = None
    for l in range(LAYERS):
        first = l == 0
        gather = fast and first
        if first:
            arrays = [("image", patches), ("whole", enter)]
        else:
            arrays = [("image", before[0]), ("image", before[1]), ("whole", before[2])]
        arrays += [
            ("smem", image_valid),
            ("image", col_form),
            ("image", row_form),
            ("any", qkv_rows) if gather else ("whole", gathered[l][0]),
            ("any", proj_rows) if gather else ("whole", gathered[l][1]),
            ("whole", table_rows) if first else (l, biases),
            ("whole", moves[l]),
            ("whole", backs[l]),
            (l, norm_gain),
            (l, norm_bias),
            (l, routers),
        ]
        if first:
            arrays.append(("whole", entry_row))
        if gather:
            arrays += [("any", core_up), ("any", down_rows)]
        outs = [("image", token, f32)]
        if first:
            outs.append(("whole", (LAYERS, HEADS, WPAD, LANES), f32))
        else:
            outs.append(("image", token, f32))
        outs += [
            ("image", token, f32),
            ("image", token, bf16),
            ("image", (images, IMGROWS, 1), f32),
            ("whole", buffer_shape, bf16),
            ("image", token, bf16),
            ("image", (images, 2 * width, IMGROWS), bf16),
            ("image", token, bf16),
            ("image", (images, PAIRS * HEADS, WPAD, LANES), bf16),
            ("image", (images, width, IMGROWS), bf16),
            ("whole", (width, width), bf16),
        ]
        scratch = [pltpu.VMEM(buffer_shape, f32)]
        gathered_shapes = [(mp, *a.shape[1:]) for a in shards]
        if gather:
            outs.append(("whole", (3 * width, width), bf16))
            outs += [("any", shape, bf16) for shape in gathered_shapes[2:]]
            scratch += [pltpu.VMEM(shape, bf16) for shape in gathered_shapes[:2]] + WeightGather.scratch(4)
        results = list(
            image_call(
                functools.partial(attention_forward_kernel, first, l % 2 == 1, mp, gather),
                images, arrays, outs, scratch, f"attend_{l}", 3 * LAYERS + 1 if gather else None,
            )
        )
        if gather:
            gathered[l] = [results[-3], None] + results[-2:]
            results = results[:-3]
        carried = results.pop(0)
        if first:
            biases = results.pop(0)
        else:
            records[-1]["expert_out"] = results.pop(0)
        middle, second_low, gate, buffer = results[:4]
        gather = fast and l < LAYERS - 1
        received, returned, up_eff, down_eff, *more = expert_call(
            functools.partial(expert_forward_kernel, dp, mp, l, gather),
            [buffer.reshape(EXPERTS, SLOTS, width)],
            [
                (block_rows, bf16),
                (block_rows, bf16),
                ((width, hidden), bf16),
                ((hidden, width), bf16),
            ],
            [
                pltpu.VMEM(block_rows, bf16),
                pltpu.VMEM((8, LANES) if fast else (width, hidden), f32),
                pltpu.VMEM(gathered_shapes[2], bf16),
                pltpu.VMEM(gathered_shapes[3], bf16),
                pltpu.VMEM((width, hidden), bf16),
                pltpu.VMEM((hidden, width), bf16),
                pltpu.SemaphoreType.DMA((4,)),
            ]
            + (WeightGather.scratch(4) if gather else []),
            dp, l, f"experts_{l}", 4 * dp * SLOTS * width * hidden,
            [gathered[l][2], gathered[l][3], residual_up, residual_down, *(shards if gather else ())],
            [(shape, bf16) for shape in gathered_shapes] if gather else (),
        )
        if gather:
            gathered[l + 1] = more
        returned = by_piece(returned)
        before = (middle, gate, returned)
        records.append(
            dict(
                carried=carried, middle=middle, second_low=second_low, gate=gate, saved=results[4:], received=received,
                up_eff=up_eff, down_eff=down_eff,
            )
        )

    top = records[-1]
    block_output, grad, logit_grad, router_part, buffer = image_call(
        turn_kernel,
        images,
        [
            ("image", before[0]),
            ("image", before[1]),
            ("whole", before[2]),
            ("image", cotangent),
            ("whole", enter),
            ("whole", leave),
            ("image", col_form),
            ("image", row_form),
            ("image", top["second_low"]),
            (LAYERS - 1, routers),
        ],
        [
            ("image", patches.shape, bf16),
            ("image", token, f32),
            ("image", (images, IMGROWS, LANES), f32),
            ("whole", (LANES, width), f32),
            ("whole", buffer_shape, bf16),
        ],
        [pltpu.VMEM(buffer_shape, f32)],
        "turn",
    )
    router_parts, tables, smalls = [None] * LAYERS, [None] * LAYERS, [None] * LAYERS
    residual_sums, shard_sums = [None] * LAYERS, [None] * LAYERS
    router_parts[LAYERS - 1] = router_part
    units, attn_units, mines = [None] * LAYERS, [None] * LAYERS, [None] * LAYERS
    for l in reversed(range(LAYERS)):
        rec = records[l]
        last = l == 0
        reduce = fast and l < LAYERS - 1
        arrays = [buffer.reshape(EXPERTS, SLOTS, width), rec["received"], rec["up_eff"], rec["down_eff"]]
        outs = [(block_rows, bf16)]
        scratch = [
            pltpu.VMEM(block_rows, bf16),
            pltpu.VMEM((dp, SLOTS, hidden), bf16),
            pltpu.VMEM((dp, SLOTS, hidden), f32),
            pltpu.VMEM((dp, SLOTS, hidden), bf16),
            pltpu.VMEM(block_rows, bf16),
        ]
        if fast:
            outs.append(((2, mp, width, width), bf16))
            scratch += [pltpu.VMEM((width, hidden), f32)] * 2
        else:
            outs += [((width, hidden), f32)] * 2
        if reduce:
            arrays += [mines[l + 1], attn_units[l + 1]]
            outs += [((2, mp, width, width), bf16), ((width, width), bf16)]
            scratch += RowSum.scratch(1, width) + RowGather.scratch(2)
        results = list(
            expert_call(
                functools.partial(expert_backward_kernel, dp, mp, fast, reduce), arrays, outs, scratch, dp, LAYERS + l,
                f"experts_back_{l}", 10 * dp * SLOTS * width * hidden,
            )
        )
        returned_grad = results.pop(0)
        if fast:
            units[l] = results.pop(0)
        else:
            residual_sums[l] = lax.psum(tuple(t.astype(bf16) for t in results[:2]), "mp")
        if reduce:
            full_above, mine_above = results
        window_in, qk, v, probs, att, proj_full = rec["saved"]
        qkv_full = gathered[l][0].reshape(3 * width, width)
        arrays = [
            ("smem", image_valid),
            ("image", grad),
            ("whole", by_piece(returned_grad)),
            ("image", logit_grad),
            ("image", rec["middle"]),
            ("image", rec["carried"]),
            (l, routers),
            ("image", col_form),
            ("whole", moves[l]),
            ("whole", backs[l]),
            (l, norm_gain),
            ("whole", proj_full),
            ("whole", qkv_full),
            ("image", window_in),
            ("image", qk),
            ("image", v),
            ("image", probs),
            ("image", att),
        ]
        outs = [("image", patches.shape if last else token, f32)]
        scratch = [pltpu.VMEM((3 * width, (2 - images % 2) * IMGROWS), bf16)]
        closes = fast and last
        table_shape, small_shape = (HEADS, WPAD, LANES), (8, width)
        if fast:
            arrays.append(("whole", units[l]))
            scratch += [pltpu.VMEM((3 * width, width), f32), pltpu.VMEM((width, width), f32)]
        if closes:
            outs += [
                ("whole", (2, mp, width, width), bf16),
                ("whole", (3, width, width), bf16),
                ("whole", (Closing.lines, width), f32),
                ("whole", (3, width, width), bf16),
            ]
        else:
            if fast:
                outs += [
                    ("whole", (width // 2, width), bf16),
                    ("whole", (mp, width, width), bf16),
                    ("whole", (2, width, width), bf16),
                ]
            else:
                outs += [("whole", (3 * width, width), f32), ("whole", (width, width), f32)]
            outs += [("whole", table_shape, f32), ("whole", small_shape, f32)]
        if last:
            arrays.append(("whole", leave))
            if fast:
                arrays += [
                    ("whole", a)
                    for a in (
                        tables[1], smalls[1], router_parts[1], router_parts[0], entry_col, halves_above, mines[1],
                        mine_above,
                    )
                ]
        else:
            below = records[l - 1]
            arrays += [
                ("image", row_form),
                ("image", below["expert_out"]),
                ("image", below["second_low"]),
                (l - 1, routers),
            ]
            outs += [
                ("image", (images, IMGROWS, LANES), f32),
                ("whole", (LANES, width), f32),
                ("whole", buffer_shape, bf16),
            ]
            scratch.append(pltpu.VMEM(buffer_shape, f32))
        if closes:
            scratch += [
                pltpu.VMEM(table_shape, f32),
                pltpu.VMEM(small_shape, f32),
                pltpu.VMEM((mp, width, width), bf16),
                pltpu.VMEM((Closing.lines, width), f32),
            ]
            scratch += [pltpu.VMEM(shape, dtype) for _, shape, dtype in outs[1:5]] + Closing.scratch(dp, width)
        elif fast:
            scratch += RowSum.scratch(2, width) + [pltpu.VMEM((width // 2, width), bf16)]
            scratch += [pltpu.SemaphoreType.DMA((1,))] * 2
        results = list(
            image_call(
                functools.partial(attention_backward_kernel, last, dp, mp, fast),
                images, arrays, outs, scratch, f"attend_back_{l}", 2 * LAYERS + 1 + l if fast else None,
            )
        )
        grad = results.pop(0)
        if closes:
            full, closed, lines, shard_above = results
            continue
        if fast:
            halves_above = results.pop(0)
            attn_units[l], mines[l] = results[:2]
        else:
            qkv_part, proj_part = results[:2]
        tables[l], smalls[l] = results[2:4]
        if not last:
            logit_grad, router_parts[l - 1], buffer = results[4:]
        if fast:
            continue
        attn = (
            lax.psum_scatter(qkv_part.astype(bf16), "mp", scatter_dimension=0, tiled=True),
            lax.psum_scatter(proj_part.T.astype(bf16), "mp", scatter_dimension=0, tiled=True),
        )
        up_sum, down_sum = residual_sums[l]
        if split > 1:
            begin = lax.axis_index("dp") % split * hidden
            empty = jnp.zeros((width, hidden_full), bf16)
            up_sum = lax.dynamic_update_slice_in_dim(empty, up_sum, begin, 1)
            down_sum = lax.dynamic_update_slice_in_dim(empty, down_sum, begin, 1)
        up_columns, down_columns = core_up.shape[-1], core_down.shape[-1]
        up_shard = lax.dynamic_slice_in_dim(up_sum, row_index * up_columns, up_columns, 1)
        down_shard = lax.dynamic_slice_in_dim(down_sum, row_index * down_columns, down_columns, 0)
        shard_sums[l] = lax.psum((attn[0], attn[1], up_shard, down_shard), "dp")

    if fast:
        *attn_grads, core_up_grad, core_down_grad, residual_up_grad, residual_down_grad = format_call(
            [full, full_above], [closed, shard_above], qkv_weight.shape[-1]
        )
        attn_grads = [a.transpose(0, 2, 1) for a in attn_grads]
        core_grads = (core_up_grad, core_down_grad.transpose(0, 2, 1))
        at = LAYERS * HEADS
        table_sum = lines[:at, :OFFSETS]
        router_sum = lines[at : at + LAYERS * EXPERTS].reshape(LAYERS, EXPERTS, width)
        at += LAYERS * EXPERTS
        small_sum = lines[at : at + LAYERS * 8].reshape(LAYERS, 8, width)[:, :4]
    else:
        entry = cell_entries()[None, :] + np.array([key_base_of(key) for key in range(WPAD)])[:, None]
        entry = jnp.asarray(np.where(np.arange(WPAD)[:, None] < WINPOS, entry, -1).reshape(-1))
        entry_turned = (entry[:, None] == jnp.arange(OFFSETS)[None, :]).astype(f32)
        table_part = jnp.dot(
            jnp.stack(tables, 0).reshape(LAYERS * HEADS, WPAD * LANES), entry_turned, precision=highest
        )
        small_part = jnp.stack(smalls, 0)[:, :4]
        router_part = jnp.stack(router_parts, 0)[:, :EXPERTS]
        table_sum, small_sum, router_sum = lax.psum((table_part, small_part, router_part), ("dp", "mp"))

        def shard(k):
            return jnp.stack([shard_sums[l][k] for l in range(LAYERS)], 0).astype(f32)

        attn_grads = (shard(0).transpose(0, 2, 1), shard(1).transpose(0, 2, 1))
        core_grads = (shard(2), shard(3).transpose(0, 2, 1))
        residual_up_grad, residual_down_grad = (
            jnp.stack([residual_sums[l][k] for l in range(LAYERS)], 0).astype(f32) for k in range(2)
        )
        residual_up_grad = residual_up_grad[:, None]
        residual_down_grad = residual_down_grad.transpose(0, 2, 1)[:, None]

    return (
        block_output,
        grad,
        attn_grads[0],
        attn_grads[1],
        core_grads[0],
        core_grads[1],
        residual_up_grad,
        residual_down_grad,
        table_sum.reshape(LAYERS, HEADS, OFFSETS).transpose(0, 2, 1),
        router_sum.transpose(0, 2, 1),
        small_sum[:, 0:2],
        small_sum[:, 2:4],
    )


def solution(mesh):
    placed = (
        P(("dp", "mp"), None, None),
        P(None, None, "mp"),
        P(None, None, "mp"),
        P(None, None, "mp"),
        P(None, None, "mp"),
        P(None, "dp", None, None),
        P(None, "dp", None, None),
        P(),
        P(),
        P(),
        P(),
        P(("dp", "mp"), None, None),
        P(("dp", "mp")),
        P(("dp", "mp"), None),
        P(("dp", "mp"), None),
        P(("dp", "mp"), None, None),
    )
    return jax.shard_map(
        per_device,
        mesh=mesh,
        in_specs=placed,
        out_specs=(
            P(("dp", "mp"), None, None),
            P(("dp", "mp"), None, None),
            P(None, None, "mp"),
            P(None, None, "mp"),
            P(None, None, "mp"),
            P(None, None, "mp"),
            P(None, "dp", None, None),
            P(None, "dp", None, None),
            P(),
            P(),
            P(),
            P(),
        ),
        check_vma=False,
    )
```

```python
import functools

import jax
import jax.numpy as jnp
import numpy as np
from jax import lax
from jax.experimental import pallas as pl
from jax.experimental.pallas import tpu as pltpu
from jax.sharding import PartitionSpec as P

HEADS = 12
HEAD_DIM = 32
EXPERTS = 8
WINDOW = 7
GRID = 14
SHIFT = 3
LAYERS = 2
WINPOS = 49
OFFSETS = 169
CAP = 122

WPAD = 64
IMGROWS = 256
PATCHES = 196
SLOTS = 128
ROWS = EXPERTS * SLOTS
LANES = 128
GROUP = 4
PAIRS = 2
TABLE = 256

bf16 = jnp.bfloat16
f32 = jnp.float32
highest = lax.Precision.HIGHEST
norm_epsilon = 1e-05
mask_fill = -100.0
head_scale = HEAD_DIM ** (-0.5)
MESH = pl.DeviceIdType.MESH
MIB = 1024 * 1024


def nn(a, b):
    return lax.dot_general(a, b, (((1,), (0,)), ((), ())), preferred_element_type=f32)


def nt(a, b):
    return lax.dot_general(a, b, (((1,), (1,)), ((), ())), preferred_element_type=f32)


def tn(a, b):
    return lax.dot_general(a, b, (((0,), (0,)), ((), ())), preferred_element_type=f32)


def iota(shape, dim):
    return lax.broadcasted_iota(jnp.int32, shape, dim)


def onehot(flags):
    return jnp.where(flags, 1.0, 0.0).astype(bf16)


def natural_of_row(shifted):
    moved = SHIFT if shifted else 0
    blocks = GRID // WINDOW
    out = -np.ones(IMGROWS, np.int32)
    for window in range(blocks * blocks):
        for cell in range(WINPOS):
            row = (window // blocks * WINDOW + cell // WINDOW + moved) % GRID
            col = (window % blocks * WINDOW + cell % WINDOW + moved) % GRID
            out[window * WPAD + cell] = row * GRID + col
    return out


def key_base_of(key):
    return (2 * WINDOW) * (WINDOW - 1) - (key // WINDOW * (2 * WINDOW - 1) + key % WINDOW)


def enter_table():
    held = natural_of_row(False)
    return (held[:, None] == np.arange(PATCHES)[None, :]).astype(np.float32)


def move_table(shifted):
    first, second = natural_of_row(False), natural_of_row(shifted)
    same = (second[:, None] == first[None, :]) & (second[:, None] >= 0)
    return same.astype(np.float32)


def cell_entries():
    cell = np.arange(LANES) % WPAD
    return np.where(cell < WINPOS, cell // WINDOW * (2 * WINDOW - 1) + cell % WINDOW, -4 * TABLE).astype(np.int32)


def norm_parts(x):
    width = x.shape[-1]
    center = x - jnp.sum(x, -1, keepdims=True) * (1.0 / width)
    spread = jnp.sum(center * center, -1, keepdims=True) * (1.0 / width)
    rstd = lax.rsqrt(spread + norm_epsilon)
    return center * rstd, rstd


def norm_back(grad, gain, xhat, rstd):
    width = xhat.shape[-1]
    dxhat = grad * gain
    mean_one = jnp.sum(dxhat, -1, keepdims=True) * (1.0 / width)
    mean_two = jnp.sum(dxhat * xhat, -1, keepdims=True) * (1.0 / width)
    return rstd * (dxhat - mean_one - xhat * mean_two)


def turn_blocks(x):
    size = x.shape[0]
    same = onehot(iota((size, size), 0) == iota((size, size), 1))
    return jnp.concatenate([nt(same, x[:, at : at + size]) for at in range(0, x.shape[1], size)], 0)


def split_two(x):
    high = x.astype(bf16)
    return high, (x - high.astype(f32)).astype(bf16)


def collect(pos_col, returned_ref):
    pick = onehot(pos_col == iota((pos_col.shape[0], ROWS), 1))
    out = nn(pick, returned_ref[0])
    for piece in range(1, returned_ref.shape[0]):
        out = out + nn(pick, returned_ref[piece])
    return out


def join(ref):
    return ref[...].reshape(ref.shape[0] * ref.shape[1], *ref.shape[2:])


def store(ref, rows):
    ref[...] = rows.reshape(ref.shape).astype(ref.dtype)


def per_image(function, count):
    return jnp.concatenate([function(i) for i in range(count)], 0)


def image_rows(i):
    return slice(i * IMGROWS, (i + 1) * IMGROWS)


def lay_positions(row_ref):
    return jnp.concatenate([row_ref[i, 0:1, :] for i in range(row_ref.shape[0])], 1)


def spread_rows(pos_row, rows_low):
    return nn(onehot(iota((ROWS, pos_row.shape[1]), 0) == pos_row), rows_low)


def route(second_low, router, pos_col):
    logits = nt(second_low, router)
    lane = iota(logits.shape, 1)
    logits = jnp.where(lane < EXPERTS, logits, -1e30)
    expo = jnp.exp(logits - jnp.max(logits, -1, keepdims=True))
    probs = expo / jnp.sum(expo, -1, keepdims=True)
    expert = jnp.where(pos_col >= 0, pos_col // SLOTS, -1)
    chosen = jnp.where(lane == expert, 1.0, 0.0)
    return probs, chosen, jnp.sum(probs * chosen, -1, keepdims=True)


def head_masks():
    rows = iota((LANES, LANES), 0) // HEAD_DIM
    return [onehot(rows == h) for h in range(GROUP)]


def lane_masks():
    lane = iota((WPAD, LANES), 1)
    return [onehot(lane < WPAD), onehot(lane >= WPAD)]


def keys_entry(cells, key_row, turned):
    parts = [cells + (key_base_of(col) - key_row * (2 * WINDOW - 1)) for col in range(WINDOW)]
    return jnp.concatenate(parts, 0 if turned else 1)


def form_bias(bias_ref, table_ref, entry_row):
    layers, heads = bias_ref.shape[:2]
    lines = layers * heads
    bias_ref[...] = jnp.where(iota(bias_ref.shape, 2) < WINPOS, 0.0, -1e30)
    table = table_ref[...]
    high = table.astype(bf16)
    mid, low = split_two(table - high.astype(f32))
    parts = jnp.concatenate([high.astype(f32), mid.astype(f32), low.astype(f32)], 0).astype(bf16)

    def step(key_row, carry):
        pick = onehot(iota((TABLE, WINDOW * LANES), 0) == keys_entry(entry_row, key_row, False))
        rows = nn(parts, pick)
        rows = rows[:lines] + rows[lines : 2 * lines] + rows[2 * lines :]
        for col in range(WINDOW):
            for layer in range(layers):
                part = rows[layer * heads : (layer + 1) * heads, col * LANES : (col + 1) * LANES]
                bias_ref[layer, :, pl.ds(key_row * WINDOW + col, 1), :] = part.reshape(heads, 1, LANES)
        return carry

    lax.fori_loop(0, WINDOW, step, 0)


def table_grad(parts, entry_col):
    heads = parts[0].shape[0]
    lines = heads * len(parts)

    def step(key_row, total):
        keys = [
            jnp.concatenate([ref[:, pl.ds(key_row * WINDOW + col, 1), :].reshape(heads, LANES) for ref in parts], 0)
            for col in range(WINDOW)
        ]
        rows = jnp.concatenate(keys, 1)
        high = rows.astype(bf16).astype(f32)
        both = jnp.concatenate([high, rows - high], 0).astype(bf16)
        entry = keys_entry(entry_col, key_row, True)
        out = nn(both, onehot(iota((WINDOW * LANES, TABLE), 1) == entry))
        return total + out[:lines] + out[lines:]

    return lax.fori_loop(0, WINDOW, step, jnp.zeros((lines, TABLE), f32))


def attention_forward_kernel(first, shifted, mp, gather, *refs):
    refs = list(refs)
    if first:
        patches_ref, enter_ref = refs[:2]
        refs = refs[2:]
    else:
        prev_ref, prev_gate_ref, returned_ref = refs[:3]
        refs = refs[3:]
    (
        valid_ref, col_ref, row_ref, qkv_ref, proj_ref, bias_ref, move_ref, back_ref, gain_ref, nbias_ref, router_ref,
    ) = refs[:11]
    gain_ref, nbias_ref, router_ref = (ref.at[0] for ref in (gain_ref, nbias_ref, router_ref))
    refs = refs[11:]
    if first:
        table_ref, entry_ref = bias_ref, refs.pop(0)
    if gather:
        core_up_ref, core_down_ref = refs[:2]
        refs = refs[2:]
    carried_ref = refs.pop(0)
    if first:
        biases_ref = refs.pop(0)
        bias_ref = biases_ref.at[0]
    else:
        expert_out_ref = refs.pop(0)
        bias_ref = bias_ref.at[0]
    middle_ref, second_ref, gate_ref, buffer_ref, window_ref, qk_ref, v_ref, probs_ref, att_ref, proj_full = refs[:10]
    refs = refs[10:]
    if gather:
        qkv_full = refs.pop(0)
        up_out, down_out = refs[:2]
        refs = refs[2:]
    total_ref = refs.pop(0)
    step = pl.program_id(0)
    final = pl.num_programs(0) - 1
    count, _, width = carried_ref.shape
    if gather:
        shards = [ref.at[0] for ref in (qkv_ref, proj_ref, core_up_ref, core_down_ref)]
        qkv_ref, proj_ref = refs[:2]
        moving = WeightGather(shards, [qkv_ref, proj_ref, up_out, down_out], refs[2:])

        @pl.when(step == 0)
        def _():
            pl.semaphore_wait(moving.row.greet(), 2)
            for k in (0, 1):
                moving.start(k)
            form_bias(biases_ref, table_ref, entry_ref[...])

    pos_col = join(col_ref)[:, 0:1]
    if first:
        x = per_image(lambda i: nn(enter_ref[...], patches_ref[i]), count)
    else:
        expert_out = collect(pos_col, returned_ref)
        store(expert_out_ref, expert_out)
        x = join(prev_ref) + join(prev_gate_ref) * expert_out
    store(carried_ref, x)
    xhat, _ = norm_parts(x)
    normed = (xhat * gain_ref[0:1, :] + nbias_ref[0:1, :]).astype(bf16)
    window_in = per_image(lambda i: nn(move_ref[...], normed[image_rows(i)]), count).astype(bf16)
    store(window_ref, window_in)

    @pl.when(step == 0)
    def _():
        if gather:
            for k in (0, 1):
                moving.forward(k)
            for k in (2, 3):
                moving.start(k)
            for k in (0, 1):
                moving.arrive(k)
            qkv_full[...] = join(qkv_ref)
        elif first:
            form_bias(biases_ref, table_ref, entry_ref[...])
        proj_full[...] = join(proj_ref).astype(f32).T.astype(bf16)
        total_ref[...] = jnp.zeros(total_ref.shape, f32)

    qkv = join(qkv_ref)
    turned = nt(qkv, window_in).astype(bf16)
    straight = nt(window_in, qkv[width:]).astype(bf16)
    for i in range(count):
        qk_ref[i] = turned[: 2 * width, image_rows(i)]
    store(v_ref, straight[:, width:])
    heads_rows = head_masks()
    halves = lane_masks()
    low_lane = iota((WPAD, LANES), 1) < WPAD
    if shifted:
        row_labels = [nt(row_ref[i].astype(f32).astype(bf16), move_ref[...]) for i in range(count)]
        col_labels = [nn(move_ref[...], col_ref[i].astype(f32).astype(bf16)) for i in range(count)]
    for pair in range(PAIRS * count):
        image, side = pair // PAIRS, pair % PAIRS
        across = slice(pair * LANES, (pair + 1) * LANES)
        within = slice(side * LANES, (side + 1) * LANES)
        if shifted:
            ahead = col_labels[image][side * LANES : side * LANES + WPAD, 1:2]
            behind = col_labels[image][side * LANES + WPAD : (side + 1) * LANES, 1:2]
            key_label = jnp.where(low_lane, ahead, behind)
            mask = jnp.where(key_label == row_labels[image][1:2, within], 0.0, mask_fill)
        for group in range(HEADS // GROUP):
            features = slice(group * LANES, (group + 1) * LANES)
            queries = turned[features, across]
            spread = jnp.concatenate([queries * heads_rows[h] for h in range(GROUP)], 1)
            raw = nn(straight[across, features], spread)
            for h in range(GROUP):
                head = group * GROUP + h
                part = raw[:, h * LANES : (h + 1) * LANES]
                scores = jnp.where(low_lane, part[:WPAD], part[WPAD:]) * head_scale + bias_ref[head]
                if shifted:
                    scores = scores + mask
                expo = jnp.exp(scores - jnp.max(scores, 0, keepdims=True))
                probs = (expo * (1.0 / jnp.sum(expo, 0, keepdims=True))).astype(bf16)
                probs_ref[image, side * HEADS + head] = probs
                both = jnp.concatenate([probs * halves[0], probs * halves[1]], 0)
                at = slice(head * HEAD_DIM, (head + 1) * HEAD_DIM)
                values = turned[2 * width + head * HEAD_DIM : 2 * width + (head + 1) * HEAD_DIM, across]
                att_ref[image, at, within] = nn(values, both).astype(bf16)
    attended = per_image(lambda i: nt(back_ref[...], att_ref[i]), count).astype(bf16)
    branch = nt(attended, join(proj_ref))
    middle = x + per_image(lambda i: valid_ref[step * count + i].astype(f32) * branch[image_rows(i)], count)
    store(middle_ref, middle)
    xhat, _ = norm_parts(middle)
    second_low = (xhat * gain_ref[1:2, :] + nbias_ref[1:2, :]).astype(bf16)
    store(second_ref, second_low)
    _, _, gate = route(second_low, router_ref[...], pos_col)
    store(gate_ref, gate)
    total_ref[...] += spread_rows(lay_positions(row_ref), second_low)

    @pl.when(step == final)
    def _():
        buffer_ref[...] = total_ref[...].astype(bf16)
        if gather:
            for k in (2, 3):
                moving.forward(k)
            for k in (2, 3):
                moving.arrive(k)
            for k in range(4):
                moving.sent(k)


def image_spec(array_shape, count):
    rest = tuple(array_shape[1:])
    zeros = (0,) * len(rest)
    return pl.BlockSpec((count,) + rest, lambda i: (i,) + zeros)


def whole_spec(array_shape):
    zeros = (0,) * len(array_shape)
    return pl.BlockSpec(tuple(array_shape), lambda i: zeros)


def image_call(kernel, images, arrays, outs, scratch, name, collective_id=None):
    count = 2 - images % 2

    def spec(kind, shape):
        if isinstance(kind, int):
            rest = tuple(shape[1:])
            return pl.BlockSpec((1,) + rest, lambda i: (kind,) + (0,) * len(rest))
        if kind in ("smem", "any"):
            return pl.BlockSpec(memory_space=pltpu.SMEM if kind == "smem" else pl.ANY)
        return image_spec(shape, count) if kind == "image" else whole_spec(shape)

    return pl.pallas_call(
        kernel,
        grid=(images // count,),
        out_shape=[jax.ShapeDtypeStruct(shape, dtype) for _, shape, dtype in outs],
        in_specs=[spec(kind, array.shape) for kind, array in arrays],
        out_specs=[spec(kind, shape) for kind, shape, _ in outs],
        scratch_shapes=scratch,
        compiler_params=pltpu.CompilerParams(
            vmem_limit_bytes=51 * MIB,
            dimension_semantics=("arbitrary",),
            collective_id=collective_id,
            has_side_effects=collective_id is not None,
        ),
        name=name,
    )(*[array for _, array in arrays])


def send_part(g, expert_out, second_low, router, pos_col, pos_row, logit_ref, router_grad_ref, total_ref):
    probs, chosen, gate = route(second_low, router, pos_col)
    gate_grad = jnp.where(pos_col >= 0, jnp.sum(g * expert_out, -1, keepdims=True), 0.0)
    sent = (gate * g).astype(bf16)
    logit_grad = gate_grad * gate * (chosen - probs)
    store(logit_ref, logit_grad)
    high, low = split_two(logit_grad)
    router_grad_ref[...] += tn(high, second_low) + tn(low, second_low)
    total_ref[...] += spread_rows(pos_row, sent)


def turn_kernel(
    prev_ref, gate_ref, returned_ref, cotangent_ref, enter_ref, leave_ref, col_ref, row_ref, second_ref, router_ref,
    block_ref, grad_ref, logit_ref, router_grad_ref, buffer_ref, total_ref,
):
    step = pl.program_id(0)
    count = cotangent_ref.shape[0]

    @pl.when(step == 0)
    def _():
        total_ref[...] = jnp.zeros(total_ref.shape, f32)
        router_grad_ref[...] = jnp.zeros(router_grad_ref.shape, f32)

    pos_col = join(col_ref)[:, 0:1]
    expert_out = collect(pos_col, returned_ref)
    x = (join(prev_ref) + join(gate_ref) * expert_out).astype(bf16)
    for i in range(count):
        block_ref[i] = nn(leave_ref[...], x[image_rows(i)]).astype(bf16)
    g = per_image(lambda i: nn(enter_ref[...], cotangent_ref[i]), count)
    store(grad_ref, g)
    send_part(
        g, expert_out, join(second_ref), router_ref[0], pos_col, lay_positions(row_ref), logit_ref, router_grad_ref, total_ref
    )

    @pl.when(step == pl.num_programs(0) - 1)
    def _():
        buffer_ref[...] = total_ref[...].astype(bf16)


def attention_backward_kernel(last, dp, mp, fast, *refs):
    (
        valid_ref, grad_ref, returned_ref, logit_ref, middle_ref, carried_ref, router_ref, col_ref, move_ref, back_ref,
        gain_ref, proj_ref, qkv_ref, window_ref, qk_ref, v_ref, probs_ref, att_ref,
    ) = refs[:18]
    refs = refs[18:]
    refs = list(refs)
    if fast:
        units_ref = refs.pop(0)
    if last:
        leave_ref = refs.pop(0)
        if fast:
            table_above, small_above, router_above, router_here, entry_ref, half_above, down_above, attn_above = refs[:8]
            refs = refs[8:]
    else:
        row_ref, expert_out_ref, second_ref, router_next_ref = refs[:4]
        refs = refs[4:]
    out_ref = refs.pop(0)
    closing = None
    if fast and last:
        results, refs = refs[:4], refs[4:]
    else:
        if fast:
            halves_ref = refs.pop(0)
            unit_ref, mine_ref = refs[:2]
        else:
            qkv_grad_ref, proj_grad_ref = refs[:2]
        table_ref, small_ref = refs[2:4]
        refs = refs[4:]
    if not last:
        logit_out_ref, router_grad_ref, buffer_ref = refs[:3]
        refs = refs[3:]
    turned = refs.pop(0)
    if fast:
        qkv_grad_ref, proj_grad_ref = refs[:2]
        refs = refs[2:]
    if not last:
        total_ref = refs.pop(0)
    step = pl.program_id(0)
    final = pl.num_programs(0) - 1
    count, _, width = carried_ref.shape
    if fast:
        row = Row()
        if last:
            table_ref, small_ref, unit_ref, lines_ref = refs[:4]
            landing, refs = refs[4:8], refs[8:]
            above = (half_above, down_above.at[1], attn_above)
            closing = Closing(row, dp, units_ref, unit_ref, lines_ref, above, landing, refs)
        else:
            sums = RowSum(row, blocks(units_ref), refs[0], refs[1], refs[2], blocks(mine_ref), refs[3:7])
            across_x = DeepSum(dp, [mine_ref.at[0]], [refs[7]], [halves_ref], [None], [None], refs[8:10] * 4)

        def take(k):
            if closing:
                closing.take(k)
            else:
                sums.end(k)
                if k == 0:
                    across_x.over_x(k).start()

        @pl.when(step == 0)
        def _():
            if closing:
                closing.enter()
            else:
                barrier = row.greet()
                pl.semaphore_wait(barrier, 2 + across_x.greet(barrier, False))
                for k in range(2):
                    sums.start(k)

    @pl.when(step == 0)
    def _():
        qkv_grad_ref[...] = jnp.zeros(qkv_grad_ref.shape, f32)
        proj_grad_ref[...] = jnp.zeros(proj_grad_ref.shape, f32)
        table_ref[...] = jnp.zeros(table_ref.shape, f32)
        small_ref[...] = jnp.zeros(small_ref.shape, f32)
        if not last:
            total_ref[...] = jnp.zeros(total_ref.shape, f32)
            router_grad_ref[...] = jnp.zeros(router_grad_ref.shape, f32)

    pos_col = join(col_ref)[:, 0:1]
    g = join(grad_ref)
    high, low = split_two(join(logit_ref))
    gain_ref, router = gain_ref.at[0], router_ref[0]
    normed_grad = collect(pos_col, returned_ref) + nn(high, router) + nn(low, router)
    xhat, rstd = norm_parts(join(middle_ref))
    small_ref[1:2, :] += jnp.sum(normed_grad * xhat, 0, keepdims=True)
    small_ref[3:4, :] += jnp.sum(normed_grad, 0, keepdims=True)
    middle_grad = g + norm_back(normed_grad, gain_ref[1:2, :], xhat, rstd)

    def branch_part(i):
        low_part = (valid_ref[step * count + i].astype(f32) * middle_grad[image_rows(i)]).astype(bf16)
        return nn(move_ref[...], low_part)

    branch_grad = per_image(branch_part, count).astype(bf16)
    for i in range(count):
        proj_grad_ref[...] += nn(att_ref[i], branch_grad[image_rows(i)])
    att_grad = nt(proj_ref[...], branch_grad).astype(bf16)
    if fast:

        @pl.when(step == 0)
        def _():
            if closing:
                closing.early()
            else:
                for k in range(2):
                    sums.middle(k)

        pl.when(step == final)(functools.partial(take, 0))

    heads_rows = head_masks()
    halves = lane_masks()
    low_lane = iota((WPAD, LANES), 1) < WPAD
    for pair in range(PAIRS * count):
        image, side = pair // PAIRS, pair % PAIRS
        across = slice(pair * LANES, (pair + 1) * LANES)
        within = slice(side * LANES, (side + 1) * LANES)
        for group in range(HEADS // GROUP):
            features = slice(group * LANES, (group + 1) * LANES)
            grads = att_grad[features, across]
            spread = jnp.concatenate([grads * heads_rows[h] for h in range(GROUP)], 1)
            raw = nn(v_ref[image, within, features], spread)
            for h in range(GROUP):
                head = group * GROUP + h
                at = slice(head * HEAD_DIM, (head + 1) * HEAD_DIM)
                below = slice(width + head * HEAD_DIM, width + (head + 1) * HEAD_DIM)
                lowest = slice(2 * width + head * HEAD_DIM, 2 * width + (head + 1) * HEAD_DIM)
                part = raw[:, h * LANES : (h + 1) * LANES]
                probs_grad = jnp.where(low_lane, part[:WPAD], part[WPAD:])
                probs_low = probs_ref[image, side * HEADS + head]
                probs = probs_low.astype(f32)
                weighted = probs * probs_grad
                scores_grad = weighted - probs * jnp.sum(weighted, 0, keepdims=True)
                table_ref[head] += scores_grad
                scores_low = scores_grad.astype(bf16)
                both = jnp.concatenate([scores_low * halves[0], scores_low * halves[1]], 0)
                probs_both = jnp.concatenate([probs_low * halves[0], probs_low * halves[1]], 0)
                turned[at, across] = (nn(qk_ref[image, below, within], both) * head_scale).astype(bf16)
                turned[below, across] = (nt(qk_ref[image, at, within], both) * head_scale).astype(bf16)
                turned[lowest, across] = nt(att_grad[at, across], probs_both).astype(bf16)
    qkv_grad_ref[...] += nn(turned[...], join(window_ref))
    if fast:

        @pl.when(step == final)
        def _():
            columns, rows = 3 * width // mp, width // mp
            proj_turned = proj_grad_ref[...].T
            for place in range(mp):
                q = quarter_at(place, mp)
                unit_ref[place, :columns] = qkv_grad_ref[q * columns : (q + 1) * columns].astype(bf16)
                unit_ref[place, columns:] = proj_turned[q * rows : (q + 1) * rows].astype(bf16)
            if closing:
                closing.open()
            take(1)
            if closing:
                heads = 2 * HEADS
                lines_ref[...] = jnp.zeros(lines_ref.shape, f32)
                lines_ref[:heads, :TABLE] = table_grad([table_ref, table_above], entry_ref[...])

    mixed_grad = per_image(lambda i: nt(back_ref[...], turned[:, image_rows(i)]), count).astype(bf16)
    first_grad = nn(mixed_grad, qkv_ref[...])
    if closing:

        @pl.when(step == final)
        def _():
            closing.cross()

    xhat, rstd = norm_parts(join(carried_ref))
    small_ref[0:1, :] += jnp.sum(first_grad * xhat, 0, keepdims=True)
    small_ref[2:3, :] += jnp.sum(first_grad, 0, keepdims=True)
    if closing:

        @pl.when(step == final)
        def _():
            heads = 2 * HEADS
            lines_ref[heads : heads + EXPERTS] = router_here[:EXPERTS]
            lines_ref[heads + EXPERTS : heads + 2 * EXPERTS] = router_above[:EXPERTS]
            lines_ref[heads + 2 * EXPERTS : heads + 2 * EXPERTS + 8] = small_ref[...]
            lines_ref[heads + 2 * EXPERTS + 8 : heads + 2 * EXPERTS + 16] = small_above[...]
            closing.send_lines()

    out = middle_grad + norm_back(first_grad, gain_ref[0:1, :], xhat, rstd)
    if last:
        top = out.astype(bf16)
        rest = out - top.astype(f32)
        mid, low = split_two(rest)
        leave = leave_ref[...]
        for i in range(count):
            at = image_rows(i)
            out_ref[i] = nn(leave, top[at]) + nn(leave, mid[at]) + nn(leave, low[at])
    else:
        store(out_ref, out)
        send_part(
            out, join(expert_out_ref), join(second_ref), router_next_ref[0], pos_col, lay_positions(row_ref), logit_out_ref,
            router_grad_ref, total_ref,
        )

    @pl.when(step == final)
    def _():
        if not last:
            buffer_ref[...] = total_ref[...].astype(bf16)
        if closing:
            closing.finish()
            for out, landed in zip(results, landing):
                out[...] = landed[...]
        elif fast:
            across_x.halve(0)
            across_x.over_x(0).wait_send()
            for k in range(2):
                sums.finish(k)


def quarter_at(place, mp):
    return place % (mp // 2) * 2 + place // (mp // 2)


def add_up(*parts):
    total = parts[0].astype(f32)
    for part in parts[1:]:
        total = total + part.astype(f32)
    return total


def to_row(source, target, sems, k, row):
    return pltpu.make_async_remote_copy(
        src_ref=source,
        dst_ref=target,
        send_sem=sems[0].at[k],
        recv_sem=sems[1].at[k],
        device_id={"mp": row},
        device_id_type=MESH,
    )


class Row:
    def __init__(self):
        row = lax.axis_index("mp")
        self.row, self.core, self.y = row, lax.rem(row, 2), lax.div(row, 2)
        self.sibling, self.across = row + 1 - 2 * self.core, row + 2 - 4 * self.y
        self.place = self.core * 2 + self.y
        self.place_across = self.core * 2 + 1 - self.y

    def greet(self):
        barrier = pltpu.get_barrier_semaphore()
        for row in (self.sibling, self.across):
            pl.semaphore_signal(barrier, inc=1, device_id={"mp": row}, device_id_type=MESH)
        return barrier


class RowSum:
    semaphores = 4

    def __init__(self, row, units, core_in, y_out, y_in, mine, sems):
        self.row, self.units, self.mine = row, units, mine
        self.core_in, self.y_out, self.y_in = core_in, y_out, y_in
        self.sems = (sems[:2], sems[2:])

    def pair(self, k):
        theirs = self.units[k].at[pl.ds(2 * (1 - self.row.core), 2)]
        return to_row(theirs, self.core_in.at[k], self.sems[0], k, self.row.sibling)

    def cross(self, k):
        return to_row(self.y_out.at[k], self.y_in.at[k], self.sems[1], k, self.row.across)

    def start(self, k):
        self.pair(k).start()

    def middle(self, k):
        self.pair(k).wait_recv()
        other = 1 - self.row.y
        mixed = add_up(self.units[k][self.row.core * 2 + other], self.core_in[k, other])
        self.y_out[k] = mixed.astype(bf16)
        self.cross(k).start()

    def end(self, k):
        self.cross(k).wait_recv()
        self.mine[k][...] = add_up(
            self.units[k][self.row.place], self.core_in[k, self.row.y], self.y_in[k]
        ).astype(bf16)

    def finish(self, k):
        self.pair(k).wait_send()
        self.cross(k).wait_send()

    @classmethod
    def scratch(cls, count, width):
        return [
            pltpu.VMEM((count, 2, width, width), bf16),
            pltpu.VMEM((count, width, width), bf16),
            pltpu.VMEM((count, width, width), bf16),
        ] + [pltpu.SemaphoreType.DMA((count,))] * cls.semaphores


class RowGather:
    semaphores = 6

    def __init__(self, row, sources, fulls, slot, slot_across, sems):
        self.row, self.sources, self.fulls = row, sources, fulls
        self.slot, self.slot_across = slot, slot_across
        self.sems = (sems[:2], sems[2:4], sems[4:])

    def over(self, k):
        return to_row(self.sources[k], self.fulls[k].at[self.slot], self.sems[0], k, self.row.across)

    def near(self, k):
        return to_row(self.sources[k], self.fulls[k].at[self.slot], self.sems[1], k, self.row.sibling)

    def onward(self, k):
        block = self.fulls[k].at[self.slot_across]
        return to_row(block, block, self.sems[2], k, self.row.sibling)

    def start(self, k):
        self.over(k).start()
        self.near(k).start()

    def forward(self, k):
        self.over(k).wait_recv()
        self.onward(k).start()

    def arrive(self, k):
        self.near(k).wait_recv()
        self.onward(k).wait_recv()

    def sent(self, k):
        self.over(k).wait_send()
        self.near(k).wait_send()
        self.onward(k).wait_send()

    @classmethod
    def scratch(cls, count):
        return [pltpu.SemaphoreType.DMA((count,))] * cls.semaphores


class WeightGather(RowGather):
    def __init__(self, shards, fulls, sems):
        row = Row()
        super().__init__(row, shards, fulls, row.row, row.across, sems[:6])
        self.own_sem = sems[6]

    def own(self, k):
        return pltpu.make_async_copy(self.sources[k], self.fulls[k].at[self.slot], self.own_sem.at[k])

    def start(self, k):
        super().start(k)
        self.own(k).start()

    def arrive(self, k):
        super().arrive(k)
        self.own(k).wait()

    @classmethod
    def scratch(cls, count):
        return super().scratch(count) + [pltpu.SemaphoreType.DMA((count,))]


class DeepSum:
    def __init__(self, dp, total, arrived, halves, slots, result, sems):
        self.total, self.arrived, self.halves, self.slots, self.result = total, arrived, halves, slots, result
        self.x_sems, self.z_sems, self.z_back, self.x_back = (sems[2 * k : 2 * k + 2] for k in range(4))
        me = lax.axis_index("dp")
        self.x, self.z, self.deep = lax.rem(me, 2), lax.div(me, 2), dp // 2
        self.partner = me + 1 - 2 * self.x

    def greet(self, barrier, whole=True):
        pl.semaphore_signal(barrier, inc=1, device_id={"dp": self.partner}, device_id_type=MESH)
        if not whole:
            return 1
        for off in range(1, self.deep):
            peer = lax.rem(self.z + off, self.deep) * 2 + self.x
            pl.semaphore_signal(barrier, inc=1, device_id={"dp": peer}, device_id_type=MESH)
        return self.deep

    def cut(self, k):
        height = self.halves[k].shape[0]
        return height, height // self.deep

    def over_x(self, k):
        height, _ = self.cut(k)
        away = self.total[k].at[pl.ds(pl.multiple_of((1 - self.x) * height, height), height)]
        return to_peer(away, self.arrived[k], self.x_sems[0].at[k], self.x_sems[1].at[k], self.partner)

    def over_z(self, k, off):
        _, piece = self.cut(k)
        to = lax.rem(self.z + off, self.deep)
        part = self.halves[k].at[pl.ds(pl.multiple_of(to * piece, piece), piece)]
        sems = [sem.at[k, off] for sem in self.z_sems]
        return to_peer(part, self.slots[k].at[off], *sems, to * 2 + self.x)

    def own_piece(self, k):
        height, piece = self.cut(k)
        return self.result[k].at[pl.ds(pl.multiple_of(self.x * height + self.z * piece, piece), piece)]

    def own_half(self, k):
        height, _ = self.cut(k)
        return self.result[k].at[pl.ds(pl.multiple_of(self.x * height, height), height)]

    def back_z(self, k, off):
        to = lax.rem(self.z + off, self.deep)
        sems = [sem.at[k, off] for sem in self.z_back]
        return to_peer(self.own_piece(k), self.own_piece(k), *sems, to * 2 + self.x)

    def back_x(self, k):
        return to_peer(self.own_half(k), self.own_half(k), self.x_back[0].at[k], self.x_back[1].at[k], self.partner)

    def halve(self, k):
        self.over_x(k).wait_recv()
        height, _ = self.cut(k)
        keep = self.total[k][pl.ds(pl.multiple_of(self.x * height, height), height)]
        self.halves[k][...] = add_up(keep, self.arrived[k][...]).astype(self.halves[k].dtype)

    def deepen(self, k):
        for off in range(1, self.deep):
            self.over_z(k, off).start()

    def quarter(self, k):
        for off in range(1, self.deep):
            self.over_z(k, off).wait_recv()
        _, piece = self.cut(k)
        keep = self.halves[k][pl.ds(pl.multiple_of(self.z * piece, piece), piece)]
        total = add_up(keep, *[self.slots[k][off] for off in range(1, self.deep)])
        self.own_piece(k)[...] = total.astype(self.result[k].dtype)
        for off in range(1, self.deep):
            self.back_z(k, off).start()

    def widen(self, k):
        for off in range(1, self.deep):
            self.back_z(k, off).wait_recv()
        self.back_x(k).start()

    def finish(self, k, halved=True):
        if halved:
            self.over_x(k).wait_send()
        for off in range(1, self.deep):
            self.over_z(k, off).wait_send()
            self.back_z(k, off).wait_send()
        self.back_x(k).wait()

    @staticmethod
    def semaphores(dp, count):
        one, many = pltpu.SemaphoreType.DMA((count,)), pltpu.SemaphoreType.DMA((count, dp // 2))
        return [one, one, many, many, many, many, one, one]


def blocks(ref):
    return [ref.at[k] for k in range(ref.shape[0])]


class WideSum:
    def __init__(self, dp, total, slots, result, sems):
        self.dp, self.total, self.slots, self.result, self.sems = dp, total, slots, result, sems
        self.me = lax.axis_index("dp")

    def piece(self, ref, at):
        size = ref.shape[0] // self.dp
        return ref.at[pl.ds(pl.multiple_of(at * size, size), size)]

    def out(self, k, p):
        peer = partner_of(self.me, p, self.dp)
        sems = self.sems[0].at[k, p], self.sems[1].at[k, p]
        return to_peer(self.piece(self.total[k], peer), self.slots[k].at[p], *sems, peer)

    def back(self, k, p):
        mine = self.piece(self.result[k], self.me)
        sems = self.sems[2].at[k, p], self.sems[3].at[k, p]
        return to_peer(mine, mine, *sems, partner_of(self.me, p, self.dp))

    def start(self, k):
        for p in range(self.dp - 1, 0, -1):
            self.out(k, p).start()

    def middle(self, k):
        for p in range(1, self.dp):
            self.out(k, p).wait_recv()
        total = add_up(self.piece(self.total[k], self.me)[...], *[self.slots[k][p] for p in range(1, self.dp)])
        self.piece(self.result[k], self.me)[...] = total.astype(self.result[k].dtype)
        for p in range(self.dp - 1, 0, -1):
            self.back(k, p).start()

    def finish(self, k):
        for p in range(1, self.dp):
            self.out(k, p).wait_send()
            self.back(k, p).wait()

    @staticmethod
    def semaphores(dp, count):
        return [pltpu.SemaphoreType.DMA((count, dp))] * 4


class Closing:
    lines = 64

    def __init__(self, row, dp, units_ref, attn_ref, lines_ref, given, results, refs):
        self.row, self.lines_ref, self.dp = row, lines_ref, dp
        self.full, shard, small, above = results
        core_in, y_out, y_in = refs[:3]
        mine, x_in, half, z_in, self.s_core, self.s_one, self.s_y, self.s_mine, s_slots, wide_in = refs[7:17]
        x_above, half_above, z_above = refs[17:20]
        refs_sems, refs = refs[3:7], refs[20:]
        self.mine = mine
        self.sums = RowSum(row, blocks(units_ref) + [attn_ref], core_in, y_out, y_in, blocks(mine), refs_sems)
        self.gather = RowGather(
            row, [mine.at[k] for k in range(2)], blocks(self.full), row.place, row.place_across, refs[:6]
        )
        self.s_pair = to_row(lines_ref, self.s_core, refs[6:8], 0, row.sibling)
        self.s_cross = to_row(self.s_one, self.s_y, refs[8:10], 0, row.across)
        self.here = DeepSum(
            dp, [mine.at[0], mine.at[1]], blocks(x_in), blocks(half), blocks(z_in), [shard.at[0], shard.at[1]], refs[10:18]
        )
        self.above = DeepSum(
            dp, [None, *given[1:]], [None] + blocks(x_above), [given[0]] + blocks(half_above), blocks(z_above), blocks(above),
            refs[18:26],
        )
        self.wide = WideSum(dp, [mine.at[2], self.s_mine], [wide_in, s_slots], [shard.at[2], small], refs[26:30])

    def enter(self):
        greet(self.dp, lax.axis_index("dp"), (self.row.sibling, self.row.across))
        for k in range(2):
            self.sums.start(k)
        self.above.deepen(0)
        for k in (1, 2):
            self.above.over_x(k).start()

    def early(self):
        for k in range(2):
            self.sums.middle(k)
        for k in (1, 2):
            self.above.halve(k)
            self.above.deepen(k)
        self.above.quarter(0)

    def take(self, k):
        self.sums.end(k)
        self.here.over_x(k).start()
        if k == 0:
            self.above.widen(0)
            for j in (1, 2):
                self.above.quarter(j)
        else:
            for j in (1, 2):
                self.above.widen(j)

    def open(self):
        self.sums.start(2)

    def cross(self):
        self.sums.middle(2)
        for k in range(2):
            self.here.halve(k)
            self.here.deepen(k)

    def send_lines(self):
        self.s_pair.start()
        for k in range(2):
            self.here.quarter(k)
        self.s_pair.wait_recv()
        self.s_one[...] = self.lines_ref[...] + self.s_core[...]
        self.s_cross.start()

    def finish(self):
        self.sums.end(2)
        self.wide.start(0)
        self.s_cross.wait_recv()
        self.s_mine[...] = self.s_one[...] + self.s_y[...]
        self.wide.start(1)
        for k in range(2):
            self.gather.start(k)
            self.full[k, self.row.place] = self.mine[k]
        self.wide.middle(0)
        self.wide.middle(1)
        for k in range(2):
            self.here.widen(k)
        for k in range(2):
            self.gather.forward(k)
        self.s_pair.wait_send()
        self.s_cross.wait_send()
        for k in range(3):
            self.sums.finish(k)
            self.above.finish(k, k > 0)
        for k in range(2):
            self.here.finish(k)
            self.wide.finish(k)
            self.gather.arrive(k)
            self.gather.sent(k)

    @classmethod
    def scratch(cls, dp, width):
        deep = dp // 2
        lines = cls.lines
        flat = pltpu.VMEM((lines, width), f32)
        half, slots = (width // 2, width), (deep, width // dp, width)
        return (
            RowSum.scratch(3, width)
            + [
                pltpu.VMEM((3, width, width), bf16),
                pltpu.VMEM((2, *half), bf16),
                pltpu.VMEM((2, *half), bf16),
                pltpu.VMEM((2, *slots), bf16),
                flat, flat, flat, flat,
                pltpu.VMEM((dp, lines // dp, width), f32),
                pltpu.VMEM((dp, width // dp, width), bf16),
                pltpu.VMEM((2, *half), bf16),
                pltpu.VMEM((2, *half), bf16),
                pltpu.VMEM((3, *slots), bf16),
            ]
            + RowGather.scratch(2)
            + [pltpu.SemaphoreType.DMA((1,))] * 4
            + DeepSum.semaphores(dp, 2)
            + DeepSum.semaphores(dp, 3)
            + WideSum.semaphores(dp, 2)
        )


def format_kernel(columns, *refs):
    count = (len(refs) - 6) // 2
    qkv_out, proj_out, core_up_out, core_down_out, up_out, down_out = refs[2 * count :]

    def form(full, shard):
        mp, width = full.shape[1], full.shape[2]
        rows = width // mp
        qkv_out[0] = shard[2, :columns].astype(f32)
        proj_out[0] = shard[2, columns:].astype(f32)
        core_up_out[0] = shard[0].astype(f32)
        for place in range(mp):
            q = quarter_at(place, mp)
            up_out[0, 0, :, q * width : (q + 1) * width] = full[0, place].astype(f32)
        for chunk in range(mp):
            at = slice(chunk * width, (chunk + 1) * width)
            core_down_out[0, :, at] = shard[1, chunk * rows : (chunk + 1) * rows].astype(f32)
            block = [None] * mp
            for place in range(mp):
                block[quarter_at(place, mp)] = full[1, place, chunk * rows : (chunk + 1) * rows]
            down_out[0, 0, at, :] = turn_blocks(jnp.concatenate(block, 0))

    for layer in range(count):
        pl.when(pl.program_id(0) == layer)(functools.partial(form, refs[layer], refs[count + layer]))


def format_call(fulls, shards, columns):
    layers = len(fulls)
    _, mp, width, _ = fulls[0].shape
    hidden = mp * width
    shapes = [
        (layers, columns, width),
        (layers, width - columns, width),
        (layers, width, width),
        (layers, width // mp, hidden),
        (layers, 1, width, hidden),
        (layers, 1, hidden, width),
    ]
    return pl.pallas_call(
        functools.partial(format_kernel, columns),
        grid=(layers,),
        out_shape=[jax.ShapeDtypeStruct(shape, f32) for shape in shapes],
        in_specs=[whole_spec(a.shape) for a in (*fulls, *shards)],
        out_specs=[image_spec(shape, 1) for shape in shapes],
        compiler_params=pltpu.CompilerParams(vmem_limit_bytes=56 * MIB),
        name="format",
    )(*fulls, *shards)


def greet(dp, me, rows=()):
    barrier = pltpu.get_barrier_semaphore()
    for row in rows:
        pl.semaphore_signal(barrier, inc=1, device_id={"mp": row}, device_id_type=MESH)

    def signal(off, carry):
        pl.semaphore_signal(barrier, inc=1, device_id={"dp": lax.rem(me + off, dp)}, device_id_type=MESH)
        return carry

    lax.fori_loop(1, dp, signal, 0)
    pl.semaphore_wait(barrier, dp - 1 + len(rows))


def partner_of(me, p, dp):
    out, bit = 0, 1
    while bit < dp:
        one, two = lax.rem(lax.div(me, bit), 2), lax.rem(lax.div(p, bit), 2)
        out = out + bit * (one + two - 2 * one * two)
        bit *= 2
    return out


def to_peer(source, target, send_sem, recv_sem, peer):
    return pltpu.make_async_remote_copy(
        src_ref=source,
        dst_ref=target,
        send_sem=send_sem,
        recv_sem=recv_sem,
        device_id={"dp": peer},
        device_id_type=MESH,
    )


def gelu_parts(h):
    root = np.float32(np.sqrt(2.0 / np.pi))
    square = h * h
    t = jnp.tanh(root * h * (1.0 + 0.044715 * square))
    half = 0.5 * (1.0 + t)
    slope = half + 0.5 * h * (1.0 - t * t) * root * (1.0 + 3 * 0.044715 * square)
    return h * half, slope


def expert_forward_kernel(dp, mp, layer, gather, *refs):
    refs = list(refs)
    buffer_ref, up_any, down_any, rup_any, rdown_any = refs[:5]
    refs = refs[5:]
    if gather:
        shards = [ref.at[layer + 1] for ref in refs[:4]]
        refs = refs[4:]
    recv_ref, returned_ref, up_eff, down_eff = refs[:4]
    refs = refs[4:]
    if gather:
        fulls = refs[:4]
        refs = refs[4:]
    part, core, up_ref, down_ref, rup_ref, rdown_ref, local = refs[:7]
    refs = refs[7:]
    moving = WeightGather(shards, fulls, refs[:7]) if gather else None
    send_one, recv_one, send_two, recv_two = refs[-4:]
    split = dp // EXPERTS
    me = lax.axis_index("dp")
    loads = [
        pltpu.make_async_copy(source, target, local.at[k])
        for k, (source, target) in enumerate(
            [
                (up_any, up_ref),
                (rup_any.at[layer, 0], rup_ref),
                (down_any, down_ref),
                (rdown_any.at[layer, 0], rdown_ref),
            ]
        )
    ]
    for load in loads:
        load.start()
    greet(dp, me, (moving.row.sibling, moving.row.across) if gather else ())

    def first(off):
        peer = partner_of(me, off, dp)
        return to_peer(
            buffer_ref.at[lax.div(peer, split)], recv_ref.at[me], send_one.at[off], recv_one.at[off], peer
        )

    def second(off):
        source = partner_of(me, off, dp)
        return to_peer(part.at[source], returned_ref.at[me], send_two.at[off], recv_two.at[off], source)

    def start_first(off, carry):
        first(dp - off).start()
        return carry

    lax.fori_loop(1, dp, start_first, 0)
    if gather:
        for k in range(4):
            moving.start(k)
    recv_ref[me] = buffer_ref[lax.div(me, split)]
    hidden = up_eff.shape[1]
    columns = up_ref.shape[-1]
    loads[0].wait()
    loads[1].wait()
    if split == 1 and columns % LANES == 0:
        for m in range(mp):
            at = slice(m * columns, (m + 1) * columns)
            up_eff[:, at] = (up_ref[m].astype(f32) + rup_ref[:, at].astype(f32)).astype(bf16)
    else:
        core[...] = rup_ref[...].astype(f32)
        begin = lax.rem(me, split) * hidden
        for m in range(mp):
            put = onehot(iota((columns, hidden), 0) + m * columns == iota((columns, hidden), 1) + begin)
            core[...] += nn(up_ref[m], put)
        up_eff[...] = core[...].astype(bf16)
    begin = pl.multiple_of(lax.rem(me, split) * hidden, LANES)
    loads[2].wait()
    loads[3].wait()
    core_part = down_ref[:, :, pl.ds(begin, hidden)].reshape(down_eff.shape[1], hidden)
    down_eff[...] = (core_part.astype(f32).T + rdown_ref[...].astype(f32)).astype(bf16)

    def work(source):
        hidden_pre = nn(recv_ref[source], up_eff[...])
        hidden_low = gelu_parts(hidden_pre)[0].astype(bf16)
        return nn(hidden_low, down_eff[...]).astype(bf16)

    returned_ref[me] = work(me)

    def step(off, carry):
        source = partner_of(me, off, dp)
        first(off).wait_recv()
        part[source] = work(source)
        second(off).start()
        return carry

    lax.fori_loop(1, dp, step, 0)
    if gather:
        for k in range(4):
            moving.forward(k)

    def finish(off, carry):
        first(off).wait_send()
        second(off).wait()
        return carry

    lax.fori_loop(1, dp, finish, 0)
    if gather:
        for k in range(4):
            moving.arrive(k)
            moving.sent(k)


def expert_backward_kernel(dp, mp, fast, reduce, *refs):
    refs = list(refs)
    buffer_ref, recv_ref, up_ref, down_ref = refs[:4]
    refs = refs[4:]
    if reduce:
        given_ref, attn_ref = refs[:2]
        refs = refs[2:]
    returned_ref = refs.pop(0)
    if fast:
        units_ref = refs.pop(0)
    else:
        up_term, down_term = refs[:2]
        refs = refs[2:]
    if reduce:
        full_ref, mine_ref = refs[:2]
        refs = refs[2:]
    grads, hidden_low, slope, pre, part = refs[:5]
    refs = refs[5:]
    if fast:
        up_term, down_term = refs[:2]
        refs = refs[2:]
    row = Row() if reduce else None
    if reduce:
        core_in, y_out, y_in = refs[:3]
        sums = RowSum(row, [attn_ref], core_in, y_out, y_in, [mine_ref], refs[3:7])
        gather = RowGather(
            row, [given_ref.at[k] for k in range(2)], [full_ref.at[k] for k in range(2)], row.place, row.place_across,
            refs[7:13],
        )
        refs = refs[13:]
    send_one, recv_one, send_two, recv_two = refs
    split = dp // EXPERTS
    me = lax.axis_index("dp")
    greet(dp, me, (row.sibling, row.across) if reduce else ())

    def first(off):
        peer = partner_of(me, off, dp)
        return to_peer(buffer_ref.at[lax.div(peer, split)], grads.at[me], send_one.at[off], recv_one.at[off], peer)

    def second(off):
        source = partner_of(me, off, dp)
        return to_peer(part.at[source], returned_ref.at[me], send_two.at[off], recv_two.at[off], source)

    def start_first(off, carry):
        first(dp - off).start()
        return carry

    lax.fori_loop(1, dp, start_first, 0)
    if reduce:
        sums.start(0)
        for k in range(2):
            gather.start(k)
    grads[me] = buffer_ref[lax.div(me, split)]

    def again(source, carry):
        value, rate = gelu_parts(nn(recv_ref[source], up_ref[...]))
        hidden_low[source] = value.astype(bf16)
        slope[source] = rate
        return carry

    lax.fori_loop(0, dp, again, 0)
    if reduce:
        sums.middle(0)
        for k in range(2):
            full_ref[k, row.place] = given_ref[k]

    def work(source):
        hidden_grad = nt(grads[source], down_ref[...])
        pre_grad = (slope[source] * hidden_grad).astype(bf16)
        pre[source] = pre_grad
        return nt(pre_grad, up_ref[...]).astype(bf16)

    returned_ref[me] = work(me)

    def step(off, carry):
        source = partner_of(me, off, dp)
        first(off).wait_recv()
        part[source] = work(source)
        second(off).start()
        return carry

    lax.fori_loop(1, dp, step, 0)
    if reduce:
        for k in range(2):
            gather.forward(k)
        sums.end(0)
    up_term[...] = jnp.zeros(up_term.shape, f32)
    down_term[...] = jnp.zeros(down_term.shape, f32)

    def terms(block, carry):
        up_term[...] += tn(recv_ref[block], pre[block])
        down_term[...] += tn(grads[block], hidden_low[block])
        return carry

    lax.fori_loop(0, dp, terms, 0)
    if fast:
        width = up_term.shape[0]
        height = width // mp
        for place in range(mp):
            q = quarter_at(place, mp)
            units_ref[0, place] = up_term[:, q * width : (q + 1) * width].astype(bf16)
            for chunk in range(mp):
                block = down_term[q * height : (q + 1) * height, chunk * width : (chunk + 1) * width]
                units_ref[1, place, chunk * height : (chunk + 1) * height] = block.astype(bf16)

    def finish(off, carry):
        first(off).wait_send()
        second(off).wait()
        return carry

    lax.fori_loop(1, dp, finish, 0)
    if reduce:
        sums.finish(0)
        for k in range(2):
            gather.arrive(k)
            gather.sent(k)


def expert_call(kernel, arrays, outs, scratch, dp, collective_id, name, flops, anys=(), any_outs=()):
    sems = [pltpu.SemaphoreType.DMA((dp,))] * 4
    vmem, anywhere = pl.BlockSpec(memory_space=pltpu.VMEM), pl.BlockSpec(memory_space=pl.ANY)
    return pl.pallas_call(
        kernel,
        out_shape=[jax.ShapeDtypeStruct(shape, dtype) for shape, dtype in (*outs, *any_outs)],
        in_specs=[vmem] * len(arrays) + [anywhere] * len(anys),
        out_specs=[vmem] * len(outs) + [anywhere] * len(any_outs),
        scratch_shapes=scratch + sems,
        compiler_params=pltpu.CompilerParams(
            vmem_limit_bytes=51 * MIB, collective_id=collective_id, has_side_effects=True
        ),
        cost_estimate=pl.CostEstimate(flops=flops, bytes_accessed=20 * MIB, transcendentals=0),
        name=name,
    )(*arrays, *anys)


def by_windows(grid):
    images, kinds = grid.shape[:2]
    blocks = GRID // WINDOW
    grid = grid.reshape(images, kinds, blocks, WINDOW, blocks, WINDOW).transpose(0, 1, 2, 4, 3, 5)
    grid = grid.reshape(images, kinds, blocks * blocks, WINPOS)
    grid = jnp.pad(grid, ((0, 0), (0, 0), (0, 0), (0, WPAD - WINPOS)), constant_values=-1)
    return grid.reshape(images, kinds, IMGROWS)


def per_device(
    patches,
    qkv_weight,
    proj_weight,
    core_up,
    core_down,
    residual_up,
    residual_down,
    position_bias,
    router_weight,
    norm_gain,
    norm_bias,
    cotangent,
    image_valid,
    expert_index,
    slot_index,
    region_id,
):
    dp, mp = lax.axis_size("dp"), lax.axis_size("mp")
    images, _, width = patches.shape
    split = dp // EXPERTS
    hidden = residual_up.shape[-1]
    hidden_full = core_up.shape[-1] * mp
    row_index = lax.axis_index("mp")

    fast = split == 1 and dp == 8 and mp == 4 and hidden == mp * width
    qkv_rows, proj_rows, down_rows = (a.transpose(0, 2, 1) for a in (qkv_weight, proj_weight, core_down))
    shards = (qkv_rows, proj_rows, core_up, down_rows)
    gathered = [[None] * len(shards)] * LAYERS
    if not fast:
        gathered = [[lax.all_gather(a[l], "mp", axis=0, tiled=False) for a in shards] for l in range(LAYERS)]

    position = jnp.where(slot_index >= 0, expert_index * SLOTS + slot_index, -1)
    row_form = by_windows(jnp.stack([position.reshape(images, GRID, GRID), region_id], 1))
    col_form = row_form.transpose(0, 2, 1)
    enter = jnp.asarray(enter_table(), bf16)
    leave = jnp.asarray(enter_table().T, bf16)
    moves = [jnp.asarray(move_table(l % 2 == 1), bf16) for l in range(LAYERS)]
    backs = [jnp.asarray(move_table(l % 2 == 1).T, bf16) for l in range(LAYERS)]
    table_rows = position_bias.transpose(0, 2, 1).reshape(LAYERS * HEADS, OFFSETS)
    table_rows = jnp.pad(table_rows, ((0, 0), (0, TABLE - OFFSETS)))
    entry_row, entry_col = jnp.asarray(cell_entries()[None, :]), jnp.asarray(cell_entries()[:, None])
    routers = jnp.pad(router_weight.transpose(0, 2, 1), ((0, 0), (0, LANES - EXPERTS), (0, 0)))

    token = (images, IMGROWS, width)
    buffer_shape = (ROWS, width)
    block_rows = (dp, SLOTS, width)
    pieces = (split, ROWS, width)

    def by_piece(returned):
        return returned.reshape(EXPERTS, split, SLOTS, width).transpose(1, 0, 2, 3).reshape(pieces)

    records = []
    before = None
    for l in range(LAYERS):
        first = l == 0
        gather = fast and first
        if first:
            arrays = [("image", patches), ("whole", enter)]
        else:
            arrays = [("image", before[0]), ("image", before[1]), ("whole", before[2])]
        arrays += [
            ("smem", image_valid),
            ("image", col_form),
            ("image", row_form),
            ("any", qkv_rows) if gather else ("whole", gathered[l][0]),
            ("any", proj_rows) if gather else ("whole", gathered[l][1]),
            ("whole", table_rows) if first else (l, biases),
            ("whole", moves[l]),
            ("whole", backs[l]),
            (l, norm_gain),
            (l, norm_bias),
            (l, routers),
        ]
        if first:
            arrays.append(("whole", entry_row))
        if gather:
            arrays += [("any", core_up), ("any", down_rows)]
        outs = [("image", token, f32)]
        if first:
            outs.append(("whole", (LAYERS, HEADS, WPAD, LANES), f32))
        else:
            outs.append(("image", token, f32))
        outs += [
            ("image", token, f32),
            ("image", token, bf16),
            ("image", (images, IMGROWS, 1), f32),
            ("whole", buffer_shape, bf16),
            ("image", token, bf16),
            ("image", (images, 2 * width, IMGROWS), bf16),
            ("image", token, bf16),
            ("image", (images, PAIRS * HEADS, WPAD, LANES), bf16),
            ("image", (images, width, IMGROWS), bf16),
            ("whole", (width, width), bf16),
        ]
        scratch = [pltpu.VMEM(buffer_shape, f32)]
        gathered_shapes = [(mp, *a.shape[1:]) for a in shards]
        if gather:
            outs.append(("whole", (3 * width, width), bf16))
            outs += [("any", shape, bf16) for shape in gathered_shapes[2:]]
            scratch += [pltpu.VMEM(shape, bf16) for shape in gathered_shapes[:2]] + WeightGather.scratch(4)
        results = list(
            image_call(
                functools.partial(attention_forward_kernel, first, l % 2 == 1, mp, gather),
                images, arrays, outs, scratch, f"attend_{l}", 3 * LAYERS + 1 if gather else None,
            )
        )
        if gather:
            gathered[l] = [results[-3], None] + results[-2:]
            results = results[:-3]
        carried = results.pop(0)
        if first:
            biases = results.pop(0)
        else:
            records[-1]["expert_out"] = results.pop(0)
        middle, second_low, gate, buffer = results[:4]
        gather = fast and l < LAYERS - 1
        received, returned, up_eff, down_eff, *more = expert_call(
            functools.partial(expert_forward_kernel, dp, mp, l, gather),
            [buffer.reshape(EXPERTS, SLOTS, width)],
            [
                (block_rows, bf16),
                (block_rows, bf16),
                ((width, hidden), bf16),
                ((hidden, width), bf16),
            ],
            [
                pltpu.VMEM(block_rows, bf16),
                pltpu.VMEM((8, LANES) if fast else (width, hidden), f32),
                pltpu.VMEM(gathered_shapes[2], bf16),
                pltpu.VMEM(gathered_shapes[3], bf16),
                pltpu.VMEM((width, hidden), bf16),
                pltpu.VMEM((hidden, width), bf16),
                pltpu.SemaphoreType.DMA((4,)),
            ]
            + (WeightGather.scratch(4) if gather else []),
            dp, l, f"experts_{l}", 4 * dp * SLOTS * width * hidden,
            [gathered[l][2], gathered[l][3], residual_up, residual_down, *(shards if gather else ())],
            [(shape, bf16) for shape in gathered_shapes] if gather else (),
        )
        if gather:
            gathered[l + 1] = more
        returned = by_piece(returned)
        before = (middle, gate, returned)
        records.append(
            dict(
                carried=carried, middle=middle, second_low=second_low, gate=gate, saved=results[4:], received=received,
                up_eff=up_eff, down_eff=down_eff,
            )
        )

    top = records[-1]
    block_output, grad, logit_grad, router_part, buffer = image_call(
        turn_kernel,
        images,
        [
            ("image", before[0]),
            ("image", before[1]),
            ("whole", before[2]),
            ("image", cotangent),
            ("whole", enter),
            ("whole", leave),
            ("image", col_form),
            ("image", row_form),
            ("image", top["second_low"]),
            (LAYERS - 1, routers),
        ],
        [
            ("image", patches.shape, bf16),
            ("image", token, f32),
            ("image", (images, IMGROWS, LANES), f32),
            ("whole", (LANES, width), f32),
            ("whole", buffer_shape, bf16),
        ],
        [pltpu.VMEM(buffer_shape, f32)],
        "turn",
    )
    router_parts, tables, smalls = [None] * LAYERS, [None] * LAYERS, [None] * LAYERS
    residual_sums, shard_sums = [None] * LAYERS, [None] * LAYERS
    router_parts[LAYERS - 1] = router_part
    units, attn_units, mines = [None] * LAYERS, [None] * LAYERS, [None] * LAYERS
    for l in reversed(range(LAYERS)):
        rec = records[l]
        last = l == 0
        reduce = fast and l < LAYERS - 1
        arrays = [buffer.reshape(EXPERTS, SLOTS, width), rec["received"], rec["up_eff"], rec["down_eff"]]
        outs = [(block_rows, bf16)]
        scratch = [
            pltpu.VMEM(block_rows, bf16),
            pltpu.VMEM((dp, SLOTS, hidden), bf16),
            pltpu.VMEM((dp, SLOTS, hidden), f32),
            pltpu.VMEM((dp, SLOTS, hidden), bf16),
            pltpu.VMEM(block_rows, bf16),
        ]
        if fast:
            outs.append(((2, mp, width, width), bf16))
            scratch += [pltpu.VMEM((width, hidden), f32)] * 2
        else:
            outs += [((width, hidden), f32)] * 2
        if reduce:
            arrays += [mines[l + 1], attn_units[l + 1]]
            outs += [((2, mp, width, width), bf16), ((width, width), bf16)]
            scratch += RowSum.scratch(1, width) + RowGather.scratch(2)
        results = list(
            expert_call(
                functools.partial(expert_backward_kernel, dp, mp, fast, reduce), arrays, outs, scratch, dp, LAYERS + l,
                f"experts_back_{l}", 10 * dp * SLOTS * width * hidden,
            )
        )
        returned_grad = results.pop(0)
        if fast:
            units[l] = results.pop(0)
        else:
            residual_sums[l] = lax.psum(tuple(t.astype(bf16) for t in results[:2]), "mp")
        if reduce:
            full_above, mine_above = results
        window_in, qk, v, probs, att, proj_full = rec["saved"]
        qkv_full = gathered[l][0].reshape(3 * width, width)
        arrays = [
            ("smem", image_valid),
            ("image", grad),
            ("whole", by_piece(returned_grad)),
            ("image", logit_grad),
            ("image", rec["middle"]),
            ("image", rec["carried"]),
            (l, routers),
            ("image", col_form),
            ("whole", moves[l]),
            ("whole", backs[l]),
            (l, norm_gain),
            ("whole", proj_full),
            ("whole", qkv_full),
            ("image", window_in),
            ("image", qk),
            ("image", v),
            ("image", probs),
            ("image", att),
        ]
        outs = [("image", patches.shape if last else token, f32)]
        scratch = [pltpu.VMEM((3 * width, (2 - images % 2) * IMGROWS), bf16)]
        closes = fast and last
        table_shape, small_shape = (HEADS, WPAD, LANES), (8, width)
        if fast:
            arrays.append(("whole", units[l]))
            scratch += [pltpu.VMEM((3 * width, width), f32), pltpu.VMEM((width, width), f32)]
        if closes:
            outs += [
                ("whole", (2, mp, width, width), bf16),
                ("whole", (3, width, width), bf16),
                ("whole", (Closing.lines, width), f32),
                ("whole", (3, width, width), bf16),
            ]
        else:
            if fast:
                outs += [
                    ("whole", (width // 2, width), bf16),
                    ("whole", (mp, width, width), bf16),
                    ("whole", (2, width, width), bf16),
                ]
            else:
                outs += [("whole", (3 * width, width), f32), ("whole", (width, width), f32)]
            outs += [("whole", table_shape, f32), ("whole", small_shape, f32)]
        if last:
            arrays.append(("whole", leave))
            if fast:
                arrays += [
                    ("whole", a)
                    for a in (
                        tables[1], smalls[1], router_parts[1], router_parts[0], entry_col, halves_above, mines[1],
                        mine_above,
                    )
                ]
        else:
            below = records[l - 1]
            arrays += [
                ("image", row_form),
                ("image", below["expert_out"]),
                ("image", below["second_low"]),
                (l - 1, routers),
            ]
            outs += [
                ("image", (images, IMGROWS, LANES), f32),
                ("whole", (LANES, width), f32),
                ("whole", buffer_shape, bf16),
            ]
            scratch.append(pltpu.VMEM(buffer_shape, f32))
        if closes:
            scratch += [
                pltpu.VMEM(table_shape, f32),
                pltpu.VMEM(small_shape, f32),
                pltpu.VMEM((mp, width, width), bf16),
                pltpu.VMEM((Closing.lines, width), f32),
            ]
            scratch += [pltpu.VMEM(shape, dtype) for _, shape, dtype in outs[1:5]] + Closing.scratch(dp, width)
        elif fast:
            scratch += RowSum.scratch(2, width) + [pltpu.VMEM((width // 2, width), bf16)]
            scratch += [pltpu.SemaphoreType.DMA((1,))] * 2
        results = list(
            image_call(
                functools.partial(attention_backward_kernel, last, dp, mp, fast),
                images, arrays, outs, scratch, f"attend_back_{l}", 2 * LAYERS + 1 + l if fast else None,
            )
        )
        grad = results.pop(0)
        if closes:
            full, closed, lines, shard_above = results
            continue
        if fast:
            halves_above = results.pop(0)
            attn_units[l], mines[l] = results[:2]
        else:
            qkv_part, proj_part = results[:2]
        tables[l], smalls[l] = results[2:4]
        if not last:
            logit_grad, router_parts[l - 1], buffer = results[4:]
        if fast:
            continue
        attn = (
            lax.psum_scatter(qkv_part.astype(bf16), "mp", scatter_dimension=0, tiled=True),
            lax.psum_scatter(proj_part.T.astype(bf16), "mp", scatter_dimension=0, tiled=True),
        )
        up_sum, down_sum = residual_sums[l]
        if split > 1:
            begin = lax.axis_index("dp") % split * hidden
            empty = jnp.zeros((width, hidden_full), bf16)
            up_sum = lax.dynamic_update_slice_in_dim(empty, up_sum, begin, 1)
            down_sum = lax.dynamic_update_slice_in_dim(empty, down_sum, begin, 1)
        up_columns, down_columns = core_up.shape[-1], core_down.shape[-1]
        up_shard = lax.dynamic_slice_in_dim(up_sum, row_index * up_columns, up_columns, 1)
        down_shard = lax.dynamic_slice_in_dim(down_sum, row_index * down_columns, down_columns, 0)
        shard_sums[l] = lax.psum((attn[0], attn[1], up_shard, down_shard), "dp")

    if fast:
        *attn_grads, core_up_grad, core_down_grad, residual_up_grad, residual_down_grad = format_call(
            [full, full_above], [closed, shard_above], qkv_weight.shape[-1]
        )
        attn_grads = [a.transpose(0, 2, 1) for a in attn_grads]
        core_grads = (core_up_grad, core_down_grad.transpose(0, 2, 1))
        at = LAYERS * HEADS
        table_sum = lines[:at, :OFFSETS]
        router_sum = lines[at : at + LAYERS * EXPERTS].reshape(LAYERS, EXPERTS, width)
        at += LAYERS * EXPERTS
        small_sum = lines[at : at + LAYERS * 8].reshape(LAYERS, 8, width)[:, :4]
    else:
        entry = cell_entries()[None, :] + np.array([key_base_of(key) for key in range(WPAD)])[:, None]
        entry = jnp.asarray(np.where(np.arange(WPAD)[:, None] < WINPOS, entry, -1).reshape(-1))
        entry_turned = (entry[:, None] == jnp.arange(OFFSETS)[None, :]).astype(f32)
        table_part = jnp.dot(
            jnp.stack(tables, 0).reshape(LAYERS * HEADS, WPAD * LANES), entry_turned, precision=highest
        )
        small_part = jnp.stack(smalls, 0)[:, :4]
        router_part = jnp.stack(router_parts, 0)[:, :EXPERTS]
        table_sum, small_sum, router_sum = lax.psum((table_part, small_part, router_part), ("dp", "mp"))

        def shard(k):
            return jnp.stack([shard_sums[l][k] for l in range(LAYERS)], 0).astype(f32)

        attn_grads = (shard(0).transpose(0, 2, 1), shard(1).transpose(0, 2, 1))
        core_grads = (shard(2), shard(3).transpose(0, 2, 1))
        residual_up_grad, residual_down_grad = (
            jnp.stack([residual_sums[l][k] for l in range(LAYERS)], 0).astype(f32) for k in range(2)
        )
        residual_up_grad = residual_up_grad[:, None]
        residual_down_grad = residual_down_grad.transpose(0, 2, 1)[:, None]

    return (
        block_output,
        grad,
        attn_grads[0],
        attn_grads[1],
        core_grads[0],
        core_grads[1],
        residual_up_grad,
        residual_down_grad,
        table_sum.reshape(LAYERS, HEADS, OFFSETS).transpose(0, 2, 1),
        router_sum.transpose(0, 2, 1),
        small_sum[:, 0:2],
        small_sum[:, 2:4],
    )


def solution(mesh):
    placed = (
        P(("dp", "mp"), None, None),
        P(None, None, "mp"),
        P(None, None, "mp"),
        P(None, None, "mp"),
        P(None, None, "mp"),
        P(None, "dp", None, None),
        P(None, "dp", None, None),
        P(),
        P(),
        P(),
        P(),
        P(("dp", "mp"), None, None),
        P(("dp", "mp")),
        P(("dp", "mp"), None),
        P(("dp", "mp"), None),
        P(("dp", "mp"), None, None),
    )
    return jax.shard_map(
        per_device,
        mesh=mesh,
        in_specs=placed,
        out_specs=(
            P(("dp", "mp"), None, None),
            P(("dp", "mp"), None, None),
            P(None, None, "mp"),
            P(None, None, "mp"),
            P(None, None, "mp"),
            P(None, None, "mp"),
            P(None, "dp", None, None),
            P(None, "dp", None, None),
            P(),
            P(),
            P(),
            P(),
        ),
        check_vma=False,
    )
```

```python
import functools

import jax
import jax.numpy as jnp
import numpy as np
from jax import lax
from jax.experimental import pallas as pl
from jax.experimental.pallas import tpu as pltpu
from jax.sharding import PartitionSpec as P

HEADS = 12
HEAD_DIM = 32
EXPERTS = 8
WINDOW = 7
GRID = 14
SHIFT = 3
LAYERS = 2
WINPOS = 49
OFFSETS = 169
CAP = 122

WPAD = 64
IMGROWS = 256
PATCHES = 196
SLOTS = 128
ROWS = EXPERTS * SLOTS
LANES = 128
GROUP = 4
PAIRS = 2
TABLE = 256

bf16 = jnp.bfloat16
f32 = jnp.float32
highest = lax.Precision.HIGHEST
norm_epsilon = 1e-05
mask_fill = -100.0
head_scale = HEAD_DIM ** (-0.5)
MESH = pl.DeviceIdType.MESH
MIB = 1024 * 1024


def nn(a, b):
    return lax.dot_general(a, b, (((1,), (0,)), ((), ())), preferred_element_type=f32)


def nt(a, b):
    return lax.dot_general(a, b, (((1,), (1,)), ((), ())), preferred_element_type=f32)


def tn(a, b):
    return lax.dot_general(a, b, (((0,), (0,)), ((), ())), preferred_element_type=f32)


def iota(shape, dim):
    return lax.broadcasted_iota(jnp.int32, shape, dim)


def onehot(flags):
    return jnp.where(flags, 1.0, 0.0).astype(bf16)


def natural_of_row(shifted):
    moved = SHIFT if shifted else 0
    blocks = GRID // WINDOW
    out = -np.ones(IMGROWS, np.int32)
    for window in range(blocks * blocks):
        for cell in range(WINPOS):
            row = (window // blocks * WINDOW + cell // WINDOW + moved) % GRID
            col = (window % blocks * WINDOW + cell % WINDOW + moved) % GRID
            out[window * WPAD + cell] = row * GRID + col
    return out


def key_base_of(key):
    return (2 * WINDOW) * (WINDOW - 1) - (key // WINDOW * (2 * WINDOW - 1) + key % WINDOW)


def enter_table():
    held = natural_of_row(False)
    return (held[:, None] == np.arange(PATCHES)[None, :]).astype(np.float32)


def move_table(shifted):
    first, second = natural_of_row(False), natural_of_row(shifted)
    same = (second[:, None] == first[None, :]) & (second[:, None] >= 0)
    return same.astype(np.float32)


def cell_entries():
    cell = np.arange(LANES) % WPAD
    return np.where(cell < WINPOS, cell // WINDOW * (2 * WINDOW - 1) + cell % WINDOW, -4 * TABLE).astype(np.int32)


def norm_parts(x):
    width = x.shape[-1]
    center = x - jnp.sum(x, -1, keepdims=True) * (1.0 / width)
    spread = jnp.sum(center * center, -1, keepdims=True) * (1.0 / width)
    rstd = lax.rsqrt(spread + norm_epsilon)
    return center * rstd, rstd


def norm_back(grad, gain, xhat, rstd):
    width = xhat.shape[-1]
    dxhat = grad * gain
    mean_one = jnp.sum(dxhat, -1, keepdims=True) * (1.0 / width)
    mean_two = jnp.sum(dxhat * xhat, -1, keepdims=True) * (1.0 / width)
    return rstd * (dxhat - mean_one - xhat * mean_two)


def turn_blocks(x):
    size = x.shape[0]
    same = onehot(iota((size, size), 0) == iota((size, size), 1))
    return jnp.concatenate([nt(same, x[:, at : at + size]) for at in range(0, x.shape[1], size)], 0)


def split_two(x):
    high = x.astype(bf16)
    return high, (x - high.astype(f32)).astype(bf16)


def collect(pos_col, returned_ref):
    pick = onehot(pos_col == iota((pos_col.shape[0], ROWS), 1))
    out = nn(pick, returned_ref[0])
    for piece in range(1, returned_ref.shape[0]):
        out = out + nn(pick, returned_ref[piece])
    return out


def join(ref):
    return ref[...].reshape(ref.shape[0] * ref.shape[1], *ref.shape[2:])


def store(ref, rows):
    ref[...] = rows.reshape(ref.shape).astype(ref.dtype)


def per_image(function, count):
    return jnp.concatenate([function(i) for i in range(count)], 0)


def image_rows(i):
    return slice(i * IMGROWS, (i + 1) * IMGROWS)


def lay_positions(row_ref):
    return jnp.concatenate([row_ref[i, 0:1, :] for i in range(row_ref.shape[0])], 1)


def spread_rows(pos_row, rows_low):
    return nn(onehot(iota((ROWS, pos_row.shape[1]), 0) == pos_row), rows_low)


def route(second_low, router, pos_col):
    logits = nt(second_low, router)
    lane = iota(logits.shape, 1)
    logits = jnp.where(lane < EXPERTS, logits, -1e30)
    expo = jnp.exp(logits - jnp.max(logits, -1, keepdims=True))
    probs = expo / jnp.sum(expo, -1, keepdims=True)
    expert = jnp.where(pos_col >= 0, pos_col // SLOTS, -1)
    chosen = jnp.where(lane == expert, 1.0, 0.0)
    return probs, chosen, jnp.sum(probs * chosen, -1, keepdims=True)


def head_masks():
    rows = iota((LANES, LANES), 0) // HEAD_DIM
    return [onehot(rows == h) for h in range(GROUP)]


def lane_masks():
    lane = iota((WPAD, LANES), 1)
    return [onehot(lane < WPAD), onehot(lane >= WPAD)]


def keys_entry(cells, key_row, turned):
    parts = [cells + (key_base_of(col) - key_row * (2 * WINDOW - 1)) for col in range(WINDOW)]
    return jnp.concatenate(parts, 0 if turned else 1)


def form_bias(bias_ref, table_ref, entry_row):
    layers, heads = bias_ref.shape[:2]
    lines = layers * heads
    bias_ref[...] = jnp.where(iota(bias_ref.shape, 2) < WINPOS, 0.0, -1e30)
    table = table_ref[...]
    high = table.astype(bf16)
    mid, low = split_two(table - high.astype(f32))
    parts = jnp.concatenate([high.astype(f32), mid.astype(f32), low.astype(f32)], 0).astype(bf16)

    def step(key_row, carry):
        pick = onehot(iota((TABLE, WINDOW * LANES), 0) == keys_entry(entry_row, key_row, False))
        rows = nn(parts, pick)
        rows = rows[:lines] + rows[lines : 2 * lines] + rows[2 * lines :]
        for col in range(WINDOW):
            for layer in range(layers):
                part = rows[layer * heads : (layer + 1) * heads, col * LANES : (col + 1) * LANES]
                bias_ref[layer, :, pl.ds(key_row * WINDOW + col, 1), :] = part.reshape(heads, 1, LANES)
        return carry

    lax.fori_loop(0, WINDOW, step, 0)


def table_grad(parts, entry_col):
    heads = parts[0].shape[0]
    lines = heads * len(parts)

    def step(key_row, total):
        keys = [
            jnp.concatenate([ref[:, pl.ds(key_row * WINDOW + col, 1), :].reshape(heads, LANES) for ref in parts], 0)
            for col in range(WINDOW)
        ]
        rows = jnp.concatenate(keys, 1)
        high = rows.astype(bf16).astype(f32)
        both = jnp.concatenate([high, rows - high], 0).astype(bf16)
        entry = keys_entry(entry_col, key_row, True)
        out = nn(both, onehot(iota((WINDOW * LANES, TABLE), 1) == entry))
        return total + out[:lines] + out[lines:]

    return lax.fori_loop(0, WINDOW, step, jnp.zeros((lines, TABLE), f32))


def attention_forward_kernel(first, shifted, mp, gather, *refs):
    refs = list(refs)
    if first:
        patches_ref, enter_ref = refs[:2]
        refs = refs[2:]
    else:
        prev_ref, prev_gate_ref, returned_ref = refs[:3]
        refs = refs[3:]
    (
        valid_ref, col_ref, row_ref, qkv_ref, proj_ref, bias_ref, move_ref, back_ref, gain_ref, nbias_ref, router_ref,
    ) = refs[:11]
    gain_ref, nbias_ref, router_ref = (ref.at[0] for ref in (gain_ref, nbias_ref, router_ref))
    refs = refs[11:]
    if first:
        table_ref, entry_ref = bias_ref, refs.pop(0)
    if gather:
        core_up_ref, core_down_ref = refs[:2]
        refs = refs[2:]
    carried_ref = refs.pop(0)
    if first:
        biases_ref = refs.pop(0)
        bias_ref = biases_ref.at[0]
    else:
        expert_out_ref = refs.pop(0)
        bias_ref = bias_ref.at[0]
    middle_ref, second_ref, gate_ref, buffer_ref, window_ref, qk_ref, v_ref, probs_ref, att_ref, proj_full = refs[:10]
    refs = refs[10:]
    if gather:
        qkv_full = refs.pop(0)
        up_out, down_out = refs[:2]
        refs = refs[2:]
    total_ref = refs.pop(0)
    step = pl.program_id(0)
    final = pl.num_programs(0) - 1
    count, _, width = carried_ref.shape
    if gather:
        shards = [ref.at[0] for ref in (qkv_ref, proj_ref, core_up_ref, core_down_ref)]
        qkv_ref, proj_ref = refs[:2]
        moving = WeightGather(shards, [qkv_ref, proj_ref, up_out, down_out], refs[2:])

        @pl.when(step == 0)
        def _():
            pl.semaphore_wait(moving.row.greet(), 2)
            for k in (0, 1):
                moving.start(k)
            form_bias(biases_ref, table_ref, entry_ref[...])

    pos_col = join(col_ref)[:, 0:1]
    if first:
        x = per_image(lambda i: nn(enter_ref[...], patches_ref[i]), count)
    else:
        expert_out = collect(pos_col, returned_ref)
        store(expert_out_ref, expert_out)
        x = join(prev_ref) + join(prev_gate_ref) * expert_out
    store(carried_ref, x)
    xhat, _ = norm_parts(x)
    normed = (xhat * gain_ref[0:1, :] + nbias_ref[0:1, :]).astype(bf16)
    window_in = per_image(lambda i: nn(move_ref[...], normed[image_rows(i)]), count).astype(bf16)
    store(window_ref, window_in)

    @pl.when(step == 0)
    def _():
        if gather:
            for k in (0, 1):
                moving.forward(k)
            for k in (2, 3):
                moving.start(k)
            for k in (0, 1):
                moving.arrive(k)
            qkv_full[...] = join(qkv_ref)
        elif first:
            form_bias(biases_ref, table_ref, entry_ref[...])
        proj_full[...] = join(proj_ref).astype(f32).T.astype(bf16)
        total_ref[...] = jnp.zeros(total_ref.shape, f32)

    qkv = join(qkv_ref)
    turned = nt(qkv, window_in).astype(bf16)
    straight = nt(window_in, qkv[width:]).astype(bf16)
    for i in range(count):
        qk_ref[i] = turned[: 2 * width, image_rows(i)]
    store(v_ref, straight[:, width:])
    heads_rows = head_masks()
    halves = lane_masks()
    low_lane = iota((WPAD, LANES), 1) < WPAD
    if shifted:
        row_labels = [nt(row_ref[i].astype(f32).astype(bf16), move_ref[...]) for i in range(count)]
        col_labels = [nn(move_ref[...], col_ref[i].astype(f32).astype(bf16)) for i in range(count)]
    for pair in range(PAIRS * count):
        image, side = pair // PAIRS, pair % PAIRS
        across = slice(pair * LANES, (pair + 1) * LANES)
        within = slice(side * LANES, (side + 1) * LANES)
        if shifted:
            ahead = col_labels[image][side * LANES : side * LANES + WPAD, 1:2]
            behind = col_labels[image][side * LANES + WPAD : (side + 1) * LANES, 1:2]
            key_label = jnp.where(low_lane, ahead, behind)
            mask = jnp.where(key_label == row_labels[image][1:2, within], 0.0, mask_fill)
        for group in range(HEADS // GROUP):
            features = slice(group * LANES, (group + 1) * LANES)
            queries = turned[features, across]
            spread = jnp.concatenate([queries * heads_rows[h] for h in range(GROUP)], 1)
            raw = nn(straight[across, features], spread)
            for h in range(GROUP):
                head = group * GROUP + h
                part = raw[:, h * LANES : (h + 1) * LANES]
                scores = jnp.where(low_lane, part[:WPAD], part[WPAD:]) * head_scale + bias_ref[head]
                if shifted:
                    scores = scores + mask
                expo = jnp.exp(scores - jnp.max(scores, 0, keepdims=True))
                probs = (expo * (1.0 / jnp.sum(expo, 0, keepdims=True))).astype(bf16)
                probs_ref[image, side * HEADS + head] = probs
                both = jnp.concatenate([probs * halves[0], probs * halves[1]], 0)
                at = slice(head * HEAD_DIM, (head + 1) * HEAD_DIM)
                values = turned[2 * width + head * HEAD_DIM : 2 * width + (head + 1) * HEAD_DIM, across]
                att_ref[image, at, within] = nn(values, both).astype(bf16)
    attended = per_image(lambda i: nt(back_ref[...], att_ref[i]), count).astype(bf16)
    branch = nt(attended, join(proj_ref))
    middle = x + per_image(lambda i: valid_ref[step * count + i].astype(f32) * branch[image_rows(i)], count)
    store(middle_ref, middle)
    xhat, _ = norm_parts(middle)
    second_low = (xhat * gain_ref[1:2, :] + nbias_ref[1:2, :]).astype(bf16)
    store(second_ref, second_low)
    _, _, gate = route(second_low, router_ref[...], pos_col)
    store(gate_ref, gate)
    total_ref[...] += spread_rows(lay_positions(row_ref), second_low)

    @pl.when(step == final)
    def _():
        buffer_ref[...] = total_ref[...].astype(bf16)
        if gather:
            for k in (2, 3):
                moving.forward(k)
            for k in (2, 3):
                moving.arrive(k)
            for k in range(4):
                moving.sent(k)


def image_spec(array_shape, count):
    rest = tuple(array_shape[1:])
    zeros = (0,) * len(rest)
    return pl.BlockSpec((count,) + rest, lambda i: (i,) + zeros)


def whole_spec(array_shape):
    zeros = (0,) * len(array_shape)
    return pl.BlockSpec(tuple(array_shape), lambda i: zeros)


def image_call(kernel, images, arrays, outs, scratch, name, collective_id=None):
    count = 2 - images % 2

    def spec(kind, shape):
        if isinstance(kind, int):
            rest = tuple(shape[1:])
            return pl.BlockSpec((1,) + rest, lambda i: (kind,) + (0,) * len(rest))
        if kind in ("smem", "any"):
            return pl.BlockSpec(memory_space=pltpu.SMEM if kind == "smem" else pl.ANY)
        return image_spec(shape, count) if kind == "image" else whole_spec(shape)

    return pl.pallas_call(
        kernel,
        grid=(images // count,),
        out_shape=[jax.ShapeDtypeStruct(shape, dtype) for _, shape, dtype in outs],
        in_specs=[spec(kind, array.shape) for kind, array in arrays],
        out_specs=[spec(kind, shape) for kind, shape, _ in outs],
        scratch_shapes=scratch,
        compiler_params=pltpu.CompilerParams(
            vmem_limit_bytes=51 * MIB,
            dimension_semantics=("arbitrary",),
            collective_id=collective_id,
            has_side_effects=collective_id is not None,
        ),
        name=name,
    )(*[array for _, array in arrays])


def send_part(g, expert_out, second_low, router, pos_col, pos_row, logit_ref, router_grad_ref, total_ref):
    probs, chosen, gate = route(second_low, router, pos_col)
    gate_grad = jnp.where(pos_col >= 0, jnp.sum(g * expert_out, -1, keepdims=True), 0.0)
    sent = (gate * g).astype(bf16)
    logit_grad = gate_grad * gate * (chosen - probs)
    store(logit_ref, logit_grad)
    high, low = split_two(logit_grad)
    router_grad_ref[...] += tn(high, second_low) + tn(low, second_low)
    total_ref[...] += spread_rows(pos_row, sent)


def turn_kernel(
    prev_ref, gate_ref, returned_ref, cotangent_ref, enter_ref, leave_ref, col_ref, row_ref, second_ref, router_ref,
    block_ref, grad_ref, logit_ref, router_grad_ref, buffer_ref, total_ref,
):
    step = pl.program_id(0)
    count = cotangent_ref.shape[0]

    @pl.when(step == 0)
    def _():
        total_ref[...] = jnp.zeros(total_ref.shape, f32)
        router_grad_ref[...] = jnp.zeros(router_grad_ref.shape, f32)

    pos_col = join(col_ref)[:, 0:1]
    expert_out = collect(pos_col, returned_ref)
    x = (join(prev_ref) + join(gate_ref) * expert_out).astype(bf16)
    for i in range(count):
        block_ref[i] = nn(leave_ref[...], x[image_rows(i)]).astype(bf16)
    g = per_image(lambda i: nn(enter_ref[...], cotangent_ref[i]), count)
    store(grad_ref, g)
    send_part(
        g, expert_out, join(second_ref), router_ref[0], pos_col, lay_positions(row_ref), logit_ref, router_grad_ref, total_ref
    )

    @pl.when(step == pl.num_programs(0) - 1)
    def _():
        buffer_ref[...] = total_ref[...].astype(bf16)


def attention_backward_kernel(last, dp, mp, fast, *refs):
    (
        valid_ref, grad_ref, returned_ref, logit_ref, middle_ref, carried_ref, router_ref, col_ref, move_ref, back_ref,
        gain_ref, proj_ref, qkv_ref, window_ref, qk_ref, v_ref, probs_ref, att_ref,
    ) = refs[:18]
    refs = refs[18:]
    refs = list(refs)
    if fast:
        units_ref = refs.pop(0)
    if last:
        leave_ref = refs.pop(0)
        if fast:
            table_above, small_above, router_above, router_here, entry_ref, half_above, down_above, attn_above = refs[:8]
            refs = refs[8:]
    else:
        row_ref, expert_out_ref, second_ref, router_next_ref = refs[:4]
        refs = refs[4:]
    out_ref = refs.pop(0)
    closing = None
    if fast and last:
        results, refs = refs[:4], refs[4:]
    else:
        if fast:
            halves_ref = refs.pop(0)
            unit_ref, mine_ref = refs[:2]
        else:
            qkv_grad_ref, proj_grad_ref = refs[:2]
        table_ref, small_ref = refs[2:4]
        refs = refs[4:]
    if not last:
        logit_out_ref, router_grad_ref, buffer_ref = refs[:3]
        refs = refs[3:]
    turned = refs.pop(0)
    if fast:
        qkv_grad_ref, proj_grad_ref = refs[:2]
        refs = refs[2:]
    if not last:
        total_ref = refs.pop(0)
    step = pl.program_id(0)
    final = pl.num_programs(0) - 1
    count, _, width = carried_ref.shape
    if fast:
        row = Row()
        if last:
            table_ref, small_ref, unit_ref, lines_ref = refs[:4]
            landing, refs = refs[4:8], refs[8:]
            above = (half_above, down_above.at[1], attn_above)
            closing = Closing(row, dp, units_ref, unit_ref, lines_ref, above, landing, refs)
        else:
            sums = RowSum(row, blocks(units_ref), refs[0], refs[1], refs[2], blocks(mine_ref), refs[3:7])
            across_x = DeepSum(dp, [mine_ref.at[0]], [refs[7]], [halves_ref], [None], [None], refs[8:10] * 4)

        def take(k):
            if closing:
                closing.take(k)
            else:
                sums.end(k)
                if k == 0:
                    across_x.over_x(k).start()

        @pl.when(step == 0)
        def _():
            if closing:
                closing.enter()
            else:
                barrier = row.greet()
                pl.semaphore_wait(barrier, 2 + across_x.greet(barrier, False))
                for k in range(2):
                    sums.start(k)

    @pl.when(step == 0)
    def _():
        qkv_grad_ref[...] = jnp.zeros(qkv_grad_ref.shape, f32)
        proj_grad_ref[...] = jnp.zeros(proj_grad_ref.shape, f32)
        table_ref[...] = jnp.zeros(table_ref.shape, f32)
        small_ref[...] = jnp.zeros(small_ref.shape, f32)
        if not last:
            total_ref[...] = jnp.zeros(total_ref.shape, f32)
            router_grad_ref[...] = jnp.zeros(router_grad_ref.shape, f32)

    pos_col = join(col_ref)[:, 0:1]
    g = join(grad_ref)
    high, low = split_two(join(logit_ref))
    gain_ref, router = gain_ref.at[0], router_ref[0]
    normed_grad = collect(pos_col, returned_ref) + nn(high, router) + nn(low, router)
    xhat, rstd = norm_parts(join(middle_ref))
    small_ref[1:2, :] += jnp.sum(normed_grad * xhat, 0, keepdims=True)
    small_ref[3:4, :] += jnp.sum(normed_grad, 0, keepdims=True)
    middle_grad = g + norm_back(normed_grad, gain_ref[1:2, :], xhat, rstd)

    def branch_part(i):
        low_part = (valid_ref[step * count + i].astype(f32) * middle_grad[image_rows(i)]).astype(bf16)
        return nn(move_ref[...], low_part)

    branch_grad = per_image(branch_part, count).astype(bf16)
    for i in range(count):
        proj_grad_ref[...] += nn(att_ref[i], branch_grad[image_rows(i)])
    att_grad = nt(proj_ref[...], branch_grad).astype(bf16)
    if fast:

        @pl.when(step == 0)
        def _():
            if closing:
                closing.early()
            else:
                for k in range(2):
                    sums.middle(k)

        pl.when(step == final)(functools.partial(take, 0))

    heads_rows = head_masks()
    halves = lane_masks()
    low_lane = iota((WPAD, LANES), 1) < WPAD
    for pair in range(PAIRS * count):
        image, side = pair // PAIRS, pair % PAIRS
        across = slice(pair * LANES, (pair + 1) * LANES)
        within = slice(side * LANES, (side + 1) * LANES)
        for group in range(HEADS // GROUP):
            features = slice(group * LANES, (group + 1) * LANES)
            grads = att_grad[features, across]
            spread = jnp.concatenate([grads * heads_rows[h] for h in range(GROUP)], 1)
            raw = nn(v_ref[image, within, features], spread)
            for h in range(GROUP):
                head = group * GROUP + h
                at = slice(head * HEAD_DIM, (head + 1) * HEAD_DIM)
                below = slice(width + head * HEAD_DIM, width + (head + 1) * HEAD_DIM)
                lowest = slice(2 * width + head * HEAD_DIM, 2 * width + (head + 1) * HEAD_DIM)
                part = raw[:, h * LANES : (h + 1) * LANES]
                probs_grad = jnp.where(low_lane, part[:WPAD], part[WPAD:])
                probs_low = probs_ref[image, side * HEADS + head]
                probs = probs_low.astype(f32)
                weighted = probs * probs_grad
                scores_grad = weighted - probs * jnp.sum(weighted, 0, keepdims=True)
                table_ref[head] += scores_grad
                scores_low = scores_grad.astype(bf16)
                both = jnp.concatenate([scores_low * halves[0], scores_low * halves[1]], 0)
                probs_both = jnp.concatenate([probs_low * halves[0], probs_low * halves[1]], 0)
                turned[at, across] = (nn(qk_ref[image, below, within], both) * head_scale).astype(bf16)
                turned[below, across] = (nt(qk_ref[image, at, within], both) * head_scale).astype(bf16)
                turned[lowest, across] = nt(att_grad[at, across], probs_both).astype(bf16)
    qkv_grad_ref[...] += nn(turned[...], join(window_ref))
    if fast:

        @pl.when(step == final)
        def _():
            columns, rows = 3 * width // mp, width // mp
            proj_turned = proj_grad_ref[...].T
            for place in range(mp):
                q = quarter_at(place, mp)
                unit_ref[place, :columns] = qkv_grad_ref[q * columns : (q + 1) * columns].astype(bf16)
                unit_ref[place, columns:] = proj_turned[q * rows : (q + 1) * rows].astype(bf16)
            if closing:
                closing.open()
            take(1)
            if closing:
                heads = 2 * HEADS
                lines_ref[...] = jnp.zeros(lines_ref.shape, f32)
                lines_ref[:heads, :TABLE] = table_grad([table_ref, table_above], entry_ref[...])

    mixed_grad = per_image(lambda i: nt(back_ref[...], turned[:, image_rows(i)]), count).astype(bf16)
    first_grad = nn(mixed_grad, qkv_ref[...])
    if closing:

        @pl.when(step == final)
        def _():
            closing.cross()

    xhat, rstd = norm_parts(join(carried_ref))
    small_ref[0:1, :] += jnp.sum(first_grad * xhat, 0, keepdims=True)
    small_ref[2:3, :] += jnp.sum(first_grad, 0, keepdims=True)
    if closing:

        @pl.when(step == final)
        def _():
            heads = 2 * HEADS
            lines_ref[heads : heads + EXPERTS] = router_here[:EXPERTS]
            lines_ref[heads + EXPERTS : heads + 2 * EXPERTS] = router_above[:EXPERTS]
            lines_ref[heads + 2 * EXPERTS : heads + 2 * EXPERTS + 8] = small_ref[...]
            lines_ref[heads + 2 * EXPERTS + 8 : heads + 2 * EXPERTS + 16] = small_above[...]
            closing.send_lines()

    out = middle_grad + norm_back(first_grad, gain_ref[0:1, :], xhat, rstd)
    if last:
        top = out.astype(bf16)
        rest = out - top.astype(f32)
        mid, low = split_two(rest)
        leave = leave_ref[...]
        for i in range(count):
            at = image_rows(i)
            out_ref[i] = nn(leave, top[at]) + nn(leave, mid[at]) + nn(leave, low[at])
    else:
        store(out_ref, out)
        send_part(
            out, join(expert_out_ref), join(second_ref), router_next_ref[0], pos_col, lay_positions(row_ref), logit_out_ref,
            router_grad_ref, total_ref,
        )

    @pl.when(step == final)
    def _():
        if not last:
            buffer_ref[...] = total_ref[...].astype(bf16)
        if closing:
            closing.finish()
            for out, landed in zip(results, landing):
                out[...] = landed[...]
        elif fast:
            across_x.halve(0)
            across_x.over_x(0).wait_send()
            for k in range(2):
                sums.finish(k)


def quarter_at(place, mp):
    return place % (mp // 2) * 2 + place // (mp // 2)


def add_up(*parts):
    total = parts[0].astype(f32)
    for part in parts[1:]:
        total = total + part.astype(f32)
    return total


def to_row(source, target, sems, k, row):
    return pltpu.make_async_remote_copy(
        src_ref=source,
        dst_ref=target,
        send_sem=sems[0].at[k],
        recv_sem=sems[1].at[k],
        device_id={"mp": row},
        device_id_type=MESH,
    )


class Row:
    def __init__(self):
        row = lax.axis_index("mp")
        self.row, self.core, self.y = row, lax.rem(row, 2), lax.div(row, 2)
        self.sibling, self.across = row + 1 - 2 * self.core, row + 2 - 4 * self.y
        self.place = self.core * 2 + self.y
        self.place_across = self.core * 2 + 1 - self.y

    def greet(self):
        barrier = pltpu.get_barrier_semaphore()
        for row in (self.sibling, self.across):
            pl.semaphore_signal(barrier, inc=1, device_id={"mp": row}, device_id_type=MESH)
        return barrier


class RowSum:
    semaphores = 4

    def __init__(self, row, units, core_in, y_out, y_in, mine, sems):
        self.row, self.units, self.mine = row, units, mine
        self.core_in, self.y_out, self.y_in = core_in, y_out, y_in
        self.sems = (sems[:2], sems[2:])

    def pair(self, k):
        theirs = self.units[k].at[pl.ds(2 * (1 - self.row.core), 2)]
        return to_row(theirs, self.core_in.at[k], self.sems[0], k, self.row.sibling)

    def cross(self, k):
        return to_row(self.y_out.at[k], self.y_in.at[k], self.sems[1], k, self.row.across)

    def start(self, k):
        self.pair(k).start()

    def middle(self, k):
        self.pair(k).wait_recv()
        other = 1 - self.row.y
        mixed = add_up(self.units[k][self.row.core * 2 + other], self.core_in[k, other])
        self.y_out[k] = mixed.astype(bf16)
        self.cross(k).start()

    def end(self, k):
        self.cross(k).wait_recv()
        self.mine[k][...] = add_up(
            self.units[k][self.row.place], self.core_in[k, self.row.y], self.y_in[k]
        ).astype(bf16)

    def finish(self, k):
        self.pair(k).wait_send()
        self.cross(k).wait_send()

    @classmethod
    def scratch(cls, count, width):
        return [
            pltpu.VMEM((count, 2, width, width), bf16),
            pltpu.VMEM((count, width, width), bf16),
            pltpu.VMEM((count, width, width), bf16),
        ] + [pltpu.SemaphoreType.DMA((count,))] * cls.semaphores


class RowGather:
    semaphores = 6

    def __init__(self, row, sources, fulls, slot, slot_across, sems):
        self.row, self.sources, self.fulls = row, sources, fulls
        self.slot, self.slot_across = slot, slot_across
        self.sems = (sems[:2], sems[2:4], sems[4:])

    def over(self, k):
        return to_row(self.sources[k], self.fulls[k].at[self.slot], self.sems[0], k, self.row.across)

    def near(self, k):
        return to_row(self.sources[k], self.fulls[k].at[self.slot], self.sems[1], k, self.row.sibling)

    def onward(self, k):
        block = self.fulls[k].at[self.slot_across]
        return to_row(block, block, self.sems[2], k, self.row.sibling)

    def start(self, k):
        self.over(k).start()
        self.near(k).start()

    def forward(self, k):
        self.over(k).wait_recv()
        self.onward(k).start()

    def arrive(self, k):
        self.near(k).wait_recv()
        self.onward(k).wait_recv()

    def sent(self, k):
        self.over(k).wait_send()
        self.near(k).wait_send()
        self.onward(k).wait_send()

    @classmethod
    def scratch(cls, count):
        return [pltpu.SemaphoreType.DMA((count,))] * cls.semaphores


class WeightGather(RowGather):
    def __init__(self, shards, fulls, sems):
        row = Row()
        super().__init__(row, shards, fulls, row.row, row.across, sems[:6])
        self.own_sem = sems[6]

    def own(self, k):
        return pltpu.make_async_copy(self.sources[k], self.fulls[k].at[self.slot], self.own_sem.at[k])

    def start(self, k):
        super().start(k)
        self.own(k).start()

    def arrive(self, k):
        super().arrive(k)
        self.own(k).wait()

    @classmethod
    def scratch(cls, count):
        return super().scratch(count) + [pltpu.SemaphoreType.DMA((count,))]


class DeepSum:
    def __init__(self, dp, total, arrived, halves, slots, result, sems):
        self.total, self.arrived, self.halves, self.slots, self.result = total, arrived, halves, slots, result
        self.x_sems, self.z_sems, self.z_back, self.x_back = (sems[2 * k : 2 * k + 2] for k in range(4))
        me = lax.axis_index("dp")
        self.x, self.z, self.deep = lax.rem(me, 2), lax.div(me, 2), dp // 2
        self.partner = me + 1 - 2 * self.x

    def greet(self, barrier, whole=True):
        pl.semaphore_signal(barrier, inc=1, device_id={"dp": self.partner}, device_id_type=MESH)
        if not whole:
            return 1
        for off in range(1, self.deep):
            peer = lax.rem(self.z + off, self.deep) * 2 + self.x
            pl.semaphore_signal(barrier, inc=1, device_id={"dp": peer}, device_id_type=MESH)
        return self.deep

    def cut(self, k):
        height = self.halves[k].shape[0]
        return height, height // self.deep

    def over_x(self, k):
        height, _ = self.cut(k)
        away = self.total[k].at[pl.ds(pl.multiple_of((1 - self.x) * height, height), height)]
        return to_peer(away, self.arrived[k], self.x_sems[0].at[k], self.x_sems[1].at[k], self.partner)

    def over_z(self, k, off):
        _, piece = self.cut(k)
        to = lax.rem(self.z + off, self.deep)
        part = self.halves[k].at[pl.ds(pl.multiple_of(to * piece, piece), piece)]
        sems = [sem.at[k, off] for sem in self.z_sems]
        return to_peer(part, self.slots[k].at[off], *sems, to * 2 + self.x)

    def own_piece(self, k):
        height, piece = self.cut(k)
        return self.result[k].at[pl.ds(pl.multiple_of(self.x * height + self.z * piece, piece), piece)]

    def own_half(self, k):
        height, _ = self.cut(k)
        return self.result[k].at[pl.ds(pl.multiple_of(self.x * height, height), height)]

    def back_z(self, k, off):
        to = lax.rem(self.z + off, self.deep)
        sems = [sem.at[k, off] for sem in self.z_back]
        return to_peer(self.own_piece(k), self.own_piece(k), *sems, to * 2 + self.x)

    def back_x(self, k):
        return to_peer(self.own_half(k), self.own_half(k), self.x_back[0].at[k], self.x_back[1].at[k], self.partner)

    def halve(self, k):
        self.over_x(k).wait_recv()
        height, _ = self.cut(k)
        keep = self.total[k][pl.ds(pl.multiple_of(self.x * height, height), height)]
        self.halves[k][...] = add_up(keep, self.arrived[k][...]).astype(self.halves[k].dtype)

    def deepen(self, k):
        for off in range(1, self.deep):
            self.over_z(k, off).start()

    def quarter(self, k):
        for off in range(1, self.deep):
            self.over_z(k, off).wait_recv()
        _, piece = self.cut(k)
        keep = self.halves[k][pl.ds(pl.multiple_of(self.z * piece, piece), piece)]
        total = add_up(keep, *[self.slots[k][off] for off in range(1, self.deep)])
        self.own_piece(k)[...] = total.astype(self.result[k].dtype)
        for off in range(1, self.deep):
            self.back_z(k, off).start()

    def widen(self, k):
        for off in range(1, self.deep):
            self.back_z(k, off).wait_recv()
        self.back_x(k).start()

    def finish(self, k, halved=True):
        if halved:
            self.over_x(k).wait_send()
        for off in range(1, self.deep):
            self.over_z(k, off).wait_send()
            self.back_z(k, off).wait_send()
        self.back_x(k).wait()

    @staticmethod
    def semaphores(dp, count):
        one, many = pltpu.SemaphoreType.DMA((count,)), pltpu.SemaphoreType.DMA((count, dp // 2))
        return [one, one, many, many, many, many, one, one]


def blocks(ref):
    return [ref.at[k] for k in range(ref.shape[0])]


class WideSum:
    def __init__(self, dp, total, slots, result, sems):
        self.dp, self.total, self.slots, self.result, self.sems = dp, total, slots, result, sems
        self.me = lax.axis_index("dp")

    def piece(self, ref, at):
        size = ref.shape[0] // self.dp
        return ref.at[pl.ds(pl.multiple_of(at * size, size), size)]

    def out(self, k, p):
        peer = partner_of(self.me, p, self.dp)
        sems = self.sems[0].at[k, p], self.sems[1].at[k, p]
        return to_peer(self.piece(self.total[k], peer), self.slots[k].at[p], *sems, peer)

    def back(self, k, p):
        mine = self.piece(self.result[k], self.me)
        sems = self.sems[2].at[k, p], self.sems[3].at[k, p]
        return to_peer(mine, mine, *sems, partner_of(self.me, p, self.dp))

    def start(self, k):
        for p in range(self.dp - 1, 0, -1):
            self.out(k, p).start()

    def middle(self, k):
        for p in range(1, self.dp):
            self.out(k, p).wait_recv()
        total = add_up(self.piece(self.total[k], self.me)[...], *[self.slots[k][p] for p in range(1, self.dp)])
        self.piece(self.result[k], self.me)[...] = total.astype(self.result[k].dtype)
        for p in range(self.dp - 1, 0, -1):
            self.back(k, p).start()

    def finish(self, k):
        for p in range(1, self.dp):
            self.out(k, p).wait_send()
            self.back(k, p).wait()

    @staticmethod
    def semaphores(dp, count):
        return [pltpu.SemaphoreType.DMA((count, dp))] * 4


class Closing:
    lines = 64

    def __init__(self, row, dp, units_ref, attn_ref, lines_ref, given, results, refs):
        self.row, self.lines_ref, self.dp = row, lines_ref, dp
        self.full, shard, small, above = results
        core_in, y_out, y_in = refs[:3]
        mine, x_in, half, z_in, self.s_core, self.s_one, self.s_y, self.s_mine, s_slots, wide_in = refs[7:17]
        x_above, half_above, z_above = refs[17:20]
        refs_sems, refs = refs[3:7], refs[20:]
        self.mine = mine
        self.sums = RowSum(row, blocks(units_ref) + [attn_ref], core_in, y_out, y_in, blocks(mine), refs_sems)
        self.gather = RowGather(
            row, [mine.at[k] for k in range(2)], blocks(self.full), row.place, row.place_across, refs[:6]
        )
        self.s_pair = to_row(lines_ref, self.s_core, refs[6:8], 0, row.sibling)
        self.s_cross = to_row(self.s_one, self.s_y, refs[8:10], 0, row.across)
        self.here = DeepSum(
            dp, [mine.at[0], mine.at[1]], blocks(x_in), blocks(half), blocks(z_in), [shard.at[0], shard.at[1]], refs[10:18]
        )
        self.above = DeepSum(
            dp, [None, *given[1:]], [None] + blocks(x_above), [given[0]] + blocks(half_above), blocks(z_above), blocks(above),
            refs[18:26],
        )
        self.wide = WideSum(dp, [mine.at[2], self.s_mine], [wide_in, s_slots], [shard.at[2], small], refs[26:30])

    def enter(self):
        greet(self.dp, lax.axis_index("dp"), (self.row.sibling, self.row.across))
        for k in range(2):
            self.sums.start(k)
        self.above.deepen(0)
        for k in (1, 2):
            self.above.over_x(k).start()

    def early(self):
        for k in range(2):
            self.sums.middle(k)
        for k in (1, 2):
            self.above.halve(k)
            self.above.deepen(k)
        self.above.quarter(0)

    def take(self, k):
        self.sums.end(k)
        self.here.over_x(k).start()
        if k == 0:
            self.above.widen(0)
            for j in (1, 2):
                self.above.quarter(j)
        else:
            for j in (1, 2):
                self.above.widen(j)

    def open(self):
        self.sums.start(2)

    def cross(self):
        self.sums.middle(2)
        for k in range(2):
            self.here.halve(k)
            self.here.deepen(k)

    def send_lines(self):
        self.s_pair.start()
        for k in range(2):
            self.here.quarter(k)
        self.s_pair.wait_recv()
        self.s_one[...] = self.lines_ref[...] + self.s_core[...]
        self.s_cross.start()

    def finish(self):
        self.sums.end(2)
        self.wide.start(0)
        self.s_cross.wait_recv()
        self.s_mine[...] = self.s_one[...] + self.s_y[...]
        self.wide.start(1)
        for k in range(2):
            self.gather.start(k)
            self.full[k, self.row.place] = self.mine[k]
        self.wide.middle(0)
        self.wide.middle(1)
        for k in range(2):
            self.here.widen(k)
        for k in range(2):
            self.gather.forward(k)
        self.s_pair.wait_send()
        self.s_cross.wait_send()
        for k in range(3):
            self.sums.finish(k)
            self.above.finish(k, k > 0)
        for k in range(2):
            self.here.finish(k)
            self.wide.finish(k)
            self.gather.arrive(k)
            self.gather.sent(k)

    @classmethod
    def scratch(cls, dp, width):
        deep = dp // 2
        lines = cls.lines
        flat = pltpu.VMEM((lines, width), f32)
        half, slots = (width // 2, width), (deep, width // dp, width)
        return (
            RowSum.scratch(3, width)
            + [
                pltpu.VMEM((3, width, width), bf16),
                pltpu.VMEM((2, *half), bf16),
                pltpu.VMEM((2, *half), bf16),
                pltpu.VMEM((2, *slots), bf16),
                flat, flat, flat, flat,
                pltpu.VMEM((dp, lines // dp, width), f32),
                pltpu.VMEM((dp, width // dp, width), bf16),
                pltpu.VMEM((2, *half), bf16),
                pltpu.VMEM((2, *half), bf16),
                pltpu.VMEM((3, *slots), bf16),
            ]
            + RowGather.scratch(2)
            + [pltpu.SemaphoreType.DMA((1,))] * 4
            + DeepSum.semaphores(dp, 2)
            + DeepSum.semaphores(dp, 3)
            + WideSum.semaphores(dp, 2)
        )


def format_kernel(columns, *refs):
    count = (len(refs) - 6) // 2
    qkv_out, proj_out, core_up_out, core_down_out, up_out, down_out = refs[2 * count :]

    def form(full, shard):
        mp, width = full.shape[1], full.shape[2]
        rows = width // mp
        qkv_out[0] = shard[2, :columns].astype(f32)
        proj_out[0] = shard[2, columns:].astype(f32)
        core_up_out[0] = shard[0].astype(f32)
        for place in range(mp):
            q = quarter_at(place, mp)
            up_out[0, 0, :, q * width : (q + 1) * width] = full[0, place].astype(f32)
        for chunk in range(mp):
            at = slice(chunk * width, (chunk + 1) * width)
            core_down_out[0, :, at] = shard[1, chunk * rows : (chunk + 1) * rows].astype(f32)
            block = [None] * mp
            for place in range(mp):
                block[quarter_at(place, mp)] = full[1, place, chunk * rows : (chunk + 1) * rows]
            down_out[0, 0, at, :] = turn_blocks(jnp.concatenate(block, 0))

    for layer in range(count):
        pl.when(pl.program_id(0) == layer)(functools.partial(form, refs[layer], refs[count + layer]))


def format_call(fulls, shards, columns):
    layers = len(fulls)
    _, mp, width, _ = fulls[0].shape
    hidden = mp * width
    shapes = [
        (layers, columns, width),
        (layers, width - columns, width),
        (layers, width, width),
        (layers, width // mp, hidden),
        (layers, 1, width, hidden),
        (layers, 1, hidden, width),
    ]
    return pl.pallas_call(
        functools.partial(format_kernel, columns),
        grid=(layers,),
        out_shape=[jax.ShapeDtypeStruct(shape, f32) for shape in shapes],
        in_specs=[whole_spec(a.shape) for a in (*fulls, *shards)],
        out_specs=[image_spec(shape, 1) for shape in shapes],
        compiler_params=pltpu.CompilerParams(vmem_limit_bytes=56 * MIB),
        name="format",
    )(*fulls, *shards)


def greet(dp, me, rows=()):
    barrier = pltpu.get_barrier_semaphore()
    for row in rows:
        pl.semaphore_signal(barrier, inc=1, device_id={"mp": row}, device_id_type=MESH)

    def signal(off, carry):
        pl.semaphore_signal(barrier, inc=1, device_id={"dp": lax.rem(me + off, dp)}, device_id_type=MESH)
        return carry

    lax.fori_loop(1, dp, signal, 0)
    pl.semaphore_wait(barrier, dp - 1 + len(rows))


def partner_of(me, p, dp):
    out, bit = 0, 1
    while bit < dp:
        one, two = lax.rem(lax.div(me, bit), 2), lax.rem(lax.div(p, bit), 2)
        out = out + bit * (one + two - 2 * one * two)
        bit *= 2
    return out


def to_peer(source, target, send_sem, recv_sem, peer):
    return pltpu.make_async_remote_copy(
        src_ref=source,
        dst_ref=target,
        send_sem=send_sem,
        recv_sem=recv_sem,
        device_id={"dp": peer},
        device_id_type=MESH,
    )


def gelu_parts(h):
    root = np.float32(np.sqrt(2.0 / np.pi))
    square = h * h
    t = jnp.tanh(root * h * (1.0 + 0.044715 * square))
    half = 0.5 * (1.0 + t)
    slope = half + 0.5 * h * (1.0 - t * t) * root * (1.0 + 3 * 0.044715 * square)
    return h * half, slope


def expert_forward_kernel(dp, mp, layer, gather, *refs):
    refs = list(refs)
    buffer_ref, up_any, down_any, rup_any, rdown_any = refs[:5]
    refs = refs[5:]
    if gather:
        shards = [ref.at[layer + 1] for ref in refs[:4]]
        refs = refs[4:]
    returned_ref, recv_out, up_out, down_out = refs[:4]
    refs = refs[4:]
    if gather:
        fulls = refs[:4]
        refs = refs[4:]
    part, core, up_ref, down_ref, rup_ref, rdown_ref, recv_ref, up_eff, down_eff, local = refs[:10]
    refs = refs[10:]
    moving = WeightGather(shards, fulls, refs[:7]) if gather else None
    send_one, recv_one, send_two, recv_two = refs[-4:]
    split = dp // EXPERTS
    me = lax.axis_index("dp")
    loads = [
        pltpu.make_async_copy(source, target, local.at[k])
        for k, (source, target) in enumerate(
            [
                (up_any, up_ref),
                (rup_any.at[layer, 0], rup_ref),
                (down_any, down_ref),
                (rdown_any.at[layer, 0], rdown_ref),
                (buffer_ref.at[lax.div(me, split)], recv_ref.at[me]),
            ]
        )
    ]
    stores = [
        pltpu.make_async_copy(source, target, local.at[5 + k])
        for k, (source, target) in enumerate([(up_eff, up_out), (down_eff, down_out), (recv_ref, recv_out)])
    ]
    for load in loads:
        load.start()
    greet(dp, me, (moving.row.sibling, moving.row.across) if gather else ())

    def first(off):
        peer = partner_of(me, off, dp)
        return to_peer(
            buffer_ref.at[lax.div(peer, split)], recv_ref.at[me], send_one.at[off], recv_one.at[off], peer
        )

    def second(off):
        source = partner_of(me, off, dp)
        return to_peer(part.at[source], returned_ref.at[me], send_two.at[off], recv_two.at[off], source)

    def start_first(off, carry):
        first(dp - off).start()
        return carry

    lax.fori_loop(1, dp, start_first, 0)
    if gather:
        for k in range(4):
            moving.start(k)
    hidden = up_eff.shape[1]
    columns = up_ref.shape[-1]
    loads[0].wait()
    loads[1].wait()
    if split == 1 and columns % LANES == 0:
        for m in range(mp):
            at = slice(m * columns, (m + 1) * columns)
            up_eff[:, at] = (up_ref[m].astype(f32) + rup_ref[:, at].astype(f32)).astype(bf16)
    else:
        core[...] = rup_ref[...].astype(f32)
        begin = lax.rem(me, split) * hidden
        for m in range(mp):
            put = onehot(iota((columns, hidden), 0) + m * columns == iota((columns, hidden), 1) + begin)
            core[...] += nn(up_ref[m], put)
        up_eff[...] = core[...].astype(bf16)
    begin = pl.multiple_of(lax.rem(me, split) * hidden, LANES)
    loads[2].wait()
    loads[3].wait()
    core_part = down_ref[:, :, pl.ds(begin, hidden)].reshape(down_eff.shape[1], hidden)
    down_eff[...] = (core_part.astype(f32).T + rdown_ref[...].astype(f32)).astype(bf16)

    stores[0].start()
    stores[1].start()
    loads[4].wait()

    def work(source):
        hidden_pre = nn(recv_ref[source], up_eff[...])
        hidden_low = gelu_parts(hidden_pre)[0].astype(bf16)
        return nn(hidden_low, down_eff[...]).astype(bf16)

    returned_ref[me] = work(me)

    def step(off, carry):
        source = partner_of(me, off, dp)
        first(off).wait_recv()
        part[source] = work(source)
        second(off).start()
        return carry

    lax.fori_loop(1, dp, step, 0)
    stores[2].start()
    if gather:
        for k in range(4):
            moving.forward(k)

    def finish(off, carry):
        first(off).wait_send()
        second(off).wait()
        return carry

    lax.fori_loop(1, dp, finish, 0)
    if gather:
        for k in range(4):
            moving.arrive(k)
            moving.sent(k)
    for store_out in stores:
        store_out.wait()


def expert_backward_kernel(dp, mp, fast, reduce, *refs):
    refs = list(refs)
    if reduce:
        given_ref, attn_ref = refs[:2]
        refs = refs[2:]
    buffer_ref, recv_any, up_any, down_any = refs[:4]
    refs = refs[4:]
    returned_ref = refs.pop(0)
    if not fast:
        up_term, down_term = refs[:2]
        refs = refs[2:]
    if reduce:
        full_ref, mine_ref = refs[:2]
        refs = refs[2:]
    if fast:
        units_out = refs.pop(0)
    recv_ref, up_ref, down_ref, local = refs[:4]
    refs = refs[4:]
    if fast:
        units_ref = refs.pop(0)
    grads, hidden_low, slope, pre, part = refs[:5]
    refs = refs[5:]
    if fast:
        up_term, down_term = refs[:2]
        refs = refs[2:]
    row = Row() if reduce else None
    if reduce:
        core_in, y_out, y_in = refs[:3]
        sums = RowSum(row, [attn_ref], core_in, y_out, y_in, [mine_ref], refs[3:7])
        gather = RowGather(
            row, [given_ref.at[k] for k in range(2)], [full_ref.at[k] for k in range(2)], row.place, row.place_across,
            refs[7:13],
        )
        refs = refs[13:]
    send_one, recv_one, send_two, recv_two = refs
    split = dp // EXPERTS
    me = lax.axis_index("dp")
    loads = [
        pltpu.make_async_copy(source, target, local.at[k])
        for k, (source, target) in enumerate(
            [
                (recv_any, recv_ref),
                (up_any, up_ref),
                (down_any, down_ref),
                (buffer_ref.at[lax.div(me, split)], grads.at[me]),
            ]
        )
    ]
    for load in loads:
        load.start()
    greet(dp, me, (row.sibling, row.across) if reduce else ())

    def first(off):
        peer = partner_of(me, off, dp)
        return to_peer(buffer_ref.at[lax.div(peer, split)], grads.at[me], send_one.at[off], recv_one.at[off], peer)

    def second(off):
        source = partner_of(me, off, dp)
        return to_peer(part.at[source], returned_ref.at[me], send_two.at[off], recv_two.at[off], source)

    def start_first(off, carry):
        first(dp - off).start()
        return carry

    lax.fori_loop(1, dp, start_first, 0)
    if reduce:
        sums.start(0)
        for k in range(2):
            gather.start(k)
    for load in loads[:2]:
        load.wait()

    def again(source, carry):
        value, rate = gelu_parts(nn(recv_ref[source], up_ref[...]))
        hidden_low[source] = value.astype(bf16)
        slope[source] = rate
        return carry

    lax.fori_loop(0, dp, again, 0)
    if reduce:
        sums.middle(0)
        for k in range(2):
            full_ref[k, row.place] = given_ref[k]

    for load in loads[2:]:
        load.wait()

    def work(source):
        hidden_grad = nt(grads[source], down_ref[...])
        pre_grad = (slope[source] * hidden_grad).astype(bf16)
        pre[source] = pre_grad
        return nt(pre_grad, up_ref[...]).astype(bf16)

    returned_ref[me] = work(me)

    def step(off, carry):
        source = partner_of(me, off, dp)
        first(off).wait_recv()
        part[source] = work(source)
        second(off).start()
        return carry

    lax.fori_loop(1, dp, step, 0)
    if reduce:
        for k in range(2):
            gather.forward(k)
        sums.end(0)
    up_term[...] = jnp.zeros(up_term.shape, f32)
    down_term[...] = jnp.zeros(down_term.shape, f32)

    def terms(block, carry):
        up_term[...] += tn(recv_ref[block], pre[block])
        down_term[...] += tn(grads[block], hidden_low[block])
        return carry

    lax.fori_loop(0, dp, terms, 0)
    if fast:
        width = up_term.shape[0]
        height = width // mp
        for place in range(mp):
            q = quarter_at(place, mp)
            units_ref[0, place] = up_term[:, q * width : (q + 1) * width].astype(bf16)
            for chunk in range(mp):
                block = down_term[q * height : (q + 1) * height, chunk * width : (chunk + 1) * width]
                units_ref[1, place, chunk * height : (chunk + 1) * height] = block.astype(bf16)
        units_store = pltpu.make_async_copy(units_ref, units_out, local.at[4])
        units_store.start()

    def finish(off, carry):
        first(off).wait_send()
        second(off).wait()
        return carry

    lax.fori_loop(1, dp, finish, 0)
    if reduce:
        sums.finish(0)
        for k in range(2):
            gather.arrive(k)
            gather.sent(k)
    if fast:
        units_store.wait()


def expert_call(kernel, arrays, outs, scratch, dp, collective_id, name, flops, anys=(), any_outs=()):
    sems = [pltpu.SemaphoreType.DMA((dp,))] * 4
    vmem, anywhere = pl.BlockSpec(memory_space=pltpu.VMEM), pl.BlockSpec(memory_space=pl.ANY)
    return pl.pallas_call(
        kernel,
        out_shape=[jax.ShapeDtypeStruct(shape, dtype) for shape, dtype in (*outs, *any_outs)],
        in_specs=[vmem] * len(arrays) + [anywhere] * len(anys),
        out_specs=[vmem] * len(outs) + [anywhere] * len(any_outs),
        scratch_shapes=scratch + sems,
        compiler_params=pltpu.CompilerParams(
            vmem_limit_bytes=51 * MIB, collective_id=collective_id, has_side_effects=True
        ),
        cost_estimate=pl.CostEstimate(flops=flops, bytes_accessed=20 * MIB, transcendentals=0),
        name=name,
    )(*arrays, *anys)


def by_windows(grid):
    images, kinds = grid.shape[:2]
    blocks = GRID // WINDOW
    grid = grid.reshape(images, kinds, blocks, WINDOW, blocks, WINDOW).transpose(0, 1, 2, 4, 3, 5)
    grid = grid.reshape(images, kinds, blocks * blocks, WINPOS)
    grid = jnp.pad(grid, ((0, 0), (0, 0), (0, 0), (0, WPAD - WINPOS)), constant_values=-1)
    return grid.reshape(images, kinds, IMGROWS)


def per_device(
    patches,
    qkv_weight,
    proj_weight,
    core_up,
    core_down,
    residual_up,
    residual_down,
    position_bias,
    router_weight,
    norm_gain,
    norm_bias,
    cotangent,
    image_valid,
    expert_index,
    slot_index,
    region_id,
):
    dp, mp = lax.axis_size("dp"), lax.axis_size("mp")
    images, _, width = patches.shape
    split = dp // EXPERTS
    hidden = residual_up.shape[-1]
    hidden_full = core_up.shape[-1] * mp
    row_index = lax.axis_index("mp")

    fast = split == 1 and dp == 8 and mp == 4 and hidden == mp * width
    qkv_rows, proj_rows, down_rows = (a.transpose(0, 2, 1) for a in (qkv_weight, proj_weight, core_down))
    shards = (qkv_rows, proj_rows, core_up, down_rows)
    gathered = [[None] * len(shards)] * LAYERS
    if not fast:
        gathered = [[lax.all_gather(a[l], "mp", axis=0, tiled=False) for a in shards] for l in range(LAYERS)]

    position = jnp.where(slot_index >= 0, expert_index * SLOTS + slot_index, -1)
    row_form = by_windows(jnp.stack([position.reshape(images, GRID, GRID), region_id], 1))
    col_form = row_form.transpose(0, 2, 1)
    enter = jnp.asarray(enter_table(), bf16)
    leave = jnp.asarray(enter_table().T, bf16)
    moves = [jnp.asarray(move_table(l % 2 == 1), bf16) for l in range(LAYERS)]
    backs = [jnp.asarray(move_table(l % 2 == 1).T, bf16) for l in range(LAYERS)]
    table_rows = position_bias.transpose(0, 2, 1).reshape(LAYERS * HEADS, OFFSETS)
    table_rows = jnp.pad(table_rows, ((0, 0), (0, TABLE - OFFSETS)))
    entry_row, entry_col = jnp.asarray(cell_entries()[None, :]), jnp.asarray(cell_entries()[:, None])
    routers = jnp.pad(router_weight.transpose(0, 2, 1), ((0, 0), (0, LANES - EXPERTS), (0, 0)))

    token = (images, IMGROWS, width)
    buffer_shape = (ROWS, width)
    block_rows = (dp, SLOTS, width)
    pieces = (split, ROWS, width)

    def by_piece(returned):
        return returned.reshape(EXPERTS, split, SLOTS, width).transpose(1, 0, 2, 3).reshape(pieces)

    records = []
    before = None
    for l in range(LAYERS):
        first = l == 0
        gather = fast and first
        if first:
            arrays = [("image", patches), ("whole", enter)]
        else:
            arrays = [("image", before[0]), ("image", before[1]), ("whole", before[2])]
        arrays += [
            ("smem", image_valid),
            ("image", col_form),
            ("image", row_form),
            ("any", qkv_rows) if gather else ("whole", gathered[l][0]),
            ("any", proj_rows) if gather else ("whole", gathered[l][1]),
            ("whole", table_rows) if first else (l, biases),
            ("whole", moves[l]),
            ("whole", backs[l]),
            (l, norm_gain),
            (l, norm_bias),
            (l, routers),
        ]
        if first:
            arrays.append(("whole", entry_row))
        if gather:
            arrays += [("any", core_up), ("any", down_rows)]
        outs = [("image", token, f32)]
        if first:
            outs.append(("whole", (LAYERS, HEADS, WPAD, LANES), f32))
        else:
            outs.append(("image", token, f32))
        outs += [
            ("image", token, f32),
            ("image", token, bf16),
            ("image", (images, IMGROWS, 1), f32),
            ("whole", buffer_shape, bf16),
            ("image", token, bf16),
            ("image", (images, 2 * width, IMGROWS), bf16),
            ("image", token, bf16),
            ("image", (images, PAIRS * HEADS, WPAD, LANES), bf16),
            ("image", (images, width, IMGROWS), bf16),
            ("whole", (width, width), bf16),
        ]
        scratch = [pltpu.VMEM(buffer_shape, f32)]
        gathered_shapes = [(mp, *a.shape[1:]) for a in shards]
        if gather:
            outs.append(("whole", (3 * width, width), bf16))
            outs += [("any", shape, bf16) for shape in gathered_shapes[2:]]
            scratch += [pltpu.VMEM(shape, bf16) for shape in gathered_shapes[:2]] + WeightGather.scratch(4)
        results = list(
            image_call(
                functools.partial(attention_forward_kernel, first, l % 2 == 1, mp, gather),
                images, arrays, outs, scratch, f"attend_{l}", 3 * LAYERS + 1 if gather else None,
            )
        )
        if gather:
            gathered[l] = [results[-3], None] + results[-2:]
            results = results[:-3]
        carried = results.pop(0)
        if first:
            biases = results.pop(0)
        else:
            records[-1]["expert_out"] = results.pop(0)
        middle, second_low, gate, buffer = results[:4]
        gather = fast and l < LAYERS - 1
        eff_shapes = [((width, hidden), bf16), ((hidden, width), bf16)]
        returned, received, up_eff, down_eff, *more = expert_call(
            functools.partial(expert_forward_kernel, dp, mp, l, gather),
            [],
            [(block_rows, bf16)],
            [
                pltpu.VMEM(block_rows, bf16),
                pltpu.VMEM((8, LANES) if fast else (width, hidden), f32),
                pltpu.VMEM(gathered_shapes[2], bf16),
                pltpu.VMEM(gathered_shapes[3], bf16),
                pltpu.VMEM((width, hidden), bf16),
                pltpu.VMEM((hidden, width), bf16),
                pltpu.VMEM(block_rows, bf16),
                pltpu.VMEM((width, hidden), bf16),
                pltpu.VMEM((hidden, width), bf16),
                pltpu.SemaphoreType.DMA((8,)),
            ]
            + (WeightGather.scratch(4) if gather else []),
            dp, l, f"experts_{l}", 4 * dp * SLOTS * width * hidden,
            [
                buffer.reshape(EXPERTS, SLOTS, width), gathered[l][2], gathered[l][3], residual_up, residual_down,
                *(shards if gather else ()),
            ],
            [(block_rows, bf16), *eff_shapes, *([(shape, bf16) for shape in gathered_shapes] if gather else ())],
        )
        if gather:
            gathered[l + 1] = more
        returned = by_piece(returned)
        before = (middle, gate, returned)
        records.append(
            dict(
                carried=carried, middle=middle, second_low=second_low, gate=gate, saved=results[4:], received=received,
                up_eff=up_eff, down_eff=down_eff,
            )
        )

    top = records[-1]
    block_output, grad, logit_grad, router_part, buffer = image_call(
        turn_kernel,
        images,
        [
            ("image", before[0]),
            ("image", before[1]),
            ("whole", before[2]),
            ("image", cotangent),
            ("whole", enter),
            ("whole", leave),
            ("image", col_form),
            ("image", row_form),
            ("image", top["second_low"]),
            (LAYERS - 1, routers),
        ],
        [
            ("image", patches.shape, bf16),
            ("image", token, f32),
            ("image", (images, IMGROWS, LANES), f32),
            ("whole", (LANES, width), f32),
            ("whole", buffer_shape, bf16),
        ],
        [pltpu.VMEM(buffer_shape, f32)],
        "turn",
    )
    router_parts, tables, smalls = [None] * LAYERS, [None] * LAYERS, [None] * LAYERS
    residual_sums, shard_sums = [None] * LAYERS, [None] * LAYERS
    router_parts[LAYERS - 1] = router_part
    units, attn_units, mines = [None] * LAYERS, [None] * LAYERS, [None] * LAYERS
    for l in reversed(range(LAYERS)):
        rec = records[l]
        last = l == 0
        reduce = fast and l < LAYERS - 1
        arrays = []
        anys = [buffer.reshape(EXPERTS, SLOTS, width), rec["received"], rec["up_eff"], rec["down_eff"]]
        outs, any_outs = [(block_rows, bf16)], []
        scratch = [pltpu.VMEM(block_rows, bf16)] + [pltpu.VMEM(*shape) for shape in eff_shapes]
        scratch.append(pltpu.SemaphoreType.DMA((5,)))
        if fast:
            any_outs.append(((2, mp, width, width), bf16))
            scratch.append(pltpu.VMEM(*any_outs[0]))
        scratch += [
            pltpu.VMEM(block_rows, bf16),
            pltpu.VMEM((dp, SLOTS, hidden), bf16),
            pltpu.VMEM((dp, SLOTS, hidden), f32),
            pltpu.VMEM((dp, SLOTS, hidden), bf16),
            pltpu.VMEM(block_rows, bf16),
        ]
        if fast:
            scratch += [pltpu.VMEM((width, hidden), f32)] * 2
        else:
            outs += [((width, hidden), f32)] * 2
        if reduce:
            arrays += [mines[l + 1], attn_units[l + 1]]
            outs += [((2, mp, width, width), bf16), ((width, width), bf16)]
            scratch += RowSum.scratch(1, width) + RowGather.scratch(2)
        results = list(
            expert_call(
                functools.partial(expert_backward_kernel, dp, mp, fast, reduce), arrays, outs, scratch, dp, LAYERS + l,
                f"experts_back_{l}", 10 * dp * SLOTS * width * hidden, anys, any_outs,
            )
        )
        returned_grad = results.pop(0)
        if fast:
            units[l] = results.pop(-1)
        else:
            residual_sums[l] = lax.psum(tuple(t.astype(bf16) for t in results[:2]), "mp")
        if reduce:
            full_above, mine_above = results
        window_in, qk, v, probs, att, proj_full = rec["saved"]
        qkv_full = gathered[l][0].reshape(3 * width, width)
        arrays = [
            ("smem", image_valid),
            ("image", grad),
            ("whole", by_piece(returned_grad)),
            ("image", logit_grad),
            ("image", rec["middle"]),
            ("image", rec["carried"]),
            (l, routers),
            ("image", col_form),
            ("whole", moves[l]),
            ("whole", backs[l]),
            (l, norm_gain),
            ("whole", proj_full),
            ("whole", qkv_full),
            ("image", window_in),
            ("image", qk),
            ("image", v),
            ("image", probs),
            ("image", att),
        ]
        outs = [("image", patches.shape if last else token, f32)]
        scratch = [pltpu.VMEM((3 * width, (2 - images % 2) * IMGROWS), bf16)]
        closes = fast and last
        table_shape, small_shape = (HEADS, WPAD, LANES), (8, width)
        if fast:
            arrays.append(("whole", units[l]))
            scratch += [pltpu.VMEM((3 * width, width), f32), pltpu.VMEM((width, width), f32)]
        if closes:
            outs += [
                ("whole", (2, mp, width, width), bf16),
                ("whole", (3, width, width), bf16),
                ("whole", (Closing.lines, width), f32),
                ("whole", (3, width, width), bf16),
            ]
        else:
            if fast:
                outs += [
                    ("whole", (width // 2, width), bf16),
                    ("whole", (mp, width, width), bf16),
                    ("whole", (2, width, width), bf16),
                ]
            else:
                outs += [("whole", (3 * width, width), f32), ("whole", (width, width), f32)]
            outs += [("whole", table_shape, f32), ("whole", small_shape, f32)]
        if last:
            arrays.append(("whole", leave))
            if fast:
                arrays += [
                    ("whole", a)
                    for a in (
                        tables[1], smalls[1], router_parts[1], router_parts[0], entry_col, halves_above, mines[1],
                        mine_above,
                    )
                ]
        else:
            below = records[l - 1]
            arrays += [
                ("image", row_form),
                ("image", below["expert_out"]),
                ("image", below["second_low"]),
                (l - 1, routers),
            ]
            outs += [
                ("image", (images, IMGROWS, LANES), f32),
                ("whole", (LANES, width), f32),
                ("whole", buffer_shape, bf16),
            ]
            scratch.append(pltpu.VMEM(buffer_shape, f32))
        if closes:
            scratch += [
                pltpu.VMEM(table_shape, f32),
                pltpu.VMEM(small_shape, f32),
                pltpu.VMEM((mp, width, width), bf16),
                pltpu.VMEM((Closing.lines, width), f32),
            ]
            scratch += [pltpu.VMEM(shape, dtype) for _, shape, dtype in outs[1:5]] + Closing.scratch(dp, width)
        elif fast:
            scratch += RowSum.scratch(2, width) + [pltpu.VMEM((width // 2, width), bf16)]
            scratch += [pltpu.SemaphoreType.DMA((1,))] * 2
        results = list(
            image_call(
                functools.partial(attention_backward_kernel, last, dp, mp, fast),
                images, arrays, outs, scratch, f"attend_back_{l}", 2 * LAYERS + 1 + l if fast else None,
            )
        )
        grad = results.pop(0)
        if closes:
            full, closed, lines, shard_above = results
            continue
        if fast:
            halves_above = results.pop(0)
            attn_units[l], mines[l] = results[:2]
        else:
            qkv_part, proj_part = results[:2]
        tables[l], smalls[l] = results[2:4]
        if not last:
            logit_grad, router_parts[l - 1], buffer = results[4:]
        if fast:
            continue
        attn = (
            lax.psum_scatter(qkv_part.astype(bf16), "mp", scatter_dimension=0, tiled=True),
            lax.psum_scatter(proj_part.T.astype(bf16), "mp", scatter_dimension=0, tiled=True),
        )
        up_sum, down_sum = residual_sums[l]
        if split > 1:
            begin = lax.axis_index("dp") % split * hidden
            empty = jnp.zeros((width, hidden_full), bf16)
            up_sum = lax.dynamic_update_slice_in_dim(empty, up_sum, begin, 1)
            down_sum = lax.dynamic_update_slice_in_dim(empty, down_sum, begin, 1)
        up_columns, down_columns = core_up.shape[-1], core_down.shape[-1]
        up_shard = lax.dynamic_slice_in_dim(up_sum, row_index * up_columns, up_columns, 1)
        down_shard = lax.dynamic_slice_in_dim(down_sum, row_index * down_columns, down_columns, 0)
        shard_sums[l] = lax.psum((attn[0], attn[1], up_shard, down_shard), "dp")

    if fast:
        *attn_grads, core_up_grad, core_down_grad, residual_up_grad, residual_down_grad = format_call(
            [full, full_above], [closed, shard_above], qkv_weight.shape[-1]
        )
        attn_grads = [a.transpose(0, 2, 1) for a in attn_grads]
        core_grads = (core_up_grad, core_down_grad.transpose(0, 2, 1))
        at = LAYERS * HEADS
        table_sum = lines[:at, :OFFSETS]
        router_sum = lines[at : at + LAYERS * EXPERTS].reshape(LAYERS, EXPERTS, width)
        at += LAYERS * EXPERTS
        small_sum = lines[at : at + LAYERS * 8].reshape(LAYERS, 8, width)[:, :4]
    else:
        entry = cell_entries()[None, :] + np.array([key_base_of(key) for key in range(WPAD)])[:, None]
        entry = jnp.asarray(np.where(np.arange(WPAD)[:, None] < WINPOS, entry, -1).reshape(-1))
        entry_turned = (entry[:, None] == jnp.arange(OFFSETS)[None, :]).astype(f32)
        table_part = jnp.dot(
            jnp.stack(tables, 0).reshape(LAYERS * HEADS, WPAD * LANES), entry_turned, precision=highest
        )
        small_part = jnp.stack(smalls, 0)[:, :4]
        router_part = jnp.stack(router_parts, 0)[:, :EXPERTS]
        table_sum, small_sum, router_sum = lax.psum((table_part, small_part, router_part), ("dp", "mp"))

        def shard(k):
            return jnp.stack([shard_sums[l][k] for l in range(LAYERS)], 0).astype(f32)

        attn_grads = (shard(0).transpose(0, 2, 1), shard(1).transpose(0, 2, 1))
        core_grads = (shard(2), shard(3).transpose(0, 2, 1))
        residual_up_grad, residual_down_grad = (
            jnp.stack([residual_sums[l][k] for l in range(LAYERS)], 0).astype(f32) for k in range(2)
        )
        residual_up_grad = residual_up_grad[:, None]
        residual_down_grad = residual_down_grad.transpose(0, 2, 1)[:, None]

    return (
        block_output,
        grad,
        attn_grads[0],
        attn_grads[1],
        core_grads[0],
        core_grads[1],
        residual_up_grad,
        residual_down_grad,
        table_sum.reshape(LAYERS, HEADS, OFFSETS).transpose(0, 2, 1),
        router_sum.transpose(0, 2, 1),
        small_sum[:, 0:2],
        small_sum[:, 2:4],
    )


def solution(mesh):
    placed = (
        P(("dp", "mp"), None, None),
        P(None, None, "mp"),
        P(None, None, "mp"),
        P(None, None, "mp"),
        P(None, None, "mp"),
        P(None, "dp", None, None),
        P(None, "dp", None, None),
        P(),
        P(),
        P(),
        P(),
        P(("dp", "mp"), None, None),
        P(("dp", "mp")),
        P(("dp", "mp"), None),
        P(("dp", "mp"), None),
        P(("dp", "mp"), None, None),
    )
    return jax.shard_map(
        per_device,
        mesh=mesh,
        in_specs=placed,
        out_specs=(
            P(("dp", "mp"), None, None),
            P(("dp", "mp"), None, None),
            P(None, None, "mp"),
            P(None, None, "mp"),
            P(None, None, "mp"),
            P(None, None, "mp"),
            P(None, "dp", None, None),
            P(None, "dp", None, None),
            P(),
            P(),
            P(),
            P(),
        ),
        check_vma=False,
    )
```

```python
import functools

import jax
import jax.numpy as jnp
import numpy as np
from jax import lax
from jax.experimental import pallas as pl
from jax.experimental.pallas import tpu as pltpu
from jax.sharding import PartitionSpec as P

HEADS = 12
HEAD_DIM = 32
EXPERTS = 8
WINDOW = 7
GRID = 14
SHIFT = 3
LAYERS = 2
WINPOS = 49
OFFSETS = 169
CAP = 122

WPAD = 64
IMGROWS = 256
PATCHES = 196
SLOTS = 128
ROWS = EXPERTS * SLOTS
LANES = 128
GROUP = 4
PAIRS = 2
TABLE = 256

bf16 = jnp.bfloat16
f32 = jnp.float32
highest = lax.Precision.HIGHEST
norm_epsilon = 1e-05
mask_fill = -100.0
head_scale = HEAD_DIM ** (-0.5)
MESH = pl.DeviceIdType.MESH
MIB = 1024 * 1024


def nn(a, b):
    return lax.dot_general(a, b, (((1,), (0,)), ((), ())), preferred_element_type=f32)


def nt(a, b):
    return lax.dot_general(a, b, (((1,), (1,)), ((), ())), preferred_element_type=f32)


def tn(a, b):
    return lax.dot_general(a, b, (((0,), (0,)), ((), ())), preferred_element_type=f32)


def iota(shape, dim):
    return lax.broadcasted_iota(jnp.int32, shape, dim)


def onehot(flags):
    return jnp.where(flags, 1.0, 0.0).astype(bf16)


def natural_of_row(shifted):
    moved = SHIFT if shifted else 0
    blocks = GRID // WINDOW
    out = -np.ones(IMGROWS, np.int32)
    for window in range(blocks * blocks):
        for cell in range(WINPOS):
            row = (window // blocks * WINDOW + cell // WINDOW + moved) % GRID
            col = (window % blocks * WINDOW + cell % WINDOW + moved) % GRID
            out[window * WPAD + cell] = row * GRID + col
    return out


def key_base_of(key):
    return (2 * WINDOW) * (WINDOW - 1) - (key // WINDOW * (2 * WINDOW - 1) + key % WINDOW)


def enter_table():
    held = natural_of_row(False)
    return (held[:, None] == np.arange(PATCHES)[None, :]).astype(np.float32)


def move_table(shifted):
    first, second = natural_of_row(False), natural_of_row(shifted)
    same = (second[:, None] == first[None, :]) & (second[:, None] >= 0)
    return same.astype(np.float32)


def cell_entries():
    cell = np.arange(LANES) % WPAD
    return np.where(cell < WINPOS, cell // WINDOW * (2 * WINDOW - 1) + cell % WINDOW, -4 * TABLE).astype(np.int32)


def norm_parts(x):
    width = x.shape[-1]
    center = x - jnp.sum(x, -1, keepdims=True) * (1.0 / width)
    spread = jnp.sum(center * center, -1, keepdims=True) * (1.0 / width)
    rstd = lax.rsqrt(spread + norm_epsilon)
    return center * rstd, rstd


def norm_back(grad, gain, xhat, rstd):
    width = xhat.shape[-1]
    dxhat = grad * gain
    mean_one = jnp.sum(dxhat, -1, keepdims=True) * (1.0 / width)
    mean_two = jnp.sum(dxhat * xhat, -1, keepdims=True) * (1.0 / width)
    return rstd * (dxhat - mean_one - xhat * mean_two)


def turn_blocks(x):
    size = x.shape[0]
    same = onehot(iota((size, size), 0) == iota((size, size), 1))
    return jnp.concatenate([nt(same, x[:, at : at + size]) for at in range(0, x.shape[1], size)], 0)


def split_two(x):
    high = x.astype(bf16)
    return high, (x - high.astype(f32)).astype(bf16)


def collect(pos_col, returned_ref):
    pick = onehot(pos_col == iota((pos_col.shape[0], ROWS), 1))
    out = nn(pick, returned_ref[0])
    for piece in range(1, returned_ref.shape[0]):
        out = out + nn(pick, returned_ref[piece])
    return out


def join(ref):
    return ref[...].reshape(ref.shape[0] * ref.shape[1], *ref.shape[2:])


def store(ref, rows):
    ref[...] = rows.reshape(ref.shape).astype(ref.dtype)


def per_image(function, count):
    return jnp.concatenate([function(i) for i in range(count)], 0)


def image_rows(i):
    return slice(i * IMGROWS, (i + 1) * IMGROWS)


def lay_positions(row_ref):
    return jnp.concatenate([row_ref[i, 0:1, :] for i in range(row_ref.shape[0])], 1)


def spread_rows(pos_row, rows_low):
    return nn(onehot(iota((ROWS, pos_row.shape[1]), 0) == pos_row), rows_low)


def route(second_low, router, pos_col):
    logits = nt(second_low, router)
    lane = iota(logits.shape, 1)
    logits = jnp.where(lane < EXPERTS, logits, -1e30)
    expo = jnp.exp(logits - jnp.max(logits, -1, keepdims=True))
    probs = expo / jnp.sum(expo, -1, keepdims=True)
    expert = jnp.where(pos_col >= 0, pos_col // SLOTS, -1)
    chosen = jnp.where(lane == expert, 1.0, 0.0)
    return probs, chosen, jnp.sum(probs * chosen, -1, keepdims=True)


def head_masks():
    rows = iota((LANES, LANES), 0) // HEAD_DIM
    return [onehot(rows == h) for h in range(GROUP)]


def lane_masks():
    lane = iota((WPAD, LANES), 1)
    return [onehot(lane < WPAD), onehot(lane >= WPAD)]


def keys_entry(cells, key_row, turned):
    parts = [cells + (key_base_of(col) - key_row * (2 * WINDOW - 1)) for col in range(WINDOW)]
    return jnp.concatenate(parts, 0 if turned else 1)


def form_bias(bias_ref, table_ref, entry_row):
    layers, heads = bias_ref.shape[:2]
    lines = layers * heads
    bias_ref[...] = jnp.where(iota(bias_ref.shape, 2) < WINPOS, 0.0, -1e30)
    table = table_ref[...]
    high = table.astype(bf16)
    mid, low = split_two(table - high.astype(f32))
    parts = jnp.concatenate([high.astype(f32), mid.astype(f32), low.astype(f32)], 0).astype(bf16)

    def step(key_row, carry):
        pick = onehot(iota((TABLE, WINDOW * LANES), 0) == keys_entry(entry_row, key_row, False))
        rows = nn(parts, pick)
        rows = rows[:lines] + rows[lines : 2 * lines] + rows[2 * lines :]
        for col in range(WINDOW):
            for layer in range(layers):
                part = rows[layer * heads : (layer + 1) * heads, col * LANES : (col + 1) * LANES]
                bias_ref[layer, :, pl.ds(key_row * WINDOW + col, 1), :] = part.reshape(heads, 1, LANES)
        return carry

    lax.fori_loop(0, WINDOW, step, 0)


def table_grad(parts, entry_col):
    heads = parts[0].shape[0]
    lines = heads * len(parts)

    def step(key_row, total):
        keys = [
            jnp.concatenate([ref[:, pl.ds(key_row * WINDOW + col, 1), :].reshape(heads, LANES) for ref in parts], 0)
            for col in range(WINDOW)
        ]
        rows = jnp.concatenate(keys, 1)
        high = rows.astype(bf16).astype(f32)
        both = jnp.concatenate([high, rows - high], 0).astype(bf16)
        entry = keys_entry(entry_col, key_row, True)
        out = nn(both, onehot(iota((WINDOW * LANES, TABLE), 1) == entry))
        return total + out[:lines] + out[lines:]

    return lax.fori_loop(0, WINDOW, step, jnp.zeros((lines, TABLE), f32))


def attention_forward_kernel(first, shifted, mp, gather, *refs):
    refs = list(refs)
    if first:
        patches_ref, enter_ref = refs[:2]
        refs = refs[2:]
    else:
        prev_ref, prev_gate_ref, returned_ref = refs[:3]
        refs = refs[3:]
    (
        valid_ref, col_ref, row_ref, qkv_ref, proj_ref, bias_ref, move_ref, back_ref, gain_ref, nbias_ref, router_ref,
    ) = refs[:11]
    gain_ref, nbias_ref, router_ref = (ref.at[0] for ref in (gain_ref, nbias_ref, router_ref))
    refs = refs[11:]
    if first:
        table_ref, entry_ref = bias_ref, refs.pop(0)
    if gather:
        core_up_ref, core_down_ref = refs[:2]
        refs = refs[2:]
    carried_ref = refs.pop(0)
    if first:
        biases_ref = refs.pop(0)
        bias_ref = biases_ref.at[0]
    else:
        expert_out_ref = refs.pop(0)
        bias_ref = bias_ref.at[0]
    middle_ref, second_ref, gate_ref, buffer_ref, window_ref, qk_ref, v_ref, probs_ref, att_ref, proj_full = refs[:10]
    refs = refs[10:]
    if gather:
        qkv_full = refs.pop(0)
        up_out, down_out = refs[:2]
        refs = refs[2:]
    total_ref = refs.pop(0)
    step = pl.program_id(0)
    final = pl.num_programs(0) - 1
    count, _, width = carried_ref.shape
    if gather:
        shards = [ref.at[0] for ref in (qkv_ref, proj_ref, core_up_ref, core_down_ref)]
        qkv_ref, proj_ref = refs[:2]
        moving = WeightGather(shards, [qkv_ref, proj_ref, up_out, down_out], refs[2:])

        @pl.when(step == 0)
        def _():
            pl.semaphore_wait(moving.row.greet(), 2)
            for k in (0, 1):
                moving.start(k)
            form_bias(biases_ref, table_ref, entry_ref[...])

    pos_col = join(col_ref)[:, 0:1]
    if first:
        x = per_image(lambda i: nn(enter_ref[...], patches_ref[i]), count)
    else:
        expert_out = collect(pos_col, returned_ref)
        store(expert_out_ref, expert_out)
        x = join(prev_ref) + join(prev_gate_ref) * expert_out
    store(carried_ref, x)
    xhat, _ = norm_parts(x)
    normed = (xhat * gain_ref[0:1, :] + nbias_ref[0:1, :]).astype(bf16)
    window_in = per_image(lambda i: nn(move_ref[...], normed[image_rows(i)]), count).astype(bf16)
    store(window_ref, window_in)

    @pl.when(step == 0)
    def _():
        if gather:
            for k in (0, 1):
                moving.forward(k)
            for k in (2, 3):
                moving.start(k)
            for k in (0, 1):
                moving.arrive(k)
            qkv_full[...] = join(qkv_ref)
        elif first:
            form_bias(biases_ref, table_ref, entry_ref[...])
        proj_full[...] = join(proj_ref).astype(f32).T.astype(bf16)
        total_ref[...] = jnp.zeros(total_ref.shape, f32)

    qkv = join(qkv_ref)
    turned = nt(qkv, window_in).astype(bf16)
    straight = nt(window_in, qkv[width:]).astype(bf16)
    for i in range(count):
        qk_ref[i] = turned[: 2 * width, image_rows(i)]
    store(v_ref, straight[:, width:])
    heads_rows = head_masks()
    halves = lane_masks()
    low_lane = iota((WPAD, LANES), 1) < WPAD
    if shifted:
        row_labels = [nt(row_ref[i].astype(f32).astype(bf16), move_ref[...]) for i in range(count)]
        col_labels = [nn(move_ref[...], col_ref[i].astype(f32).astype(bf16)) for i in range(count)]
    for pair in range(PAIRS * count):
        image, side = pair // PAIRS, pair % PAIRS
        across = slice(pair * LANES, (pair + 1) * LANES)
        within = slice(side * LANES, (side + 1) * LANES)
        if shifted:
            ahead = col_labels[image][side * LANES : side * LANES + WPAD, 1:2]
            behind = col_labels[image][side * LANES + WPAD : (side + 1) * LANES, 1:2]
            key_label = jnp.where(low_lane, ahead, behind)
            mask = jnp.where(key_label == row_labels[image][1:2, within], 0.0, mask_fill)
        for group in range(HEADS // GROUP):
            features = slice(group * LANES, (group + 1) * LANES)
            queries = turned[features, across]
            spread = jnp.concatenate([queries * heads_rows[h] for h in range(GROUP)], 1)
            raw = nn(straight[across, features], spread)
            for h in range(GROUP):
                head = group * GROUP + h
                part = raw[:, h * LANES : (h + 1) * LANES]
                scores = jnp.where(low_lane, part[:WPAD], part[WPAD:]) * head_scale + bias_ref[head]
                if shifted:
                    scores = scores + mask
                expo = jnp.exp(scores - jnp.max(scores, 0, keepdims=True))
                probs = (expo * (1.0 / jnp.sum(expo, 0, keepdims=True))).astype(bf16)
                probs_ref[image, side * HEADS + head] = probs
                both = jnp.concatenate([probs * halves[0], probs * halves[1]], 0)
                at = slice(head * HEAD_DIM, (head + 1) * HEAD_DIM)
                values = turned[2 * width + head * HEAD_DIM : 2 * width + (head + 1) * HEAD_DIM, across]
                att_ref[image, at, within] = nn(values, both).astype(bf16)
    attended = per_image(lambda i: nt(back_ref[...], att_ref[i]), count).astype(bf16)
    branch = nt(attended, join(proj_ref))
    middle = x + per_image(lambda i: valid_ref[step * count + i].astype(f32) * branch[image_rows(i)], count)
    store(middle_ref, middle)
    xhat, _ = norm_parts(middle)
    second_low = (xhat * gain_ref[1:2, :] + nbias_ref[1:2, :]).astype(bf16)
    store(second_ref, second_low)
    _, _, gate = route(second_low, router_ref[...], pos_col)
    store(gate_ref, gate)
    total_ref[...] += spread_rows(lay_positions(row_ref), second_low)

    @pl.when(step == final)
    def _():
        buffer_ref[...] = total_ref[...].astype(bf16)
        if gather:
            for k in (2, 3):
                moving.forward(k)
            for k in (2, 3):
                moving.arrive(k)
            for k in range(4):
                moving.sent(k)


def image_spec(array_shape, count):
    rest = tuple(array_shape[1:])
    zeros = (0,) * len(rest)
    return pl.BlockSpec((count,) + rest, lambda i: (i,) + zeros)


def whole_spec(array_shape):
    zeros = (0,) * len(array_shape)
    return pl.BlockSpec(tuple(array_shape), lambda i: zeros)


def image_call(kernel, images, arrays, outs, scratch, name, collective_id=None):
    count = 2 - images % 2

    def spec(kind, shape):
        if isinstance(kind, int):
            rest = tuple(shape[1:])
            return pl.BlockSpec((1,) + rest, lambda i: (kind,) + (0,) * len(rest))
        if kind in ("smem", "any"):
            return pl.BlockSpec(memory_space=pltpu.SMEM if kind == "smem" else pl.ANY)
        return image_spec(shape, count) if kind == "image" else whole_spec(shape)

    return pl.pallas_call(
        kernel,
        grid=(images // count,),
        out_shape=[jax.ShapeDtypeStruct(shape, dtype) for _, shape, dtype in outs],
        in_specs=[spec(kind, array.shape) for kind, array in arrays],
        out_specs=[spec(kind, shape) for kind, shape, _ in outs],
        scratch_shapes=scratch,
        compiler_params=pltpu.CompilerParams(
            vmem_limit_bytes=(51 if name == "attend_0" else 56) * MIB,
            dimension_semantics=("arbitrary",),
            collective_id=collective_id,
            has_side_effects=collective_id is not None,
        ),
        name=name,
    )(*[array for _, array in arrays])


def send_part(g, expert_out, second_low, router, pos_col, pos_row, logit_ref, router_grad_ref, total_ref):
    probs, chosen, gate = route(second_low, router, pos_col)
    gate_grad = jnp.where(pos_col >= 0, jnp.sum(g * expert_out, -1, keepdims=True), 0.0)
    sent = (gate * g).astype(bf16)
    logit_grad = gate_grad * gate * (chosen - probs)
    store(logit_ref, logit_grad)
    high, low = split_two(logit_grad)
    router_grad_ref[...] += tn(high, second_low) + tn(low, second_low)
    total_ref[...] += spread_rows(pos_row, sent)


def turn_kernel(
    prev_ref, gate_ref, returned_ref, cotangent_ref, enter_ref, leave_ref, col_ref, row_ref, second_ref, router_ref,
    block_ref, grad_ref, logit_ref, router_grad_ref, buffer_ref, total_ref,
):
    step = pl.program_id(0)
    count = cotangent_ref.shape[0]

    @pl.when(step == 0)
    def _():
        total_ref[...] = jnp.zeros(total_ref.shape, f32)
        router_grad_ref[...] = jnp.zeros(router_grad_ref.shape, f32)

    pos_col = join(col_ref)[:, 0:1]
    expert_out = collect(pos_col, returned_ref)
    x = (join(prev_ref) + join(gate_ref) * expert_out).astype(bf16)
    for i in range(count):
        block_ref[i] = nn(leave_ref[...], x[image_rows(i)]).astype(bf16)
    g = per_image(lambda i: nn(enter_ref[...], cotangent_ref[i]), count)
    store(grad_ref, g)
    send_part(
        g, expert_out, join(second_ref), router_ref[0], pos_col, lay_positions(row_ref), logit_ref, router_grad_ref, total_ref
    )

    @pl.when(step == pl.num_programs(0) - 1)
    def _():
        buffer_ref[...] = total_ref[...].astype(bf16)


def attention_backward_kernel(last, dp, mp, fast, *refs):
    (
        valid_ref, grad_ref, returned_ref, logit_ref, middle_ref, carried_ref, router_ref, col_ref, move_ref, back_ref,
        gain_ref, proj_ref, qkv_ref, window_ref, qk_ref, v_ref, probs_ref, att_ref,
    ) = refs[:18]
    refs = refs[18:]
    refs = list(refs)
    if fast:
        units_ref = refs.pop(0)
    if last:
        leave_ref = refs.pop(0)
        if fast:
            table_above, small_above, router_above, router_here, entry_ref, half_above, down_above, attn_above = refs[:8]
            refs = refs[8:]
    else:
        row_ref, expert_out_ref, second_ref, router_next_ref = refs[:4]
        refs = refs[4:]
    out_ref = refs.pop(0)
    closing = None
    if fast and last:
        results, refs = refs[:4], refs[4:]
    else:
        if fast:
            halves_ref = refs.pop(0)
            unit_ref, mine_ref = refs[:2]
        else:
            qkv_grad_ref, proj_grad_ref = refs[:2]
        table_ref, small_ref = refs[2:4]
        refs = refs[4:]
    if not last:
        logit_out_ref, router_grad_ref, buffer_ref = refs[:3]
        refs = refs[3:]
    turned = refs.pop(0)
    if fast:
        qkv_grad_ref, proj_grad_ref = refs[:2]
        refs = refs[2:]
    if not last:
        total_ref = refs.pop(0)
    step = pl.program_id(0)
    final = pl.num_programs(0) - 1
    count, _, width = carried_ref.shape
    if fast:
        row = Row()
        if last:
            table_ref, small_ref, unit_ref, lines_ref = refs[:4]
            landing, refs = refs[4:8], refs[8:]
            above = (half_above, down_above.at[1], attn_above)
            closing = Closing(row, dp, units_ref, unit_ref, lines_ref, above, landing, refs)
        else:
            sums = RowSum(row, blocks(units_ref), refs[0], refs[1], refs[2], blocks(mine_ref), refs[3:7])
            across_x = DeepSum(dp, [mine_ref.at[0]], [refs[7]], [halves_ref], [None], [None], refs[8:10] * 4)

        def take(k):
            if closing:
                closing.take(k)
            else:
                sums.end(k)
                if k == 0:
                    across_x.over_x(k).start()

        @pl.when(step == 0)
        def _():
            if closing:
                closing.enter()
            else:
                barrier = row.greet()
                pl.semaphore_wait(barrier, 2 + across_x.greet(barrier, False))
                for k in range(2):
                    sums.start(k)

    @pl.when(step == 0)
    def _():
        qkv_grad_ref[...] = jnp.zeros(qkv_grad_ref.shape, f32)
        proj_grad_ref[...] = jnp.zeros(proj_grad_ref.shape, f32)
        table_ref[...] = jnp.zeros(table_ref.shape, f32)
        small_ref[...] = jnp.zeros(small_ref.shape, f32)
        if not last:
            total_ref[...] = jnp.zeros(total_ref.shape, f32)
            router_grad_ref[...] = jnp.zeros(router_grad_ref.shape, f32)

    pos_col = join(col_ref)[:, 0:1]
    g = join(grad_ref)
    high, low = split_two(join(logit_ref))
    gain_ref, router = gain_ref.at[0], router_ref[0]
    normed_grad = collect(pos_col, returned_ref) + nn(high, router) + nn(low, router)
    xhat, rstd = norm_parts(join(middle_ref))
    small_ref[1:2, :] += jnp.sum(normed_grad * xhat, 0, keepdims=True)
    small_ref[3:4, :] += jnp.sum(normed_grad, 0, keepdims=True)
    middle_grad = g + norm_back(normed_grad, gain_ref[1:2, :], xhat, rstd)

    def branch_part(i):
        low_part = (valid_ref[step * count + i].astype(f32) * middle_grad[image_rows(i)]).astype(bf16)
        return nn(move_ref[...], low_part)

    branch_grad = per_image(branch_part, count).astype(bf16)
    for i in range(count):
        proj_grad_ref[...] += nn(att_ref[i], branch_grad[image_rows(i)])
    att_grad = nt(proj_ref[...], branch_grad).astype(bf16)
    if fast:

        @pl.when(step == 0)
        def _():
            if closing:
                closing.early()
            else:
                for k in range(2):
                    sums.middle(k)

        pl.when(step == final)(functools.partial(take, 0))

    heads_rows = head_masks()
    halves = lane_masks()
    low_lane = iota((WPAD, LANES), 1) < WPAD
    for pair in range(PAIRS * count):
        image, side = pair // PAIRS, pair % PAIRS
        across = slice(pair * LANES, (pair + 1) * LANES)
        within = slice(side * LANES, (side + 1) * LANES)
        for group in range(HEADS // GROUP):
            features = slice(group * LANES, (group + 1) * LANES)
            grads = att_grad[features, across]
            spread = jnp.concatenate([grads * heads_rows[h] for h in range(GROUP)], 1)
            raw = nn(v_ref[image, within, features], spread)
            for h in range(GROUP):
                head = group * GROUP + h
                at = slice(head * HEAD_DIM, (head + 1) * HEAD_DIM)
                below = slice(width + head * HEAD_DIM, width + (head + 1) * HEAD_DIM)
                lowest = slice(2 * width + head * HEAD_DIM, 2 * width + (head + 1) * HEAD_DIM)
                part = raw[:, h * LANES : (h + 1) * LANES]
                probs_grad = jnp.where(low_lane, part[:WPAD], part[WPAD:])
                probs_low = probs_ref[image, side * HEADS + head]
                probs = probs_low.astype(f32)
                weighted = probs * probs_grad
                scores_grad = weighted - probs * jnp.sum(weighted, 0, keepdims=True)
                table_ref[head] += scores_grad
                scores_low = scores_grad.astype(bf16)
                both = jnp.concatenate([scores_low * halves[0], scores_low * halves[1]], 0)
                probs_both = jnp.concatenate([probs_low * halves[0], probs_low * halves[1]], 0)
                turned[at, across] = (nn(qk_ref[image, below, within], both) * head_scale).astype(bf16)
                turned[below, across] = (nt(qk_ref[image, at, within], both) * head_scale).astype(bf16)
                turned[lowest, across] = nt(att_grad[at, across], probs_both).astype(bf16)
    qkv_grad_ref[...] += nn(turned[...], join(window_ref))
    if fast:

        @pl.when(step == final)
        def _():
            columns, rows = 3 * width // mp, width // mp
            proj_turned = proj_grad_ref[...].T
            for place in range(mp):
                q = quarter_at(place, mp)
                unit_ref[place, :columns] = qkv_grad_ref[q * columns : (q + 1) * columns].astype(bf16)
                unit_ref[place, columns:] = proj_turned[q * rows : (q + 1) * rows].astype(bf16)
            if closing:
                closing.open()
            take(1)
            if closing:
                heads = 2 * HEADS
                lines_ref[...] = jnp.zeros(lines_ref.shape, f32)
                lines_ref[:heads, :TABLE] = table_grad([table_ref, table_above], entry_ref[...])

    mixed_grad = per_image(lambda i: nt(back_ref[...], turned[:, image_rows(i)]), count).astype(bf16)
    first_grad = nn(mixed_grad, qkv_ref[...])
    if closing:

        @pl.when(step == final)
        def _():
            closing.cross()

    xhat, rstd = norm_parts(join(carried_ref))
    small_ref[0:1, :] += jnp.sum(first_grad * xhat, 0, keepdims=True)
    small_ref[2:3, :] += jnp.sum(first_grad, 0, keepdims=True)
    if closing:

        @pl.when(step == final)
        def _():
            heads = 2 * HEADS
            lines_ref[heads : heads + EXPERTS] = router_here[:EXPERTS]
            lines_ref[heads + EXPERTS : heads + 2 * EXPERTS] = router_above[:EXPERTS]
            lines_ref[heads + 2 * EXPERTS : heads + 2 * EXPERTS + 8] = small_ref[...]
            lines_ref[heads + 2 * EXPERTS + 8 : heads + 2 * EXPERTS + 16] = small_above[...]
            closing.send_lines()

    out = middle_grad + norm_back(first_grad, gain_ref[0:1, :], xhat, rstd)
    if last:
        top = out.astype(bf16)
        rest = out - top.astype(f32)
        mid, low = split_two(rest)
        leave = leave_ref[...]
        for i in range(count):
            at = image_rows(i)
            out_ref[i] = nn(leave, top[at]) + nn(leave, mid[at]) + nn(leave, low[at])
    else:
        store(out_ref, out)
        send_part(
            out, join(expert_out_ref), join(second_ref), router_next_ref[0], pos_col, lay_positions(row_ref), logit_out_ref,
            router_grad_ref, total_ref,
        )

    @pl.when(step == final)
    def _():
        if not last:
            buffer_ref[...] = total_ref[...].astype(bf16)
        if closing:
            closing.finish()
            for out, landed in zip(results, landing):
                out[...] = landed[...]
        elif fast:
            across_x.halve(0)
            across_x.over_x(0).wait_send()
            for k in range(2):
                sums.finish(k)


def quarter_at(place, mp):
    return place % (mp // 2) * 2 + place // (mp // 2)


def add_up(*parts):
    total = parts[0].astype(f32)
    for part in parts[1:]:
        total = total + part.astype(f32)
    return total


def to_row(source, target, sems, k, row):
    return pltpu.make_async_remote_copy(
        src_ref=source,
        dst_ref=target,
        send_sem=sems[0].at[k],
        recv_sem=sems[1].at[k],
        device_id={"mp": row},
        device_id_type=MESH,
    )


class Row:
    def __init__(self):
        row = lax.axis_index("mp")
        self.row, self.core, self.y = row, lax.rem(row, 2), lax.div(row, 2)
        self.sibling, self.across = row + 1 - 2 * self.core, row + 2 - 4 * self.y
        self.place = self.core * 2 + self.y
        self.place_across = self.core * 2 + 1 - self.y

    def greet(self):
        barrier = pltpu.get_barrier_semaphore()
        for row in (self.sibling, self.across):
            pl.semaphore_signal(barrier, inc=1, device_id={"mp": row}, device_id_type=MESH)
        return barrier


class RowSum:
    semaphores = 4

    def __init__(self, row, units, core_in, y_out, y_in, mine, sems):
        self.row, self.units, self.mine = row, units, mine
        self.core_in, self.y_out, self.y_in = core_in, y_out, y_in
        self.sems = (sems[:2], sems[2:])

    def pair(self, k):
        theirs = self.units[k].at[pl.ds(2 * (1 - self.row.core), 2)]
        return to_row(theirs, self.core_in.at[k], self.sems[0], k, self.row.sibling)

    def cross(self, k):
        return to_row(self.y_out.at[k], self.y_in.at[k], self.sems[1], k, self.row.across)

    def start(self, k):
        self.pair(k).start()

    def middle(self, k):
        self.pair(k).wait_recv()
        other = 1 - self.row.y
        mixed = add_up(self.units[k][self.row.core * 2 + other], self.core_in[k, other])
        self.y_out[k] = mixed.astype(bf16)
        self.cross(k).start()

    def end(self, k):
        self.cross(k).wait_recv()
        self.mine[k][...] = add_up(
            self.units[k][self.row.place], self.core_in[k, self.row.y], self.y_in[k]
        ).astype(bf16)

    def finish(self, k):
        self.pair(k).wait_send()
        self.cross(k).wait_send()

    @classmethod
    def scratch(cls, count, width):
        return [
            pltpu.VMEM((count, 2, width, width), bf16),
            pltpu.VMEM((count, width, width), bf16),
            pltpu.VMEM((count, width, width), bf16),
        ] + [pltpu.SemaphoreType.DMA((count,))] * cls.semaphores


class RowGather:
    semaphores = 6

    def __init__(self, row, sources, fulls, slot, slot_across, sems):
        self.row, self.sources, self.fulls = row, sources, fulls
        self.slot, self.slot_across = slot, slot_across
        self.sems = (sems[:2], sems[2:4], sems[4:])

    def over(self, k):
        return to_row(self.sources[k], self.fulls[k].at[self.slot], self.sems[0], k, self.row.across)

    def near(self, k):
        return to_row(self.sources[k], self.fulls[k].at[self.slot], self.sems[1], k, self.row.sibling)

    def onward(self, k):
        block = self.fulls[k].at[self.slot_across]
        return to_row(block, block, self.sems[2], k, self.row.sibling)

    def start(self, k):
        self.over(k).start()
        self.near(k).start()

    def forward(self, k):
        self.over(k).wait_recv()
        self.onward(k).start()

    def arrive(self, k):
        self.near(k).wait_recv()
        self.onward(k).wait_recv()

    def sent(self, k):
        self.over(k).wait_send()
        self.near(k).wait_send()
        self.onward(k).wait_send()

    @classmethod
    def scratch(cls, count):
        return [pltpu.SemaphoreType.DMA((count,))] * cls.semaphores


class WeightGather(RowGather):
    def __init__(self, shards, fulls, sems):
        row = Row()
        super().__init__(row, shards, fulls, row.row, row.across, sems[:6])
        self.own_sem = sems[6]

    def own(self, k):
        return pltpu.make_async_copy(self.sources[k], self.fulls[k].at[self.slot], self.own_sem.at[k])

    def start(self, k):
        super().start(k)
        self.own(k).start()

    def arrive(self, k):
        super().arrive(k)
        self.own(k).wait()

    @classmethod
    def scratch(cls, count):
        return super().scratch(count) + [pltpu.SemaphoreType.DMA((count,))]


class DeepSum:
    def __init__(self, dp, total, arrived, halves, slots, result, sems):
        self.total, self.arrived, self.halves, self.slots, self.result = total, arrived, halves, slots, result
        self.x_sems, self.z_sems, self.z_back, self.x_back = (sems[2 * k : 2 * k + 2] for k in range(4))
        me = lax.axis_index("dp")
        self.x, self.z, self.deep = lax.rem(me, 2), lax.div(me, 2), dp // 2
        self.partner = me + 1 - 2 * self.x

    def greet(self, barrier, whole=True):
        pl.semaphore_signal(barrier, inc=1, device_id={"dp": self.partner}, device_id_type=MESH)
        if not whole:
            return 1
        for off in range(1, self.deep):
            peer = lax.rem(self.z + off, self.deep) * 2 + self.x
            pl.semaphore_signal(barrier, inc=1, device_id={"dp": peer}, device_id_type=MESH)
        return self.deep

    def cut(self, k):
        height = self.halves[k].shape[0]
        return height, height // self.deep

    def over_x(self, k):
        height, _ = self.cut(k)
        away = self.total[k].at[pl.ds(pl.multiple_of((1 - self.x) * height, height), height)]
        return to_peer(away, self.arrived[k], self.x_sems[0].at[k], self.x_sems[1].at[k], self.partner)

    def over_z(self, k, off):
        _, piece = self.cut(k)
        to = lax.rem(self.z + off, self.deep)
        part = self.halves[k].at[pl.ds(pl.multiple_of(to * piece, piece), piece)]
        sems = [sem.at[k, off] for sem in self.z_sems]
        return to_peer(part, self.slots[k].at[off], *sems, to * 2 + self.x)

    def own_piece(self, k):
        height, piece = self.cut(k)
        return self.result[k].at[pl.ds(pl.multiple_of(self.x * height + self.z * piece, piece), piece)]

    def own_half(self, k):
        height, _ = self.cut(k)
        return self.result[k].at[pl.ds(pl.multiple_of(self.x * height, height), height)]

    def back_z(self, k, off):
        to = lax.rem(self.z + off, self.deep)
        sems = [sem.at[k, off] for sem in self.z_back]
        return to_peer(self.own_piece(k), self.own_piece(k), *sems, to * 2 + self.x)

    def back_x(self, k):
        return to_peer(self.own_half(k), self.own_half(k), self.x_back[0].at[k], self.x_back[1].at[k], self.partner)

    def halve(self, k):
        self.over_x(k).wait_recv()
        height, _ = self.cut(k)
        keep = self.total[k][pl.ds(pl.multiple_of(self.x * height, height), height)]
        self.halves[k][...] = add_up(keep, self.arrived[k][...]).astype(self.halves[k].dtype)

    def deepen(self, k):
        for off in range(1, self.deep):
            self.over_z(k, off).start()

    def quarter(self, k):
        for off in range(1, self.deep):
            self.over_z(k, off).wait_recv()
        _, piece = self.cut(k)
        keep = self.halves[k][pl.ds(pl.multiple_of(self.z * piece, piece), piece)]
        total = add_up(keep, *[self.slots[k][off] for off in range(1, self.deep)])
        self.own_piece(k)[...] = total.astype(self.result[k].dtype)
        for off in range(1, self.deep):
            self.back_z(k, off).start()

    def widen(self, k):
        for off in range(1, self.deep):
            self.back_z(k, off).wait_recv()
        self.back_x(k).start()

    def finish(self, k, halved=True):
        if halved:
            self.over_x(k).wait_send()
        for off in range(1, self.deep):
            self.over_z(k, off).wait_send()
            self.back_z(k, off).wait_send()
        self.back_x(k).wait()

    @staticmethod
    def semaphores(dp, count):
        one, many = pltpu.SemaphoreType.DMA((count,)), pltpu.SemaphoreType.DMA((count, dp // 2))
        return [one, one, many, many, many, many, one, one]


def blocks(ref):
    return [ref.at[k] for k in range(ref.shape[0])]


class WideSum:
    def __init__(self, dp, total, slots, result, sems):
        self.dp, self.total, self.slots, self.result, self.sems = dp, total, slots, result, sems
        self.me = lax.axis_index("dp")

    def piece(self, ref, at):
        size = ref.shape[0] // self.dp
        return ref.at[pl.ds(pl.multiple_of(at * size, size), size)]

    def out(self, k, p):
        peer = partner_of(self.me, p, self.dp)
        sems = self.sems[0].at[k, p], self.sems[1].at[k, p]
        return to_peer(self.piece(self.total[k], peer), self.slots[k].at[p], *sems, peer)

    def back(self, k, p):
        mine = self.piece(self.result[k], self.me)
        sems = self.sems[2].at[k, p], self.sems[3].at[k, p]
        return to_peer(mine, mine, *sems, partner_of(self.me, p, self.dp))

    def start(self, k):
        for p in range(self.dp - 1, 0, -1):
            self.out(k, p).start()

    def middle(self, k):
        for p in range(1, self.dp):
            self.out(k, p).wait_recv()
        total = add_up(self.piece(self.total[k], self.me)[...], *[self.slots[k][p] for p in range(1, self.dp)])
        self.piece(self.result[k], self.me)[...] = total.astype(self.result[k].dtype)
        for p in range(self.dp - 1, 0, -1):
            self.back(k, p).start()

    def finish(self, k):
        for p in range(1, self.dp):
            self.out(k, p).wait_send()
            self.back(k, p).wait()

    @staticmethod
    def semaphores(dp, count):
        return [pltpu.SemaphoreType.DMA((count, dp))] * 4


class Closing:
    lines = 64

    def __init__(self, row, dp, units_ref, attn_ref, lines_ref, given, results, refs):
        self.row, self.lines_ref, self.dp = row, lines_ref, dp
        self.full, shard, small, above = results
        core_in, y_out, y_in = refs[:3]
        mine, x_in, half, z_in, self.s_core, self.s_one, self.s_y, self.s_mine, s_slots, wide_in = refs[7:17]
        x_above, half_above, z_above = refs[17:20]
        refs_sems, refs = refs[3:7], refs[20:]
        self.mine = mine
        self.sums = RowSum(row, blocks(units_ref) + [attn_ref], core_in, y_out, y_in, blocks(mine), refs_sems)
        self.gather = RowGather(
            row, [mine.at[k] for k in range(2)], blocks(self.full), row.place, row.place_across, refs[:6]
        )
        self.s_pair = to_row(lines_ref, self.s_core, refs[6:8], 0, row.sibling)
        self.s_cross = to_row(self.s_one, self.s_y, refs[8:10], 0, row.across)
        self.here = DeepSum(
            dp, [mine.at[0], mine.at[1]], blocks(x_in), blocks(half), blocks(z_in), [shard.at[0], shard.at[1]], refs[10:18]
        )
        self.above = DeepSum(
            dp, [None, *given[1:]], [None] + blocks(x_above), [given[0]] + blocks(half_above), blocks(z_above), blocks(above),
            refs[18:26],
        )
        self.wide = WideSum(dp, [mine.at[2], self.s_mine], [wide_in, s_slots], [shard.at[2], small], refs[26:30])

    def enter(self):
        greet(self.dp, lax.axis_index("dp"), (self.row.sibling, self.row.across))
        for k in range(2):
            self.sums.start(k)
        self.above.deepen(0)
        for k in (1, 2):
            self.above.over_x(k).start()

    def early(self):
        for k in range(2):
            self.sums.middle(k)
        for k in (1, 2):
            self.above.halve(k)
            self.above.deepen(k)
        self.above.quarter(0)

    def take(self, k):
        self.sums.end(k)
        self.here.over_x(k).start()
        if k == 0:
            self.above.widen(0)
            for j in (1, 2):
                self.above.quarter(j)
        else:
            for j in (1, 2):
                self.above.widen(j)

    def open(self):
        self.sums.start(2)

    def cross(self):
        self.sums.middle(2)
        for k in range(2):
            self.here.halve(k)
            self.here.deepen(k)

    def send_lines(self):
        self.s_pair.start()
        for k in range(2):
            self.here.quarter(k)
        self.s_pair.wait_recv()
        self.s_one[...] = self.lines_ref[...] + self.s_core[...]
        self.s_cross.start()

    def finish(self):
        self.sums.end(2)
        self.wide.start(0)
        self.s_cross.wait_recv()
        self.s_mine[...] = self.s_one[...] + self.s_y[...]
        self.wide.start(1)
        for k in range(2):
            self.gather.start(k)
            self.full[k, self.row.place] = self.mine[k]
        self.wide.middle(0)
        self.wide.middle(1)
        for k in range(2):
            self.here.widen(k)
        for k in range(2):
            self.gather.forward(k)
        self.s_pair.wait_send()
        self.s_cross.wait_send()
        for k in range(3):
            self.sums.finish(k)
            self.above.finish(k, k > 0)
        for k in range(2):
            self.here.finish(k)
            self.wide.finish(k)
            self.gather.arrive(k)
            self.gather.sent(k)

    @classmethod
    def scratch(cls, dp, width):
        deep = dp // 2
        lines = cls.lines
        flat = pltpu.VMEM((lines, width), f32)
        half, slots = (width // 2, width), (deep, width // dp, width)
        return (
            RowSum.scratch(3, width)
            + [
                pltpu.VMEM((3, width, width), bf16),
                pltpu.VMEM((2, *half), bf16),
                pltpu.VMEM((2, *half), bf16),
                pltpu.VMEM((2, *slots), bf16),
                flat, flat, flat, flat,
                pltpu.VMEM((dp, lines // dp, width), f32),
                pltpu.VMEM((dp, width // dp, width), bf16),
                pltpu.VMEM((2, *half), bf16),
                pltpu.VMEM((2, *half), bf16),
                pltpu.VMEM((3, *slots), bf16),
            ]
            + RowGather.scratch(2)
            + [pltpu.SemaphoreType.DMA((1,))] * 4
            + DeepSum.semaphores(dp, 2)
            + DeepSum.semaphores(dp, 3)
            + WideSum.semaphores(dp, 2)
        )


def format_kernel(columns, *refs):
    count = (len(refs) - 6) // 2
    qkv_out, proj_out, core_up_out, core_down_out, up_out, down_out = refs[2 * count :]

    def form(full, shard):
        mp, width = full.shape[1], full.shape[2]
        rows = width // mp
        qkv_out[0] = shard[2, :columns].astype(f32)
        proj_out[0] = shard[2, columns:].astype(f32)
        core_up_out[0] = shard[0].astype(f32)
        for place in range(mp):
            q = quarter_at(place, mp)
            up_out[0, 0, :, q * width : (q + 1) * width] = full[0, place].astype(f32)
        for chunk in range(mp):
            at = slice(chunk * width, (chunk + 1) * width)
            core_down_out[0, :, at] = shard[1, chunk * rows : (chunk + 1) * rows].astype(f32)
            block = [None] * mp
            for place in range(mp):
                block[quarter_at(place, mp)] = full[1, place, chunk * rows : (chunk + 1) * rows]
            down_out[0, 0, at, :] = turn_blocks(jnp.concatenate(block, 0))

    for layer in range(count):
        pl.when(pl.program_id(0) == layer)(functools.partial(form, refs[layer], refs[count + layer]))


def format_call(fulls, shards, columns):
    layers = len(fulls)
    _, mp, width, _ = fulls[0].shape
    hidden = mp * width
    shapes = [
        (layers, columns, width),
        (layers, width - columns, width),
        (layers, width, width),
        (layers, width // mp, hidden),
        (layers, 1, width, hidden),
        (layers, 1, hidden, width),
    ]
    return pl.pallas_call(
        functools.partial(format_kernel, columns),
        grid=(layers,),
        out_shape=[jax.ShapeDtypeStruct(shape, f32) for shape in shapes],
        in_specs=[whole_spec(a.shape) for a in (*fulls, *shards)],
        out_specs=[image_spec(shape, 1) for shape in shapes],
        compiler_params=pltpu.CompilerParams(vmem_limit_bytes=56 * MIB),
        name="format",
    )(*fulls, *shards)


def greet(dp, me, rows=()):
    barrier = pltpu.get_barrier_semaphore()
    for row in rows:
        pl.semaphore_signal(barrier, inc=1, device_id={"mp": row}, device_id_type=MESH)

    def signal(off, carry):
        pl.semaphore_signal(barrier, inc=1, device_id={"dp": lax.rem(me + off, dp)}, device_id_type=MESH)
        return carry

    lax.fori_loop(1, dp, signal, 0)
    pl.semaphore_wait(barrier, dp - 1 + len(rows))


def partner_of(me, p, dp):
    out, bit = 0, 1
    while bit < dp:
        one, two = lax.rem(lax.div(me, bit), 2), lax.rem(lax.div(p, bit), 2)
        out = out + bit * (one + two - 2 * one * two)
        bit *= 2
    return out


def to_peer(source, target, send_sem, recv_sem, peer):
    return pltpu.make_async_remote_copy(
        src_ref=source,
        dst_ref=target,
        send_sem=send_sem,
        recv_sem=recv_sem,
        device_id={"dp": peer},
        device_id_type=MESH,
    )


def gelu_parts(h):
    root = np.float32(np.sqrt(2.0 / np.pi))
    square = h * h
    t = jnp.tanh(root * h * (1.0 + 0.044715 * square))
    half = 0.5 * (1.0 + t)
    slope = half + 0.5 * h * (1.0 - t * t) * root * (1.0 + 3 * 0.044715 * square)
    return h * half, slope


def expert_forward_kernel(dp, mp, layer, gather, *refs):
    refs = list(refs)
    buffer_ref, up_any, down_any, rup_any, rdown_any = refs[:5]
    refs = refs[5:]
    if gather:
        shards = [ref.at[layer + 1] for ref in refs[:4]]
        refs = refs[4:]
    returned_ref, recv_out, up_out, down_out = refs[:4]
    refs = refs[4:]
    if gather:
        fulls = refs[:4]
        refs = refs[4:]
    part, core, up_ref, down_ref, rup_ref, rdown_ref, recv_ref, up_eff, down_eff, local = refs[:10]
    refs = refs[10:]
    moving = WeightGather(shards, fulls, refs[:7]) if gather else None
    send_one, recv_one, send_two, recv_two = refs[-4:]
    split = dp // EXPERTS
    me = lax.axis_index("dp")
    loads = [
        pltpu.make_async_copy(source, target, local.at[k])
        for k, (source, target) in enumerate(
            [
                (up_any, up_ref),
                (rup_any.at[layer, 0], rup_ref),
                (down_any, down_ref),
                (rdown_any.at[layer, 0], rdown_ref),
                (buffer_ref.at[lax.div(me, split)], recv_ref.at[me]),
            ]
        )
    ]
    stores = [
        pltpu.make_async_copy(source, target, local.at[5 + k])
        for k, (source, target) in enumerate([(up_eff, up_out), (down_eff, down_out), (recv_ref, recv_out)])
    ]
    for load in loads:
        load.start()
    greet(dp, me, (moving.row.sibling, moving.row.across) if gather else ())

    def first(off):
        peer = partner_of(me, off, dp)
        return to_peer(
            buffer_ref.at[lax.div(peer, split)], recv_ref.at[me], send_one.at[off], recv_one.at[off], peer
        )

    def second(off):
        source = partner_of(me, off, dp)
        return to_peer(part.at[source], returned_ref.at[me], send_two.at[off], recv_two.at[off], source)

    def start_first(off, carry):
        first(dp - off).start()
        return carry

    lax.fori_loop(1, dp, start_first, 0)
    if gather:
        for k in range(4):
            moving.start(k)
    hidden = up_eff.shape[1]
    columns = up_ref.shape[-1]
    loads[0].wait()
    loads[1].wait()
    if split == 1 and columns % LANES == 0:
        for m in range(mp):
            at = slice(m * columns, (m + 1) * columns)
            up_eff[:, at] = (up_ref[m].astype(f32) + rup_ref[:, at].astype(f32)).astype(bf16)
    else:
        core[...] = rup_ref[...].astype(f32)
        begin = lax.rem(me, split) * hidden
        for m in range(mp):
            put = onehot(iota((columns, hidden), 0) + m * columns == iota((columns, hidden), 1) + begin)
            core[...] += nn(up_ref[m], put)
        up_eff[...] = core[...].astype(bf16)
    begin = pl.multiple_of(lax.rem(me, split) * hidden, LANES)
    loads[2].wait()
    loads[3].wait()
    core_part = down_ref[:, :, pl.ds(begin, hidden)].reshape(down_eff.shape[1], hidden)
    down_eff[...] = (core_part.astype(f32).T + rdown_ref[...].astype(f32)).astype(bf16)

    stores[0].start()
    stores[1].start()
    loads[4].wait()

    def work(source):
        hidden_pre = nn(recv_ref[source], up_eff[...])
        hidden_low = gelu_parts(hidden_pre)[0].astype(bf16)
        return nn(hidden_low, down_eff[...]).astype(bf16)

    returned_ref[me] = work(me)

    def step(off, carry):
        source = partner_of(me, off, dp)
        first(off).wait_recv()
        part[source] = work(source)
        second(off).start()
        return carry

    lax.fori_loop(1, dp, step, 0)
    stores[2].start()
    if gather:
        for k in range(4):
            moving.forward(k)

    def finish(off, carry):
        first(off).wait_send()
        second(off).wait()
        return carry

    lax.fori_loop(1, dp, finish, 0)
    if gather:
        for k in range(4):
            moving.arrive(k)
            moving.sent(k)
    for store_out in stores:
        store_out.wait()


def expert_backward_kernel(dp, mp, fast, reduce, *refs):
    refs = list(refs)
    if reduce:
        given_ref, attn_ref = refs[:2]
        refs = refs[2:]
    buffer_ref, recv_any, up_any, down_any = refs[:4]
    refs = refs[4:]
    returned_ref = refs.pop(0)
    if not fast:
        up_term, down_term = refs[:2]
        refs = refs[2:]
    if reduce:
        full_ref, mine_ref = refs[:2]
        refs = refs[2:]
    if fast:
        units_out = refs.pop(0)
    recv_ref, up_ref, down_ref, local = refs[:4]
    refs = refs[4:]
    if fast:
        units_ref = refs.pop(0)
    grads, hidden_low, slope, pre, part = refs[:5]
    refs = refs[5:]
    if fast:
        up_term, down_term = refs[:2]
        refs = refs[2:]
    row = Row() if reduce else None
    if reduce:
        core_in, y_out, y_in = refs[:3]
        sums = RowSum(row, [attn_ref], core_in, y_out, y_in, [mine_ref], refs[3:7])
        gather = RowGather(
            row, [given_ref.at[k] for k in range(2)], [full_ref.at[k] for k in range(2)], row.place, row.place_across,
            refs[7:13],
        )
        refs = refs[13:]
    send_one, recv_one, send_two, recv_two = refs
    split = dp // EXPERTS
    me = lax.axis_index("dp")
    loads = [
        pltpu.make_async_copy(source, target, local.at[k])
        for k, (source, target) in enumerate(
            [
                (recv_any, recv_ref),
                (up_any, up_ref),
                (down_any, down_ref),
                (buffer_ref.at[lax.div(me, split)], grads.at[me]),
            ]
        )
    ]
    for load in loads:
        load.start()
    greet(dp, me, (row.sibling, row.across) if reduce else ())

    def first(off):
        peer = partner_of(me, off, dp)
        return to_peer(buffer_ref.at[lax.div(peer, split)], grads.at[me], send_one.at[off], recv_one.at[off], peer)

    def second(off):
        source = partner_of(me, off, dp)
        return to_peer(part.at[source], returned_ref.at[me], send_two.at[off], recv_two.at[off], source)

    def start_first(off, carry):
        first(dp - off).start()
        return carry

    lax.fori_loop(1, dp, start_first, 0)
    if reduce:
        sums.start(0)
        for k in range(2):
            gather.start(k)
    for load in loads[:2]:
        load.wait()

    def again(source, carry):
        value, rate = gelu_parts(nn(recv_ref[source], up_ref[...]))
        hidden_low[source] = value.astype(bf16)
        slope[source] = rate
        return carry

    lax.fori_loop(0, dp, again, 0)
    if reduce:
        sums.middle(0)
        for k in range(2):
            full_ref[k, row.place] = given_ref[k]

    for load in loads[2:]:
        load.wait()

    def work(source):
        hidden_grad = nt(grads[source], down_ref[...])
        pre_grad = (slope[source] * hidden_grad).astype(bf16)
        pre[source] = pre_grad
        return nt(pre_grad, up_ref[...]).astype(bf16)

    returned_ref[me] = work(me)

    def step(off, carry):
        source = partner_of(me, off, dp)
        first(off).wait_recv()
        part[source] = work(source)
        second(off).start()
        return carry

    lax.fori_loop(1, dp, step, 0)
    if reduce:
        for k in range(2):
            gather.forward(k)
        sums.end(0)
    up_term[...] = jnp.zeros(up_term.shape, f32)
    down_term[...] = jnp.zeros(down_term.shape, f32)

    def terms(block, carry):
        up_term[...] += tn(recv_ref[block], pre[block])
        down_term[...] += tn(grads[block], hidden_low[block])
        return carry

    lax.fori_loop(0, dp, terms, 0)
    if fast:
        width = up_term.shape[0]
        height = width // mp
        for place in range(mp):
            q = quarter_at(place, mp)
            units_ref[0, place] = up_term[:, q * width : (q + 1) * width].astype(bf16)
            for chunk in range(mp):
                block = down_term[q * height : (q + 1) * height, chunk * width : (chunk + 1) * width]
                units_ref[1, place, chunk * height : (chunk + 1) * height] = block.astype(bf16)
        units_store = pltpu.make_async_copy(units_ref, units_out, local.at[4])
        units_store.start()

    def finish(off, carry):
        first(off).wait_send()
        second(off).wait()
        return carry

    lax.fori_loop(1, dp, finish, 0)
    if reduce:
        sums.finish(0)
        for k in range(2):
            gather.arrive(k)
            gather.sent(k)
    if fast:
        units_store.wait()


def expert_call(kernel, arrays, outs, scratch, dp, collective_id, name, flops, anys=(), any_outs=()):
    sems = [pltpu.SemaphoreType.DMA((dp,))] * 4
    vmem, anywhere = pl.BlockSpec(memory_space=pltpu.VMEM), pl.BlockSpec(memory_space=pl.ANY)
    return pl.pallas_call(
        kernel,
        out_shape=[jax.ShapeDtypeStruct(shape, dtype) for shape, dtype in (*outs, *any_outs)],
        in_specs=[vmem] * len(arrays) + [anywhere] * len(anys),
        out_specs=[vmem] * len(outs) + [anywhere] * len(any_outs),
        scratch_shapes=scratch + sems,
        compiler_params=pltpu.CompilerParams(
            vmem_limit_bytes=56 * MIB, collective_id=collective_id, has_side_effects=True
        ),
        cost_estimate=pl.CostEstimate(flops=flops, bytes_accessed=20 * MIB, transcendentals=0),
        name=name,
    )(*arrays, *anys)


def by_windows(grid):
    images, kinds = grid.shape[:2]
    blocks = GRID // WINDOW
    grid = grid.reshape(images, kinds, blocks, WINDOW, blocks, WINDOW).transpose(0, 1, 2, 4, 3, 5)
    grid = grid.reshape(images, kinds, blocks * blocks, WINPOS)
    grid = jnp.pad(grid, ((0, 0), (0, 0), (0, 0), (0, WPAD - WINPOS)), constant_values=-1)
    return grid.reshape(images, kinds, IMGROWS)


def per_device(
    patches,
    qkv_weight,
    proj_weight,
    core_up,
    core_down,
    residual_up,
    residual_down,
    position_bias,
    router_weight,
    norm_gain,
    norm_bias,
    cotangent,
    image_valid,
    expert_index,
    slot_index,
    region_id,
):
    dp, mp = lax.axis_size("dp"), lax.axis_size("mp")
    images, _, width = patches.shape
    split = dp // EXPERTS
    hidden = residual_up.shape[-1]
    hidden_full = core_up.shape[-1] * mp
    row_index = lax.axis_index("mp")

    fast = split == 1 and dp == 8 and mp == 4 and hidden == mp * width
    qkv_rows, proj_rows, down_rows = (a.transpose(0, 2, 1) for a in (qkv_weight, proj_weight, core_down))
    shards = (qkv_rows, proj_rows, core_up, down_rows)
    gathered = [[None] * len(shards)] * LAYERS
    if not fast:
        gathered = [[lax.all_gather(a[l], "mp", axis=0, tiled=False) for a in shards] for l in range(LAYERS)]

    position = jnp.where(slot_index >= 0, expert_index * SLOTS + slot_index, -1)
    row_form = by_windows(jnp.stack([position.reshape(images, GRID, GRID), region_id], 1))
    col_form = row_form.transpose(0, 2, 1)
    enter = jnp.asarray(enter_table(), bf16)
    leave = jnp.asarray(enter_table().T, bf16)
    moves = [jnp.asarray(move_table(l % 2 == 1), bf16) for l in range(LAYERS)]
    backs = [jnp.asarray(move_table(l % 2 == 1).T, bf16) for l in range(LAYERS)]
    table_rows = position_bias.transpose(0, 2, 1).reshape(LAYERS * HEADS, OFFSETS)
    table_rows = jnp.pad(table_rows, ((0, 0), (0, TABLE - OFFSETS)))
    entry_row, entry_col = jnp.asarray(cell_entries()[None, :]), jnp.asarray(cell_entries()[:, None])
    routers = jnp.pad(router_weight.transpose(0, 2, 1), ((0, 0), (0, LANES - EXPERTS), (0, 0)))

    token = (images, IMGROWS, width)
    buffer_shape = (ROWS, width)
    block_rows = (dp, SLOTS, width)
    pieces = (split, ROWS, width)

    def by_piece(returned):
        return returned.reshape(EXPERTS, split, SLOTS, width).transpose(1, 0, 2, 3).reshape(pieces)

    records = []
    before = None
    for l in range(LAYERS):
        first = l == 0
        gather = fast and first
        if first:
            arrays = [("image", patches), ("whole", enter)]
        else:
            arrays = [("image", before[0]), ("image", before[1]), ("whole", before[2])]
        arrays += [
            ("smem", image_valid),
            ("image", col_form),
            ("image", row_form),
            ("any", qkv_rows) if gather else ("whole", gathered[l][0]),
            ("any", proj_rows) if gather else ("whole", gathered[l][1]),
            ("whole", table_rows) if first else (l, biases),
            ("whole", moves[l]),
            ("whole", backs[l]),
            (l, norm_gain),
            (l, norm_bias),
            (l, routers),
        ]
        if first:
            arrays.append(("whole", entry_row))
        if gather:
            arrays += [("any", core_up), ("any", down_rows)]
        outs = [("image", token, f32)]
        if first:
            outs.append(("whole", (LAYERS, HEADS, WPAD, LANES), f32))
        else:
            outs.append(("image", token, f32))
        outs += [
            ("image", token, f32),
            ("image", token, bf16),
            ("image", (images, IMGROWS, 1), f32),
            ("whole", buffer_shape, bf16),
            ("image", token, bf16),
            ("image", (images, 2 * width, IMGROWS), bf16),
            ("image", token, bf16),
            ("image", (images, PAIRS * HEADS, WPAD, LANES), bf16),
            ("image", (images, width, IMGROWS), bf16),
            ("whole", (width, width), bf16),
        ]
        scratch = [pltpu.VMEM(buffer_shape, f32)]
        gathered_shapes = [(mp, *a.shape[1:]) for a in shards]
        if gather:
            outs.append(("whole", (3 * width, width), bf16))
            outs += [("any", shape, bf16) for shape in gathered_shapes[2:]]
            scratch += [pltpu.VMEM(shape, bf16) for shape in gathered_shapes[:2]] + WeightGather.scratch(4)
        results = list(
            image_call(
                functools.partial(attention_forward_kernel, first, l % 2 == 1, mp, gather),
                images, arrays, outs, scratch, f"attend_{l}", 3 * LAYERS + 1 if gather else None,
            )
        )
        if gather:
            gathered[l] = [results[-3], None] + results[-2:]
            results = results[:-3]
        carried = results.pop(0)
        if first:
            biases = results.pop(0)
        else:
            records[-1]["expert_out"] = results.pop(0)
        middle, second_low, gate, buffer = results[:4]
        gather = fast and l < LAYERS - 1
        eff_shapes = [((width, hidden), bf16), ((hidden, width), bf16)]
        returned, received, up_eff, down_eff, *more = expert_call(
            functools.partial(expert_forward_kernel, dp, mp, l, gather),
            [],
            [(block_rows, bf16)],
            [
                pltpu.VMEM(block_rows, bf16),
                pltpu.VMEM((8, LANES) if fast else (width, hidden), f32),
                pltpu.VMEM(gathered_shapes[2], bf16),
                pltpu.VMEM(gathered_shapes[3], bf16),
                pltpu.VMEM((width, hidden), bf16),
                pltpu.VMEM((hidden, width), bf16),
                pltpu.VMEM(block_rows, bf16),
                pltpu.VMEM((width, hidden), bf16),
                pltpu.VMEM((hidden, width), bf16),
                pltpu.SemaphoreType.DMA((8,)),
            ]
            + (WeightGather.scratch(4) if gather else []),
            dp, l, f"experts_{l}", 4 * dp * SLOTS * width * hidden,
            [
                buffer.reshape(EXPERTS, SLOTS, width), gathered[l][2], gathered[l][3], residual_up, residual_down,
                *(shards if gather else ()),
            ],
            [(block_rows, bf16), *eff_shapes, *([(shape, bf16) for shape in gathered_shapes] if gather else ())],
        )
        if gather:
            gathered[l + 1] = more
        returned = by_piece(returned)
        before = (middle, gate, returned)
        records.append(
            dict(
                carried=carried, middle=middle, second_low=second_low, gate=gate, saved=results[4:], received=received,
                up_eff=up_eff, down_eff=down_eff,
            )
        )

    top = records[-1]
    block_output, grad, logit_grad, router_part, buffer = image_call(
        turn_kernel,
        images,
        [
            ("image", before[0]),
            ("image", before[1]),
            ("whole", before[2]),
            ("image", cotangent),
            ("whole", enter),
            ("whole", leave),
            ("image", col_form),
            ("image", row_form),
            ("image", top["second_low"]),
            (LAYERS - 1, routers),
        ],
        [
            ("image", patches.shape, bf16),
            ("image", token, f32),
            ("image", (images, IMGROWS, LANES), f32),
            ("whole", (LANES, width), f32),
            ("whole", buffer_shape, bf16),
        ],
        [pltpu.VMEM(buffer_shape, f32)],
        "turn",
    )
    router_parts, tables, smalls = [None] * LAYERS, [None] * LAYERS, [None] * LAYERS
    residual_sums, shard_sums = [None] * LAYERS, [None] * LAYERS
    router_parts[LAYERS - 1] = router_part
    units, attn_units, mines = [None] * LAYERS, [None] * LAYERS, [None] * LAYERS
    for l in reversed(range(LAYERS)):
        rec = records[l]
        last = l == 0
        reduce = fast and l < LAYERS - 1
        arrays = []
        anys = [buffer.reshape(EXPERTS, SLOTS, width), rec["received"], rec["up_eff"], rec["down_eff"]]
        outs, any_outs = [(block_rows, bf16)], []
        scratch = [pltpu.VMEM(block_rows, bf16)] + [pltpu.VMEM(*shape) for shape in eff_shapes]
        scratch.append(pltpu.SemaphoreType.DMA((5,)))
        if fast:
            any_outs.append(((2, mp, width, width), bf16))
            scratch.append(pltpu.VMEM(*any_outs[0]))
        scratch += [
            pltpu.VMEM(block_rows, bf16),
            pltpu.VMEM((dp, SLOTS, hidden), bf16),
            pltpu.VMEM((dp, SLOTS, hidden), f32),
            pltpu.VMEM((dp, SLOTS, hidden), bf16),
            pltpu.VMEM(block_rows, bf16),
        ]
        if fast:
            scratch += [pltpu.VMEM((width, hidden), f32)] * 2
        else:
            outs += [((width, hidden), f32)] * 2
        if reduce:
            arrays += [mines[l + 1], attn_units[l + 1]]
            outs += [((2, mp, width, width), bf16), ((width, width), bf16)]
            scratch += RowSum.scratch(1, width) + RowGather.scratch(2)
        results = list(
            expert_call(
                functools.partial(expert_backward_kernel, dp, mp, fast, reduce), arrays, outs, scratch, dp, LAYERS + l,
                f"experts_back_{l}", 10 * dp * SLOTS * width * hidden, anys, any_outs,
            )
        )
        returned_grad = results.pop(0)
        if fast:
            units[l] = results.pop(-1)
        else:
            residual_sums[l] = lax.psum(tuple(t.astype(bf16) for t in results[:2]), "mp")
        if reduce:
            full_above, mine_above = results
        window_in, qk, v, probs, att, proj_full = rec["saved"]
        qkv_full = gathered[l][0].reshape(3 * width, width)
        arrays = [
            ("smem", image_valid),
            ("image", grad),
            ("whole", by_piece(returned_grad)),
            ("image", logit_grad),
            ("image", rec["middle"]),
            ("image", rec["carried"]),
            (l, routers),
            ("image", col_form),
            ("whole", moves[l]),
            ("whole", backs[l]),
            (l, norm_gain),
            ("whole", proj_full),
            ("whole", qkv_full),
            ("image", window_in),
            ("image", qk),
            ("image", v),
            ("image", probs),
            ("image", att),
        ]
        outs = [("image", patches.shape if last else token, f32)]
        scratch = [pltpu.VMEM((3 * width, (2 - images % 2) * IMGROWS), bf16)]
        closes = fast and last
        table_shape, small_shape = (HEADS, WPAD, LANES), (8, width)
        if fast:
            arrays.append(("whole", units[l]))
            scratch += [pltpu.VMEM((3 * width, width), f32), pltpu.VMEM((width, width), f32)]
        if closes:
            outs += [
                ("whole", (2, mp, width, width), bf16),
                ("whole", (3, width, width), bf16),
                ("whole", (Closing.lines, width), f32),
                ("whole", (3, width, width), bf16),
            ]
        else:
            if fast:
                outs += [
                    ("whole", (width // 2, width), bf16),
                    ("whole", (mp, width, width), bf16),
                    ("whole", (2, width, width), bf16),
                ]
            else:
                outs += [("whole", (3 * width, width), f32), ("whole", (width, width), f32)]
            outs += [("whole", table_shape, f32), ("whole", small_shape, f32)]
        if last:
            arrays.append(("whole", leave))
            if fast:
                arrays += [
                    ("whole", a)
                    for a in (
                        tables[1], smalls[1], router_parts[1], router_parts[0], entry_col, halves_above, mines[1],
                        mine_above,
                    )
                ]
        else:
            below = records[l - 1]
            arrays += [
                ("image", row_form),
                ("image", below["expert_out"]),
                ("image", below["second_low"]),
                (l - 1, routers),
            ]
            outs += [
                ("image", (images, IMGROWS, LANES), f32),
                ("whole", (LANES, width), f32),
                ("whole", buffer_shape, bf16),
            ]
            scratch.append(pltpu.VMEM(buffer_shape, f32))
        if closes:
            scratch += [
                pltpu.VMEM(table_shape, f32),
                pltpu.VMEM(small_shape, f32),
                pltpu.VMEM((mp, width, width), bf16),
                pltpu.VMEM((Closing.lines, width), f32),
            ]
            scratch += [pltpu.VMEM(shape, dtype) for _, shape, dtype in outs[1:5]] + Closing.scratch(dp, width)
        elif fast:
            scratch += RowSum.scratch(2, width) + [pltpu.VMEM((width // 2, width), bf16)]
            scratch += [pltpu.SemaphoreType.DMA((1,))] * 2
        results = list(
            image_call(
                functools.partial(attention_backward_kernel, last, dp, mp, fast),
                images, arrays, outs, scratch, f"attend_back_{l}", 2 * LAYERS + 1 + l if fast else None,
            )
        )
        grad = results.pop(0)
        if closes:
            full, closed, lines, shard_above = results
            continue
        if fast:
            halves_above = results.pop(0)
            attn_units[l], mines[l] = results[:2]
        else:
            qkv_part, proj_part = results[:2]
        tables[l], smalls[l] = results[2:4]
        if not last:
            logit_grad, router_parts[l - 1], buffer = results[4:]
        if fast:
            continue
        attn = (
            lax.psum_scatter(qkv_part.astype(bf16), "mp", scatter_dimension=0, tiled=True),
            lax.psum_scatter(proj_part.T.astype(bf16), "mp", scatter_dimension=0, tiled=True),
        )
        up_sum, down_sum = residual_sums[l]
        if split > 1:
            begin = lax.axis_index("dp") % split * hidden
            empty = jnp.zeros((width, hidden_full), bf16)
            up_sum = lax.dynamic_update_slice_in_dim(empty, up_sum, begin, 1)
            down_sum = lax.dynamic_update_slice_in_dim(empty, down_sum, begin, 1)
        up_columns, down_columns = core_up.shape[-1], core_down.shape[-1]
        up_shard = lax.dynamic_slice_in_dim(up_sum, row_index * up_columns, up_columns, 1)
        down_shard = lax.dynamic_slice_in_dim(down_sum, row_index * down_columns, down_columns, 0)
        shard_sums[l] = lax.psum((attn[0], attn[1], up_shard, down_shard), "dp")

    if fast:
        *attn_grads, core_up_grad, core_down_grad, residual_up_grad, residual_down_grad = format_call(
            [full, full_above], [closed, shard_above], qkv_weight.shape[-1]
        )
        attn_grads = [a.transpose(0, 2, 1) for a in attn_grads]
        core_grads = (core_up_grad, core_down_grad.transpose(0, 2, 1))
        at = LAYERS * HEADS
        table_sum = lines[:at, :OFFSETS]
        router_sum = lines[at : at + LAYERS * EXPERTS].reshape(LAYERS, EXPERTS, width)
        at += LAYERS * EXPERTS
        small_sum = lines[at : at + LAYERS * 8].reshape(LAYERS, 8, width)[:, :4]
    else:
        entry = cell_entries()[None, :] + np.array([key_base_of(key) for key in range(WPAD)])[:, None]
        entry = jnp.asarray(np.where(np.arange(WPAD)[:, None] < WINPOS, entry, -1).reshape(-1))
        entry_turned = (entry[:, None] == jnp.arange(OFFSETS)[None, :]).astype(f32)
        table_part = jnp.dot(
            jnp.stack(tables, 0).reshape(LAYERS * HEADS, WPAD * LANES), entry_turned, precision=highest
        )
        small_part = jnp.stack(smalls, 0)[:, :4]
        router_part = jnp.stack(router_parts, 0)[:, :EXPERTS]
        table_sum, small_sum, router_sum = lax.psum((table_part, small_part, router_part), ("dp", "mp"))

        def shard(k):
            return jnp.stack([shard_sums[l][k] for l in range(LAYERS)], 0).astype(f32)

        attn_grads = (shard(0).transpose(0, 2, 1), shard(1).transpose(0, 2, 1))
        core_grads = (shard(2), shard(3).transpose(0, 2, 1))
        residual_up_grad, residual_down_grad = (
            jnp.stack([residual_sums[l][k] for l in range(LAYERS)], 0).astype(f32) for k in range(2)
        )
        residual_up_grad = residual_up_grad[:, None]
        residual_down_grad = residual_down_grad.transpose(0, 2, 1)[:, None]

    return (
        block_output,
        grad,
        attn_grads[0],
        attn_grads[1],
        core_grads[0],
        core_grads[1],
        residual_up_grad,
        residual_down_grad,
        table_sum.reshape(LAYERS, HEADS, OFFSETS).transpose(0, 2, 1),
        router_sum.transpose(0, 2, 1),
        small_sum[:, 0:2],
        small_sum[:, 2:4],
    )


def solution(mesh):
    placed = (
        P(("dp", "mp"), None, None),
        P(None, None, "mp"),
        P(None, None, "mp"),
        P(None, None, "mp"),
        P(None, None, "mp"),
        P(None, "dp", None, None),
        P(None, "dp", None, None),
        P(),
        P(),
        P(),
        P(),
        P(("dp", "mp"), None, None),
        P(("dp", "mp")),
        P(("dp", "mp"), None),
        P(("dp", "mp"), None),
        P(("dp", "mp"), None, None),
    )
    return jax.shard_map(
        per_device,
        mesh=mesh,
        in_specs=placed,
        out_specs=(
            P(("dp", "mp"), None, None),
            P(("dp", "mp"), None, None),
            P(None, None, "mp"),
            P(None, None, "mp"),
            P(None, None, "mp"),
            P(None, None, "mp"),
            P(None, "dp", None, None),
            P(None, "dp", None, None),
            P(),
            P(),
            P(),
            P(),
        ),
        check_vma=False,
    )
```
